32 devices in a mesh: dp: 8 (over z, x), head: 4 (over y, core).
Axes of the slice: x: 2, y: 2, z: 4, core: 2. Of those that a mesh axis runs over, the one named last changes fastest.
Arguments:
- tokens: bfloat16 [8192, 768], P(('dp', 'head')), may hold values from -6 to 6
- cotangent: bfloat16 [8192, 768], P(('dp', 'head')), may hold values from -6 to 6
- qkv_weight: bfloat16 [768, 2304], replicated, may hold values from -0.21875 to 0.21875
- out_weight: bfloat16 [768, 768], replicated, may hold values from -0.875 to 0.875
- up_weight: bfloat16 [768, 3072], replicated, may hold values from -0.21875 to 0.21875
- down_weight: bfloat16 [3072, 768], replicated, may hold values from -0.109375 to 0.109375
- vectors: float32 [9216], replicated, may hold values from -1.2 to 1.4
- qkv_moment: float32 [768, 2304], P(None, 'dp'), may hold values from -160 to 160
- out_moment: float32 [768, 768], P(None, 'dp'), may hold values from -160 to 160
- up_moment: float32 [768, 3072], P(None, 'dp'), may hold values from -128 to 128
- down_moment: float32 [768, 3072], P(None, 'dp'), may hold values from -256 to 256
- adam_first: float32 [9216], P('dp'), may hold values from -120.67956 to 120.67956
- adam_second: float32 [9216], P('dp'), may hold values from 2.05005 to 295.2072
- bucket_class: int32 [8], P('dp'), may hold values from 0 to 2, as said below
- row_lengths: int32 [8, 8], P('dp'), may hold values from 0 to 512, as said below
Outputs:
- mixed: float32 [8192, 768], P(('dp', 'head'))
- input_grad: float32 [8192, 768], P(('dp', 'head'))
- qkv_moment_new: float32 [768, 2304], P(None, 'dp')
- out_moment_new: float32 [768, 768], P(None, 'dp')
- up_moment_new: float32 [768, 3072], P(None, 'dp')
- down_moment_new: float32 [768, 3072], P(None, 'dp')
- new_qkv: float32 [768, 2304], P(None, 'dp')
- new_out: float32 [768, 768], P(None, 'dp')
- new_up: float32 [768, 3072], P(None, 'dp')
- new_down: float32 [3072, 768], P('dp')
- vector_moment: float32 [9216], P('dp')
- vector_second: float32 [9216], P('dp')
- vector_new: float32 [9216], P('dp')
The draws below stay inside these ranges and needn't reach their ends.
Inputs may be any that keep to these rules, and one draw needn't show every extreme that they name: `bucket_class`: every class 0, 1, 2 occurs. `row_lengths`: with span = 128 * 2 ** bucket_class[g], entries 0 to 1024 / span - 1 of bucket g are lengths from 1 to span, one of them equal to span; the other entries are 0.
All inputs are finite; a program needn't handle non-finite values.
Results may differ from the reference program's by a relative error of at most 0.019.
Values may be sent and summed in bfloat16 or wider, within the bound.
A program may use at most 256 MiB of HBM per device.

```python
import math
import jax
import jax.numpy as jnp
from jax import lax

D = 768
HEADS = 12
HEAD_DIM = 64
FF = 3072
BASE_LEN = 128
NS_STEPS = 5
STEP = 5
MAX_LEN = 512
GROUP_TOK = 1024
TOKENS = 8192
SLOTS = 8
N_DP = 8


def segment_ids():
    places = jnp.arange(8 * D + FF, dtype=jnp.int32)
    bounds = jnp.array([D, 2 * D, 3 * D, 4 * D, 5 * D, 5 * D + FF, 6 * D + FF, 7 * D + FF], dtype=jnp.int32)
    return jnp.sum((places[:, None] >= bounds[None, :]).astype(jnp.int32), axis=1)


def grad_scales():
    table = jnp.array([1.0, 3.0, 1.0, 1.0, 1.0, 0.5, 1.0, 1.0, 1.0], dtype=jnp.float32)
    return table[segment_ids()] * TOKENS ** 0.5


def row_plan(key):
    row_class = (jax.random.permutation(jax.random.fold_in(key, 11), N_DP) % 3).astype(jnp.int32)
    row_span = BASE_LEN * jnp.left_shift(jnp.int32(1), row_class)
    row_count = GROUP_TOK // row_span
    raw_draw = jax.random.randint(jax.random.fold_in(key, 12), (N_DP, SLOTS), 0, 1 << 20, dtype=jnp.int32)
    lengths = raw_draw % row_span[:, None] + 1
    full_row = jax.random.randint(jax.random.fold_in(key, 13), (N_DP,), 0, 1 << 20, dtype=jnp.int32) % row_count
    slot_ids = jnp.arange(SLOTS, dtype=jnp.int32)
    lengths = jnp.where(slot_ids[None, :] == full_row[:, None], row_span[:, None], lengths)
    lengths = jnp.where(slot_ids[None, :] < row_count[:, None], lengths, 0)
    return (row_class, lengths.astype(jnp.int32))


def draw_bucket_class(key, part):
    plan = row_plan(key)
    return plan[0]


def draw_row_lengths(key, part):
    plan = row_plan(key)
    return plan[1]


def draw_vectors(key, part):
    key = jax.random.fold_in(key, 1)
    segments = segment_ids()
    noise = jnp.clip(jax.random.normal(key, (8 * D + FF,), jnp.float32), -4.0, 4.0)
    is_gain = (segments == 3) | (segments == 7)
    return jnp.where(is_gain, 1.0 + 0.1 * noise, 0.3 * noise)


def draw_adam_first(key, part):
    key = jax.random.fold_in(key, 2)
    noise = jnp.clip(jax.random.normal(key, (8 * D + FF,), jnp.float32), -4.0, 4.0)
    return noise * grad_scales() / 9.0


def draw_adam_second(key, part):
    key = jax.random.fold_in(key, 3)
    factor = jnp.exp(jax.random.uniform(key, (8 * D + FF,), jnp.float32, 0.0, math.log(4.0)))
    scales = grad_scales()
    return factor * scales * scales / 999.0


def level_of(stream_key, dims, cuts, least, top_value):
    level = 1.0
    for position, shards_of in cuts:
        heights = jax.random.uniform(jax.random.fold_in(jax.random.fold_in(stream_key, 6), position), (shards_of,), jnp.float32, least / len(cuts), top_value / len(cuts))
        level = level * jnp.repeat(jnp.exp(heights), dims[position] // shards_of).reshape((-1,) + (1,) * (len(dims) - 1 - position))
    return level


def gaussian(own_key, extent, scale, limit, split=(), kind=jnp.bfloat16):
    values = scale * jax.random.normal(own_key, extent, jnp.float32)
    if split:
        values = values * level_of(own_key, extent, split, -0.22, 0.18)
    return jnp.clip(values, -limit, limit).astype(kind)


def setup_inputs(seed: int = 0) -> dict:
    arg_keys = jax.random.split(jax.random.key(seed), 16)
    tokens = gaussian(arg_keys[0], (TOKENS, D), 1.0, 6.0, ((0, 32),))
    cotangent = gaussian(arg_keys[1], (TOKENS, D), 1.0, 6.0, ((0, 32),))
    qkv_weight = gaussian(arg_keys[2], (D, 3 * D), D ** -0.5, 0.21875)
    out_weight = gaussian(arg_keys[3], (D, D), (D // 16) ** -0.5, 0.875)
    up_weight = gaussian(arg_keys[4], (D, FF), D ** -0.5, 0.21875)
    down_weight = gaussian(arg_keys[5], (FF, D), FF ** -0.5, 0.109375)
    vectors = draw_vectors(jax.random.fold_in(arg_keys[15], 71), 0)
    qkv_moment = gaussian(arg_keys[7], (D, 3 * D), (0.3 * TOKENS ** 0.5), 160.0, ((1, 8),), jnp.float32)
    out_moment = gaussian(arg_keys[8], (D, D), (0.3 * TOKENS ** 0.5), 160.0, ((1, 8),), jnp.float32)
    up_moment = gaussian(arg_keys[9], (D, FF), (0.25 * TOKENS ** 0.5), 128.0, ((1, 8),), jnp.float32)
    down_moment = gaussian(arg_keys[10], (D, FF), (0.5 * TOKENS ** 0.5), 256.0, ((1, 8),), jnp.float32)
    adam_first = draw_adam_first(jax.random.fold_in(arg_keys[15], 71), 0)
    adam_second = draw_adam_second(jax.random.fold_in(arg_keys[15], 71), 0)
    bucket_class = draw_bucket_class(jax.random.fold_in(arg_keys[15], 71), 0)
    row_lengths = draw_row_lengths(jax.random.fold_in(arg_keys[15], 71), 0)
    return {"tokens": tokens, "cotangent": cotangent, "qkv_weight": qkv_weight, "out_weight": out_weight, "up_weight": up_weight, "down_weight": down_weight, "vectors": vectors, "qkv_moment": qkv_moment, "out_moment": out_moment, "up_moment": up_moment, "down_moment": down_moment, "adam_first": adam_first, "adam_second": adam_second, "bucket_class": bucket_class, "row_lengths": row_lengths}


@jax.custom_vjp
def low(v):
    return lax.optimization_barrier(v.astype(jnp.bfloat16)).astype(jnp.float32)

@jax.custom_vjp
def low_back(v):
    return v

def low_keep(v):
    return (low(v), None)

def low_pass(kept, grad):
    return (grad,)

def back_keep(v):
    return (v, None)

def back_low(kept, grad):
    return (low(grad),)
low.defvjp(low_keep, low_pass)
low_back.defvjp(back_keep, back_low)
highest = lax.Precision.HIGHEST
norm_eps = 1e-12
masked_score = -1000000000.0
quintic_a = 3.4445
quintic_b = -4.775
quintic_c = 2.0315
muon_rate = 1.0
muon_decay = 0.01
muon_keep = 0.5
adam_rate = 0.2
beta_first = 0.9
beta_second = 0.999
adam_eps = 1e-08

def split_vectors(vectors, width, hidden):
    lengths_list = [width] * 5 + [hidden] + [width] * 3
    pieces = []
    offset = 0
    for length in lengths_list:
        pieces.append(vectors[offset:offset + length])
        offset = offset + length
    return pieces

def layer_norm(values, scale_vec, shift_vec):
    centre = values - lax.optimization_barrier(jnp.mean(values, axis=-1, keepdims=True))
    spread = lax.optimization_barrier(jnp.mean(centre * centre, axis=-1, keepdims=True))
    return centre * lax.rsqrt(spread + norm_eps) * scale_vec + shift_vec

def row_layout(row_class, lengths, first_pos, how_many):
    row_span = BASE_LEN * jnp.left_shift(jnp.int32(1), row_class)
    places = first_pos + jnp.arange(how_many, dtype=jnp.int32)
    row_ids = places // row_span
    offsets = places - row_ids * row_span
    slot_ids = jnp.arange(lengths.shape[0], dtype=jnp.int32)
    row_len = lax.optimization_barrier(jnp.sum(jnp.where(row_ids[:, None] == slot_ids[None, :], lengths[None, :], 0), axis=1))
    return (row_ids, offsets < row_len)

def attend_block(queries, keys_in, values_in, row_ids, valid_keys):
    raw_score = jnp.einsum('qhe,khe->hqk', queries, keys_in, precision=highest) * HEAD_DIM ** (-0.5)
    allowed = (row_ids[:, None] == row_ids[None, :]) & valid_keys[None, :]
    scores = low_back(jnp.where(allowed[None], raw_score, masked_score))
    attn_prob = jax.nn.softmax(scores, axis=-1)
    return jnp.einsum('hqk,khe->qhe', low(attn_prob), values_in, precision=highest)
checked_block = jax.checkpoint(attend_block)

def run_block(block_in):
    return checked_block(block_in[0], block_in[1], block_in[2], block_in[3], block_in[4])

def layer(params, inputs, row_ids, valid_keys):
    qkv_w, out_w, up_w, down_w, vectors = params
    pieces = split_vectors(vectors, D, FF)
    bias_query, bias_value, bias_out, gain_one, shift_one = (pieces[0], pieces[1], pieces[2], pieces[3], pieces[4])
    bias_up, bias_down, gain_two, shift_two = (pieces[5], pieces[6], pieces[7], pieces[8])
    bias_qkv = jnp.concatenate([bias_query, jnp.zeros_like(bias_query), bias_value])
    qkv = low(low_back(jnp.dot(inputs, qkv_w, precision=highest) + bias_qkv))
    blocks = GROUP_TOK // MAX_LEN
    qkv_blocks = qkv.reshape(blocks, MAX_LEN, 3, HEADS, HEAD_DIM)
    heads_out = lax.map(run_block, (qkv_blocks[:, :, 0], qkv_blocks[:, :, 1], qkv_blocks[:, :, 2], row_ids.reshape(blocks, MAX_LEN), valid_keys.reshape(blocks, MAX_LEN)))
    heads = low(low_back(heads_out.reshape(GROUP_TOK, D)))
    attn_out = low_back(jnp.dot(heads, out_w, precision=highest) + bias_out)
    normed_one = layer_norm(inputs + attn_out, gain_one, shift_one)
    up_val = low_back(jnp.dot(low(normed_one), up_w, precision=highest) + bias_up)
    active = low(jax.nn.gelu(up_val, approximate=False))
    down_val = low_back(jnp.dot(active, down_w, precision=highest) + bias_down)
    return layer_norm(normed_one + down_val, gain_two, shift_two)

def newton_schulz(current, gram_mat):
    factor = 1.0 / (jnp.sqrt(jnp.trace(gram_mat)) + 1e-07)
    current = current * factor
    gram_mat = gram_mat * (factor * factor)
    for ns_step in range(NS_STEPS):
        square = jnp.dot(gram_mat, gram_mat, precision=highest)
        poly = quintic_b * gram_mat + quintic_c * square
        current = quintic_a * current + jnp.dot(poly, current, precision=highest)
        if ns_step + 1 < NS_STEPS:
            cube = jnp.dot(square, gram_mat, precision=highest)
            times_poly = quintic_a * gram_mat + quintic_b * square + quintic_c * cube
            gram_mat = quintic_a * times_poly + jnp.dot(times_poly, poly, precision=highest)
    return current

def orthogonalize(moment):
    gram_mat = jnp.dot(moment, moment.T, precision=highest)
    return newton_schulz(moment, gram_mat)

def reference(tokens, cotangent, qkv_weight, out_weight, up_weight, down_weight, vectors, qkv_moment, out_moment, up_moment, down_moment, adam_first, adam_second, bucket_class, row_lengths):
    params = (qkv_weight.astype(jnp.float32), out_weight.astype(jnp.float32), up_weight.astype(jnp.float32), down_weight.astype(jnp.float32), vectors)
    token_groups = tokens.astype(jnp.float32).reshape(N_DP, GROUP_TOK, D)
    cot_groups = cotangent.astype(jnp.float32).reshape(N_DP, GROUP_TOK, D)

    def one_group(grad_total, group_in):
        inputs, cot_in, row_class, lengths = group_in
        row_ids, valid_keys = row_layout(row_class, lengths, 0, GROUP_TOK)

        def forward(param_in, token_in):
            return layer(param_in, token_in, row_ids, valid_keys)
        output, backward = jax.vjp(forward, params, inputs)
        grad_params, grad_tokens = backward(cot_in)
        grad_total = jax.tree.map(jnp.add, grad_total, grad_params)
        return (grad_total, (output, grad_tokens))
    start_total = jax.tree.map(jnp.zeros_like, params)
    grads, outputs = lax.scan(one_group, start_total, (token_groups, cot_groups, bucket_class, row_lengths))
    mixed, input_grad = outputs
    grad_qkv, grad_out, grad_up, grad_down, grad_vec = grads
    moments = (muon_keep * qkv_moment + grad_qkv, muon_keep * out_moment + grad_out, muon_keep * up_moment + grad_up, muon_keep * down_moment + grad_down.T)
    ortho = [orthogonalize(moment) for moment in moments]
    shrink = 1.0 - muon_rate * muon_decay
    new_qkv = qkv_weight.astype(jnp.float32) * shrink - muon_rate * math.sqrt(3.0) * ortho[0]
    new_out = out_weight.astype(jnp.float32) * shrink - muon_rate * ortho[1]
    new_up = up_weight.astype(jnp.float32) * shrink - muon_rate * math.sqrt(max(1.0, FF / D)) * ortho[2]
    new_down = down_weight.astype(jnp.float32) * shrink - muon_rate * ortho[3].T
    vec_first = beta_first * adam_first + (1.0 - beta_first) * grad_vec
    vec_second = beta_second * adam_second + (1.0 - beta_second) * grad_vec * grad_vec
    first_hat = vec_first / (1.0 - beta_first ** STEP)
    second_hat = vec_second / (1.0 - beta_second ** STEP)
    vec_new = vectors - adam_rate * first_hat / (jnp.sqrt(second_hat) + adam_eps)
    return (mixed.reshape(TOKENS, D), input_grad.reshape(TOKENS, D), moments[0], moments[1], moments[2], moments[3], new_qkv, new_out, new_up, new_down, vec_first, vec_second, vec_new)
```

```python
import functools
import math

import jax
import jax.numpy as jnp
from jax import lax
from jax.experimental import pallas as pl
from jax.experimental.pallas import tpu as pltpu
from jax.sharding import PartitionSpec as P

D = 768
HEADS = 12
HEAD_DIM = 64
FF = 3072
BASE_LEN = 128
NS_STEPS = 5
STEP = 5
MAX_LEN = 512

f32 = jnp.float32
bf16 = jnp.bfloat16

norm_eps = 1e-12
masked_score = -1000000000.0
quintic_a = 3.4445
quintic_b = -4.775
quintic_c = 2.0315
muon_rate = 1.0
muon_decay = 0.01
muon_keep = 0.5
adam_rate = 0.2
beta_first = 0.9
beta_second = 0.999
adam_eps = 1e-08
MIB = 1024 * 1024


def dot(left, right, left_dim, right_dim):
    return lax.dot_general(
        left, right, (((left_dim,), (right_dim,)), ((), ())), preferred_element_type=f32
    )


def split_vectors(vectors, width, hidden):
    lengths_list = [width] * 5 + [hidden] + [width] * 3
    pieces = []
    offset = 0
    for length in lengths_list:
        pieces.append(vectors[offset : offset + length])
        offset = offset + length
    return pieces


def allowed_mask(class_ref, length_ref, block, tok):
    shift = class_ref[0] + int(math.log2(BASE_LEN))
    query_place = block * tok + lax.broadcasted_iota(jnp.int32, (tok, 1), 0)
    lane = lax.broadcasted_iota(jnp.int32, (1, 2 * tok), 1)
    own = lane < tok
    key_place = jnp.where(own, block * tok + lane, (block ^ 1) * tok + lane - tok)
    key_row = lax.shift_right_logical(key_place, jnp.broadcast_to(shift, key_place.shape))
    offset = key_place - lax.shift_left(key_row, jnp.broadcast_to(shift, key_place.shape))
    row_len = jnp.zeros_like(key_row)
    for slot in range(length_ref.shape[1]):
        row_len = jnp.where(key_row == slot, length_ref[0, slot], row_len)
    key_row = jnp.where(offset < row_len, key_row, -1)
    query_row = lax.shift_right_logical(query_place, jnp.broadcast_to(shift, query_place.shape))
    return query_row == key_row


def half_masks():
    lane = lax.broadcasted_iota(jnp.int32, (1, 2 * HEAD_DIM), 1)
    first = (lane < HEAD_DIM).astype(f32)
    return (first.astype(bf16), (1.0 - first).astype(bf16)), lane < HEAD_DIM


def head_prob(query, keys, allowed):
    score = jnp.where(allowed, dot(query, keys, 1, 1) * HEAD_DIM ** (-0.5), masked_score)
    exponent = jnp.exp(score - jnp.max(score, axis=-1, keepdims=True))
    return exponent / jnp.sum(exponent, axis=-1, keepdims=True)


def attend_kernel(block_ref, class_ref, length_ref, qkv_ref, other_ref, out_ref):
    tok = qkv_ref.shape[0]
    allowed = allowed_mask(class_ref, length_ref, block_ref[0], tok)
    masks, first = half_masks()
    for pair in range(HEADS // 2):
        cols = pl.ds(pair * 2 * HEAD_DIM, 2 * HEAD_DIM)
        kcols = pl.ds(D + pair * 2 * HEAD_DIM, 2 * HEAD_DIM)
        vcols = pl.ds(2 * D + pair * 2 * HEAD_DIM, 2 * HEAD_DIM)
        query = qkv_ref[:, cols]
        keys = jnp.concatenate([qkv_ref[:, kcols], other_ref[:, cols]], axis=0)
        values = jnp.concatenate([qkv_ref[:, vcols], other_ref[:, kcols]], axis=0)
        outs = []
        for mask in masks:
            prob = head_prob(query * mask, keys, allowed)
            outs.append(dot(prob.astype(bf16), values, 1, 0))
        out_ref[:, cols] = jnp.where(first, outs[0], outs[1]).astype(bf16)


def attend_back_kernel(
    block_ref, class_ref, length_ref, qkv_ref, other_ref, grad_ref, dq_ref, own_ref, send_ref
):
    tok = qkv_ref.shape[0]
    allowed = allowed_mask(class_ref, length_ref, block_ref[0], tok)
    masks, first = half_masks()
    scale = HEAD_DIM ** (-0.5)
    for pair in range(HEADS // 2):
        cols = pl.ds(pair * 2 * HEAD_DIM, 2 * HEAD_DIM)
        kcols = pl.ds(D + pair * 2 * HEAD_DIM, 2 * HEAD_DIM)
        vcols = pl.ds(2 * D + pair * 2 * HEAD_DIM, 2 * HEAD_DIM)
        query = qkv_ref[:, cols]
        keys = jnp.concatenate([qkv_ref[:, kcols], other_ref[:, cols]], axis=0)
        values = jnp.concatenate([qkv_ref[:, vcols], other_ref[:, kcols]], axis=0)
        grad = grad_ref[:, cols]
        dqs, dk, dv = [], None, None
        for mask in masks:
            head_query = query * mask
            head_grad = grad * mask
            prob = head_prob(head_query, keys, allowed)
            part_v = dot(prob.astype(bf16), head_grad, 0, 0)
            dprob = dot(head_grad, values, 1, 1)
            dscore = prob * (dprob - jnp.sum(prob * dprob, axis=-1, keepdims=True))
            dscore = dscore.astype(bf16)
            dqs.append(dot(dscore, keys, 1, 0))
            part_k = dot(dscore, head_query, 0, 0)
            dk = part_k if dk is None else dk + part_k
            dv = part_v if dv is None else dv + part_v
        dk = dk * scale
        dq_ref[:, cols] = (jnp.where(first, dqs[0], dqs[1]) * scale).astype(bf16)
        own_ref[:, cols] = dk[:tok]
        own_ref[:, kcols] = dv[:tok]
        send_ref[:, cols] = dk[tok:].astype(bf16)
        send_ref[:, kcols] = dv[tok:].astype(bf16)


SMEM = pl.BlockSpec(memory_space=pltpu.SMEM)
VMEM = pl.BlockSpec(memory_space=pltpu.VMEM)


def attend(block, row_class, lengths, qkv, other):
    tok = qkv.shape[0]
    return pl.pallas_call(
        attend_kernel,
        out_shape=jax.ShapeDtypeStruct((tok, D), bf16),
        in_specs=[SMEM, SMEM, SMEM, VMEM, VMEM],
        out_specs=VMEM,
        compiler_params=pltpu.CompilerParams(vmem_limit_bytes=32 * MIB),
        name="attend",
    )(block, row_class, lengths, qkv, other)


def attend_back(block, row_class, lengths, qkv, other, grad):
    tok = qkv.shape[0]
    return pl.pallas_call(
        attend_back_kernel,
        out_shape=(
            jax.ShapeDtypeStruct((tok, D), bf16),
            jax.ShapeDtypeStruct((tok, 2 * D), f32),
            jax.ShapeDtypeStruct((tok, 2 * D), bf16),
        ),
        in_specs=[SMEM, SMEM, SMEM, VMEM, VMEM, VMEM],
        out_specs=(VMEM, VMEM, VMEM),
        compiler_params=pltpu.CompilerParams(vmem_limit_bytes=32 * MIB),
        name="attend_back",
    )(block, row_class, lengths, qkv, other, grad)


def split_store(value, high_ref, low_ref, rows):
    high = value.astype(bf16)
    high_ref[rows, :] = high
    low_ref[rows, :] = (value - high.astype(f32)).astype(bf16)


def dot3(left_high, left_low, right_high, right_low, rows):
    high = left_high[rows, :]
    total = dot(high, right_high[...], 1, 0)
    total = total + dot(high, right_low[...], 1, 0)
    return total + dot(left_low[rows, :], right_high[...], 1, 0)


TILE = 256


def ortho_kernel(gram_ref, moment_ref, out_ref, a, s, q, t, ah, al, bh, bl, yh, yl, y):
    size = gram_ref.shape[0]
    tiles = size // TILE
    row_id = lax.broadcasted_iota(jnp.int32, (size, size), 0)
    col_id = lax.broadcasted_iota(jnp.int32, (size, size), 1)
    trace = jnp.sum(jnp.where(row_id == col_id, gram_ref[...], 0.0))
    factor = 1.0 / (jnp.sqrt(jnp.full((1, 1), trace, f32)) + 1e-07)

    def each(body):
        def step(i, carry):
            body(pl.ds(pl.multiple_of(i * TILE, TILE), TILE))
            return carry

        lax.fori_loop(0, tiles, step, 0)

    def start(rows):
        value = gram_ref[rows, :] * (factor * factor)
        a[rows, :] = value
        split_store(value, ah, al, rows)
        moment = moment_ref[rows, :] * factor
        y[rows, :] = moment
        split_store(moment, yh, yl, rows)

    each(start)
    for step in range(NS_STEPS):
        last = step + 1 == NS_STEPS

        def square(rows):
            value = dot3(ah, al, ah, al, rows)
            s[rows, :] = value
            q[rows, :] = quintic_b * a[rows, :] + quintic_c * value
            if not last:
                split_store(value, bh, bl, rows)

        each(square)

        if not last:

            def cube(rows):
                value = dot3(bh, bl, ah, al, rows)
                t[rows, :] = quintic_a * a[rows, :] + quintic_b * s[rows, :] + quintic_c * value

            each(cube)

        def keep_poly(rows):
            split_store(q[rows, :], bh, bl, rows)

        each(keep_poly)

        def move(rows):
            value = quintic_a * y[rows, :] + dot3(bh, bl, yh, yl, rows)
            if last:
                out_ref[rows, :] = value.astype(out_ref.dtype)
            else:
                y[rows, :] = value

        each(move)
        if last:
            break

        def keep_y(rows):
            split_store(y[rows, :], yh, yl, rows)
            split_store(t[rows, :], ah, al, rows)

        each(keep_y)

        def advance(rows):
            a[rows, :] = quintic_a * t[rows, :] + dot3(ah, al, bh, bl, rows)

        each(advance)

        def keep_gram(rows):
            split_store(a[rows, :], ah, al, rows)

        each(keep_gram)


def orthogonalize(gram_mat, moment):
    size, cols = moment.shape
    square = pltpu.VMEM((size, size), f32)
    square_low = pltpu.VMEM((size, size), bf16)
    return pl.pallas_call(
        ortho_kernel,
        out_shape=jax.ShapeDtypeStruct((size, cols), bf16),
        in_specs=[VMEM, VMEM],
        out_specs=VMEM,
        scratch_shapes=[
            square,
            square,
            square,
            square,
            square_low,
            square_low,
            square_low,
            square_low,
            pltpu.VMEM((size, cols), bf16),
            pltpu.VMEM((size, cols), bf16),
            pltpu.VMEM((size, cols), f32),
        ],
        compiler_params=pltpu.CompilerParams(vmem_limit_bytes=48 * MIB),
        name="ortho",
    )(gram_mat, moment)


def swap(value, axis, bit):
    size = lax.axis_size(axis)
    return lax.ppermute(value, axis, [(i, i ^ bit) for i in range(size)])


def scatter_head(value, bit, position):
    half = value.shape[1] // 2
    mine = lax.dynamic_slice_in_dim(value, position * half, half, 1)
    other = lax.dynamic_slice_in_dim(value, (1 - position) * half, half, 1)
    return (mine.astype(f32) + swap(other, "head", bit).astype(f32)).astype(bf16)


def scatter_dp_pair(value, position):
    paired = value.reshape((value.shape[0] // 2, 2) + value.shape[1:])
    mine = lax.dynamic_index_in_dim(paired, position, 1, False)
    other = lax.dynamic_index_in_dim(paired, 1 - position, 1, False)
    return (mine.astype(f32) + swap(other, "dp", 1).astype(f32)).astype(bf16)


def scatter_dp_rest(value, place):
    ranks = value.shape[0]
    total = lax.dynamic_index_in_dim(value, place, 0, False).astype(f32)
    for step in range(1, ranks):
        sent = lax.dynamic_index_in_dim(value, place ^ step, 0, False)
        total = total + swap(sent, "dp", 2 * step).astype(f32)
    return total


def local(
    tokens,
    cotangent,
    qkv_weight,
    out_weight,
    up_weight,
    down_weight,
    vectors,
    qkv_moment,
    out_moment,
    up_moment,
    down_moment,
    adam_first,
    adam_second,
    bucket_class,
    row_lengths,
):
    n_dp = lax.axis_size("dp")
    n_head = lax.axis_size("head")
    dp_id = lax.axis_index("dp")
    head_id = lax.axis_index("head")
    core, side = head_id % 2, head_id // 2
    tok, width = tokens.shape
    hidden = up_weight.shape[1]
    half = width // 2
    pieces = split_vectors(vectors, width, hidden)
    bias_query, bias_value, bias_out, gain_one, shift_one = pieces[:5]
    bias_up, bias_down, gain_two, shift_two = pieces[5:]
    bias_qkv = jnp.concatenate([bias_query, jnp.zeros_like(bias_query), bias_value])

    def column_half(value, which):
        return lax.dynamic_slice_in_dim(value, which * half, half, 1)

    def both_halves(value):
        return jnp.concatenate(
            [column_half(value, core), swap(column_half(value, 1 - core), "head", 1)], axis=0
        )

    def both(value):
        return jnp.concatenate([value, swap(value, "head", 1)], axis=0)

    qkv = (dot(tokens, qkv_weight, 1, 0) + bias_qkv).astype(bf16)
    other = swap(qkv[:, width:], "head", 1)
    block = head_id.astype(jnp.int32)[None]
    attended = attend(block, bucket_class, row_lengths, qkv, other)
    attn_val = dot(attended, out_weight, 1, 0) + bias_out
    resid_one = tokens.astype(f32) + attn_val
    centre = resid_one - jnp.mean(resid_one, axis=-1, keepdims=True)
    rstd_one = lax.rsqrt(jnp.mean(centre * centre, axis=-1, keepdims=True) + norm_eps)
    zhat_one = centre * rstd_one
    normed_one = zhat_one * gain_one + shift_one
    normed_low = normed_one.astype(bf16)
    up_val = dot(normed_low, up_weight, 1, 0) + bias_up
    phi_cum = 0.5 * (1.0 + lax.erf(up_val * (0.5**0.5)))
    active_low = (up_val * phi_cum).astype(bf16)
    slope = phi_cum + up_val * jnp.exp(-0.5 * up_val * up_val) * (1.0 / math.sqrt(2.0 * math.pi))
    down_val = dot(active_low, down_weight, 1, 0) + bias_down
    resid_two = normed_one + down_val
    centre = resid_two - jnp.mean(resid_two, axis=-1, keepdims=True)
    rstd_two = lax.rsqrt(jnp.mean(centre * centre, axis=-1, keepdims=True) + norm_eps)
    zhat_two = centre * rstd_two
    mixed = zhat_two * gain_two + shift_two

    def norm_back(grad, gain, zhat, rstd):
        inner = grad * gain
        mean = jnp.mean(inner, axis=-1, keepdims=True)
        slant = jnp.mean(inner * zhat, axis=-1, keepdims=True)
        return (inner - mean - zhat * slant) * rstd, jnp.sum(grad * zhat, axis=0), jnp.sum(grad, axis=0)

    grad_two, grad_gain_two, grad_shift_two = norm_back(
        cotangent.astype(f32), gain_two, zhat_two, rstd_two
    )
    grad_down_low = grad_two.astype(bf16)
    grad_bias_down = jnp.sum(grad_down_low, axis=0, dtype=f32)

    def weight_grad(wide, narrow):
        value = dot(wide, narrow, 0, 0).astype(bf16)
        return value.reshape(n_dp, value.shape[0] // n_dp, half)

    x_id, z_id = dp_id % 2, dp_id // 2

    def reduce_y_first(value):
        return scatter_dp_rest(scatter_dp_pair(scatter_head(value, 2, side), x_id), z_id)

    def reduce_x_first(value):
        return scatter_dp_rest(scatter_head(scatter_dp_pair(value, x_id), 2, side), z_id)

    def spread(value):
        value = value.astype(bf16)
        came = swap(value, "head", 2)
        value = jnp.concatenate(
            [jnp.where(side == 0, value, came), jnp.where(side == 0, came, value)], axis=0
        )
        came = swap(value, "head", 1)
        return jnp.concatenate(
            [jnp.where(core == 0, value, came), jnp.where(core == 0, came, value)], axis=1
        ).astype(f32)

    down_sum = reduce_x_first(weight_grad(both(active_low), both_halves(grad_down_low)))
    grad_up_low = (dot(grad_down_low, down_weight, 1, 1) * slope).astype(bf16)
    grad_bias_up = jnp.sum(grad_up_low, axis=0, dtype=f32)
    up_sum = reduce_y_first(weight_grad(both(grad_up_low), both_halves(normed_low)))
    grad_normed = grad_two + dot(grad_up_low, up_weight, 1, 1)
    grad_one, grad_gain_one, grad_shift_one = norm_back(grad_normed, gain_one, zhat_one, rstd_one)
    grad_attn_low = grad_one.astype(bf16)
    grad_bias_out = jnp.sum(grad_attn_low, axis=0, dtype=f32)
    out_part = weight_grad(both(grad_attn_low), both_halves(attended))
    grad_heads = dot(grad_attn_low, out_weight, 1, 1).astype(bf16)
    grad_query, own, sent = attend_back(block, bucket_class, row_lengths, qkv, other, grad_heads)
    grad_kv = (own + swap(sent, "head", 1).astype(f32)).astype(bf16)
    grad_qkv = jnp.concatenate([grad_query, grad_kv], axis=1)
    grad_bias_qkv = jnp.sum(grad_qkv, axis=0, dtype=f32)
    input_grad = grad_one + dot(grad_qkv, qkv_weight, 1, 1)
    qkv_part = weight_grad(both(grad_qkv), both_halves(tokens))

    grad_vector = jnp.concatenate(
        [
            grad_bias_qkv[:width],
            grad_bias_qkv[2 * width :],
            grad_bias_out,
            grad_gain_one,
            grad_shift_one,
            grad_bias_up,
            grad_bias_down,
            grad_gain_two,
            grad_shift_two,
        ]
    )
    grad_vector = grad_vector + swap(grad_vector, "head", 1)
    vec_len = grad_vector.shape[0] // n_dp
    vec_rows = 16
    vec_part = grad_vector.reshape(n_dp, vec_len)
    vec_part = jnp.pad(vec_part, ((0, 0), (0, vec_rows * width - vec_len)))
    vec_part = vec_part.reshape(n_dp, vec_rows, width)
    vec_part = lax.dynamic_slice_in_dim(vec_part, core * half, half, 2).astype(bf16)
    tail = jnp.concatenate([qkv_part, out_part, vec_part], axis=1)
    qkv_cols, out_cols = qkv_part.shape[1], out_part.shape[1]
    tail_sum = reduce_y_first(tail)

    down_new = spread(down_sum)
    up_new = spread(up_sum)
    tail_new = spread(tail_sum)
    grads = [
        tail_new[:qkv_cols].T,
        tail_new[qkv_cols : qkv_cols + out_cols].T,
        up_new.T,
        down_new.T,
    ]
    grad_vec = tail_new[qkv_cols + out_cols :].reshape(-1)[:vec_len]
    moments = [
        muon_keep * old + grad
        for old, grad in zip([qkv_moment, out_moment, up_moment, down_moment], grads)
    ]
    most = max(m.shape[1] for m in moments)
    padded = [jnp.pad(m, ((0, 0), (0, most - m.shape[1]))) for m in moments]
    chosen = padded[-1]
    for index in range(len(padded) - 2, -1, -1):
        chosen = jnp.where(head_id == index, padded[index], chosen)
    gram_mat = lax.psum(
        lax.dot_general(
            chosen, chosen, (((1,), (1,)), ((), ())), precision=lax.Precision.HIGH
        ),
        "dp",
    )
    ortho_own = orthogonalize(gram_mat, chosen)
    across = swap(ortho_own, "head", 2)
    low_pair = jnp.where(side == 0, ortho_own, across)
    high_pair = jnp.where(side == 0, across, ortho_own)
    near_low = swap(low_pair, "head", 1)
    near_high = swap(high_pair, "head", 1)
    ortho = [
        jnp.where(core == 0, low_pair, near_low),
        jnp.where(core == 0, near_low, low_pair),
        jnp.where(core == 0, high_pair, near_high),
        jnp.where(core == 0, near_high, high_pair),
    ]
    ortho = [o[:, : m.shape[1]].astype(f32) for o, m in zip(ortho, moments)]

    shrink = 1.0 - muon_rate * muon_decay

    def weight_block(weight, cols, dim):
        return lax.dynamic_slice_in_dim(weight, dp_id * cols, cols, dim).astype(f32) * shrink

    up_cols, down_rows = moments[2].shape[1], moments[3].shape[1]
    new_qkv = weight_block(qkv_weight, qkv_cols, 1) - muon_rate * math.sqrt(3.0) * ortho[0]
    new_out = weight_block(out_weight, out_cols, 1) - muon_rate * ortho[1]
    new_up = (
        weight_block(up_weight, up_cols, 1)
        - muon_rate * math.sqrt(max(1.0, hidden / width)) * ortho[2]
    )
    new_down = weight_block(down_weight, down_rows, 0) - muon_rate * ortho[3].T
    vec_old = lax.dynamic_slice_in_dim(vectors, dp_id * vec_len, vec_len, 0)
    vec_first = beta_first * adam_first + (1.0 - beta_first) * grad_vec
    vec_second = beta_second * adam_second + (1.0 - beta_second) * grad_vec * grad_vec
    first_hat = vec_first / (1.0 - beta_first**STEP)
    second_hat = vec_second / (1.0 - beta_second**STEP)
    vec_new = vec_old - adam_rate * first_hat / (jnp.sqrt(second_hat) + adam_eps)
    return (
        mixed,
        input_grad,
        moments[0],
        moments[1],
        moments[2],
        moments[3],
        new_qkv,
        new_out,
        new_up,
        new_down,
        vec_first,
        vec_second,
        vec_new,
    )


def solution(mesh):
    tokens_spec = P(("dp", "head"), None)
    block_spec = P(None, "dp")
    return jax.shard_map(
        local,
        mesh=mesh,
        in_specs=(
            tokens_spec,
            tokens_spec,
            P(),
            P(),
            P(),
            P(),
            P(),
            block_spec,
            block_spec,
            block_spec,
            block_spec,
            P("dp"),
            P("dp"),
            P("dp"),
            P("dp", None),
        ),
        out_specs=(
            tokens_spec,
            tokens_spec,
            block_spec,
            block_spec,
            block_spec,
            block_spec,
            block_spec,
            block_spec,
            block_spec,
            P("dp", None),
            P("dp"),
            P("dp"),
            P("dp"),
        ),
        check_vma=False,
    )
```

```python
import functools
import math

import jax
import jax.numpy as jnp
from jax import lax
from jax.experimental import pallas as pl
from jax.experimental.pallas import tpu as pltpu
from jax.sharding import PartitionSpec as P

D = 768
HEADS = 12
HEAD_DIM = 64
FF = 3072
BASE_LEN = 128
NS_STEPS = 5
STEP = 5
MAX_LEN = 512

f32 = jnp.float32
bf16 = jnp.bfloat16

norm_eps = 1e-12
masked_score = -1000000000.0
quintic_a = 3.4445
quintic_b = -4.775
quintic_c = 2.0315
muon_rate = 1.0
muon_decay = 0.01
muon_keep = 0.5
adam_rate = 0.2
beta_first = 0.9
beta_second = 0.999
adam_eps = 1e-08
MIB = 1024 * 1024


def dot(left, right, left_dim, right_dim):
    return lax.dot_general(
        left, right, (((left_dim,), (right_dim,)), ((), ())), preferred_element_type=f32
    )


def split_vectors(vectors, width, hidden):
    lengths_list = [width] * 5 + [hidden] + [width] * 3
    pieces = []
    offset = 0
    for length in lengths_list:
        pieces.append(vectors[offset : offset + length])
        offset = offset + length
    return pieces


def allowed_mask(class_ref, length_ref, block, tok):
    shift = class_ref[0] + int(math.log2(BASE_LEN))
    query_place = block * tok + lax.broadcasted_iota(jnp.int32, (tok, 1), 0)
    lane = lax.broadcasted_iota(jnp.int32, (1, 2 * tok), 1)
    own = lane < tok
    key_place = jnp.where(own, block * tok + lane, (block ^ 1) * tok + lane - tok)
    key_row = lax.shift_right_logical(key_place, jnp.broadcast_to(shift, key_place.shape))
    offset = key_place - lax.shift_left(key_row, jnp.broadcast_to(shift, key_place.shape))
    row_len = jnp.zeros_like(key_row)
    for slot in range(length_ref.shape[1]):
        row_len = jnp.where(key_row == slot, length_ref[0, slot], row_len)
    key_row = jnp.where(offset < row_len, key_row, -1)
    query_row = lax.shift_right_logical(query_place, jnp.broadcast_to(shift, query_place.shape))
    return query_row == key_row


def half_masks():
    lane = lax.broadcasted_iota(jnp.int32, (1, 2 * HEAD_DIM), 1)
    first = (lane < HEAD_DIM).astype(f32)
    return (first.astype(bf16), (1.0 - first).astype(bf16)), lane < HEAD_DIM


def head_prob(query, keys, allowed):
    score = jnp.where(allowed, dot(query, keys, 1, 1) * HEAD_DIM ** (-0.5), masked_score)
    exponent = jnp.exp(score - jnp.max(score, axis=-1, keepdims=True))
    return exponent / jnp.sum(exponent, axis=-1, keepdims=True)


def attend_kernel(block_ref, class_ref, length_ref, qkv_ref, other_ref, out_ref):
    tok = qkv_ref.shape[0]
    allowed = allowed_mask(class_ref, length_ref, block_ref[0], tok)
    masks, first = half_masks()
    for pair in range(HEADS // 2):
        cols = pl.ds(pair * 2 * HEAD_DIM, 2 * HEAD_DIM)
        kcols = pl.ds(D + pair * 2 * HEAD_DIM, 2 * HEAD_DIM)
        vcols = pl.ds(2 * D + pair * 2 * HEAD_DIM, 2 * HEAD_DIM)
        query = qkv_ref[:, cols]
        keys = jnp.concatenate([qkv_ref[:, kcols], other_ref[:, cols]], axis=0)
        values = jnp.concatenate([qkv_ref[:, vcols], other_ref[:, kcols]], axis=0)
        outs = []
        for mask in masks:
            prob = head_prob(query * mask, keys, allowed)
            outs.append(dot(prob.astype(bf16), values, 1, 0))
        out_ref[:, cols] = jnp.where(first, outs[0], outs[1]).astype(bf16)


def attend_back_kernel(
    block_ref, class_ref, length_ref, qkv_ref, other_ref, grad_ref, dq_ref, own_ref, send_ref
):
    tok = qkv_ref.shape[0]
    allowed = allowed_mask(class_ref, length_ref, block_ref[0], tok)
    masks, first = half_masks()
    scale = HEAD_DIM ** (-0.5)
    for pair in range(HEADS // 2):
        cols = pl.ds(pair * 2 * HEAD_DIM, 2 * HEAD_DIM)
        kcols = pl.ds(D + pair * 2 * HEAD_DIM, 2 * HEAD_DIM)
        vcols = pl.ds(2 * D + pair * 2 * HEAD_DIM, 2 * HEAD_DIM)
        query = qkv_ref[:, cols]
        keys = jnp.concatenate([qkv_ref[:, kcols], other_ref[:, cols]], axis=0)
        values = jnp.concatenate([qkv_ref[:, vcols], other_ref[:, kcols]], axis=0)
        grad = grad_ref[:, cols]
        dqs, dk, dv = [], None, None
        for mask in masks:
            head_query = query * mask
            head_grad = grad * mask
            prob = head_prob(head_query, keys, allowed)
            part_v = dot(prob.astype(bf16), head_grad, 0, 0)
            dprob = dot(head_grad, values, 1, 1)
            dscore = prob * (dprob - jnp.sum(prob * dprob, axis=-1, keepdims=True))
            dscore = dscore.astype(bf16)
            dqs.append(dot(dscore, keys, 1, 0))
            part_k = dot(dscore, head_query, 0, 0)
            dk = part_k if dk is None else dk + part_k
            dv = part_v if dv is None else dv + part_v
        dk = dk * scale
        dq_ref[:, cols] = (jnp.where(first, dqs[0], dqs[1]) * scale).astype(bf16)
        own_ref[:, cols] = dk[:tok]
        own_ref[:, kcols] = dv[:tok]
        send_ref[:, cols] = dk[tok:].astype(bf16)
        send_ref[:, kcols] = dv[tok:].astype(bf16)


SMEM = pl.BlockSpec(memory_space=pltpu.SMEM)
VMEM = pl.BlockSpec(memory_space=pltpu.VMEM)


def attend(block, row_class, lengths, qkv, other):
    tok = qkv.shape[0]
    return pl.pallas_call(
        attend_kernel,
        out_shape=jax.ShapeDtypeStruct((tok, D), bf16),
        in_specs=[SMEM, SMEM, SMEM, VMEM, VMEM],
        out_specs=VMEM,
        compiler_params=pltpu.CompilerParams(vmem_limit_bytes=32 * MIB),
        name="attend",
    )(block, row_class, lengths, qkv, other)


def attend_back(block, row_class, lengths, qkv, other, grad):
    tok = qkv.shape[0]
    return pl.pallas_call(
        attend_back_kernel,
        out_shape=(
            jax.ShapeDtypeStruct((tok, D), bf16),
            jax.ShapeDtypeStruct((tok, 2 * D), f32),
            jax.ShapeDtypeStruct((tok, 2 * D), bf16),
        ),
        in_specs=[SMEM, SMEM, SMEM, VMEM, VMEM, VMEM],
        out_specs=(VMEM, VMEM, VMEM),
        compiler_params=pltpu.CompilerParams(vmem_limit_bytes=32 * MIB),
        name="attend_back",
    )(block, row_class, lengths, qkv, other, grad)


CENTRES = (0.0, 0.0, 0.0, 0.8, 0.8)
TILE = 256
SUB = 128


def sub_blocks(size):
    count = size // SUB
    return [(i, j) for i in range(count) for j in range(i, count)]


def ortho_kernel(packed, gram_ref, moment_ref, out_ref, e, f, g, eb, fb, gb, ya, yb, y):
    size = e.shape[0]
    tiles = [slice(i * TILE, (i + 1) * TILE) for i in range(size // TILE)]

    def unit(rows):
        row_id = rows.start + lax.broadcasted_iota(jnp.int32, (TILE, size), 0)
        col_id = lax.broadcasted_iota(jnp.int32, (TILE, size), 1)
        return (row_id == col_id).astype(f32)

    if packed:
        for index, (i, j) in enumerate(sub_blocks(size)):
            value = gram_ref[:, index].reshape(SUB, SUB)
            e[i * SUB : (i + 1) * SUB, j * SUB : (j + 1) * SUB] = value
            if i != j:
                e[j * SUB : (j + 1) * SUB, i * SUB : (i + 1) * SUB] = value.T
        gram = e
    else:
        gram = gram_ref
    diagonal = jnp.zeros((TILE, size), f32)
    for rows in tiles:
        diagonal = diagonal + gram[rows, :] * unit(rows)
    trace = jnp.sum(jnp.sum(diagonal, axis=0, keepdims=True), axis=1, keepdims=True)
    factor = 1.0 / (jnp.sqrt(trace) + 1e-07)
    square_factor = factor * factor
    for rows in tiles:
        value = gram[rows, :] * square_factor
        e[rows, :] = value
        eb[rows, :] = value.astype(bf16)
        moment = moment_ref[rows, :] * factor
        y[rows, :] = moment
        ya[rows, :] = moment.astype(bf16)
    now, then = ya, yb
    for step in range(NS_STEPS):
        last = step + 1 == NS_STEPS
        centre = CENTRES[step]
        after = 0.0 if last else CENTRES[step + 1]
        keep = quintic_a + quintic_b * centre + quintic_c * centre * centre
        linear = quintic_b + 2.0 * quintic_c * centre
        for rows in tiles:
            value = linear * e[rows, :] + quintic_c * dot(eb[rows, :], eb[...], 1, 0)
            fb[rows, :] = value.astype(bf16)
            if not last:
                f[rows, :] = value
        for rows in tiles:
            value = keep * y[rows, :] + dot(fb[rows, :], now[...], 1, 0)
            if last:
                out_ref[rows, :] = value.astype(out_ref.dtype)
            else:
                y[rows, :] = value
                then[rows, :] = value.astype(bf16)
        if last:
            break
        now, then = then, now
        for rows in tiles:
            value = keep * e[rows, :] + dot(eb[rows, :], fb[...], 1, 0)
            if centre:
                value = value + centre * f[rows, :]
            g[rows, :] = value
            gb[rows, :] = value.astype(bf16)
        for rows in tiles:
            value = keep * g[rows, :] + dot(gb[rows, :], fb[...], 1, 0)
            if centre:
                value = value + (centre * keep) * f[rows, :]
            shift = centre * keep * keep - after
            if shift:
                value = value + shift * unit(rows)
            e[rows, :] = value
            eb[rows, :] = value.astype(bf16)


def orthogonalize(gram_mat, moment):
    size, cols = moment.shape
    square = pltpu.VMEM((size, size), f32)
    square_low = pltpu.VMEM((size, size), bf16)
    return pl.pallas_call(
        functools.partial(ortho_kernel, gram_mat.ndim != 2),
        out_shape=jax.ShapeDtypeStruct((size, cols), bf16),
        in_specs=[VMEM, VMEM],
        out_specs=VMEM,
        scratch_shapes=[
            square,
            square,
            square,
            square_low,
            square_low,
            square_low,
            pltpu.VMEM((size, cols), bf16),
            pltpu.VMEM((size, cols), bf16),
            pltpu.VMEM((size, cols), f32),
        ],
        compiler_params=pltpu.CompilerParams(vmem_limit_bytes=48 * MIB),
        name="ortho",
    )(gram_mat, moment)


MESH = pl.DeviceIdType.MESH
CHUNK = 48
PARTS = 4
UNIT = 2 * PARTS * CHUNK
VEC_ROWS = 16
VEC_COLS = 128


def position():
    dp_id, head_id = lax.axis_index("dp"), lax.axis_index("head")
    z, x = dp_id // 2, dp_id % 2
    y, core = head_id // 2, head_id % 2
    return z, x, y, core


def device(z, x, y, core):
    return (2 * z + x, 2 * y + core)


def flip_z(z, step):
    high, low = z // 2, z % 2
    high = 1 - high if step // 2 else high
    low = 1 - low if step % 2 else low
    return 2 * high + low


def greet(others):
    barrier = pltpu.get_barrier_semaphore()
    for other in others:
        pl.semaphore_signal(barrier, inc=1, device_id=other, device_id_type=MESH)
    pl.semaphore_wait(barrier, len(others))


def reduce_kernel(
    active,
    active_far,
    grad_up,
    grad_up_far,
    grad_attn,
    grad_attn_far,
    grad_qkv,
    grad_qkv_far,
    grad_down,
    grad_down_far,
    normed,
    normed_far,
    attended,
    attended_far,
    tokens,
    tokens_far,
    vec_in,
    out,
    out_vec,
    part,
    vec_part,
    came_one,
    came_two,
    came_three,
    vec_one,
    vec_two,
    vec_three,
    send_sem,
    recv_sem,
):
    z, x, y, core = position()
    beyond = device(z, x, 1 - y, core)
    beside = device(z, 1 - x, y, core)
    partner = device(z, x, y, 1 - core)
    along = [device(flip_z(z, step), x, y, core) for step in (1, 2, 3)]
    greet([beyond, beside, partner] + along)
    started = []

    def send(source, target, chunk, slot, other):
        copy = pltpu.make_async_remote_copy(
            src_ref=source,
            dst_ref=target,
            send_sem=send_sem.at[chunk, slot],
            recv_sem=recv_sem.at[chunk, slot],
            device_id=other,
            device_id_type=MESH,
        )
        copy.start()
        started.append(copy)
        return copy

    class Chain:
        def __init__(self, index, y_first, own, one, two, three, final):
            self.index, self.y_first = index, y_first
            self.own, self.one, self.two, self.three, self.final = own, one, two, three, final

        def first(self):
            if self.y_first:
                source, other = self.own.at[:, :, 1 - y], beyond
            else:
                source, other = self.own.at[:, 1 - x], beside
            self.copy = send(source, self.one, self.index, 0, other)

        def second(self):
            self.copy.wait_recv()
            for i in range(4):
                for j in range(2):
                    at = (i, j, y) if self.y_first else (i, x, j)
                    self.own[at] = self.own[at] + self.one[i, j]
            if self.y_first:
                source, other = self.own.at[:, 1 - x, y], beside
            else:
                source, other = self.own.at[:, x, 1 - y], beyond
            self.copy = send(source, self.two, self.index, 1, other)

        def third(self):
            self.copy.wait_recv()
            for i in range(4):
                self.own[i, x, y] = self.own[i, x, y] + self.two[i]
            self.copies = [
                send(
                    self.own.at[flip_z(z, step), x, y],
                    self.three.at[step - 1],
                    self.index,
                    1 + step,
                    along[step - 1],
                )
                for step in (1, 2, 3)
            ]

        def fourth(self):
            total = self.own[z, x, y].astype(f32)
            for step, copy in enumerate(self.copies):
                copy.wait_recv()
                total = total + self.three[step].astype(f32)
            self.final[core, y] = total.astype(bf16)
            self.copy = send(
                self.final.at[core, y], self.final.at[core, y], self.index, 5, beyond
            )

        def fifth(self):
            self.copy.wait_recv()
            self.copy = send(self.final.at[core], self.final.at[core], self.index, 6, partner)

        def sixth(self):
            self.copy.wait_recv()

    def chain(matrix, quarter, y_first):
        return Chain(
            matrix * PARTS + quarter,
            y_first,
            part.at[matrix, quarter],
            came_one.at[matrix, quarter],
            came_two.at[matrix, quarter],
            came_three.at[matrix, quarter],
            out.at[matrix, :, :, quarter],
        )

    def feed_forward(matrix, narrow, narrow_far, wide, wide_far):
        left = narrow[...].astype(f32).T.astype(bf16)
        left_far = narrow_far[...].astype(f32).T.astype(bf16)

        def block(index, carry):
            cols = pl.ds(pl.multiple_of(index * UNIT, UNIT), UNIT)
            value = dot(left, wide[:, cols], 1, 0) + dot(left_far, wide_far[:, cols], 1, 0)
            value = value.astype(bf16)
            for side in range(2):
                for quarter in range(PARTS):
                    start = (side * PARTS + quarter) * CHUNK
                    part[matrix, quarter, index // 2, index % 2, side] = value[
                        start : start + CHUNK
                    ]
            return carry

        lax.fori_loop(0, 8, block, 0)

    def projections(matrix, wide, wide_far, narrow, narrow_far, width, offset):
        for tile in range(wide.shape[1] // UNIT):
            cols = slice(tile * UNIT, (tile + 1) * UNIT)
            value = dot(wide[:, cols], narrow[...], 0, 0)
            value = value + dot(wide_far[:, cols], narrow_far[...], 0, 0)
            value = value.astype(bf16)
            for start in range(0, UNIT, CHUNK):
                block, row = divmod(tile * UNIT + start, width)
                side, row = divmod(offset + row, PARTS * CHUNK)
                part[matrix, row // CHUNK, block // 2, block % 2, side] = value[
                    start : start + CHUNK
                ]

    y_first = [chain(0, quarter, True) for quarter in range(4)] + [chain(2, 0, True)]
    x_first = [chain(1, quarter, False) for quarter in range(4)]
    x_first += [chain(2, quarter, False) for quarter in (1, 2, 3)]
    vec_part[...] = vec_in[...]
    y_first.append(Chain(3 * PARTS, True, vec_part, vec_one, vec_two, vec_three, out_vec))

    feed_forward(0, normed, normed_far, grad_up, grad_up_far)
    y_first[0].first()
    y_first[1].first()
    feed_forward(1, grad_down, grad_down_far, active, active_far)
    x_first[0].first()
    x_first[1].first()
    projections(2, grad_qkv, grad_qkv_far, tokens, tokens_far, 3 * D // 8, 0)
    projections(2, grad_attn, grad_attn_far, attended, attended_far, D // 8, 3 * D // 8)
    chains = (y_first, x_first)
    for turn in range(max(map(len, chains)) + 4):
        for line in chains:
            if turn + 2 < len(line):
                line[turn + 2].first()
        for behind, stage in enumerate(("second", "third", "fourth", "fifth", "sixth")):
            for line in chains:
                if 0 <= turn - behind < len(line):
                    getattr(line[turn - behind], stage)()
    for copy in started:
        copy.wait_send()


def reduce_gradients(wides, narrows, vec):
    block = (4, 2, 2, CHUNK, UNIT)
    vec_block = (VEC_ROWS, VEC_COLS)
    return pl.pallas_call(
        reduce_kernel,
        out_shape=(
            jax.ShapeDtypeStruct((3, 2, 2, PARTS, CHUNK, UNIT), bf16),
            jax.ShapeDtypeStruct((2, 2) + vec_block, bf16),
        ),
        in_specs=[VMEM] * 17,
        out_specs=(VMEM, VMEM),
        scratch_shapes=[
            pltpu.VMEM((3, PARTS) + block, bf16),
            pltpu.VMEM((4, 2, 2) + vec_block, bf16),
            pltpu.VMEM((3, PARTS, 4, 2, CHUNK, UNIT), bf16),
            pltpu.VMEM((3, PARTS, 4, CHUNK, UNIT), bf16),
            pltpu.VMEM((3, PARTS, 3, CHUNK, UNIT), bf16),
            pltpu.VMEM((4, 2) + vec_block, bf16),
            pltpu.VMEM((4,) + vec_block, bf16),
            pltpu.VMEM((3,) + vec_block, bf16),
            pltpu.SemaphoreType.DMA((3 * PARTS + 1, 7)),
            pltpu.SemaphoreType.DMA((3 * PARTS + 1, 7)),
        ],
        compiler_params=pltpu.CompilerParams(
            vmem_limit_bytes=52 * MIB, collective_id=0, has_side_effects=True
        ),
        name="reduce_gradients",
    )(*wides, *narrows, vec)


def update_kernel(head_ref, sums, tail_old, up_old, down_old, qkv_new, out_new, up_new, down_new, chosen):
    head_id = head_ref[0]
    half = D // 2
    qkv_cols = qkv_new.shape[1]

    up_new[...] = muon_keep * up_old[...] + sums[0].astype(f32)
    down_new[...] = muon_keep * down_old[...] + sums[1].astype(f32)
    tail = jnp.concatenate(
        [sums[2, :half].astype(f32).T, sums[2, half:].astype(f32).T], axis=0
    )
    tail = muon_keep * tail_old[...] + tail
    qkv_new[...] = tail[:, :qkv_cols]
    out_new[...] = tail[:, qkv_cols:]
    in_qkv = lax.broadcasted_iota(jnp.int32, tail.shape, 1) < qkv_cols

    @pl.when(head_id == 0)
    def _():
        chosen[...] = jnp.where(in_qkv, tail, 0.0)

    @pl.when(head_id == 1)
    def _():
        chosen[...] = jnp.where(in_qkv, 0.0, tail)

    @pl.when(head_id == 2)
    def _():
        chosen[...] = up_new[...]

    @pl.when(head_id == 3)
    def _():
        chosen[...] = down_new[...]


def update_moments(head, sums, tail_old, up_old, down_old, qkv_cols):
    rows, cols = tail_old.shape

    def shape(width):
        return jax.ShapeDtypeStruct((rows, width), f32)

    return pl.pallas_call(
        update_kernel,
        out_shape=(shape(qkv_cols), shape(cols - qkv_cols), shape(cols), shape(cols), shape(cols)),
        in_specs=[SMEM, VMEM, VMEM, VMEM, VMEM],
        out_specs=(VMEM,) * 5,
        compiler_params=pltpu.CompilerParams(vmem_limit_bytes=40 * MIB),
        name="update_moments",
    )(head, sums, tail_old, up_old, down_old)


GROUP = 3
GRAM_AXES = ("far", "near", "x")


def gram_kernel(moment, out, part, came_one, came_two, came_three, high, low, send_sem, recv_sem):
    z, x, y, core = position()
    here = {"far": z // 2, "near": z % 2, "x": x}
    others = {
        "far": device(flip_z(z, 2), x, y, core),
        "near": device(flip_z(z, 1), x, y, core),
        "x": device(z, 1 - x, y, core),
    }
    greet(list(others.values()))
    blocks = sub_blocks(moment.shape[0])
    groups = len(blocks) // GROUP
    high[...] = moment[...].astype(bf16)
    low[...] = (moment[...] - high[...].astype(f32)).astype(bf16)
    started = []

    def product(index):
        i, j = blocks[index]
        left, right = pl.ds(i * SUB, SUB), pl.ds(j * SUB, SUB)
        total = dot(high[left, :], high[right, :], 1, 1)
        total = total + dot(high[left, :], low[right, :], 1, 1)
        total = total + dot(low[left, :], high[right, :], 1, 1)
        rows = SUB // 8
        for owner in range(8):
            cell = (owner // 4, owner // 2 % 2, owner % 2)
            part[(index // GROUP,) + cell + (index % GROUP,)] = total[
                owner * rows : (owner + 1) * rows
            ]

    def send(source, target, group, slot, axis):
        copy = pltpu.make_async_remote_copy(
            src_ref=source,
            dst_ref=target,
            send_sem=send_sem.at[group, slot],
            recv_sem=recv_sem.at[group, slot],
            device_id=others[axis],
            device_id_type=MESH,
        )
        copy.start()
        started.append(copy)
        return copy

    def cells(fixed, flipped=None):
        return tuple(
            1 - here[name] if name == flipped else here[name] if name in fixed else slice(None)
            for name in GRAM_AXES
        )

    class Walk:
        def __init__(self, group, order):
            self.group, self.order, self.stage = group, order, 0
            self.part = part.at[group]
            self.came = (came_one.at[group], came_two.at[group], came_three.at[group])

        def advance(self):
            stage, order = self.stage, self.order
            mine = pl.ds(self.group * GROUP, GROUP)
            if stage:
                self.copy.wait_recv()
            if 1 <= stage <= 3:
                kept = cells(order[:stage])
                total = self.part[kept] + self.came[stage - 1][...]
                if stage == 3:
                    out[kept + (mine,)] = total
                else:
                    self.part[kept] = total
            if stage < 3:
                source = self.part.at[cells(order[:stage], order[stage])]
                self.copy = send(source, self.came[stage], self.group, stage, order[stage])
            elif stage < 6:
                block = out.at[cells(order[: 6 - stage]) + (mine,)]
                self.copy = send(block, block, self.group, stage, order[5 - stage])
            self.stage += 1

    walks = []
    for group in range(groups):
        for index in range(group * GROUP, (group + 1) * GROUP):
            product(index)
        order = ("near", "far", "x") if group == 1 else ("x", "near", "far")
        walks.append(Walk(group, order))
        walks[-1].advance()
    for turn in range(groups + 5):
        for group, walk in enumerate(walks):
            if 0 <= turn - group < 6:
                walk.advance()
    for copy in started:
        copy.wait_send()


def gram_sum(moment):
    size, cols = moment.shape
    count = len(sub_blocks(size))
    groups = count // GROUP
    rows = (SUB // 8, SUB)
    return pl.pallas_call(
        gram_kernel,
        out_shape=jax.ShapeDtypeStruct((2, 2, 2, count) + rows, f32),
        in_specs=[VMEM],
        out_specs=VMEM,
        scratch_shapes=[
            pltpu.VMEM((groups, 2, 2, 2, GROUP) + rows, f32),
            pltpu.VMEM((groups, 2, 2, GROUP) + rows, f32),
            pltpu.VMEM((groups, 2, GROUP) + rows, f32),
            pltpu.VMEM((groups, GROUP) + rows, f32),
            pltpu.VMEM((size, cols), bf16),
            pltpu.VMEM((size, cols), bf16),
            pltpu.SemaphoreType.DMA((groups, 6)),
            pltpu.SemaphoreType.DMA((groups, 6)),
        ],
        compiler_params=pltpu.CompilerParams(
            vmem_limit_bytes=32 * MIB, collective_id=1, has_side_effects=True
        ),
        name="gram_sum",
    )(moment).reshape((8, count) + rows)


STRIPS = 2


def share_kernel(mine, out, send_sem, recv_sem):
    z, x, y, core = position()
    beyond = device(z, x, 1 - y, core)
    partner = device(z, x, y, 1 - core)
    greet([beyond, partner])
    own = 2 * y + core
    far = 2 * (1 - y) + core
    out[own] = mine[...]
    rows = mine.shape[0] // STRIPS
    started = []

    def send(slot, strip, kind, other):
        block = out.at[slot, pl.ds(strip * rows, rows)]
        copy = pltpu.make_async_remote_copy(
            src_ref=block,
            dst_ref=block,
            send_sem=send_sem.at[strip, kind],
            recv_sem=recv_sem.at[strip, kind],
            device_id=other,
            device_id_type=MESH,
        )
        copy.start()
        started.append(copy)
        return copy

    across = [send(own, strip, 0, beyond) for strip in range(STRIPS)]
    late = [send(own, strip, 1, partner) for strip in range(STRIPS)]
    for strip, copy in enumerate(across):
        copy.wait_recv()
        late.append(send(far, strip, 2, partner))
    for copy in late:
        copy.wait_recv()
    for copy in started:
        copy.wait_send()


def share_factors(mine):
    return pl.pallas_call(
        share_kernel,
        out_shape=jax.ShapeDtypeStruct((4,) + mine.shape, bf16),
        in_specs=[VMEM],
        out_specs=VMEM,
        scratch_shapes=[
            pltpu.SemaphoreType.DMA((STRIPS, 3)),
            pltpu.SemaphoreType.DMA((STRIPS, 3)),
        ],
        compiler_params=pltpu.CompilerParams(
            vmem_limit_bytes=16 * MIB, collective_id=2, has_side_effects=True
        ),
        name="share_factors",
    )(mine)


def finish_kernel(factors, tail_old, up_old, down_old, qkv_new, out_new, up_new, down_new):
    shrink = 1.0 - muon_rate * muon_decay
    qkv_cols = qkv_new.shape[1]
    old = tail_old[...].astype(f32) * shrink
    step = muon_rate * math.sqrt(3.0) * factors[0].astype(f32)
    qkv_new[...] = (old - step)[:, :qkv_cols]
    out_new[...] = (old - muon_rate * factors[1].astype(f32))[:, qkv_cols:]
    up_rate = muon_rate * math.sqrt(max(1.0, FF / D))
    up_new[...] = up_old[...].astype(f32) * shrink - up_rate * factors[2].astype(f32)
    down_new[...] = down_old[...].astype(f32) * shrink - muon_rate * factors[3].astype(f32).T


def finish_weights(factors, tail_old, up_old, down_old, qkv_cols):
    rows, cols = tail_old.shape

    def shape(*dims):
        return jax.ShapeDtypeStruct(dims, f32)

    return pl.pallas_call(
        finish_kernel,
        out_shape=(
            shape(rows, qkv_cols),
            shape(rows, cols - qkv_cols),
            shape(rows, cols),
            shape(cols, rows),
        ),
        in_specs=[VMEM] * 4,
        out_specs=(VMEM,) * 4,
        compiler_params=pltpu.CompilerParams(vmem_limit_bytes=32 * MIB),
        name="finish_weights",
    )(factors, tail_old, up_old, down_old)


def swap(value, axis, bit):
    size = lax.axis_size(axis)
    return lax.ppermute(value, axis, [(i, i ^ bit) for i in range(size)])


def scatter_head(value, bit, position):
    half = value.shape[1] // 2
    mine = lax.dynamic_slice_in_dim(value, position * half, half, 1)
    other = lax.dynamic_slice_in_dim(value, (1 - position) * half, half, 1)
    return (mine.astype(f32) + swap(other, "head", bit).astype(f32)).astype(bf16)


def scatter_dp_pair(value, position):
    paired = value.reshape((value.shape[0] // 2, 2) + value.shape[1:])
    mine = lax.dynamic_index_in_dim(paired, position, 1, False)
    other = lax.dynamic_index_in_dim(paired, 1 - position, 1, False)
    return (mine.astype(f32) + swap(other, "dp", 1).astype(f32)).astype(bf16)


def scatter_dp_rest(value, place):
    ranks = value.shape[0]
    total = lax.dynamic_index_in_dim(value, place, 0, False).astype(f32)
    for step in range(1, ranks):
        sent = lax.dynamic_index_in_dim(value, place ^ step, 0, False)
        total = total + swap(sent, "dp", 2 * step).astype(f32)
    return total


def local(
    tokens,
    cotangent,
    qkv_weight,
    out_weight,
    up_weight,
    down_weight,
    vectors,
    qkv_moment,
    out_moment,
    up_moment,
    down_moment,
    adam_first,
    adam_second,
    bucket_class,
    row_lengths,
):
    n_dp = lax.axis_size("dp")
    n_head = lax.axis_size("head")
    dp_id = lax.axis_index("dp")
    head_id = lax.axis_index("head")
    core, side = head_id % 2, head_id // 2
    tok, width = tokens.shape
    hidden = up_weight.shape[1]
    half = width // 2
    pieces = split_vectors(vectors, width, hidden)
    bias_query, bias_value, bias_out, gain_one, shift_one = pieces[:5]
    bias_up, bias_down, gain_two, shift_two = pieces[5:]
    bias_qkv = jnp.concatenate([bias_query, jnp.zeros_like(bias_query), bias_value])

    def column_half(value, which):
        return lax.dynamic_slice_in_dim(value, which * half, half, 1)

    qkv = (dot(tokens, qkv_weight, 1, 0) + bias_qkv).astype(bf16)
    other = swap(qkv[:, width:], "head", 1)
    block = head_id.astype(jnp.int32)[None]
    attended = attend(block, bucket_class, row_lengths, qkv, other)
    attn_val = dot(attended, out_weight, 1, 0) + bias_out
    resid_one = tokens.astype(f32) + attn_val
    centre = resid_one - jnp.mean(resid_one, axis=-1, keepdims=True)
    rstd_one = lax.rsqrt(jnp.mean(centre * centre, axis=-1, keepdims=True) + norm_eps)
    zhat_one = centre * rstd_one
    normed_one = zhat_one * gain_one + shift_one
    normed_low = normed_one.astype(bf16)
    up_val = dot(normed_low, up_weight, 1, 0) + bias_up
    phi_cum = 0.5 * (1.0 + lax.erf(up_val * (0.5**0.5)))
    active_low = (up_val * phi_cum).astype(bf16)
    slope = phi_cum + up_val * jnp.exp(-0.5 * up_val * up_val) * (1.0 / math.sqrt(2.0 * math.pi))
    down_val = dot(active_low, down_weight, 1, 0) + bias_down
    resid_two = normed_one + down_val
    centre = resid_two - jnp.mean(resid_two, axis=-1, keepdims=True)
    rstd_two = lax.rsqrt(jnp.mean(centre * centre, axis=-1, keepdims=True) + norm_eps)
    zhat_two = centre * rstd_two
    mixed = zhat_two * gain_two + shift_two

    def norm_back(grad, gain, zhat, rstd):
        inner = grad * gain
        mean = jnp.mean(inner, axis=-1, keepdims=True)
        slant = jnp.mean(inner * zhat, axis=-1, keepdims=True)
        return (inner - mean - zhat * slant) * rstd, jnp.sum(grad * zhat, axis=0), jnp.sum(grad, axis=0)

    grad_two, grad_gain_two, grad_shift_two = norm_back(
        cotangent.astype(f32), gain_two, zhat_two, rstd_two
    )
    grad_down_low = grad_two.astype(bf16)
    grad_bias_down = jnp.sum(grad_down_low, axis=0, dtype=f32)

    x_id, z_id = dp_id % 2, dp_id // 2

    grad_up_low = (dot(grad_down_low, down_weight, 1, 1) * slope).astype(bf16)
    grad_bias_up = jnp.sum(grad_up_low, axis=0, dtype=f32)
    grad_normed = grad_two + dot(grad_up_low, up_weight, 1, 1)
    grad_one, grad_gain_one, grad_shift_one = norm_back(grad_normed, gain_one, zhat_one, rstd_one)
    grad_attn_low = grad_one.astype(bf16)
    grad_bias_out = jnp.sum(grad_attn_low, axis=0, dtype=f32)
    grad_heads = dot(grad_attn_low, out_weight, 1, 1).astype(bf16)
    grad_query, own, sent = attend_back(block, bucket_class, row_lengths, qkv, other, grad_heads)
    grad_kv = (own + swap(sent, "head", 1).astype(f32)).astype(bf16)
    grad_qkv = jnp.concatenate([grad_query, grad_kv], axis=1)
    grad_bias_qkv = jnp.sum(grad_qkv, axis=0, dtype=f32)
    input_grad = grad_one + dot(grad_qkv, qkv_weight, 1, 1)
    grad_vector = jnp.concatenate(
        [
            grad_bias_qkv[:width],
            grad_bias_qkv[2 * width :],
            grad_bias_out,
            grad_gain_one,
            grad_shift_one,
            grad_bias_up,
            grad_bias_down,
            grad_gain_two,
            grad_shift_two,
        ]
    )
    grad_vector = grad_vector + swap(grad_vector, "head", 1)
    vec_len = grad_vector.shape[0] // n_dp
    wides = [active_low, grad_up_low, grad_attn_low, grad_qkv]
    narrows = [grad_down_low, normed_low, attended, tokens]
    qkv_cols, out_cols = qkv_moment.shape[1], out_moment.shape[1]
    shrink = 1.0 - muon_rate * muon_decay

    def weight_block(weight, cols, dim):
        return lax.dynamic_slice_in_dim(weight, dp_id * cols, cols, dim)

    old_weights = [
        weight_block(qkv_weight, qkv_cols, 1),
        weight_block(out_weight, out_cols, 1),
        weight_block(up_weight, up_moment.shape[1], 1),
        weight_block(down_weight, down_moment.shape[1], 0),
    ]

    if (n_dp, n_head, tok) == (8, 4, 256):
        vec = jnp.pad(grad_vector.reshape(n_dp, vec_len), ((0, 0), (0, 4 * VEC_ROWS * VEC_COLS - vec_len)))
        vec = vec.reshape(4, 2, 2, 2, VEC_ROWS, VEC_COLS)
        vec = lax.dynamic_index_in_dim(vec, core, 2, False).astype(bf16)
        sums, vec = reduce_gradients(
            [part for value in wides for part in (value, swap(value, "head", 1))],
            [
                part
                for value in narrows
                for part in (
                    column_half(value, core),
                    swap(column_half(value, 1 - core), "head", 1),
                )
            ],
            vec,
        )
        grad_vec = vec.reshape(-1)[:vec_len].astype(f32)
        *moments, chosen = update_moments(
            block,
            sums.reshape(3, width, -1),
            jnp.concatenate([qkv_moment, out_moment], axis=1),
            up_moment,
            down_moment,
            qkv_cols,
        )
        factors = share_factors(orthogonalize(gram_sum(chosen), chosen))
        new_weights = finish_weights(
            factors,
            jnp.concatenate(old_weights[:2], axis=1),
            old_weights[2],
            old_weights[3],
            qkv_cols,
        )
    else:

        def both_halves(value):
            return jnp.concatenate(
                [column_half(value, core), swap(column_half(value, 1 - core), "head", 1)], axis=0
            )

        def weight_grad(wide, narrow):
            wide = jnp.concatenate([wide, swap(wide, "head", 1)], axis=0)
            value = dot(wide, both_halves(narrow), 0, 0).astype(bf16)
            return value.reshape(n_dp, value.shape[0] // n_dp, half)

        def reduce_y_first(value):
            return scatter_dp_rest(scatter_dp_pair(scatter_head(value, 2, side), x_id), z_id)

        def reduce_x_first(value):
            return scatter_dp_rest(scatter_head(scatter_dp_pair(value, x_id), 2, side), z_id)

        def spread(value):
            value = value.astype(bf16)
            came = swap(value, "head", 2)
            value = jnp.concatenate(
                [jnp.where(side == 0, value, came), jnp.where(side == 0, came, value)], axis=0
            )
            came = swap(value, "head", 1)
            return jnp.concatenate(
                [jnp.where(core == 0, value, came), jnp.where(core == 0, came, value)], axis=1
            ).astype(f32)

        down_part, up_part, out_part, qkv_part = [
            weight_grad(wide, narrow) for wide, narrow in zip(wides, narrows)
        ]
        vec_rows = 16
        vec_part = grad_vector.reshape(n_dp, vec_len)
        vec_part = jnp.pad(vec_part, ((0, 0), (0, vec_rows * width - vec_len)))
        vec_part = vec_part.reshape(n_dp, vec_rows, width)
        vec_part = lax.dynamic_slice_in_dim(vec_part, core * half, half, 2).astype(bf16)
        down_new = spread(reduce_x_first(down_part))
        up_new = spread(reduce_y_first(up_part))
        tail_new = spread(
            reduce_y_first(jnp.concatenate([qkv_part, out_part, vec_part], axis=1))
        )
        grads = [
            tail_new[:qkv_cols].T,
            tail_new[qkv_cols : qkv_cols + out_cols].T,
            up_new.T,
            down_new.T,
        ]
        grad_vec = tail_new[qkv_cols + out_cols :].reshape(-1)[:vec_len]
        moments = [
            muon_keep * old + grad
            for old, grad in zip([qkv_moment, out_moment, up_moment, down_moment], grads)
        ]
        most = max(m.shape[1] for m in moments)
        padded = [jnp.pad(m, ((0, 0), (0, most - m.shape[1]))) for m in moments]
        chosen = padded[-1]
        for index in range(len(padded) - 2, -1, -1):
            chosen = jnp.where(head_id == index, padded[index], chosen)
        gram_mat = lax.dot_general(
            chosen, chosen, (((1,), (1,)), ((), ())), precision=lax.Precision.HIGH
        )
        own_factor = orthogonalize(lax.psum(gram_mat, "dp"), chosen)
        across = swap(own_factor, "head", 2)
        low_pair = jnp.where(side == 0, own_factor, across)
        high_pair = jnp.where(side == 0, across, own_factor)
        near_low = swap(low_pair, "head", 1)
        near_high = swap(high_pair, "head", 1)
        factors = [
            jnp.where(core == 0, low_pair, near_low),
            jnp.where(core == 0, near_low, low_pair),
            jnp.where(core == 0, high_pair, near_high),
            jnp.where(core == 0, near_high, high_pair),
        ]
        factors = [o[:, : m.shape[1]].astype(f32) for o, m in zip(factors, moments)]
        factors[3] = factors[3].T
        rates = (math.sqrt(3.0), 1.0, math.sqrt(max(1.0, hidden / width)), 1.0)
        new_weights = [
            old.astype(f32) * shrink - muon_rate * rate * factor
            for old, rate, factor in zip(old_weights, rates, factors)
        ]

    vec_old = lax.dynamic_slice_in_dim(vectors, dp_id * vec_len, vec_len, 0)
    vec_first = beta_first * adam_first + (1.0 - beta_first) * grad_vec
    vec_second = beta_second * adam_second + (1.0 - beta_second) * grad_vec * grad_vec
    first_hat = vec_first / (1.0 - beta_first**STEP)
    second_hat = vec_second / (1.0 - beta_second**STEP)
    vec_new = vec_old - adam_rate * first_hat / (jnp.sqrt(second_hat) + adam_eps)
    return (mixed, input_grad, *moments, *new_weights, vec_first, vec_second, vec_new)


def solution(mesh):
    tokens_spec = P(("dp", "head"), None)
    block_spec = P(None, "dp")
    return jax.shard_map(
        local,
        mesh=mesh,
        in_specs=(
            tokens_spec,
            tokens_spec,
            P(),
            P(),
            P(),
            P(),
            P(),
            block_spec,
            block_spec,
            block_spec,
            block_spec,
            P("dp"),
            P("dp"),
            P("dp"),
            P("dp", None),
        ),
        out_specs=(
            tokens_spec,
            tokens_spec,
            block_spec,
            block_spec,
            block_spec,
            block_spec,
            block_spec,
            block_spec,
            block_spec,
            P("dp", None),
            P("dp"),
            P("dp"),
            P("dp"),
        ),
        check_vma=False,
    )
```

```python
import functools
import math

import jax
import jax.numpy as jnp
from jax import lax
from jax.experimental import pallas as pl
from jax.experimental.pallas import tpu as pltpu
from jax.sharding import PartitionSpec as P

D = 768
HEADS = 12
HEAD_DIM = 64
FF = 3072
BASE_LEN = 128
NS_STEPS = 5
STEP = 5
MAX_LEN = 512

f32 = jnp.float32
bf16 = jnp.bfloat16

norm_eps = 1e-12
masked_score = -1000000000.0
quintic_a = 3.4445
quintic_b = -4.775
quintic_c = 2.0315
muon_rate = 1.0
muon_decay = 0.01
muon_keep = 0.5
adam_rate = 0.2
beta_first = 0.9
beta_second = 0.999
adam_eps = 1e-08
MIB = 1024 * 1024


def dot(left, right, left_dim, right_dim):
    return lax.dot_general(
        left, right, (((left_dim,), (right_dim,)), ((), ())), preferred_element_type=f32
    )


def split_vectors(vectors, width, hidden):
    lengths_list = [width] * 5 + [hidden] + [width] * 3
    pieces = []
    offset = 0
    for length in lengths_list:
        pieces.append(vectors[offset : offset + length])
        offset = offset + length
    return pieces


def allowed_mask(class_ref, length_ref, block, tok):
    shift = class_ref[0] + int(math.log2(BASE_LEN))
    query_place = block * tok + lax.broadcasted_iota(jnp.int32, (tok, 1), 0)
    lane = lax.broadcasted_iota(jnp.int32, (1, 2 * tok), 1)
    own = lane < tok
    key_place = jnp.where(own, block * tok + lane, (block ^ 1) * tok + lane - tok)
    key_row = lax.shift_right_logical(key_place, jnp.broadcast_to(shift, key_place.shape))
    offset = key_place - lax.shift_left(key_row, jnp.broadcast_to(shift, key_place.shape))
    row_len = jnp.zeros_like(key_row)
    for slot in range(length_ref.shape[1]):
        row_len = jnp.where(key_row == slot, length_ref[0, slot], row_len)
    key_row = jnp.where(offset < row_len, key_row, -1)
    query_row = lax.shift_right_logical(query_place, jnp.broadcast_to(shift, query_place.shape))
    return query_row == key_row


def half_masks():
    lane = lax.broadcasted_iota(jnp.int32, (1, 2 * HEAD_DIM), 1)
    first = (lane < HEAD_DIM).astype(f32)
    return (first.astype(bf16), (1.0 - first).astype(bf16)), lane < HEAD_DIM


def head_prob(query, keys, allowed):
    score = jnp.where(allowed, dot(query, keys, 1, 1) * HEAD_DIM ** (-0.5), masked_score)
    exponent = jnp.exp(score - jnp.max(score, axis=-1, keepdims=True))
    return exponent / jnp.sum(exponent, axis=-1, keepdims=True)


def attend_kernel(block_ref, class_ref, length_ref, qkv_ref, other_ref, out_ref):
    tok = qkv_ref.shape[0]
    allowed = allowed_mask(class_ref, length_ref, block_ref[0], tok)
    masks, first = half_masks()
    for pair in range(HEADS // 2):
        cols = pl.ds(pair * 2 * HEAD_DIM, 2 * HEAD_DIM)
        kcols = pl.ds(D + pair * 2 * HEAD_DIM, 2 * HEAD_DIM)
        vcols = pl.ds(2 * D + pair * 2 * HEAD_DIM, 2 * HEAD_DIM)
        query = qkv_ref[:, cols]
        keys = jnp.concatenate([qkv_ref[:, kcols], other_ref[:, cols]], axis=0)
        values = jnp.concatenate([qkv_ref[:, vcols], other_ref[:, kcols]], axis=0)
        outs = []
        for mask in masks:
            prob = head_prob(query * mask, keys, allowed)
            outs.append(dot(prob.astype(bf16), values, 1, 0))
        out_ref[:, cols] = jnp.where(first, outs[0], outs[1]).astype(bf16)


def attend_back_kernel(
    block_ref, class_ref, length_ref, qkv_ref, other_ref, grad_ref, dq_ref, own_ref, send_ref
):
    tok = qkv_ref.shape[0]
    allowed = allowed_mask(class_ref, length_ref, block_ref[0], tok)
    masks, first = half_masks()
    scale = HEAD_DIM ** (-0.5)
    for pair in range(HEADS // 2):
        cols = pl.ds(pair * 2 * HEAD_DIM, 2 * HEAD_DIM)
        kcols = pl.ds(D + pair * 2 * HEAD_DIM, 2 * HEAD_DIM)
        vcols = pl.ds(2 * D + pair * 2 * HEAD_DIM, 2 * HEAD_DIM)
        query = qkv_ref[:, cols]
        keys = jnp.concatenate([qkv_ref[:, kcols], other_ref[:, cols]], axis=0)
        values = jnp.concatenate([qkv_ref[:, vcols], other_ref[:, kcols]], axis=0)
        grad = grad_ref[:, cols]
        dqs, dk, dv = [], None, None
        for mask in masks:
            head_query = query * mask
            head_grad = grad * mask
            prob = head_prob(head_query, keys, allowed)
            part_v = dot(prob.astype(bf16), head_grad, 0, 0)
            dprob = dot(head_grad, values, 1, 1)
            dscore = prob * (dprob - jnp.sum(prob * dprob, axis=-1, keepdims=True))
            dscore = dscore.astype(bf16)
            dqs.append(dot(dscore, keys, 1, 0))
            part_k = dot(dscore, head_query, 0, 0)
            dk = part_k if dk is None else dk + part_k
            dv = part_v if dv is None else dv + part_v
        dk = dk * scale
        dq_ref[:, cols] = (jnp.where(first, dqs[0], dqs[1]) * scale).astype(bf16)
        own_ref[:, cols] = dk[:tok]
        own_ref[:, kcols] = dv[:tok]
        send_ref[:, cols] = dk[tok:].astype(bf16)
        send_ref[:, kcols] = dv[tok:].astype(bf16)


SMEM = pl.BlockSpec(memory_space=pltpu.SMEM)
VMEM = pl.BlockSpec(memory_space=pltpu.VMEM)


def attend(block, row_class, lengths, qkv, other):
    tok = qkv.shape[0]
    return pl.pallas_call(
        attend_kernel,
        out_shape=jax.ShapeDtypeStruct((tok, D), bf16),
        in_specs=[SMEM, SMEM, SMEM, VMEM, VMEM],
        out_specs=VMEM,
        compiler_params=pltpu.CompilerParams(vmem_limit_bytes=32 * MIB),
        name="attend",
    )(block, row_class, lengths, qkv, other)


def attend_back(block, row_class, lengths, qkv, other, grad):
    tok = qkv.shape[0]
    return pl.pallas_call(
        attend_back_kernel,
        out_shape=(
            jax.ShapeDtypeStruct((tok, D), bf16),
            jax.ShapeDtypeStruct((tok, 2 * D), f32),
            jax.ShapeDtypeStruct((tok, 2 * D), bf16),
        ),
        in_specs=[SMEM, SMEM, SMEM, VMEM, VMEM, VMEM],
        out_specs=(VMEM, VMEM, VMEM),
        compiler_params=pltpu.CompilerParams(vmem_limit_bytes=32 * MIB),
        name="attend_back",
    )(block, row_class, lengths, qkv, other, grad)


CENTRES = (0.0, 0.0, 0.0, 0.8, 0.8)
TILE = 256
SUB = 128


def sub_blocks(size):
    count = size // SUB
    return [(i, j) for i in range(count) for j in range(i, count)]


def ortho_kernel(packed, gram_ref, moment_ref, out_ref, e, f, g, eb, fb, gb, ya, yb, y):
    size = e.shape[0]
    tiles = [slice(i * TILE, (i + 1) * TILE) for i in range(size // TILE)]

    def unit(rows):
        row_id = rows.start + lax.broadcasted_iota(jnp.int32, (TILE, size), 0)
        col_id = lax.broadcasted_iota(jnp.int32, (TILE, size), 1)
        return (row_id == col_id).astype(f32)

    if packed:
        for index, (i, j) in enumerate(sub_blocks(size)):
            value = gram_ref[:, index].reshape(SUB, SUB)
            e[i * SUB : (i + 1) * SUB, j * SUB : (j + 1) * SUB] = value
            if i != j:
                e[j * SUB : (j + 1) * SUB, i * SUB : (i + 1) * SUB] = value.T
        gram = e
    else:
        gram = gram_ref
    diagonal = jnp.zeros((TILE, size), f32)
    for rows in tiles:
        diagonal = diagonal + gram[rows, :] * unit(rows)
    trace = jnp.sum(jnp.sum(diagonal, axis=0, keepdims=True), axis=1, keepdims=True)
    factor = 1.0 / (jnp.sqrt(trace) + 1e-07)
    square_factor = factor * factor
    for rows in tiles:
        value = gram[rows, :] * square_factor
        e[rows, :] = value
        eb[rows, :] = value.astype(bf16)
        moment = moment_ref[rows, :] * factor
        y[rows, :] = moment
        ya[rows, :] = moment.astype(bf16)
    now, then = ya, yb
    for step in range(NS_STEPS):
        last = step + 1 == NS_STEPS
        centre = CENTRES[step]
        after = 0.0 if last else CENTRES[step + 1]
        keep = quintic_a + quintic_b * centre + quintic_c * centre * centre
        linear = quintic_b + 2.0 * quintic_c * centre
        for rows in tiles:
            value = linear * e[rows, :] + quintic_c * dot(eb[rows, :], eb[...], 1, 0)
            fb[rows, :] = value.astype(bf16)
            if not last:
                f[rows, :] = value
        for rows in tiles:
            value = keep * y[rows, :] + dot(fb[rows, :], now[...], 1, 0)
            if last:
                out_ref[rows, :] = value.astype(out_ref.dtype)
            else:
                y[rows, :] = value
                then[rows, :] = value.astype(bf16)
        if last:
            break
        now, then = then, now
        for rows in tiles:
            value = keep * e[rows, :] + dot(eb[rows, :], fb[...], 1, 0)
            if centre:
                value = value + centre * f[rows, :]
            g[rows, :] = value
            gb[rows, :] = value.astype(bf16)
        for rows in tiles:
            value = keep * g[rows, :] + dot(gb[rows, :], fb[...], 1, 0)
            if centre:
                value = value + (centre * keep) * f[rows, :]
            shift = centre * keep * keep - after
            if shift:
                value = value + shift * unit(rows)
            e[rows, :] = value
            eb[rows, :] = value.astype(bf16)


def orthogonalize(gram_mat, moment):
    size, cols = moment.shape
    square = pltpu.VMEM((size, size), f32)
    square_low = pltpu.VMEM((size, size), bf16)
    return pl.pallas_call(
        functools.partial(ortho_kernel, gram_mat.ndim != 2),
        out_shape=jax.ShapeDtypeStruct((size, cols), bf16),
        in_specs=[VMEM, VMEM],
        out_specs=VMEM,
        scratch_shapes=[
            square,
            square,
            square,
            square_low,
            square_low,
            square_low,
            pltpu.VMEM((size, cols), bf16),
            pltpu.VMEM((size, cols), bf16),
            pltpu.VMEM((size, cols), f32),
        ],
        compiler_params=pltpu.CompilerParams(vmem_limit_bytes=48 * MIB),
        name="ortho",
    )(gram_mat, moment)


MESH = pl.DeviceIdType.MESH
CHUNK = 48
PARTS = 4
UNIT = 2 * PARTS * CHUNK
HALF = D // 2
LANES = 128
VEC_BLOCK = 9
ROWS = 16
BIAS_QUERY, BIAS_VALUE, BIAS_OUT, GAIN_ONE, SHIFT_ONE, BIAS_UP = (i * D for i in range(6))
BIAS_DOWN, GAIN_TWO, SHIFT_TWO = (BIAS_UP + FF + i * D for i in range(3))


def position():
    dp_id, head_id = lax.axis_index("dp"), lax.axis_index("head")
    z, x = dp_id // 2, dp_id % 2
    y, core = head_id // 2, head_id % 2
    return z, x, y, core


def device(z, x, y, core):
    return (2 * z + x, 2 * y + core)


def flip_z(z, step):
    high, low = z // 2, z % 2
    high = 1 - high if step // 2 else high
    low = 1 - low if step % 2 else low
    return 2 * high + low


def greet(others):
    barrier = pltpu.get_barrier_semaphore()
    for other in others:
        pl.semaphore_signal(barrier, inc=1, device_id=other, device_id_type=MESH)
    pl.semaphore_wait(barrier, len(others))


def by_rows(count, body, init=None):
    def step(index, carry):
        return body(pl.ds(pl.multiple_of(index * ROWS, ROWS), ROWS), carry)

    return lax.fori_loop(0, count // ROWS, step, init)


def row_mean(value):
    return jnp.sum(value, axis=-1, keepdims=True) * (1.0 / D)


def fold(value):
    return jnp.sum(value.reshape(value.shape[0] // 8, 8, value.shape[1]), axis=0)


def column_sum(value):
    return jnp.sum(value, axis=0, keepdims=True)


def layer_kernel(
    row_class,
    lengths,
    tokens,
    cotangent,
    vectors,
    qkv_hbm,
    out_hbm,
    up_hbm,
    down_hbm,
    mixed,
    input_grad,
    sums,
    vec_sum,
    qkv_w,
    out_w,
    up_w,
    down_w,
    query,
    keys_values,
    prob,
    attended,
    normed_low,
    grad_down,
    grad_attn,
    tokens_far,
    attended_far,
    normed_far,
    grad_down_far,
    active,
    active_far,
    grad_up,
    grad_up_far,
    grad_attn_far,
    grad_qkv,
    grad_qkv_far,
    grad_heads,
    slope,
    normed_one,
    zhat_one,
    rstd_one,
    grad_two,
    grad_one,
    work,
    kv_own,
    kv_sent,
    kv_came,
    vec,
    vec_core,
    vec_y,
    vec_x,
    vec_z,
    part,
    came_one,
    came_two,
    came_three,
    load_sem,
    pair_send,
    pair_recv,
    send_sem,
    recv_sem,
):
    z, x, y, core = position()
    tok = tokens.shape[0]
    loads = {
        name: pltpu.make_async_copy(source, target, load_sem.at[index])
        for index, (name, source, target) in enumerate(
            (
                ("qkv", qkv_hbm, qkv_w),
                ("out", out_hbm, out_w),
                ("up", up_hbm, up_w),
                ("down", down_hbm, down_w),
            )
        )
    }
    for load in loads.values():
        load.start()
    beyond = device(z, x, 1 - y, core)
    beside = device(z, 1 - x, y, core)
    partner = device(z, x, y, 1 - core)
    along = [device(flip_z(z, step), x, y, core) for step in (1, 2, 3)]
    greet([beyond, beside, partner] + along)
    started = []

    def remote(source, target, send_at, recv_at, other):
        copy = pltpu.make_async_remote_copy(
            src_ref=source,
            dst_ref=target,
            send_sem=send_at,
            recv_sem=recv_at,
            device_id=other,
            device_id_type=MESH,
        )
        copy.start()
        started.append(copy)
        return copy

    pair_count = []

    def to_partner(source, target):
        slot = len(pair_count)
        pair_count.append(slot)
        return remote(source, target, pair_send.at[slot], pair_recv.at[slot], partner)

    own_half = pl.ds(pl.multiple_of(core * HALF, HALF), HALF)
    other_half = pl.ds(pl.multiple_of((1 - core) * HALF, HALF), HALF)

    def span(start, length=D):
        return vectors[0:1, start : start + length]

    def put_vec(start, value):
        for index in range(value.shape[1] // LANES):
            block, row = divmod(start // LANES + index, VEC_BLOCK)
            vec[block, row : row + 1, :] = value[:, index * LANES : (index + 1) * LANES]

    vec[...] = jnp.zeros_like(vec)

    loads["qkv"].wait()
    tokens_came = to_partner(tokens.at[:, other_half], tokens_far)
    own_rows = pl.ds(0, tok)
    far_rows = pl.ds(tok, tok)
    for index, start in ((1, None), (2, BIAS_VALUE)):
        value = dot(tokens[...], qkv_w[:, index * D : (index + 1) * D], 1, 0)
        if start is not None:
            value = value + span(start)
        keys_values[own_rows, (index - 1) * D : index * D] = value.astype(bf16)
    kv_arrived = to_partner(keys_values.at[own_rows], keys_values.at[far_rows])
    value = dot(tokens[...], qkv_w[:, :D], 1, 0) + span(BIAS_QUERY)
    query[...] = value.astype(bf16)
    allowed = allowed_mask(row_class, lengths, 2 * y + core, tok)
    masks, first = half_masks()
    kv_arrived.wait_recv()

    scale = HEAD_DIM ** (-0.5)
    for pair in range(HEADS // 2):
        cols = slice(pair * LANES, (pair + 1) * LANES)
        keys = keys_values[:, cols]
        values = keys_values[:, D + cols.start : D + cols.stop]
        outs = []
        for side, mask in enumerate(masks):
            score = dot(query[:, cols] * (mask * scale), keys, 1, 1)
            score = jnp.where(allowed, score, masked_score)
            exponent = jnp.exp(score - jnp.max(score, axis=-1, keepdims=True))
            chance = exponent * (1.0 / jnp.sum(exponent, axis=-1, keepdims=True))
            prob[2 * pair + side] = chance
            outs.append(dot(chance.astype(bf16), values, 1, 0))
        attended[:, cols] = jnp.where(first, outs[0], outs[1]).astype(bf16)
    attended_came = to_partner(attended.at[:, other_half], attended_far)

    loads["out"].wait()
    work[...] = dot(attended[...], out_w[...], 1, 0)

    def norm_one(rows, carry):
        value = tokens[rows, :].astype(f32) + (work[rows, :] + span(BIAS_OUT))
        centre = value - row_mean(value)
        rstd = lax.rsqrt(row_mean(centre * centre) + norm_eps)
        zhat = centre * rstd
        normed = zhat * span(GAIN_ONE) + span(SHIFT_ONE)
        zhat_one[rows, :] = zhat
        rstd_one[rows, :] = jnp.broadcast_to(rstd, (ROWS, LANES))
        normed_one[rows, :] = normed
        normed_low[rows, :] = normed.astype(bf16)
        return carry

    by_rows(tok, norm_one)
    normed_came = to_partner(normed_low.at[:, other_half], normed_far)

    loads["up"].wait()
    for tile in range(FF // D):
        cols = slice(tile * D, (tile + 1) * D)
        work[...] = dot(normed_low[...], up_w[:, cols], 1, 0)

        def gelu(rows, carry):
            value = work[rows, :] + span(BIAS_UP + cols.start)
            chance = 0.5 * (1.0 + lax.erf(value * (0.5**0.5)))
            active[rows, cols] = (value * chance).astype(bf16)
            density = jnp.exp(-0.5 * value * value) * (1.0 / math.sqrt(2.0 * math.pi))
            slope[rows, cols] = chance + value * density
            return carry

        by_rows(tok, gelu)
    active_came = to_partner(active, active_far)
    loads["down"].wait()
    work[...] = dot(active[...], down_w[...], 1, 0)

    def norm_two(rows, carry):
        value = normed_one[rows, :] + (work[rows, :] + span(BIAS_DOWN))
        centre = value - row_mean(value)
        rstd = lax.rsqrt(row_mean(centre * centre) + norm_eps)
        zhat = centre * rstd
        mixed[rows, :] = zhat * span(GAIN_TWO) + span(SHIFT_TWO)
        grad = cotangent[rows, :].astype(f32)
        inner = grad * span(GAIN_TWO)
        grad_in = (inner - row_mean(inner) - zhat * row_mean(inner * zhat)) * rstd
        grad_two[rows, :] = grad_in
        low = grad_in.astype(bf16)
        grad_down[rows, :] = low
        gain, shift, bias = carry
        return gain + fold(grad * zhat), shift + fold(grad), bias + fold(low.astype(f32))

    zero = jnp.zeros((8, D), f32)
    gain, shift, bias = by_rows(tok, norm_two, (zero, zero, zero))
    put_vec(GAIN_TWO, column_sum(gain))
    put_vec(SHIFT_TWO, column_sum(shift))
    put_vec(BIAS_DOWN, column_sum(bias))
    grad_down_came = to_partner(grad_down.at[:, other_half], grad_down_far)

    for tile in range(FF // D):
        cols = slice(tile * D, (tile + 1) * D)
        work[...] = dot(grad_down[...], down_w[cols, :], 1, 1)

        def gelu_back(rows, carry):
            low = (work[rows, :] * slope[rows, cols]).astype(bf16)
            grad_up[rows, cols] = low
            return carry + fold(low.astype(f32))

        put_vec(BIAS_UP + cols.start, column_sum(by_rows(tok, gelu_back, zero)))
    grad_up_came = to_partner(grad_up, grad_up_far)

    class Chain:
        def __init__(self, matrix, quarter, y_first):
            self.index, self.y_first = matrix * PARTS + quarter, y_first
            self.own = part.at[matrix, quarter]
            self.one = came_one.at[matrix, quarter]
            self.two = came_two.at[matrix, quarter]
            self.three = came_three.at[matrix, quarter]
            self.final = sums.at[matrix, :, :, quarter]

        def send(self, source, target, slot, other):
            sems = (send_sem.at[self.index, slot], recv_sem.at[self.index, slot])
            return remote(source, target, *sems, other)

        def first(self):
            if self.y_first:
                source, other = self.own.at[:, :, 1 - y], beyond
            else:
                source, other = self.own.at[:, 1 - x], beside
            self.copy = self.send(source, self.one, 0, other)

        def second(self):
            self.copy.wait_recv()
            for i in range(4):
                for j in range(2):
                    at = (i, j, y) if self.y_first else (i, x, j)
                    self.own[at] = self.own[at] + self.one[i, j]
            if self.y_first:
                source, other = self.own.at[:, 1 - x, y], beside
            else:
                source, other = self.own.at[:, x, 1 - y], beyond
            self.copy = self.send(source, self.two, 1, other)

        def third(self):
            self.copy.wait_recv()
            for i in range(4):
                self.own[i, x, y] = self.own[i, x, y] + self.two[i]
            self.copies = [
                self.send(
                    self.own.at[flip_z(z, step), x, y],
                    self.three.at[step - 1],
                    1 + step,
                    along[step - 1],
                )
                for step in (1, 2, 3)
            ]

        def fourth(self):
            total = self.own[z, x, y].astype(f32)
            for step, copy in enumerate(self.copies):
                copy.wait_recv()
                total = total + self.three[step].astype(f32)
            self.final[core, y] = total.astype(bf16)
            block = self.final.at[core, y]
            self.copy = self.send(block, block, 5, beyond)

        def fifth(self):
            self.copy.wait_recv()
            block = self.final.at[core]
            self.copy = self.send(block, block, 6, partner)

        def sixth(self):
            self.copy.wait_recv()

    y_first = [Chain(0, quarter, True) for quarter in range(4)] + [Chain(2, 0, True)]
    x_first = [Chain(1, quarter, False) for quarter in range(4)]
    x_first += [Chain(2, quarter, False) for quarter in (1, 2, 3)]

    def feed_forward(matrix, narrow, narrow_far, wide, wide_far):
        left = narrow[:, own_half].astype(f32).T.astype(bf16)
        left_far = narrow_far[...].astype(f32).T.astype(bf16)

        def block(index, carry):
            cols = pl.ds(pl.multiple_of(index * UNIT, UNIT), UNIT)
            value = dot(left, wide[:, cols], 1, 0) + dot(left_far, wide_far[:, cols], 1, 0)
            value = value.astype(bf16)
            for side in range(2):
                for quarter in range(PARTS):
                    start = (side * PARTS + quarter) * CHUNK
                    part[matrix, quarter, index // 2, index % 2, side] = value[
                        start : start + CHUNK
                    ]
            return carry

        lax.fori_loop(0, 8, block, 0)

    def projections(matrix, wide, wide_far, narrow, narrow_far, width, offset):
        for tile in range(wide.shape[1] // UNIT):
            cols = slice(tile * UNIT, (tile + 1) * UNIT)
            value = dot(wide[:, cols], narrow[:, own_half], 0, 0)
            value = value + dot(wide_far[:, cols], narrow_far[...], 0, 0)
            value = value.astype(bf16)
            for start in range(0, UNIT, CHUNK):
                block, row = divmod(tile * UNIT + start, width)
                side, row = divmod(offset + row, PARTS * CHUNK)
                part[matrix, row // CHUNK, block // 2, block % 2, side] = value[
                    start : start + CHUNK
                ]

    grad_down_came.wait_recv()
    active_came.wait_recv()
    feed_forward(1, grad_down, grad_down_far, active, active_far)
    x_first[0].first()
    x_first[1].first()
    normed_came.wait_recv()
    grad_up_came.wait_recv()
    feed_forward(0, normed_low, normed_far, grad_up, grad_up_far)
    y_first[0].first()
    y_first[1].first()

    work[...] = dot(grad_up[...], up_w[...], 1, 1)

    def norm_one_back(rows, carry):
        grad = grad_two[rows, :] + work[rows, :]
        zhat = zhat_one[rows, :]
        inner = grad * span(GAIN_ONE)
        grad_in = inner - row_mean(inner) - zhat * row_mean(inner * zhat)
        grad_in = grad_in * rstd_one[rows, 0:1]
        grad_one[rows, :] = grad_in
        low = grad_in.astype(bf16)
        grad_attn[rows, :] = low
        gain, shift, bias = carry
        return gain + fold(grad * zhat), shift + fold(grad), bias + fold(low.astype(f32))

    gain, shift, bias = by_rows(tok, norm_one_back, (zero, zero, zero))
    put_vec(GAIN_ONE, column_sum(gain))
    put_vec(SHIFT_ONE, column_sum(shift))
    put_vec(BIAS_OUT, column_sum(bias))
    grad_attn_came = to_partner(grad_attn, grad_attn_far)
    grad_heads[...] = dot(grad_attn[...], out_w[...], 1, 1).astype(bf16)

    for pair in range(HEADS // 2):
        cols = slice(pair * LANES, (pair + 1) * LANES)
        value_cols = slice(D + cols.start, D + cols.stop)
        keys = keys_values[:, cols]
        values = keys_values[:, value_cols]
        queries_grad, keys_grad, values_grad = [], None, None
        for side, mask in enumerate(masks):
            head_query = query[:, cols] * mask
            head_grad = grad_heads[:, cols] * mask
            chance = prob[2 * pair + side]
            part_v = dot(chance.astype(bf16), head_grad, 0, 0)
            grad_chance = dot(head_grad, values, 1, 1)
            mean = jnp.sum(chance * grad_chance, axis=-1, keepdims=True)
            grad_score = (chance * (grad_chance - mean)).astype(bf16)
            queries_grad.append(dot(grad_score, keys, 1, 0))
            part_k = dot(grad_score, head_query, 0, 0)
            keys_grad = part_k if side == 0 else keys_grad + part_k
            values_grad = part_v if side == 0 else values_grad + part_v
        keys_grad = keys_grad * scale
        grad_query = jnp.where(first, queries_grad[0], queries_grad[1]) * scale
        grad_qkv[:, cols] = grad_query.astype(bf16)
        kv_own[:, cols] = keys_grad[:tok]
        kv_own[:, value_cols] = values_grad[:tok]
        kv_sent[:, cols] = keys_grad[tok:].astype(bf16)
        kv_sent[:, value_cols] = values_grad[tok:].astype(bf16)
    kv_grad_came = to_partner(kv_sent, kv_came)
    grad_attn_came.wait_recv()
    attended_came.wait_recv()
    projections(2, grad_attn, grad_attn_far, attended, attended_far, D // 8, 3 * D // 8)
    kv_grad_came.wait_recv()

    def join(rows, carry):
        grad_qkv[rows, D:] = (kv_own[rows, :] + kv_came[rows, :].astype(f32)).astype(bf16)
        return carry

    by_rows(tok, join)
    grad_qkv_came = to_partner(grad_qkv, grad_qkv_far)

    def query_bias(rows, carry):
        return carry + fold(grad_qkv[rows, :D].astype(f32))

    def value_bias(rows, carry):
        return carry + fold(grad_qkv[rows, 2 * D :].astype(f32))

    put_vec(BIAS_QUERY, column_sum(by_rows(tok, query_bias, zero)))
    put_vec(BIAS_VALUE, column_sum(by_rows(tok, value_bias, zero)))
    vec_came = to_partner(vec, vec_core)
    tokens_came.wait_recv()
    grad_qkv_came.wait_recv()
    projections(2, grad_qkv, grad_qkv_far, tokens, tokens_far, 3 * D // 8, 0)

    vec_slots = [(send_sem.at[3 * PARTS, i], recv_sem.at[3 * PARTS, i]) for i in range(5)]
    chains = (y_first, x_first)
    for turn in range(max(map(len, chains)) + 4):
        for line in chains:
            if turn + 2 < len(line):
                line[turn + 2].first()
        if turn == 0:
            value = dot(grad_qkv[...], qkv_w[...], 1, 1)
            input_grad[...] = grad_one[...] + value
        for behind, stage in enumerate(("second", "third", "fourth", "fifth", "sixth")):
            for line in chains:
                if 0 <= turn - behind < len(line):
                    getattr(line[turn - behind], stage)()
        if turn == 1:
            vec_came.wait_recv()
            vec_core[...] = vec[...] + vec_core[...]
            vec_came = remote(vec_core, vec_y, *vec_slots[0], beyond)
        if turn == 3:
            vec_came.wait_recv()
            for i in range(4):
                vec_x[0, i] = vec_core[2 * i + x] + vec_y[2 * i + x]
                vec_x[1, i] = vec_core[2 * i + 1 - x] + vec_y[2 * i + 1 - x]
            vec_came = remote(vec_x.at[1], vec_x.at[2], *vec_slots[1], beside)
        if turn == 5:
            vec_came.wait_recv()
            vec_x[0] = vec_x[0] + vec_x[2]
            vec_came = [
                remote(
                    vec_x.at[0, flip_z(z, step)],
                    vec_z.at[step - 1],
                    *vec_slots[1 + step],
                    along[step - 1],
                )
                for step in (1, 2, 3)
            ]
        if turn == 7:
            total = vec_x[0, z]
            for step, copy in enumerate(vec_came):
                copy.wait_recv()
                total = total + vec_z[step]
            vec_sum[...] = total
    for copy in started:
        copy.wait_send()


def layer(row_class, lengths, tokens, cotangent, vectors, qkv_w, out_w, up_w, down_w):
    tok = tokens.shape[0]
    chunk = (CHUNK, UNIT)
    any_place = pl.BlockSpec(memory_space=pl.ANY)

    def low(*dims):
        return pltpu.VMEM(dims, bf16)

    def wide(*dims):
        return pltpu.VMEM(dims, f32)

    return pl.pallas_call(
        layer_kernel,
        out_shape=(
            jax.ShapeDtypeStruct((tok, D), f32),
            jax.ShapeDtypeStruct((tok, D), f32),
            jax.ShapeDtypeStruct((3, 2, 2, PARTS) + chunk, bf16),
            jax.ShapeDtypeStruct((16, LANES), f32),
        ),
        in_specs=[SMEM, SMEM, VMEM, VMEM, VMEM] + [any_place] * 4,
        out_specs=(VMEM,) * 4,
        scratch_shapes=[
            low(D, 3 * D),
            low(D, D),
            low(D, FF),
            low(FF, D),
            low(tok, D),
            low(2 * tok, 2 * D),
            wide(HEADS, tok, 2 * tok),
            low(tok, D),
            low(tok, D),
            low(tok, D),
            low(tok, D),
            low(tok, HALF),
            low(tok, HALF),
            low(tok, HALF),
            low(tok, HALF),
            low(tok, FF),
            low(tok, FF),
            low(tok, FF),
            low(tok, FF),
            low(tok, D),
            low(tok, 3 * D),
            low(tok, 3 * D),
            low(tok, D),
            wide(tok, FF),
            wide(tok, D),
            wide(tok, D),
            wide(tok, LANES),
            wide(tok, D),
            wide(tok, D),
            wide(tok, D),
            wide(tok, 2 * D),
            low(tok, 2 * D),
            low(tok, 2 * D),
            wide(8, 16, LANES),
            wide(8, 16, LANES),
            wide(8, 16, LANES),
            wide(3, 4, 16, LANES),
            wide(3, 16, LANES),
            low(3, PARTS, 4, 2, 2, *chunk),
            low(3, PARTS, 4, 2, *chunk),
            low(3, PARTS, 4, *chunk),
            low(3, PARTS, 3, *chunk),
            pltpu.SemaphoreType.DMA((4,)),
            pltpu.SemaphoreType.DMA((11,)),
            pltpu.SemaphoreType.DMA((11,)),
            pltpu.SemaphoreType.DMA((3 * PARTS + 1, 7)),
            pltpu.SemaphoreType.DMA((3 * PARTS + 1, 7)),
        ],
        compiler_params=pltpu.CompilerParams(
            vmem_limit_bytes=63 * MIB, collective_id=0, has_side_effects=True
        ),
        name="layer",
    )(row_class, lengths, tokens, cotangent, vectors[None, :], qkv_w, out_w, up_w, down_w)


def update_kernel(
    head_ref, sums, qkv_old, out_old, up_old, down_old, qkv_new, out_new, up_new, down_new, chosen
):
    head_id = head_ref[0]
    qkv_cols = qkv_new.shape[0]
    up_new[...] = muon_keep * up_old[...] + sums[0].astype(f32)
    down_new[...] = muon_keep * down_old[...] + sums[1].astype(f32)
    for half in range(2):
        cols = slice(half * HALF, (half + 1) * HALF)
        value = sums[2, cols].astype(f32)
        qkv_new[:, cols] = muon_keep * qkv_old[:, cols] + value[:qkv_cols]
        out_new[:, cols] = muon_keep * out_old[:, cols] + value[qkv_cols:]

    @pl.when(head_id == 0)
    def _():
        chosen[:, :qkv_cols] = qkv_new[...].T
        chosen[:, qkv_cols:] = jnp.zeros((D, UNIT - qkv_cols), f32)

    @pl.when(head_id == 1)
    def _():
        chosen[:, :qkv_cols] = jnp.zeros((D, qkv_cols), f32)
        chosen[:, qkv_cols:] = out_new[...].T

    @pl.when(head_id == 2)
    def _():
        chosen[...] = up_new[...]

    @pl.when(head_id == 3)
    def _():
        chosen[...] = down_new[...]


def update_moments(head, sums, qkv_old, out_old, up_old, down_old):
    def like(value):
        return jax.ShapeDtypeStruct(value.shape, f32)

    return pl.pallas_call(
        update_kernel,
        out_shape=(like(qkv_old), like(out_old), like(up_old), like(down_old), like(up_old)),
        in_specs=[SMEM] + [VMEM] * 5,
        out_specs=(VMEM,) * 5,
        compiler_params=pltpu.CompilerParams(vmem_limit_bytes=40 * MIB),
        name="update_moments",
    )(head, sums, qkv_old, out_old, up_old, down_old)


GROUP = 3
GRAM_AXES = ("far", "near", "x")


def gram_kernel(moment, out, part, came_one, came_two, came_three, high, low, send_sem, recv_sem):
    z, x, y, core = position()
    here = {"far": z // 2, "near": z % 2, "x": x}
    others = {
        "far": device(flip_z(z, 2), x, y, core),
        "near": device(flip_z(z, 1), x, y, core),
        "x": device(z, 1 - x, y, core),
    }
    greet(list(others.values()))
    blocks = sub_blocks(moment.shape[0])
    groups = len(blocks) // GROUP
    high[...] = moment[...].astype(bf16)
    low[...] = (moment[...] - high[...].astype(f32)).astype(bf16)
    started = []

    def product(index):
        i, j = blocks[index]
        left, right = pl.ds(i * SUB, SUB), pl.ds(j * SUB, SUB)
        total = dot(high[left, :], high[right, :], 1, 1)
        total = total + dot(high[left, :], low[right, :], 1, 1)
        total = total + dot(low[left, :], high[right, :], 1, 1)
        rows = SUB // 8
        for owner in range(8):
            cell = (owner // 4, owner // 2 % 2, owner % 2)
            part[(index // GROUP,) + cell + (index % GROUP,)] = total[
                owner * rows : (owner + 1) * rows
            ]

    def send(source, target, group, slot, axis):
        copy = pltpu.make_async_remote_copy(
            src_ref=source,
            dst_ref=target,
            send_sem=send_sem.at[group, slot],
            recv_sem=recv_sem.at[group, slot],
            device_id=others[axis],
            device_id_type=MESH,
        )
        copy.start()
        started.append(copy)
        return copy

    def cells(fixed, flipped=None):
        return tuple(
            1 - here[name] if name == flipped else here[name] if name in fixed else slice(None)
            for name in GRAM_AXES
        )

    class Walk:
        def __init__(self, group, order):
            self.group, self.order, self.stage = group, order, 0
            self.part = part.at[group]
            self.came = (came_one.at[group], came_two.at[group], came_three.at[group])

        def advance(self):
            stage, order = self.stage, self.order
            mine = pl.ds(self.group * GROUP, GROUP)
            if stage:
                self.copy.wait_recv()
            if 1 <= stage <= 3:
                kept = cells(order[:stage])
                total = self.part[kept] + self.came[stage - 1][...]
                if stage == 3:
                    out[kept + (mine,)] = total
                else:
                    self.part[kept] = total
            if stage < 3:
                source = self.part.at[cells(order[:stage], order[stage])]
                self.copy = send(source, self.came[stage], self.group, stage, order[stage])
            elif stage < 6:
                block = out.at[cells(order[: 6 - stage]) + (mine,)]
                self.copy = send(block, block, self.group, stage, order[5 - stage])
            self.stage += 1

    walks = []
    for group in range(groups):
        for index in range(group * GROUP, (group + 1) * GROUP):
            product(index)
        order = ("near", "far", "x") if group == 1 else ("x", "near", "far")
        walks.append(Walk(group, order))
        walks[-1].advance()
    for turn in range(groups + 5):
        for group, walk in enumerate(walks):
            if 0 <= turn - group < 6:
                walk.advance()
    for copy in started:
        copy.wait_send()


def gram_sum(moment):
    size, cols = moment.shape
    count = len(sub_blocks(size))
    groups = count // GROUP
    rows = (SUB // 8, SUB)
    return pl.pallas_call(
        gram_kernel,
        out_shape=jax.ShapeDtypeStruct((2, 2, 2, count) + rows, f32),
        in_specs=[VMEM],
        out_specs=VMEM,
        scratch_shapes=[
            pltpu.VMEM((groups, 2, 2, 2, GROUP) + rows, f32),
            pltpu.VMEM((groups, 2, 2, GROUP) + rows, f32),
            pltpu.VMEM((groups, 2, GROUP) + rows, f32),
            pltpu.VMEM((groups, GROUP) + rows, f32),
            pltpu.VMEM((size, cols), bf16),
            pltpu.VMEM((size, cols), bf16),
            pltpu.SemaphoreType.DMA((groups, 6)),
            pltpu.SemaphoreType.DMA((groups, 6)),
        ],
        compiler_params=pltpu.CompilerParams(
            vmem_limit_bytes=32 * MIB, collective_id=1, has_side_effects=True
        ),
        name="gram_sum",
    )(moment).reshape((8, count) + rows)


STRIPS = 2


def share_kernel(mine, out, send_sem, recv_sem):
    z, x, y, core = position()
    beyond = device(z, x, 1 - y, core)
    partner = device(z, x, y, 1 - core)
    greet([beyond, partner])
    own = 2 * y + core
    far = 2 * (1 - y) + core
    out[own] = mine[...]
    rows = mine.shape[0] // STRIPS
    started = []

    def send(slot, strip, kind, other):
        block = out.at[slot, pl.ds(strip * rows, rows)]
        copy = pltpu.make_async_remote_copy(
            src_ref=block,
            dst_ref=block,
            send_sem=send_sem.at[strip, kind],
            recv_sem=recv_sem.at[strip, kind],
            device_id=other,
            device_id_type=MESH,
        )
        copy.start()
        started.append(copy)
        return copy

    across = [send(own, strip, 0, beyond) for strip in range(STRIPS)]
    late = [send(own, strip, 1, partner) for strip in range(STRIPS)]
    for strip, copy in enumerate(across):
        copy.wait_recv()
        late.append(send(far, strip, 2, partner))
    for copy in late:
        copy.wait_recv()
    for copy in started:
        copy.wait_send()


def share_factors(mine):
    return pl.pallas_call(
        share_kernel,
        out_shape=jax.ShapeDtypeStruct((4,) + mine.shape, bf16),
        in_specs=[VMEM],
        out_specs=VMEM,
        scratch_shapes=[
            pltpu.SemaphoreType.DMA((STRIPS, 3)),
            pltpu.SemaphoreType.DMA((STRIPS, 3)),
        ],
        compiler_params=pltpu.CompilerParams(
            vmem_limit_bytes=16 * MIB, collective_id=2, has_side_effects=True
        ),
        name="share_factors",
    )(mine)


def finish_kernel(factors, qkv_old, out_old, up_old, down_old, qkv_new, out_new, up_new, down_new):
    shrink = 1.0 - muon_rate * muon_decay
    qkv_cols = qkv_new.shape[0]

    def step(index, rate):
        return muon_rate * rate * factors[index].astype(f32)

    qkv_new[...] = qkv_old[...].astype(f32) * shrink - step(0, math.sqrt(3.0)).T[:qkv_cols]
    out_new[...] = out_old[...].astype(f32) * shrink - step(1, 1.0).T[qkv_cols:]
    up_new[...] = up_old[...].astype(f32) * shrink - step(2, math.sqrt(max(1.0, FF / D)))
    down_new[...] = down_old[...].astype(f32) * shrink - step(3, 1.0).T


def finish_weights(factors, old_weights):
    return pl.pallas_call(
        finish_kernel,
        out_shape=tuple(jax.ShapeDtypeStruct(old.shape, f32) for old in old_weights),
        in_specs=[VMEM] * 5,
        out_specs=(VMEM,) * 4,
        compiler_params=pltpu.CompilerParams(vmem_limit_bytes=32 * MIB),
        name="finish_weights",
    )(factors, *old_weights)


def swap(value, axis, bit):
    size = lax.axis_size(axis)
    return lax.ppermute(value, axis, [(i, i ^ bit) for i in range(size)])


def scatter_head(value, bit, position):
    half = value.shape[1] // 2
    mine = lax.dynamic_slice_in_dim(value, position * half, half, 1)
    other = lax.dynamic_slice_in_dim(value, (1 - position) * half, half, 1)
    return (mine.astype(f32) + swap(other, "head", bit).astype(f32)).astype(bf16)


def scatter_dp_pair(value, position):
    paired = value.reshape((value.shape[0] // 2, 2) + value.shape[1:])
    mine = lax.dynamic_index_in_dim(paired, position, 1, False)
    other = lax.dynamic_index_in_dim(paired, 1 - position, 1, False)
    return (mine.astype(f32) + swap(other, "dp", 1).astype(f32)).astype(bf16)


def scatter_dp_rest(value, place):
    ranks = value.shape[0]
    total = lax.dynamic_index_in_dim(value, place, 0, False).astype(f32)
    for step in range(1, ranks):
        sent = lax.dynamic_index_in_dim(value, place ^ step, 0, False)
        total = total + swap(sent, "dp", 2 * step).astype(f32)
    return total


def local(
    tokens,
    cotangent,
    qkv_weight,
    out_weight,
    up_weight,
    down_weight,
    vectors,
    qkv_moment,
    out_moment,
    up_moment,
    down_moment,
    adam_first,
    adam_second,
    bucket_class,
    row_lengths,
):
    n_dp = lax.axis_size("dp")
    n_head = lax.axis_size("head")
    dp_id = lax.axis_index("dp")
    head_id = lax.axis_index("head")
    core, side = head_id % 2, head_id // 2
    tok, width = tokens.shape
    hidden = up_weight.shape[1]
    half = width // 2
    qkv_cols, out_cols = qkv_moment.shape[1], out_moment.shape[1]
    shrink = 1.0 - muon_rate * muon_decay

    def weight_block(weight, cols, dim):
        return lax.dynamic_slice_in_dim(weight, dp_id * cols, cols, dim)

    old_weights = [
        weight_block(qkv_weight, qkv_cols, 1),
        weight_block(out_weight, out_cols, 1),
        weight_block(up_weight, up_moment.shape[1], 1),
        weight_block(down_weight, down_moment.shape[1], 0),
    ]

    block = head_id.astype(jnp.int32)[None]
    vec_len = vectors.shape[0] // n_dp
    if (n_dp, n_head, tok) == (8, 4, 256):
        mixed, input_grad, sums, vec = layer(
            bucket_class,
            row_lengths,
            tokens,
            cotangent,
            vectors,
            qkv_weight,
            out_weight,
            up_weight,
            down_weight,
        )
        grad_vec = vec[:VEC_BLOCK].reshape(vec_len)
        *moments, chosen = update_moments(
            block, sums.reshape(3, width, -1), qkv_moment.T, out_moment.T, up_moment, down_moment
        )
        factors = share_factors(orthogonalize(gram_sum(chosen), chosen))
        new_weights = finish_weights(
            factors, [old_weights[0].T, old_weights[1].T, old_weights[2], old_weights[3]]
        )
        moments = [moments[0].T, moments[1].T, *moments[2:]]
        new_weights = [new_weights[0].T, new_weights[1].T, *new_weights[2:]]
    else:
        pieces = split_vectors(vectors, width, hidden)
        bias_query, bias_value, bias_out, gain_one, shift_one = pieces[:5]
        bias_up, bias_down, gain_two, shift_two = pieces[5:]
        bias_qkv = jnp.concatenate([bias_query, jnp.zeros_like(bias_query), bias_value])

        def column_half(value, which):
            return lax.dynamic_slice_in_dim(value, which * half, half, 1)

        qkv = (dot(tokens, qkv_weight, 1, 0) + bias_qkv).astype(bf16)
        other = swap(qkv[:, width:], "head", 1)
        attended = attend(block, bucket_class, row_lengths, qkv, other)
        attn_val = dot(attended, out_weight, 1, 0) + bias_out
        resid_one = tokens.astype(f32) + attn_val
        centre = resid_one - jnp.mean(resid_one, axis=-1, keepdims=True)
        rstd_one = lax.rsqrt(jnp.mean(centre * centre, axis=-1, keepdims=True) + norm_eps)
        zhat_one = centre * rstd_one
        normed_one = zhat_one * gain_one + shift_one
        normed_low = normed_one.astype(bf16)
        up_val = dot(normed_low, up_weight, 1, 0) + bias_up
        phi_cum = 0.5 * (1.0 + lax.erf(up_val * (0.5**0.5)))
        active_low = (up_val * phi_cum).astype(bf16)
        slope = phi_cum + up_val * jnp.exp(-0.5 * up_val * up_val) * (1.0 / math.sqrt(2.0 * math.pi))
        down_val = dot(active_low, down_weight, 1, 0) + bias_down
        resid_two = normed_one + down_val
        centre = resid_two - jnp.mean(resid_two, axis=-1, keepdims=True)
        rstd_two = lax.rsqrt(jnp.mean(centre * centre, axis=-1, keepdims=True) + norm_eps)
        zhat_two = centre * rstd_two
        mixed = zhat_two * gain_two + shift_two

        def norm_back(grad, gain, zhat, rstd):
            inner = grad * gain
            mean = jnp.mean(inner, axis=-1, keepdims=True)
            slant = jnp.mean(inner * zhat, axis=-1, keepdims=True)
            return (inner - mean - zhat * slant) * rstd, jnp.sum(grad * zhat, axis=0), jnp.sum(grad, axis=0)

        grad_two, grad_gain_two, grad_shift_two = norm_back(
            cotangent.astype(f32), gain_two, zhat_two, rstd_two
        )
        grad_down_low = grad_two.astype(bf16)
        grad_bias_down = jnp.sum(grad_down_low, axis=0, dtype=f32)

        x_id, z_id = dp_id % 2, dp_id // 2

        grad_up_low = (dot(grad_down_low, down_weight, 1, 1) * slope).astype(bf16)
        grad_bias_up = jnp.sum(grad_up_low, axis=0, dtype=f32)
        grad_normed = grad_two + dot(grad_up_low, up_weight, 1, 1)
        grad_one, grad_gain_one, grad_shift_one = norm_back(grad_normed, gain_one, zhat_one, rstd_one)
        grad_attn_low = grad_one.astype(bf16)
        grad_bias_out = jnp.sum(grad_attn_low, axis=0, dtype=f32)
        grad_heads = dot(grad_attn_low, out_weight, 1, 1).astype(bf16)
        grad_query, own, sent = attend_back(block, bucket_class, row_lengths, qkv, other, grad_heads)
        grad_kv = (own + swap(sent, "head", 1).astype(f32)).astype(bf16)
        grad_qkv = jnp.concatenate([grad_query, grad_kv], axis=1)
        grad_bias_qkv = jnp.sum(grad_qkv, axis=0, dtype=f32)
        input_grad = grad_one + dot(grad_qkv, qkv_weight, 1, 1)
        grad_vector = jnp.concatenate(
            [
                grad_bias_qkv[:width],
                grad_bias_qkv[2 * width :],
                grad_bias_out,
                grad_gain_one,
                grad_shift_one,
                grad_bias_up,
                grad_bias_down,
                grad_gain_two,
                grad_shift_two,
            ]
        )
        grad_vector = grad_vector + swap(grad_vector, "head", 1)
        wides = [active_low, grad_up_low, grad_attn_low, grad_qkv]
        narrows = [grad_down_low, normed_low, attended, tokens]

        def both_halves(value):
            return jnp.concatenate(
                [column_half(value, core), swap(column_half(value, 1 - core), "head", 1)], axis=0
            )

        def weight_grad(wide, narrow):
            wide = jnp.concatenate([wide, swap(wide, "head", 1)], axis=0)
            value = dot(wide, both_halves(narrow), 0, 0).astype(bf16)
            return value.reshape(n_dp, value.shape[0] // n_dp, half)

        def reduce_y_first(value):
            return scatter_dp_rest(scatter_dp_pair(scatter_head(value, 2, side), x_id), z_id)

        def reduce_x_first(value):
            return scatter_dp_rest(scatter_head(scatter_dp_pair(value, x_id), 2, side), z_id)

        def spread(value):
            value = value.astype(bf16)
            came = swap(value, "head", 2)
            value = jnp.concatenate(
                [jnp.where(side == 0, value, came), jnp.where(side == 0, came, value)], axis=0
            )
            came = swap(value, "head", 1)
            return jnp.concatenate(
                [jnp.where(core == 0, value, came), jnp.where(core == 0, came, value)], axis=1
            ).astype(f32)

        down_part, up_part, out_part, qkv_part = [
            weight_grad(wide, narrow) for wide, narrow in zip(wides, narrows)
        ]
        vec_rows = 16
        vec_part = grad_vector.reshape(n_dp, vec_len)
        vec_part = jnp.pad(vec_part, ((0, 0), (0, vec_rows * width - vec_len)))
        vec_part = vec_part.reshape(n_dp, vec_rows, width)
        vec_part = lax.dynamic_slice_in_dim(vec_part, core * half, half, 2).astype(bf16)
        down_new = spread(reduce_x_first(down_part))
        up_new = spread(reduce_y_first(up_part))
        tail_new = spread(
            reduce_y_first(jnp.concatenate([qkv_part, out_part, vec_part], axis=1))
        )
        grads = [
            tail_new[:qkv_cols].T,
            tail_new[qkv_cols : qkv_cols + out_cols].T,
            up_new.T,
            down_new.T,
        ]
        grad_vec = tail_new[qkv_cols + out_cols :].reshape(-1)[:vec_len]
        moments = [
            muon_keep * old + grad
            for old, grad in zip([qkv_moment, out_moment, up_moment, down_moment], grads)
        ]
        most = max(m.shape[1] for m in moments)
        padded = [jnp.pad(m, ((0, 0), (0, most - m.shape[1]))) for m in moments]
        chosen = padded[-1]
        for index in range(len(padded) - 2, -1, -1):
            chosen = jnp.where(head_id == index, padded[index], chosen)
        gram_mat = lax.dot_general(
            chosen, chosen, (((1,), (1,)), ((), ())), precision=lax.Precision.HIGH
        )
        own_factor = orthogonalize(lax.psum(gram_mat, "dp"), chosen)
        across = swap(own_factor, "head", 2)
        low_pair = jnp.where(side == 0, own_factor, across)
        high_pair = jnp.where(side == 0, across, own_factor)
        near_low = swap(low_pair, "head", 1)
        near_high = swap(high_pair, "head", 1)
        factors = [
            jnp.where(core == 0, low_pair, near_low),
            jnp.where(core == 0, near_low, low_pair),
            jnp.where(core == 0, high_pair, near_high),
            jnp.where(core == 0, near_high, high_pair),
        ]
        factors = [o[:, : m.shape[1]].astype(f32) for o, m in zip(factors, moments)]
        factors[3] = factors[3].T
        rates = (math.sqrt(3.0), 1.0, math.sqrt(max(1.0, hidden / width)), 1.0)
        new_weights = [
            old.astype(f32) * shrink - muon_rate * rate * factor
            for old, rate, factor in zip(old_weights, rates, factors)
        ]

    vec_old = lax.dynamic_slice_in_dim(vectors, dp_id * vec_len, vec_len, 0)
    vec_first = beta_first * adam_first + (1.0 - beta_first) * grad_vec
    vec_second = beta_second * adam_second + (1.0 - beta_second) * grad_vec * grad_vec
    first_hat = vec_first / (1.0 - beta_first**STEP)
    second_hat = vec_second / (1.0 - beta_second**STEP)
    vec_new = vec_old - adam_rate * first_hat / (jnp.sqrt(second_hat) + adam_eps)
    return (mixed, input_grad, *moments, *new_weights, vec_first, vec_second, vec_new)


def solution(mesh):
    tokens_spec = P(("dp", "head"), None)
    block_spec = P(None, "dp")
    return jax.shard_map(
        local,
        mesh=mesh,
        in_specs=(
            tokens_spec,
            tokens_spec,
            P(),
            P(),
            P(),
            P(),
            P(),
            block_spec,
            block_spec,
            block_spec,
            block_spec,
            P("dp"),
            P("dp"),
            P("dp"),
            P("dp", None),
        ),
        out_specs=(
            tokens_spec,
            tokens_spec,
            block_spec,
            block_spec,
            block_spec,
            block_spec,
            block_spec,
            block_spec,
            block_spec,
            P("dp", None),
            P("dp"),
            P("dp"),
            P("dp"),
        ),
        check_vma=False,
    )
```

```python
import functools
import itertools
import math

import jax
import jax.numpy as jnp
from jax import lax
from jax.experimental import pallas as pl
from jax.experimental.pallas import tpu as pltpu
from jax.sharding import PartitionSpec as P

D = 768
HEADS = 12
HEAD_DIM = 64
FF = 3072
BASE_LEN = 128
NS_STEPS = 5
STEP = 5
MAX_LEN = 512

f32 = jnp.float32
bf16 = jnp.bfloat16

norm_eps = 1e-12
masked_score = -1000000000.0
quintic_a = 3.4445
quintic_b = -4.775
quintic_c = 2.0315
muon_rate = 1.0
muon_decay = 0.01
muon_keep = 0.5
adam_rate = 0.2
beta_first = 0.9
beta_second = 0.999
adam_eps = 1e-08
MIB = 1024 * 1024


def dot(left, right, left_dim, right_dim):
    return lax.dot_general(
        left, right, (((left_dim,), (right_dim,)), ((), ())), preferred_element_type=f32
    )


def split_vectors(vectors, width, hidden):
    lengths_list = [width] * 5 + [hidden] + [width] * 3
    pieces = []
    offset = 0
    for length in lengths_list:
        pieces.append(vectors[offset : offset + length])
        offset = offset + length
    return pieces


def allowed_mask(class_ref, length_ref, block, tok):
    shift = class_ref[0] + int(math.log2(BASE_LEN))
    query_place = block * tok + lax.broadcasted_iota(jnp.int32, (tok, 1), 0)
    lane = lax.broadcasted_iota(jnp.int32, (1, 2 * tok), 1)
    own = lane < tok
    key_place = jnp.where(own, block * tok + lane, (block ^ 1) * tok + lane - tok)
    key_row = lax.shift_right_logical(key_place, jnp.broadcast_to(shift, key_place.shape))
    offset = key_place - lax.shift_left(key_row, jnp.broadcast_to(shift, key_place.shape))
    row_len = jnp.zeros_like(key_row)
    for slot in range(length_ref.shape[1]):
        row_len = jnp.where(key_row == slot, length_ref[0, slot], row_len)
    key_row = jnp.where(offset < row_len, key_row, -1)
    query_row = lax.shift_right_logical(query_place, jnp.broadcast_to(shift, query_place.shape))
    return query_row == key_row


def half_masks():
    lane = lax.broadcasted_iota(jnp.int32, (1, 2 * HEAD_DIM), 1)
    first = (lane < HEAD_DIM).astype(f32)
    return (first.astype(bf16), (1.0 - first).astype(bf16)), lane < HEAD_DIM


def head_prob(query, keys, allowed):
    score = jnp.where(allowed, dot(query, keys, 1, 1) * HEAD_DIM ** (-0.5), masked_score)
    exponent = jnp.exp(score - jnp.max(score, axis=-1, keepdims=True))
    return exponent / jnp.sum(exponent, axis=-1, keepdims=True)


def attend_kernel(block_ref, class_ref, length_ref, qkv_ref, other_ref, out_ref):
    tok = qkv_ref.shape[0]
    allowed = allowed_mask(class_ref, length_ref, block_ref[0], tok)
    masks, first = half_masks()
    for pair in range(HEADS // 2):
        cols = pl.ds(pair * 2 * HEAD_DIM, 2 * HEAD_DIM)
        kcols = pl.ds(D + pair * 2 * HEAD_DIM, 2 * HEAD_DIM)
        vcols = pl.ds(2 * D + pair * 2 * HEAD_DIM, 2 * HEAD_DIM)
        query = qkv_ref[:, cols]
        keys = jnp.concatenate([qkv_ref[:, kcols], other_ref[:, cols]], axis=0)
        values = jnp.concatenate([qkv_ref[:, vcols], other_ref[:, kcols]], axis=0)
        outs = []
        for mask in masks:
            prob = head_prob(query * mask, keys, allowed)
            outs.append(dot(prob.astype(bf16), values, 1, 0))
        out_ref[:, cols] = jnp.where(first, outs[0], outs[1]).astype(bf16)


def attend_back_kernel(
    block_ref, class_ref, length_ref, qkv_ref, other_ref, grad_ref, dq_ref, own_ref, send_ref
):
    tok = qkv_ref.shape[0]
    allowed = allowed_mask(class_ref, length_ref, block_ref[0], tok)
    masks, first = half_masks()
    scale = HEAD_DIM ** (-0.5)
    for pair in range(HEADS // 2):
        cols = pl.ds(pair * 2 * HEAD_DIM, 2 * HEAD_DIM)
        kcols = pl.ds(D + pair * 2 * HEAD_DIM, 2 * HEAD_DIM)
        vcols = pl.ds(2 * D + pair * 2 * HEAD_DIM, 2 * HEAD_DIM)
        query = qkv_ref[:, cols]
        keys = jnp.concatenate([qkv_ref[:, kcols], other_ref[:, cols]], axis=0)
        values = jnp.concatenate([qkv_ref[:, vcols], other_ref[:, kcols]], axis=0)
        grad = grad_ref[:, cols]
        dqs, dk, dv = [], None, None
        for mask in masks:
            head_query = query * mask
            head_grad = grad * mask
            prob = head_prob(head_query, keys, allowed)
            part_v = dot(prob.astype(bf16), head_grad, 0, 0)
            dprob = dot(head_grad, values, 1, 1)
            dscore = prob * (dprob - jnp.sum(prob * dprob, axis=-1, keepdims=True))
            dscore = dscore.astype(bf16)
            dqs.append(dot(dscore, keys, 1, 0))
            part_k = dot(dscore, head_query, 0, 0)
            dk = part_k if dk is None else dk + part_k
            dv = part_v if dv is None else dv + part_v
        dk = dk * scale
        dq_ref[:, cols] = (jnp.where(first, dqs[0], dqs[1]) * scale).astype(bf16)
        own_ref[:, cols] = dk[:tok]
        own_ref[:, kcols] = dv[:tok]
        send_ref[:, cols] = dk[tok:].astype(bf16)
        send_ref[:, kcols] = dv[tok:].astype(bf16)


SMEM = pl.BlockSpec(memory_space=pltpu.SMEM)
VMEM = pl.BlockSpec(memory_space=pltpu.VMEM)
ANY = pl.BlockSpec(memory_space=pl.ANY)


def attend(block, row_class, lengths, qkv, other):
    tok = qkv.shape[0]
    return pl.pallas_call(
        attend_kernel,
        out_shape=jax.ShapeDtypeStruct((tok, D), bf16),
        in_specs=[SMEM, SMEM, SMEM, VMEM, VMEM],
        out_specs=VMEM,
        compiler_params=pltpu.CompilerParams(vmem_limit_bytes=32 * MIB),
        name="attend",
    )(block, row_class, lengths, qkv, other)


def attend_back(block, row_class, lengths, qkv, other, grad):
    tok = qkv.shape[0]
    return pl.pallas_call(
        attend_back_kernel,
        out_shape=(
            jax.ShapeDtypeStruct((tok, D), bf16),
            jax.ShapeDtypeStruct((tok, 2 * D), f32),
            jax.ShapeDtypeStruct((tok, 2 * D), bf16),
        ),
        in_specs=[SMEM, SMEM, SMEM, VMEM, VMEM, VMEM],
        out_specs=(VMEM, VMEM, VMEM),
        compiler_params=pltpu.CompilerParams(vmem_limit_bytes=32 * MIB),
        name="attend_back",
    )(block, row_class, lengths, qkv, other, grad)


CENTRES = (0.0, 0.0, 0.0, 0.8, 0.8)
TILE = 256
SUB = 128


def sub_blocks(size):
    count = size // SUB
    return [(i, j) for i in range(count) for j in range(i, count)]


def ortho_kernel(packed, gram_ref, moment_ref, out_ref, e, f, g, eb, fb, gb, ya, yb, y):
    size = e.shape[0]
    tiles = [slice(i * TILE, (i + 1) * TILE) for i in range(size // TILE)]

    def unit(rows):
        row_id = rows.start + lax.broadcasted_iota(jnp.int32, (TILE, size), 0)
        col_id = lax.broadcasted_iota(jnp.int32, (TILE, size), 1)
        return (row_id == col_id).astype(f32)

    if packed:
        for index, (i, j) in enumerate(sub_blocks(size)):
            value = gram_ref[:, index].reshape(SUB, SUB)
            e[i * SUB : (i + 1) * SUB, j * SUB : (j + 1) * SUB] = value
            if i != j:
                e[j * SUB : (j + 1) * SUB, i * SUB : (i + 1) * SUB] = value.T
        gram = e
    else:
        gram = gram_ref
    diagonal = jnp.zeros((TILE, size), f32)
    for rows in tiles:
        diagonal = diagonal + gram[rows, :] * unit(rows)
    trace = jnp.sum(jnp.sum(diagonal, axis=0, keepdims=True), axis=1, keepdims=True)
    factor = 1.0 / (jnp.sqrt(trace) + 1e-07)
    square_factor = factor * factor
    for rows in tiles:
        value = gram[rows, :] * square_factor
        e[rows, :] = value
        eb[rows, :] = value.astype(bf16)
        moment = moment_ref[rows, :] * factor
        y[rows, :] = moment
        ya[rows, :] = moment.astype(bf16)
    now, then = ya, yb
    for step in range(NS_STEPS):
        last = step + 1 == NS_STEPS
        centre = CENTRES[step]
        after = 0.0 if last else CENTRES[step + 1]
        keep = quintic_a + quintic_b * centre + quintic_c * centre * centre
        linear = quintic_b + 2.0 * quintic_c * centre
        for rows in tiles:
            value = linear * e[rows, :] + quintic_c * dot(eb[rows, :], eb[...], 1, 0)
            fb[rows, :] = value.astype(bf16)
            if not last:
                f[rows, :] = value
        for rows in tiles:
            value = keep * y[rows, :] + dot(fb[rows, :], now[...], 1, 0)
            if last:
                out_ref[rows, :] = value.astype(out_ref.dtype)
            else:
                y[rows, :] = value
                then[rows, :] = value.astype(bf16)
        if last:
            break
        now, then = then, now
        for rows in tiles:
            value = keep * e[rows, :] + dot(eb[rows, :], fb[...], 1, 0)
            if centre:
                value = value + centre * f[rows, :]
            g[rows, :] = value
            gb[rows, :] = value.astype(bf16)
        for rows in tiles:
            value = keep * g[rows, :] + dot(gb[rows, :], fb[...], 1, 0)
            if centre:
                value = value + (centre * keep) * f[rows, :]
            shift = centre * keep * keep - after
            if shift:
                value = value + shift * unit(rows)
            e[rows, :] = value
            eb[rows, :] = value.astype(bf16)


def orthogonalize(gram_mat, moment):
    size, cols = moment.shape
    square = pltpu.VMEM((size, size), f32)
    square_low = pltpu.VMEM((size, size), bf16)
    return pl.pallas_call(
        functools.partial(ortho_kernel, gram_mat.ndim != 2),
        out_shape=jax.ShapeDtypeStruct((size, cols), bf16),
        in_specs=[VMEM, VMEM],
        out_specs=VMEM,
        scratch_shapes=[
            square,
            square,
            square,
            square_low,
            square_low,
            square_low,
            pltpu.VMEM((size, cols), bf16),
            pltpu.VMEM((size, cols), bf16),
            pltpu.VMEM((size, cols), f32),
        ],
        compiler_params=pltpu.CompilerParams(vmem_limit_bytes=48 * MIB),
        name="ortho",
    )(gram_mat, moment)


MESH = pl.DeviceIdType.MESH
CHUNK = 48
PARTS = 4
UNIT = 2 * PARTS * CHUNK
HALF = D // 2
LANES = 128
VEC_BLOCK = 9
ROWS = 16
CHUNK_ORDERS = (
    "fxyn", "yfnx", "ynxf", "fxny",
    "yxnf", "xfny", "yxnf", "xyfn",
    "yxnf", "xnfy", "nxyf", "xynf",
)
CHUNK_PLAN = (
    (0, 1, 2, 3),
    (),
    (),
    (),
    (),
    (4, 5, 7),
    (1, 2, 6),
    (),
    (),
    (),
    (),
    (4, 5, 7),
    (6,),
    (),
    (4, 7, 2, 6, 0, 3),
    (),
    (2, 1),
    (4, 8, 9, 10, 11),
    (6, 7, 0, 3, 2, 5, 4, 1, 2, 6, 7, 0, 2, 4, 1, 4, 3, 6, 7, 5, 0, 6, 8, 7, 1, 9, 3, 1, 5, 0, 11, 10, 0, 3, 8, 5, 3, 9, 5, 11, 10, 8, 10, 9, 8, 11, 9, 10, 8, 11, 9, 8, 10, 9, 11, 10, 11),
)
BIAS_QUERY, BIAS_VALUE, BIAS_OUT, GAIN_ONE, SHIFT_ONE, BIAS_UP = (i * D for i in range(6))
BIAS_DOWN, GAIN_TWO, SHIFT_TWO = (BIAS_UP + FF + i * D for i in range(3))


def position():
    dp_id, head_id = lax.axis_index("dp"), lax.axis_index("head")
    z, x = dp_id // 2, dp_id % 2
    y, core = head_id // 2, head_id % 2
    return z, x, y, core


def device(z, x, y, core):
    return (2 * z + x, 2 * y + core)


def flip_z(z, step):
    high, low = z // 2, z % 2
    high = 1 - high if step // 2 else high
    low = 1 - low if step % 2 else low
    return 2 * high + low


def greet(others):
    barrier = pltpu.get_barrier_semaphore()
    for other in others:
        pl.semaphore_signal(barrier, inc=1, device_id=other, device_id_type=MESH)
    pl.semaphore_wait(barrier, len(others))


def by_rows(count, body, init=None, together=4):
    def step(index, carry):
        for part in range(together):
            start = (index * together + part) * ROWS
            carry = body(pl.ds(pl.multiple_of(start, ROWS), ROWS), carry)
        return carry

    return lax.fori_loop(0, count // (ROWS * together), step, init)


def row_mean(value):
    return jnp.sum(value, axis=-1, keepdims=True) * (1.0 / D)


def fold(value):
    return jnp.sum(value.reshape(value.shape[0] // 8, 8, value.shape[1]), axis=0)


def column_sum(value):
    return jnp.sum(value, axis=0, keepdims=True)


def layer_kernel(
    row_class,
    lengths,
    tokens,
    cotangent,
    vectors,
    qkv_hbm,
    out_hbm,
    up_hbm,
    down_hbm,
    mixed,
    input_grad,
    sums,
    vec_sum,
    qkv_w,
    out_w,
    up_w,
    down_w,
    query,
    keys_values,
    prob,
    attended,
    normed_low,
    grad_down,
    grad_attn,
    tokens_far,
    attended_far,
    normed_far,
    grad_down_far,
    active,
    active_far,
    grad_up,
    grad_up_far,
    grad_attn_far,
    grad_qkv,
    grad_qkv_far,
    grad_heads,
    slope,
    normed_one,
    zhat_one,
    rstd_one,
    grad_two,
    grad_one,
    work,
    kv_own,
    kv_sent,
    kv_came,
    vec,
    vec_core,
    vec_y,
    vec_x,
    vec_z,
    part,
    came_one,
    came_two,
    came_three,
    came_four,
    load_sem,
    pair_send,
    pair_recv,
    send_sem,
    recv_sem,
):
    z, x, y, core = position()
    tok = tokens.shape[0]
    loads = {
        name: pltpu.make_async_copy(source, target, load_sem.at[index])
        for index, (name, source, target) in enumerate(
            (
                ("qkv", qkv_hbm, qkv_w),
                ("out", out_hbm, out_w),
                ("up", up_hbm, up_w),
                ("down", down_hbm, down_w),
            )
        )
    }
    for load in loads.values():
        load.start()
    beyond = device(z, x, 1 - y, core)
    beside = device(z, 1 - x, y, core)
    partner = device(z, x, y, 1 - core)
    along = [device(flip_z(z, step), x, y, core) for step in (1, 2, 3)]
    greet([beyond, beside, partner] + along)
    started = []

    def remote(source, target, send_at, recv_at, other):
        copy = pltpu.make_async_remote_copy(
            src_ref=source,
            dst_ref=target,
            send_sem=send_at,
            recv_sem=recv_at,
            device_id=other,
            device_id_type=MESH,
        )
        copy.start()
        started.append(copy)
        return copy

    pair_count = []

    def to_partner(source, target):
        slot = len(pair_count)
        pair_count.append(slot)
        return remote(source, target, pair_send.at[slot], pair_recv.at[slot], partner)

    own_half = pl.ds(pl.multiple_of(core * HALF, HALF), HALF)
    other_half = pl.ds(pl.multiple_of((1 - core) * HALF, HALF), HALF)

    def span(start, length=D):
        return vectors[0:1, start : start + length]

    def put_vec(start, value):
        for index in range(value.shape[1] // LANES):
            block, row = divmod(start // LANES + index, VEC_BLOCK)
            vec[block, row : row + 1, :] = value[:, index * LANES : (index + 1) * LANES]

    vec[...] = jnp.zeros_like(vec)

    loads["qkv"].wait()
    tokens_came = to_partner(tokens.at[:, other_half], tokens_far)
    own_rows = pl.ds(0, tok)
    far_rows = pl.ds(tok, tok)
    for index, start in ((1, None), (2, BIAS_VALUE)):
        value = dot(tokens[...], qkv_w[:, index * D : (index + 1) * D], 1, 0)
        if start is not None:
            value = value + span(start)
        keys_values[own_rows, (index - 1) * D : index * D] = value.astype(bf16)
    kv_arrived = to_partner(keys_values.at[own_rows], keys_values.at[far_rows])
    value = dot(tokens[...], qkv_w[:, :D], 1, 0) + span(BIAS_QUERY)
    query[...] = value.astype(bf16)
    allowed = allowed_mask(row_class, lengths, 2 * y + core, tok)
    masks, first = half_masks()
    kv_arrived.wait_recv()

    scale = HEAD_DIM ** (-0.5)
    for pair in range(HEADS // 2):
        cols = slice(pair * LANES, (pair + 1) * LANES)
        keys = keys_values[:, cols]
        values = keys_values[:, D + cols.start : D + cols.stop]
        outs = []
        for side, mask in enumerate(masks):
            score = dot(query[:, cols] * (mask * scale), keys, 1, 1)
            score = jnp.where(allowed, score, masked_score)
            exponent = jnp.exp(score - jnp.max(score, axis=-1, keepdims=True))
            chance = exponent * (1.0 / jnp.sum(exponent, axis=-1, keepdims=True))
            prob[2 * pair + side] = chance
            outs.append(dot(chance.astype(bf16), values, 1, 0))
        attended[:, cols] = jnp.where(first, outs[0], outs[1]).astype(bf16)
    attended_came = to_partner(attended.at[:, other_half], attended_far)

    loads["out"].wait()
    work[...] = dot(attended[...], out_w[...], 1, 0)

    def norm_one(rows, carry):
        value = tokens[rows, :].astype(f32) + (work[rows, :] + span(BIAS_OUT))
        centre = value - row_mean(value)
        rstd = lax.rsqrt(row_mean(centre * centre) + norm_eps)
        zhat = centre * rstd
        normed = zhat * span(GAIN_ONE) + span(SHIFT_ONE)
        zhat_one[rows, :] = zhat
        rstd_one[rows, :] = jnp.broadcast_to(rstd, (ROWS, LANES))
        normed_one[rows, :] = normed
        normed_low[rows, :] = normed.astype(bf16)
        return carry

    by_rows(tok, norm_one)
    normed_came = to_partner(normed_low.at[:, other_half], normed_far)

    loads["up"].wait()
    for tile in range(FF // D):
        cols = slice(tile * D, (tile + 1) * D)
        work[...] = dot(normed_low[...], up_w[:, cols], 1, 0)

        def gelu(rows, carry):
            value = work[rows, :] + span(BIAS_UP + cols.start)
            chance = 0.5 * (1.0 + lax.erf(value * (0.5**0.5)))
            active[rows, cols] = (value * chance).astype(bf16)
            density = jnp.exp(-0.5 * value * value) * (1.0 / math.sqrt(2.0 * math.pi))
            slope[rows, cols] = chance + value * density
            return carry

        by_rows(tok, gelu)
    active_came = to_partner(active, active_far)
    loads["down"].wait()
    work[...] = dot(active[...], down_w[...], 1, 0)

    def norm_two(rows, carry):
        value = normed_one[rows, :] + (work[rows, :] + span(BIAS_DOWN))
        centre = value - row_mean(value)
        rstd = lax.rsqrt(row_mean(centre * centre) + norm_eps)
        zhat = centre * rstd
        mixed[rows, :] = zhat * span(GAIN_TWO) + span(SHIFT_TWO)
        grad = cotangent[rows, :].astype(f32)
        inner = grad * span(GAIN_TWO)
        grad_in = (inner - row_mean(inner) - zhat * row_mean(inner * zhat)) * rstd
        grad_two[rows, :] = grad_in
        low = grad_in.astype(bf16)
        grad_down[rows, :] = low
        gain, shift, bias = carry
        return gain + fold(grad * zhat), shift + fold(grad), bias + fold(low.astype(f32))

    zero = jnp.zeros((8, D), f32)
    gain, shift, bias = by_rows(tok, norm_two, (zero, zero, zero))
    put_vec(GAIN_TWO, column_sum(gain))
    put_vec(SHIFT_TWO, column_sum(shift))
    put_vec(BIAS_DOWN, column_sum(bias))
    grad_down_came = to_partner(grad_down.at[:, other_half], grad_down_far)

    here = {"f": z // 2, "n": z % 2, "x": x, "y": y}
    across = {"f": along[1], "n": along[0], "x": beside, "y": beyond}

    class Chain:
        def __init__(self, index):
            matrix, quarter = divmod(index, PARTS)
            self.index, self.order, self.stage = index, CHUNK_ORDERS[index], 0
            self.own = part.at[matrix, quarter]
            self.came = [ref.at[matrix, quarter] for ref in (came_one, came_two, came_three, came_four)]
            self.final = sums.at[matrix, :, :, quarter]

        def cells(self, free, flipped=None):
            return tuple(
                slice(None) if name in free else 1 - here[name] if name == flipped else here[name]
                for name in "fnxy"
            )

        def send(self, source, target, other):
            sems = (send_sem.at[self.index, self.stage], recv_sem.at[self.index, self.stage])
            self.copy = remote(source, target, *sems, other)

        def advance(self):
            stage, order = self.stage, self.order
            if stage:
                self.copy.wait_recv()
            if 1 <= stage <= 4:
                free = order[stage:]
                for choice in itertools.product((0, 1), repeat=len(free)):
                    taken = dict(zip(sorted(free, key="fnxy".index), choice))
                    at = tuple(taken.get(name, here[name]) for name in "fnxy")
                    value = self.own[at] + self.came[stage - 1][choice]
                    if stage == 4:
                        self.final[core, y] = value
                    else:
                        self.own[at] = value
            if stage < 4:
                name = order[stage]
                source = self.own.at[self.cells(order[stage + 1 :], name)]
                self.send(source, self.came[stage], across[name])
            elif stage == 4:
                block = self.final.at[core, y]
                self.send(block, block, beyond)
            elif stage == 5:
                block = self.final.at[core]
                self.send(block, block, partner)
            self.stage += 1

    chains = [Chain(index) for index in range(3 * PARTS)]
    plan = iter(CHUNK_PLAN)

    def pump():
        for index in next(plan):
            chains[index].advance()

    def feed_forward(matrix, narrow, narrow_far, wide, wide_far):
        left = narrow[:, own_half].astype(f32).T.astype(bf16)
        left_far = narrow_far[...].astype(f32).T.astype(bf16)

        def block(index, carry):
            cols = pl.ds(pl.multiple_of(index * UNIT, UNIT), UNIT)
            value = dot(left, wide[:, cols], 1, 0) + dot(left_far, wide_far[:, cols], 1, 0)
            value = value.astype(bf16)
            for side in range(2):
                for quarter in range(PARTS):
                    start = (side * PARTS + quarter) * CHUNK
                    part[matrix, quarter, index // 4, index // 2 % 2, index % 2, side] = value[
                        start : start + CHUNK
                    ]
            return carry

        lax.fori_loop(0, 8, block, 0)

    def projections(matrix, wide, wide_far, narrow, narrow_far, width, offset, between=None):
        for tile in range(wide.shape[1] // UNIT):
            if between and tile % 2 == 0:
                between()
            cols = slice(tile * UNIT, (tile + 1) * UNIT)
            value = dot(wide[:, cols], narrow[:, own_half], 0, 0)
            value = value + dot(wide_far[:, cols], narrow_far[...], 0, 0)
            value = value.astype(bf16)
            for start in range(0, UNIT, CHUNK):
                block, row = divmod(tile * UNIT + start, width)
                side, row = divmod(offset + row, PARTS * CHUNK)
                part[matrix, row // CHUNK, block // 4, block // 2 % 2, block % 2, side] = value[
                    start : start + CHUNK
                ]

    grad_down_came.wait_recv()
    active_came.wait_recv()
    feed_forward(0, grad_down, grad_down_far, active, active_far)

    for tile in range(FF // D):
        pump()
        cols = slice(tile * D, (tile + 1) * D)
        work[...] = dot(grad_down[...], down_w[cols, :], 1, 1)

        def gelu_back(rows, carry):
            low = (work[rows, :] * slope[rows, cols]).astype(bf16)
            grad_up[rows, cols] = low
            return carry + fold(low.astype(f32))

        put_vec(BIAS_UP + cols.start, column_sum(by_rows(tok, gelu_back, zero)))
    grad_up_came = to_partner(grad_up, grad_up_far)
    pump()
    normed_came.wait_recv()
    grad_up_came.wait_recv()
    feed_forward(1, normed_low, normed_far, grad_up, grad_up_far)
    pump()

    work[...] = dot(grad_up[...], up_w[...], 1, 1)

    def norm_one_back(rows, carry):
        grad = grad_two[rows, :] + work[rows, :]
        zhat = zhat_one[rows, :]
        inner = grad * span(GAIN_ONE)
        grad_in = inner - row_mean(inner) - zhat * row_mean(inner * zhat)
        grad_in = grad_in * rstd_one[rows, 0:1]
        grad_one[rows, :] = grad_in
        low = grad_in.astype(bf16)
        grad_attn[rows, :] = low
        gain, shift, bias = carry
        return gain + fold(grad * zhat), shift + fold(grad), bias + fold(low.astype(f32))

    gain, shift, bias = by_rows(tok, norm_one_back, (zero, zero, zero))
    put_vec(GAIN_ONE, column_sum(gain))
    put_vec(SHIFT_ONE, column_sum(shift))
    put_vec(BIAS_OUT, column_sum(bias))
    grad_attn_came = to_partner(grad_attn, grad_attn_far)
    grad_heads[...] = dot(grad_attn[...], out_w[...], 1, 1).astype(bf16)

    for pair in range(HEADS // 2):
        pump()
        cols = slice(pair * LANES, (pair + 1) * LANES)
        value_cols = slice(D + cols.start, D + cols.stop)
        keys = keys_values[:, cols]
        values = keys_values[:, value_cols]
        queries_grad, keys_grad, values_grad = [], None, None
        for side, mask in enumerate(masks):
            head_query = query[:, cols] * mask
            head_grad = grad_heads[:, cols] * mask
            chance = prob[2 * pair + side]
            part_v = dot(chance.astype(bf16), head_grad, 0, 0)
            grad_chance = dot(head_grad, values, 1, 1)
            mean = jnp.sum(chance * grad_chance, axis=-1, keepdims=True)
            grad_score = (chance * (grad_chance - mean)).astype(bf16)
            queries_grad.append(dot(grad_score, keys, 1, 0))
            part_k = dot(grad_score, head_query, 0, 0)
            keys_grad = part_k if side == 0 else keys_grad + part_k
            values_grad = part_v if side == 0 else values_grad + part_v
        keys_grad = keys_grad * scale
        grad_query = jnp.where(first, queries_grad[0], queries_grad[1]) * scale
        grad_qkv[:, cols] = grad_query.astype(bf16)
        kv_own[:, cols] = keys_grad[:tok]
        kv_own[:, value_cols] = values_grad[:tok]
        kv_sent[:, cols] = keys_grad[tok:].astype(bf16)
        kv_sent[:, value_cols] = values_grad[tok:].astype(bf16)
    kv_grad_came = to_partner(kv_sent, kv_came)
    pump()
    grad_attn_came.wait_recv()
    attended_came.wait_recv()
    projections(2, grad_attn, grad_attn_far, attended, attended_far, D // 8, 3 * D // 8)
    kv_grad_came.wait_recv()
    pump()

    def join(rows, carry):
        grad_qkv[rows, D:] = (kv_own[rows, :] + kv_came[rows, :].astype(f32)).astype(bf16)
        return carry

    by_rows(tok, join)
    grad_qkv_came = to_partner(grad_qkv, grad_qkv_far)

    def query_bias(rows, carry):
        return carry + fold(grad_qkv[rows, :D].astype(f32))

    def value_bias(rows, carry):
        return carry + fold(grad_qkv[rows, 2 * D :].astype(f32))

    put_vec(BIAS_QUERY, column_sum(by_rows(tok, query_bias, zero)))
    put_vec(BIAS_VALUE, column_sum(by_rows(tok, value_bias, zero)))
    vec_came = to_partner(vec, vec_core)
    tokens_came.wait_recv()
    grad_qkv_came.wait_recv()
    projections(2, grad_qkv, grad_qkv_far, tokens, tokens_far, 3 * D // 8, 0, pump)
    pump()

    value = dot(grad_qkv[...], qkv_w[...], 1, 1)
    input_grad[...] = grad_one[...] + value

    vec_slots = [(send_sem.at[3 * PARTS, i], recv_sem.at[3 * PARTS, i]) for i in range(5)]

    def vec_steps():
        vec_came.wait_recv()
        vec_core[...] = vec[...] + vec_core[...]
        copy = remote(vec_core, vec_y, *vec_slots[0], beyond)
        yield
        copy.wait_recv()
        for i in range(4):
            vec_x[0, i] = vec_core[2 * i + x] + vec_y[2 * i + x]
            vec_x[1, i] = vec_core[2 * i + 1 - x] + vec_y[2 * i + 1 - x]
        copy = remote(vec_x.at[1], vec_x.at[2], *vec_slots[1], beside)
        yield
        copy.wait_recv()
        vec_x[0] = vec_x[0] + vec_x[2]
        copies = [
            remote(
                vec_x.at[0, flip_z(z, step)],
                vec_z.at[step - 1],
                *vec_slots[1 + step],
                along[step - 1],
            )
            for step in (1, 2, 3)
        ]
        yield
        total = vec_x[0, z]
        for step, copy in enumerate(copies):
            copy.wait_recv()
            total = total + vec_z[step]
        vec_sum[...] = total
        yield

    steps = vec_steps()
    for turn, index in enumerate(next(plan)):
        chains[index].advance()
        if turn % 10 == 9 and turn < 40:
            next(steps)
    for copy in started:
        copy.wait_send()


def layer(row_class, lengths, tokens, cotangent, vectors, qkv_w, out_w, up_w, down_w):
    tok = tokens.shape[0]
    chunk = (CHUNK, UNIT)

    def low(*dims):
        return pltpu.VMEM(dims, bf16)

    def wide(*dims):
        return pltpu.VMEM(dims, f32)

    return pl.pallas_call(
        layer_kernel,
        out_shape=(
            jax.ShapeDtypeStruct((tok, D), f32),
            jax.ShapeDtypeStruct((tok, D), f32),
            jax.ShapeDtypeStruct((3, 2, 2, PARTS) + chunk, bf16),
            jax.ShapeDtypeStruct((16, LANES), f32),
        ),
        in_specs=[SMEM, SMEM, VMEM, VMEM, VMEM] + [ANY] * 4,
        out_specs=(VMEM,) * 4,
        scratch_shapes=[
            low(D, 3 * D),
            low(D, D),
            low(D, FF),
            low(FF, D),
            low(tok, D),
            low(2 * tok, 2 * D),
            wide(HEADS, tok, 2 * tok),
            low(tok, D),
            low(tok, D),
            low(tok, D),
            low(tok, D),
            low(tok, HALF),
            low(tok, HALF),
            low(tok, HALF),
            low(tok, HALF),
            low(tok, FF),
            low(tok, FF),
            low(tok, FF),
            low(tok, FF),
            low(tok, D),
            low(tok, 3 * D),
            low(tok, 3 * D),
            low(tok, D),
            wide(tok, FF),
            wide(tok, D),
            wide(tok, D),
            wide(tok, LANES),
            wide(tok, D),
            wide(tok, D),
            wide(tok, D),
            wide(tok, 2 * D),
            low(tok, 2 * D),
            low(tok, 2 * D),
            wide(8, 16, LANES),
            wide(8, 16, LANES),
            wide(8, 16, LANES),
            wide(3, 4, 16, LANES),
            wide(3, 16, LANES),
            low(3, PARTS, 2, 2, 2, 2, *chunk),
            low(3, PARTS, 2, 2, 2, *chunk),
            low(3, PARTS, 2, 2, *chunk),
            low(3, PARTS, 2, *chunk),
            low(3, PARTS, *chunk),
            pltpu.SemaphoreType.DMA((4,)),
            pltpu.SemaphoreType.DMA((11,)),
            pltpu.SemaphoreType.DMA((11,)),
            pltpu.SemaphoreType.DMA((3 * PARTS + 1, 6)),
            pltpu.SemaphoreType.DMA((3 * PARTS + 1, 6)),
        ],
        compiler_params=pltpu.CompilerParams(
            vmem_limit_bytes=63 * MIB, collective_id=0, has_side_effects=True
        ),
        name="layer",
    )(row_class, lengths, tokens, cotangent, vectors[None, :], qkv_w, out_w, up_w, down_w)


def update_kernel(
    head_ref,
    sums,
    qkv_hbm,
    out_hbm,
    up_hbm,
    down_hbm,
    qkv_new,
    out_new,
    up_new,
    down_new,
    chosen,
    qkv_old,
    out_old,
    up_old,
    down_old,
    load_sem,
):
    head_id = head_ref[0]
    qkv_cols = qkv_new.shape[0]
    loads = [
        pltpu.make_async_copy(source, target, load_sem.at[index])
        for index, (source, target) in enumerate(
            ((down_hbm, down_old), (up_hbm, up_old), (qkv_hbm, qkv_old), (out_hbm, out_old))
        )
    ]
    for load in loads:
        load.start()
    loads[0].wait()
    down_new[...] = muon_keep * down_old[...] + sums[0].astype(f32)
    loads[1].wait()
    up_new[...] = muon_keep * up_old[...] + sums[1].astype(f32)
    loads[2].wait()
    loads[3].wait()
    for half in range(2):
        cols = slice(half * HALF, (half + 1) * HALF)
        value = sums[2, cols].astype(f32)
        qkv_new[:, cols] = muon_keep * qkv_old[:, cols] + value[:qkv_cols]
        out_new[:, cols] = muon_keep * out_old[:, cols] + value[qkv_cols:]

    @pl.when(head_id == 0)
    def _():
        chosen[:, :qkv_cols] = qkv_new[...].T
        chosen[:, qkv_cols:] = jnp.zeros((D, UNIT - qkv_cols), f32)

    @pl.when(head_id == 1)
    def _():
        chosen[:, :qkv_cols] = jnp.zeros((D, qkv_cols), f32)
        chosen[:, qkv_cols:] = out_new[...].T

    @pl.when(head_id == 2)
    def _():
        chosen[...] = up_new[...]

    @pl.when(head_id == 3)
    def _():
        chosen[...] = down_new[...]


def update_moments(head, sums, *old):
    def like(value):
        return jax.ShapeDtypeStruct(value.shape, f32)

    return pl.pallas_call(
        update_kernel,
        out_shape=tuple(map(like, old)) + (like(old[2]),),
        in_specs=[SMEM, VMEM] + [ANY] * 4,
        out_specs=(VMEM,) * 5,
        scratch_shapes=[pltpu.VMEM(value.shape, f32) for value in old]
        + [pltpu.SemaphoreType.DMA((4,))],
        compiler_params=pltpu.CompilerParams(vmem_limit_bytes=40 * MIB),
        name="update_moments",
    )(head, sums, *old)


GROUP = 3
GRAM_AXES = ("far", "near", "x")
GRAM_ORDERS = tuple(
    tuple(GRAM_AXES["fnx".index(letter)] for letter in order)
    for order in ("xnf", "nxf", "xnf", "nxf", "xnf", "xnf", "fxn")
)
GRAM_PLAN = (0, 1, 2, 3, 6, 4, 0, 5, 1, 2, 0, 4, 3, 1, 6, 2, 5, 0, 3, 6, 1, 2, 4, 0, 5)
GRAM_PLAN += (3, 6, 1, 2, 4, 1, 5, 3, 6, 0, 4, 2, 5, 3, 6, 4, 1, 5, 0, 2, 3, 6, 4, 5)


def gram_kernel(moment, out, part, came_one, came_two, came_three, high, low, send_sem, recv_sem):
    z, x, y, core = position()
    here = {"far": z // 2, "near": z % 2, "x": x}
    others = {
        "far": device(flip_z(z, 2), x, y, core),
        "near": device(flip_z(z, 1), x, y, core),
        "x": device(z, 1 - x, y, core),
    }
    greet(list(others.values()))
    blocks = sub_blocks(moment.shape[0])
    groups = len(blocks) // GROUP
    high[...] = moment[...].astype(bf16)
    low[...] = (moment[...] - high[...].astype(f32)).astype(bf16)
    started = []

    def product(index):
        i, j = blocks[index]
        left, right = pl.ds(i * SUB, SUB), pl.ds(j * SUB, SUB)
        total = dot(high[left, :], high[right, :], 1, 1)
        total = total + dot(high[left, :], low[right, :], 1, 1)
        total = total + dot(low[left, :], high[right, :], 1, 1)
        rows = SUB // 8
        for owner in range(8):
            cell = (owner // 4, owner // 2 % 2, owner % 2)
            part[(index // GROUP,) + cell + (index % GROUP,)] = total[
                owner * rows : (owner + 1) * rows
            ]

    def send(source, target, group, slot, axis):
        copy = pltpu.make_async_remote_copy(
            src_ref=source,
            dst_ref=target,
            send_sem=send_sem.at[group, slot],
            recv_sem=recv_sem.at[group, slot],
            device_id=others[axis],
            device_id_type=MESH,
        )
        copy.start()
        started.append(copy)
        return copy

    def cells(fixed, flipped=None):
        return tuple(
            1 - here[name] if name == flipped else here[name] if name in fixed else slice(None)
            for name in GRAM_AXES
        )

    class Walk:
        def __init__(self, group, order):
            self.group, self.order, self.stage = group, order, 0
            self.part = part.at[group]
            self.came = (came_one.at[group], came_two.at[group], came_three.at[group])

        def advance(self):
            stage, order = self.stage, self.order
            mine = pl.ds(self.group * GROUP, GROUP)
            if stage:
                self.copy.wait_recv()
            if 1 <= stage <= 3:
                kept = cells(order[:stage])
                total = self.part[kept] + self.came[stage - 1][...]
                if stage == 3:
                    out[kept + (mine,)] = total
                else:
                    self.part[kept] = total
            if stage < 3:
                source = self.part.at[cells(order[:stage], order[stage])]
                self.copy = send(source, self.came[stage], self.group, stage, order[stage])
            elif stage < 6:
                block = out.at[cells(order[: 6 - stage]) + (mine,)]
                self.copy = send(block, block, self.group, stage, order[5 - stage])
            self.stage += 1

    walks = [Walk(group, GRAM_ORDERS[group]) for group in range(groups)]
    for group in GRAM_PLAN:
        if walks[group].stage == 0:
            for index in range(group * GROUP, (group + 1) * GROUP):
                product(index)
        walks[group].advance()
    for copy in started:
        copy.wait_send()


def gram_sum(moment):
    size, cols = moment.shape
    count = len(sub_blocks(size))
    groups = count // GROUP
    rows = (SUB // 8, SUB)
    return pl.pallas_call(
        gram_kernel,
        out_shape=jax.ShapeDtypeStruct((2, 2, 2, count) + rows, f32),
        in_specs=[VMEM],
        out_specs=VMEM,
        scratch_shapes=[
            pltpu.VMEM((groups, 2, 2, 2, GROUP) + rows, f32),
            pltpu.VMEM((groups, 2, 2, GROUP) + rows, f32),
            pltpu.VMEM((groups, 2, GROUP) + rows, f32),
            pltpu.VMEM((groups, GROUP) + rows, f32),
            pltpu.VMEM((size, cols), bf16),
            pltpu.VMEM((size, cols), bf16),
            pltpu.SemaphoreType.DMA((groups, 6)),
            pltpu.SemaphoreType.DMA((groups, 6)),
        ],
        compiler_params=pltpu.CompilerParams(
            vmem_limit_bytes=32 * MIB, collective_id=1, has_side_effects=True
        ),
        name="gram_sum",
    )(moment).reshape((8, count) + rows)


STRIPS = 2


def share_kernel(mine, out, send_sem, recv_sem):
    z, x, y, core = position()
    beyond = device(z, x, 1 - y, core)
    partner = device(z, x, y, 1 - core)
    greet([beyond, partner])
    own = 2 * y + core
    far = 2 * (1 - y) + core
    out[own] = mine[...]
    rows = mine.shape[0] // STRIPS
    started = []

    def send(slot, strip, kind, other):
        block = out.at[slot, pl.ds(strip * rows, rows)]
        copy = pltpu.make_async_remote_copy(
            src_ref=block,
            dst_ref=block,
            send_sem=send_sem.at[strip, kind],
            recv_sem=recv_sem.at[strip, kind],
            device_id=other,
            device_id_type=MESH,
        )
        copy.start()
        started.append(copy)
        return copy

    across = [send(own, strip, 0, beyond) for strip in range(STRIPS)]
    late = [send(own, strip, 1, partner) for strip in range(STRIPS)]
    for strip, copy in enumerate(across):
        copy.wait_recv()
        late.append(send(far, strip, 2, partner))
    for copy in late:
        copy.wait_recv()
    for copy in started:
        copy.wait_send()


def share_factors(mine):
    return pl.pallas_call(
        share_kernel,
        out_shape=jax.ShapeDtypeStruct((4,) + mine.shape, bf16),
        in_specs=[VMEM],
        out_specs=VMEM,
        scratch_shapes=[
            pltpu.SemaphoreType.DMA((STRIPS, 3)),
            pltpu.SemaphoreType.DMA((STRIPS, 3)),
        ],
        compiler_params=pltpu.CompilerParams(
            vmem_limit_bytes=16 * MIB, collective_id=2, has_side_effects=True
        ),
        name="share_factors",
    )(mine)


def window(start, width, total):
    size = -(-(width + 96) // LANES) * LANES
    first = jnp.minimum(start // LANES * LANES, total - size)
    return pl.ds(pl.multiple_of(first, LANES), size), start - first


def finish_kernel(
    factors,
    qkv_hbm,
    out_hbm,
    up_hbm,
    down_hbm,
    qkv_new,
    out_new,
    up_new,
    down_new,
    qkv_old,
    out_old,
    up_old,
    down_old,
    turned,
    load_sem,
):
    shrink = 1.0 - muon_rate * muon_decay
    dp_id = lax.axis_index("dp")
    qkv_cols, out_cols = qkv_new.shape[0], out_new.shape[0]
    qkv_lanes, qkv_skip = window(dp_id * qkv_cols, qkv_cols, 3 * D)
    out_lanes, out_skip = window(dp_id * out_cols, out_cols, D)
    block = pl.ds(pl.multiple_of(dp_id * UNIT, UNIT), UNIT)
    loads = [
        pltpu.make_async_copy(source, target, load_sem.at[index])
        for index, (source, target) in enumerate(
            (
                (up_hbm.at[:, block], up_old),
                (down_hbm.at[block], down_old),
                (qkv_hbm.at[:, qkv_lanes], qkv_old),
                (out_hbm.at[:, out_lanes], out_old),
            )
        )
    ]
    for load in loads:
        load.start()

    def step(index, rate):
        return muon_rate * rate * factors[index].astype(f32)

    loads[0].wait()
    up_new[...] = up_old[...].astype(f32) * shrink - step(2, math.sqrt(max(1.0, FF / D)))
    loads[1].wait()
    down_new[...] = down_old[...].astype(f32) * shrink - step(3, 1.0).T
    loads[2].wait()
    turned[...] = qkv_old[...].astype(f32).T
    rows = pl.ds(pl.multiple_of(qkv_skip, 32), qkv_cols)
    qkv_new[...] = turned[rows, :] * shrink - step(0, math.sqrt(3.0)).T[:qkv_cols]
    loads[3].wait()
    turned[: out_old.shape[1], :] = out_old[...].astype(f32).T
    rows = pl.ds(pl.multiple_of(out_skip, 32), out_cols)
    out_new[...] = turned[rows, :] * shrink - step(1, 1.0).T[qkv_cols:]


def finish_weights(factors, qkv_w, out_w, up_w, down_w, qkv_cols, out_cols):
    def shape(*dims):
        return jax.ShapeDtypeStruct(dims, f32)

    return pl.pallas_call(
        finish_kernel,
        out_shape=(shape(qkv_cols, D), shape(out_cols, D), shape(D, UNIT), shape(UNIT, D)),
        in_specs=[VMEM] + [ANY] * 4,
        out_specs=(VMEM,) * 4,
        scratch_shapes=[
            pltpu.VMEM((D, 384), bf16),
            pltpu.VMEM((D, 256), bf16),
            pltpu.VMEM((D, UNIT), bf16),
            pltpu.VMEM((UNIT, D), bf16),
            pltpu.VMEM((384, D), f32),
            pltpu.SemaphoreType.DMA((4,)),
        ],
        compiler_params=pltpu.CompilerParams(vmem_limit_bytes=32 * MIB),
        name="finish_weights",
    )(factors, qkv_w, out_w, up_w, down_w)


def swap(value, axis, bit):
    size = lax.axis_size(axis)
    return lax.ppermute(value, axis, [(i, i ^ bit) for i in range(size)])


def scatter_head(value, bit, position):
    half = value.shape[1] // 2
    mine = lax.dynamic_slice_in_dim(value, position * half, half, 1)
    other = lax.dynamic_slice_in_dim(value, (1 - position) * half, half, 1)
    return (mine.astype(f32) + swap(other, "head", bit).astype(f32)).astype(bf16)


def scatter_dp_pair(value, position):
    paired = value.reshape((value.shape[0] // 2, 2) + value.shape[1:])
    mine = lax.dynamic_index_in_dim(paired, position, 1, False)
    other = lax.dynamic_index_in_dim(paired, 1 - position, 1, False)
    return (mine.astype(f32) + swap(other, "dp", 1).astype(f32)).astype(bf16)


def scatter_dp_rest(value, place):
    ranks = value.shape[0]
    total = lax.dynamic_index_in_dim(value, place, 0, False).astype(f32)
    for step in range(1, ranks):
        sent = lax.dynamic_index_in_dim(value, place ^ step, 0, False)
        total = total + swap(sent, "dp", 2 * step).astype(f32)
    return total


def local(
    tokens,
    cotangent,
    qkv_weight,
    out_weight,
    up_weight,
    down_weight,
    vectors,
    qkv_moment,
    out_moment,
    up_moment,
    down_moment,
    adam_first,
    adam_second,
    bucket_class,
    row_lengths,
):
    n_dp = lax.axis_size("dp")
    n_head = lax.axis_size("head")
    dp_id = lax.axis_index("dp")
    head_id = lax.axis_index("head")
    core, side = head_id % 2, head_id // 2
    tok, width = tokens.shape
    hidden = up_weight.shape[1]
    half = width // 2
    qkv_cols, out_cols = qkv_moment.shape[1], out_moment.shape[1]
    shrink = 1.0 - muon_rate * muon_decay

    def weight_block(weight, cols, dim):
        return lax.dynamic_slice_in_dim(weight, dp_id * cols, cols, dim)

    block = head_id.astype(jnp.int32)[None]
    vec_len = vectors.shape[0] // n_dp
    if (n_dp, n_head, tok) == (8, 4, 256):
        mixed, input_grad, sums, vec = layer(
            bucket_class,
            row_lengths,
            tokens,
            cotangent,
            vectors,
            qkv_weight,
            out_weight,
            up_weight,
            down_weight,
        )
        grad_vec = vec[:VEC_BLOCK].reshape(vec_len)
        *moments, chosen = update_moments(
            block, sums.reshape(3, width, -1), qkv_moment.T, out_moment.T, up_moment, down_moment
        )
        factors = share_factors(orthogonalize(gram_sum(chosen), chosen))
        new_weights = finish_weights(
            factors, qkv_weight, out_weight, up_weight, down_weight, qkv_cols, out_cols
        )
        moments = [moments[0].T, moments[1].T, *moments[2:]]
        new_weights = [new_weights[0].T, new_weights[1].T, *new_weights[2:]]
    else:
        pieces = split_vectors(vectors, width, hidden)
        bias_query, bias_value, bias_out, gain_one, shift_one = pieces[:5]
        bias_up, bias_down, gain_two, shift_two = pieces[5:]
        bias_qkv = jnp.concatenate([bias_query, jnp.zeros_like(bias_query), bias_value])

        def column_half(value, which):
            return lax.dynamic_slice_in_dim(value, which * half, half, 1)

        qkv = (dot(tokens, qkv_weight, 1, 0) + bias_qkv).astype(bf16)
        other = swap(qkv[:, width:], "head", 1)
        attended = attend(block, bucket_class, row_lengths, qkv, other)
        attn_val = dot(attended, out_weight, 1, 0) + bias_out
        resid_one = tokens.astype(f32) + attn_val
        centre = resid_one - jnp.mean(resid_one, axis=-1, keepdims=True)
        rstd_one = lax.rsqrt(jnp.mean(centre * centre, axis=-1, keepdims=True) + norm_eps)
        zhat_one = centre * rstd_one
        normed_one = zhat_one * gain_one + shift_one
        normed_low = normed_one.astype(bf16)
        up_val = dot(normed_low, up_weight, 1, 0) + bias_up
        phi_cum = 0.5 * (1.0 + lax.erf(up_val * (0.5**0.5)))
        active_low = (up_val * phi_cum).astype(bf16)
        slope = phi_cum + up_val * jnp.exp(-0.5 * up_val * up_val) * (1.0 / math.sqrt(2.0 * math.pi))
        down_val = dot(active_low, down_weight, 1, 0) + bias_down
        resid_two = normed_one + down_val
        centre = resid_two - jnp.mean(resid_two, axis=-1, keepdims=True)
        rstd_two = lax.rsqrt(jnp.mean(centre * centre, axis=-1, keepdims=True) + norm_eps)
        zhat_two = centre * rstd_two
        mixed = zhat_two * gain_two + shift_two

        def norm_back(grad, gain, zhat, rstd):
            inner = grad * gain
            mean = jnp.mean(inner, axis=-1, keepdims=True)
            slant = jnp.mean(inner * zhat, axis=-1, keepdims=True)
            return (inner - mean - zhat * slant) * rstd, jnp.sum(grad * zhat, axis=0), jnp.sum(grad, axis=0)

        grad_two, grad_gain_two, grad_shift_two = norm_back(
            cotangent.astype(f32), gain_two, zhat_two, rstd_two
        )
        grad_down_low = grad_two.astype(bf16)
        grad_bias_down = jnp.sum(grad_down_low, axis=0, dtype=f32)

        x_id, z_id = dp_id % 2, dp_id // 2

        grad_up_low = (dot(grad_down_low, down_weight, 1, 1) * slope).astype(bf16)
        grad_bias_up = jnp.sum(grad_up_low, axis=0, dtype=f32)
        grad_normed = grad_two + dot(grad_up_low, up_weight, 1, 1)
        grad_one, grad_gain_one, grad_shift_one = norm_back(grad_normed, gain_one, zhat_one, rstd_one)
        grad_attn_low = grad_one.astype(bf16)
        grad_bias_out = jnp.sum(grad_attn_low, axis=0, dtype=f32)
        grad_heads = dot(grad_attn_low, out_weight, 1, 1).astype(bf16)
        grad_query, own, sent = attend_back(block, bucket_class, row_lengths, qkv, other, grad_heads)
        grad_kv = (own + swap(sent, "head", 1).astype(f32)).astype(bf16)
        grad_qkv = jnp.concatenate([grad_query, grad_kv], axis=1)
        grad_bias_qkv = jnp.sum(grad_qkv, axis=0, dtype=f32)
        input_grad = grad_one + dot(grad_qkv, qkv_weight, 1, 1)
        grad_vector = jnp.concatenate(
            [
                grad_bias_qkv[:width],
                grad_bias_qkv[2 * width :],
                grad_bias_out,
                grad_gain_one,
                grad_shift_one,
                grad_bias_up,
                grad_bias_down,
                grad_gain_two,
                grad_shift_two,
            ]
        )
        grad_vector = grad_vector + swap(grad_vector, "head", 1)
        wides = [active_low, grad_up_low, grad_attn_low, grad_qkv]
        narrows = [grad_down_low, normed_low, attended, tokens]

        def both_halves(value):
            return jnp.concatenate(
                [column_half(value, core), swap(column_half(value, 1 - core), "head", 1)], axis=0
            )

        def weight_grad(wide, narrow):
            wide = jnp.concatenate([wide, swap(wide, "head", 1)], axis=0)
            value = dot(wide, both_halves(narrow), 0, 0).astype(bf16)
            return value.reshape(n_dp, value.shape[0] // n_dp, half)

        def reduce_y_first(value):
            return scatter_dp_rest(scatter_dp_pair(scatter_head(value, 2, side), x_id), z_id)

        def reduce_x_first(value):
            return scatter_dp_rest(scatter_head(scatter_dp_pair(value, x_id), 2, side), z_id)

        def spread(value):
            value = value.astype(bf16)
            came = swap(value, "head", 2)
            value = jnp.concatenate(
                [jnp.where(side == 0, value, came), jnp.where(side == 0, came, value)], axis=0
            )
            came = swap(value, "head", 1)
            return jnp.concatenate(
                [jnp.where(core == 0, value, came), jnp.where(core == 0, came, value)], axis=1
            ).astype(f32)

        down_part, up_part, out_part, qkv_part = [
            weight_grad(wide, narrow) for wide, narrow in zip(wides, narrows)
        ]
        vec_rows = 16
        vec_part = grad_vector.reshape(n_dp, vec_len)
        vec_part = jnp.pad(vec_part, ((0, 0), (0, vec_rows * width - vec_len)))
        vec_part = vec_part.reshape(n_dp, vec_rows, width)
        vec_part = lax.dynamic_slice_in_dim(vec_part, core * half, half, 2).astype(bf16)
        down_new = spread(reduce_x_first(down_part))
        up_new = spread(reduce_y_first(up_part))
        tail_new = spread(
            reduce_y_first(jnp.concatenate([qkv_part, out_part, vec_part], axis=1))
        )
        grads = [
            tail_new[:qkv_cols].T,
            tail_new[qkv_cols : qkv_cols + out_cols].T,
            up_new.T,
            down_new.T,
        ]
        grad_vec = tail_new[qkv_cols + out_cols :].reshape(-1)[:vec_len]
        moments = [
            muon_keep * old + grad
            for old, grad in zip([qkv_moment, out_moment, up_moment, down_moment], grads)
        ]
        most = max(m.shape[1] for m in moments)
        padded = [jnp.pad(m, ((0, 0), (0, most - m.shape[1]))) for m in moments]
        chosen = padded[-1]
        for index in range(len(padded) - 2, -1, -1):
            chosen = jnp.where(head_id == index, padded[index], chosen)
        gram_mat = lax.dot_general(
            chosen, chosen, (((1,), (1,)), ((), ())), precision=lax.Precision.HIGH
        )
        own_factor = orthogonalize(lax.psum(gram_mat, "dp"), chosen)
        across = swap(own_factor, "head", 2)
        low_pair = jnp.where(side == 0, own_factor, across)
        high_pair = jnp.where(side == 0, across, own_factor)
        near_low = swap(low_pair, "head", 1)
        near_high = swap(high_pair, "head", 1)
        factors = [
            jnp.where(core == 0, low_pair, near_low),
            jnp.where(core == 0, near_low, low_pair),
            jnp.where(core == 0, high_pair, near_high),
            jnp.where(core == 0, near_high, high_pair),
        ]
        factors = [o[:, : m.shape[1]].astype(f32) for o, m in zip(factors, moments)]
        factors[3] = factors[3].T
        old_weights = [
            weight_block(qkv_weight, qkv_cols, 1),
            weight_block(out_weight, out_cols, 1),
            weight_block(up_weight, up_moment.shape[1], 1),
            weight_block(down_weight, down_moment.shape[1], 0),
        ]

        rates = (math.sqrt(3.0), 1.0, math.sqrt(max(1.0, hidden / width)), 1.0)
        new_weights = [
            old.astype(f32) * shrink - muon_rate * rate * factor
            for old, rate, factor in zip(old_weights, rates, factors)
        ]

    vec_old = lax.dynamic_slice_in_dim(vectors, dp_id * vec_len, vec_len, 0)
    vec_first = beta_first * adam_first + (1.0 - beta_first) * grad_vec
    vec_second = beta_second * adam_second + (1.0 - beta_second) * grad_vec * grad_vec
    first_hat = vec_first / (1.0 - beta_first**STEP)
    second_hat = vec_second / (1.0 - beta_second**STEP)
    vec_new = vec_old - adam_rate * first_hat / (jnp.sqrt(second_hat) + adam_eps)
    return (mixed, input_grad, *moments, *new_weights, vec_first, vec_second, vec_new)


def solution(mesh):
    tokens_spec = P(("dp", "head"), None)
    block_spec = P(None, "dp")
    return jax.shard_map(
        local,
        mesh=mesh,
        in_specs=(
            tokens_spec,
            tokens_spec,
            P(),
            P(),
            P(),
            P(),
            P(),
            block_spec,
            block_spec,
            block_spec,
            block_spec,
            P("dp"),
            P("dp"),
            P("dp"),
            P("dp", None),
        ),
        out_specs=(
            tokens_spec,
            tokens_spec,
            block_spec,
            block_spec,
            block_spec,
            block_spec,
            block_spec,
            block_spec,
            block_spec,
            P("dp", None),
            P("dp"),
            P("dp"),
            P("dp"),
        ),
        check_vma=False,
    )
```

```python
import functools
import itertools
import math

import jax
import jax.numpy as jnp
from jax import lax
from jax.experimental import pallas as pl
from jax.experimental.pallas import tpu as pltpu
from jax.sharding import PartitionSpec as P

D = 768
HEADS = 12
HEAD_DIM = 64
FF = 3072
BASE_LEN = 128
NS_STEPS = 5
STEP = 5
MAX_LEN = 512

f32 = jnp.float32
bf16 = jnp.bfloat16

norm_eps = 1e-12
masked_score = -1000000000.0
quintic_a = 3.4445
quintic_b = -4.775
quintic_c = 2.0315
muon_rate = 1.0
muon_decay = 0.01
muon_keep = 0.5
adam_rate = 0.2
beta_first = 0.9
beta_second = 0.999
adam_eps = 1e-08
MIB = 1024 * 1024


def dot(left, right, left_dim, right_dim):
    return lax.dot_general(
        left, right, (((left_dim,), (right_dim,)), ((), ())), preferred_element_type=f32
    )


def split_vectors(vectors, width, hidden):
    lengths_list = [width] * 5 + [hidden] + [width] * 3
    pieces = []
    offset = 0
    for length in lengths_list:
        pieces.append(vectors[offset : offset + length])
        offset = offset + length
    return pieces


def allowed_mask(class_ref, length_ref, block, tok):
    shift = class_ref[0] + int(math.log2(BASE_LEN))
    query_place = block * tok + lax.broadcasted_iota(jnp.int32, (tok, 1), 0)
    lane = lax.broadcasted_iota(jnp.int32, (1, 2 * tok), 1)
    own = lane < tok
    key_place = jnp.where(own, block * tok + lane, (block ^ 1) * tok + lane - tok)
    key_row = lax.shift_right_logical(key_place, jnp.broadcast_to(shift, key_place.shape))
    offset = key_place - lax.shift_left(key_row, jnp.broadcast_to(shift, key_place.shape))
    row_len = jnp.zeros_like(key_row)
    for slot in range(length_ref.shape[1]):
        row_len = jnp.where(key_row == slot, length_ref[0, slot], row_len)
    key_row = jnp.where(offset < row_len, key_row, -1)
    query_row = lax.shift_right_logical(query_place, jnp.broadcast_to(shift, query_place.shape))
    return query_row == key_row


def half_masks():
    lane = lax.broadcasted_iota(jnp.int32, (1, 2 * HEAD_DIM), 1)
    first = (lane < HEAD_DIM).astype(f32)
    return (first.astype(bf16), (1.0 - first).astype(bf16)), lane < HEAD_DIM


def head_prob(query, keys, allowed):
    score = jnp.where(allowed, dot(query, keys, 1, 1) * HEAD_DIM ** (-0.5), masked_score)
    exponent = jnp.exp(score - jnp.max(score, axis=-1, keepdims=True))
    return exponent / jnp.sum(exponent, axis=-1, keepdims=True)


def attend_kernel(block_ref, class_ref, length_ref, qkv_ref, other_ref, out_ref):
    tok = qkv_ref.shape[0]
    allowed = allowed_mask(class_ref, length_ref, block_ref[0], tok)
    masks, first = half_masks()
    for pair in range(HEADS // 2):
        cols = pl.ds(pair * 2 * HEAD_DIM, 2 * HEAD_DIM)
        kcols = pl.ds(D + pair * 2 * HEAD_DIM, 2 * HEAD_DIM)
        vcols = pl.ds(2 * D + pair * 2 * HEAD_DIM, 2 * HEAD_DIM)
        query = qkv_ref[:, cols]
        keys = jnp.concatenate([qkv_ref[:, kcols], other_ref[:, cols]], axis=0)
        values = jnp.concatenate([qkv_ref[:, vcols], other_ref[:, kcols]], axis=0)
        outs = []
        for mask in masks:
            prob = head_prob(query * mask, keys, allowed)
            outs.append(dot(prob.astype(bf16), values, 1, 0))
        out_ref[:, cols] = jnp.where(first, outs[0], outs[1]).astype(bf16)


def attend_back_kernel(
    block_ref, class_ref, length_ref, qkv_ref, other_ref, grad_ref, dq_ref, own_ref, send_ref
):
    tok = qkv_ref.shape[0]
    allowed = allowed_mask(class_ref, length_ref, block_ref[0], tok)
    masks, first = half_masks()
    scale = HEAD_DIM ** (-0.5)
    for pair in range(HEADS // 2):
        cols = pl.ds(pair * 2 * HEAD_DIM, 2 * HEAD_DIM)
        kcols = pl.ds(D + pair * 2 * HEAD_DIM, 2 * HEAD_DIM)
        vcols = pl.ds(2 * D + pair * 2 * HEAD_DIM, 2 * HEAD_DIM)
        query = qkv_ref[:, cols]
        keys = jnp.concatenate([qkv_ref[:, kcols], other_ref[:, cols]], axis=0)
        values = jnp.concatenate([qkv_ref[:, vcols], other_ref[:, kcols]], axis=0)
        grad = grad_ref[:, cols]
        dqs, dk, dv = [], None, None
        for mask in masks:
            head_query = query * mask
            head_grad = grad * mask
            prob = head_prob(head_query, keys, allowed)
            part_v = dot(prob.astype(bf16), head_grad, 0, 0)
            dprob = dot(head_grad, values, 1, 1)
            dscore = prob * (dprob - jnp.sum(prob * dprob, axis=-1, keepdims=True))
            dscore = dscore.astype(bf16)
            dqs.append(dot(dscore, keys, 1, 0))
            part_k = dot(dscore, head_query, 0, 0)
            dk = part_k if dk is None else dk + part_k
            dv = part_v if dv is None else dv + part_v
        dk = dk * scale
        dq_ref[:, cols] = (jnp.where(first, dqs[0], dqs[1]) * scale).astype(bf16)
        own_ref[:, cols] = dk[:tok]
        own_ref[:, kcols] = dv[:tok]
        send_ref[:, cols] = dk[tok:].astype(bf16)
        send_ref[:, kcols] = dv[tok:].astype(bf16)


SMEM = pl.BlockSpec(memory_space=pltpu.SMEM)
VMEM = pl.BlockSpec(memory_space=pltpu.VMEM)
ANY = pl.BlockSpec(memory_space=pl.ANY)


def attend(block, row_class, lengths, qkv, other):
    tok = qkv.shape[0]
    return pl.pallas_call(
        attend_kernel,
        out_shape=jax.ShapeDtypeStruct((tok, D), bf16),
        in_specs=[SMEM, SMEM, SMEM, VMEM, VMEM],
        out_specs=VMEM,
        compiler_params=pltpu.CompilerParams(vmem_limit_bytes=32 * MIB),
        name="attend",
    )(block, row_class, lengths, qkv, other)


def attend_back(block, row_class, lengths, qkv, other, grad):
    tok = qkv.shape[0]
    return pl.pallas_call(
        attend_back_kernel,
        out_shape=(
            jax.ShapeDtypeStruct((tok, D), bf16),
            jax.ShapeDtypeStruct((tok, 2 * D), f32),
            jax.ShapeDtypeStruct((tok, 2 * D), bf16),
        ),
        in_specs=[SMEM, SMEM, SMEM, VMEM, VMEM, VMEM],
        out_specs=(VMEM, VMEM, VMEM),
        compiler_params=pltpu.CompilerParams(vmem_limit_bytes=32 * MIB),
        name="attend_back",
    )(block, row_class, lengths, qkv, other, grad)


CENTRES = (0.0, 0.0, 0.0, 0.8, 0.8)
TILE = 256
SUB = 128


def sub_blocks(size):
    count = size // SUB
    return [(i, j) for i in range(count) for j in range(i, count)]


def ortho_kernel(packed, gram_ref, moment_ref, out_ref, e, f, g, eb, fb, gb, ya, yb, y):
    size = e.shape[0]
    tiles = [slice(i * TILE, (i + 1) * TILE) for i in range(size // TILE)]

    def unit(rows):
        row_id = rows.start + lax.broadcasted_iota(jnp.int32, (TILE, size), 0)
        col_id = lax.broadcasted_iota(jnp.int32, (TILE, size), 1)
        return (row_id == col_id).astype(f32)

    if packed:
        for index, (i, j) in enumerate(sub_blocks(size)):
            value = gram_ref[:, index].reshape(SUB, SUB)
            e[i * SUB : (i + 1) * SUB, j * SUB : (j + 1) * SUB] = value
            if i != j:
                e[j * SUB : (j + 1) * SUB, i * SUB : (i + 1) * SUB] = value.T
        gram = e
    else:
        gram = gram_ref
    diagonal = jnp.zeros((TILE, size), f32)
    for rows in tiles:
        diagonal = diagonal + gram[rows, :] * unit(rows)
    trace = jnp.sum(jnp.sum(diagonal, axis=0, keepdims=True), axis=1, keepdims=True)
    factor = 1.0 / (jnp.sqrt(trace) + 1e-07)
    square_factor = factor * factor
    for rows in tiles:
        value = gram[rows, :] * square_factor
        e[rows, :] = value
        eb[rows, :] = value.astype(bf16)
        moment = moment_ref[rows, :] * factor
        y[rows, :] = moment
        ya[rows, :] = moment.astype(bf16)
    now, then = ya, yb
    for step in range(NS_STEPS):
        last = step + 1 == NS_STEPS
        centre = CENTRES[step]
        after = 0.0 if last else CENTRES[step + 1]
        keep = quintic_a + quintic_b * centre + quintic_c * centre * centre
        linear = quintic_b + 2.0 * quintic_c * centre
        for rows in tiles:
            value = linear * e[rows, :] + quintic_c * dot(eb[rows, :], eb[...], 1, 0)
            fb[rows, :] = value.astype(bf16)
            if not last:
                f[rows, :] = value
        for rows in tiles:
            value = keep * y[rows, :] + dot(fb[rows, :], now[...], 1, 0)
            if last:
                out_ref[rows, :] = value.astype(out_ref.dtype)
            else:
                y[rows, :] = value
                then[rows, :] = value.astype(bf16)
        if last:
            break
        now, then = then, now
        for rows in tiles:
            value = keep * e[rows, :] + dot(eb[rows, :], fb[...], 1, 0)
            if centre:
                value = value + centre * f[rows, :]
            g[rows, :] = value
            gb[rows, :] = value.astype(bf16)
        for rows in tiles:
            value = keep * g[rows, :] + dot(gb[rows, :], fb[...], 1, 0)
            if centre:
                value = value + (centre * keep) * f[rows, :]
            shift = centre * keep * keep - after
            if shift:
                value = value + shift * unit(rows)
            e[rows, :] = value
            eb[rows, :] = value.astype(bf16)


def orthogonalize(gram_mat, moment):
    size, cols = moment.shape
    square = pltpu.VMEM((size, size), f32)
    square_low = pltpu.VMEM((size, size), bf16)
    return pl.pallas_call(
        functools.partial(ortho_kernel, gram_mat.ndim != 2),
        out_shape=jax.ShapeDtypeStruct((size, cols), bf16),
        in_specs=[VMEM, VMEM],
        out_specs=VMEM,
        scratch_shapes=[
            square,
            square,
            square,
            square_low,
            square_low,
            square_low,
            pltpu.VMEM((size, cols), bf16),
            pltpu.VMEM((size, cols), bf16),
            pltpu.VMEM((size, cols), f32),
        ],
        compiler_params=pltpu.CompilerParams(vmem_limit_bytes=48 * MIB),
        name="ortho",
    )(gram_mat, moment)


MESH = pl.DeviceIdType.MESH
CHUNK = 48
PARTS = 4
UNIT = 2 * PARTS * CHUNK
HALF = D // 2
LANES = 128
VEC_BLOCK = 9
ROWS = 16
CHUNK_ORDERS = (
    "yxnf", "yxfn", "xyfn", "xnfy",
    "ynfx", "xyfn", "nxyf", "fxny",
    "xfyn", "yxnf", "xynf", "nxyf",
)
CHUNK_PLAN = (
    (0, 1, 2, 3),
    (),
    (),
    (),
    (),
    (4, 5, 6, 7),
    (),
    (0, 1, 2, 3),
    (),
    (),
    (),
    (),
    (2, 4),
    (),
    (0, 1, 3, 6, 2, 7, 5),
    (),
    (),
    (2, 5, 4, 8, 9, 0, 6, 10, 11, 7, 1, 2, 3),
    (2, 3, 6, 0, 1, 3, 5, 0, 3, 1, 6, 4, 7, 0, 9, 1, 5, 8, 6, 7, 4, 6, 5, 10, 7, 5, 4, 11, 7, 9, 4, 10, 8, 9, 11, 10, 8, 9, 11, 10, 8, 9, 11, 9, 10, 8, 11, 10, 8, 11),
)
BIAS_QUERY, BIAS_VALUE, BIAS_OUT, GAIN_ONE, SHIFT_ONE, BIAS_UP = (i * D for i in range(6))
BIAS_DOWN, GAIN_TWO, SHIFT_TWO = (BIAS_UP + FF + i * D for i in range(3))


def position():
    dp_id, head_id = lax.axis_index("dp"), lax.axis_index("head")
    z, x = dp_id // 2, dp_id % 2
    y, core = head_id // 2, head_id % 2
    return z, x, y, core


def device(z, x, y, core):
    return (2 * z + x, 2 * y + core)


def flip_z(z, step):
    high, low = z // 2, z % 2
    high = 1 - high if step // 2 else high
    low = 1 - low if step % 2 else low
    return 2 * high + low


def greet(others):
    barrier = pltpu.get_barrier_semaphore()
    for other in others:
        pl.semaphore_signal(barrier, inc=1, device_id=other, device_id_type=MESH)
    pl.semaphore_wait(barrier, len(others))


def by_rows(count, body, init=None, together=4):
    def step(index, carry):
        for part in range(together):
            start = (index * together + part) * ROWS
            carry = body(pl.ds(pl.multiple_of(start, ROWS), ROWS), carry)
        return carry

    return lax.fori_loop(0, count // (ROWS * together), step, init)


def row_mean(value):
    return jnp.sum(value, axis=-1, keepdims=True) * (1.0 / D)


def fold(value):
    return jnp.sum(value.reshape(value.shape[0] // 8, 8, value.shape[1]), axis=0)


def column_sum(value):
    return jnp.sum(value, axis=0, keepdims=True)


def normal_parts(value):
    size = jnp.abs(value)
    decay = jnp.exp(-0.5 * value * value)
    t = 1.0 / (1.0 + (0.3275911 * 0.5**0.5) * size)
    series = t * (1.061405429 * 0.5)
    for term in (-1.453152027, 1.421413741, -0.284496736, 0.254829592):
        series = (series + term * 0.5) * t
    tail = series * decay
    return jnp.where(value < 0.0, tail, 1.0 - tail), decay * (1.0 / math.sqrt(2.0 * math.pi))


def transposed(value):
    return value.astype(f32).T.astype(bf16)


def layer_kernel(
    row_class,
    lengths,
    tokens,
    cotangent,
    vectors,
    qkv_hbm,
    out_hbm,
    up_hbm,
    down_hbm,
    mixed,
    input_grad,
    sums,
    vec_sum,
    qkv_w,
    out_w,
    up_w,
    down_w,
    query,
    query_turned,
    keys_values,
    keys_turned,
    prob,
    attended,
    normed_low,
    grad_down,
    grad_attn,
    narrow_tokens,
    narrow_attended,
    narrow_normed,
    narrow_grad,
    active,
    grad_up,
    attn_turned,
    qkv_turned,
    exchanged,
    grad_heads,
    heads_turned,
    slope,
    normed_one,
    zhat_one,
    rstd_one,
    grad_two,
    work,
    vec,
    vec_core,
    vec_y,
    vec_x,
    vec_z,
    part,
    came_one,
    came_two,
    came_three,
    came_four,
    load_sem,
    pair_send,
    pair_recv,
    send_sem,
    recv_sem,
):
    grad_one = normed_one
    z, x, y, core = position()
    tok = tokens.shape[0]
    loads = {
        name: pltpu.make_async_copy(source, target, load_sem.at[index])
        for index, (name, source, target) in enumerate(
            (
                ("qkv", qkv_hbm, qkv_w),
                ("out", out_hbm, out_w),
                ("up", up_hbm, up_w),
                ("down", down_hbm, down_w),
            )
        )
    }
    for load in loads.values():
        load.start()
    beyond = device(z, x, 1 - y, core)
    beside = device(z, 1 - x, y, core)
    partner = device(z, x, y, 1 - core)
    along = [device(flip_z(z, step), x, y, core) for step in (1, 2, 3)]
    greet([beyond, beside, partner] + along)
    started = []

    def remote(source, target, send_at, recv_at, other):
        copy = pltpu.make_async_remote_copy(
            src_ref=source,
            dst_ref=target,
            send_sem=send_at,
            recv_sem=recv_at,
            device_id=other,
            device_id_type=MESH,
        )
        copy.start()
        started.append(copy)
        return copy

    pair_count = []

    def to_partner(source, target):
        slot = len(pair_count)
        pair_count.append(slot)
        return remote(source, target, pair_send.at[slot], pair_recv.at[slot], partner)

    own_half = pl.ds(pl.multiple_of(core * HALF, HALF), HALF)
    other_half = pl.ds(pl.multiple_of((1 - core) * HALF, HALF), HALF)

    def span(start, length=D):
        return vectors[0:1, start : start + length]

    def put_vec(start, value):
        for index in range(value.shape[1] // LANES):
            block, row = divmod(start // LANES + index, VEC_BLOCK)
            vec[block, row : row + 1, :] = value[:, index * LANES : (index + 1) * LANES]

    vec[...] = jnp.zeros_like(vec)

    own_rows = pl.ds(0, tok)
    far_rows = pl.ds(tok, tok)
    own_lanes, far_lanes = own_rows, far_rows

    def share_half(value, narrow):
        narrow[own_rows, :] = value[:, own_half]
        return to_partner(value.at[:, other_half], narrow.at[far_rows])

    tokens_came = share_half(tokens, narrow_tokens)
    loads["qkv"].wait()
    for index, start in ((1, None), (2, BIAS_VALUE)):
        value = dot(tokens[...], qkv_w[:, index * D : (index + 1) * D], 1, 0)
        if start is not None:
            value = value + span(start)
        keys_values[own_rows, (index - 1) * D : index * D] = value.astype(bf16)
    kv_arrived = to_partner(keys_values.at[own_rows], keys_values.at[far_rows])
    value = dot(tokens[...], qkv_w[:, :D], 1, 0) + span(BIAS_QUERY)
    query[...] = value.astype(bf16)
    query_turned[...] = transposed(query[...])
    allowed = allowed_mask(row_class, lengths, 2 * y + core, tok)
    masks, first = half_masks()
    kv_arrived.wait_recv()

    scale = HEAD_DIM ** (-0.5)
    for pair in range(HEADS // 2):
        cols = slice(pair * LANES, (pair + 1) * LANES)
        keys = keys_values[:, cols]
        values = keys_values[:, D + cols.start : D + cols.stop]
        outs = []
        for side, mask in enumerate(masks):
            score = dot(query[:, cols] * (mask * scale), keys, 1, 1)
            score = jnp.where(allowed, score, masked_score)
            exponent = jnp.exp(score - jnp.max(score, axis=-1, keepdims=True))
            chance = exponent * (1.0 / jnp.sum(exponent, axis=-1, keepdims=True))
            prob[2 * pair + side] = chance.astype(bf16)
            outs.append(dot(prob[2 * pair + side], values, 1, 0))
        attended[:, cols] = jnp.where(first, outs[0], outs[1]).astype(bf16)
    attended_came = share_half(attended, narrow_attended)

    loads["out"].wait()
    work[...] = dot(attended[...], out_w[...], 1, 0)

    def norm_one(rows, carry):
        value = tokens[rows, :].astype(f32) + (work[rows, :] + span(BIAS_OUT))
        centre = value - row_mean(value)
        rstd = lax.rsqrt(row_mean(centre * centre) + norm_eps)
        zhat = centre * rstd
        normed = zhat * span(GAIN_ONE) + span(SHIFT_ONE)
        zhat_one[rows, :] = zhat
        rstd_one[rows, :] = jnp.broadcast_to(rstd, (ROWS, LANES))
        normed_one[rows, :] = normed
        normed_low[rows, :] = normed.astype(bf16)
        return carry

    by_rows(tok, norm_one)
    normed_came = share_half(normed_low, narrow_normed)

    loads["up"].wait()
    for tile in range(FF // D):
        cols = slice(tile * D, (tile + 1) * D)
        work[...] = dot(normed_low[...], up_w[:, cols], 1, 0)

        def gelu(rows, carry):
            value = work[rows, :] + span(BIAS_UP + cols.start)
            chance, density = normal_parts(value)
            active[rows, cols] = (value * chance).astype(bf16)
            slope[rows, cols] = chance + value * density
            return carry

        by_rows(tok, gelu)
    active_came = to_partner(active.at[own_rows], active.at[far_rows])
    loads["down"].wait()
    work[...] = dot(active[own_rows, :], down_w[...], 1, 0)

    def norm_two(rows, carry):
        value = normed_one[rows, :] + (work[rows, :] + span(BIAS_DOWN))
        centre = value - row_mean(value)
        rstd = lax.rsqrt(row_mean(centre * centre) + norm_eps)
        zhat = centre * rstd
        mixed[rows, :] = zhat * span(GAIN_TWO) + span(SHIFT_TWO)
        grad = cotangent[rows, :].astype(f32)
        inner = grad * span(GAIN_TWO)
        grad_in = (inner - row_mean(inner) - zhat * row_mean(inner * zhat)) * rstd
        grad_two[rows, :] = grad_in
        low = grad_in.astype(bf16)
        grad_down[rows, :] = low
        gain, shift, bias = carry
        return gain + fold(grad * zhat), shift + fold(grad), bias + fold(low.astype(f32))

    zero = jnp.zeros((8, D), f32)
    gain, shift, bias = by_rows(tok, norm_two, (zero, zero, zero))
    put_vec(GAIN_TWO, column_sum(gain))
    put_vec(SHIFT_TWO, column_sum(shift))
    put_vec(BIAS_DOWN, column_sum(bias))
    grad_down_came = share_half(grad_down, narrow_grad)
    keys_turned[...] = transposed(keys_values[:, :D])

    here = {"f": z // 2, "n": z % 2, "x": x, "y": y}
    across = {"f": along[1], "n": along[0], "x": beside, "y": beyond}

    class Chain:
        def __init__(self, index):
            matrix, quarter = divmod(index, PARTS)
            self.index, self.order, self.stage = index, CHUNK_ORDERS[index], 0
            self.own = part.at[matrix, quarter]
            self.came = [ref.at[matrix, quarter] for ref in (came_one, came_two, came_three, came_four)]
            self.final = sums.at[matrix, :, :, quarter]

        def cells(self, free, flipped=None):
            return tuple(
                slice(None) if name in free else 1 - here[name] if name == flipped else here[name]
                for name in "fnxy"
            )

        def send(self, source, target, other):
            sems = (send_sem.at[self.index, self.stage], recv_sem.at[self.index, self.stage])
            self.copy = remote(source, target, *sems, other)

        def advance(self):
            stage, order = self.stage, self.order
            if stage:
                self.copy.wait_recv()
            if 1 <= stage <= 4:
                free = order[stage:]
                for choice in itertools.product((0, 1), repeat=len(free)):
                    taken = dict(zip(sorted(free, key="fnxy".index), choice))
                    at = tuple(taken.get(name, here[name]) for name in "fnxy")
                    value = self.own[at] + self.came[stage - 1][choice]
                    if stage == 4:
                        self.final[core, y] = value
                    else:
                        self.own[at] = value
            if stage < 4:
                name = order[stage]
                source = self.own.at[self.cells(order[stage + 1 :], name)]
                self.send(source, self.came[stage], across[name])
            elif stage == 4:
                block = self.final.at[core, y]
                self.send(block, block, beyond)
            elif stage == 5:
                block = self.final.at[core]
                self.send(block, block, partner)
            self.stage += 1

    chains = [Chain(index) for index in range(3 * PARTS)]
    plan = iter(CHUNK_PLAN)

    def pump():
        for index in next(plan):
            chains[index].advance()

    def feed_forward(matrix, narrow, wide):
        left = transposed(narrow[...])

        def block(index, carry):
            cols = pl.ds(pl.multiple_of(index * UNIT, UNIT), UNIT)
            value = dot(left, wide[:, cols], 1, 0).astype(bf16)
            for side in range(2):
                for quarter in range(PARTS):
                    start = (side * PARTS + quarter) * CHUNK
                    part[matrix, quarter, index // 4, index // 2 % 2, index % 2, side] = value[
                        start : start + CHUNK
                    ]
            return carry

        lax.fori_loop(0, 8, block, 0)

    def projections(matrix, turned, narrow, width, offset, between=None):
        for tile in range(turned.shape[0] // UNIT):
            if between and tile % 2 == 0:
                between()
            value = dot(turned[tile * UNIT : (tile + 1) * UNIT, :], narrow[...], 1, 0).astype(bf16)
            for start in range(0, UNIT, CHUNK):
                block, row = divmod(tile * UNIT + start, width)
                side, row = divmod(offset + row, PARTS * CHUNK)
                part[matrix, row // CHUNK, block // 4, block // 2 % 2, block % 2, side] = value[
                    start : start + CHUNK
                ]

    grad_down_came.wait_recv()
    active_came.wait_recv()
    feed_forward(0, narrow_grad, active)

    for tile in range(FF // D):
        pump()
        cols = slice(tile * D, (tile + 1) * D)
        work[...] = dot(grad_down[...], down_w[cols, :], 1, 1)

        def gelu_back(rows, carry):
            low = (work[rows, :] * slope[rows, cols]).astype(bf16)
            grad_up[rows, cols] = low
            return carry + fold(low.astype(f32))

        put_vec(BIAS_UP + cols.start, column_sum(by_rows(tok, gelu_back, zero)))
    grad_up_came = to_partner(grad_up.at[own_rows], grad_up.at[far_rows])
    pump()
    normed_came.wait_recv()
    grad_up_came.wait_recv()
    feed_forward(1, narrow_normed, grad_up)
    pump()

    work[...] = dot(grad_up[own_rows, :], up_w[...], 1, 1)

    def norm_one_back(rows, carry):
        grad = grad_two[rows, :] + work[rows, :]
        zhat = zhat_one[rows, :]
        inner = grad * span(GAIN_ONE)
        grad_in = inner - row_mean(inner) - zhat * row_mean(inner * zhat)
        grad_in = grad_in * rstd_one[rows, 0:1]
        grad_one[rows, :] = grad_in
        low = grad_in.astype(bf16)
        grad_attn[rows, :] = low
        gain, shift, bias = carry
        return gain + fold(grad * zhat), shift + fold(grad), bias + fold(low.astype(f32))

    gain, shift, bias = by_rows(tok, norm_one_back, (zero, zero, zero))
    put_vec(GAIN_ONE, column_sum(gain))
    put_vec(SHIFT_ONE, column_sum(shift))
    put_vec(BIAS_OUT, column_sum(bias))
    grad_heads[...] = dot(grad_attn[...], out_w[...], 1, 1).astype(bf16)
    heads_turned[...] = dot(out_w[...], grad_attn[...], 1, 1).astype(bf16)

    half_lanes = LANES // 2
    pair_came = []
    for pair in range(HEADS // 2):
        pump()
        cols = slice(pair * LANES, (pair + 1) * LANES)
        values = keys_values[:, D + cols.start : D + cols.stop]
        for side, mask in enumerate(masks):
            rows = slice(cols.start + side * half_lanes, cols.start + (side + 1) * half_lanes)
            chance = prob[2 * pair + side].astype(f32)
            grad_chance = dot(grad_heads[:, cols] * mask, values, 1, 1)
            mean = jnp.sum(chance * grad_chance, axis=-1, keepdims=True)
            grad_score = (chance * (grad_chance - mean)).astype(bf16)
            values_grad = dot(heads_turned[rows, :], prob[2 * pair + side], 1, 0).astype(bf16)
            keys_grad = (dot(query_turned[rows, :], grad_score, 1, 0) * scale).astype(bf16)
            query_grad = (dot(keys_turned[rows, :], grad_score, 1, 1) * scale).astype(bf16)
            blocks = (
                query_grad,
                keys_grad[:, :tok],
                values_grad[:, :tok],
                keys_grad[:, tok:],
                values_grad[:, tok:],
            )
            for index, value in enumerate(blocks):
                start = index * LANES + side * half_lanes
                exchanged[0, pair, start : start + half_lanes, :] = value
        pair_came.append(to_partner(exchanged.at[0, pair], exchanged.at[1, pair]))
    pump()
    attn_turned[:, own_lanes] = transposed(grad_attn[...])
    grad_attn_came = to_partner(attn_turned.at[:, own_lanes], attn_turned.at[:, far_lanes])

    for pair, copy in enumerate(pair_came):
        copy.wait_recv()
        for who, lanes in enumerate((own_lanes, far_lanes)):
            start = pair * LANES
            mine, theirs = exchanged.at[who, pair], exchanged.at[1 - who, pair]
            qkv_turned[start : start + LANES, lanes] = mine[:LANES]
            for index in (1, 2):
                rows = slice(index * LANES, (index + 1) * LANES)
                sent = slice((index + 2) * LANES, (index + 3) * LANES)
                value = mine[rows].astype(f32) + theirs[sent].astype(f32)
                start = index * D + pair * LANES
                qkv_turned[start : start + LANES, lanes] = value.astype(bf16)
    pump()
    tokens_came.wait_recv()
    projections(2, qkv_turned, narrow_tokens, 3 * D // 8, 0, pump)
    attended_came.wait_recv()
    grad_attn_came.wait_recv()
    projections(2, attn_turned, narrow_attended, D // 8, 3 * D // 8)
    pump()

    ones = jnp.ones((8, tok), bf16)
    for start, rows in ((BIAS_QUERY, slice(0, D)), (BIAS_VALUE, slice(2 * D, 3 * D))):
        put_vec(start, dot(ones, qkv_turned[rows, own_lanes], 1, 1)[0:1])
    vec_came = to_partner(vec, vec_core)
    value = dot(qkv_w[...], qkv_turned[:, own_lanes], 1, 0)
    input_grad[...] = grad_one[...] + value.T

    vec_slots = [(send_sem.at[3 * PARTS, i], recv_sem.at[3 * PARTS, i]) for i in range(5)]

    def vec_steps():
        vec_came.wait_recv()
        vec_core[...] = vec[...] + vec_core[...]
        copy = remote(vec_core, vec_y, *vec_slots[0], beyond)
        yield
        copy.wait_recv()
        for i in range(4):
            vec_x[0, i] = vec_core[2 * i + x] + vec_y[2 * i + x]
            vec_x[1, i] = vec_core[2 * i + 1 - x] + vec_y[2 * i + 1 - x]
        copy = remote(vec_x.at[1], vec_x.at[2], *vec_slots[1], beside)
        yield
        copy.wait_recv()
        vec_x[0] = vec_x[0] + vec_x[2]
        copies = [
            remote(
                vec_x.at[0, flip_z(z, step)],
                vec_z.at[step - 1],
                *vec_slots[1 + step],
                along[step - 1],
            )
            for step in (1, 2, 3)
        ]
        yield
        total = vec_x[0, z]
        for step, copy in enumerate(copies):
            copy.wait_recv()
            total = total + vec_z[step]
        vec_sum[...] = total
        yield

    steps = vec_steps()
    for turn, index in enumerate(next(plan)):
        chains[index].advance()
        if turn % 10 == 9 and turn < 40:
            next(steps)
    for copy in started:
        copy.wait_send()


def layer(row_class, lengths, tokens, cotangent, vectors, qkv_w, out_w, up_w, down_w):
    tok = tokens.shape[0]
    chunk = (CHUNK, UNIT)

    def low(*dims):
        return pltpu.VMEM(dims, bf16)

    def wide(*dims):
        return pltpu.VMEM(dims, f32)

    return pl.pallas_call(
        layer_kernel,
        out_shape=(
            jax.ShapeDtypeStruct((tok, D), f32),
            jax.ShapeDtypeStruct((tok, D), f32),
            jax.ShapeDtypeStruct((3, 2, 2, PARTS) + chunk, bf16),
            jax.ShapeDtypeStruct((16, LANES), f32),
        ),
        in_specs=[SMEM, SMEM, VMEM, VMEM, VMEM] + [ANY] * 4,
        out_specs=(VMEM,) * 4,
        scratch_shapes=[
            low(D, 3 * D),
            low(D, D),
            low(D, FF),
            low(FF, D),
            low(tok, D),
            low(D, tok),
            low(2 * tok, 2 * D),
            low(D, 2 * tok),
            low(HEADS, tok, 2 * tok),
            low(tok, D),
            low(tok, D),
            low(tok, D),
            low(tok, D),
            low(2 * tok, HALF),
            low(2 * tok, HALF),
            low(2 * tok, HALF),
            low(2 * tok, HALF),
            low(2 * tok, FF),
            low(2 * tok, FF),
            low(D, 2 * tok),
            low(3 * D, 2 * tok),
            low(2, HEADS // 2, 5 * LANES, tok),
            low(tok, D),
            low(D, tok),
            wide(tok, FF),
            wide(tok, D),
            wide(tok, D),
            wide(tok, LANES),
            wide(tok, D),
            wide(tok, D),
            wide(8, 16, LANES),
            wide(8, 16, LANES),
            wide(8, 16, LANES),
            wide(3, 4, 16, LANES),
            wide(3, 16, LANES),
            low(3, PARTS, 2, 2, 2, 2, *chunk),
            low(3, PARTS, 2, 2, 2, *chunk),
            low(3, PARTS, 2, 2, *chunk),
            low(3, PARTS, 2, *chunk),
            low(3, PARTS, *chunk),
            pltpu.SemaphoreType.DMA((4,)),
            pltpu.SemaphoreType.DMA((15,)),
            pltpu.SemaphoreType.DMA((15,)),
            pltpu.SemaphoreType.DMA((3 * PARTS + 1, 6)),
            pltpu.SemaphoreType.DMA((3 * PARTS + 1, 6)),
        ],
        compiler_params=pltpu.CompilerParams(
            vmem_limit_bytes=63 * MIB, collective_id=0, has_side_effects=True
        ),
        name="layer",
    )(row_class, lengths, tokens, cotangent, vectors[None, :], qkv_w, out_w, up_w, down_w)


def update_kernel(
    head_ref,
    sums,
    qkv_hbm,
    out_hbm,
    up_hbm,
    down_hbm,
    qkv_new,
    out_new,
    up_new,
    down_new,
    chosen,
    qkv_old,
    out_old,
    up_old,
    down_old,
    load_sem,
):
    head_id = head_ref[0]
    qkv_cols = qkv_new.shape[0]
    loads = [
        pltpu.make_async_copy(source, target, load_sem.at[index])
        for index, (source, target) in enumerate(
            ((down_hbm, down_old), (up_hbm, up_old), (qkv_hbm, qkv_old), (out_hbm, out_old))
        )
    ]
    for load in loads:
        load.start()
    loads[0].wait()
    down_new[...] = muon_keep * down_old[...] + sums[0].astype(f32)
    loads[1].wait()
    up_new[...] = muon_keep * up_old[...] + sums[1].astype(f32)
    loads[2].wait()
    loads[3].wait()
    for half in range(2):
        cols = slice(half * HALF, (half + 1) * HALF)
        value = sums[2, cols].astype(f32)
        qkv_new[:, cols] = muon_keep * qkv_old[:, cols] + value[:qkv_cols]
        out_new[:, cols] = muon_keep * out_old[:, cols] + value[qkv_cols:]

    @pl.when(head_id == 0)
    def _():
        chosen[:, :qkv_cols] = qkv_new[...].T
        chosen[:, qkv_cols:] = jnp.zeros((D, UNIT - qkv_cols), f32)

    @pl.when(head_id == 1)
    def _():
        chosen[:, :qkv_cols] = jnp.zeros((D, qkv_cols), f32)
        chosen[:, qkv_cols:] = out_new[...].T

    @pl.when(head_id == 2)
    def _():
        chosen[...] = up_new[...]

    @pl.when(head_id == 3)
    def _():
        chosen[...] = down_new[...]


def update_moments(head, sums, *old):
    def like(value):
        return jax.ShapeDtypeStruct(value.shape, f32)

    return pl.pallas_call(
        update_kernel,
        out_shape=tuple(map(like, old)) + (like(old[2]),),
        in_specs=[SMEM, VMEM] + [ANY] * 4,
        out_specs=(VMEM,) * 5,
        scratch_shapes=[pltpu.VMEM(value.shape, f32) for value in old]
        + [pltpu.SemaphoreType.DMA((4,))],
        compiler_params=pltpu.CompilerParams(vmem_limit_bytes=61 * MIB),
        name="update_moments",
    )(head, sums, *old)


GROUP = 3
GRAM_AXES = ("far", "near", "x")
GRAM_ORDERS = tuple(
    tuple(GRAM_AXES["fnx".index(letter)] for letter in order)
    for order in ("xnf", "nxf", "xnf", "nxf", "xnf", "xnf", "fxn")
)
GRAM_PLAN = (0, 1, 2, 3, 6, 4, 0, 5, 1, 2, 0, 4, 3, 1, 6, 2, 5, 0, 3, 6, 1, 2, 4, 0, 5)
GRAM_PLAN += (3, 6, 1, 2, 4, 1, 5, 3, 6, 0, 4, 2, 5, 3, 6, 4, 1, 5, 0, 2, 3, 6, 4, 5)


def gram_kernel(moment, out, part, came_one, came_two, came_three, high, low, send_sem, recv_sem):
    z, x, y, core = position()
    here = {"far": z // 2, "near": z % 2, "x": x}
    others = {
        "far": device(flip_z(z, 2), x, y, core),
        "near": device(flip_z(z, 1), x, y, core),
        "x": device(z, 1 - x, y, core),
    }
    greet(list(others.values()))
    blocks = sub_blocks(moment.shape[0])
    groups = len(blocks) // GROUP
    high[...] = moment[...].astype(bf16)
    low[...] = (moment[...] - high[...].astype(f32)).astype(bf16)
    started = []

    def product(index):
        i, j = blocks[index]
        left, right = pl.ds(i * SUB, SUB), pl.ds(j * SUB, SUB)
        total = dot(high[left, :], high[right, :], 1, 1)
        total = total + dot(high[left, :], low[right, :], 1, 1)
        total = total + dot(low[left, :], high[right, :], 1, 1)
        rows = SUB // 8
        for owner in range(8):
            cell = (owner // 4, owner // 2 % 2, owner % 2)
            part[(index // GROUP,) + cell + (index % GROUP,)] = total[
                owner * rows : (owner + 1) * rows
            ]

    def send(source, target, group, slot, axis):
        copy = pltpu.make_async_remote_copy(
            src_ref=source,
            dst_ref=target,
            send_sem=send_sem.at[group, slot],
            recv_sem=recv_sem.at[group, slot],
            device_id=others[axis],
            device_id_type=MESH,
        )
        copy.start()
        started.append(copy)
        return copy

    def cells(fixed, flipped=None):
        return tuple(
            1 - here[name] if name == flipped else here[name] if name in fixed else slice(None)
            for name in GRAM_AXES
        )

    class Walk:
        def __init__(self, group, order):
            self.group, self.order, self.stage = group, order, 0
            self.part = part.at[group]
            self.came = (came_one.at[group], came_two.at[group], came_three.at[group])

        def advance(self):
            stage, order = self.stage, self.order
            mine = pl.ds(self.group * GROUP, GROUP)
            if stage:
                self.copy.wait_recv()
            if 1 <= stage <= 3:
                kept = cells(order[:stage])
                total = self.part[kept] + self.came[stage - 1][...]
                if stage == 3:
                    out[kept + (mine,)] = total
                else:
                    self.part[kept] = total
            if stage < 3:
                source = self.part.at[cells(order[:stage], order[stage])]
                self.copy = send(source, self.came[stage], self.group, stage, order[stage])
            elif stage < 6:
                block = out.at[cells(order[: 6 - stage]) + (mine,)]
                self.copy = send(block, block, self.group, stage, order[5 - stage])
            self.stage += 1

    walks = [Walk(group, GRAM_ORDERS[group]) for group in range(groups)]
    for group in GRAM_PLAN:
        if walks[group].stage == 0:
            for index in range(group * GROUP, (group + 1) * GROUP):
                product(index)
        walks[group].advance()
    for copy in started:
        copy.wait_send()


def gram_sum(moment):
    size, cols = moment.shape
    count = len(sub_blocks(size))
    groups = count // GROUP
    rows = (SUB // 8, SUB)
    return pl.pallas_call(
        gram_kernel,
        out_shape=jax.ShapeDtypeStruct((2, 2, 2, count) + rows, f32),
        in_specs=[VMEM],
        out_specs=VMEM,
        scratch_shapes=[
            pltpu.VMEM((groups, 2, 2, 2, GROUP) + rows, f32),
            pltpu.VMEM((groups, 2, 2, GROUP) + rows, f32),
            pltpu.VMEM((groups, 2, GROUP) + rows, f32),
            pltpu.VMEM((groups, GROUP) + rows, f32),
            pltpu.VMEM((size, cols), bf16),
            pltpu.VMEM((size, cols), bf16),
            pltpu.SemaphoreType.DMA((groups, 6)),
            pltpu.SemaphoreType.DMA((groups, 6)),
        ],
        compiler_params=pltpu.CompilerParams(
            vmem_limit_bytes=32 * MIB, collective_id=1, has_side_effects=True
        ),
        name="gram_sum",
    )(moment).reshape((8, count) + rows)


STRIPS = 2


def share_kernel(mine, out, send_sem, recv_sem):
    z, x, y, core = position()
    beyond = device(z, x, 1 - y, core)
    partner = device(z, x, y, 1 - core)
    greet([beyond, partner])
    own = 2 * y + core
    far = 2 * (1 - y) + core
    out[own] = mine[...]
    rows = mine.shape[0] // STRIPS
    started = []

    def send(slot, strip, kind, other):
        block = out.at[slot, pl.ds(strip * rows, rows)]
        copy = pltpu.make_async_remote_copy(
            src_ref=block,
            dst_ref=block,
            send_sem=send_sem.at[strip, kind],
            recv_sem=recv_sem.at[strip, kind],
            device_id=other,
            device_id_type=MESH,
        )
        copy.start()
        started.append(copy)
        return copy

    across = [send(own, strip, 0, beyond) for strip in range(STRIPS)]
    late = [send(own, strip, 1, partner) for strip in range(STRIPS)]
    for strip, copy in enumerate(across):
        copy.wait_recv()
        late.append(send(far, strip, 2, partner))
    for copy in late:
        copy.wait_recv()
    for copy in started:
        copy.wait_send()


def share_factors(mine):
    return pl.pallas_call(
        share_kernel,
        out_shape=jax.ShapeDtypeStruct((4,) + mine.shape, bf16),
        in_specs=[VMEM],
        out_specs=VMEM,
        scratch_shapes=[
            pltpu.SemaphoreType.DMA((STRIPS, 3)),
            pltpu.SemaphoreType.DMA((STRIPS, 3)),
        ],
        compiler_params=pltpu.CompilerParams(
            vmem_limit_bytes=16 * MIB, collective_id=2, has_side_effects=True
        ),
        name="share_factors",
    )(mine)


def window(start, width, total):
    size = -(-(width + 96) // LANES) * LANES
    first = jnp.minimum(start // LANES * LANES, total - size)
    return pl.ds(pl.multiple_of(first, LANES), size), start - first


def finish_kernel(
    factors,
    qkv_hbm,
    out_hbm,
    up_hbm,
    down_hbm,
    qkv_new,
    out_new,
    up_new,
    down_new,
    qkv_old,
    out_old,
    up_old,
    down_old,
    turned,
    load_sem,
):
    shrink = 1.0 - muon_rate * muon_decay
    dp_id = lax.axis_index("dp")
    qkv_cols, out_cols = qkv_new.shape[0], out_new.shape[0]
    qkv_lanes, qkv_skip = window(dp_id * qkv_cols, qkv_cols, 3 * D)
    out_lanes, out_skip = window(dp_id * out_cols, out_cols, D)
    block = pl.ds(pl.multiple_of(dp_id * UNIT, UNIT), UNIT)
    loads = [
        pltpu.make_async_copy(source, target, load_sem.at[index])
        for index, (source, target) in enumerate(
            (
                (up_hbm.at[:, block], up_old),
                (down_hbm.at[block], down_old),
                (qkv_hbm.at[:, qkv_lanes], qkv_old),
                (out_hbm.at[:, out_lanes], out_old),
            )
        )
    ]
    for load in loads:
        load.start()

    def step(index, rate):
        return muon_rate * rate * factors[index].astype(f32)

    loads[0].wait()
    up_new[...] = up_old[...].astype(f32) * shrink - step(2, math.sqrt(max(1.0, FF / D)))
    loads[1].wait()
    down_new[...] = down_old[...].astype(f32) * shrink - step(3, 1.0).T
    loads[2].wait()
    turned[...] = qkv_old[...].astype(f32).T
    rows = pl.ds(pl.multiple_of(qkv_skip, 32), qkv_cols)
    qkv_new[...] = turned[rows, :] * shrink - step(0, math.sqrt(3.0)).T[:qkv_cols]
    loads[3].wait()
    turned[: out_old.shape[1], :] = out_old[...].astype(f32).T
    rows = pl.ds(pl.multiple_of(out_skip, 32), out_cols)
    out_new[...] = turned[rows, :] * shrink - step(1, 1.0).T[qkv_cols:]


def finish_weights(factors, qkv_w, out_w, up_w, down_w, qkv_cols, out_cols):
    def shape(*dims):
        return jax.ShapeDtypeStruct(dims, f32)

    return pl.pallas_call(
        finish_kernel,
        out_shape=(shape(qkv_cols, D), shape(out_cols, D), shape(D, UNIT), shape(UNIT, D)),
        in_specs=[VMEM] + [ANY] * 4,
        out_specs=(VMEM,) * 4,
        scratch_shapes=[
            pltpu.VMEM((D, 384), bf16),
            pltpu.VMEM((D, 256), bf16),
            pltpu.VMEM((D, UNIT), bf16),
            pltpu.VMEM((UNIT, D), bf16),
            pltpu.VMEM((384, D), f32),
            pltpu.SemaphoreType.DMA((4,)),
        ],
        compiler_params=pltpu.CompilerParams(vmem_limit_bytes=48 * MIB),
        name="finish_weights",
    )(factors, qkv_w, out_w, up_w, down_w)


def swap(value, axis, bit):
    size = lax.axis_size(axis)
    return lax.ppermute(value, axis, [(i, i ^ bit) for i in range(size)])


def scatter_head(value, bit, position):
    half = value.shape[1] // 2
    mine = lax.dynamic_slice_in_dim(value, position * half, half, 1)
    other = lax.dynamic_slice_in_dim(value, (1 - position) * half, half, 1)
    return (mine.astype(f32) + swap(other, "head", bit).astype(f32)).astype(bf16)


def scatter_dp_pair(value, position):
    paired = value.reshape((value.shape[0] // 2, 2) + value.shape[1:])
    mine = lax.dynamic_index_in_dim(paired, position, 1, False)
    other = lax.dynamic_index_in_dim(paired, 1 - position, 1, False)
    return (mine.astype(f32) + swap(other, "dp", 1).astype(f32)).astype(bf16)


def scatter_dp_rest(value, place):
    ranks = value.shape[0]
    total = lax.dynamic_index_in_dim(value, place, 0, False).astype(f32)
    for step in range(1, ranks):
        sent = lax.dynamic_index_in_dim(value, place ^ step, 0, False)
        total = total + swap(sent, "dp", 2 * step).astype(f32)
    return total


def local(
    tokens,
    cotangent,
    qkv_weight,
    out_weight,
    up_weight,
    down_weight,
    vectors,
    qkv_moment,
    out_moment,
    up_moment,
    down_moment,
    adam_first,
    adam_second,
    bucket_class,
    row_lengths,
):
    n_dp = lax.axis_size("dp")
    n_head = lax.axis_size("head")
    dp_id = lax.axis_index("dp")
    head_id = lax.axis_index("head")
    core, side = head_id % 2, head_id // 2
    tok, width = tokens.shape
    hidden = up_weight.shape[1]
    half = width // 2
    qkv_cols, out_cols = qkv_moment.shape[1], out_moment.shape[1]
    shrink = 1.0 - muon_rate * muon_decay

    def weight_block(weight, cols, dim):
        return lax.dynamic_slice_in_dim(weight, dp_id * cols, cols, dim)

    block = head_id.astype(jnp.int32)[None]
    vec_len = vectors.shape[0] // n_dp
    if (n_dp, n_head, tok) == (8, 4, 256):
        mixed, input_grad, sums, vec = layer(
            bucket_class,
            row_lengths,
            tokens,
            cotangent,
            vectors,
            qkv_weight,
            out_weight,
            up_weight,
            down_weight,
        )
        grad_vec = vec[:VEC_BLOCK].reshape(vec_len)
        *moments, chosen = update_moments(
            block, sums.reshape(3, width, -1), qkv_moment.T, out_moment.T, up_moment, down_moment
        )
        factors = share_factors(orthogonalize(gram_sum(chosen), chosen))
        new_weights = finish_weights(
            factors, qkv_weight, out_weight, up_weight, down_weight, qkv_cols, out_cols
        )
        moments = [moments[0].T, moments[1].T, *moments[2:]]
        new_weights = [new_weights[0].T, new_weights[1].T, *new_weights[2:]]
    else:
        pieces = split_vectors(vectors, width, hidden)
        bias_query, bias_value, bias_out, gain_one, shift_one = pieces[:5]
        bias_up, bias_down, gain_two, shift_two = pieces[5:]
        bias_qkv = jnp.concatenate([bias_query, jnp.zeros_like(bias_query), bias_value])

        def column_half(value, which):
            return lax.dynamic_slice_in_dim(value, which * half, half, 1)

        qkv = (dot(tokens, qkv_weight, 1, 0) + bias_qkv).astype(bf16)
        other = swap(qkv[:, width:], "head", 1)
        attended = attend(block, bucket_class, row_lengths, qkv, other)
        attn_val = dot(attended, out_weight, 1, 0) + bias_out
        resid_one = tokens.astype(f32) + attn_val
        centre = resid_one - jnp.mean(resid_one, axis=-1, keepdims=True)
        rstd_one = lax.rsqrt(jnp.mean(centre * centre, axis=-1, keepdims=True) + norm_eps)
        zhat_one = centre * rstd_one
        normed_one = zhat_one * gain_one + shift_one
        normed_low = normed_one.astype(bf16)
        up_val = dot(normed_low, up_weight, 1, 0) + bias_up
        phi_cum = 0.5 * (1.0 + lax.erf(up_val * (0.5**0.5)))
        active_low = (up_val * phi_cum).astype(bf16)
        slope = phi_cum + up_val * jnp.exp(-0.5 * up_val * up_val) * (1.0 / math.sqrt(2.0 * math.pi))
        down_val = dot(active_low, down_weight, 1, 0) + bias_down
        resid_two = normed_one + down_val
        centre = resid_two - jnp.mean(resid_two, axis=-1, keepdims=True)
        rstd_two = lax.rsqrt(jnp.mean(centre * centre, axis=-1, keepdims=True) + norm_eps)
        zhat_two = centre * rstd_two
        mixed = zhat_two * gain_two + shift_two

        def norm_back(grad, gain, zhat, rstd):
            inner = grad * gain
            mean = jnp.mean(inner, axis=-1, keepdims=True)
            slant = jnp.mean(inner * zhat, axis=-1, keepdims=True)
            return (inner - mean - zhat * slant) * rstd, jnp.sum(grad * zhat, axis=0), jnp.sum(grad, axis=0)

        grad_two, grad_gain_two, grad_shift_two = norm_back(
            cotangent.astype(f32), gain_two, zhat_two, rstd_two
        )
        grad_down_low = grad_two.astype(bf16)
        grad_bias_down = jnp.sum(grad_down_low, axis=0, dtype=f32)

        x_id, z_id = dp_id % 2, dp_id // 2

        grad_up_low = (dot(grad_down_low, down_weight, 1, 1) * slope).astype(bf16)
        grad_bias_up = jnp.sum(grad_up_low, axis=0, dtype=f32)
        grad_normed = grad_two + dot(grad_up_low, up_weight, 1, 1)
        grad_one, grad_gain_one, grad_shift_one = norm_back(grad_normed, gain_one, zhat_one, rstd_one)
        grad_attn_low = grad_one.astype(bf16)
        grad_bias_out = jnp.sum(grad_attn_low, axis=0, dtype=f32)
        grad_heads = dot(grad_attn_low, out_weight, 1, 1).astype(bf16)
        grad_query, own, sent = attend_back(block, bucket_class, row_lengths, qkv, other, grad_heads)
        grad_kv = (own + swap(sent, "head", 1).astype(f32)).astype(bf16)
        grad_qkv = jnp.concatenate([grad_query, grad_kv], axis=1)
        grad_bias_qkv = jnp.sum(grad_qkv, axis=0, dtype=f32)
        input_grad = grad_one + dot(grad_qkv, qkv_weight, 1, 1)
        grad_vector = jnp.concatenate(
            [
                grad_bias_qkv[:width],
                grad_bias_qkv[2 * width :],
                grad_bias_out,
                grad_gain_one,
                grad_shift_one,
                grad_bias_up,
                grad_bias_down,
                grad_gain_two,
                grad_shift_two,
            ]
        )
        grad_vector = grad_vector + swap(grad_vector, "head", 1)
        wides = [active_low, grad_up_low, grad_attn_low, grad_qkv]
        narrows = [grad_down_low, normed_low, attended, tokens]

        def both_halves(value):
            return jnp.concatenate(
                [column_half(value, core), swap(column_half(value, 1 - core), "head", 1)], axis=0
            )

        def weight_grad(wide, narrow):
            wide = jnp.concatenate([wide, swap(wide, "head", 1)], axis=0)
            value = dot(wide, both_halves(narrow), 0, 0).astype(bf16)
            return value.reshape(n_dp, value.shape[0] // n_dp, half)

        def reduce_y_first(value):
            return scatter_dp_rest(scatter_dp_pair(scatter_head(value, 2, side), x_id), z_id)

        def reduce_x_first(value):
            return scatter_dp_rest(scatter_head(scatter_dp_pair(value, x_id), 2, side), z_id)

        def spread(value):
            value = value.astype(bf16)
            came = swap(value, "head", 2)
            value = jnp.concatenate(
                [jnp.where(side == 0, value, came), jnp.where(side == 0, came, value)], axis=0
            )
            came = swap(value, "head", 1)
            return jnp.concatenate(
                [jnp.where(core == 0, value, came), jnp.where(core == 0, came, value)], axis=1
            ).astype(f32)

        down_part, up_part, out_part, qkv_part = [
            weight_grad(wide, narrow) for wide, narrow in zip(wides, narrows)
        ]
        vec_rows = 16
        vec_part = grad_vector.reshape(n_dp, vec_len)
        vec_part = jnp.pad(vec_part, ((0, 0), (0, vec_rows * width - vec_len)))
        vec_part = vec_part.reshape(n_dp, vec_rows, width)
        vec_part = lax.dynamic_slice_in_dim(vec_part, core * half, half, 2).astype(bf16)
        down_new = spread(reduce_x_first(down_part))
        up_new = spread(reduce_y_first(up_part))
        tail_new = spread(
            reduce_y_first(jnp.concatenate([qkv_part, out_part, vec_part], axis=1))
        )
        grads = [
            tail_new[:qkv_cols].T,
            tail_new[qkv_cols : qkv_cols + out_cols].T,
            up_new.T,
            down_new.T,
        ]
        grad_vec = tail_new[qkv_cols + out_cols :].reshape(-1)[:vec_len]
        moments = [
            muon_keep * old + grad
            for old, grad in zip([qkv_moment, out_moment, up_moment, down_moment], grads)
        ]
        most = max(m.shape[1] for m in moments)
        padded = [jnp.pad(m, ((0, 0), (0, most - m.shape[1]))) for m in moments]
        chosen = padded[-1]
        for index in range(len(padded) - 2, -1, -1):
            chosen = jnp.where(head_id == index, padded[index], chosen)
        gram_mat = lax.dot_general(
            chosen, chosen, (((1,), (1,)), ((), ())), precision=lax.Precision.HIGH
        )
        own_factor = orthogonalize(lax.psum(gram_mat, "dp"), chosen)
        across = swap(own_factor, "head", 2)
        low_pair = jnp.where(side == 0, own_factor, across)
        high_pair = jnp.where(side == 0, across, own_factor)
        near_low = swap(low_pair, "head", 1)
        near_high = swap(high_pair, "head", 1)
        factors = [
            jnp.where(core == 0, low_pair, near_low),
            jnp.where(core == 0, near_low, low_pair),
            jnp.where(core == 0, high_pair, near_high),
            jnp.where(core == 0, near_high, high_pair),
        ]
        factors = [o[:, : m.shape[1]].astype(f32) for o, m in zip(factors, moments)]
        factors[3] = factors[3].T
        old_weights = [
            weight_block(qkv_weight, qkv_cols, 1),
            weight_block(out_weight, out_cols, 1),
            weight_block(up_weight, up_moment.shape[1], 1),
            weight_block(down_weight, down_moment.shape[1], 0),
        ]

        rates = (math.sqrt(3.0), 1.0, math.sqrt(max(1.0, hidden / width)), 1.0)
        new_weights = [
            old.astype(f32) * shrink - muon_rate * rate * factor
            for old, rate, factor in zip(old_weights, rates, factors)
        ]

    vec_old = lax.dynamic_slice_in_dim(vectors, dp_id * vec_len, vec_len, 0)
    vec_first = beta_first * adam_first + (1.0 - beta_first) * grad_vec
    vec_second = beta_second * adam_second + (1.0 - beta_second) * grad_vec * grad_vec
    first_hat = vec_first / (1.0 - beta_first**STEP)
    second_hat = vec_second / (1.0 - beta_second**STEP)
    vec_new = vec_old - adam_rate * first_hat / (jnp.sqrt(second_hat) + adam_eps)
    return (mixed, input_grad, *moments, *new_weights, vec_first, vec_second, vec_new)


def solution(mesh):
    tokens_spec = P(("dp", "head"), None)
    block_spec = P(None, "dp")
    return jax.shard_map(
        local,
        mesh=mesh,
        in_specs=(
            tokens_spec,
            tokens_spec,
            P(),
            P(),
            P(),
            P(),
            P(),
            block_spec,
            block_spec,
            block_spec,
            block_spec,
            P("dp"),
            P("dp"),
            P("dp"),
            P("dp", None),
        ),
        out_specs=(
            tokens_spec,
            tokens_spec,
            block_spec,
            block_spec,
            block_spec,
            block_spec,
            block_spec,
            block_spec,
            block_spec,
            P("dp", None),
            P("dp"),
            P("dp"),
            P("dp"),
        ),
        check_vma=False,
    )
```

```python
import functools
import itertools
import math

import jax
import jax.numpy as jnp
from jax import lax
from jax.experimental import pallas as pl
from jax.experimental.pallas import tpu as pltpu
from jax.sharding import PartitionSpec as P

D = 768
HEADS = 12
HEAD_DIM = 64
FF = 3072
BASE_LEN = 128
NS_STEPS = 5
STEP = 5
MAX_LEN = 512

f32 = jnp.float32
bf16 = jnp.bfloat16

norm_eps = 1e-12
masked_score = -1000000000.0
quintic_a = 3.4445
quintic_b = -4.775
quintic_c = 2.0315
muon_rate = 1.0
muon_decay = 0.01
muon_keep = 0.5
adam_rate = 0.2
beta_first = 0.9
beta_second = 0.999
adam_eps = 1e-08
MIB = 1024 * 1024


def dot(left, right, left_dim, right_dim):
    return lax.dot_general(
        left, right, (((left_dim,), (right_dim,)), ((), ())), preferred_element_type=f32
    )


def split_vectors(vectors, width, hidden):
    lengths_list = [width] * 5 + [hidden] + [width] * 3
    pieces = []
    offset = 0
    for length in lengths_list:
        pieces.append(vectors[offset : offset + length])
        offset = offset + length
    return pieces


def allowed_mask(class_ref, length_ref, block, tok):
    shift = class_ref[0] + int(math.log2(BASE_LEN))
    query_place = block * tok + lax.broadcasted_iota(jnp.int32, (tok, 1), 0)
    lane = lax.broadcasted_iota(jnp.int32, (1, 2 * tok), 1)
    own = lane < tok
    key_place = jnp.where(own, block * tok + lane, (block ^ 1) * tok + lane - tok)
    key_row = lax.shift_right_logical(key_place, jnp.broadcast_to(shift, key_place.shape))
    offset = key_place - lax.shift_left(key_row, jnp.broadcast_to(shift, key_place.shape))
    row_len = jnp.zeros_like(key_row)
    for slot in range(length_ref.shape[1]):
        row_len = jnp.where(key_row == slot, length_ref[0, slot], row_len)
    key_row = jnp.where(offset < row_len, key_row, -1)
    query_row = lax.shift_right_logical(query_place, jnp.broadcast_to(shift, query_place.shape))
    return query_row == key_row


def half_masks():
    lane = lax.broadcasted_iota(jnp.int32, (1, 2 * HEAD_DIM), 1)
    first = (lane < HEAD_DIM).astype(f32)
    return (first.astype(bf16), (1.0 - first).astype(bf16)), lane < HEAD_DIM


def head_prob(query, keys, allowed):
    score = jnp.where(allowed, dot(query, keys, 1, 1) * HEAD_DIM ** (-0.5), masked_score)
    exponent = jnp.exp(score - jnp.max(score, axis=-1, keepdims=True))
    return exponent / jnp.sum(exponent, axis=-1, keepdims=True)


def attend_kernel(block_ref, class_ref, length_ref, qkv_ref, other_ref, out_ref):
    tok = qkv_ref.shape[0]
    allowed = allowed_mask(class_ref, length_ref, block_ref[0], tok)
    masks, first = half_masks()
    for pair in range(HEADS // 2):
        cols = pl.ds(pair * 2 * HEAD_DIM, 2 * HEAD_DIM)
        kcols = pl.ds(D + pair * 2 * HEAD_DIM, 2 * HEAD_DIM)
        vcols = pl.ds(2 * D + pair * 2 * HEAD_DIM, 2 * HEAD_DIM)
        query = qkv_ref[:, cols]
        keys = jnp.concatenate([qkv_ref[:, kcols], other_ref[:, cols]], axis=0)
        values = jnp.concatenate([qkv_ref[:, vcols], other_ref[:, kcols]], axis=0)
        outs = []
        for mask in masks:
            prob = head_prob(query * mask, keys, allowed)
            outs.append(dot(prob.astype(bf16), values, 1, 0))
        out_ref[:, cols] = jnp.where(first, outs[0], outs[1]).astype(bf16)


def attend_back_kernel(
    block_ref, class_ref, length_ref, qkv_ref, other_ref, grad_ref, dq_ref, own_ref, send_ref
):
    tok = qkv_ref.shape[0]
    allowed = allowed_mask(class_ref, length_ref, block_ref[0], tok)
    masks, first = half_masks()
    scale = HEAD_DIM ** (-0.5)
    for pair in range(HEADS // 2):
        cols = pl.ds(pair * 2 * HEAD_DIM, 2 * HEAD_DIM)
        kcols = pl.ds(D + pair * 2 * HEAD_DIM, 2 * HEAD_DIM)
        vcols = pl.ds(2 * D + pair * 2 * HEAD_DIM, 2 * HEAD_DIM)
        query = qkv_ref[:, cols]
        keys = jnp.concatenate([qkv_ref[:, kcols], other_ref[:, cols]], axis=0)
        values = jnp.concatenate([qkv_ref[:, vcols], other_ref[:, kcols]], axis=0)
        grad = grad_ref[:, cols]
        dqs, dk, dv = [], None, None
        for mask in masks:
            head_query = query * mask
            head_grad = grad * mask
            prob = head_prob(head_query, keys, allowed)
            part_v = dot(prob.astype(bf16), head_grad, 0, 0)
            dprob = dot(head_grad, values, 1, 1)
            dscore = prob * (dprob - jnp.sum(prob * dprob, axis=-1, keepdims=True))
            dscore = dscore.astype(bf16)
            dqs.append(dot(dscore, keys, 1, 0))
            part_k = dot(dscore, head_query, 0, 0)
            dk = part_k if dk is None else dk + part_k
            dv = part_v if dv is None else dv + part_v
        dk = dk * scale
        dq_ref[:, cols] = (jnp.where(first, dqs[0], dqs[1]) * scale).astype(bf16)
        own_ref[:, cols] = dk[:tok]
        own_ref[:, kcols] = dv[:tok]
        send_ref[:, cols] = dk[tok:].astype(bf16)
        send_ref[:, kcols] = dv[tok:].astype(bf16)


SMEM = pl.BlockSpec(memory_space=pltpu.SMEM)
VMEM = pl.BlockSpec(memory_space=pltpu.VMEM)
ANY = pl.BlockSpec(memory_space=pl.ANY)


def attend(block, row_class, lengths, qkv, other):
    tok = qkv.shape[0]
    return pl.pallas_call(
        attend_kernel,
        out_shape=jax.ShapeDtypeStruct((tok, D), bf16),
        in_specs=[SMEM, SMEM, SMEM, VMEM, VMEM],
        out_specs=VMEM,
        compiler_params=pltpu.CompilerParams(vmem_limit_bytes=32 * MIB),
        name="attend",
    )(block, row_class, lengths, qkv, other)


def attend_back(block, row_class, lengths, qkv, other, grad):
    tok = qkv.shape[0]
    return pl.pallas_call(
        attend_back_kernel,
        out_shape=(
            jax.ShapeDtypeStruct((tok, D), bf16),
            jax.ShapeDtypeStruct((tok, 2 * D), f32),
            jax.ShapeDtypeStruct((tok, 2 * D), bf16),
        ),
        in_specs=[SMEM, SMEM, SMEM, VMEM, VMEM, VMEM],
        out_specs=(VMEM, VMEM, VMEM),
        compiler_params=pltpu.CompilerParams(vmem_limit_bytes=32 * MIB),
        name="attend_back",
    )(block, row_class, lengths, qkv, other, grad)


CENTRES = (0.0, 0.0, 0.0, 0.8, 0.8)
TILE = 256
SUB = 128


def sub_blocks(size):
    count = size // SUB
    return [(i, j) for i in range(count) for j in range(i, count)]


def newton_schulz(gram, moment, e, f, g, eb, fb, gb, ya, yb, y, emit):
    size = e.shape[0]
    tiles = [slice(i * TILE, (i + 1) * TILE) for i in range(size // TILE)]

    def unit(rows):
        row_id = rows.start + lax.broadcasted_iota(jnp.int32, (TILE, size), 0)
        col_id = lax.broadcasted_iota(jnp.int32, (TILE, size), 1)
        return (row_id == col_id).astype(f32)

    diagonal = jnp.zeros((TILE, size), f32)
    for rows in tiles:
        diagonal = diagonal + gram[rows, :] * unit(rows)
    trace = jnp.sum(jnp.sum(diagonal, axis=0, keepdims=True), axis=1, keepdims=True)
    factor = 1.0 / (jnp.sqrt(trace) + 1e-07)
    square_factor = factor * factor
    for rows in tiles:
        value = gram[rows, :] * square_factor
        e[rows, :] = value
        eb[rows, :] = value.astype(bf16)
        value = moment[rows, :] * factor
        y[rows, :] = value
        ya[rows, :] = value.astype(bf16)
    now, then = ya, yb
    for step in range(NS_STEPS):
        last = step + 1 == NS_STEPS
        centre = CENTRES[step]
        after = 0.0 if last else CENTRES[step + 1]
        keep = quintic_a + quintic_b * centre + quintic_c * centre * centre
        linear = quintic_b + 2.0 * quintic_c * centre
        for rows in tiles:
            value = linear * e[rows, :] + quintic_c * dot(eb[rows, :], eb[...], 1, 0)
            fb[rows, :] = value.astype(bf16)
            if not last:
                f[rows, :] = value
        for rows in tiles:
            value = keep * y[rows, :] + dot(fb[rows, :], now[...], 1, 0)
            if last:
                emit(rows, value.astype(bf16))
            else:
                y[rows, :] = value
                then[rows, :] = value.astype(bf16)
        if last:
            break
        now, then = then, now
        for rows in tiles:
            value = keep * e[rows, :] + dot(eb[rows, :], fb[...], 1, 0)
            if centre:
                value = value + centre * f[rows, :]
            g[rows, :] = value
            gb[rows, :] = value.astype(bf16)
        for rows in tiles:
            value = keep * g[rows, :] + dot(gb[rows, :], fb[...], 1, 0)
            if centre:
                value = value + (centre * keep) * f[rows, :]
            shift = centre * keep * keep - after
            if shift:
                value = value + shift * unit(rows)
            e[rows, :] = value
            eb[rows, :] = value.astype(bf16)


def ortho_kernel(gram, moment, out, *scratch):
    def emit(rows, value):
        out[rows, :] = value

    newton_schulz(gram, moment, *scratch, emit)


def ortho_scratch(size, cols):
    square, square_low = pltpu.VMEM((size, size), f32), pltpu.VMEM((size, size), bf16)
    wide_low = pltpu.VMEM((size, cols), bf16)
    return [square] * 3 + [square_low] * 3 + [wide_low] * 2 + [pltpu.VMEM((size, cols), f32)]


def orthogonalize(gram_mat, moment):
    size, cols = moment.shape
    return pl.pallas_call(
        ortho_kernel,
        out_shape=jax.ShapeDtypeStruct((size, cols), bf16),
        in_specs=[VMEM, VMEM],
        out_specs=VMEM,
        scratch_shapes=ortho_scratch(size, cols),
        compiler_params=pltpu.CompilerParams(vmem_limit_bytes=48 * MIB),
        name="ortho",
    )(gram_mat, moment)


MESH = pl.DeviceIdType.MESH
CHUNK = 48
PARTS = 4
UNIT = 2 * PARTS * CHUNK
HALF = D // 2
LANES = 128
VEC_BLOCK = 9
ROWS = 16
CHUNK_ORDERS = (
    "xyfn", "nxyf", "nxfy", "ynfx",
    "yxnf", "ynfx", "xnyf", "yxnf",
    "nyxf", "xfyn", "yxnf", "xnyf",
)
CHUNK_PLAN = (
    (0, 1, 2, 3),
    (),
    (),
    (),
    (),
    (0, 3, 4, 5, 6),
    (),
    (),
    (),
    (),
    (6, 1, 2),
    (3, 0),
    (),
    (),
    (6,),
    (1, 2, 4, 5, 7),
    (3, 0),
    (6, 8, 9, 1, 3, 10, 11),
    (
        0, 2, 4, 3, 6, 1, 3, 5, 0, 2, 4, 0, 6, 1, 6, 1, 2, 2, 4, 5, 9, 11, 7, 5,
        4, 4, 8, 5, 10, 7, 5, 8, 9, 10, 11, 7, 8, 9, 11, 7, 10, 8, 9, 7, 8, 7, 11, 9,
        8, 10, 9, 11, 10, 11, 10,
    ),
)
BIAS_QUERY, BIAS_VALUE, BIAS_OUT, GAIN_ONE, SHIFT_ONE, BIAS_UP = (i * D for i in range(6))
BIAS_DOWN, GAIN_TWO, SHIFT_TWO = (BIAS_UP + FF + i * D for i in range(3))


def position():
    dp_id, head_id = lax.axis_index("dp"), lax.axis_index("head")
    z, x = dp_id // 2, dp_id % 2
    y, core = head_id // 2, head_id % 2
    return z, x, y, core


def device(z, x, y, core):
    return (2 * z + x, 2 * y + core)


def flip_z(z, step):
    high, low = z // 2, z % 2
    high = 1 - high if step // 2 else high
    low = 1 - low if step % 2 else low
    return 2 * high + low


def greet(others):
    barrier = pltpu.get_barrier_semaphore()
    for other in others:
        pl.semaphore_signal(barrier, inc=1, device_id=other, device_id_type=MESH)
    pl.semaphore_wait(barrier, len(others))


def by_rows(count, body, init=None, together=4):
    def step(index, carry):
        for part in range(together):
            start = (index * together + part) * ROWS
            carry = body(pl.ds(pl.multiple_of(start, ROWS), ROWS), carry)
        return carry

    return lax.fori_loop(0, count // (ROWS * together), step, init)


def row_mean(value):
    return jnp.sum(value, axis=-1, keepdims=True) * (1.0 / D)


def fold(value):
    return jnp.sum(value.reshape(value.shape[0] // 8, 8, value.shape[1]), axis=0)


def column_sum(value):
    return jnp.sum(value, axis=0, keepdims=True)


def normal_parts(value):
    size = jnp.abs(value)
    decay = jnp.exp(-0.5 * value * value)
    t = 1.0 / (1.0 + (0.3275911 * 0.5**0.5) * size)
    series = t * (1.061405429 * 0.5)
    for term in (-1.453152027, 1.421413741, -0.284496736, 0.254829592):
        series = (series + term * 0.5) * t
    tail = series * decay
    return jnp.where(value < 0.0, tail, 1.0 - tail), decay * (1.0 / math.sqrt(2.0 * math.pi))


def transposed(value):
    side = 2 * LANES
    row_id = lax.broadcasted_iota(jnp.int32, (side, side), 0)
    unit = (row_id == lax.broadcasted_iota(jnp.int32, (side, side), 1)).astype(f32).astype(bf16)
    blocks = []
    for start in range(0, value.shape[1], side):
        block = value[:, start : start + side]
        size = block.shape[1]
        blocks.append(dot(unit[:size, :size], block, 1, 1).astype(bf16))
    return jnp.concatenate(blocks, axis=0)


def layer_kernel(
    row_class,
    lengths,
    tokens,
    cotangent,
    vectors,
    qkv_hbm,
    out_hbm,
    up_hbm,
    down_hbm,
    mixed,
    input_grad,
    sums,
    vec_sum,
    qkv_w,
    out_w,
    up_w,
    down_w,
    query,
    query_turned,
    keys_values,
    keys_turned,
    prob,
    attended,
    normed_low,
    grad_down,
    grad_attn,
    narrow_tokens,
    narrow_attended,
    narrow_normed,
    narrow_grad,
    active,
    grad_up,
    attn_turned,
    qkv_turned,
    exchanged,
    grad_heads,
    heads_turned,
    slope,
    normed_one,
    zhat_one,
    rstd_one,
    grad_two,
    work,
    vec,
    vec_core,
    vec_y,
    vec_x,
    vec_z,
    part,
    came_one,
    came_two,
    came_three,
    came_four,
    load_sem,
    pair_send,
    pair_recv,
    send_sem,
    recv_sem,
):
    grad_one = normed_one
    z, x, y, core = position()
    tok = tokens.shape[0]
    loads = {
        name: pltpu.make_async_copy(source, target, load_sem.at[index])
        for index, (name, source, target) in enumerate(
            (
                ("qkv", qkv_hbm, qkv_w),
                ("out", out_hbm, out_w),
                ("up", up_hbm, up_w),
                ("down", down_hbm, down_w),
            )
        )
    }
    loads["qkv"].start()
    beyond = device(z, x, 1 - y, core)
    beside = device(z, 1 - x, y, core)
    partner = device(z, x, y, 1 - core)
    along = [device(flip_z(z, step), x, y, core) for step in (1, 2, 3)]
    greet([beyond, beside, partner] + along)
    started = []

    def remote(source, target, send_at, recv_at, other):
        copy = pltpu.make_async_remote_copy(
            src_ref=source,
            dst_ref=target,
            send_sem=send_at,
            recv_sem=recv_at,
            device_id=other,
            device_id_type=MESH,
        )
        copy.start()
        started.append(copy)
        return copy

    pair_count = []

    def to_partner(source, target):
        slot = len(pair_count)
        pair_count.append(slot)
        return remote(source, target, pair_send.at[slot], pair_recv.at[slot], partner)

    own_half = pl.ds(pl.multiple_of(core * HALF, HALF), HALF)
    other_half = pl.ds(pl.multiple_of((1 - core) * HALF, HALF), HALF)

    def span(start, length=D):
        return vectors[0:1, start : start + length]

    def put_vec(start, value):
        for index in range(value.shape[1] // LANES):
            block, row = divmod(start // LANES + index, VEC_BLOCK)
            vec[block, row : row + 1, :] = value[:, index * LANES : (index + 1) * LANES]

    vec[...] = jnp.zeros_like(vec)

    own_rows = pl.ds(0, tok)
    far_rows = pl.ds(tok, tok)
    own_lanes, far_lanes = own_rows, far_rows

    def share_half(value, narrow):
        narrow[own_rows, :] = value[:, own_half]
        return to_partner(value.at[:, other_half], narrow.at[far_rows])

    tokens_came = share_half(tokens, narrow_tokens)
    loads["qkv"].wait()
    for name in ("out", "up", "down"):
        loads[name].start()
    for index, start in ((1, None), (2, BIAS_VALUE)):
        value = dot(tokens[...], qkv_w[:, index * D : (index + 1) * D], 1, 0)
        if start is not None:
            value = value + span(start)
        keys_values[own_rows, (index - 1) * D : index * D] = value.astype(bf16)
    kv_arrived = to_partner(keys_values.at[own_rows], keys_values.at[far_rows])
    value = dot(tokens[...], qkv_w[:, :D], 1, 0) + span(BIAS_QUERY)
    query[...] = value.astype(bf16)
    query_turned[...] = transposed(query[...])
    allowed = allowed_mask(row_class, lengths, 2 * y + core, tok)
    masks, first = half_masks()
    kv_arrived.wait_recv()

    scale = HEAD_DIM ** (-0.5)
    for pair in range(HEADS // 2):
        cols = slice(pair * LANES, (pair + 1) * LANES)
        keys = keys_values[:, cols]
        values = keys_values[:, D + cols.start : D + cols.stop]
        outs = []
        for side, mask in enumerate(masks):
            score = dot(query[:, cols] * (mask * scale), keys, 1, 1)
            score = jnp.where(allowed, score, masked_score)
            exponent = jnp.exp(score - jnp.max(score, axis=-1, keepdims=True))
            chance = exponent * (1.0 / jnp.sum(exponent, axis=-1, keepdims=True))
            prob[2 * pair + side] = chance.astype(bf16)
            outs.append(dot(prob[2 * pair + side], values, 1, 0))
        attended[:, cols] = jnp.where(first, outs[0], outs[1]).astype(bf16)
    attended_came = share_half(attended, narrow_attended)

    loads["out"].wait()
    work[...] = dot(attended[...], out_w[...], 1, 0)

    def norm_one(rows, carry):
        value = tokens[rows, :].astype(f32) + (work[rows, :] + span(BIAS_OUT))
        centre = value - row_mean(value)
        rstd = lax.rsqrt(row_mean(centre * centre) + norm_eps)
        zhat = centre * rstd
        normed = zhat * span(GAIN_ONE) + span(SHIFT_ONE)
        zhat_one[rows, :] = zhat
        rstd_one[rows, :] = jnp.broadcast_to(rstd, (ROWS, LANES))
        normed_one[rows, :] = normed
        normed_low[rows, :] = normed.astype(bf16)
        return carry

    by_rows(tok, norm_one)
    normed_came = share_half(normed_low, narrow_normed)

    loads["up"].wait()
    for tile in range(FF // D):
        cols = slice(tile * D, (tile + 1) * D)
        work[...] = dot(normed_low[...], up_w[:, cols], 1, 0)

        def gelu(rows, carry):
            value = work[rows, :] + span(BIAS_UP + cols.start)
            chance, density = normal_parts(value)
            active[rows, cols] = (value * chance).astype(bf16)
            slope[rows, cols] = chance + value * density
            return carry

        by_rows(tok, gelu)
    active_came = to_partner(active.at[own_rows], active.at[far_rows])
    loads["down"].wait()
    work[...] = dot(active[own_rows, :], down_w[...], 1, 0)

    def norm_two(rows, carry):
        value = normed_one[rows, :] + (work[rows, :] + span(BIAS_DOWN))
        centre = value - row_mean(value)
        rstd = lax.rsqrt(row_mean(centre * centre) + norm_eps)
        zhat = centre * rstd
        mixed[rows, :] = zhat * span(GAIN_TWO) + span(SHIFT_TWO)
        grad = cotangent[rows, :].astype(f32)
        inner = grad * span(GAIN_TWO)
        grad_in = (inner - row_mean(inner) - zhat * row_mean(inner * zhat)) * rstd
        grad_two[rows, :] = grad_in
        low = grad_in.astype(bf16)
        grad_down[rows, :] = low
        gain, shift, bias = carry
        return gain + fold(grad * zhat), shift + fold(grad), bias + fold(low.astype(f32))

    zero = jnp.zeros((8, D), f32)
    gain, shift, bias = by_rows(tok, norm_two, (zero, zero, zero))
    put_vec(GAIN_TWO, column_sum(gain))
    put_vec(SHIFT_TWO, column_sum(shift))
    put_vec(BIAS_DOWN, column_sum(bias))
    grad_down_came = share_half(grad_down, narrow_grad)
    keys_turned[...] = transposed(keys_values[:, :D])

    here = {"f": z // 2, "n": z % 2, "x": x, "y": y}
    across = {"f": along[1], "n": along[0], "x": beside, "y": beyond}

    class Chain:
        def __init__(self, index):
            matrix, quarter = divmod(index, PARTS)
            self.index, self.order, self.stage = index, CHUNK_ORDERS[index], 0
            self.own = part.at[matrix, quarter]
            self.came = [ref.at[matrix, quarter] for ref in (came_one, came_two, came_three, came_four)]
            self.final = sums.at[matrix, :, :, quarter]

        def cells(self, free, flipped=None):
            return tuple(
                slice(None) if name in free else 1 - here[name] if name == flipped else here[name]
                for name in "fnxy"
            )

        def send(self, source, target, other):
            sems = (send_sem.at[self.index, self.stage], recv_sem.at[self.index, self.stage])
            self.copy = remote(source, target, *sems, other)

        def advance(self):
            stage, order = self.stage, self.order
            if stage:
                self.copy.wait_recv()
            if 1 <= stage <= 4:
                free = order[stage:]
                for choice in itertools.product((0, 1), repeat=len(free)):
                    taken = dict(zip(sorted(free, key="fnxy".index), choice))
                    at = tuple(taken.get(name, here[name]) for name in "fnxy")
                    value = self.own[at] + self.came[stage - 1][choice]
                    if stage == 4:
                        self.final[core, y] = value
                    else:
                        self.own[at] = value
            if stage < 4:
                name = order[stage]
                source = self.own.at[self.cells(order[stage + 1 :], name)]
                self.send(source, self.came[stage], across[name])
            elif stage == 4:
                block = self.final.at[core, y]
                self.send(block, block, beyond)
            elif stage == 5:
                block = self.final.at[core]
                self.send(block, block, partner)
            self.stage += 1

    chains = [Chain(index) for index in range(3 * PARTS)]
    plan = iter(CHUNK_PLAN)

    def pump():
        for index in next(plan):
            chains[index].advance()

    def feed_forward(matrix, narrow, wide):
        left = transposed(narrow[...])

        def block(index, carry):
            cols = pl.ds(pl.multiple_of(index * UNIT, UNIT), UNIT)
            value = dot(left, wide[:, cols], 1, 0).astype(bf16)
            for side in range(2):
                for quarter in range(PARTS):
                    start = (side * PARTS + quarter) * CHUNK
                    part[matrix, quarter, index // 4, index // 2 % 2, index % 2, side] = value[
                        start : start + CHUNK
                    ]
            return carry

        lax.fori_loop(0, 8, block, 0)

    def projections(matrix, turned, narrow, width, offset, between=None):
        for tile in range(turned.shape[0] // UNIT):
            if between and tile % 2 == 0:
                between()
            value = dot(turned[tile * UNIT : (tile + 1) * UNIT, :], narrow[...], 1, 0).astype(bf16)
            for start in range(0, UNIT, CHUNK):
                block, row = divmod(tile * UNIT + start, width)
                side, row = divmod(offset + row, PARTS * CHUNK)
                part[matrix, row // CHUNK, block // 4, block // 2 % 2, block % 2, side] = value[
                    start : start + CHUNK
                ]

    grad_down_came.wait_recv()
    active_came.wait_recv()
    feed_forward(0, narrow_grad, active)

    for tile in range(FF // D):
        pump()
        cols = slice(tile * D, (tile + 1) * D)
        work[...] = dot(grad_down[...], down_w[cols, :], 1, 1)

        def gelu_back(rows, carry):
            low = (work[rows, :] * slope[rows, cols]).astype(bf16)
            grad_up[rows, cols] = low
            return carry + fold(low.astype(f32))

        put_vec(BIAS_UP + cols.start, column_sum(by_rows(tok, gelu_back, zero)))
    grad_up_came = to_partner(grad_up.at[own_rows], grad_up.at[far_rows])
    pump()
    normed_came.wait_recv()
    grad_up_came.wait_recv()
    feed_forward(1, narrow_normed, grad_up)
    pump()

    work[...] = dot(grad_up[own_rows, :], up_w[...], 1, 1)

    def norm_one_back(rows, carry):
        grad = grad_two[rows, :] + work[rows, :]
        zhat = zhat_one[rows, :]
        inner = grad * span(GAIN_ONE)
        grad_in = inner - row_mean(inner) - zhat * row_mean(inner * zhat)
        grad_in = grad_in * rstd_one[rows, 0:1]
        grad_one[rows, :] = grad_in
        low = grad_in.astype(bf16)
        grad_attn[rows, :] = low
        gain, shift, bias = carry
        return gain + fold(grad * zhat), shift + fold(grad), bias + fold(low.astype(f32))

    gain, shift, bias = by_rows(tok, norm_one_back, (zero, zero, zero))
    put_vec(GAIN_ONE, column_sum(gain))
    put_vec(SHIFT_ONE, column_sum(shift))
    put_vec(BIAS_OUT, column_sum(bias))
    grad_heads[...] = dot(grad_attn[...], out_w[...], 1, 1).astype(bf16)
    heads_turned[...] = dot(out_w[...], grad_attn[...], 1, 1).astype(bf16)

    half_lanes = LANES // 2
    pair_came = []
    for pair in range(HEADS // 2):
        pump()
        cols = slice(pair * LANES, (pair + 1) * LANES)
        values = keys_values[:, D + cols.start : D + cols.stop]
        for side, mask in enumerate(masks):
            rows = slice(cols.start + side * half_lanes, cols.start + (side + 1) * half_lanes)
            chance = prob[2 * pair + side].astype(f32)
            grad_chance = dot(grad_heads[:, cols] * mask, values, 1, 1)
            mean = jnp.sum(chance * grad_chance, axis=-1, keepdims=True)
            grad_score = (chance * (grad_chance - mean)).astype(bf16)
            values_grad = dot(heads_turned[rows, :], prob[2 * pair + side], 1, 0).astype(bf16)
            keys_grad = (dot(query_turned[rows, :], grad_score, 1, 0) * scale).astype(bf16)
            query_grad = (dot(keys_turned[rows, :], grad_score, 1, 1) * scale).astype(bf16)
            blocks = (
                query_grad,
                keys_grad[:, :tok],
                values_grad[:, :tok],
                keys_grad[:, tok:],
                values_grad[:, tok:],
            )
            for index, value in enumerate(blocks):
                start = index * LANES + side * half_lanes
                exchanged[0, pair, start : start + half_lanes, :] = value
        pair_came.append(to_partner(exchanged.at[0, pair], exchanged.at[1, pair]))
    pump()
    attn_turned[:, own_lanes] = transposed(grad_attn[...])
    grad_attn_came = to_partner(attn_turned.at[:, own_lanes], attn_turned.at[:, far_lanes])

    for pair, copy in enumerate(pair_came):
        copy.wait_recv()
        for who, lanes in enumerate((own_lanes, far_lanes)):
            start = pair * LANES
            mine, theirs = exchanged.at[who, pair], exchanged.at[1 - who, pair]
            qkv_turned[start : start + LANES, lanes] = mine[:LANES]
            for index in (1, 2):
                rows = slice(index * LANES, (index + 1) * LANES)
                sent = slice((index + 2) * LANES, (index + 3) * LANES)
                value = mine[rows].astype(f32) + theirs[sent].astype(f32)
                start = index * D + pair * LANES
                qkv_turned[start : start + LANES, lanes] = value.astype(bf16)
    pump()
    tokens_came.wait_recv()
    projections(2, qkv_turned, narrow_tokens, 3 * D // 8, 0, pump)
    attended_came.wait_recv()
    grad_attn_came.wait_recv()
    projections(2, attn_turned, narrow_attended, D // 8, 3 * D // 8)
    pump()

    ones = jnp.ones((8, tok), bf16)
    for start, rows in ((BIAS_QUERY, slice(0, D)), (BIAS_VALUE, slice(2 * D, 3 * D))):
        put_vec(start, dot(ones, qkv_turned[rows, own_lanes], 1, 1)[0:1])
    vec_came = to_partner(vec, vec_core)
    value = dot(qkv_w[...], qkv_turned[:, own_lanes], 1, 0)
    input_grad[...] = grad_one[...] + value.T

    vec_slots = [(send_sem.at[3 * PARTS, i], recv_sem.at[3 * PARTS, i]) for i in range(5)]

    def vec_steps():
        vec_came.wait_recv()
        vec_core[...] = vec[...] + vec_core[...]
        copy = remote(vec_core, vec_y, *vec_slots[0], beyond)
        yield
        copy.wait_recv()
        for i in range(4):
            vec_x[0, i] = vec_core[2 * i + x] + vec_y[2 * i + x]
            vec_x[1, i] = vec_core[2 * i + 1 - x] + vec_y[2 * i + 1 - x]
        copy = remote(vec_x.at[1], vec_x.at[2], *vec_slots[1], beside)
        yield
        copy.wait_recv()
        vec_x[0] = vec_x[0] + vec_x[2]
        copies = [
            remote(
                vec_x.at[0, flip_z(z, step)],
                vec_z.at[step - 1],
                *vec_slots[1 + step],
                along[step - 1],
            )
            for step in (1, 2, 3)
        ]
        yield
        total = vec_x[0, z]
        for step, copy in enumerate(copies):
            copy.wait_recv()
            total = total + vec_z[step]
        vec_sum[...] = total
        yield

    steps = vec_steps()
    for turn, index in enumerate(next(plan)):
        chains[index].advance()
        if turn % 10 == 9 and turn < 40:
            next(steps)
    for copy in started:
        copy.wait_send()


def layer(row_class, lengths, tokens, cotangent, vectors, qkv_w, out_w, up_w, down_w):
    tok = tokens.shape[0]
    chunk = (CHUNK, UNIT)

    def low(*dims):
        return pltpu.VMEM(dims, bf16)

    def wide(*dims):
        return pltpu.VMEM(dims, f32)

    return pl.pallas_call(
        layer_kernel,
        out_shape=(
            jax.ShapeDtypeStruct((tok, D), f32),
            jax.ShapeDtypeStruct((tok, D), f32),
            jax.ShapeDtypeStruct((3, 2, 2, PARTS) + chunk, bf16),
            jax.ShapeDtypeStruct((16, LANES), f32),
        ),
        in_specs=[SMEM, SMEM, VMEM, VMEM, VMEM] + [ANY] * 4,
        out_specs=(VMEM,) * 4,
        scratch_shapes=[
            low(D, 3 * D),
            low(D, D),
            low(D, FF),
            low(FF, D),
            low(tok, D),
            low(D, tok),
            low(2 * tok, 2 * D),
            low(D, 2 * tok),
            low(HEADS, tok, 2 * tok),
            low(tok, D),
            low(tok, D),
            low(tok, D),
            low(tok, D),
            low(2 * tok, HALF),
            low(2 * tok, HALF),
            low(2 * tok, HALF),
            low(2 * tok, HALF),
            low(2 * tok, FF),
            low(2 * tok, FF),
            low(D, 2 * tok),
            low(3 * D, 2 * tok),
            low(2, HEADS // 2, 5 * LANES, tok),
            low(tok, D),
            low(D, tok),
            wide(tok, FF),
            wide(tok, D),
            wide(tok, D),
            wide(tok, LANES),
            wide(tok, D),
            wide(tok, D),
            wide(8, 16, LANES),
            wide(8, 16, LANES),
            wide(8, 16, LANES),
            wide(3, 4, 16, LANES),
            wide(3, 16, LANES),
            low(3, PARTS, 2, 2, 2, 2, *chunk),
            low(3, PARTS, 2, 2, 2, *chunk),
            low(3, PARTS, 2, 2, *chunk),
            low(3, PARTS, 2, *chunk),
            low(3, PARTS, *chunk),
            pltpu.SemaphoreType.DMA((4,)),
            pltpu.SemaphoreType.DMA((15,)),
            pltpu.SemaphoreType.DMA((15,)),
            pltpu.SemaphoreType.DMA((3 * PARTS + 1, 6)),
            pltpu.SemaphoreType.DMA((3 * PARTS + 1, 6)),
        ],
        compiler_params=pltpu.CompilerParams(
            vmem_limit_bytes=63 * MIB, collective_id=0, has_side_effects=True
        ),
        name="layer",
    )(row_class, lengths, tokens, cotangent, vectors[None, :], qkv_w, out_w, up_w, down_w)


GROUP = 3
GRAM_AXES = ("far", "near", "x")
GRAM_ORDERS = tuple(
    tuple(GRAM_AXES["fnx".index(letter)] for letter in order)
    for order in ("xnf", "nxf", "xnf", "nxf", "xnf", "xnf", "fxn")
)
GRAM_PLAN = (0, 1, 2, 3, 6, 4, 0, 5, 1, 2, 0, 4, 3, 1, 6, 2, 5, 0, 3, 6, 1, 2, 4, 0, 5)
GRAM_PLAN += (3, 6, 1, 2, 4, 1, 5, 3, 6, 0, 4, 2, 5, 3, 6, 4, 1, 5, 0, 2, 3, 6, 4, 5)


def muon_kernel(
    sums,
    qkv_hbm,
    out_hbm,
    up_hbm,
    down_hbm,
    factors,
    own_sum,
    qkv_old,
    out_old,
    old,
    moment,
    out,
    part,
    came_one,
    came_two,
    came_three,
    high,
    low,
    load_sem,
    send_sem,
    recv_sem,
    share_send,
    share_recv,
    *ortho,
):
    z, x, y, core = position()
    here = {"far": z // 2, "near": z % 2, "x": x}
    others = {
        "far": device(flip_z(z, 2), x, y, core),
        "near": device(flip_z(z, 1), x, y, core),
        "x": device(z, 1 - x, y, core),
    }
    beyond = device(z, x, 1 - y, core)
    partner = device(z, x, y, 1 - core)
    own = 2 * y + core

    def load_two(source, target, matrix):
        loads = [
            pltpu.make_async_copy(source, target, load_sem.at[0]),
            pltpu.make_async_copy(sums.at[matrix], own_sum, load_sem.at[1]),
        ]
        for load in loads:
            load.start()
        for load in loads:
            load.wait()

    def from_turned(source, target, skip):
        load_two(source, target, 2)
        rows = target.shape[0]
        moment[...] = jnp.zeros_like(moment)
        for half in range(2):
            cols = slice(half * HALF, (half + 1) * HALF)
            start = half * UNIT + skip
            value = own_sum[start : start + rows, :].astype(f32)
            moment[cols, skip : skip + rows] = (muon_keep * target[:, cols] + value).T

    @pl.when(own == 0)
    def _():
        from_turned(qkv_hbm, qkv_old, 0)

    @pl.when(own == 1)
    def _():
        from_turned(out_hbm, out_old, qkv_old.shape[0])

    @pl.when(own == 2)
    def _():
        load_two(up_hbm, old, 1)
        moment[...] = muon_keep * old[...] + own_sum[...].astype(f32)

    @pl.when(own == 3)
    def _():
        load_two(down_hbm, old, 0)
        moment[...] = muon_keep * old[...] + own_sum[...].astype(f32)

    greet(list(others.values()) + [beyond, partner])
    blocks = sub_blocks(moment.shape[0])
    groups = len(blocks) // GROUP
    high[...] = moment[...].astype(bf16)
    low[...] = (moment[...] - high[...].astype(f32)).astype(bf16)
    started = []

    def product(index):
        i, j = blocks[index]
        left, right = pl.ds(i * SUB, SUB), pl.ds(j * SUB, SUB)
        total = dot(high[left, :], high[right, :], 1, 1)
        total = total + dot(high[left, :], low[right, :], 1, 1)
        total = total + dot(low[left, :], high[right, :], 1, 1)
        rows = SUB // 8
        for owner in range(8):
            cell = (owner // 4, owner // 2 % 2, owner % 2)
            part[(index // GROUP,) + cell + (index % GROUP,)] = total[
                owner * rows : (owner + 1) * rows
            ]

    def send(source, target, group, slot, axis):
        copy = pltpu.make_async_remote_copy(
            src_ref=source,
            dst_ref=target,
            send_sem=send_sem.at[group, slot],
            recv_sem=recv_sem.at[group, slot],
            device_id=others[axis],
            device_id_type=MESH,
        )
        copy.start()
        started.append(copy)
        return copy

    def cells(fixed, flipped=None):
        return tuple(
            1 - here[name] if name == flipped else here[name] if name in fixed else slice(None)
            for name in GRAM_AXES
        )

    class Walk:
        def __init__(self, group, order):
            self.group, self.order, self.stage = group, order, 0
            self.part = part.at[group]
            self.came = (came_one.at[group], came_two.at[group], came_three.at[group])

        def advance(self):
            stage, order = self.stage, self.order
            mine = pl.ds(self.group * GROUP, GROUP)
            if stage:
                self.copy.wait_recv()
            if 1 <= stage <= 3:
                kept = cells(order[:stage])
                total = self.part[kept] + self.came[stage - 1][...]
                if stage == 3:
                    out[kept + (mine,)] = total
                else:
                    self.part[kept] = total
            if stage < 3:
                source = self.part.at[cells(order[:stage], order[stage])]
                self.copy = send(source, self.came[stage], self.group, stage, order[stage])
            elif stage < 6:
                block = out.at[cells(order[: 6 - stage]) + (mine,)]
                self.copy = send(block, block, self.group, stage, order[5 - stage])
            self.stage += 1

    walks = [Walk(group, GRAM_ORDERS[group]) for group in range(groups)]
    for group in GRAM_PLAN:
        if walks[group].stage == 0:
            for index in range(group * GROUP, (group + 1) * GROUP):
                product(index)
        walks[group].advance()

    e = ortho[0]
    for index, (i, j) in enumerate(blocks):
        value = out[:, :, :, index].reshape(SUB, SUB)
        e[i * SUB : (i + 1) * SUB, j * SUB : (j + 1) * SUB] = value
        if i != j:
            e[j * SUB : (j + 1) * SUB, i * SUB : (i + 1) * SUB] = value.T

    across, beside = [], []

    def share(slot, rows, kind, other):
        block = factors.at[slot, rows]
        index = rows.start // TILE
        copy = pltpu.make_async_remote_copy(
            src_ref=block,
            dst_ref=block,
            send_sem=share_send.at[index, kind],
            recv_sem=share_recv.at[index, kind],
            device_id=other,
            device_id_type=MESH,
        )
        copy.start()
        started.append(copy)
        return copy

    def emit(rows, value):
        factors[own, rows, :] = value
        across.append((rows, share(own, rows, 0, beyond)))
        beside.append(share(own, rows, 1, partner))

    newton_schulz(e, moment, *ortho, emit)
    for rows, copy in across:
        copy.wait_recv()
        beside.append(share(2 * (1 - y) + core, rows, 2, partner))
    for copy in beside:
        copy.wait_recv()
    for copy in started:
        copy.wait_send()


def muon_factors(sums, *olds):
    size, cols = olds[2].shape
    count = len(sub_blocks(size))
    groups = count // GROUP
    rows = (SUB // 8, SUB)

    def wide(*dims):
        return pltpu.VMEM(dims, f32)

    return pl.pallas_call(
        muon_kernel,
        out_shape=jax.ShapeDtypeStruct((4, size, cols), bf16),
        in_specs=[ANY] * 5,
        out_specs=VMEM,
        scratch_shapes=[
            pltpu.VMEM((size, cols), bf16),
            wide(*olds[0].shape),
            wide(*olds[1].shape),
            wide(size, cols),
            wide(size, cols),
            wide(2, 2, 2, count, *rows),
            wide(groups, 2, 2, 2, GROUP, *rows),
            wide(groups, 2, 2, GROUP, *rows),
            wide(groups, 2, GROUP, *rows),
            wide(groups, GROUP, *rows),
            pltpu.VMEM((size, cols), bf16),
            pltpu.VMEM((size, cols), bf16),
            pltpu.SemaphoreType.DMA((2,)),
            pltpu.SemaphoreType.DMA((groups, 6)),
            pltpu.SemaphoreType.DMA((groups, 6)),
            pltpu.SemaphoreType.DMA((size // TILE, 3)),
            pltpu.SemaphoreType.DMA((size // TILE, 3)),
        ]
        + ortho_scratch(size, cols),
        compiler_params=pltpu.CompilerParams(
            vmem_limit_bytes=58 * MIB, collective_id=1, has_side_effects=True
        ),
        name="muon_factors",
    )(sums, *olds)


def window(start, width, total):
    size = -(-(width + 96) // LANES) * LANES
    first = jnp.minimum(start // LANES * LANES, total - size)
    return pl.ds(pl.multiple_of(first, LANES), size), start - first


def finish_kernel(
    factors,
    sums_hbm,
    qkv_hbm,
    out_hbm,
    up_hbm,
    down_hbm,
    qkv_old_hbm,
    out_old_hbm,
    up_old_hbm,
    down_old_hbm,
    mixed_hbm,
    grad_hbm,
    mixed_out,
    grad_out,
    qkv_moment_out,
    out_moment_out,
    up_moment_out,
    down_moment_out,
    qkv_out,
    out_out,
    up_out,
    down_out,
    sums,
    qkv_w,
    out_w,
    up_w,
    down_w,
    qkv_moment,
    out_moment,
    up_moment,
    down_moment,
    qkv_new,
    out_new,
    up_new,
    down_new,
    turned,
    load_sem,
    store_sem,
):
    shrink = 1.0 - muon_rate * muon_decay
    dp_id = lax.axis_index("dp")
    qkv_cols, out_cols = qkv_new.shape[0], out_new.shape[0]
    qkv_lanes, qkv_skip = window(dp_id * qkv_cols, qkv_cols, 3 * D)
    out_lanes, out_skip = window(dp_id * out_cols, out_cols, D)
    block = pl.ds(pl.multiple_of(dp_id * UNIT, UNIT), UNIT)
    pairs = {
        "sums": (sums_hbm, sums),
        "up_moment": (up_old_hbm, up_moment),
        "down_moment": (down_old_hbm, down_moment),
        "up": (up_hbm.at[:, block], up_w),
        "down": (down_hbm.at[block], down_w),
        "qkv_moment": (qkv_old_hbm, qkv_moment),
        "out_moment": (out_old_hbm, out_moment),
        "qkv": (qkv_hbm.at[:, qkv_lanes], qkv_w),
        "out": (out_hbm.at[:, out_lanes], out_w),
    }
    loads = {
        name: pltpu.make_async_copy(source, target, load_sem.at[index])
        for index, (name, (source, target)) in enumerate(pairs.items())
    }
    for load in loads.values():
        load.start()
    stores = []

    def store(source, target):
        stores.append(pltpu.make_async_copy(source, target, store_sem.at[len(stores)]))
        stores[-1].start()

    store(mixed_hbm, mixed_out)
    store(grad_hbm, grad_out)

    def step(index, rate):
        return muon_rate * rate * factors[index].astype(f32)

    loads["sums"].wait()
    for index, name, target, out in (
        (1, "up_moment", up_moment, up_moment_out),
        (0, "down_moment", down_moment, down_moment_out),
    ):
        loads[name].wait()
        target[...] = muon_keep * target[...] + sums[index].astype(f32)
        store(target, out)
    loads["up"].wait()
    up_new[...] = up_w[...].astype(f32) * shrink - step(2, math.sqrt(max(1.0, FF / D)))
    store(up_new, up_out)
    loads["down"].wait()
    down_new[...] = down_w[...].astype(f32) * shrink - step(3, 1.0).T
    store(down_new, down_out)
    loads["qkv_moment"].wait()
    loads["out_moment"].wait()
    for half in range(2):
        cols = slice(half * HALF, (half + 1) * HALF)
        value = sums[2, cols].astype(f32)
        qkv_moment[:, cols] = muon_keep * qkv_moment[:, cols] + value[:qkv_cols]
        out_moment[:, cols] = muon_keep * out_moment[:, cols] + value[qkv_cols:]
    store(qkv_moment, qkv_moment_out)
    store(out_moment, out_moment_out)
    loads["qkv"].wait()
    turned[...] = qkv_w[...].astype(f32).T
    rows = pl.ds(pl.multiple_of(qkv_skip, 32), qkv_cols)
    qkv_new[...] = turned[rows, :] * shrink - step(0, math.sqrt(3.0)).T[:qkv_cols]
    store(qkv_new, qkv_out)
    loads["out"].wait()
    turned[: out_w.shape[1], :] = out_w[...].astype(f32).T
    rows = pl.ds(pl.multiple_of(out_skip, 32), out_cols)
    out_new[...] = turned[rows, :] * shrink - step(1, 1.0).T[qkv_cols:]
    store(out_new, out_out)
    for copy in stores:
        copy.wait()


def finish(factors, sums, weights, olds, mixed, input_grad):
    shapes = [old.shape for old in olds]
    news = shapes[:3] + [shapes[3][::-1]]

    def wide(shape):
        return pltpu.VMEM(shape, f32)

    return pl.pallas_call(
        finish_kernel,
        out_shape=tuple(
            jax.ShapeDtypeStruct(shape, f32)
            for shape in [mixed.shape, input_grad.shape] + shapes + news
        ),
        in_specs=[VMEM] + [ANY] * 11,
        out_specs=(ANY,) * 10,
        scratch_shapes=[
            pltpu.VMEM(sums.shape, bf16),
            pltpu.VMEM((D, 384), bf16),
            pltpu.VMEM((D, 256), bf16),
            pltpu.VMEM((D, UNIT), bf16),
            pltpu.VMEM((UNIT, D), bf16),
        ]
        + [wide(shape) for shape in shapes + news]
        + [
            wide((384, D)),
            pltpu.SemaphoreType.DMA((9,)),
            pltpu.SemaphoreType.DMA((10,)),
        ],
        compiler_params=pltpu.CompilerParams(vmem_limit_bytes=48 * MIB),
        name="finish",
    )(factors, sums, *weights, *olds, mixed, input_grad)


def swap(value, axis, bit):
    size = lax.axis_size(axis)
    return lax.ppermute(value, axis, [(i, i ^ bit) for i in range(size)])


def scatter_head(value, bit, position):
    half = value.shape[1] // 2
    mine = lax.dynamic_slice_in_dim(value, position * half, half, 1)
    other = lax.dynamic_slice_in_dim(value, (1 - position) * half, half, 1)
    return (mine.astype(f32) + swap(other, "head", bit).astype(f32)).astype(bf16)


def scatter_dp_pair(value, position):
    paired = value.reshape((value.shape[0] // 2, 2) + value.shape[1:])
    mine = lax.dynamic_index_in_dim(paired, position, 1, False)
    other = lax.dynamic_index_in_dim(paired, 1 - position, 1, False)
    return (mine.astype(f32) + swap(other, "dp", 1).astype(f32)).astype(bf16)


def scatter_dp_rest(value, place):
    ranks = value.shape[0]
    total = lax.dynamic_index_in_dim(value, place, 0, False).astype(f32)
    for step in range(1, ranks):
        sent = lax.dynamic_index_in_dim(value, place ^ step, 0, False)
        total = total + swap(sent, "dp", 2 * step).astype(f32)
    return total


def local(
    tokens,
    cotangent,
    qkv_weight,
    out_weight,
    up_weight,
    down_weight,
    vectors,
    qkv_moment,
    out_moment,
    up_moment,
    down_moment,
    adam_first,
    adam_second,
    bucket_class,
    row_lengths,
):
    n_dp = lax.axis_size("dp")
    n_head = lax.axis_size("head")
    dp_id = lax.axis_index("dp")
    head_id = lax.axis_index("head")
    core, side = head_id % 2, head_id // 2
    tok, width = tokens.shape
    hidden = up_weight.shape[1]
    half = width // 2
    qkv_cols, out_cols = qkv_moment.shape[1], out_moment.shape[1]
    shrink = 1.0 - muon_rate * muon_decay

    def weight_block(weight, cols, dim):
        return lax.dynamic_slice_in_dim(weight, dp_id * cols, cols, dim)

    block = head_id.astype(jnp.int32)[None]
    vec_len = vectors.shape[0] // n_dp
    if (n_dp, n_head, tok) == (8, 4, 256):
        mixed, input_grad, sums, vec = layer(
            bucket_class,
            row_lengths,
            tokens,
            cotangent,
            vectors,
            qkv_weight,
            out_weight,
            up_weight,
            down_weight,
        )
        grad_vec = vec[:VEC_BLOCK].reshape(vec_len)
        sums = sums.reshape(3, width, -1)
        olds = [qkv_moment.T, out_moment.T, up_moment, down_moment]
        mixed, input_grad, *results = finish(
            muon_factors(sums, *olds),
            sums,
            [qkv_weight, out_weight, up_weight, down_weight],
            olds,
            mixed,
            input_grad,
        )
        moments, new_weights = results[:4], results[4:]
        moments = [moments[0].T, moments[1].T, *moments[2:]]
        new_weights = [new_weights[0].T, new_weights[1].T, *new_weights[2:]]
    else:
        pieces = split_vectors(vectors, width, hidden)
        bias_query, bias_value, bias_out, gain_one, shift_one = pieces[:5]
        bias_up, bias_down, gain_two, shift_two = pieces[5:]
        bias_qkv = jnp.concatenate([bias_query, jnp.zeros_like(bias_query), bias_value])

        def column_half(value, which):
            return lax.dynamic_slice_in_dim(value, which * half, half, 1)

        qkv = (dot(tokens, qkv_weight, 1, 0) + bias_qkv).astype(bf16)
        other = swap(qkv[:, width:], "head", 1)
        attended = attend(block, bucket_class, row_lengths, qkv, other)
        attn_val = dot(attended, out_weight, 1, 0) + bias_out
        resid_one = tokens.astype(f32) + attn_val
        centre = resid_one - jnp.mean(resid_one, axis=-1, keepdims=True)
        rstd_one = lax.rsqrt(jnp.mean(centre * centre, axis=-1, keepdims=True) + norm_eps)
        zhat_one = centre * rstd_one
        normed_one = zhat_one * gain_one + shift_one
        normed_low = normed_one.astype(bf16)
        up_val = dot(normed_low, up_weight, 1, 0) + bias_up
        phi_cum = 0.5 * (1.0 + lax.erf(up_val * (0.5**0.5)))
        active_low = (up_val * phi_cum).astype(bf16)
        slope = phi_cum + up_val * jnp.exp(-0.5 * up_val * up_val) * (1.0 / math.sqrt(2.0 * math.pi))
        down_val = dot(active_low, down_weight, 1, 0) + bias_down
        resid_two = normed_one + down_val
        centre = resid_two - jnp.mean(resid_two, axis=-1, keepdims=True)
        rstd_two = lax.rsqrt(jnp.mean(centre * centre, axis=-1, keepdims=True) + norm_eps)
        zhat_two = centre * rstd_two
        mixed = zhat_two * gain_two + shift_two

        def norm_back(grad, gain, zhat, rstd):
            inner = grad * gain
            mean = jnp.mean(inner, axis=-1, keepdims=True)
            slant = jnp.mean(inner * zhat, axis=-1, keepdims=True)
            return (inner - mean - zhat * slant) * rstd, jnp.sum(grad * zhat, axis=0), jnp.sum(grad, axis=0)

        grad_two, grad_gain_two, grad_shift_two = norm_back(
            cotangent.astype(f32), gain_two, zhat_two, rstd_two
        )
        grad_down_low = grad_two.astype(bf16)
        grad_bias_down = jnp.sum(grad_down_low, axis=0, dtype=f32)

        x_id, z_id = dp_id % 2, dp_id // 2

        grad_up_low = (dot(grad_down_low, down_weight, 1, 1) * slope).astype(bf16)
        grad_bias_up = jnp.sum(grad_up_low, axis=0, dtype=f32)
        grad_normed = grad_two + dot(grad_up_low, up_weight, 1, 1)
        grad_one, grad_gain_one, grad_shift_one = norm_back(grad_normed, gain_one, zhat_one, rstd_one)
        grad_attn_low = grad_one.astype(bf16)
        grad_bias_out = jnp.sum(grad_attn_low, axis=0, dtype=f32)
        grad_heads = dot(grad_attn_low, out_weight, 1, 1).astype(bf16)
        grad_query, own, sent = attend_back(block, bucket_class, row_lengths, qkv, other, grad_heads)
        grad_kv = (own + swap(sent, "head", 1).astype(f32)).astype(bf16)
        grad_qkv = jnp.concatenate([grad_query, grad_kv], axis=1)
        grad_bias_qkv = jnp.sum(grad_qkv, axis=0, dtype=f32)
        input_grad = grad_one + dot(grad_qkv, qkv_weight, 1, 1)
        grad_vector = jnp.concatenate(
            [
                grad_bias_qkv[:width],
                grad_bias_qkv[2 * width :],
                grad_bias_out,
                grad_gain_one,
                grad_shift_one,
                grad_bias_up,
                grad_bias_down,
                grad_gain_two,
                grad_shift_two,
            ]
        )
        grad_vector = grad_vector + swap(grad_vector, "head", 1)
        wides = [active_low, grad_up_low, grad_attn_low, grad_qkv]
        narrows = [grad_down_low, normed_low, attended, tokens]

        def both_halves(value):
            return jnp.concatenate(
                [column_half(value, core), swap(column_half(value, 1 - core), "head", 1)], axis=0
            )

        def weight_grad(wide, narrow):
            wide = jnp.concatenate([wide, swap(wide, "head", 1)], axis=0)
            value = dot(wide, both_halves(narrow), 0, 0).astype(bf16)
            return value.reshape(n_dp, value.shape[0] // n_dp, half)

        def reduce_y_first(value):
            return scatter_dp_rest(scatter_dp_pair(scatter_head(value, 2, side), x_id), z_id)

        def reduce_x_first(value):
            return scatter_dp_rest(scatter_head(scatter_dp_pair(value, x_id), 2, side), z_id)

        def spread(value):
            value = value.astype(bf16)
            came = swap(value, "head", 2)
            value = jnp.concatenate(
                [jnp.where(side == 0, value, came), jnp.where(side == 0, came, value)], axis=0
            )
            came = swap(value, "head", 1)
            return jnp.concatenate(
                [jnp.where(core == 0, value, came), jnp.where(core == 0, came, value)], axis=1
            ).astype(f32)

        down_part, up_part, out_part, qkv_part = [
            weight_grad(wide, narrow) for wide, narrow in zip(wides, narrows)
        ]
        vec_rows = 16
        vec_part = grad_vector.reshape(n_dp, vec_len)
        vec_part = jnp.pad(vec_part, ((0, 0), (0, vec_rows * width - vec_len)))
        vec_part = vec_part.reshape(n_dp, vec_rows, width)
        vec_part = lax.dynamic_slice_in_dim(vec_part, core * half, half, 2).astype(bf16)
        down_new = spread(reduce_x_first(down_part))
        up_new = spread(reduce_y_first(up_part))
        tail_new = spread(
            reduce_y_first(jnp.concatenate([qkv_part, out_part, vec_part], axis=1))
        )
        grads = [
            tail_new[:qkv_cols].T,
            tail_new[qkv_cols : qkv_cols + out_cols].T,
            up_new.T,
            down_new.T,
        ]
        grad_vec = tail_new[qkv_cols + out_cols :].reshape(-1)[:vec_len]
        moments = [
            muon_keep * old + grad
            for old, grad in zip([qkv_moment, out_moment, up_moment, down_moment], grads)
        ]
        most = max(m.shape[1] for m in moments)
        padded = [jnp.pad(m, ((0, 0), (0, most - m.shape[1]))) for m in moments]
        chosen = padded[-1]
        for index in range(len(padded) - 2, -1, -1):
            chosen = jnp.where(head_id == index, padded[index], chosen)
        gram_mat = lax.dot_general(
            chosen, chosen, (((1,), (1,)), ((), ())), precision=lax.Precision.HIGH
        )
        own_factor = orthogonalize(lax.psum(gram_mat, "dp"), chosen)
        across = swap(own_factor, "head", 2)
        low_pair = jnp.where(side == 0, own_factor, across)
        high_pair = jnp.where(side == 0, across, own_factor)
        near_low = swap(low_pair, "head", 1)
        near_high = swap(high_pair, "head", 1)
        factors = [
            jnp.where(core == 0, low_pair, near_low),
            jnp.where(core == 0, near_low, low_pair),
            jnp.where(core == 0, high_pair, near_high),
            jnp.where(core == 0, near_high, high_pair),
        ]
        factors = [o[:, : m.shape[1]].astype(f32) for o, m in zip(factors, moments)]
        factors[3] = factors[3].T
        old_weights = [
            weight_block(qkv_weight, qkv_cols, 1),
            weight_block(out_weight, out_cols, 1),
            weight_block(up_weight, up_moment.shape[1], 1),
            weight_block(down_weight, down_moment.shape[1], 0),
        ]

        rates = (math.sqrt(3.0), 1.0, math.sqrt(max(1.0, hidden / width)), 1.0)
        new_weights = [
            old.astype(f32) * shrink - muon_rate * rate * factor
            for old, rate, factor in zip(old_weights, rates, factors)
        ]

    vec_old = lax.dynamic_slice_in_dim(vectors, dp_id * vec_len, vec_len, 0)
    vec_first = beta_first * adam_first + (1.0 - beta_first) * grad_vec
    vec_second = beta_second * adam_second + (1.0 - beta_second) * grad_vec * grad_vec
    first_hat = vec_first / (1.0 - beta_first**STEP)
    second_hat = vec_second / (1.0 - beta_second**STEP)
    vec_new = vec_old - adam_rate * first_hat / (jnp.sqrt(second_hat) + adam_eps)
    return (mixed, input_grad, *moments, *new_weights, vec_first, vec_second, vec_new)


def solution(mesh):
    tokens_spec = P(("dp", "head"), None)
    block_spec = P(None, "dp")
    return jax.shard_map(
        local,
        mesh=mesh,
        in_specs=(
            tokens_spec,
            tokens_spec,
            P(),
            P(),
            P(),
            P(),
            P(),
            block_spec,
            block_spec,
            block_spec,
            block_spec,
            P("dp"),
            P("dp"),
            P("dp"),
            P("dp", None),
        ),
        out_specs=(
            tokens_spec,
            tokens_spec,
            block_spec,
            block_spec,
            block_spec,
            block_spec,
            block_spec,
            block_spec,
            block_spec,
            P("dp", None),
            P("dp"),
            P("dp"),
            P("dp"),
        ),
        check_vma=False,
    )
```

```python
import functools
import itertools
import math

import jax
import jax.numpy as jnp
from jax import lax
from jax.experimental import pallas as pl
from jax.experimental.pallas import tpu as pltpu
from jax.sharding import PartitionSpec as P

D = 768
HEADS = 12
HEAD_DIM = 64
FF = 3072
BASE_LEN = 128
NS_STEPS = 5
STEP = 5
MAX_LEN = 512

f32 = jnp.float32
bf16 = jnp.bfloat16

norm_eps = 1e-12
masked_score = -1000000000.0
quintic_a = 3.4445
quintic_b = -4.775
quintic_c = 2.0315
muon_rate = 1.0
muon_decay = 0.01
muon_keep = 0.5
adam_rate = 0.2
beta_first = 0.9
beta_second = 0.999
adam_eps = 1e-08
MIB = 1024 * 1024


def dot(left, right, left_dim, right_dim):
    return lax.dot_general(
        left, right, (((left_dim,), (right_dim,)), ((), ())), preferred_element_type=f32
    )


def split_vectors(vectors, width, hidden):
    lengths_list = [width] * 5 + [hidden] + [width] * 3
    pieces = []
    offset = 0
    for length in lengths_list:
        pieces.append(vectors[offset : offset + length])
        offset = offset + length
    return pieces


def allowed_mask(class_ref, length_ref, block, tok):
    shift = class_ref[0] + int(math.log2(BASE_LEN))
    query_place = block * tok + lax.broadcasted_iota(jnp.int32, (tok, 1), 0)
    lane = lax.broadcasted_iota(jnp.int32, (1, 2 * tok), 1)
    own = lane < tok
    key_place = jnp.where(own, block * tok + lane, (block ^ 1) * tok + lane - tok)
    key_row = lax.shift_right_logical(key_place, jnp.broadcast_to(shift, key_place.shape))
    offset = key_place - lax.shift_left(key_row, jnp.broadcast_to(shift, key_place.shape))
    row_len = jnp.zeros_like(key_row)
    for slot in range(length_ref.shape[1]):
        row_len = jnp.where(key_row == slot, length_ref[0, slot], row_len)
    key_row = jnp.where(offset < row_len, key_row, -1)
    query_row = lax.shift_right_logical(query_place, jnp.broadcast_to(shift, query_place.shape))
    return query_row == key_row


def half_masks():
    lane = lax.broadcasted_iota(jnp.int32, (1, 2 * HEAD_DIM), 1)
    first = (lane < HEAD_DIM).astype(f32)
    return (first.astype(bf16), (1.0 - first).astype(bf16)), lane < HEAD_DIM


def head_prob(query, keys, allowed):
    score = jnp.where(allowed, dot(query, keys, 1, 1) * HEAD_DIM ** (-0.5), masked_score)
    exponent = jnp.exp(score - jnp.max(score, axis=-1, keepdims=True))
    return exponent / jnp.sum(exponent, axis=-1, keepdims=True)


def attend_kernel(block_ref, class_ref, length_ref, qkv_ref, other_ref, out_ref):
    tok = qkv_ref.shape[0]
    allowed = allowed_mask(class_ref, length_ref, block_ref[0], tok)
    masks, first = half_masks()
    for pair in range(HEADS // 2):
        cols = pl.ds(pair * 2 * HEAD_DIM, 2 * HEAD_DIM)
        kcols = pl.ds(D + pair * 2 * HEAD_DIM, 2 * HEAD_DIM)
        vcols = pl.ds(2 * D + pair * 2 * HEAD_DIM, 2 * HEAD_DIM)
        query = qkv_ref[:, cols]
        keys = jnp.concatenate([qkv_ref[:, kcols], other_ref[:, cols]], axis=0)
        values = jnp.concatenate([qkv_ref[:, vcols], other_ref[:, kcols]], axis=0)
        outs = []
        for mask in masks:
            prob = head_prob(query * mask, keys, allowed)
            outs.append(dot(prob.astype(bf16), values, 1, 0))
        out_ref[:, cols] = jnp.where(first, outs[0], outs[1]).astype(bf16)


def attend_back_kernel(
    block_ref, class_ref, length_ref, qkv_ref, other_ref, grad_ref, dq_ref, own_ref, send_ref
):
    tok = qkv_ref.shape[0]
    allowed = allowed_mask(class_ref, length_ref, block_ref[0], tok)
    masks, first = half_masks()
    scale = HEAD_DIM ** (-0.5)
    for pair in range(HEADS // 2):
        cols = pl.ds(pair * 2 * HEAD_DIM, 2 * HEAD_DIM)
        kcols = pl.ds(D + pair * 2 * HEAD_DIM, 2 * HEAD_DIM)
        vcols = pl.ds(2 * D + pair * 2 * HEAD_DIM, 2 * HEAD_DIM)
        query = qkv_ref[:, cols]
        keys = jnp.concatenate([qkv_ref[:, kcols], other_ref[:, cols]], axis=0)
        values = jnp.concatenate([qkv_ref[:, vcols], other_ref[:, kcols]], axis=0)
        grad = grad_ref[:, cols]
        dqs, dk, dv = [], None, None
        for mask in masks:
            head_query = query * mask
            head_grad = grad * mask
            prob = head_prob(head_query, keys, allowed)
            part_v = dot(prob.astype(bf16), head_grad, 0, 0)
            dprob = dot(head_grad, values, 1, 1)
            dscore = prob * (dprob - jnp.sum(prob * dprob, axis=-1, keepdims=True))
            dscore = dscore.astype(bf16)
            dqs.append(dot(dscore, keys, 1, 0))
            part_k = dot(dscore, head_query, 0, 0)
            dk = part_k if dk is None else dk + part_k
            dv = part_v if dv is None else dv + part_v
        dk = dk * scale
        dq_ref[:, cols] = (jnp.where(first, dqs[0], dqs[1]) * scale).astype(bf16)
        own_ref[:, cols] = dk[:tok]
        own_ref[:, kcols] = dv[:tok]
        send_ref[:, cols] = dk[tok:].astype(bf16)
        send_ref[:, kcols] = dv[tok:].astype(bf16)


SMEM = pl.BlockSpec(memory_space=pltpu.SMEM)
VMEM = pl.BlockSpec(memory_space=pltpu.VMEM)
ANY = pl.BlockSpec(memory_space=pl.ANY)


def attend(block, row_class, lengths, qkv, other):
    tok = qkv.shape[0]
    return pl.pallas_call(
        attend_kernel,
        out_shape=jax.ShapeDtypeStruct((tok, D), bf16),
        in_specs=[SMEM, SMEM, SMEM, VMEM, VMEM],
        out_specs=VMEM,
        compiler_params=pltpu.CompilerParams(vmem_limit_bytes=32 * MIB),
        name="attend",
    )(block, row_class, lengths, qkv, other)


def attend_back(block, row_class, lengths, qkv, other, grad):
    tok = qkv.shape[0]
    return pl.pallas_call(
        attend_back_kernel,
        out_shape=(
            jax.ShapeDtypeStruct((tok, D), bf16),
            jax.ShapeDtypeStruct((tok, 2 * D), f32),
            jax.ShapeDtypeStruct((tok, 2 * D), bf16),
        ),
        in_specs=[SMEM, SMEM, SMEM, VMEM, VMEM, VMEM],
        out_specs=(VMEM, VMEM, VMEM),
        compiler_params=pltpu.CompilerParams(vmem_limit_bytes=32 * MIB),
        name="attend_back",
    )(block, row_class, lengths, qkv, other, grad)


CENTRES = (0.0, 0.0, 0.0, 0.8, 0.8)
TILE = 256
SUB = 128


def sub_blocks(size):
    count = size // SUB
    return [(i, j) for i in range(count) for j in range(i, count)]


def newton_schulz(gram, moment, e, f, g, eb, fb, gb, ya, yb, y, emit):
    size = e.shape[0]
    tiles = [slice(i * TILE, (i + 1) * TILE) for i in range(size // TILE)]

    def unit(rows):
        row_id = rows.start + lax.broadcasted_iota(jnp.int32, (TILE, size), 0)
        col_id = lax.broadcasted_iota(jnp.int32, (TILE, size), 1)
        return (row_id == col_id).astype(f32)

    diagonal = jnp.zeros((TILE, size), f32)
    for rows in tiles:
        diagonal = diagonal + gram[rows, :] * unit(rows)
    trace = jnp.sum(jnp.sum(diagonal, axis=0, keepdims=True), axis=1, keepdims=True)
    factor = 1.0 / (jnp.sqrt(trace) + 1e-07)
    square_factor = factor * factor
    for rows in tiles:
        value = gram[rows, :] * square_factor
        e[rows, :] = value
        eb[rows, :] = value.astype(bf16)
        value = moment[rows, :] * factor
        y[rows, :] = value
        ya[rows, :] = value.astype(bf16)
    now, then = ya, yb
    for step in range(NS_STEPS):
        last = step + 1 == NS_STEPS
        centre = CENTRES[step]
        after = 0.0 if last else CENTRES[step + 1]
        keep = quintic_a + quintic_b * centre + quintic_c * centre * centre
        linear = quintic_b + 2.0 * quintic_c * centre
        for rows in tiles:
            value = linear * e[rows, :] + quintic_c * dot(eb[rows, :], eb[...], 1, 0)
            fb[rows, :] = value.astype(bf16)
            if not last:
                f[rows, :] = value
        for rows in tiles:
            value = keep * y[rows, :] + dot(fb[rows, :], now[...], 1, 0)
            if last:
                emit(rows, value.astype(bf16))
            else:
                y[rows, :] = value
                then[rows, :] = value.astype(bf16)
        if last:
            break
        now, then = then, now
        for rows in tiles:
            value = keep * e[rows, :] + dot(eb[rows, :], fb[...], 1, 0)
            if centre:
                value = value + centre * f[rows, :]
            g[rows, :] = value
            gb[rows, :] = value.astype(bf16)
        for rows in tiles:
            value = keep * g[rows, :] + dot(gb[rows, :], fb[...], 1, 0)
            if centre:
                value = value + (centre * keep) * f[rows, :]
            shift = centre * keep * keep - after
            if shift:
                value = value + shift * unit(rows)
            e[rows, :] = value
            eb[rows, :] = value.astype(bf16)


def ortho_kernel(gram, moment, out, *scratch):
    def emit(rows, value):
        out[rows, :] = value

    newton_schulz(gram, moment, *scratch, emit)


def ortho_scratch(size, cols):
    square, square_low = pltpu.VMEM((size, size), f32), pltpu.VMEM((size, size), bf16)
    wide_low = pltpu.VMEM((size, cols), bf16)
    return [square] * 3 + [square_low] * 3 + [wide_low] * 2 + [pltpu.VMEM((size, cols), f32)]


def orthogonalize(gram_mat, moment):
    size, cols = moment.shape
    return pl.pallas_call(
        ortho_kernel,
        out_shape=jax.ShapeDtypeStruct((size, cols), bf16),
        in_specs=[VMEM, VMEM],
        out_specs=VMEM,
        scratch_shapes=ortho_scratch(size, cols),
        compiler_params=pltpu.CompilerParams(vmem_limit_bytes=48 * MIB),
        name="ortho",
    )(gram_mat, moment)


MESH = pl.DeviceIdType.MESH
CHUNK = 48
PARTS = 4
UNIT = 2 * PARTS * CHUNK
HALF = D // 2
LANES = 128
VEC_BLOCK = 9
ROWS = 16
CHUNK_ORDERS = (
    "xyfn", "nxyf", "nxfy", "ynfx",
    "yxnf", "ynfx", "xnyf", "yxnf",
    "nyxf", "xfyn", "yxnf", "xnyf",
)
CHUNK_PLAN = (
    (0, 1, 2, 3),
    (),
    (),
    (),
    (),
    (0, 3, 4, 5, 6),
    (),
    (),
    (),
    (),
    (6, 1, 2),
    (3, 0),
    (),
    (),
    (6,),
    (1, 2, 4, 5, 7),
    (3, 0),
    (6, 8, 9, 1, 3, 10, 11),
    (
        0, 2, 4, 3, 6, 1, 3, 5, 0, 2, 4, 0, 6, 1, 6, 1, 2, 2, 4, 5, 9, 11, 7, 5,
        4, 4, 8, 5, 10, 7, 5, 8, 9, 10, 11, 7, 8, 9, 11, 7, 10, 8, 9, 7, 8, 7, 11, 9,
        8, 10, 9, 11, 10, 11, 10,
    ),
)
BIAS_QUERY, BIAS_VALUE, BIAS_OUT, GAIN_ONE, SHIFT_ONE, BIAS_UP = (i * D for i in range(6))
BIAS_DOWN, GAIN_TWO, SHIFT_TWO = (BIAS_UP + FF + i * D for i in range(3))


def position():
    dp_id, head_id = lax.axis_index("dp"), lax.axis_index("head")
    z, x = dp_id // 2, dp_id % 2
    y, core = head_id // 2, head_id % 2
    return z, x, y, core


def device(z, x, y, core):
    return (2 * z + x, 2 * y + core)


def flip_z(z, step):
    high, low = z // 2, z % 2
    high = 1 - high if step // 2 else high
    low = 1 - low if step % 2 else low
    return 2 * high + low


def greet(others):
    barrier = pltpu.get_barrier_semaphore()
    for other in others:
        pl.semaphore_signal(barrier, inc=1, device_id=other, device_id_type=MESH)
    return lambda: pl.semaphore_wait(barrier, len(others))


def by_rows(count, body, init=None, together=4):
    def step(index, carry):
        for part in range(together):
            start = (index * together + part) * ROWS
            carry = body(pl.ds(pl.multiple_of(start, ROWS), ROWS), carry)
        return carry

    return lax.fori_loop(0, count // (ROWS * together), step, init)


def row_mean(value):
    return jnp.sum(value, axis=-1, keepdims=True) * (1.0 / D)


def fold(value):
    return jnp.sum(value.reshape(value.shape[0] // 8, 8, value.shape[1]), axis=0)


def column_sum(value):
    return jnp.sum(value, axis=0, keepdims=True)


def normal_parts(value):
    size = jnp.abs(value)
    decay = jnp.exp(-0.5 * value * value)
    below = 1.0 + (0.3275911 * 0.5**0.5) * size
    t = pl.reciprocal(below, approx=True)
    t = t * (2.0 - below * t)
    series = t * (1.061405429 * 0.5)
    for term in (-1.453152027, 1.421413741, -0.284496736, 0.254829592):
        series = (series + term * 0.5) * t
    tail = series * decay
    return jnp.where(value < 0.0, tail, 1.0 - tail), decay * (1.0 / math.sqrt(2.0 * math.pi))


def transposed(value):
    side = 2 * LANES
    row_id = lax.broadcasted_iota(jnp.int32, (side, side), 0)
    unit = (row_id == lax.broadcasted_iota(jnp.int32, (side, side), 1)).astype(f32).astype(bf16)
    blocks = []
    for start in range(0, value.shape[1], side):
        block = value[:, start : start + side]
        size = block.shape[1]
        blocks.append(dot(unit[:size, :size], block, 1, 1).astype(bf16))
    return jnp.concatenate(blocks, axis=0)


def layer_kernel(
    row_class,
    lengths,
    tokens,
    cotangent,
    vectors,
    qkv_hbm,
    out_hbm,
    up_hbm,
    down_hbm,
    mixed,
    input_grad,
    sums,
    vec_sum,
    qkv_w,
    out_w,
    up_w,
    down_w,
    query,
    query_turned,
    keys_values,
    keys_turned,
    prob,
    attended,
    normed_low,
    grad_down,
    grad_attn,
    narrow_tokens,
    narrow_attended,
    narrow_normed,
    narrow_grad,
    active,
    grad_up,
    attn_turned,
    qkv_turned,
    exchanged,
    grad_heads,
    heads_turned,
    slope,
    normed_one,
    zhat_one,
    rstd_one,
    grad_two,
    work,
    vec,
    vec_core,
    vec_y,
    vec_x,
    vec_z,
    part,
    came_one,
    came_two,
    came_three,
    came_four,
    load_sem,
    pair_send,
    pair_recv,
    send_sem,
    recv_sem,
):
    grad_one = normed_one
    z, x, y, core = position()
    tok = tokens.shape[0]
    loads = {
        name: pltpu.make_async_copy(source, target, load_sem.at[index])
        for index, (name, source, target) in enumerate(
            (
                ("qkv", qkv_hbm, qkv_w),
                ("out", out_hbm, out_w),
                ("up", up_hbm, up_w),
                ("down", down_hbm, down_w),
            )
        )
    }
    loads["qkv"].start()
    beyond = device(z, x, 1 - y, core)
    beside = device(z, 1 - x, y, core)
    partner = device(z, x, y, 1 - core)
    along = [device(flip_z(z, step), x, y, core) for step in (1, 2, 3)]
    all_here = greet([beyond, beside, partner] + along)
    started = []

    def remote(source, target, send_at, recv_at, other):
        copy = pltpu.make_async_remote_copy(
            src_ref=source,
            dst_ref=target,
            send_sem=send_at,
            recv_sem=recv_at,
            device_id=other,
            device_id_type=MESH,
        )
        copy.start()
        started.append(copy)
        return copy

    pair_count = []

    def to_partner(source, target):
        slot = len(pair_count)
        pair_count.append(slot)
        return remote(source, target, pair_send.at[slot], pair_recv.at[slot], partner)

    own_half = pl.ds(pl.multiple_of(core * HALF, HALF), HALF)
    other_half = pl.ds(pl.multiple_of((1 - core) * HALF, HALF), HALF)

    def span(start, length=D):
        return vectors[0:1, start : start + length]

    def put_vec(start, value):
        for index in range(value.shape[1] // LANES):
            block, row = divmod(start // LANES + index, VEC_BLOCK)
            vec[block, row : row + 1, :] = value[:, index * LANES : (index + 1) * LANES]

    vec[...] = jnp.zeros_like(vec)

    own_rows = pl.ds(0, tok)
    far_rows = pl.ds(tok, tok)
    own_lanes, far_lanes = own_rows, far_rows

    def share_half(value, narrow):
        narrow[own_rows, :] = value[:, own_half]
        return to_partner(value.at[:, other_half], narrow.at[far_rows])

    loads["qkv"].wait()
    for name in ("out", "up", "down"):
        loads[name].start()
    kv_came = []
    for index, start in ((1, None), (2, BIAS_VALUE)):
        value = dot(tokens[...], qkv_w[:, index * D : (index + 1) * D], 1, 0)
        if start is not None:
            value = value + span(start)
        cols = slice((index - 1) * D, index * D)
        keys_values[own_rows, cols] = value.astype(bf16)
        if index == 1:
            all_here()
        kv_came.append(
            to_partner(keys_values.at[own_rows, cols], keys_values.at[far_rows, cols])
        )
    value = dot(tokens[...], qkv_w[:, :D], 1, 0) + span(BIAS_QUERY)
    query[...] = value.astype(bf16)
    query_turned[...] = transposed(query[...])
    allowed = allowed_mask(row_class, lengths, 2 * y + core, tok)
    masks, first = half_masks()
    tokens_came = share_half(tokens, narrow_tokens)
    for copy in kv_came:
        copy.wait_recv()

    scale = HEAD_DIM ** (-0.5)
    for pair in range(HEADS // 2):
        cols = slice(pair * LANES, (pair + 1) * LANES)
        keys = keys_values[:, cols]
        values = keys_values[:, D + cols.start : D + cols.stop]
        outs = []
        for side, mask in enumerate(masks):
            score = dot(query[:, cols] * (mask * scale), keys, 1, 1)
            score = jnp.where(allowed, score, masked_score)
            exponent = jnp.exp(score - jnp.max(score, axis=-1, keepdims=True))
            chance = exponent * (1.0 / jnp.sum(exponent, axis=-1, keepdims=True))
            prob[2 * pair + side] = chance.astype(bf16)
            outs.append(dot(prob[2 * pair + side], values, 1, 0))
        attended[:, cols] = jnp.where(first, outs[0], outs[1]).astype(bf16)
    attended_came = share_half(attended, narrow_attended)

    loads["out"].wait()
    work[...] = dot(attended[...], out_w[...], 1, 0)

    def norm_one(rows, carry):
        value = tokens[rows, :].astype(f32) + (work[rows, :] + span(BIAS_OUT))
        centre = value - row_mean(value)
        rstd = lax.rsqrt(row_mean(centre * centre) + norm_eps)
        zhat = centre * rstd
        normed = zhat * span(GAIN_ONE) + span(SHIFT_ONE)
        zhat_one[rows, :] = zhat
        rstd_one[rows, :] = jnp.broadcast_to(rstd, (ROWS, LANES))
        normed_one[rows, :] = normed
        normed_low[rows, :] = normed.astype(bf16)
        return carry

    by_rows(tok, norm_one)
    normed_came = share_half(normed_low, narrow_normed)

    loads["up"].wait()
    for tile in range(FF // D):
        cols = slice(tile * D, (tile + 1) * D)
        work[...] = dot(normed_low[...], up_w[:, cols], 1, 0)

        def gelu(rows, carry):
            value = work[rows, :] + span(BIAS_UP + cols.start)
            chance, density = normal_parts(value)
            active[rows, cols] = (value * chance).astype(bf16)
            slope[rows, cols] = chance + value * density
            return carry

        by_rows(tok, gelu)
    active_came = to_partner(active.at[own_rows], active.at[far_rows])
    loads["down"].wait()
    work[...] = dot(active[own_rows, :], down_w[...], 1, 0)

    def norm_two(rows, carry):
        value = normed_one[rows, :] + (work[rows, :] + span(BIAS_DOWN))
        centre = value - row_mean(value)
        rstd = lax.rsqrt(row_mean(centre * centre) + norm_eps)
        zhat = centre * rstd
        mixed[rows, :] = zhat * span(GAIN_TWO) + span(SHIFT_TWO)
        grad = cotangent[rows, :].astype(f32)
        inner = grad * span(GAIN_TWO)
        grad_in = (inner - row_mean(inner) - zhat * row_mean(inner * zhat)) * rstd
        grad_two[rows, :] = grad_in
        low = grad_in.astype(bf16)
        grad_down[rows, :] = low
        gain, shift, bias = carry
        return gain + fold(grad * zhat), shift + fold(grad), bias + fold(low.astype(f32))

    zero = jnp.zeros((8, D), f32)
    gain, shift, bias = by_rows(tok, norm_two, (zero, zero, zero))
    put_vec(GAIN_TWO, column_sum(gain))
    put_vec(SHIFT_TWO, column_sum(shift))
    put_vec(BIAS_DOWN, column_sum(bias))
    grad_down_came = share_half(grad_down, narrow_grad)
    keys_turned[...] = transposed(keys_values[:, :D])

    here = {"f": z // 2, "n": z % 2, "x": x, "y": y}
    across = {"f": along[1], "n": along[0], "x": beside, "y": beyond}

    class Chain:
        def __init__(self, index):
            matrix, quarter = divmod(index, PARTS)
            self.index, self.order, self.stage = index, CHUNK_ORDERS[index], 0
            self.own = part.at[matrix, quarter]
            self.came = [ref.at[matrix, quarter] for ref in (came_one, came_two, came_three, came_four)]
            self.final = sums.at[matrix, :, :, quarter]

        def cells(self, free, flipped=None):
            return tuple(
                slice(None) if name in free else 1 - here[name] if name == flipped else here[name]
                for name in "fnxy"
            )

        def send(self, source, target, other):
            sems = (send_sem.at[self.index, self.stage], recv_sem.at[self.index, self.stage])
            self.copy = remote(source, target, *sems, other)

        def advance(self):
            stage, order = self.stage, self.order
            if stage:
                self.copy.wait_recv()
            if 1 <= stage <= 4:
                free = order[stage:]
                for choice in itertools.product((0, 1), repeat=len(free)):
                    taken = dict(zip(sorted(free, key="fnxy".index), choice))
                    at = tuple(taken.get(name, here[name]) for name in "fnxy")
                    value = self.own[at] + self.came[stage - 1][choice]
                    if stage == 4:
                        self.final[core, y] = value
                    else:
                        self.own[at] = value
            if stage < 4:
                name = order[stage]
                source = self.own.at[self.cells(order[stage + 1 :], name)]
                self.send(source, self.came[stage], across[name])
            elif stage == 4:
                block = self.final.at[core, y]
                self.send(block, block, beyond)
            elif stage == 5:
                block = self.final.at[core]
                self.send(block, block, partner)
            self.stage += 1

    chains = [Chain(index) for index in range(3 * PARTS)]
    plan = iter(CHUNK_PLAN)

    def pump():
        for index in next(plan):
            chains[index].advance()

    def feed_forward(matrix, narrow, wide):
        left = transposed(narrow[...])

        def block(index, carry):
            cols = pl.ds(pl.multiple_of(index * UNIT, UNIT), UNIT)
            value = dot(left, wide[:, cols], 1, 0).astype(bf16)
            for side in range(2):
                for quarter in range(PARTS):
                    start = (side * PARTS + quarter) * CHUNK
                    part[matrix, quarter, index // 4, index // 2 % 2, index % 2, side] = value[
                        start : start + CHUNK
                    ]
            return carry

        lax.fori_loop(0, 8, block, 0)

    def projections(matrix, turned, narrow, width, offset, between=None):
        for tile in range(turned.shape[0] // UNIT):
            if between and tile % 2 == 0:
                between()
            value = dot(turned[tile * UNIT : (tile + 1) * UNIT, :], narrow[...], 1, 0).astype(bf16)
            for start in range(0, UNIT, CHUNK):
                block, row = divmod(tile * UNIT + start, width)
                side, row = divmod(offset + row, PARTS * CHUNK)
                part[matrix, row // CHUNK, block // 4, block // 2 % 2, block % 2, side] = value[
                    start : start + CHUNK
                ]

    grad_down_came.wait_recv()
    active_came.wait_recv()
    feed_forward(0, narrow_grad, active)

    for tile in range(FF // D):
        pump()
        cols = slice(tile * D, (tile + 1) * D)
        work[...] = dot(grad_down[...], down_w[cols, :], 1, 1)

        def gelu_back(rows, carry):
            low = (work[rows, :] * slope[rows, cols]).astype(bf16)
            grad_up[rows, cols] = low
            return carry + fold(low.astype(f32))

        put_vec(BIAS_UP + cols.start, column_sum(by_rows(tok, gelu_back, zero)))
    grad_up_came = to_partner(grad_up.at[own_rows], grad_up.at[far_rows])
    pump()
    normed_came.wait_recv()
    grad_up_came.wait_recv()
    feed_forward(1, narrow_normed, grad_up)
    pump()

    work[...] = dot(grad_up[own_rows, :], up_w[...], 1, 1)

    def norm_one_back(rows, carry):
        grad = grad_two[rows, :] + work[rows, :]
        zhat = zhat_one[rows, :]
        inner = grad * span(GAIN_ONE)
        grad_in = inner - row_mean(inner) - zhat * row_mean(inner * zhat)
        grad_in = grad_in * rstd_one[rows, 0:1]
        grad_one[rows, :] = grad_in
        low = grad_in.astype(bf16)
        grad_attn[rows, :] = low
        gain, shift, bias = carry
        return gain + fold(grad * zhat), shift + fold(grad), bias + fold(low.astype(f32))

    gain, shift, bias = by_rows(tok, norm_one_back, (zero, zero, zero))
    put_vec(GAIN_ONE, column_sum(gain))
    put_vec(SHIFT_ONE, column_sum(shift))
    put_vec(BIAS_OUT, column_sum(bias))
    grad_heads[...] = dot(grad_attn[...], out_w[...], 1, 1).astype(bf16)
    heads_turned[...] = dot(out_w[...], grad_attn[...], 1, 1).astype(bf16)

    half_lanes = LANES // 2
    pair_came = []
    for pair in range(HEADS // 2):
        pump()
        cols = slice(pair * LANES, (pair + 1) * LANES)
        values = keys_values[:, D + cols.start : D + cols.stop]
        for side, mask in enumerate(masks):
            rows = slice(cols.start + side * half_lanes, cols.start + (side + 1) * half_lanes)
            chance = prob[2 * pair + side].astype(f32)
            grad_chance = dot(grad_heads[:, cols] * mask, values, 1, 1)
            mean = jnp.sum(chance * grad_chance, axis=-1, keepdims=True)
            grad_score = (chance * (grad_chance - mean)).astype(bf16)
            values_grad = dot(heads_turned[rows, :], prob[2 * pair + side], 1, 0).astype(bf16)
            keys_grad = (dot(query_turned[rows, :], grad_score, 1, 0) * scale).astype(bf16)
            query_grad = (dot(keys_turned[rows, :], grad_score, 1, 1) * scale).astype(bf16)
            blocks = (
                query_grad,
                keys_grad[:, :tok],
                values_grad[:, :tok],
                keys_grad[:, tok:],
                values_grad[:, tok:],
            )
            for index, value in enumerate(blocks):
                start = index * LANES + side * half_lanes
                exchanged[0, pair, start : start + half_lanes, :] = value
        pair_came.append(to_partner(exchanged.at[0, pair], exchanged.at[1, pair]))
    pump()
    attn_turned[:, own_lanes] = transposed(grad_attn[...])
    grad_attn_came = to_partner(attn_turned.at[:, own_lanes], attn_turned.at[:, far_lanes])

    for pair, copy in enumerate(pair_came):
        copy.wait_recv()
        for who, lanes in enumerate((own_lanes, far_lanes)):
            start = pair * LANES
            mine, theirs = exchanged.at[who, pair], exchanged.at[1 - who, pair]
            qkv_turned[start : start + LANES, lanes] = mine[:LANES]
            for index in (1, 2):
                rows = slice(index * LANES, (index + 1) * LANES)
                sent = slice((index + 2) * LANES, (index + 3) * LANES)
                value = mine[rows].astype(f32) + theirs[sent].astype(f32)
                start = index * D + pair * LANES
                qkv_turned[start : start + LANES, lanes] = value.astype(bf16)
    pump()
    tokens_came.wait_recv()
    projections(2, qkv_turned, narrow_tokens, 3 * D // 8, 0, pump)
    attended_came.wait_recv()
    grad_attn_came.wait_recv()
    projections(2, attn_turned, narrow_attended, D // 8, 3 * D // 8)
    pump()

    ones = jnp.ones((8, tok), bf16)
    for start, rows in ((BIAS_QUERY, slice(0, D)), (BIAS_VALUE, slice(2 * D, 3 * D))):
        put_vec(start, dot(ones, qkv_turned[rows, own_lanes], 1, 1)[0:1])
    vec_came = to_partner(vec, vec_core)
    value = dot(qkv_w[...], qkv_turned[:, own_lanes], 1, 0)
    input_grad[...] = grad_one[...] + value.T

    vec_slots = [(send_sem.at[3 * PARTS, i], recv_sem.at[3 * PARTS, i]) for i in range(5)]

    def vec_steps():
        vec_came.wait_recv()
        vec_core[...] = vec[...] + vec_core[...]
        copy = remote(vec_core, vec_y, *vec_slots[0], beyond)
        yield
        copy.wait_recv()
        for i in range(4):
            vec_x[0, i] = vec_core[2 * i + x] + vec_y[2 * i + x]
            vec_x[1, i] = vec_core[2 * i + 1 - x] + vec_y[2 * i + 1 - x]
        copy = remote(vec_x.at[1], vec_x.at[2], *vec_slots[1], beside)
        yield
        copy.wait_recv()
        vec_x[0] = vec_x[0] + vec_x[2]
        copies = [
            remote(
                vec_x.at[0, flip_z(z, step)],
                vec_z.at[step - 1],
                *vec_slots[1 + step],
                along[step - 1],
            )
            for step in (1, 2, 3)
        ]
        yield
        total = vec_x[0, z]
        for step, copy in enumerate(copies):
            copy.wait_recv()
            total = total + vec_z[step]
        vec_sum[...] = total
        yield

    steps = vec_steps()
    for turn, index in enumerate(next(plan)):
        chains[index].advance()
        if turn % 10 == 9 and turn < 40:
            next(steps)
    for copy in started:
        copy.wait_send()


def layer(row_class, lengths, tokens, cotangent, vectors, qkv_w, out_w, up_w, down_w):
    tok = tokens.shape[0]
    chunk = (CHUNK, UNIT)

    def low(*dims):
        return pltpu.VMEM(dims, bf16)

    def wide(*dims):
        return pltpu.VMEM(dims, f32)

    return pl.pallas_call(
        layer_kernel,
        out_shape=(
            jax.ShapeDtypeStruct((tok, D), f32),
            jax.ShapeDtypeStruct((tok, D), f32),
            jax.ShapeDtypeStruct((3, 2, 2, PARTS) + chunk, bf16),
            jax.ShapeDtypeStruct((16, LANES), f32),
        ),
        in_specs=[SMEM, SMEM, VMEM, VMEM, VMEM] + [ANY] * 4,
        out_specs=(VMEM,) * 4,
        scratch_shapes=[
            low(D, 3 * D),
            low(D, D),
            low(D, FF),
            low(FF, D),
            low(tok, D),
            low(D, tok),
            low(2 * tok, 2 * D),
            low(D, 2 * tok),
            low(HEADS, tok, 2 * tok),
            low(tok, D),
            low(tok, D),
            low(tok, D),
            low(tok, D),
            low(2 * tok, HALF),
            low(2 * tok, HALF),
            low(2 * tok, HALF),
            low(2 * tok, HALF),
            low(2 * tok, FF),
            low(2 * tok, FF),
            low(D, 2 * tok),
            low(3 * D, 2 * tok),
            low(2, HEADS // 2, 5 * LANES, tok),
            low(tok, D),
            low(D, tok),
            wide(tok, FF),
            wide(tok, D),
            wide(tok, D),
            wide(tok, LANES),
            wide(tok, D),
            wide(tok, D),
            wide(8, 16, LANES),
            wide(8, 16, LANES),
            wide(8, 16, LANES),
            wide(3, 4, 16, LANES),
            wide(3, 16, LANES),
            low(3, PARTS, 2, 2, 2, 2, *chunk),
            low(3, PARTS, 2, 2, 2, *chunk),
            low(3, PARTS, 2, 2, *chunk),
            low(3, PARTS, 2, *chunk),
            low(3, PARTS, *chunk),
            pltpu.SemaphoreType.DMA((4,)),
            pltpu.SemaphoreType.DMA((16,)),
            pltpu.SemaphoreType.DMA((16,)),
            pltpu.SemaphoreType.DMA((3 * PARTS + 1, 6)),
            pltpu.SemaphoreType.DMA((3 * PARTS + 1, 6)),
        ],
        compiler_params=pltpu.CompilerParams(
            vmem_limit_bytes=63 * MIB, collective_id=0, has_side_effects=True
        ),
        name="layer",
    )(row_class, lengths, tokens, cotangent, vectors[None, :], qkv_w, out_w, up_w, down_w)


GROUP = 3
GRAM_AXES = ("far", "near", "x")
GRAM_ORDERS = tuple(
    tuple(GRAM_AXES["fnx".index(letter)] for letter in order)
    for order in ("xnf", "nxf", "xnf", "nxf", "xnf", "xnf", "fxn")
)
GRAM_PLAN = (0, 1, 2, 3, 6, 4, 0, 5, 1, 2, 0, 4, 3, 1, 6, 2, 5, 0, 3, 6, 1, 2, 4, 0, 5)
GRAM_PLAN += (3, 6, 1, 2, 4, 1, 5, 3, 6, 0, 4, 2, 5, 3, 6, 4, 1, 5, 0, 2, 3, 6, 4, 5)


def muon_kernel(
    sums,
    qkv_hbm,
    out_hbm,
    up_hbm,
    down_hbm,
    factors,
    own_sum,
    qkv_old,
    out_old,
    old,
    moment,
    out,
    part,
    came_one,
    came_two,
    came_three,
    high,
    low,
    load_sem,
    send_sem,
    recv_sem,
    share_send,
    share_recv,
    *ortho,
):
    z, x, y, core = position()
    here = {"far": z // 2, "near": z % 2, "x": x}
    others = {
        "far": device(flip_z(z, 2), x, y, core),
        "near": device(flip_z(z, 1), x, y, core),
        "x": device(z, 1 - x, y, core),
    }
    beyond = device(z, x, 1 - y, core)
    partner = device(z, x, y, 1 - core)
    own = 2 * y + core
    all_here = greet(list(others.values()) + [beyond, partner])

    def load_two(source, target, matrix):
        loads = [
            pltpu.make_async_copy(source, target, load_sem.at[0]),
            pltpu.make_async_copy(sums.at[matrix], own_sum, load_sem.at[1]),
        ]
        for load in loads:
            load.start()
        for load in loads:
            load.wait()

    def from_turned(source, target, skip):
        load_two(source, target, 2)
        rows = target.shape[0]
        moment[...] = jnp.zeros_like(moment)
        for half in range(2):
            cols = slice(half * HALF, (half + 1) * HALF)
            start = half * UNIT + skip
            value = own_sum[start : start + rows, :].astype(f32)
            moment[cols, skip : skip + rows] = (muon_keep * target[:, cols] + value).T

    @pl.when(own == 0)
    def _():
        from_turned(qkv_hbm, qkv_old, 0)

    @pl.when(own == 1)
    def _():
        from_turned(out_hbm, out_old, qkv_old.shape[0])

    @pl.when(own == 2)
    def _():
        load_two(up_hbm, old, 1)
        moment[...] = muon_keep * old[...] + own_sum[...].astype(f32)

    @pl.when(own == 3)
    def _():
        load_two(down_hbm, old, 0)
        moment[...] = muon_keep * old[...] + own_sum[...].astype(f32)

    all_here()
    blocks = sub_blocks(moment.shape[0])
    groups = len(blocks) // GROUP
    high[...] = moment[...].astype(bf16)
    low[...] = (moment[...] - high[...].astype(f32)).astype(bf16)
    started = []

    def product(index):
        i, j = blocks[index]
        left, right = pl.ds(i * SUB, SUB), pl.ds(j * SUB, SUB)
        total = dot(high[left, :], high[right, :], 1, 1)
        total = total + dot(high[left, :], low[right, :], 1, 1)
        total = total + dot(low[left, :], high[right, :], 1, 1)
        rows = SUB // 8
        for owner in range(8):
            cell = (owner // 4, owner // 2 % 2, owner % 2)
            part[(index // GROUP,) + cell + (index % GROUP,)] = total[
                owner * rows : (owner + 1) * rows
            ]

    def send(source, target, group, slot, axis):
        copy = pltpu.make_async_remote_copy(
            src_ref=source,
            dst_ref=target,
            send_sem=send_sem.at[group, slot],
            recv_sem=recv_sem.at[group, slot],
            device_id=others[axis],
            device_id_type=MESH,
        )
        copy.start()
        started.append(copy)
        return copy

    def cells(fixed, flipped=None):
        return tuple(
            1 - here[name] if name == flipped else here[name] if name in fixed else slice(None)
            for name in GRAM_AXES
        )

    class Walk:
        def __init__(self, group, order):
            self.group, self.order, self.stage = group, order, 0
            self.part = part.at[group]
            self.came = (came_one.at[group], came_two.at[group], came_three.at[group])

        def advance(self):
            stage, order = self.stage, self.order
            mine = pl.ds(self.group * GROUP, GROUP)
            if stage:
                self.copy.wait_recv()
            if 1 <= stage <= 3:
                kept = cells(order[:stage])
                total = self.part[kept] + self.came[stage - 1][...]
                if stage == 3:
                    out[kept + (mine,)] = total
                else:
                    self.part[kept] = total
            if stage < 3:
                source = self.part.at[cells(order[:stage], order[stage])]
                self.copy = send(source, self.came[stage], self.group, stage, order[stage])
            elif stage < 6:
                block = out.at[cells(order[: 6 - stage]) + (mine,)]
                self.copy = send(block, block, self.group, stage, order[5 - stage])
            self.stage += 1

    walks = [Walk(group, GRAM_ORDERS[group]) for group in range(groups)]
    for group in GRAM_PLAN:
        if walks[group].stage == 0:
            for index in range(group * GROUP, (group + 1) * GROUP):
                product(index)
        walks[group].advance()

    e = ortho[0]
    for index, (i, j) in enumerate(blocks):
        value = out[:, :, :, index].reshape(SUB, SUB)
        e[i * SUB : (i + 1) * SUB, j * SUB : (j + 1) * SUB] = value
        if i != j:
            e[j * SUB : (j + 1) * SUB, i * SUB : (i + 1) * SUB] = value.T

    across, beside = [], []

    def share(slot, rows, kind, other):
        block = factors.at[slot, rows]
        index = rows.start // TILE
        copy = pltpu.make_async_remote_copy(
            src_ref=block,
            dst_ref=block,
            send_sem=share_send.at[index, kind],
            recv_sem=share_recv.at[index, kind],
            device_id=other,
            device_id_type=MESH,
        )
        copy.start()
        started.append(copy)
        return copy

    def emit(rows, value):
        factors[own, rows, :] = value
        across.append((rows, share(own, rows, 0, beyond)))
        beside.append(share(own, rows, 1, partner))

    newton_schulz(e, moment, *ortho, emit)
    for rows, copy in across:
        copy.wait_recv()
        beside.append(share(2 * (1 - y) + core, rows, 2, partner))
    for copy in beside:
        copy.wait_recv()
    for copy in started:
        copy.wait_send()


def muon_factors(sums, *olds):
    size, cols = olds[2].shape
    count = len(sub_blocks(size))
    groups = count // GROUP
    rows = (SUB // 8, SUB)

    def wide(*dims):
        return pltpu.VMEM(dims, f32)

    return pl.pallas_call(
        muon_kernel,
        out_shape=jax.ShapeDtypeStruct((4, size, cols), bf16),
        in_specs=[ANY] * 5,
        out_specs=VMEM,
        scratch_shapes=[
            pltpu.VMEM((size, cols), bf16),
            wide(*olds[0].shape),
            wide(*olds[1].shape),
            wide(size, cols),
            wide(size, cols),
            wide(2, 2, 2, count, *rows),
            wide(groups, 2, 2, 2, GROUP, *rows),
            wide(groups, 2, 2, GROUP, *rows),
            wide(groups, 2, GROUP, *rows),
            wide(groups, GROUP, *rows),
            pltpu.VMEM((size, cols), bf16),
            pltpu.VMEM((size, cols), bf16),
            pltpu.SemaphoreType.DMA((2,)),
            pltpu.SemaphoreType.DMA((groups, 6)),
            pltpu.SemaphoreType.DMA((groups, 6)),
            pltpu.SemaphoreType.DMA((size // TILE, 3)),
            pltpu.SemaphoreType.DMA((size // TILE, 3)),
        ]
        + ortho_scratch(size, cols),
        compiler_params=pltpu.CompilerParams(
            vmem_limit_bytes=58 * MIB, collective_id=1, has_side_effects=True
        ),
        name="muon_factors",
    )(sums, *olds)


def window(start, width, total):
    size = -(-(width + 96) // LANES) * LANES
    first = jnp.minimum(start // LANES * LANES, total - size)
    return pl.ds(pl.multiple_of(first, LANES), size), start - first


def finish_kernel(
    factors_hbm,
    sums_hbm,
    qkv_hbm,
    out_hbm,
    up_hbm,
    down_hbm,
    qkv_old_hbm,
    out_old_hbm,
    up_old_hbm,
    down_old_hbm,
    mixed_hbm,
    grad_hbm,
    mixed_out,
    grad_out,
    qkv_moment_out,
    out_moment_out,
    up_moment_out,
    down_moment_out,
    qkv_out,
    out_out,
    up_out,
    down_out,
    factors,
    sums,
    qkv_w,
    out_w,
    up_w,
    down_w,
    qkv_moment,
    out_moment,
    up_moment,
    down_moment,
    qkv_new,
    out_new,
    up_new,
    down_new,
    turned,
    load_sem,
    store_sem,
):
    shrink = 1.0 - muon_rate * muon_decay
    dp_id = lax.axis_index("dp")
    qkv_cols, out_cols = qkv_new.shape[0], out_new.shape[0]
    qkv_lanes, qkv_skip = window(dp_id * qkv_cols, qkv_cols, 3 * D)
    out_lanes, out_skip = window(dp_id * out_cols, out_cols, D)
    block = pl.ds(pl.multiple_of(dp_id * UNIT, UNIT), UNIT)
    pairs = {
        "sums": (sums_hbm, sums),
        "up_moment": (up_old_hbm, up_moment),
        "down_moment": (down_old_hbm, down_moment),
        "factors": (factors_hbm, factors),
        "up": (up_hbm.at[:, block], up_w),
        "down": (down_hbm.at[block], down_w),
        "qkv_moment": (qkv_old_hbm, qkv_moment),
        "out_moment": (out_old_hbm, out_moment),
        "qkv": (qkv_hbm.at[:, qkv_lanes], qkv_w),
        "out": (out_hbm.at[:, out_lanes], out_w),
    }
    loads = {
        name: pltpu.make_async_copy(source, target, load_sem.at[index])
        for index, (name, (source, target)) in enumerate(pairs.items())
    }
    for load in loads.values():
        load.start()
    stores = []

    def store(source, target):
        stores.append(pltpu.make_async_copy(source, target, store_sem.at[len(stores)]))
        stores[-1].start()

    store(mixed_hbm, mixed_out)
    store(grad_hbm, grad_out)

    def step(index, rate):
        return muon_rate * rate * factors[index].astype(f32)

    loads["sums"].wait()
    for index, name, target, out in (
        (1, "up_moment", up_moment, up_moment_out),
        (0, "down_moment", down_moment, down_moment_out),
    ):
        loads[name].wait()
        target[...] = muon_keep * target[...] + sums[index].astype(f32)
        store(target, out)
    loads["qkv_moment"].wait()
    loads["out_moment"].wait()
    for half in range(2):
        cols = slice(half * HALF, (half + 1) * HALF)
        value = sums[2, cols].astype(f32)
        qkv_moment[:, cols] = muon_keep * qkv_moment[:, cols] + value[:qkv_cols]
        out_moment[:, cols] = muon_keep * out_moment[:, cols] + value[qkv_cols:]
    store(qkv_moment, qkv_moment_out)
    store(out_moment, out_moment_out)
    loads["factors"].wait()
    loads["up"].wait()
    up_new[...] = up_w[...].astype(f32) * shrink - step(2, math.sqrt(max(1.0, FF / D)))
    store(up_new, up_out)
    loads["down"].wait()
    down_new[...] = down_w[...].astype(f32) * shrink - step(3, 1.0).T
    store(down_new, down_out)
    loads["qkv"].wait()
    turned[...] = qkv_w[...].astype(f32).T
    rows = pl.ds(pl.multiple_of(qkv_skip, 32), qkv_cols)
    qkv_new[...] = turned[rows, :] * shrink - step(0, math.sqrt(3.0)).T[:qkv_cols]
    store(qkv_new, qkv_out)
    loads["out"].wait()
    turned[: out_w.shape[1], :] = out_w[...].astype(f32).T
    rows = pl.ds(pl.multiple_of(out_skip, 32), out_cols)
    out_new[...] = turned[rows, :] * shrink - step(1, 1.0).T[qkv_cols:]
    store(out_new, out_out)
    for copy in stores:
        copy.wait()


def finish(factors, sums, weights, olds, mixed, input_grad):
    shapes = [old.shape for old in olds]
    news = shapes[:3] + [shapes[3][::-1]]

    def wide(shape):
        return pltpu.VMEM(shape, f32)

    return pl.pallas_call(
        finish_kernel,
        out_shape=tuple(
            jax.ShapeDtypeStruct(shape, f32)
            for shape in [mixed.shape, input_grad.shape] + shapes + news
        ),
        in_specs=[ANY] * 12,
        out_specs=(ANY,) * 10,
        scratch_shapes=[
            pltpu.VMEM(factors.shape, bf16),
            pltpu.VMEM(sums.shape, bf16),
            pltpu.VMEM((D, 384), bf16),
            pltpu.VMEM((D, 256), bf16),
            pltpu.VMEM((D, UNIT), bf16),
            pltpu.VMEM((UNIT, D), bf16),
        ]
        + [wide(shape) for shape in shapes + news]
        + [
            wide((384, D)),
            pltpu.SemaphoreType.DMA((10,)),
            pltpu.SemaphoreType.DMA((10,)),
        ],
        compiler_params=pltpu.CompilerParams(vmem_limit_bytes=48 * MIB),
        name="finish",
    )(factors, sums, *weights, *olds, mixed, input_grad)


def swap(value, axis, bit):
    size = lax.axis_size(axis)
    return lax.ppermute(value, axis, [(i, i ^ bit) for i in range(size)])


def scatter_head(value, bit, position):
    half = value.shape[1] // 2
    mine = lax.dynamic_slice_in_dim(value, position * half, half, 1)
    other = lax.dynamic_slice_in_dim(value, (1 - position) * half, half, 1)
    return (mine.astype(f32) + swap(other, "head", bit).astype(f32)).astype(bf16)


def scatter_dp_pair(value, position):
    paired = value.reshape((value.shape[0] // 2, 2) + value.shape[1:])
    mine = lax.dynamic_index_in_dim(paired, position, 1, False)
    other = lax.dynamic_index_in_dim(paired, 1 - position, 1, False)
    return (mine.astype(f32) + swap(other, "dp", 1).astype(f32)).astype(bf16)


def scatter_dp_rest(value, place):
    ranks = value.shape[0]
    total = lax.dynamic_index_in_dim(value, place, 0, False).astype(f32)
    for step in range(1, ranks):
        sent = lax.dynamic_index_in_dim(value, place ^ step, 0, False)
        total = total + swap(sent, "dp", 2 * step).astype(f32)
    return total


def local(
    tokens,
    cotangent,
    qkv_weight,
    out_weight,
    up_weight,
    down_weight,
    vectors,
    qkv_moment,
    out_moment,
    up_moment,
    down_moment,
    adam_first,
    adam_second,
    bucket_class,
    row_lengths,
):
    n_dp = lax.axis_size("dp")
    n_head = lax.axis_size("head")
    dp_id = lax.axis_index("dp")
    head_id = lax.axis_index("head")
    core, side = head_id % 2, head_id // 2
    tok, width = tokens.shape
    hidden = up_weight.shape[1]
    half = width // 2
    qkv_cols, out_cols = qkv_moment.shape[1], out_moment.shape[1]
    shrink = 1.0 - muon_rate * muon_decay

    def weight_block(weight, cols, dim):
        return lax.dynamic_slice_in_dim(weight, dp_id * cols, cols, dim)

    block = head_id.astype(jnp.int32)[None]
    vec_len = vectors.shape[0] // n_dp
    if (n_dp, n_head, tok) == (8, 4, 256):
        mixed, input_grad, sums, vec = layer(
            bucket_class,
            row_lengths,
            tokens,
            cotangent,
            vectors,
            qkv_weight,
            out_weight,
            up_weight,
            down_weight,
        )
        grad_vec = vec[:VEC_BLOCK].reshape(vec_len)
        sums = sums.reshape(3, width, -1)
        olds = [qkv_moment.T, out_moment.T, up_moment, down_moment]
        mixed, input_grad, *results = finish(
            muon_factors(sums, *olds),
            sums,
            [qkv_weight, out_weight, up_weight, down_weight],
            olds,
            mixed,
            input_grad,
        )
        moments, new_weights = results[:4], results[4:]
        moments = [moments[0].T, moments[1].T, *moments[2:]]
        new_weights = [new_weights[0].T, new_weights[1].T, *new_weights[2:]]
    else:
        pieces = split_vectors(vectors, width, hidden)
        bias_query, bias_value, bias_out, gain_one, shift_one = pieces[:5]
        bias_up, bias_down, gain_two, shift_two = pieces[5:]
        bias_qkv = jnp.concatenate([bias_query, jnp.zeros_like(bias_query), bias_value])

        def column_half(value, which):
            return lax.dynamic_slice_in_dim(value, which * half, half, 1)

        qkv = (dot(tokens, qkv_weight, 1, 0) + bias_qkv).astype(bf16)
        other = swap(qkv[:, width:], "head", 1)
        attended = attend(block, bucket_class, row_lengths, qkv, other)
        attn_val = dot(attended, out_weight, 1, 0) + bias_out
        resid_one = tokens.astype(f32) + attn_val
        centre = resid_one - jnp.mean(resid_one, axis=-1, keepdims=True)
        rstd_one = lax.rsqrt(jnp.mean(centre * centre, axis=-1, keepdims=True) + norm_eps)
        zhat_one = centre * rstd_one
        normed_one = zhat_one * gain_one + shift_one
        normed_low = normed_one.astype(bf16)
        up_val = dot(normed_low, up_weight, 1, 0) + bias_up
        phi_cum = 0.5 * (1.0 + lax.erf(up_val * (0.5**0.5)))
        active_low = (up_val * phi_cum).astype(bf16)
        slope = phi_cum + up_val * jnp.exp(-0.5 * up_val * up_val) * (1.0 / math.sqrt(2.0 * math.pi))
        down_val = dot(active_low, down_weight, 1, 0) + bias_down
        resid_two = normed_one + down_val
        centre = resid_two - jnp.mean(resid_two, axis=-1, keepdims=True)
        rstd_two = lax.rsqrt(jnp.mean(centre * centre, axis=-1, keepdims=True) + norm_eps)
        zhat_two = centre * rstd_two
        mixed = zhat_two * gain_two + shift_two

        def norm_back(grad, gain, zhat, rstd):
            inner = grad * gain
            mean = jnp.mean(inner, axis=-1, keepdims=True)
            slant = jnp.mean(inner * zhat, axis=-1, keepdims=True)
            return (inner - mean - zhat * slant) * rstd, jnp.sum(grad * zhat, axis=0), jnp.sum(grad, axis=0)

        grad_two, grad_gain_two, grad_shift_two = norm_back(
            cotangent.astype(f32), gain_two, zhat_two, rstd_two
        )
        grad_down_low = grad_two.astype(bf16)
        grad_bias_down = jnp.sum(grad_down_low, axis=0, dtype=f32)

        x_id, z_id = dp_id % 2, dp_id // 2

        grad_up_low = (dot(grad_down_low, down_weight, 1, 1) * slope).astype(bf16)
        grad_bias_up = jnp.sum(grad_up_low, axis=0, dtype=f32)
        grad_normed = grad_two + dot(grad_up_low, up_weight, 1, 1)
        grad_one, grad_gain_one, grad_shift_one = norm_back(grad_normed, gain_one, zhat_one, rstd_one)
        grad_attn_low = grad_one.astype(bf16)
        grad_bias_out = jnp.sum(grad_attn_low, axis=0, dtype=f32)
        grad_heads = dot(grad_attn_low, out_weight, 1, 1).astype(bf16)
        grad_query, own, sent = attend_back(block, bucket_class, row_lengths, qkv, other, grad_heads)
        grad_kv = (own + swap(sent, "head", 1).astype(f32)).astype(bf16)
        grad_qkv = jnp.concatenate([grad_query, grad_kv], axis=1)
        grad_bias_qkv = jnp.sum(grad_qkv, axis=0, dtype=f32)
        input_grad = grad_one + dot(grad_qkv, qkv_weight, 1, 1)
        grad_vector = jnp.concatenate(
            [
                grad_bias_qkv[:width],
                grad_bias_qkv[2 * width :],
                grad_bias_out,
                grad_gain_one,
                grad_shift_one,
                grad_bias_up,
                grad_bias_down,
                grad_gain_two,
                grad_shift_two,
            ]
        )
        grad_vector = grad_vector + swap(grad_vector, "head", 1)
        wides = [active_low, grad_up_low, grad_attn_low, grad_qkv]
        narrows = [grad_down_low, normed_low, attended, tokens]

        def both_halves(value):
            return jnp.concatenate(
                [column_half(value, core), swap(column_half(value, 1 - core), "head", 1)], axis=0
            )

        def weight_grad(wide, narrow):
            wide = jnp.concatenate([wide, swap(wide, "head", 1)], axis=0)
            value = dot(wide, both_halves(narrow), 0, 0).astype(bf16)
            return value.reshape(n_dp, value.shape[0] // n_dp, half)

        def reduce_y_first(value):
            return scatter_dp_rest(scatter_dp_pair(scatter_head(value, 2, side), x_id), z_id)

        def reduce_x_first(value):
            return scatter_dp_rest(scatter_head(scatter_dp_pair(value, x_id), 2, side), z_id)

        def spread(value):
            value = value.astype(bf16)
            came = swap(value, "head", 2)
            value = jnp.concatenate(
                [jnp.where(side == 0, value, came), jnp.where(side == 0, came, value)], axis=0
            )
            came = swap(value, "head", 1)
            return jnp.concatenate(
                [jnp.where(core == 0, value, came), jnp.where(core == 0, came, value)], axis=1
            ).astype(f32)

        down_part, up_part, out_part, qkv_part = [
            weight_grad(wide, narrow) for wide, narrow in zip(wides, narrows)
        ]
        vec_rows = 16
        vec_part = grad_vector.reshape(n_dp, vec_len)
        vec_part = jnp.pad(vec_part, ((0, 0), (0, vec_rows * width - vec_len)))
        vec_part = vec_part.reshape(n_dp, vec_rows, width)
        vec_part = lax.dynamic_slice_in_dim(vec_part, core * half, half, 2).astype(bf16)
        down_new = spread(reduce_x_first(down_part))
        up_new = spread(reduce_y_first(up_part))
        tail_new = spread(
            reduce_y_first(jnp.concatenate([qkv_part, out_part, vec_part], axis=1))
        )
        grads = [
            tail_new[:qkv_cols].T,
            tail_new[qkv_cols : qkv_cols + out_cols].T,
            up_new.T,
            down_new.T,
        ]
        grad_vec = tail_new[qkv_cols + out_cols :].reshape(-1)[:vec_len]
        moments = [
            muon_keep * old + grad
            for old, grad in zip([qkv_moment, out_moment, up_moment, down_moment], grads)
        ]
        most = max(m.shape[1] for m in moments)
        padded = [jnp.pad(m, ((0, 0), (0, most - m.shape[1]))) for m in moments]
        chosen = padded[-1]
        for index in range(len(padded) - 2, -1, -1):
            chosen = jnp.where(head_id == index, padded[index], chosen)
        gram_mat = lax.dot_general(
            chosen, chosen, (((1,), (1,)), ((), ())), precision=lax.Precision.HIGH
        )
        own_factor = orthogonalize(lax.psum(gram_mat, "dp"), chosen)
        across = swap(own_factor, "head", 2)
        low_pair = jnp.where(side == 0, own_factor, across)
        high_pair = jnp.where(side == 0, across, own_factor)
        near_low = swap(low_pair, "head", 1)
        near_high = swap(high_pair, "head", 1)
        factors = [
            jnp.where(core == 0, low_pair, near_low),
            jnp.where(core == 0, near_low, low_pair),
            jnp.where(core == 0, high_pair, near_high),
            jnp.where(core == 0, near_high, high_pair),
        ]
        factors = [o[:, : m.shape[1]].astype(f32) for o, m in zip(factors, moments)]
        factors[3] = factors[3].T
        old_weights = [
            weight_block(qkv_weight, qkv_cols, 1),
            weight_block(out_weight, out_cols, 1),
            weight_block(up_weight, up_moment.shape[1], 1),
            weight_block(down_weight, down_moment.shape[1], 0),
        ]

        rates = (math.sqrt(3.0), 1.0, math.sqrt(max(1.0, hidden / width)), 1.0)
        new_weights = [
            old.astype(f32) * shrink - muon_rate * rate * factor
            for old, rate, factor in zip(old_weights, rates, factors)
        ]

    vec_old = lax.dynamic_slice_in_dim(vectors, dp_id * vec_len, vec_len, 0)
    vec_first = beta_first * adam_first + (1.0 - beta_first) * grad_vec
    vec_second = beta_second * adam_second + (1.0 - beta_second) * grad_vec * grad_vec
    first_hat = vec_first / (1.0 - beta_first**STEP)
    second_hat = vec_second / (1.0 - beta_second**STEP)
    vec_new = vec_old - adam_rate * first_hat / (jnp.sqrt(second_hat) + adam_eps)
    return (mixed, input_grad, *moments, *new_weights, vec_first, vec_second, vec_new)


def solution(mesh):
    tokens_spec = P(("dp", "head"), None)
    block_spec = P(None, "dp")
    return jax.shard_map(
        local,
        mesh=mesh,
        in_specs=(
            tokens_spec,
            tokens_spec,
            P(),
            P(),
            P(),
            P(),
            P(),
            block_spec,
            block_spec,
            block_spec,
            block_spec,
            P("dp"),
            P("dp"),
            P("dp"),
            P("dp", None),
        ),
        out_specs=(
            tokens_spec,
            tokens_spec,
            block_spec,
            block_spec,
            block_spec,
            block_spec,
            block_spec,
            block_spec,
            block_spec,
            P("dp", None),
            P("dp"),
            P("dp"),
            P("dp"),
        ),
        check_vma=False,
    )
```

```python
import functools
import itertools
import math

import jax
import jax.numpy as jnp
from jax import lax
from jax.experimental import pallas as pl
from jax.experimental.pallas import tpu as pltpu
from jax.sharding import PartitionSpec as P

D = 768
HEADS = 12
HEAD_DIM = 64
FF = 3072
BASE_LEN = 128
NS_STEPS = 5
STEP = 5
MAX_LEN = 512

f32 = jnp.float32
bf16 = jnp.bfloat16

norm_eps = 1e-12
masked_score = -1000000000.0
quintic_a = 3.4445
quintic_b = -4.775
quintic_c = 2.0315
muon_rate = 1.0
muon_decay = 0.01
muon_keep = 0.5
adam_rate = 0.2
beta_first = 0.9
beta_second = 0.999
adam_eps = 1e-08
MIB = 1024 * 1024


def dot(left, right, left_dim, right_dim):
    return lax.dot_general(
        left, right, (((left_dim,), (right_dim,)), ((), ())), preferred_element_type=f32
    )


def split_vectors(vectors, width, hidden):
    lengths_list = [width] * 5 + [hidden] + [width] * 3
    pieces = []
    offset = 0
    for length in lengths_list:
        pieces.append(vectors[offset : offset + length])
        offset = offset + length
    return pieces


def allowed_mask(class_ref, length_ref, block, tok):
    shift = class_ref[0] + int(math.log2(BASE_LEN))
    query_place = block * tok + lax.broadcasted_iota(jnp.int32, (tok, 1), 0)
    lane = lax.broadcasted_iota(jnp.int32, (1, 2 * tok), 1)
    own = lane < tok
    key_place = jnp.where(own, block * tok + lane, (block ^ 1) * tok + lane - tok)
    key_row = lax.shift_right_logical(key_place, jnp.broadcast_to(shift, key_place.shape))
    offset = key_place - lax.shift_left(key_row, jnp.broadcast_to(shift, key_place.shape))
    row_len = jnp.zeros_like(key_row)
    for slot in range(length_ref.shape[1]):
        row_len = jnp.where(key_row == slot, length_ref[0, slot], row_len)
    key_row = jnp.where(offset < row_len, key_row, -1)
    query_row = lax.shift_right_logical(query_place, jnp.broadcast_to(shift, query_place.shape))
    return query_row == key_row


def half_masks():
    lane = lax.broadcasted_iota(jnp.int32, (1, 2 * HEAD_DIM), 1)
    first = (lane < HEAD_DIM).astype(f32)
    return (first.astype(bf16), (1.0 - first).astype(bf16)), lane < HEAD_DIM


def head_prob(query, keys, allowed):
    score = jnp.where(allowed, dot(query, keys, 1, 1) * HEAD_DIM ** (-0.5), masked_score)
    exponent = jnp.exp(score - jnp.max(score, axis=-1, keepdims=True))
    return exponent / jnp.sum(exponent, axis=-1, keepdims=True)


def attend_kernel(block_ref, class_ref, length_ref, qkv_ref, other_ref, out_ref):
    tok = qkv_ref.shape[0]
    allowed = allowed_mask(class_ref, length_ref, block_ref[0], tok)
    masks, first = half_masks()
    for pair in range(HEADS // 2):
        cols = pl.ds(pair * 2 * HEAD_DIM, 2 * HEAD_DIM)
        kcols = pl.ds(D + pair * 2 * HEAD_DIM, 2 * HEAD_DIM)
        vcols = pl.ds(2 * D + pair * 2 * HEAD_DIM, 2 * HEAD_DIM)
        query = qkv_ref[:, cols]
        keys = jnp.concatenate([qkv_ref[:, kcols], other_ref[:, cols]], axis=0)
        values = jnp.concatenate([qkv_ref[:, vcols], other_ref[:, kcols]], axis=0)
        outs = []
        for mask in masks:
            prob = head_prob(query * mask, keys, allowed)
            outs.append(dot(prob.astype(bf16), values, 1, 0))
        out_ref[:, cols] = jnp.where(first, outs[0], outs[1]).astype(bf16)


def attend_back_kernel(
    block_ref, class_ref, length_ref, qkv_ref, other_ref, grad_ref, dq_ref, own_ref, send_ref
):
    tok = qkv_ref.shape[0]
    allowed = allowed_mask(class_ref, length_ref, block_ref[0], tok)
    masks, first = half_masks()
    scale = HEAD_DIM ** (-0.5)
    for pair in range(HEADS // 2):
        cols = pl.ds(pair * 2 * HEAD_DIM, 2 * HEAD_DIM)
        kcols = pl.ds(D + pair * 2 * HEAD_DIM, 2 * HEAD_DIM)
        vcols = pl.ds(2 * D + pair * 2 * HEAD_DIM, 2 * HEAD_DIM)
        query = qkv_ref[:, cols]
        keys = jnp.concatenate([qkv_ref[:, kcols], other_ref[:, cols]], axis=0)
        values = jnp.concatenate([qkv_ref[:, vcols], other_ref[:, kcols]], axis=0)
        grad = grad_ref[:, cols]
        dqs, dk, dv = [], None, None
        for mask in masks:
            head_query = query * mask
            head_grad = grad * mask
            prob = head_prob(head_query, keys, allowed)
            part_v = dot(prob.astype(bf16), head_grad, 0, 0)
            dprob = dot(head_grad, values, 1, 1)
            dscore = prob * (dprob - jnp.sum(prob * dprob, axis=-1, keepdims=True))
            dscore = dscore.astype(bf16)
            dqs.append(dot(dscore, keys, 1, 0))
            part_k = dot(dscore, head_query, 0, 0)
            dk = part_k if dk is None else dk + part_k
            dv = part_v if dv is None else dv + part_v
        dk = dk * scale
        dq_ref[:, cols] = (jnp.where(first, dqs[0], dqs[1]) * scale).astype(bf16)
        own_ref[:, cols] = dk[:tok]
        own_ref[:, kcols] = dv[:tok]
        send_ref[:, cols] = dk[tok:].astype(bf16)
        send_ref[:, kcols] = dv[tok:].astype(bf16)


SMEM = pl.BlockSpec(memory_space=pltpu.SMEM)
VMEM = pl.BlockSpec(memory_space=pltpu.VMEM)
ANY = pl.BlockSpec(memory_space=pl.ANY)


def attend(block, row_class, lengths, qkv, other):
    tok = qkv.shape[0]
    return pl.pallas_call(
        attend_kernel,
        out_shape=jax.ShapeDtypeStruct((tok, D), bf16),
        in_specs=[SMEM, SMEM, SMEM, VMEM, VMEM],
        out_specs=VMEM,
        compiler_params=pltpu.CompilerParams(vmem_limit_bytes=32 * MIB),
        name="attend",
    )(block, row_class, lengths, qkv, other)


def attend_back(block, row_class, lengths, qkv, other, grad):
    tok = qkv.shape[0]
    return pl.pallas_call(
        attend_back_kernel,
        out_shape=(
            jax.ShapeDtypeStruct((tok, D), bf16),
            jax.ShapeDtypeStruct((tok, 2 * D), f32),
            jax.ShapeDtypeStruct((tok, 2 * D), bf16),
        ),
        in_specs=[SMEM, SMEM, SMEM, VMEM, VMEM, VMEM],
        out_specs=(VMEM, VMEM, VMEM),
        compiler_params=pltpu.CompilerParams(vmem_limit_bytes=32 * MIB),
        name="attend_back",
    )(block, row_class, lengths, qkv, other, grad)


CENTRES = (0.0, 0.0, 0.0, 0.8, 0.8)
TILE = 256
SUB = 128


def sub_blocks(size):
    count = size // SUB
    return [(i, j) for i in range(count) for j in range(i, count)]


def newton_schulz(gram, moment, e, f, g, eb, fb, gb, ya, yb, y, emit):
    size = e.shape[0]
    tiles = [slice(i * TILE, (i + 1) * TILE) for i in range(size // TILE)]

    def unit(rows):
        row_id = rows.start + lax.broadcasted_iota(jnp.int32, (TILE, size), 0)
        col_id = lax.broadcasted_iota(jnp.int32, (TILE, size), 1)
        return (row_id == col_id).astype(f32)

    diagonal = jnp.zeros((TILE, size), f32)
    for rows in tiles:
        diagonal = diagonal + gram[rows, :] * unit(rows)
    trace = jnp.sum(jnp.sum(diagonal, axis=0, keepdims=True), axis=1, keepdims=True)
    factor = 1.0 / (jnp.sqrt(trace) + 1e-07)
    square_factor = factor * factor
    for rows in tiles:
        value = gram[rows, :] * square_factor
        e[rows, :] = value
        eb[rows, :] = value.astype(bf16)
        value = moment[rows, :] * factor
        y[rows, :] = value
        ya[rows, :] = value.astype(bf16)
    now, then = ya, yb
    for step in range(NS_STEPS):
        last = step + 1 == NS_STEPS
        centre = CENTRES[step]
        after = 0.0 if last else CENTRES[step + 1]
        keep = quintic_a + quintic_b * centre + quintic_c * centre * centre
        linear = quintic_b + 2.0 * quintic_c * centre
        for rows in tiles:
            value = linear * e[rows, :] + quintic_c * dot(eb[rows, :], eb[...], 1, 0)
            fb[rows, :] = value.astype(bf16)
            if not last:
                f[rows, :] = value
        for rows in tiles:
            value = keep * y[rows, :] + dot(fb[rows, :], now[...], 1, 0)
            if last:
                emit(rows, value.astype(bf16))
            else:
                y[rows, :] = value
                then[rows, :] = value.astype(bf16)
        if last:
            break
        now, then = then, now
        for rows in tiles:
            value = keep * e[rows, :] + dot(eb[rows, :], fb[...], 1, 0)
            if centre:
                value = value + centre * f[rows, :]
            g[rows, :] = value
            gb[rows, :] = value.astype(bf16)
        for rows in tiles:
            value = keep * g[rows, :] + dot(gb[rows, :], fb[...], 1, 0)
            if centre:
                value = value + (centre * keep) * f[rows, :]
            shift = centre * keep * keep - after
            if shift:
                value = value + shift * unit(rows)
            e[rows, :] = value
            eb[rows, :] = value.astype(bf16)


def ortho_kernel(gram, moment, out, *scratch):
    def emit(rows, value):
        out[rows, :] = value

    newton_schulz(gram, moment, *scratch, emit)


def ortho_scratch(size, cols):
    square, square_low = pltpu.VMEM((size, size), f32), pltpu.VMEM((size, size), bf16)
    wide_low = pltpu.VMEM((size, cols), bf16)
    return [square] * 3 + [square_low] * 3 + [wide_low] * 2 + [pltpu.VMEM((size, cols), f32)]


def orthogonalize(gram_mat, moment):
    size, cols = moment.shape
    return pl.pallas_call(
        ortho_kernel,
        out_shape=jax.ShapeDtypeStruct((size, cols), bf16),
        in_specs=[VMEM, VMEM],
        out_specs=VMEM,
        scratch_shapes=ortho_scratch(size, cols),
        compiler_params=pltpu.CompilerParams(vmem_limit_bytes=48 * MIB),
        name="ortho",
    )(gram_mat, moment)


MESH = pl.DeviceIdType.MESH
PIECE = 48
SIDE = 192
UNIT = 2 * SIDE
HALF = D // 2
LANES = 128
VEC_BLOCK = 9
ROWS = 16
CHUNKS = (
    (0, 0, 64, "nfyx"),
    (0, 64, 64, "xynf"),
    (0, 128, 64, "yxnf"),
    (1, 0, 64, "ynxf"),
    (1, 64, 64, "nxyf"),
    (1, 128, 64, "xynf"),
    (2, 0, 48, "xynf"),
    (2, 48, 48, "nxyf"),
    (2, 96, 48, "yxnf"),
    (2, 144, 32, "xynf"),
    (2, 176, 16, "xfyn"),
)
CHUNK_PLAN = (
    (0, 1, 2),
    (),
    (),
    (),
    (),
    (3, 5, 4),
    (),
    (0, 1, 2),
    (),
    (),
    (),
    (),
    (),
    (),
    (0, 1, 2, 4, 5, 3),
    (),
    (),
    (0, 7, 8, 10, 9, 6),
    (
        1, 4, 2, 5, 0, 1, 10, 4, 0, 2, 0, 1, 9, 1, 3, 2, 5, 10, 4, 8, 2, 6,
        10, 5, 9, 3, 4, 10, 7, 4, 8, 10, 5, 9, 3, 10, 5, 6, 9, 8, 7, 3, 9, 6,
        3, 9, 8, 7, 8, 6, 8, 7, 6, 7, 6, 7,
    ),
)
BIAS_QUERY, BIAS_VALUE, BIAS_OUT, GAIN_ONE, SHIFT_ONE, BIAS_UP = (i * D for i in range(6))
BIAS_DOWN, GAIN_TWO, SHIFT_TWO = (BIAS_UP + FF + i * D for i in range(3))


def position():
    dp_id, head_id = lax.axis_index("dp"), lax.axis_index("head")
    z, x = dp_id // 2, dp_id % 2
    y, core = head_id // 2, head_id % 2
    return z, x, y, core


def device(z, x, y, core):
    return (2 * z + x, 2 * y + core)


def flip_z(z, step):
    high, low = z // 2, z % 2
    high = 1 - high if step // 2 else high
    low = 1 - low if step % 2 else low
    return 2 * high + low


def greet(others):
    barrier = pltpu.get_barrier_semaphore()
    for other in others:
        pl.semaphore_signal(barrier, inc=1, device_id=other, device_id_type=MESH)
    return lambda: pl.semaphore_wait(barrier, len(others))


def by_rows(count, body, init=None, together=4):
    def step(index, carry):
        for part in range(together):
            start = (index * together + part) * ROWS
            carry = body(pl.ds(pl.multiple_of(start, ROWS), ROWS), carry)
        return carry

    return lax.fori_loop(0, count // (ROWS * together), step, init)


def row_mean(value):
    return jnp.sum(value, axis=-1, keepdims=True) * (1.0 / D)


def fold(value):
    return jnp.sum(value.reshape(value.shape[0] // 8, 8, value.shape[1]), axis=0)


def column_sum(value):
    return jnp.sum(value, axis=0, keepdims=True)


def normal_parts(value):
    size = jnp.abs(value)
    decay = jnp.exp(-0.5 * value * value)
    below = 1.0 + (0.3275911 * 0.5**0.5) * size
    t = pl.reciprocal(below, approx=True)
    t = t * (2.0 - below * t)
    series = t * (1.061405429 * 0.5)
    for term in (-1.453152027, 1.421413741, -0.284496736, 0.254829592):
        series = (series + term * 0.5) * t
    tail = series * decay
    return jnp.where(value < 0.0, tail, 1.0 - tail), decay * (1.0 / math.sqrt(2.0 * math.pi))


def transposed(value):
    side = 2 * LANES
    row_id = lax.broadcasted_iota(jnp.int32, (side, side), 0)
    unit = (row_id == lax.broadcasted_iota(jnp.int32, (side, side), 1)).astype(f32).astype(bf16)
    blocks = []
    for start in range(0, value.shape[1], side):
        block = value[:, start : start + side]
        size = block.shape[1]
        blocks.append(dot(unit[:size, :size], block, 1, 1).astype(bf16))
    return jnp.concatenate(blocks, axis=0)


def layer_kernel(
    row_class,
    lengths,
    tokens,
    cotangent,
    vectors,
    qkv_hbm,
    out_hbm,
    up_hbm,
    down_hbm,
    mixed,
    input_grad,
    sums,
    vec_sum,
    qkv_w,
    out_w,
    up_w,
    down_w,
    query,
    query_turned,
    keys_values,
    keys_turned,
    prob,
    attended,
    normed_low,
    grad_down,
    grad_attn,
    narrow_tokens,
    narrow_attended,
    narrow_normed,
    narrow_grad,
    active,
    grad_up,
    attn_turned,
    qkv_turned,
    exchanged,
    grad_heads,
    heads_turned,
    slope,
    normed_one,
    zhat_one,
    rstd_one,
    grad_two,
    work,
    vec,
    vec_core,
    vec_y,
    vec_x,
    vec_z,
    part,
    came_one,
    came_two,
    came_three,
    came_four,
    load_sem,
    pair_send,
    pair_recv,
    send_sem,
    recv_sem,
):
    grad_one = normed_one
    z, x, y, core = position()
    tok = tokens.shape[0]
    loads = {
        name: pltpu.make_async_copy(source, target, load_sem.at[index])
        for index, (name, source, target) in enumerate(
            (
                ("qkv", qkv_hbm, qkv_w),
                ("out", out_hbm, out_w),
                ("up", up_hbm, up_w),
                ("down", down_hbm, down_w),
            )
        )
    }
    loads["qkv"].start()
    beyond = device(z, x, 1 - y, core)
    beside = device(z, 1 - x, y, core)
    partner = device(z, x, y, 1 - core)
    along = [device(flip_z(z, step), x, y, core) for step in (1, 2, 3)]
    all_here = greet([beyond, beside, partner] + along)
    started = []

    def remote(source, target, send_at, recv_at, other):
        copy = pltpu.make_async_remote_copy(
            src_ref=source,
            dst_ref=target,
            send_sem=send_at,
            recv_sem=recv_at,
            device_id=other,
            device_id_type=MESH,
        )
        copy.start()
        started.append(copy)
        return copy

    pair_count = []

    def to_partner(source, target):
        slot = len(pair_count)
        pair_count.append(slot)
        return remote(source, target, pair_send.at[slot], pair_recv.at[slot], partner)

    own_half = pl.ds(pl.multiple_of(core * HALF, HALF), HALF)
    other_half = pl.ds(pl.multiple_of((1 - core) * HALF, HALF), HALF)

    def span(start, length=D):
        return vectors[0:1, start : start + length]

    def put_vec(start, value):
        for index in range(value.shape[1] // LANES):
            block, row = divmod(start // LANES + index, VEC_BLOCK)
            vec[block, row : row + 1, :] = value[:, index * LANES : (index + 1) * LANES]

    vec[...] = jnp.zeros_like(vec)

    own_rows = pl.ds(0, tok)
    far_rows = pl.ds(tok, tok)
    own_lanes, far_lanes = own_rows, far_rows

    def share_half(value, narrow):
        narrow[own_rows, :] = value[:, own_half]
        return to_partner(value.at[:, other_half], narrow.at[far_rows])

    loads["qkv"].wait()
    for name in ("out", "up", "down"):
        loads[name].start()
    kv_came = []
    for index, start in ((1, None), (2, BIAS_VALUE)):
        value = dot(tokens[...], qkv_w[:, index * D : (index + 1) * D], 1, 0)
        if start is not None:
            value = value + span(start)
        cols = slice((index - 1) * D, index * D)
        keys_values[own_rows, cols] = value.astype(bf16)
        if index == 1:
            all_here()
        kv_came.append(
            to_partner(keys_values.at[own_rows, cols], keys_values.at[far_rows, cols])
        )
    value = dot(tokens[...], qkv_w[:, :D], 1, 0) + span(BIAS_QUERY)
    query[...] = value.astype(bf16)
    query_turned[...] = transposed(query[...])
    allowed = allowed_mask(row_class, lengths, 2 * y + core, tok)
    masks, first = half_masks()
    tokens_came = share_half(tokens, narrow_tokens)
    for copy in kv_came:
        copy.wait_recv()

    scale = HEAD_DIM ** (-0.5)
    for pair in range(HEADS // 2):
        cols = slice(pair * LANES, (pair + 1) * LANES)
        keys = keys_values[:, cols]
        values = keys_values[:, D + cols.start : D + cols.stop]
        outs = []
        for side, mask in enumerate(masks):
            score = dot(query[:, cols] * (mask * scale), keys, 1, 1)
            score = jnp.where(allowed, score, masked_score)
            exponent = jnp.exp(score - jnp.max(score, axis=-1, keepdims=True))
            chance = exponent * (1.0 / jnp.sum(exponent, axis=-1, keepdims=True))
            prob[2 * pair + side] = chance.astype(bf16)
            outs.append(dot(prob[2 * pair + side], values, 1, 0))
        attended[:, cols] = jnp.where(first, outs[0], outs[1]).astype(bf16)
    attended_came = share_half(attended, narrow_attended)

    loads["out"].wait()
    work[...] = dot(attended[...], out_w[...], 1, 0)

    def norm_one(rows, carry):
        value = tokens[rows, :].astype(f32) + (work[rows, :] + span(BIAS_OUT))
        centre = value - row_mean(value)
        rstd = lax.rsqrt(row_mean(centre * centre) + norm_eps)
        zhat = centre * rstd
        normed = zhat * span(GAIN_ONE) + span(SHIFT_ONE)
        zhat_one[rows, :] = zhat
        rstd_one[rows, :] = jnp.broadcast_to(rstd, (ROWS, LANES))
        normed_one[rows, :] = normed
        normed_low[rows, :] = normed.astype(bf16)
        return carry

    by_rows(tok, norm_one)
    normed_came = share_half(normed_low, narrow_normed)

    loads["up"].wait()
    for tile in range(FF // D):
        cols = slice(tile * D, (tile + 1) * D)
        work[...] = dot(normed_low[...], up_w[:, cols], 1, 0)

        def gelu(rows, carry):
            value = work[rows, :] + span(BIAS_UP + cols.start)
            chance, density = normal_parts(value)
            active[rows, cols] = (value * chance).astype(bf16)
            slope[rows, cols] = chance + value * density
            return carry

        by_rows(tok, gelu)
    active_came = to_partner(active.at[own_rows], active.at[far_rows])
    loads["down"].wait()
    work[...] = dot(active[own_rows, :], down_w[...], 1, 0)

    def norm_two(rows, carry):
        value = normed_one[rows, :] + (work[rows, :] + span(BIAS_DOWN))
        centre = value - row_mean(value)
        rstd = lax.rsqrt(row_mean(centre * centre) + norm_eps)
        zhat = centre * rstd
        mixed[rows, :] = zhat * span(GAIN_TWO) + span(SHIFT_TWO)
        grad = cotangent[rows, :].astype(f32)
        inner = grad * span(GAIN_TWO)
        grad_in = (inner - row_mean(inner) - zhat * row_mean(inner * zhat)) * rstd
        grad_two[rows, :] = grad_in
        low = grad_in.astype(bf16)
        grad_down[rows, :] = low
        gain, shift, bias = carry
        return gain + fold(grad * zhat), shift + fold(grad), bias + fold(low.astype(f32))

    zero = jnp.zeros((8, D), f32)
    gain, shift, bias = by_rows(tok, norm_two, (zero, zero, zero))
    put_vec(GAIN_TWO, column_sum(gain))
    put_vec(SHIFT_TWO, column_sum(shift))
    put_vec(BIAS_DOWN, column_sum(bias))
    grad_down_came = share_half(grad_down, narrow_grad)
    keys_turned[...] = transposed(keys_values[:, :D])

    here = {"f": z // 2, "n": z % 2, "x": x, "y": y}
    across = {"f": along[1], "n": along[0], "x": beside, "y": beyond}

    class Chain:
        def __init__(self, index):
            matrix, start, rows, order = CHUNKS[index]
            self.index, self.order, self.stage = index, order, 0
            self.rows = pl.ds(start, rows)
            self.own = part.at[matrix]
            self.came = [ref.at[matrix] for ref in (came_one, came_two, came_three, came_four)]
            self.final = sums.at[matrix]

        def cells(self, free, flipped=None):
            return tuple(
                slice(None) if name in free else 1 - here[name] if name == flipped else here[name]
                for name in "fnxy"
            ) + (self.rows,)

        def send(self, source, target, other):
            sems = (send_sem.at[self.index, self.stage], recv_sem.at[self.index, self.stage])
            self.copy = remote(source, target, *sems, other)

        def advance(self):
            stage, order = self.stage, self.order
            if stage:
                self.copy.wait_recv()
            if 1 <= stage <= 4:
                free = order[stage:]
                for choice in itertools.product((0, 1), repeat=len(free)):
                    taken = dict(zip(sorted(free, key="fnxy".index), choice))
                    at = tuple(taken.get(name, here[name]) for name in "fnxy") + (self.rows,)
                    value = self.own[at] + self.came[stage - 1][choice + (self.rows,)]
                    if stage == 4:
                        self.final[core, y, self.rows] = value
                    else:
                        self.own[at] = value
            if stage < 4:
                name = order[stage]
                source = self.own.at[self.cells(order[stage + 1 :], name)]
                target = self.came[stage].at[(slice(None),) * (3 - stage) + (self.rows,)]
                self.send(source, target, across[name])
            elif stage == 4:
                block = self.final.at[core, y, self.rows]
                self.send(block, block, beyond)
            elif stage == 5:
                block = self.final.at[core, :, self.rows]
                self.send(block, block, partner)
            self.stage += 1

    chains = [Chain(index) for index in range(len(CHUNKS))]
    plan = iter(CHUNK_PLAN)

    def pump():
        for index in next(plan):
            chains[index].advance()

    def feed_forward(matrix, narrow, wide):
        left = transposed(narrow[...])

        def block(index, carry):
            cols = pl.ds(pl.multiple_of(index * UNIT, UNIT), UNIT)
            value = dot(left, wide[:, cols], 1, 0).astype(bf16)
            for side in range(2):
                part[matrix, index // 4, index // 2 % 2, index % 2, side] = value[
                    side * SIDE : (side + 1) * SIDE
                ]
            return carry

        lax.fori_loop(0, 8, block, 0)

    def projections(matrix, turned, narrow, width, offset, between=None):
        for tile in range(turned.shape[0] // UNIT):
            if between and tile % 2 == 0:
                between()
            value = dot(turned[tile * UNIT : (tile + 1) * UNIT, :], narrow[...], 1, 0).astype(bf16)
            for start in range(0, UNIT, PIECE):
                block, row = divmod(tile * UNIT + start, width)
                side, row = divmod(offset + row, SIDE)
                cell = (matrix, block // 4, block // 2 % 2, block % 2, side)
                part[cell + (pl.ds(row, PIECE),)] = value[start : start + PIECE]

    grad_down_came.wait_recv()
    active_came.wait_recv()
    feed_forward(0, narrow_grad, active)

    for tile in range(FF // D):
        pump()
        cols = slice(tile * D, (tile + 1) * D)
        work[...] = dot(grad_down[...], down_w[cols, :], 1, 1)

        def gelu_back(rows, carry):
            low = (work[rows, :] * slope[rows, cols]).astype(bf16)
            grad_up[rows, cols] = low
            return carry + fold(low.astype(f32))

        put_vec(BIAS_UP + cols.start, column_sum(by_rows(tok, gelu_back, zero)))
    grad_up_came = to_partner(grad_up.at[own_rows], grad_up.at[far_rows])
    pump()
    normed_came.wait_recv()
    grad_up_came.wait_recv()
    feed_forward(1, narrow_normed, grad_up)
    pump()

    work[...] = dot(grad_up[own_rows, :], up_w[...], 1, 1)

    def norm_one_back(rows, carry):
        grad = grad_two[rows, :] + work[rows, :]
        zhat = zhat_one[rows, :]
        inner = grad * span(GAIN_ONE)
        grad_in = inner - row_mean(inner) - zhat * row_mean(inner * zhat)
        grad_in = grad_in * rstd_one[rows, 0:1]
        grad_one[rows, :] = grad_in
        low = grad_in.astype(bf16)
        grad_attn[rows, :] = low
        gain, shift, bias = carry
        return gain + fold(grad * zhat), shift + fold(grad), bias + fold(low.astype(f32))

    gain, shift, bias = by_rows(tok, norm_one_back, (zero, zero, zero))
    put_vec(GAIN_ONE, column_sum(gain))
    put_vec(SHIFT_ONE, column_sum(shift))
    put_vec(BIAS_OUT, column_sum(bias))
    grad_heads[...] = dot(grad_attn[...], out_w[...], 1, 1).astype(bf16)
    heads_turned[...] = dot(out_w[...], grad_attn[...], 1, 1).astype(bf16)

    half_lanes = LANES // 2
    pair_came = []
    for pair in range(HEADS // 2):
        pump()
        cols = slice(pair * LANES, (pair + 1) * LANES)
        values = keys_values[:, D + cols.start : D + cols.stop]
        for side, mask in enumerate(masks):
            rows = slice(cols.start + side * half_lanes, cols.start + (side + 1) * half_lanes)
            chance = prob[2 * pair + side].astype(f32)
            grad_chance = dot(grad_heads[:, cols] * mask, values, 1, 1)
            mean = jnp.sum(chance * grad_chance, axis=-1, keepdims=True)
            grad_score = (chance * (grad_chance - mean)).astype(bf16)
            values_grad = dot(heads_turned[rows, :], prob[2 * pair + side], 1, 0).astype(bf16)
            keys_grad = (dot(query_turned[rows, :], grad_score, 1, 0) * scale).astype(bf16)
            query_grad = (dot(keys_turned[rows, :], grad_score, 1, 1) * scale).astype(bf16)
            blocks = (
                query_grad,
                keys_grad[:, :tok],
                values_grad[:, :tok],
                keys_grad[:, tok:],
                values_grad[:, tok:],
            )
            for index, value in enumerate(blocks):
                start = index * LANES + side * half_lanes
                exchanged[0, pair, start : start + half_lanes, :] = value
        pair_came.append(to_partner(exchanged.at[0, pair], exchanged.at[1, pair]))
    pump()
    attn_turned[:, own_lanes] = transposed(grad_attn[...])
    grad_attn_came = to_partner(attn_turned.at[:, own_lanes], attn_turned.at[:, far_lanes])

    for pair, copy in enumerate(pair_came):
        copy.wait_recv()
        for who, lanes in enumerate((own_lanes, far_lanes)):
            start = pair * LANES
            mine, theirs = exchanged.at[who, pair], exchanged.at[1 - who, pair]
            qkv_turned[start : start + LANES, lanes] = mine[:LANES]
            for index in (1, 2):
                rows = slice(index * LANES, (index + 1) * LANES)
                sent = slice((index + 2) * LANES, (index + 3) * LANES)
                value = mine[rows].astype(f32) + theirs[sent].astype(f32)
                start = index * D + pair * LANES
                qkv_turned[start : start + LANES, lanes] = value.astype(bf16)
    pump()
    tokens_came.wait_recv()
    projections(2, qkv_turned, narrow_tokens, 3 * D // 8, 0, pump)
    attended_came.wait_recv()
    grad_attn_came.wait_recv()
    projections(2, attn_turned, narrow_attended, D // 8, 3 * D // 8)
    pump()

    ones = jnp.ones((8, tok), bf16)
    for start, rows in ((BIAS_QUERY, slice(0, D)), (BIAS_VALUE, slice(2 * D, 3 * D))):
        put_vec(start, dot(ones, qkv_turned[rows, own_lanes], 1, 1)[0:1])
    vec_came = to_partner(vec, vec_core)
    value = dot(qkv_w[...], qkv_turned[:, own_lanes], 1, 0)
    input_grad[...] = grad_one[...] + value.T

    vec_slots = [(send_sem.at[len(CHUNKS), i], recv_sem.at[len(CHUNKS), i]) for i in range(5)]

    def vec_steps():
        vec_came.wait_recv()
        vec_core[...] = vec[...] + vec_core[...]
        copy = remote(vec_core, vec_y, *vec_slots[0], beyond)
        yield
        copy.wait_recv()
        for i in range(4):
            vec_x[0, i] = vec_core[2 * i + x] + vec_y[2 * i + x]
            vec_x[1, i] = vec_core[2 * i + 1 - x] + vec_y[2 * i + 1 - x]
        copy = remote(vec_x.at[1], vec_x.at[2], *vec_slots[1], beside)
        yield
        copy.wait_recv()
        vec_x[0] = vec_x[0] + vec_x[2]
        copies = [
            remote(
                vec_x.at[0, flip_z(z, step)],
                vec_z.at[step - 1],
                *vec_slots[1 + step],
                along[step - 1],
            )
            for step in (1, 2, 3)
        ]
        yield
        total = vec_x[0, z]
        for step, copy in enumerate(copies):
            copy.wait_recv()
            total = total + vec_z[step]
        vec_sum[...] = total
        yield

    steps = vec_steps()
    for turn, index in enumerate(next(plan)):
        chains[index].advance()
        if turn % 10 == 9 and turn < 40:
            next(steps)
    for copy in started:
        copy.wait_send()


def layer(row_class, lengths, tokens, cotangent, vectors, qkv_w, out_w, up_w, down_w):
    tok = tokens.shape[0]
    side = (SIDE, UNIT)

    def low(*dims):
        return pltpu.VMEM(dims, bf16)

    def wide(*dims):
        return pltpu.VMEM(dims, f32)

    return pl.pallas_call(
        layer_kernel,
        out_shape=(
            jax.ShapeDtypeStruct((tok, D), f32),
            jax.ShapeDtypeStruct((tok, D), f32),
            jax.ShapeDtypeStruct((3, 2, 2) + side, bf16),
            jax.ShapeDtypeStruct((16, LANES), f32),
        ),
        in_specs=[SMEM, SMEM, VMEM, VMEM, VMEM] + [ANY] * 4,
        out_specs=(VMEM,) * 4,
        scratch_shapes=[
            low(D, 3 * D),
            low(D, D),
            low(D, FF),
            low(FF, D),
            low(tok, D),
            low(D, tok),
            low(2 * tok, 2 * D),
            low(D, 2 * tok),
            low(HEADS, tok, 2 * tok),
            low(tok, D),
            low(tok, D),
            low(tok, D),
            low(tok, D),
            low(2 * tok, HALF),
            low(2 * tok, HALF),
            low(2 * tok, HALF),
            low(2 * tok, HALF),
            low(2 * tok, FF),
            low(2 * tok, FF),
            low(D, 2 * tok),
            low(3 * D, 2 * tok),
            low(2, HEADS // 2, 5 * LANES, tok),
            low(tok, D),
            low(D, tok),
            wide(tok, FF),
            wide(tok, D),
            wide(tok, D),
            wide(tok, LANES),
            wide(tok, D),
            wide(tok, D),
            wide(8, 16, LANES),
            wide(8, 16, LANES),
            wide(8, 16, LANES),
            wide(3, 4, 16, LANES),
            wide(3, 16, LANES),
            low(3, 2, 2, 2, 2, *side),
            low(3, 2, 2, 2, *side),
            low(3, 2, 2, *side),
            low(3, 2, *side),
            low(3, *side),
            pltpu.SemaphoreType.DMA((4,)),
            pltpu.SemaphoreType.DMA((16,)),
            pltpu.SemaphoreType.DMA((16,)),
            pltpu.SemaphoreType.DMA((len(CHUNKS) + 1, 6)),
            pltpu.SemaphoreType.DMA((len(CHUNKS) + 1, 6)),
        ],
        compiler_params=pltpu.CompilerParams(
            vmem_limit_bytes=63 * MIB, collective_id=0, has_side_effects=True
        ),
        name="layer",
    )(row_class, lengths, tokens, cotangent, vectors[None, :], qkv_w, out_w, up_w, down_w)


GRAM_AXES = ("far", "near", "x")
GRAM_GROUPS = (
    (1, "xnf"),
    (2, "xnf"),
    (2, "xnf"),
    (3, "xnf"),
    (3, "nxf"),
    (3, "fxn"),
    (3, "nxf"),
    (2, "xnf"),
    (1, "xnf"),
    (1, "xnf"),
)
GRAM_PLAN = (
    6, 0, 9, 2, 5, 4, 7, 3, 0, 9, 6, 8, 2, 0, 9, 1, 0, 7, 9, 8, 2, 6,
    0, 5, 4, 3, 1, 8, 2, 7, 0, 6, 9, 5, 4, 8, 0, 2, 7, 1, 8, 9, 6, 3,
    5, 4, 7, 1, 8, 6, 2, 9, 3, 5, 8, 1, 4, 7, 2, 3, 5, 1, 4, 6, 7, 3,
    1, 5, 3, 4,
)


def muon_kernel(
    sums,
    qkv_hbm,
    out_hbm,
    up_hbm,
    down_hbm,
    factors,
    own_sum,
    qkv_old,
    out_old,
    old,
    moment,
    out,
    part,
    came_one,
    came_two,
    came_three,
    high,
    low,
    load_sem,
    send_sem,
    recv_sem,
    share_send,
    share_recv,
    *ortho,
):
    z, x, y, core = position()
    here = {"far": z // 2, "near": z % 2, "x": x}
    others = {
        "far": device(flip_z(z, 2), x, y, core),
        "near": device(flip_z(z, 1), x, y, core),
        "x": device(z, 1 - x, y, core),
    }
    beyond = device(z, x, 1 - y, core)
    partner = device(z, x, y, 1 - core)
    own = 2 * y + core
    all_here = greet(list(others.values()) + [beyond, partner])

    def load_two(source, target, matrix):
        loads = [
            pltpu.make_async_copy(source, target, load_sem.at[0]),
            pltpu.make_async_copy(sums.at[matrix], own_sum, load_sem.at[1]),
        ]
        for load in loads:
            load.start()
        for load in loads:
            load.wait()

    def from_turned(source, target, skip):
        load_two(source, target, 2)
        rows = target.shape[0]
        moment[...] = jnp.zeros_like(moment)
        for half in range(2):
            cols = slice(half * HALF, (half + 1) * HALF)
            start = half * UNIT + skip
            value = own_sum[start : start + rows, :].astype(f32)
            moment[cols, skip : skip + rows] = (muon_keep * target[:, cols] + value).T

    @pl.when(own == 0)
    def _():
        from_turned(qkv_hbm, qkv_old, 0)

    @pl.when(own == 1)
    def _():
        from_turned(out_hbm, out_old, qkv_old.shape[0])

    @pl.when(own == 2)
    def _():
        load_two(up_hbm, old, 1)
        moment[...] = muon_keep * old[...] + own_sum[...].astype(f32)

    @pl.when(own == 3)
    def _():
        load_two(down_hbm, old, 0)
        moment[...] = muon_keep * old[...] + own_sum[...].astype(f32)

    all_here()
    blocks = sub_blocks(moment.shape[0])
    starts = [sum(count for count, _ in GRAM_GROUPS[:group]) for group in range(len(GRAM_GROUPS))]
    high[...] = moment[...].astype(bf16)
    low[...] = (moment[...] - high[...].astype(f32)).astype(bf16)
    started = []

    def product(index):
        i, j = blocks[index]
        left, right = pl.ds(i * SUB, SUB), pl.ds(j * SUB, SUB)
        total = dot(high[left, :], high[right, :], 1, 1)
        total = total + dot(high[left, :], low[right, :], 1, 1)
        total = total + dot(low[left, :], high[right, :], 1, 1)
        rows = SUB // 8
        for owner in range(8):
            cell = (owner // 4, owner // 2 % 2, owner % 2)
            part[cell + (index,)] = total[
                owner * rows : (owner + 1) * rows
            ]

    def send(source, target, group, slot, axis):
        copy = pltpu.make_async_remote_copy(
            src_ref=source,
            dst_ref=target,
            send_sem=send_sem.at[group, slot],
            recv_sem=recv_sem.at[group, slot],
            device_id=others[axis],
            device_id_type=MESH,
        )
        copy.start()
        started.append(copy)
        return copy

    def cells(fixed, flipped=None):
        return tuple(
            1 - here[name] if name == flipped else here[name] if name in fixed else slice(None)
            for name in GRAM_AXES
        )

    class Walk:
        def __init__(self, group):
            count, order = GRAM_GROUPS[group]
            self.group, self.stage = group, 0
            self.order = [GRAM_AXES["fnx".index(letter)] for letter in order]
            self.mine = (pl.ds(starts[group], count),)
            self.came = [
                ref.at[(slice(None),) * (2 - stage) + self.mine]
                for stage, ref in enumerate((came_one, came_two, came_three))
            ]

        def advance(self):
            stage, order = self.stage, self.order
            mine = self.mine
            if stage:
                self.copy.wait_recv()
            if 1 <= stage <= 3:
                kept = cells(order[:stage]) + mine
                total = part[kept] + self.came[stage - 1][...]
                if stage == 3:
                    out[kept] = total
                else:
                    part[kept] = total
            if stage < 3:
                source = part.at[cells(order[:stage], order[stage]) + mine]
                self.copy = send(source, self.came[stage], self.group, stage, order[stage])
            elif stage < 6:
                block = out.at[cells(order[: 6 - stage]) + mine]
                self.copy = send(block, block, self.group, stage, order[5 - stage])
            self.stage += 1

    walks = [Walk(group) for group in range(len(GRAM_GROUPS))]
    for group in GRAM_PLAN:
        if walks[group].stage == 0:
            for index in range(starts[group], starts[group] + GRAM_GROUPS[group][0]):
                product(index)
        walks[group].advance()

    e = ortho[0]
    for index, (i, j) in enumerate(blocks):
        value = out[:, :, :, index].reshape(SUB, SUB)
        e[i * SUB : (i + 1) * SUB, j * SUB : (j + 1) * SUB] = value
        if i != j:
            e[j * SUB : (j + 1) * SUB, i * SUB : (i + 1) * SUB] = value.T

    across, beside = [], []

    def share(slot, rows, kind, other):
        block = factors.at[slot, rows]
        index = rows.start // TILE
        copy = pltpu.make_async_remote_copy(
            src_ref=block,
            dst_ref=block,
            send_sem=share_send.at[index, kind],
            recv_sem=share_recv.at[index, kind],
            device_id=other,
            device_id_type=MESH,
        )
        copy.start()
        started.append(copy)
        return copy

    def emit(rows, value):
        factors[own, rows, :] = value
        across.append((rows, share(own, rows, 0, beyond)))
        beside.append(share(own, rows, 1, partner))

    newton_schulz(e, moment, *ortho, emit)
    for rows, copy in across:
        copy.wait_recv()
        beside.append(share(2 * (1 - y) + core, rows, 2, partner))
    for copy in beside:
        copy.wait_recv()
    for copy in started:
        copy.wait_send()


def muon_factors(sums, *olds):
    size, cols = olds[2].shape
    count = len(sub_blocks(size))
    groups = len(GRAM_GROUPS)
    rows = (SUB // 8, SUB)

    def wide(*dims):
        return pltpu.VMEM(dims, f32)

    return pl.pallas_call(
        muon_kernel,
        out_shape=jax.ShapeDtypeStruct((4, size, cols), bf16),
        in_specs=[ANY] * 5,
        out_specs=VMEM,
        scratch_shapes=[
            pltpu.VMEM((size, cols), bf16),
            wide(*olds[0].shape),
            wide(*olds[1].shape),
            wide(size, cols),
            wide(size, cols),
            wide(2, 2, 2, count, *rows),
            wide(2, 2, 2, count, *rows),
            wide(2, 2, count, *rows),
            wide(2, count, *rows),
            wide(count, *rows),
            pltpu.VMEM((size, cols), bf16),
            pltpu.VMEM((size, cols), bf16),
            pltpu.SemaphoreType.DMA((2,)),
            pltpu.SemaphoreType.DMA((groups, 6)),
            pltpu.SemaphoreType.DMA((groups, 6)),
            pltpu.SemaphoreType.DMA((size // TILE, 3)),
            pltpu.SemaphoreType.DMA((size // TILE, 3)),
        ]
        + ortho_scratch(size, cols),
        compiler_params=pltpu.CompilerParams(
            vmem_limit_bytes=58 * MIB, collective_id=1, has_side_effects=True
        ),
        name="muon_factors",
    )(sums, *olds)


def window(start, width, total):
    size = -(-(width + 96) // LANES) * LANES
    first = jnp.minimum(start // LANES * LANES, total - size)
    return pl.ds(pl.multiple_of(first, LANES), size), start - first


def finish_kernel(
    factors_hbm,
    sums_hbm,
    qkv_hbm,
    out_hbm,
    up_hbm,
    down_hbm,
    qkv_old_hbm,
    out_old_hbm,
    up_old_hbm,
    down_old_hbm,
    mixed_hbm,
    grad_hbm,
    mixed_out,
    grad_out,
    qkv_moment_out,
    out_moment_out,
    up_moment_out,
    down_moment_out,
    qkv_out,
    out_out,
    up_out,
    down_out,
    factors,
    sums,
    qkv_w,
    out_w,
    up_w,
    down_w,
    qkv_moment,
    out_moment,
    up_moment,
    down_moment,
    qkv_new,
    out_new,
    up_new,
    down_new,
    turned,
    load_sem,
    store_sem,
):
    shrink = 1.0 - muon_rate * muon_decay
    dp_id = lax.axis_index("dp")
    qkv_cols, out_cols = qkv_new.shape[0], out_new.shape[0]
    qkv_lanes, qkv_skip = window(dp_id * qkv_cols, qkv_cols, 3 * D)
    out_lanes, out_skip = window(dp_id * out_cols, out_cols, D)
    block = pl.ds(pl.multiple_of(dp_id * UNIT, UNIT), UNIT)
    pairs = {
        "sums": (sums_hbm, sums),
        "up_moment": (up_old_hbm, up_moment),
        "down_moment": (down_old_hbm, down_moment),
        "factors": (factors_hbm, factors),
        "up": (up_hbm.at[:, block], up_w),
        "down": (down_hbm.at[block], down_w),
        "qkv_moment": (qkv_old_hbm, qkv_moment),
        "out_moment": (out_old_hbm, out_moment),
        "qkv": (qkv_hbm.at[:, qkv_lanes], qkv_w),
        "out": (out_hbm.at[:, out_lanes], out_w),
    }
    loads = {
        name: pltpu.make_async_copy(source, target, load_sem.at[index])
        for index, (name, (source, target)) in enumerate(pairs.items())
    }
    for load in loads.values():
        load.start()
    stores = []

    def store(source, target):
        stores.append(pltpu.make_async_copy(source, target, store_sem.at[len(stores)]))
        stores[-1].start()

    store(mixed_hbm, mixed_out)
    store(grad_hbm, grad_out)

    def step(index, rate):
        return muon_rate * rate * factors[index].astype(f32)

    loads["sums"].wait()
    for index, name, target, out in (
        (1, "up_moment", up_moment, up_moment_out),
        (0, "down_moment", down_moment, down_moment_out),
    ):
        loads[name].wait()
        target[...] = muon_keep * target[...] + sums[index].astype(f32)
        store(target, out)
    loads["qkv_moment"].wait()
    loads["out_moment"].wait()
    for half in range(2):
        cols = slice(half * HALF, (half + 1) * HALF)
        value = sums[2, cols].astype(f32)
        qkv_moment[:, cols] = muon_keep * qkv_moment[:, cols] + value[:qkv_cols]
        out_moment[:, cols] = muon_keep * out_moment[:, cols] + value[qkv_cols:]
    store(qkv_moment, qkv_moment_out)
    store(out_moment, out_moment_out)
    loads["factors"].wait()
    loads["up"].wait()
    up_new[...] = up_w[...].astype(f32) * shrink - step(2, math.sqrt(max(1.0, FF / D)))
    store(up_new, up_out)
    loads["down"].wait()
    down_new[...] = down_w[...].astype(f32) * shrink - step(3, 1.0).T
    store(down_new, down_out)
    loads["qkv"].wait()
    turned[...] = qkv_w[...].astype(f32).T
    rows = pl.ds(pl.multiple_of(qkv_skip, 32), qkv_cols)
    qkv_new[...] = turned[rows, :] * shrink - step(0, math.sqrt(3.0)).T[:qkv_cols]
    store(qkv_new, qkv_out)
    loads["out"].wait()
    turned[: out_w.shape[1], :] = out_w[...].astype(f32).T
    rows = pl.ds(pl.multiple_of(out_skip, 32), out_cols)
    out_new[...] = turned[rows, :] * shrink - step(1, 1.0).T[qkv_cols:]
    store(out_new, out_out)
    for copy in stores:
        copy.wait()


def finish(factors, sums, weights, olds, mixed, input_grad):
    shapes = [old.shape for old in olds]
    news = shapes[:3] + [shapes[3][::-1]]

    def wide(shape):
        return pltpu.VMEM(shape, f32)

    return pl.pallas_call(
        finish_kernel,
        out_shape=tuple(
            jax.ShapeDtypeStruct(shape, f32)
            for shape in [mixed.shape, input_grad.shape] + shapes + news
        ),
        in_specs=[ANY] * 12,
        out_specs=(ANY,) * 10,
        scratch_shapes=[
            pltpu.VMEM(factors.shape, bf16),
            pltpu.VMEM(sums.shape, bf16),
            pltpu.VMEM((D, 384), bf16),
            pltpu.VMEM((D, 256), bf16),
            pltpu.VMEM((D, UNIT), bf16),
            pltpu.VMEM((UNIT, D), bf16),
        ]
        + [wide(shape) for shape in shapes + news]
        + [
            wide((384, D)),
            pltpu.SemaphoreType.DMA((10,)),
            pltpu.SemaphoreType.DMA((10,)),
        ],
        compiler_params=pltpu.CompilerParams(vmem_limit_bytes=48 * MIB),
        name="finish",
    )(factors, sums, *weights, *olds, mixed, input_grad)


def swap(value, axis, bit):
    size = lax.axis_size(axis)
    return lax.ppermute(value, axis, [(i, i ^ bit) for i in range(size)])


def scatter_head(value, bit, position):
    half = value.shape[1] // 2
    mine = lax.dynamic_slice_in_dim(value, position * half, half, 1)
    other = lax.dynamic_slice_in_dim(value, (1 - position) * half, half, 1)
    return (mine.astype(f32) + swap(other, "head", bit).astype(f32)).astype(bf16)


def scatter_dp_pair(value, position):
    paired = value.reshape((value.shape[0] // 2, 2) + value.shape[1:])
    mine = lax.dynamic_index_in_dim(paired, position, 1, False)
    other = lax.dynamic_index_in_dim(paired, 1 - position, 1, False)
    return (mine.astype(f32) + swap(other, "dp", 1).astype(f32)).astype(bf16)


def scatter_dp_rest(value, place):
    ranks = value.shape[0]
    total = lax.dynamic_index_in_dim(value, place, 0, False).astype(f32)
    for step in range(1, ranks):
        sent = lax.dynamic_index_in_dim(value, place ^ step, 0, False)
        total = total + swap(sent, "dp", 2 * step).astype(f32)
    return total


def local(
    tokens,
    cotangent,
    qkv_weight,
    out_weight,
    up_weight,
    down_weight,
    vectors,
    qkv_moment,
    out_moment,
    up_moment,
    down_moment,
    adam_first,
    adam_second,
    bucket_class,
    row_lengths,
):
    n_dp = lax.axis_size("dp")
    n_head = lax.axis_size("head")
    dp_id = lax.axis_index("dp")
    head_id = lax.axis_index("head")
    core, side = head_id % 2, head_id // 2
    tok, width = tokens.shape
    hidden = up_weight.shape[1]
    half = width // 2
    qkv_cols, out_cols = qkv_moment.shape[1], out_moment.shape[1]
    shrink = 1.0 - muon_rate * muon_decay

    def weight_block(weight, cols, dim):
        return lax.dynamic_slice_in_dim(weight, dp_id * cols, cols, dim)

    block = head_id.astype(jnp.int32)[None]
    vec_len = vectors.shape[0] // n_dp
    if (n_dp, n_head, tok) == (8, 4, 256):
        mixed, input_grad, sums, vec = layer(
            bucket_class,
            row_lengths,
            tokens,
            cotangent,
            vectors,
            qkv_weight,
            out_weight,
            up_weight,
            down_weight,
        )
        grad_vec = vec[:VEC_BLOCK].reshape(vec_len)
        sums = sums.reshape(3, width, -1)
        olds = [qkv_moment.T, out_moment.T, up_moment, down_moment]
        mixed, input_grad, *results = finish(
            muon_factors(sums, *olds),
            sums,
            [qkv_weight, out_weight, up_weight, down_weight],
            olds,
            mixed,
            input_grad,
        )
        moments, new_weights = results[:4], results[4:]
        moments = [moments[0].T, moments[1].T, *moments[2:]]
        new_weights = [new_weights[0].T, new_weights[1].T, *new_weights[2:]]
    else:
        pieces = split_vectors(vectors, width, hidden)
        bias_query, bias_value, bias_out, gain_one, shift_one = pieces[:5]
        bias_up, bias_down, gain_two, shift_two = pieces[5:]
        bias_qkv = jnp.concatenate([bias_query, jnp.zeros_like(bias_query), bias_value])

        def column_half(value, which):
            return lax.dynamic_slice_in_dim(value, which * half, half, 1)

        qkv = (dot(tokens, qkv_weight, 1, 0) + bias_qkv).astype(bf16)
        other = swap(qkv[:, width:], "head", 1)
        attended = attend(block, bucket_class, row_lengths, qkv, other)
        attn_val = dot(attended, out_weight, 1, 0) + bias_out
        resid_one = tokens.astype(f32) + attn_val
        centre = resid_one - jnp.mean(resid_one, axis=-1, keepdims=True)
        rstd_one = lax.rsqrt(jnp.mean(centre * centre, axis=-1, keepdims=True) + norm_eps)
        zhat_one = centre * rstd_one
        normed_one = zhat_one * gain_one + shift_one
        normed_low = normed_one.astype(bf16)
        up_val = dot(normed_low, up_weight, 1, 0) + bias_up
        phi_cum = 0.5 * (1.0 + lax.erf(up_val * (0.5**0.5)))
        active_low = (up_val * phi_cum).astype(bf16)
        slope = phi_cum + up_val * jnp.exp(-0.5 * up_val * up_val) * (1.0 / math.sqrt(2.0 * math.pi))
        down_val = dot(active_low, down_weight, 1, 0) + bias_down
        resid_two = normed_one + down_val
        centre = resid_two - jnp.mean(resid_two, axis=-1, keepdims=True)
        rstd_two = lax.rsqrt(jnp.mean(centre * centre, axis=-1, keepdims=True) + norm_eps)
        zhat_two = centre * rstd_two
        mixed = zhat_two * gain_two + shift_two

        def norm_back(grad, gain, zhat, rstd):
            inner = grad * gain
            mean = jnp.mean(inner, axis=-1, keepdims=True)
            slant = jnp.mean(inner * zhat, axis=-1, keepdims=True)
            return (inner - mean - zhat * slant) * rstd, jnp.sum(grad * zhat, axis=0), jnp.sum(grad, axis=0)

        grad_two, grad_gain_two, grad_shift_two = norm_back(
            cotangent.astype(f32), gain_two, zhat_two, rstd_two
        )
        grad_down_low = grad_two.astype(bf16)
        grad_bias_down = jnp.sum(grad_down_low, axis=0, dtype=f32)

        x_id, z_id = dp_id % 2, dp_id // 2

        grad_up_low = (dot(grad_down_low, down_weight, 1, 1) * slope).astype(bf16)
        grad_bias_up = jnp.sum(grad_up_low, axis=0, dtype=f32)
        grad_normed = grad_two + dot(grad_up_low, up_weight, 1, 1)
        grad_one, grad_gain_one, grad_shift_one = norm_back(grad_normed, gain_one, zhat_one, rstd_one)
        grad_attn_low = grad_one.astype(bf16)
        grad_bias_out = jnp.sum(grad_attn_low, axis=0, dtype=f32)
        grad_heads = dot(grad_attn_low, out_weight, 1, 1).astype(bf16)
        grad_query, own, sent = attend_back(block, bucket_class, row_lengths, qkv, other, grad_heads)
        grad_kv = (own + swap(sent, "head", 1).astype(f32)).astype(bf16)
        grad_qkv = jnp.concatenate([grad_query, grad_kv], axis=1)
        grad_bias_qkv = jnp.sum(grad_qkv, axis=0, dtype=f32)
        input_grad = grad_one + dot(grad_qkv, qkv_weight, 1, 1)
        grad_vector = jnp.concatenate(
            [
                grad_bias_qkv[:width],
                grad_bias_qkv[2 * width :],
                grad_bias_out,
                grad_gain_one,
                grad_shift_one,
                grad_bias_up,
                grad_bias_down,
                grad_gain_two,
                grad_shift_two,
            ]
        )
        grad_vector = grad_vector + swap(grad_vector, "head", 1)
        wides = [active_low, grad_up_low, grad_attn_low, grad_qkv]
        narrows = [grad_down_low, normed_low, attended, tokens]

        def both_halves(value):
            return jnp.concatenate(
                [column_half(value, core), swap(column_half(value, 1 - core), "head", 1)], axis=0
            )

        def weight_grad(wide, narrow):
            wide = jnp.concatenate([wide, swap(wide, "head", 1)], axis=0)
            value = dot(wide, both_halves(narrow), 0, 0).astype(bf16)
            return value.reshape(n_dp, value.shape[0] // n_dp, half)

        def reduce_y_first(value):
            return scatter_dp_rest(scatter_dp_pair(scatter_head(value, 2, side), x_id), z_id)

        def reduce_x_first(value):
            return scatter_dp_rest(scatter_head(scatter_dp_pair(value, x_id), 2, side), z_id)

        def spread(value):
            value = value.astype(bf16)
            came = swap(value, "head", 2)
            value = jnp.concatenate(
                [jnp.where(side == 0, value, came), jnp.where(side == 0, came, value)], axis=0
            )
            came = swap(value, "head", 1)
            return jnp.concatenate(
                [jnp.where(core == 0, value, came), jnp.where(core == 0, came, value)], axis=1
            ).astype(f32)

        down_part, up_part, out_part, qkv_part = [
            weight_grad(wide, narrow) for wide, narrow in zip(wides, narrows)
        ]
        vec_rows = 16
        vec_part = grad_vector.reshape(n_dp, vec_len)
        vec_part = jnp.pad(vec_part, ((0, 0), (0, vec_rows * width - vec_len)))
        vec_part = vec_part.reshape(n_dp, vec_rows, width)
        vec_part = lax.dynamic_slice_in_dim(vec_part, core * half, half, 2).astype(bf16)
        down_new = spread(reduce_x_first(down_part))
        up_new = spread(reduce_y_first(up_part))
        tail_new = spread(
            reduce_y_first(jnp.concatenate([qkv_part, out_part, vec_part], axis=1))
        )
        grads = [
            tail_new[:qkv_cols].T,
            tail_new[qkv_cols : qkv_cols + out_cols].T,
            up_new.T,
            down_new.T,
        ]
        grad_vec = tail_new[qkv_cols + out_cols :].reshape(-1)[:vec_len]
        moments = [
            muon_keep * old + grad
            for old, grad in zip([qkv_moment, out_moment, up_moment, down_moment], grads)
        ]
        most = max(m.shape[1] for m in moments)
        padded = [jnp.pad(m, ((0, 0), (0, most - m.shape[1]))) for m in moments]
        chosen = padded[-1]
        for index in range(len(padded) - 2, -1, -1):
            chosen = jnp.where(head_id == index, padded[index], chosen)
        gram_mat = lax.dot_general(
            chosen, chosen, (((1,), (1,)), ((), ())), precision=lax.Precision.HIGH
        )
        own_factor = orthogonalize(lax.psum(gram_mat, "dp"), chosen)
        across = swap(own_factor, "head", 2)
        low_pair = jnp.where(side == 0, own_factor, across)
        high_pair = jnp.where(side == 0, across, own_factor)
        near_low = swap(low_pair, "head", 1)
        near_high = swap(high_pair, "head", 1)
        factors = [
            jnp.where(core == 0, low_pair, near_low),
            jnp.where(core == 0, near_low, low_pair),
            jnp.where(core == 0, high_pair, near_high),
            jnp.where(core == 0, near_high, high_pair),
        ]
        factors = [o[:, : m.shape[1]].astype(f32) for o, m in zip(factors, moments)]
        factors[3] = factors[3].T
        old_weights = [
            weight_block(qkv_weight, qkv_cols, 1),
            weight_block(out_weight, out_cols, 1),
            weight_block(up_weight, up_moment.shape[1], 1),
            weight_block(down_weight, down_moment.shape[1], 0),
        ]

        rates = (math.sqrt(3.0), 1.0, math.sqrt(max(1.0, hidden / width)), 1.0)
        new_weights = [
            old.astype(f32) * shrink - muon_rate * rate * factor
            for old, rate, factor in zip(old_weights, rates, factors)
        ]

    vec_old = lax.dynamic_slice_in_dim(vectors, dp_id * vec_len, vec_len, 0)
    vec_first = beta_first * adam_first + (1.0 - beta_first) * grad_vec
    vec_second = beta_second * adam_second + (1.0 - beta_second) * grad_vec * grad_vec
    first_hat = vec_first / (1.0 - beta_first**STEP)
    second_hat = vec_second / (1.0 - beta_second**STEP)
    vec_new = vec_old - adam_rate * first_hat / (jnp.sqrt(second_hat) + adam_eps)
    return (mixed, input_grad, *moments, *new_weights, vec_first, vec_second, vec_new)


def solution(mesh):
    tokens_spec = P(("dp", "head"), None)
    block_spec = P(None, "dp")
    return jax.shard_map(
        local,
        mesh=mesh,
        in_specs=(
            tokens_spec,
            tokens_spec,
            P(),
            P(),
            P(),
            P(),
            P(),
            block_spec,
            block_spec,
            block_spec,
            block_spec,
            P("dp"),
            P("dp"),
            P("dp"),
            P("dp", None),
        ),
        out_specs=(
            tokens_spec,
            tokens_spec,
            block_spec,
            block_spec,
            block_spec,
            block_spec,
            block_spec,
            block_spec,
            block_spec,
            P("dp", None),
            P("dp"),
            P("dp"),
            P("dp"),
        ),
        check_vma=False,
    )
```

```python
import functools
import itertools
import math

import jax
import jax.numpy as jnp
from jax import lax
from jax.experimental import pallas as pl
from jax.experimental.pallas import tpu as pltpu
from jax.sharding import PartitionSpec as P

D = 768
HEADS = 12
HEAD_DIM = 64
FF = 3072
BASE_LEN = 128
NS_STEPS = 5
STEP = 5
MAX_LEN = 512

f32 = jnp.float32
bf16 = jnp.bfloat16

norm_eps = 1e-12
masked_score = -1000000000.0
quintic_a = 3.4445
quintic_b = -4.775
quintic_c = 2.0315
muon_rate = 1.0
muon_decay = 0.01
muon_keep = 0.5
adam_rate = 0.2
beta_first = 0.9
beta_second = 0.999
adam_eps = 1e-08
MIB = 1024 * 1024


def dot(left, right, left_dim, right_dim):
    return lax.dot_general(
        left, right, (((left_dim,), (right_dim,)), ((), ())), preferred_element_type=f32
    )


def split_vectors(vectors, width, hidden):
    lengths_list = [width] * 5 + [hidden] + [width] * 3
    pieces = []
    offset = 0
    for length in lengths_list:
        pieces.append(vectors[offset : offset + length])
        offset = offset + length
    return pieces


def allowed_mask(class_ref, length_ref, block, tok):
    shift = class_ref[0] + int(math.log2(BASE_LEN))
    query_place = block * tok + lax.broadcasted_iota(jnp.int32, (tok, 1), 0)
    lane = lax.broadcasted_iota(jnp.int32, (1, 2 * tok), 1)
    own = lane < tok
    key_place = jnp.where(own, block * tok + lane, (block ^ 1) * tok + lane - tok)
    key_row = lax.shift_right_logical(key_place, jnp.broadcast_to(shift, key_place.shape))
    offset = key_place - lax.shift_left(key_row, jnp.broadcast_to(shift, key_place.shape))
    row_len = jnp.zeros_like(key_row)
    for slot in range(length_ref.shape[1]):
        row_len = jnp.where(key_row == slot, length_ref[0, slot], row_len)
    key_row = jnp.where(offset < row_len, key_row, -1)
    query_row = lax.shift_right_logical(query_place, jnp.broadcast_to(shift, query_place.shape))
    return query_row == key_row


def half_masks():
    lane = lax.broadcasted_iota(jnp.int32, (1, 2 * HEAD_DIM), 1)
    first = (lane < HEAD_DIM).astype(f32)
    return (first.astype(bf16), (1.0 - first).astype(bf16)), lane < HEAD_DIM


def head_prob(query, keys, allowed):
    score = jnp.where(allowed, dot(query, keys, 1, 1) * HEAD_DIM ** (-0.5), masked_score)
    exponent = jnp.exp(score - jnp.max(score, axis=-1, keepdims=True))
    return exponent / jnp.sum(exponent, axis=-1, keepdims=True)


def attend_kernel(block_ref, class_ref, length_ref, qkv_ref, other_ref, out_ref):
    tok = qkv_ref.shape[0]
    allowed = allowed_mask(class_ref, length_ref, block_ref[0], tok)
    masks, first = half_masks()
    for pair in range(HEADS // 2):
        cols = pl.ds(pair * 2 * HEAD_DIM, 2 * HEAD_DIM)
        kcols = pl.ds(D + pair * 2 * HEAD_DIM, 2 * HEAD_DIM)
        vcols = pl.ds(2 * D + pair * 2 * HEAD_DIM, 2 * HEAD_DIM)
        query = qkv_ref[:, cols]
        keys = jnp.concatenate([qkv_ref[:, kcols], other_ref[:, cols]], axis=0)
        values = jnp.concatenate([qkv_ref[:, vcols], other_ref[:, kcols]], axis=0)
        outs = []
        for mask in masks:
            prob = head_prob(query * mask, keys, allowed)
            outs.append(dot(prob.astype(bf16), values, 1, 0))
        out_ref[:, cols] = jnp.where(first, outs[0], outs[1]).astype(bf16)


def attend_back_kernel(
    block_ref, class_ref, length_ref, qkv_ref, other_ref, grad_ref, dq_ref, own_ref, send_ref
):
    tok = qkv_ref.shape[0]
    allowed = allowed_mask(class_ref, length_ref, block_ref[0], tok)
    masks, first = half_masks()
    scale = HEAD_DIM ** (-0.5)
    for pair in range(HEADS // 2):
        cols = pl.ds(pair * 2 * HEAD_DIM, 2 * HEAD_DIM)
        kcols = pl.ds(D + pair * 2 * HEAD_DIM, 2 * HEAD_DIM)
        vcols = pl.ds(2 * D + pair * 2 * HEAD_DIM, 2 * HEAD_DIM)
        query = qkv_ref[:, cols]
        keys = jnp.concatenate([qkv_ref[:, kcols], other_ref[:, cols]], axis=0)
        values = jnp.concatenate([qkv_ref[:, vcols], other_ref[:, kcols]], axis=0)
        grad = grad_ref[:, cols]
        dqs, dk, dv = [], None, None
        for mask in masks:
            head_query = query * mask
            head_grad = grad * mask
            prob = head_prob(head_query, keys, allowed)
            part_v = dot(prob.astype(bf16), head_grad, 0, 0)
            dprob = dot(head_grad, values, 1, 1)
            dscore = prob * (dprob - jnp.sum(prob * dprob, axis=-1, keepdims=True))
            dscore = dscore.astype(bf16)
            dqs.append(dot(dscore, keys, 1, 0))
            part_k = dot(dscore, head_query, 0, 0)
            dk = part_k if dk is None else dk + part_k
            dv = part_v if dv is None else dv + part_v
        dk = dk * scale
        dq_ref[:, cols] = (jnp.where(first, dqs[0], dqs[1]) * scale).astype(bf16)
        own_ref[:, cols] = dk[:tok]
        own_ref[:, kcols] = dv[:tok]
        send_ref[:, cols] = dk[tok:].astype(bf16)
        send_ref[:, kcols] = dv[tok:].astype(bf16)


SMEM = pl.BlockSpec(memory_space=pltpu.SMEM)
VMEM = pl.BlockSpec(memory_space=pltpu.VMEM)
ANY = pl.BlockSpec(memory_space=pl.ANY)


def attend(block, row_class, lengths, qkv, other):
    tok = qkv.shape[0]
    return pl.pallas_call(
        attend_kernel,
        out_shape=jax.ShapeDtypeStruct((tok, D), bf16),
        in_specs=[SMEM, SMEM, SMEM, VMEM, VMEM],
        out_specs=VMEM,
        compiler_params=pltpu.CompilerParams(vmem_limit_bytes=32 * MIB),
        name="attend",
    )(block, row_class, lengths, qkv, other)


def attend_back(block, row_class, lengths, qkv, other, grad):
    tok = qkv.shape[0]
    return pl.pallas_call(
        attend_back_kernel,
        out_shape=(
            jax.ShapeDtypeStruct((tok, D), bf16),
            jax.ShapeDtypeStruct((tok, 2 * D), f32),
            jax.ShapeDtypeStruct((tok, 2 * D), bf16),
        ),
        in_specs=[SMEM, SMEM, SMEM, VMEM, VMEM, VMEM],
        out_specs=(VMEM, VMEM, VMEM),
        compiler_params=pltpu.CompilerParams(vmem_limit_bytes=32 * MIB),
        name="attend_back",
    )(block, row_class, lengths, qkv, other, grad)


CENTRES = (0.0, 0.0, 0.0, 0.8, 0.8)
TILE = 256
SUB = 128


def sub_blocks(size):
    count = size // SUB
    return [(i, j) for i in range(count) for j in range(i, count)]


def newton_schulz(gram, moment, e, f, g, eb, fb, gb, yy, y, emit):
    size = e.shape[0]
    tiles = [slice(i * TILE, (i + 1) * TILE) for i in range(size // TILE)]

    def unit(rows):
        row_id = rows.start + lax.broadcasted_iota(jnp.int32, (TILE, size), 0)
        col_id = lax.broadcasted_iota(jnp.int32, (TILE, size), 1)
        return (row_id == col_id).astype(f32)

    diagonal = jnp.zeros((TILE, size), f32)
    for rows in tiles:
        diagonal = diagonal + gram[rows, :] * unit(rows)
    trace = jnp.sum(jnp.sum(diagonal, axis=0, keepdims=True), axis=1, keepdims=True)
    factor = 1.0 / (jnp.sqrt(trace) + 1e-07)
    square_factor = factor * factor
    for rows in tiles:
        value = gram[rows, :] * square_factor
        e[rows, :] = value
        eb[rows, :] = value.astype(bf16)
        value = moment[rows, :] * factor
        y[rows, :] = value
        yy[0, rows, :] = value.astype(bf16)

    def one_step(centre, after, now, then, last=False):
        keep = quintic_a + quintic_b * centre + quintic_c * centre * centre
        linear = quintic_b + 2.0 * quintic_c * centre
        for rows in tiles:
            value = linear * e[rows, :] + quintic_c * dot(eb[rows, :], eb[...], 1, 0)
            fb[rows, :] = value.astype(bf16)
            if centre:
                f[rows, :] = value
        for rows in tiles:
            value = keep * y[rows, :] + dot(fb[rows, :], now[...], 1, 0)
            if last:
                emit(rows, value.astype(bf16))
            else:
                y[rows, :] = value
                then[rows, :] = value.astype(bf16)
        if last:
            return
        for rows in tiles:
            value = keep * e[rows, :] + dot(eb[rows, :], fb[...], 1, 0)
            if centre:
                value = value + centre * f[rows, :]
            g[rows, :] = value
            gb[rows, :] = value.astype(bf16)
        for rows in tiles:
            value = keep * g[rows, :] + dot(gb[rows, :], fb[...], 1, 0)
            if centre:
                value = value + (centre * keep) * f[rows, :]
            shift = centre * keep * keep - after
            if not isinstance(shift, float) or shift:
                value = value + shift * unit(rows)
            e[rows, :] = value
            eb[rows, :] = value.astype(bf16)

    plain = sum(centre == 0.0 for centre in CENTRES)

    def plain_step(step, carry):
        after = jnp.where(step == plain - 1, CENTRES[plain], 0.0)
        one_step(0.0, after, yy.at[step % 2], yy.at[(step + 1) % 2])
        return carry

    lax.fori_loop(0, plain, plain_step, 0)
    for step in range(plain, NS_STEPS):
        last = step + 1 == NS_STEPS
        after = 0.0 if last else CENTRES[step + 1]
        one_step(CENTRES[step], after, yy.at[step % 2], yy.at[(step + 1) % 2], last)


def ortho_kernel(gram, moment, out, *scratch):
    def emit(rows, value):
        out[rows, :] = value

    newton_schulz(gram, moment, *scratch, emit)


def ortho_scratch(size, cols):
    square, square_low = pltpu.VMEM((size, size), f32), pltpu.VMEM((size, size), bf16)
    wide_low = pltpu.VMEM((2, size, cols), bf16)
    return [square] * 3 + [square_low] * 3 + [wide_low, pltpu.VMEM((size, cols), f32)]


def orthogonalize(gram_mat, moment):
    size, cols = moment.shape
    return pl.pallas_call(
        ortho_kernel,
        out_shape=jax.ShapeDtypeStruct((size, cols), bf16),
        in_specs=[VMEM, VMEM],
        out_specs=VMEM,
        scratch_shapes=ortho_scratch(size, cols),
        compiler_params=pltpu.CompilerParams(vmem_limit_bytes=48 * MIB),
        name="ortho",
    )(gram_mat, moment)


MESH = pl.DeviceIdType.MESH
PIECE = 48
SIDE = 192
UNIT = 2 * SIDE
HALF = D // 2
LANES = 128
VEC_BLOCK = 9
ROWS = 16
CHUNKS = (
    (0, 0, 64, "nfyx"),
    (0, 64, 64, "xynf"),
    (0, 128, 64, "yxnf"),
    (1, 0, 64, "ynxf"),
    (1, 64, 64, "nxyf"),
    (1, 128, 64, "xynf"),
    (2, 0, 48, "xynf"),
    (2, 48, 48, "nxyf"),
    (2, 96, 48, "yxnf"),
    (2, 144, 32, "xynf"),
    (2, 176, 16, "xfyn"),
)
CHUNK_PLAN = (
    (0, 1, 2),
    (),
    (),
    (),
    (),
    (3, 5, 4),
    (0, 1, 2),
    (),
    (),
    (),
    (0, 1, 2, 4, 5, 3),
    (),
    (),
    (0, 7, 8, 10, 9, 6),
    (
        1, 4, 2, 5, 0, 1, 10, 4, 0, 2, 0, 1, 9, 1, 3, 2, 5, 10, 4, 8, 2, 6,
        10, 5, 9, 3, 4, 10, 7, 4, 8, 10, 5, 9, 3, 10, 5, 6, 9, 8, 7, 3, 9, 6,
        3, 9, 8, 7, 8, 6, 8, 7, 6, 7, 6, 7,
    ),
)
BIAS_QUERY, BIAS_VALUE, BIAS_OUT, GAIN_ONE, SHIFT_ONE, BIAS_UP = (i * D for i in range(6))
BIAS_DOWN, GAIN_TWO, SHIFT_TWO = (BIAS_UP + FF + i * D for i in range(3))


def position():
    dp_id, head_id = lax.axis_index("dp"), lax.axis_index("head")
    z, x = dp_id // 2, dp_id % 2
    y, core = head_id // 2, head_id % 2
    return z, x, y, core


def device(z, x, y, core):
    return (2 * z + x, 2 * y + core)


def flip_z(z, step):
    high, low = z // 2, z % 2
    high = 1 - high if step // 2 else high
    low = 1 - low if step % 2 else low
    return 2 * high + low


def greet(others):
    barrier = pltpu.get_barrier_semaphore()
    for other in others:
        pl.semaphore_signal(barrier, inc=1, device_id=other, device_id_type=MESH)
    return lambda: pl.semaphore_wait(barrier, len(others))


def by_rows(count, body, init=None, together=4):
    def step(index, carry):
        for part in range(together):
            start = (index * together + part) * ROWS
            carry = body(pl.ds(pl.multiple_of(start, ROWS), ROWS), carry)
        return carry

    return lax.fori_loop(0, count // (ROWS * together), step, init)


def row_mean(value):
    return jnp.sum(value, axis=-1, keepdims=True) * (1.0 / D)


def fold(value):
    return jnp.sum(value.reshape(value.shape[0] // 8, 8, value.shape[1]), axis=0)


def column_sum(value):
    return jnp.sum(value, axis=0, keepdims=True)


def normal_parts(value):
    size = jnp.abs(value)
    decay = jnp.exp(-0.5 * value * value)
    below = 1.0 + (0.3275911 * 0.5**0.5) * size
    t = pl.reciprocal(below, approx=True)
    t = t * (2.0 - below * t)
    series = t * (1.061405429 * 0.5)
    for term in (-1.453152027, 1.421413741, -0.284496736, 0.254829592):
        series = (series + term * 0.5) * t
    tail = series * decay
    return jnp.where(value < 0.0, tail, 1.0 - tail), decay * (1.0 / math.sqrt(2.0 * math.pi))


def transposed(value):
    side = 2 * LANES
    row_id = lax.broadcasted_iota(jnp.int32, (side, side), 0)
    unit = (row_id == lax.broadcasted_iota(jnp.int32, (side, side), 1)).astype(f32).astype(bf16)
    blocks = []
    for start in range(0, value.shape[1], side):
        block = value[:, start : start + side]
        size = block.shape[1]
        blocks.append(dot(unit[:size, :size], block, 1, 1).astype(bf16))
    return jnp.concatenate(blocks, axis=0)


def layer_kernel(
    row_class,
    lengths,
    tokens,
    cotangent,
    vectors,
    qkv_hbm,
    out_hbm,
    up_hbm,
    down_hbm,
    mixed,
    input_grad,
    sums,
    vec_sum,
    qkv_w,
    out_w,
    up_w,
    down_w,
    query,
    query_turned,
    keys_values,
    keys_turned,
    prob,
    attended,
    normed_low,
    grad_down,
    grad_attn,
    narrow_tokens,
    narrow_attended,
    narrow_normed,
    narrow_grad,
    active,
    grad_up,
    attn_turned,
    qkv_turned,
    exchanged,
    grad_heads,
    heads_turned,
    slope,
    normed_one,
    zhat_one,
    rstd_one,
    grad_two,
    work,
    vec,
    vec_core,
    vec_y,
    vec_x,
    vec_z,
    part,
    came_one,
    came_two,
    came_three,
    came_four,
    load_sem,
    pair_send,
    pair_recv,
    send_sem,
    recv_sem,
):
    grad_one = normed_one
    z, x, y, core = position()
    tok = tokens.shape[0]
    loads = {
        name: pltpu.make_async_copy(source, target, load_sem.at[index])
        for index, (name, source, target) in enumerate(
            (
                ("qkv", qkv_hbm, qkv_w),
                ("out", out_hbm, out_w),
                ("up", up_hbm, up_w),
                ("down", down_hbm, down_w),
            )
        )
    }
    loads["qkv"].start()
    beyond = device(z, x, 1 - y, core)
    beside = device(z, 1 - x, y, core)
    partner = device(z, x, y, 1 - core)
    along = [device(flip_z(z, step), x, y, core) for step in (1, 2, 3)]
    all_here = greet([beyond, beside, partner] + along)
    started = []

    def remote(source, target, send_at, recv_at, other):
        copy = pltpu.make_async_remote_copy(
            src_ref=source,
            dst_ref=target,
            send_sem=send_at,
            recv_sem=recv_at,
            device_id=other,
            device_id_type=MESH,
        )
        copy.start()
        started.append(copy)
        return copy

    pair_count = []

    def to_partner(source, target):
        slot = len(pair_count)
        pair_count.append(slot)
        return remote(source, target, pair_send.at[slot], pair_recv.at[slot], partner)

    own_half = pl.ds(pl.multiple_of(core * HALF, HALF), HALF)
    other_half = pl.ds(pl.multiple_of((1 - core) * HALF, HALF), HALF)

    def span(start, length=D):
        return vectors[0:1, start : start + length]

    def put_vec(start, value):
        for index in range(value.shape[1] // LANES):
            block, row = divmod(start // LANES + index, VEC_BLOCK)
            vec[block, row : row + 1, :] = value[:, index * LANES : (index + 1) * LANES]

    vec[...] = jnp.zeros_like(vec)

    own_rows = pl.ds(0, tok)
    far_rows = pl.ds(tok, tok)
    own_lanes, far_lanes = own_rows, far_rows

    def share_half(value, narrow):
        narrow[own_rows, :] = value[:, own_half]
        return to_partner(value.at[:, other_half], narrow.at[far_rows])

    loads["qkv"].wait()
    for name in ("out", "up", "down"):
        loads[name].start()
    kv_came = []
    for index, start in ((1, None), (2, BIAS_VALUE)):
        value = dot(tokens[...], qkv_w[:, index * D : (index + 1) * D], 1, 0)
        if start is not None:
            value = value + span(start)
        cols = slice((index - 1) * D, index * D)
        keys_values[own_rows, cols] = value.astype(bf16)
        if index == 1:
            all_here()
        kv_came.append(
            to_partner(keys_values.at[own_rows, cols], keys_values.at[far_rows, cols])
        )
    value = dot(tokens[...], qkv_w[:, :D], 1, 0) + span(BIAS_QUERY)
    query[...] = value.astype(bf16)
    query_turned[...] = transposed(query[...])
    allowed = allowed_mask(row_class, lengths, 2 * y + core, tok)
    masks, first = half_masks()
    tokens_came = share_half(tokens, narrow_tokens)
    for copy in kv_came:
        copy.wait_recv()

    scale = HEAD_DIM ** (-0.5)

    def lanes_at(start):
        return pl.ds(pl.multiple_of(start, LANES), LANES)

    def attend_pair(pair, carry):
        cols = lanes_at(pair * LANES)
        keys = keys_values[:, cols]
        values = keys_values[:, lanes_at(D + pair * LANES)]
        outs = []
        for side, mask in enumerate(masks):
            score = dot(query[:, cols] * (mask * scale), keys, 1, 1)
            score = jnp.where(allowed, score, masked_score)
            exponent = jnp.exp(score - jnp.max(score, axis=-1, keepdims=True))
            chance = exponent * (1.0 / jnp.sum(exponent, axis=-1, keepdims=True))
            chance = chance.astype(bf16)
            prob[2 * pair + side] = chance
            outs.append(dot(chance, values, 1, 0))
        attended[:, cols] = jnp.where(first, outs[0], outs[1]).astype(bf16)
        return carry

    lax.fori_loop(0, HEADS // 2, attend_pair, 0)
    attended_came = share_half(attended, narrow_attended)

    loads["out"].wait()
    work[...] = dot(attended[...], out_w[...], 1, 0)

    def norm_one(rows, carry):
        value = tokens[rows, :].astype(f32) + (work[rows, :] + span(BIAS_OUT))
        centre = value - row_mean(value)
        rstd = lax.rsqrt(row_mean(centre * centre) + norm_eps)
        zhat = centre * rstd
        normed = zhat * span(GAIN_ONE) + span(SHIFT_ONE)
        zhat_one[rows, :] = zhat
        rstd_one[rows, :] = jnp.broadcast_to(rstd, (ROWS, LANES))
        normed_one[rows, :] = normed
        normed_low[rows, :] = normed.astype(bf16)
        return carry

    by_rows(tok, norm_one)
    normed_came = share_half(normed_low, narrow_normed)

    loads["up"].wait()
    for tile in range(FF // D):
        cols = slice(tile * D, (tile + 1) * D)
        work[...] = dot(normed_low[...], up_w[:, cols], 1, 0)

        def gelu(rows, carry):
            value = work[rows, :] + span(BIAS_UP + cols.start)
            chance, density = normal_parts(value)
            active[rows, cols] = (value * chance).astype(bf16)
            slope[rows, cols] = chance + value * density
            return carry

        by_rows(tok, gelu)
    active_came = to_partner(active.at[own_rows], active.at[far_rows])
    loads["down"].wait()
    work[...] = dot(active[own_rows, :], down_w[...], 1, 0)

    def norm_two(rows, carry):
        value = normed_one[rows, :] + (work[rows, :] + span(BIAS_DOWN))
        centre = value - row_mean(value)
        rstd = lax.rsqrt(row_mean(centre * centre) + norm_eps)
        zhat = centre * rstd
        mixed[rows, :] = zhat * span(GAIN_TWO) + span(SHIFT_TWO)
        grad = cotangent[rows, :].astype(f32)
        inner = grad * span(GAIN_TWO)
        grad_in = (inner - row_mean(inner) - zhat * row_mean(inner * zhat)) * rstd
        grad_two[rows, :] = grad_in
        low = grad_in.astype(bf16)
        grad_down[rows, :] = low
        gain, shift, bias = carry
        return gain + fold(grad * zhat), shift + fold(grad), bias + fold(low.astype(f32))

    zero = jnp.zeros((8, D), f32)
    gain, shift, bias = by_rows(tok, norm_two, (zero, zero, zero))
    put_vec(GAIN_TWO, column_sum(gain))
    put_vec(SHIFT_TWO, column_sum(shift))
    put_vec(BIAS_DOWN, column_sum(bias))
    grad_down_came = share_half(grad_down, narrow_grad)
    keys_turned[...] = transposed(keys_values[:, :D])

    here = {"f": z // 2, "n": z % 2, "x": x, "y": y}
    across = {"f": along[1], "n": along[0], "x": beside, "y": beyond}

    class Chain:
        def __init__(self, index):
            matrix, start, rows, order = CHUNKS[index]
            self.index, self.order, self.stage = index, order, 0
            self.rows = pl.ds(start, rows)
            self.own = part.at[matrix]
            self.came = [ref.at[matrix] for ref in (came_one, came_two, came_three, came_four)]
            self.final = sums.at[matrix]

        def cells(self, free, flipped=None):
            return tuple(
                slice(None) if name in free else 1 - here[name] if name == flipped else here[name]
                for name in "fnxy"
            ) + (self.rows,)

        def send(self, source, target, other):
            sems = (send_sem.at[self.index, self.stage], recv_sem.at[self.index, self.stage])
            self.copy = remote(source, target, *sems, other)

        def advance(self):
            stage, order = self.stage, self.order
            if stage:
                self.copy.wait_recv()
            if 1 <= stage <= 4:
                free = order[stage:]
                for choice in itertools.product((0, 1), repeat=len(free)):
                    taken = dict(zip(sorted(free, key="fnxy".index), choice))
                    at = tuple(taken.get(name, here[name]) for name in "fnxy") + (self.rows,)
                    value = self.own[at] + self.came[stage - 1][choice + (self.rows,)]
                    if stage == 4:
                        self.final[core, y, self.rows] = value
                    else:
                        self.own[at] = value
            if stage < 4:
                name = order[stage]
                source = self.own.at[self.cells(order[stage + 1 :], name)]
                target = self.came[stage].at[(slice(None),) * (3 - stage) + (self.rows,)]
                self.send(source, target, across[name])
            elif stage == 4:
                block = self.final.at[core, y, self.rows]
                self.send(block, block, beyond)
            elif stage == 5:
                block = self.final.at[core, :, self.rows]
                self.send(block, block, partner)
            self.stage += 1

    chains = [Chain(index) for index in range(len(CHUNKS))]
    plan = iter(CHUNK_PLAN)

    def pump():
        for index in next(plan):
            chains[index].advance()

    def feed_forward(matrix, narrow, wide):
        left = transposed(narrow[...])

        def block(index, carry):
            cols = pl.ds(pl.multiple_of(index * UNIT, UNIT), UNIT)
            value = dot(left, wide[:, cols], 1, 0).astype(bf16)
            for side in range(2):
                part[matrix, index // 4, index // 2 % 2, index % 2, side] = value[
                    side * SIDE : (side + 1) * SIDE
                ]
            return carry

        lax.fori_loop(0, 8, block, 0)

    def projections(matrix, turned, narrow, width, offset, between=None):
        for tile in range(turned.shape[0] // UNIT):
            if between and tile % 2 == 0:
                between()
            value = dot(turned[tile * UNIT : (tile + 1) * UNIT, :], narrow[...], 1, 0).astype(bf16)
            for start in range(0, UNIT, PIECE):
                block, row = divmod(tile * UNIT + start, width)
                side, row = divmod(offset + row, SIDE)
                cell = (matrix, block // 4, block // 2 % 2, block % 2, side)
                part[cell + (pl.ds(row, PIECE),)] = value[start : start + PIECE]

    grad_down_came.wait_recv()
    active_came.wait_recv()
    feed_forward(0, narrow_grad, active)

    for tile in range(FF // D):
        pump()
        cols = slice(tile * D, (tile + 1) * D)
        work[...] = dot(grad_down[...], down_w[cols, :], 1, 1)

        def gelu_back(rows, carry):
            low = (work[rows, :] * slope[rows, cols]).astype(bf16)
            grad_up[rows, cols] = low
            return carry + fold(low.astype(f32))

        put_vec(BIAS_UP + cols.start, column_sum(by_rows(tok, gelu_back, zero)))
    grad_up_came = to_partner(grad_up.at[own_rows], grad_up.at[far_rows])
    pump()
    normed_came.wait_recv()
    grad_up_came.wait_recv()
    feed_forward(1, narrow_normed, grad_up)
    pump()

    work[...] = dot(grad_up[own_rows, :], up_w[...], 1, 1)

    def norm_one_back(rows, carry):
        grad = grad_two[rows, :] + work[rows, :]
        zhat = zhat_one[rows, :]
        inner = grad * span(GAIN_ONE)
        grad_in = inner - row_mean(inner) - zhat * row_mean(inner * zhat)
        grad_in = grad_in * rstd_one[rows, 0:1]
        grad_one[rows, :] = grad_in
        low = grad_in.astype(bf16)
        grad_attn[rows, :] = low
        gain, shift, bias = carry
        return gain + fold(grad * zhat), shift + fold(grad), bias + fold(low.astype(f32))

    gain, shift, bias = by_rows(tok, norm_one_back, (zero, zero, zero))
    put_vec(GAIN_ONE, column_sum(gain))
    put_vec(SHIFT_ONE, column_sum(shift))
    put_vec(BIAS_OUT, column_sum(bias))
    grad_heads[...] = dot(grad_attn[...], out_w[...], 1, 1).astype(bf16)
    heads_turned[...] = dot(out_w[...], grad_attn[...], 1, 1).astype(bf16)

    half_lanes = LANES // 2

    def attend_pair_back(pair, carry):
        cols = lanes_at(pair * LANES)
        values = keys_values[:, lanes_at(D + pair * LANES)]
        for side, mask in enumerate(masks):
            start = pl.multiple_of(pair * LANES + side * half_lanes, half_lanes)
            rows = pl.ds(start, half_lanes)
            low_chance = prob[2 * pair + side]
            chance = low_chance.astype(f32)
            grad_chance = dot(grad_heads[:, cols] * mask, values, 1, 1)
            mean = jnp.sum(chance * grad_chance, axis=-1, keepdims=True)
            grad_score = (chance * (grad_chance - mean)).astype(bf16)
            values_grad = dot(heads_turned[rows, :], low_chance, 1, 0).astype(bf16)
            keys_grad = (dot(query_turned[rows, :], grad_score, 1, 0) * scale).astype(bf16)
            query_grad = (dot(keys_turned[rows, :], grad_score, 1, 1) * scale).astype(bf16)
            blocks = (
                query_grad,
                keys_grad[:, :tok],
                values_grad[:, :tok],
                keys_grad[:, tok:],
                values_grad[:, tok:],
            )
            for index, value in enumerate(blocks):
                start = index * LANES + side * half_lanes
                exchanged[0, pair, start : start + half_lanes, :] = value
        return carry

    half_came = []
    for half in range(2):
        pump()
        pairs = pl.ds(half * HEADS // 4, HEADS // 4)
        lax.fori_loop(half * HEADS // 4, (half + 1) * HEADS // 4, attend_pair_back, 0)
        half_came.append(to_partner(exchanged.at[0, pairs], exchanged.at[1, pairs]))
    pump()
    attn_turned[:, own_lanes] = transposed(grad_attn[...])
    grad_attn_came = to_partner(attn_turned.at[:, own_lanes], attn_turned.at[:, far_lanes])

    for pair in range(HEADS // 2):
        if pair % (HEADS // 4) == 0:
            half_came[pair // (HEADS // 4)].wait_recv()
        for who, lanes in enumerate((own_lanes, far_lanes)):
            start = pair * LANES
            mine, theirs = exchanged.at[who, pair], exchanged.at[1 - who, pair]
            qkv_turned[start : start + LANES, lanes] = mine[:LANES]
            for index in (1, 2):
                rows = slice(index * LANES, (index + 1) * LANES)
                sent = slice((index + 2) * LANES, (index + 3) * LANES)
                value = mine[rows].astype(f32) + theirs[sent].astype(f32)
                start = index * D + pair * LANES
                qkv_turned[start : start + LANES, lanes] = value.astype(bf16)
    pump()
    tokens_came.wait_recv()
    projections(2, qkv_turned, narrow_tokens, 3 * D // 8, 0, pump)
    attended_came.wait_recv()
    grad_attn_came.wait_recv()
    projections(2, attn_turned, narrow_attended, D // 8, 3 * D // 8)
    pump()

    ones = jnp.ones((8, tok), bf16)
    for start, rows in ((BIAS_QUERY, slice(0, D)), (BIAS_VALUE, slice(2 * D, 3 * D))):
        put_vec(start, dot(ones, qkv_turned[rows, own_lanes], 1, 1)[0:1])
    vec_came = to_partner(vec, vec_core)
    value = dot(qkv_w[...], qkv_turned[:, own_lanes], 1, 0)
    input_grad[...] = grad_one[...] + value.T

    vec_slots = [(send_sem.at[len(CHUNKS), i], recv_sem.at[len(CHUNKS), i]) for i in range(5)]

    def vec_steps():
        vec_came.wait_recv()
        vec_core[...] = vec[...] + vec_core[...]
        copy = remote(vec_core, vec_y, *vec_slots[0], beyond)
        yield
        copy.wait_recv()
        for i in range(4):
            vec_x[0, i] = vec_core[2 * i + x] + vec_y[2 * i + x]
            vec_x[1, i] = vec_core[2 * i + 1 - x] + vec_y[2 * i + 1 - x]
        copy = remote(vec_x.at[1], vec_x.at[2], *vec_slots[1], beside)
        yield
        copy.wait_recv()
        vec_x[0] = vec_x[0] + vec_x[2]
        copies = [
            remote(
                vec_x.at[0, flip_z(z, step)],
                vec_z.at[step - 1],
                *vec_slots[1 + step],
                along[step - 1],
            )
            for step in (1, 2, 3)
        ]
        yield
        total = vec_x[0, z]
        for step, copy in enumerate(copies):
            copy.wait_recv()
            total = total + vec_z[step]
        vec_sum[...] = total
        yield

    steps = vec_steps()
    for turn, index in enumerate(next(plan)):
        chains[index].advance()
        if turn % 10 == 9 and turn < 40:
            next(steps)
    for copy in started:
        copy.wait_send()


def layer(row_class, lengths, tokens, cotangent, vectors, qkv_w, out_w, up_w, down_w):
    tok = tokens.shape[0]
    side = (SIDE, UNIT)

    def low(*dims):
        return pltpu.VMEM(dims, bf16)

    def wide(*dims):
        return pltpu.VMEM(dims, f32)

    return pl.pallas_call(
        layer_kernel,
        out_shape=(
            jax.ShapeDtypeStruct((tok, D), f32),
            jax.ShapeDtypeStruct((tok, D), f32),
            jax.ShapeDtypeStruct((3, 2, 2) + side, bf16),
            jax.ShapeDtypeStruct((16, LANES), f32),
        ),
        in_specs=[SMEM, SMEM, VMEM, VMEM, VMEM] + [ANY] * 4,
        out_specs=(VMEM,) * 4,
        scratch_shapes=[
            low(D, 3 * D),
            low(D, D),
            low(D, FF),
            low(FF, D),
            low(tok, D),
            low(D, tok),
            low(2 * tok, 2 * D),
            low(D, 2 * tok),
            low(HEADS, tok, 2 * tok),
            low(tok, D),
            low(tok, D),
            low(tok, D),
            low(tok, D),
            low(2 * tok, HALF),
            low(2 * tok, HALF),
            low(2 * tok, HALF),
            low(2 * tok, HALF),
            low(2 * tok, FF),
            low(2 * tok, FF),
            low(D, 2 * tok),
            low(3 * D, 2 * tok),
            low(2, HEADS // 2, 5 * LANES, tok),
            low(tok, D),
            low(D, tok),
            wide(tok, FF),
            wide(tok, D),
            wide(tok, D),
            wide(tok, LANES),
            wide(tok, D),
            wide(tok, D),
            wide(8, 16, LANES),
            wide(8, 16, LANES),
            wide(8, 16, LANES),
            wide(3, 4, 16, LANES),
            wide(3, 16, LANES),
            low(3, 2, 2, 2, 2, *side),
            low(3, 2, 2, 2, *side),
            low(3, 2, 2, *side),
            low(3, 2, *side),
            low(3, *side),
            pltpu.SemaphoreType.DMA((4,)),
            pltpu.SemaphoreType.DMA((12,)),
            pltpu.SemaphoreType.DMA((12,)),
            pltpu.SemaphoreType.DMA((len(CHUNKS) + 1, 6)),
            pltpu.SemaphoreType.DMA((len(CHUNKS) + 1, 6)),
        ],
        compiler_params=pltpu.CompilerParams(
            vmem_limit_bytes=63 * MIB, collective_id=0, has_side_effects=True
        ),
        name="layer",
    )(row_class, lengths, tokens, cotangent, vectors[None, :], qkv_w, out_w, up_w, down_w)


GRAM_AXES = ("far", "near", "x")
GRAM_GROUPS = (
    (1, "xnf"),
    (2, "xnf"),
    (2, "xnf"),
    (3, "xnf"),
    (3, "nxf"),
    (3, "fxn"),
    (3, "nxf"),
    (2, "xnf"),
    (1, "xnf"),
    (1, "xnf"),
)
GRAM_PLAN = (
    6, 0, 9, 2, 5, 4, 7, 3, 0, 9, 6, 8, 2, 0, 9, 1, 0, 7, 9, 8, 2, 6,
    0, 5, 4, 3, 1, 8, 2, 7, 0, 6, 9, 5, 4, 8, 0, 2, 7, 1, 8, 9, 6, 3,
    5, 4, 7, 1, 8, 6, 2, 9, 3, 5, 8, 1, 4, 7, 2, 3, 5, 1, 4, 6, 7, 3,
    1, 5, 3, 4,
)


def muon_kernel(
    sums,
    qkv_hbm,
    out_hbm,
    up_hbm,
    down_hbm,
    factors,
    own_sum,
    qkv_old,
    out_old,
    old,
    moment,
    out,
    part,
    came_one,
    came_two,
    came_three,
    high,
    low,
    load_sem,
    send_sem,
    recv_sem,
    share_send,
    share_recv,
    *ortho,
):
    z, x, y, core = position()
    here = {"far": z // 2, "near": z % 2, "x": x}
    others = {
        "far": device(flip_z(z, 2), x, y, core),
        "near": device(flip_z(z, 1), x, y, core),
        "x": device(z, 1 - x, y, core),
    }
    beyond = device(z, x, 1 - y, core)
    partner = device(z, x, y, 1 - core)
    own = 2 * y + core
    all_here = greet(list(others.values()) + [beyond, partner])

    def load_two(source, target, matrix):
        loads = [
            pltpu.make_async_copy(source, target, load_sem.at[0]),
            pltpu.make_async_copy(sums.at[matrix], own_sum, load_sem.at[1]),
        ]
        for load in loads:
            load.start()
        for load in loads:
            load.wait()

    def from_turned(source, target, skip):
        load_two(source, target, 2)
        rows = target.shape[0]
        moment[...] = jnp.zeros_like(moment)
        for half in range(2):
            cols = slice(half * HALF, (half + 1) * HALF)
            start = half * UNIT + skip
            value = own_sum[start : start + rows, :].astype(f32)
            moment[cols, skip : skip + rows] = (muon_keep * target[:, cols] + value).T

    @pl.when(own == 0)
    def _():
        from_turned(qkv_hbm, qkv_old, 0)

    @pl.when(own == 1)
    def _():
        from_turned(out_hbm, out_old, qkv_old.shape[0])

    @pl.when(own == 2)
    def _():
        load_two(up_hbm, old, 1)
        moment[...] = muon_keep * old[...] + own_sum[...].astype(f32)

    @pl.when(own == 3)
    def _():
        load_two(down_hbm, old, 0)
        moment[...] = muon_keep * old[...] + own_sum[...].astype(f32)

    all_here()
    blocks = sub_blocks(moment.shape[0])
    starts = [sum(count for count, _ in GRAM_GROUPS[:group]) for group in range(len(GRAM_GROUPS))]
    high[...] = moment[...].astype(bf16)
    low[...] = (moment[...] - high[...].astype(f32)).astype(bf16)
    started = []

    def product(index):
        i, j = blocks[index]
        left, right = pl.ds(i * SUB, SUB), pl.ds(j * SUB, SUB)
        total = dot(high[left, :], high[right, :], 1, 1)
        total = total + dot(high[left, :], low[right, :], 1, 1)
        total = total + dot(low[left, :], high[right, :], 1, 1)
        rows = SUB // 8
        for owner in range(8):
            cell = (owner // 4, owner // 2 % 2, owner % 2)
            part[cell + (index,)] = total[
                owner * rows : (owner + 1) * rows
            ]

    def send(source, target, group, slot, axis):
        copy = pltpu.make_async_remote_copy(
            src_ref=source,
            dst_ref=target,
            send_sem=send_sem.at[group, slot],
            recv_sem=recv_sem.at[group, slot],
            device_id=others[axis],
            device_id_type=MESH,
        )
        copy.start()
        started.append(copy)
        return copy

    def cells(fixed, flipped=None):
        return tuple(
            1 - here[name] if name == flipped else here[name] if name in fixed else slice(None)
            for name in GRAM_AXES
        )

    class Walk:
        def __init__(self, group):
            count, order = GRAM_GROUPS[group]
            self.group, self.stage = group, 0
            self.order = [GRAM_AXES["fnx".index(letter)] for letter in order]
            self.mine = (pl.ds(starts[group], count),)
            self.came = [
                ref.at[(slice(None),) * (2 - stage) + self.mine]
                for stage, ref in enumerate((came_one, came_two, came_three))
            ]

        def advance(self):
            stage, order = self.stage, self.order
            mine = self.mine
            if stage:
                self.copy.wait_recv()
            if 1 <= stage <= 3:
                kept = cells(order[:stage]) + mine
                total = part[kept] + self.came[stage - 1][...]
                if stage == 3:
                    out[kept] = total
                else:
                    part[kept] = total
            if stage < 3:
                source = part.at[cells(order[:stage], order[stage]) + mine]
                self.copy = send(source, self.came[stage], self.group, stage, order[stage])
            elif stage < 6:
                block = out.at[cells(order[: 6 - stage]) + mine]
                self.copy = send(block, block, self.group, stage, order[5 - stage])
            self.stage += 1

    walks = [Walk(group) for group in range(len(GRAM_GROUPS))]
    for group in GRAM_PLAN:
        if walks[group].stage == 0:
            for index in range(starts[group], starts[group] + GRAM_GROUPS[group][0]):
                product(index)
        walks[group].advance()

    e = ortho[0]
    for index, (i, j) in enumerate(blocks):
        value = out[:, :, :, index].reshape(SUB, SUB)
        e[i * SUB : (i + 1) * SUB, j * SUB : (j + 1) * SUB] = value
        if i != j:
            e[j * SUB : (j + 1) * SUB, i * SUB : (i + 1) * SUB] = value.T

    across, beside = [], []

    def share(slot, rows, kind, other):
        block = factors.at[slot, rows]
        index = rows.start // TILE
        copy = pltpu.make_async_remote_copy(
            src_ref=block,
            dst_ref=block,
            send_sem=share_send.at[index, kind],
            recv_sem=share_recv.at[index, kind],
            device_id=other,
            device_id_type=MESH,
        )
        copy.start()
        started.append(copy)
        return copy

    def emit(rows, value):
        factors[own, rows, :] = value
        across.append((rows, share(own, rows, 0, beyond)))
        beside.append(share(own, rows, 1, partner))

    newton_schulz(e, moment, *ortho, emit)
    for rows, copy in across:
        copy.wait_recv()
        beside.append(share(2 * (1 - y) + core, rows, 2, partner))
    for copy in beside:
        copy.wait_recv()
    for copy in started:
        copy.wait_send()


def muon_factors(sums, *olds):
    size, cols = olds[2].shape
    count = len(sub_blocks(size))
    groups = len(GRAM_GROUPS)
    rows = (SUB // 8, SUB)

    def wide(*dims):
        return pltpu.VMEM(dims, f32)

    return pl.pallas_call(
        muon_kernel,
        out_shape=jax.ShapeDtypeStruct((4, size, cols), bf16),
        in_specs=[ANY] * 5,
        out_specs=VMEM,
        scratch_shapes=[
            pltpu.VMEM((size, cols), bf16),
            wide(*olds[0].shape),
            wide(*olds[1].shape),
            wide(size, cols),
            wide(size, cols),
            wide(2, 2, 2, count, *rows),
            wide(2, 2, 2, count, *rows),
            wide(2, 2, count, *rows),
            wide(2, count, *rows),
            wide(count, *rows),
            pltpu.VMEM((size, cols), bf16),
            pltpu.VMEM((size, cols), bf16),
            pltpu.SemaphoreType.DMA((2,)),
            pltpu.SemaphoreType.DMA((groups, 6)),
            pltpu.SemaphoreType.DMA((groups, 6)),
            pltpu.SemaphoreType.DMA((size // TILE, 3)),
            pltpu.SemaphoreType.DMA((size // TILE, 3)),
        ]
        + ortho_scratch(size, cols),
        compiler_params=pltpu.CompilerParams(
            vmem_limit_bytes=58 * MIB, collective_id=1, has_side_effects=True
        ),
        name="muon_factors",
    )(sums, *olds)


def window(start, width, total):
    size = -(-(width + 96) // LANES) * LANES
    first = jnp.minimum(start // LANES * LANES, total - size)
    return pl.ds(pl.multiple_of(first, LANES), size), start - first


def finish_kernel(
    factors_hbm,
    sums_hbm,
    qkv_hbm,
    out_hbm,
    up_hbm,
    down_hbm,
    qkv_old_hbm,
    out_old_hbm,
    up_old_hbm,
    down_old_hbm,
    mixed_hbm,
    grad_hbm,
    mixed_out,
    grad_out,
    qkv_moment_out,
    out_moment_out,
    up_moment_out,
    down_moment_out,
    qkv_out,
    out_out,
    up_out,
    down_out,
    factors,
    sums,
    qkv_w,
    out_w,
    up_w,
    down_w,
    qkv_moment,
    out_moment,
    up_moment,
    down_moment,
    qkv_new,
    out_new,
    up_new,
    down_new,
    turned,
    load_sem,
    store_sem,
):
    shrink = 1.0 - muon_rate * muon_decay
    dp_id = lax.axis_index("dp")
    qkv_cols, out_cols = qkv_new.shape[0], out_new.shape[0]
    qkv_lanes, qkv_skip = window(dp_id * qkv_cols, qkv_cols, 3 * D)
    out_lanes, out_skip = window(dp_id * out_cols, out_cols, D)
    block = pl.ds(pl.multiple_of(dp_id * UNIT, UNIT), UNIT)
    pairs = {
        "sums": (sums_hbm, sums),
        "up_moment": (up_old_hbm, up_moment),
        "down_moment": (down_old_hbm, down_moment),
        "factors": (factors_hbm, factors),
        "up": (up_hbm.at[:, block], up_w),
        "down": (down_hbm.at[block], down_w),
        "qkv_moment": (qkv_old_hbm, qkv_moment),
        "out_moment": (out_old_hbm, out_moment),
        "qkv": (qkv_hbm.at[:, qkv_lanes], qkv_w),
        "out": (out_hbm.at[:, out_lanes], out_w),
    }
    loads = {
        name: pltpu.make_async_copy(source, target, load_sem.at[index])
        for index, (name, (source, target)) in enumerate(pairs.items())
    }
    for load in loads.values():
        load.start()
    stores = []

    def store(source, target):
        stores.append(pltpu.make_async_copy(source, target, store_sem.at[len(stores)]))
        stores[-1].start()

    store(mixed_hbm, mixed_out)
    store(grad_hbm, grad_out)

    def step(index, rate):
        return muon_rate * rate * factors[index].astype(f32)

    loads["sums"].wait()
    for index, name, target, out in (
        (1, "up_moment", up_moment, up_moment_out),
        (0, "down_moment", down_moment, down_moment_out),
    ):
        loads[name].wait()
        target[...] = muon_keep * target[...] + sums[index].astype(f32)
        store(target, out)
    loads["qkv_moment"].wait()
    loads["out_moment"].wait()
    for half in range(2):
        cols = slice(half * HALF, (half + 1) * HALF)
        value = sums[2, cols].astype(f32)
        qkv_moment[:, cols] = muon_keep * qkv_moment[:, cols] + value[:qkv_cols]
        out_moment[:, cols] = muon_keep * out_moment[:, cols] + value[qkv_cols:]
    store(qkv_moment, qkv_moment_out)
    store(out_moment, out_moment_out)
    loads["factors"].wait()
    loads["up"].wait()
    up_new[...] = up_w[...].astype(f32) * shrink - step(2, math.sqrt(max(1.0, FF / D)))
    store(up_new, up_out)
    loads["down"].wait()
    down_new[...] = down_w[...].astype(f32) * shrink - step(3, 1.0).T
    store(down_new, down_out)
    loads["qkv"].wait()
    turned[...] = qkv_w[...].astype(f32).T
    rows = pl.ds(pl.multiple_of(qkv_skip, 32), qkv_cols)
    qkv_new[...] = turned[rows, :] * shrink - step(0, math.sqrt(3.0)).T[:qkv_cols]
    store(qkv_new, qkv_out)
    loads["out"].wait()
    turned[: out_w.shape[1], :] = out_w[...].astype(f32).T
    rows = pl.ds(pl.multiple_of(out_skip, 32), out_cols)
    out_new[...] = turned[rows, :] * shrink - step(1, 1.0).T[qkv_cols:]
    store(out_new, out_out)
    for copy in stores:
        copy.wait()


def finish(factors, sums, weights, olds, mixed, input_grad):
    shapes = [old.shape for old in olds]
    news = shapes[:3] + [shapes[3][::-1]]

    def wide(shape):
        return pltpu.VMEM(shape, f32)

    return pl.pallas_call(
        finish_kernel,
        out_shape=tuple(
            jax.ShapeDtypeStruct(shape, f32)
            for shape in [mixed.shape, input_grad.shape] + shapes + news
        ),
        in_specs=[ANY] * 12,
        out_specs=(ANY,) * 10,
        scratch_shapes=[
            pltpu.VMEM(factors.shape, bf16),
            pltpu.VMEM(sums.shape, bf16),
            pltpu.VMEM((D, 384), bf16),
            pltpu.VMEM((D, 256), bf16),
            pltpu.VMEM((D, UNIT), bf16),
            pltpu.VMEM((UNIT, D), bf16),
        ]
        + [wide(shape) for shape in shapes + news]
        + [
            wide((384, D)),
            pltpu.SemaphoreType.DMA((10,)),
            pltpu.SemaphoreType.DMA((10,)),
        ],
        compiler_params=pltpu.CompilerParams(vmem_limit_bytes=48 * MIB),
        name="finish",
    )(factors, sums, *weights, *olds, mixed, input_grad)


def swap(value, axis, bit):
    size = lax.axis_size(axis)
    return lax.ppermute(value, axis, [(i, i ^ bit) for i in range(size)])


def scatter_head(value, bit, position):
    half = value.shape[1] // 2
    mine = lax.dynamic_slice_in_dim(value, position * half, half, 1)
    other = lax.dynamic_slice_in_dim(value, (1 - position) * half, half, 1)
    return (mine.astype(f32) + swap(other, "head", bit).astype(f32)).astype(bf16)


def scatter_dp_pair(value, position):
    paired = value.reshape((value.shape[0] // 2, 2) + value.shape[1:])
    mine = lax.dynamic_index_in_dim(paired, position, 1, False)
    other = lax.dynamic_index_in_dim(paired, 1 - position, 1, False)
    return (mine.astype(f32) + swap(other, "dp", 1).astype(f32)).astype(bf16)


def scatter_dp_rest(value, place):
    ranks = value.shape[0]
    total = lax.dynamic_index_in_dim(value, place, 0, False).astype(f32)
    for step in range(1, ranks):
        sent = lax.dynamic_index_in_dim(value, place ^ step, 0, False)
        total = total + swap(sent, "dp", 2 * step).astype(f32)
    return total


def local(
    tokens,
    cotangent,
    qkv_weight,
    out_weight,
    up_weight,
    down_weight,
    vectors,
    qkv_moment,
    out_moment,
    up_moment,
    down_moment,
    adam_first,
    adam_second,
    bucket_class,
    row_lengths,
):
    n_dp = lax.axis_size("dp")
    n_head = lax.axis_size("head")
    dp_id = lax.axis_index("dp")
    head_id = lax.axis_index("head")
    core, side = head_id % 2, head_id // 2
    tok, width = tokens.shape
    hidden = up_weight.shape[1]
    half = width // 2
    qkv_cols, out_cols = qkv_moment.shape[1], out_moment.shape[1]
    shrink = 1.0 - muon_rate * muon_decay

    def weight_block(weight, cols, dim):
        return lax.dynamic_slice_in_dim(weight, dp_id * cols, cols, dim)

    block = head_id.astype(jnp.int32)[None]
    vec_len = vectors.shape[0] // n_dp
    if (n_dp, n_head, tok) == (8, 4, 256):
        mixed, input_grad, sums, vec = layer(
            bucket_class,
            row_lengths,
            tokens,
            cotangent,
            vectors,
            qkv_weight,
            out_weight,
            up_weight,
            down_weight,
        )
        grad_vec = vec[:VEC_BLOCK].reshape(vec_len)
        sums = sums.reshape(3, width, -1)
        olds = [qkv_moment.T, out_moment.T, up_moment, down_moment]
        mixed, input_grad, *results = finish(
            muon_factors(sums, *olds),
            sums,
            [qkv_weight, out_weight, up_weight, down_weight],
            olds,
            mixed,
            input_grad,
        )
        moments, new_weights = results[:4], results[4:]
        moments = [moments[0].T, moments[1].T, *moments[2:]]
        new_weights = [new_weights[0].T, new_weights[1].T, *new_weights[2:]]
    else:
        pieces = split_vectors(vectors, width, hidden)
        bias_query, bias_value, bias_out, gain_one, shift_one = pieces[:5]
        bias_up, bias_down, gain_two, shift_two = pieces[5:]
        bias_qkv = jnp.concatenate([bias_query, jnp.zeros_like(bias_query), bias_value])

        def column_half(value, which):
            return lax.dynamic_slice_in_dim(value, which * half, half, 1)

        qkv = (dot(tokens, qkv_weight, 1, 0) + bias_qkv).astype(bf16)
        other = swap(qkv[:, width:], "head", 1)
        attended = attend(block, bucket_class, row_lengths, qkv, other)
        attn_val = dot(attended, out_weight, 1, 0) + bias_out
        resid_one = tokens.astype(f32) + attn_val
        centre = resid_one - jnp.mean(resid_one, axis=-1, keepdims=True)
        rstd_one = lax.rsqrt(jnp.mean(centre * centre, axis=-1, keepdims=True) + norm_eps)
        zhat_one = centre * rstd_one
        normed_one = zhat_one * gain_one + shift_one
        normed_low = normed_one.astype(bf16)
        up_val = dot(normed_low, up_weight, 1, 0) + bias_up
        phi_cum = 0.5 * (1.0 + lax.erf(up_val * (0.5**0.5)))
        active_low = (up_val * phi_cum).astype(bf16)
        slope = phi_cum + up_val * jnp.exp(-0.5 * up_val * up_val) * (1.0 / math.sqrt(2.0 * math.pi))
        down_val = dot(active_low, down_weight, 1, 0) + bias_down
        resid_two = normed_one + down_val
        centre = resid_two - jnp.mean(resid_two, axis=-1, keepdims=True)
        rstd_two = lax.rsqrt(jnp.mean(centre * centre, axis=-1, keepdims=True) + norm_eps)
        zhat_two = centre * rstd_two
        mixed = zhat_two * gain_two + shift_two

        def norm_back(grad, gain, zhat, rstd):
            inner = grad * gain
            mean = jnp.mean(inner, axis=-1, keepdims=True)
            slant = jnp.mean(inner * zhat, axis=-1, keepdims=True)
            return (inner - mean - zhat * slant) * rstd, jnp.sum(grad * zhat, axis=0), jnp.sum(grad, axis=0)

        grad_two, grad_gain_two, grad_shift_two = norm_back(
            cotangent.astype(f32), gain_two, zhat_two, rstd_two
        )
        grad_down_low = grad_two.astype(bf16)
        grad_bias_down = jnp.sum(grad_down_low, axis=0, dtype=f32)

        x_id, z_id = dp_id % 2, dp_id // 2

        grad_up_low = (dot(grad_down_low, down_weight, 1, 1) * slope).astype(bf16)
        grad_bias_up = jnp.sum(grad_up_low, axis=0, dtype=f32)
        grad_normed = grad_two + dot(grad_up_low, up_weight, 1, 1)
        grad_one, grad_gain_one, grad_shift_one = norm_back(grad_normed, gain_one, zhat_one, rstd_one)
        grad_attn_low = grad_one.astype(bf16)
        grad_bias_out = jnp.sum(grad_attn_low, axis=0, dtype=f32)
        grad_heads = dot(grad_attn_low, out_weight, 1, 1).astype(bf16)
        grad_query, own, sent = attend_back(block, bucket_class, row_lengths, qkv, other, grad_heads)
        grad_kv = (own + swap(sent, "head", 1).astype(f32)).astype(bf16)
        grad_qkv = jnp.concatenate([grad_query, grad_kv], axis=1)
        grad_bias_qkv = jnp.sum(grad_qkv, axis=0, dtype=f32)
        input_grad = grad_one + dot(grad_qkv, qkv_weight, 1, 1)
        grad_vector = jnp.concatenate(
            [
                grad_bias_qkv[:width],
                grad_bias_qkv[2 * width :],
                grad_bias_out,
                grad_gain_one,
                grad_shift_one,
                grad_bias_up,
                grad_bias_down,
                grad_gain_two,
                grad_shift_two,
            ]
        )
        grad_vector = grad_vector + swap(grad_vector, "head", 1)
        wides = [active_low, grad_up_low, grad_attn_low, grad_qkv]
        narrows = [grad_down_low, normed_low, attended, tokens]

        def both_halves(value):
            return jnp.concatenate(
                [column_half(value, core), swap(column_half(value, 1 - core), "head", 1)], axis=0
            )

        def weight_grad(wide, narrow):
            wide = jnp.concatenate([wide, swap(wide, "head", 1)], axis=0)
            value = dot(wide, both_halves(narrow), 0, 0).astype(bf16)
            return value.reshape(n_dp, value.shape[0] // n_dp, half)

        def reduce_y_first(value):
            return scatter_dp_rest(scatter_dp_pair(scatter_head(value, 2, side), x_id), z_id)

        def reduce_x_first(value):
            return scatter_dp_rest(scatter_head(scatter_dp_pair(value, x_id), 2, side), z_id)

        def spread(value):
            value = value.astype(bf16)
            came = swap(value, "head", 2)
            value = jnp.concatenate(
                [jnp.where(side == 0, value, came), jnp.where(side == 0, came, value)], axis=0
            )
            came = swap(value, "head", 1)
            return jnp.concatenate(
                [jnp.where(core == 0, value, came), jnp.where(core == 0, came, value)], axis=1
            ).astype(f32)

        down_part, up_part, out_part, qkv_part = [
            weight_grad(wide, narrow) for wide, narrow in zip(wides, narrows)
        ]
        vec_rows = 16
        vec_part = grad_vector.reshape(n_dp, vec_len)
        vec_part = jnp.pad(vec_part, ((0, 0), (0, vec_rows * width - vec_len)))
        vec_part = vec_part.reshape(n_dp, vec_rows, width)
        vec_part = lax.dynamic_slice_in_dim(vec_part, core * half, half, 2).astype(bf16)
        down_new = spread(reduce_x_first(down_part))
        up_new = spread(reduce_y_first(up_part))
        tail_new = spread(
            reduce_y_first(jnp.concatenate([qkv_part, out_part, vec_part], axis=1))
        )
        grads = [
            tail_new[:qkv_cols].T,
            tail_new[qkv_cols : qkv_cols + out_cols].T,
            up_new.T,
            down_new.T,
        ]
        grad_vec = tail_new[qkv_cols + out_cols :].reshape(-1)[:vec_len]
        moments = [
            muon_keep * old + grad
            for old, grad in zip([qkv_moment, out_moment, up_moment, down_moment], grads)
        ]
        most = max(m.shape[1] for m in moments)
        padded = [jnp.pad(m, ((0, 0), (0, most - m.shape[1]))) for m in moments]
        chosen = padded[-1]
        for index in range(len(padded) - 2, -1, -1):
            chosen = jnp.where(head_id == index, padded[index], chosen)
        gram_mat = lax.dot_general(
            chosen, chosen, (((1,), (1,)), ((), ())), precision=lax.Precision.HIGH
        )
        own_factor = orthogonalize(lax.psum(gram_mat, "dp"), chosen)
        across = swap(own_factor, "head", 2)
        low_pair = jnp.where(side == 0, own_factor, across)
        high_pair = jnp.where(side == 0, across, own_factor)
        near_low = swap(low_pair, "head", 1)
        near_high = swap(high_pair, "head", 1)
        factors = [
            jnp.where(core == 0, low_pair, near_low),
            jnp.where(core == 0, near_low, low_pair),
            jnp.where(core == 0, high_pair, near_high),
            jnp.where(core == 0, near_high, high_pair),
        ]
        factors = [o[:, : m.shape[1]].astype(f32) for o, m in zip(factors, moments)]
        factors[3] = factors[3].T
        old_weights = [
            weight_block(qkv_weight, qkv_cols, 1),
            weight_block(out_weight, out_cols, 1),
            weight_block(up_weight, up_moment.shape[1], 1),
            weight_block(down_weight, down_moment.shape[1], 0),
        ]

        rates = (math.sqrt(3.0), 1.0, math.sqrt(max(1.0, hidden / width)), 1.0)
        new_weights = [
            old.astype(f32) * shrink - muon_rate * rate * factor
            for old, rate, factor in zip(old_weights, rates, factors)
        ]

    vec_old = lax.dynamic_slice_in_dim(vectors, dp_id * vec_len, vec_len, 0)
    vec_first = beta_first * adam_first + (1.0 - beta_first) * grad_vec
    vec_second = beta_second * adam_second + (1.0 - beta_second) * grad_vec * grad_vec
    first_hat = vec_first / (1.0 - beta_first**STEP)
    second_hat = vec_second / (1.0 - beta_second**STEP)
    vec_new = vec_old - adam_rate * first_hat / (jnp.sqrt(second_hat) + adam_eps)
    return (mixed, input_grad, *moments, *new_weights, vec_first, vec_second, vec_new)


def solution(mesh):
    tokens_spec = P(("dp", "head"), None)
    block_spec = P(None, "dp")
    return jax.shard_map(
        local,
        mesh=mesh,
        in_specs=(
            tokens_spec,
            tokens_spec,
            P(),
            P(),
            P(),
            P(),
            P(),
            block_spec,
            block_spec,
            block_spec,
            block_spec,
            P("dp"),
            P("dp"),
            P("dp"),
            P("dp", None),
        ),
        out_specs=(
            tokens_spec,
            tokens_spec,
            block_spec,
            block_spec,
            block_spec,
            block_spec,
            block_spec,
            block_spec,
            block_spec,
            P("dp", None),
            P("dp"),
            P("dp"),
            P("dp"),
        ),
        check_vma=False,
    )
```

```python
import functools
import itertools
import math

import jax
import jax.numpy as jnp
from jax import lax
from jax.experimental import pallas as pl
from jax.experimental.pallas import tpu as pltpu
from jax.sharding import PartitionSpec as P

D = 768
HEADS = 12
HEAD_DIM = 64
FF = 3072
BASE_LEN = 128
NS_STEPS = 5
STEP = 5
MAX_LEN = 512

f32 = jnp.float32
bf16 = jnp.bfloat16

norm_eps = 1e-12
masked_score = -1000000000.0
quintic_a = 3.4445
quintic_b = -4.775
quintic_c = 2.0315
muon_rate = 1.0
muon_decay = 0.01
muon_keep = 0.5
adam_rate = 0.2
beta_first = 0.9
beta_second = 0.999
adam_eps = 1e-08
MIB = 1024 * 1024


def dot(left, right, left_dim, right_dim):
    return lax.dot_general(
        left, right, (((left_dim,), (right_dim,)), ((), ())), preferred_element_type=f32
    )


def split_vectors(vectors, width, hidden):
    lengths_list = [width] * 5 + [hidden] + [width] * 3
    pieces = []
    offset = 0
    for length in lengths_list:
        pieces.append(vectors[offset : offset + length])
        offset = offset + length
    return pieces


def allowed_mask(class_ref, length_ref, block, tok):
    shift = class_ref[0] + int(math.log2(BASE_LEN))
    query_place = block * tok + lax.broadcasted_iota(jnp.int32, (tok, 1), 0)
    lane = lax.broadcasted_iota(jnp.int32, (1, 2 * tok), 1)
    own = lane < tok
    key_place = jnp.where(own, block * tok + lane, (block ^ 1) * tok + lane - tok)
    key_row = lax.shift_right_logical(key_place, jnp.broadcast_to(shift, key_place.shape))
    offset = key_place - lax.shift_left(key_row, jnp.broadcast_to(shift, key_place.shape))
    row_len = jnp.zeros_like(key_row)
    for slot in range(length_ref.shape[1]):
        row_len = jnp.where(key_row == slot, length_ref[0, slot], row_len)
    key_row = jnp.where(offset < row_len, key_row, -1)
    query_row = lax.shift_right_logical(query_place, jnp.broadcast_to(shift, query_place.shape))
    return query_row == key_row


def half_masks():
    lane = lax.broadcasted_iota(jnp.int32, (1, 2 * HEAD_DIM), 1)
    first = (lane < HEAD_DIM).astype(f32)
    return (first.astype(bf16), (1.0 - first).astype(bf16)), lane < HEAD_DIM


def head_prob(query, keys, allowed):
    score = jnp.where(allowed, dot(query, keys, 1, 1) * HEAD_DIM ** (-0.5), masked_score)
    exponent = jnp.exp(score - jnp.max(score, axis=-1, keepdims=True))
    return exponent / jnp.sum(exponent, axis=-1, keepdims=True)


def attend_kernel(block_ref, class_ref, length_ref, qkv_ref, other_ref, out_ref):
    tok = qkv_ref.shape[0]
    allowed = allowed_mask(class_ref, length_ref, block_ref[0], tok)
    masks, first = half_masks()
    for pair in range(HEADS // 2):
        cols = pl.ds(pair * 2 * HEAD_DIM, 2 * HEAD_DIM)
        kcols = pl.ds(D + pair * 2 * HEAD_DIM, 2 * HEAD_DIM)
        vcols = pl.ds(2 * D + pair * 2 * HEAD_DIM, 2 * HEAD_DIM)
        query = qkv_ref[:, cols]
        keys = jnp.concatenate([qkv_ref[:, kcols], other_ref[:, cols]], axis=0)
        values = jnp.concatenate([qkv_ref[:, vcols], other_ref[:, kcols]], axis=0)
        outs = []
        for mask in masks:
            prob = head_prob(query * mask, keys, allowed)
            outs.append(dot(prob.astype(bf16), values, 1, 0))
        out_ref[:, cols] = jnp.where(first, outs[0], outs[1]).astype(bf16)


def attend_back_kernel(
    block_ref, class_ref, length_ref, qkv_ref, other_ref, grad_ref, dq_ref, own_ref, send_ref
):
    tok = qkv_ref.shape[0]
    allowed = allowed_mask(class_ref, length_ref, block_ref[0], tok)
    masks, first = half_masks()
    scale = HEAD_DIM ** (-0.5)
    for pair in range(HEADS // 2):
        cols = pl.ds(pair * 2 * HEAD_DIM, 2 * HEAD_DIM)
        kcols = pl.ds(D + pair * 2 * HEAD_DIM, 2 * HEAD_DIM)
        vcols = pl.ds(2 * D + pair * 2 * HEAD_DIM, 2 * HEAD_DIM)
        query = qkv_ref[:, cols]
        keys = jnp.concatenate([qkv_ref[:, kcols], other_ref[:, cols]], axis=0)
        values = jnp.concatenate([qkv_ref[:, vcols], other_ref[:, kcols]], axis=0)
        grad = grad_ref[:, cols]
        dqs, dk, dv = [], None, None
        for mask in masks:
            head_query = query * mask
            head_grad = grad * mask
            prob = head_prob(head_query, keys, allowed)
            part_v = dot(prob.astype(bf16), head_grad, 0, 0)
            dprob = dot(head_grad, values, 1, 1)
            dscore = prob * (dprob - jnp.sum(prob * dprob, axis=-1, keepdims=True))
            dscore = dscore.astype(bf16)
            dqs.append(dot(dscore, keys, 1, 0))
            part_k = dot(dscore, head_query, 0, 0)
            dk = part_k if dk is None else dk + part_k
            dv = part_v if dv is None else dv + part_v
        dk = dk * scale
        dq_ref[:, cols] = (jnp.where(first, dqs[0], dqs[1]) * scale).astype(bf16)
        own_ref[:, cols] = dk[:tok]
        own_ref[:, kcols] = dv[:tok]
        send_ref[:, cols] = dk[tok:].astype(bf16)
        send_ref[:, kcols] = dv[tok:].astype(bf16)


SMEM = pl.BlockSpec(memory_space=pltpu.SMEM)
VMEM = pl.BlockSpec(memory_space=pltpu.VMEM)
ANY = pl.BlockSpec(memory_space=pl.ANY)


def attend(block, row_class, lengths, qkv, other):
    tok = qkv.shape[0]
    return pl.pallas_call(
        attend_kernel,
        out_shape=jax.ShapeDtypeStruct((tok, D), bf16),
        in_specs=[SMEM, SMEM, SMEM, VMEM, VMEM],
        out_specs=VMEM,
        compiler_params=pltpu.CompilerParams(vmem_limit_bytes=32 * MIB),
        name="attend",
    )(block, row_class, lengths, qkv, other)


def attend_back(block, row_class, lengths, qkv, other, grad):
    tok = qkv.shape[0]
    return pl.pallas_call(
        attend_back_kernel,
        out_shape=(
            jax.ShapeDtypeStruct((tok, D), bf16),
            jax.ShapeDtypeStruct((tok, 2 * D), f32),
            jax.ShapeDtypeStruct((tok, 2 * D), bf16),
        ),
        in_specs=[SMEM, SMEM, SMEM, VMEM, VMEM, VMEM],
        out_specs=(VMEM, VMEM, VMEM),
        compiler_params=pltpu.CompilerParams(vmem_limit_bytes=32 * MIB),
        name="attend_back",
    )(block, row_class, lengths, qkv, other, grad)


CENTRES = (0.0, 0.0, 0.0, 0.8, 0.8)
TILE = 256
SUB = 128


def sub_blocks(size):
    count = size // SUB
    return [(i, j) for i in range(count) for j in range(i, count)]


def newton_schulz(gram, moment, e, f, g, eb, fb, gb, yy, y, emit):
    size = e.shape[0]
    tiles = [slice(i * TILE, (i + 1) * TILE) for i in range(size // TILE)]

    def unit(rows):
        row_id = rows.start + lax.broadcasted_iota(jnp.int32, (TILE, size), 0)
        col_id = lax.broadcasted_iota(jnp.int32, (TILE, size), 1)
        return (row_id == col_id).astype(f32)

    diagonal = jnp.zeros((TILE, size), f32)
    for rows in tiles:
        diagonal = diagonal + gram[rows, :] * unit(rows)
    trace = jnp.sum(jnp.sum(diagonal, axis=0, keepdims=True), axis=1, keepdims=True)
    factor = 1.0 / (jnp.sqrt(trace) + 1e-07)
    square_factor = factor * factor
    for rows in tiles:
        value = gram[rows, :] * square_factor
        e[rows, :] = value
        eb[rows, :] = value.astype(bf16)
        value = moment[rows, :] * factor
        y[rows, :] = value
        yy[0, rows, :] = value.astype(bf16)

    def one_step(centre, after, now, then, last=False):
        keep = quintic_a + quintic_b * centre + quintic_c * centre * centre
        linear = quintic_b + 2.0 * quintic_c * centre
        for rows in tiles:
            value = linear * e[rows, :] + quintic_c * dot(eb[rows, :], eb[...], 1, 0)
            fb[rows, :] = value.astype(bf16)
            if centre:
                f[rows, :] = value
        for rows in tiles:
            value = keep * y[rows, :] + dot(fb[rows, :], now[...], 1, 0)
            if last:
                emit(rows, value.astype(bf16))
            else:
                y[rows, :] = value
                then[rows, :] = value.astype(bf16)
        if last:
            return
        for rows in tiles:
            value = keep * e[rows, :] + dot(eb[rows, :], fb[...], 1, 0)
            if centre:
                value = value + centre * f[rows, :]
            g[rows, :] = value
            gb[rows, :] = value.astype(bf16)
        for rows in tiles:
            value = keep * g[rows, :] + dot(gb[rows, :], fb[...], 1, 0)
            if centre:
                value = value + (centre * keep) * f[rows, :]
            shift = centre * keep * keep - after
            if not isinstance(shift, float) or shift:
                value = value + shift * unit(rows)
            e[rows, :] = value
            eb[rows, :] = value.astype(bf16)

    plain = sum(centre == 0.0 for centre in CENTRES)

    def plain_step(step, carry):
        after = jnp.where(step == plain - 1, CENTRES[plain], 0.0)
        one_step(0.0, after, yy.at[step % 2], yy.at[(step + 1) % 2])
        return carry

    lax.fori_loop(0, plain, plain_step, 0)
    for step in range(plain, NS_STEPS):
        last = step + 1 == NS_STEPS
        after = 0.0 if last else CENTRES[step + 1]
        one_step(CENTRES[step], after, yy.at[step % 2], yy.at[(step + 1) % 2], last)


def ortho_kernel(gram, moment, out, *scratch):
    def emit(rows, value):
        out[rows, :] = value

    newton_schulz(gram, moment, *scratch, emit)


def ortho_scratch(size, cols):
    square, square_low = pltpu.VMEM((size, size), f32), pltpu.VMEM((size, size), bf16)
    wide_low = pltpu.VMEM((2, size, cols), bf16)
    return [square] * 3 + [square_low] * 3 + [wide_low, pltpu.VMEM((size, cols), f32)]


def orthogonalize(gram_mat, moment):
    size, cols = moment.shape
    return pl.pallas_call(
        ortho_kernel,
        out_shape=jax.ShapeDtypeStruct((size, cols), bf16),
        in_specs=[VMEM, VMEM],
        out_specs=VMEM,
        scratch_shapes=ortho_scratch(size, cols),
        compiler_params=pltpu.CompilerParams(vmem_limit_bytes=48 * MIB),
        name="ortho",
    )(gram_mat, moment)


MESH = pl.DeviceIdType.MESH
PIECE = 48
SIDE = 192
UNIT = 2 * SIDE
HALF = D // 2
LANES = 128
VEC_BLOCK = 9
ROWS = 16
CHUNKS = (
    (0, 0, 96, "xfyn"),
    (0, 96, 96, "nyxf"),
    (1, 0, 96, "nxfy"),
    (1, 96, 96, "xyfn"),
    (2, 0, 48, "nxyf"),
    (2, 48, 48, "yxfn"),
    (2, 96, 48, "xnyf"),
    (2, 144, 32, "xyfn"),
    (2, 176, 16, "ynxf"),
)
CHUNK_PLAN = (
    (1, 0),
    (),
    (),
    (),
    (),
    (2, 3),
    (1, 0),
    (1, 3),
    (),
    (),
    (1, 0, 2, 3),
    (),
    (0, 1),
    (6, 8, 2, 1, 4, 0, 5, 7),
    (
        1, 8, 3, 0, 0, 2, 8, 5, 7, 6, 8, 3, 2, 4, 8, 7, 5, 6, 8, 3, 2, 4,
        8, 7, 6, 3, 5, 4, 7, 2, 6, 5, 7, 4, 6, 7, 5, 4, 6, 5, 4,
    ),
)
BIAS_QUERY, BIAS_VALUE, BIAS_OUT, GAIN_ONE, SHIFT_ONE, BIAS_UP = (i * D for i in range(6))
BIAS_DOWN, GAIN_TWO, SHIFT_TWO = (BIAS_UP + FF + i * D for i in range(3))


def position():
    dp_id, head_id = lax.axis_index("dp"), lax.axis_index("head")
    z, x = dp_id // 2, dp_id % 2
    y, core = head_id // 2, head_id % 2
    return z, x, y, core


def device(z, x, y, core):
    return (2 * z + x, 2 * y + core)


def flip_z(z, step):
    high, low = z // 2, z % 2
    high = 1 - high if step // 2 else high
    low = 1 - low if step % 2 else low
    return 2 * high + low


def greet(others):
    barrier = pltpu.get_barrier_semaphore()
    for other in others:
        pl.semaphore_signal(barrier, inc=1, device_id=other, device_id_type=MESH)
    return lambda: pl.semaphore_wait(barrier, len(others))


def by_rows(count, body, init=None, together=4):
    def step(index, carry):
        for part in range(together):
            start = (index * together + part) * ROWS
            carry = body(pl.ds(pl.multiple_of(start, ROWS), ROWS), carry)
        return carry

    return lax.fori_loop(0, count // (ROWS * together), step, init)


def row_mean(value):
    return jnp.sum(value, axis=-1, keepdims=True) * (1.0 / D)


def fold(value):
    return jnp.sum(value.reshape(value.shape[0] // 8, 8, value.shape[1]), axis=0)


def column_sum(value):
    return jnp.sum(value, axis=0, keepdims=True)


def normal_parts(value):
    size = jnp.abs(value)
    decay = jnp.exp(-0.5 * value * value)
    below = 1.0 + (0.3275911 * 0.5**0.5) * size
    t = pl.reciprocal(below, approx=True)
    t = t * (2.0 - below * t)
    series = t * (1.061405429 * 0.5)
    for term in (-1.453152027, 1.421413741, -0.284496736, 0.254829592):
        series = (series + term * 0.5) * t
    tail = series * decay
    return jnp.where(value < 0.0, tail, 1.0 - tail), decay * (1.0 / math.sqrt(2.0 * math.pi))


def transposed(value):
    side = 2 * LANES
    row_id = lax.broadcasted_iota(jnp.int32, (side, side), 0)
    unit = (row_id == lax.broadcasted_iota(jnp.int32, (side, side), 1)).astype(f32).astype(bf16)
    blocks = []
    for start in range(0, value.shape[1], side):
        block = value[:, start : start + side]
        size = block.shape[1]
        blocks.append(dot(unit[:size, :size], block, 1, 1).astype(bf16))
    return jnp.concatenate(blocks, axis=0)


def layer_kernel(
    row_class,
    lengths,
    tokens,
    cotangent,
    vectors,
    qkv_hbm,
    out_hbm,
    up_hbm,
    down_hbm,
    mixed,
    input_grad,
    sums,
    vec_sum,
    qkv_w,
    out_w,
    up_w,
    down_w,
    query,
    query_turned,
    keys_values,
    keys_turned,
    prob,
    attended,
    normed_low,
    grad_down,
    grad_attn,
    narrow_tokens,
    narrow_attended,
    narrow_normed,
    narrow_grad,
    active,
    grad_up,
    attn_turned,
    qkv_turned,
    exchanged,
    grad_heads,
    heads_turned,
    slope,
    normed_one,
    zhat_one,
    rstd_one,
    grad_two,
    work,
    vec,
    vec_core,
    vec_y,
    vec_x,
    vec_z,
    part,
    came_one,
    came_two,
    came_three,
    came_four,
    load_sem,
    pair_send,
    pair_recv,
    send_sem,
    recv_sem,
):
    grad_one = normed_one
    z, x, y, core = position()
    tok = tokens.shape[0]
    loads = {
        name: pltpu.make_async_copy(source, target, load_sem.at[index])
        for index, (name, source, target) in enumerate(
            (
                ("qkv", qkv_hbm, qkv_w),
                ("out", out_hbm, out_w),
                ("up", up_hbm, up_w),
                ("down", down_hbm, down_w),
            )
        )
    }
    loads["qkv"].start()
    beyond = device(z, x, 1 - y, core)
    beside = device(z, 1 - x, y, core)
    partner = device(z, x, y, 1 - core)
    along = [device(flip_z(z, step), x, y, core) for step in (1, 2, 3)]
    all_here = greet([beyond, beside, partner] + along)
    started = []

    def remote(source, target, send_at, recv_at, other):
        copy = pltpu.make_async_remote_copy(
            src_ref=source,
            dst_ref=target,
            send_sem=send_at,
            recv_sem=recv_at,
            device_id=other,
            device_id_type=MESH,
        )
        copy.start()
        started.append(copy)
        return copy

    pair_count = []

    def to_partner(source, target):
        slot = len(pair_count)
        pair_count.append(slot)
        return remote(source, target, pair_send.at[slot], pair_recv.at[slot], partner)

    own_half = pl.ds(pl.multiple_of(core * HALF, HALF), HALF)
    other_half = pl.ds(pl.multiple_of((1 - core) * HALF, HALF), HALF)

    def span(start, length=D):
        return vectors[0:1, start : start + length]

    def put_vec(start, value):
        for index in range(value.shape[1] // LANES):
            block, row = divmod(start // LANES + index, VEC_BLOCK)
            vec[block, row : row + 1, :] = value[:, index * LANES : (index + 1) * LANES]

    vec[...] = jnp.zeros_like(vec)

    own_rows = pl.ds(0, tok)
    far_rows = pl.ds(tok, tok)
    own_lanes, far_lanes = own_rows, far_rows

    def share_half(value, narrow):
        narrow[own_rows, :] = value[:, own_half]
        return to_partner(value.at[:, other_half], narrow.at[far_rows])

    loads["qkv"].wait()
    for name in ("out", "up", "down"):
        loads[name].start()
    kv_came = []
    for index, start in ((1, None), (2, BIAS_VALUE)):
        value = dot(tokens[...], qkv_w[:, index * D : (index + 1) * D], 1, 0)
        if start is not None:
            value = value + span(start)
        cols = slice((index - 1) * D, index * D)
        keys_values[own_rows, cols] = value.astype(bf16)
        if index == 1:
            all_here()
        kv_came.append(
            to_partner(keys_values.at[own_rows, cols], keys_values.at[far_rows, cols])
        )
    value = dot(tokens[...], qkv_w[:, :D], 1, 0) + span(BIAS_QUERY)
    query[...] = value.astype(bf16)
    query_turned[...] = transposed(query[...])
    allowed = allowed_mask(row_class, lengths, 2 * y + core, tok)
    masks, first = half_masks()
    tokens_came = share_half(tokens, narrow_tokens)
    for copy in kv_came:
        copy.wait_recv()

    scale = HEAD_DIM ** (-0.5)

    def lanes_at(start):
        return pl.ds(pl.multiple_of(start, LANES), LANES)

    def attend_pair(pair, carry):
        cols = lanes_at(pair * LANES)
        keys = keys_values[:, cols]
        values = keys_values[:, lanes_at(D + pair * LANES)]
        outs = []
        for side, mask in enumerate(masks):
            score = dot(query[:, cols] * (mask * scale), keys, 1, 1)
            score = jnp.where(allowed, score, masked_score)
            exponent = jnp.exp(score - jnp.max(score, axis=-1, keepdims=True))
            chance = exponent * (1.0 / jnp.sum(exponent, axis=-1, keepdims=True))
            chance = chance.astype(bf16)
            prob[2 * pair + side] = chance
            outs.append(dot(chance, values, 1, 0))
        attended[:, cols] = jnp.where(first, outs[0], outs[1]).astype(bf16)
        return carry

    lax.fori_loop(0, HEADS // 2, attend_pair, 0)
    attended_came = share_half(attended, narrow_attended)

    loads["out"].wait()
    work[...] = dot(attended[...], out_w[...], 1, 0)

    def norm_one(rows, carry):
        value = tokens[rows, :].astype(f32) + (work[rows, :] + span(BIAS_OUT))
        centre = value - row_mean(value)
        rstd = lax.rsqrt(row_mean(centre * centre) + norm_eps)
        zhat = centre * rstd
        normed = zhat * span(GAIN_ONE) + span(SHIFT_ONE)
        zhat_one[rows, :] = zhat
        rstd_one[rows, :] = jnp.broadcast_to(rstd, (ROWS, LANES))
        normed_one[rows, :] = normed
        normed_low[rows, :] = normed.astype(bf16)
        return carry

    by_rows(tok, norm_one)
    normed_came = share_half(normed_low, narrow_normed)

    loads["up"].wait()
    for tile in range(FF // D):
        cols = slice(tile * D, (tile + 1) * D)
        work[...] = dot(normed_low[...], up_w[:, cols], 1, 0)

        def gelu(rows, carry):
            value = work[rows, :] + span(BIAS_UP + cols.start)
            chance, density = normal_parts(value)
            active[rows, cols] = (value * chance).astype(bf16)
            slope[rows, cols] = chance + value * density
            return carry

        by_rows(tok, gelu)
    active_came = to_partner(active.at[own_rows], active.at[far_rows])
    loads["down"].wait()
    work[...] = dot(active[own_rows, :], down_w[...], 1, 0)

    def norm_two(rows, carry):
        value = normed_one[rows, :] + (work[rows, :] + span(BIAS_DOWN))
        centre = value - row_mean(value)
        rstd = lax.rsqrt(row_mean(centre * centre) + norm_eps)
        zhat = centre * rstd
        mixed[rows, :] = zhat * span(GAIN_TWO) + span(SHIFT_TWO)
        grad = cotangent[rows, :].astype(f32)
        inner = grad * span(GAIN_TWO)
        grad_in = (inner - row_mean(inner) - zhat * row_mean(inner * zhat)) * rstd
        grad_two[rows, :] = grad_in
        low = grad_in.astype(bf16)
        grad_down[rows, :] = low
        gain, shift, bias = carry
        return gain + fold(grad * zhat), shift + fold(grad), bias + fold(low.astype(f32))

    zero = jnp.zeros((8, D), f32)
    gain, shift, bias = by_rows(tok, norm_two, (zero, zero, zero))
    put_vec(GAIN_TWO, column_sum(gain))
    put_vec(SHIFT_TWO, column_sum(shift))
    put_vec(BIAS_DOWN, column_sum(bias))
    grad_down_came = share_half(grad_down, narrow_grad)
    keys_turned[...] = transposed(keys_values[:, :D])

    here = {"f": z // 2, "n": z % 2, "x": x, "y": y}
    across = {"f": along[1], "n": along[0], "x": beside, "y": beyond}

    class Chain:
        def __init__(self, index):
            matrix, start, rows, order = CHUNKS[index]
            self.index, self.order, self.stage = index, order, 0
            self.rows = pl.ds(start, rows)
            self.own = part.at[matrix]
            self.came = [ref.at[matrix] for ref in (came_one, came_two, came_three, came_four)]
            self.final = sums.at[matrix]

        def cells(self, free, flipped=None):
            return tuple(
                slice(None) if name in free else 1 - here[name] if name == flipped else here[name]
                for name in "fnxy"
            ) + (self.rows,)

        def send(self, source, target, other):
            sems = (send_sem.at[self.index, self.stage], recv_sem.at[self.index, self.stage])
            self.copy = remote(source, target, *sems, other)

        def advance(self):
            stage, order = self.stage, self.order
            if stage:
                self.copy.wait_recv()
            if 1 <= stage <= 4:
                free = order[stage:]
                for choice in itertools.product((0, 1), repeat=len(free)):
                    taken = dict(zip(sorted(free, key="fnxy".index), choice))
                    at = tuple(taken.get(name, here[name]) for name in "fnxy") + (self.rows,)
                    value = self.own[at] + self.came[stage - 1][choice + (self.rows,)]
                    if stage == 4:
                        self.final[core, y, self.rows] = value
                    else:
                        self.own[at] = value
            if stage < 4:
                name = order[stage]
                source = self.own.at[self.cells(order[stage + 1 :], name)]
                target = self.came[stage].at[(slice(None),) * (3 - stage) + (self.rows,)]
                self.send(source, target, across[name])
            elif stage == 4:
                block = self.final.at[core, y, self.rows]
                self.send(block, block, beyond)
            elif stage == 5:
                block = self.final.at[core, :, self.rows]
                self.send(block, block, partner)
            self.stage += 1

    chains = [Chain(index) for index in range(len(CHUNKS))]
    plan = iter(CHUNK_PLAN)

    def pump():
        for index in next(plan):
            chains[index].advance()

    def feed_forward(matrix, narrow, wide):
        left = transposed(narrow[...])

        def block(index, carry):
            cols = pl.ds(pl.multiple_of(index * UNIT, UNIT), UNIT)
            value = dot(left, wide[:, cols], 1, 0).astype(bf16)
            for side in range(2):
                part[matrix, index // 4, index // 2 % 2, index % 2, side] = value[
                    side * SIDE : (side + 1) * SIDE
                ]
            return carry

        lax.fori_loop(0, 8, block, 0)

    def projections(matrix, turned, narrow, width, offset, between=None):
        for tile in range(turned.shape[0] // UNIT):
            if between and tile % 2 == 0:
                between()
            value = dot(turned[tile * UNIT : (tile + 1) * UNIT, :], narrow[...], 1, 0).astype(bf16)
            for start in range(0, UNIT, PIECE):
                block, row = divmod(tile * UNIT + start, width)
                side, row = divmod(offset + row, SIDE)
                cell = (matrix, block // 4, block // 2 % 2, block % 2, side)
                part[cell + (pl.ds(row, PIECE),)] = value[start : start + PIECE]

    grad_down_came.wait_recv()
    active_came.wait_recv()
    feed_forward(0, narrow_grad, active)

    for tile in range(FF // D):
        pump()
        cols = slice(tile * D, (tile + 1) * D)
        work[...] = dot(grad_down[...], down_w[cols, :], 1, 1)

        def gelu_back(rows, carry):
            low = (work[rows, :] * slope[rows, cols]).astype(bf16)
            grad_up[rows, cols] = low
            return carry + fold(low.astype(f32))

        put_vec(BIAS_UP + cols.start, column_sum(by_rows(tok, gelu_back, zero)))
    grad_up_came = to_partner(grad_up.at[own_rows], grad_up.at[far_rows])
    pump()
    normed_came.wait_recv()
    grad_up_came.wait_recv()
    feed_forward(1, narrow_normed, grad_up)
    pump()

    work[...] = dot(grad_up[own_rows, :], up_w[...], 1, 1)

    def norm_one_back(rows, carry):
        grad = grad_two[rows, :] + work[rows, :]
        zhat = zhat_one[rows, :]
        inner = grad * span(GAIN_ONE)
        grad_in = inner - row_mean(inner) - zhat * row_mean(inner * zhat)
        grad_in = grad_in * rstd_one[rows, 0:1]
        grad_one[rows, :] = grad_in
        low = grad_in.astype(bf16)
        grad_attn[rows, :] = low
        gain, shift, bias = carry
        return gain + fold(grad * zhat), shift + fold(grad), bias + fold(low.astype(f32))

    gain, shift, bias = by_rows(tok, norm_one_back, (zero, zero, zero))
    put_vec(GAIN_ONE, column_sum(gain))
    put_vec(SHIFT_ONE, column_sum(shift))
    put_vec(BIAS_OUT, column_sum(bias))
    grad_heads[...] = dot(grad_attn[...], out_w[...], 1, 1).astype(bf16)
    heads_turned[...] = dot(out_w[...], grad_attn[...], 1, 1).astype(bf16)

    half_lanes = LANES // 2

    def attend_pair_back(pair, carry):
        cols = lanes_at(pair * LANES)
        values = keys_values[:, lanes_at(D + pair * LANES)]
        for side, mask in enumerate(masks):
            start = pl.multiple_of(pair * LANES + side * half_lanes, half_lanes)
            rows = pl.ds(start, half_lanes)
            low_chance = prob[2 * pair + side]
            chance = low_chance.astype(f32)
            grad_chance = dot(grad_heads[:, cols] * mask, values, 1, 1)
            mean = jnp.sum(chance * grad_chance, axis=-1, keepdims=True)
            grad_score = (chance * (grad_chance - mean)).astype(bf16)
            values_grad = dot(heads_turned[rows, :], low_chance, 1, 0).astype(bf16)
            keys_grad = (dot(query_turned[rows, :], grad_score, 1, 0) * scale).astype(bf16)
            query_grad = (dot(keys_turned[rows, :], grad_score, 1, 1) * scale).astype(bf16)
            blocks = (
                query_grad,
                keys_grad[:, :tok],
                values_grad[:, :tok],
                keys_grad[:, tok:],
                values_grad[:, tok:],
            )
            for index, value in enumerate(blocks):
                start = index * LANES + side * half_lanes
                exchanged[0, pair, start : start + half_lanes, :] = value
        return carry

    half_came = []
    for half in range(2):
        pump()
        pairs = pl.ds(half * HEADS // 4, HEADS // 4)
        lax.fori_loop(half * HEADS // 4, (half + 1) * HEADS // 4, attend_pair_back, 0)
        half_came.append(to_partner(exchanged.at[0, pairs], exchanged.at[1, pairs]))
    pump()
    attn_turned[:, own_lanes] = transposed(grad_attn[...])
    grad_attn_came = to_partner(attn_turned.at[:, own_lanes], attn_turned.at[:, far_lanes])

    for pair in range(HEADS // 2):
        if pair % (HEADS // 4) == 0:
            half_came[pair // (HEADS // 4)].wait_recv()
        for who, lanes in enumerate((own_lanes, far_lanes)):
            start = pair * LANES
            mine, theirs = exchanged.at[who, pair], exchanged.at[1 - who, pair]
            qkv_turned[start : start + LANES, lanes] = mine[:LANES]
            for index in (1, 2):
                rows = slice(index * LANES, (index + 1) * LANES)
                sent = slice((index + 2) * LANES, (index + 3) * LANES)
                value = mine[rows].astype(f32) + theirs[sent].astype(f32)
                start = index * D + pair * LANES
                qkv_turned[start : start + LANES, lanes] = value.astype(bf16)
    pump()
    tokens_came.wait_recv()
    projections(2, qkv_turned, narrow_tokens, 3 * D // 8, 0, pump)
    attended_came.wait_recv()
    grad_attn_came.wait_recv()
    projections(2, attn_turned, narrow_attended, D // 8, 3 * D // 8)
    pump()

    ones = jnp.ones((8, tok), bf16)
    for start, rows in ((BIAS_QUERY, slice(0, D)), (BIAS_VALUE, slice(2 * D, 3 * D))):
        put_vec(start, dot(ones, qkv_turned[rows, own_lanes], 1, 1)[0:1])
    vec_came = to_partner(vec, vec_core)
    value = dot(qkv_w[...], qkv_turned[:, own_lanes], 1, 0)
    input_grad[...] = grad_one[...] + value.T

    vec_slots = [(send_sem.at[len(CHUNKS), i], recv_sem.at[len(CHUNKS), i]) for i in range(5)]

    def vec_steps():
        vec_came.wait_recv()
        vec_core[...] = vec[...] + vec_core[...]
        copy = remote(vec_core, vec_y, *vec_slots[0], beyond)
        yield
        copy.wait_recv()
        for i in range(4):
            vec_x[0, i] = vec_core[2 * i + x] + vec_y[2 * i + x]
            vec_x[1, i] = vec_core[2 * i + 1 - x] + vec_y[2 * i + 1 - x]
        copy = remote(vec_x.at[1], vec_x.at[2], *vec_slots[1], beside)
        yield
        copy.wait_recv()
        vec_x[0] = vec_x[0] + vec_x[2]
        copies = [
            remote(
                vec_x.at[0, flip_z(z, step)],
                vec_z.at[step - 1],
                *vec_slots[1 + step],
                along[step - 1],
            )
            for step in (1, 2, 3)
        ]
        yield
        total = vec_x[0, z]
        for step, copy in enumerate(copies):
            copy.wait_recv()
            total = total + vec_z[step]
        vec_sum[...] = total
        yield

    steps = vec_steps()
    for turn, index in enumerate(next(plan)):
        chains[index].advance()
        if turn % 10 == 9 and turn < 40:
            next(steps)
    for copy in started:
        copy.wait_send()


def layer(row_class, lengths, tokens, cotangent, vectors, qkv_w, out_w, up_w, down_w):
    tok = tokens.shape[0]
    side = (SIDE, UNIT)

    def low(*dims):
        return pltpu.VMEM(dims, bf16)

    def wide(*dims):
        return pltpu.VMEM(dims, f32)

    return pl.pallas_call(
        layer_kernel,
        out_shape=(
            jax.ShapeDtypeStruct((tok, D), f32),
            jax.ShapeDtypeStruct((tok, D), f32),
            jax.ShapeDtypeStruct((3, 2, 2) + side, bf16),
            jax.ShapeDtypeStruct((16, LANES), f32),
        ),
        in_specs=[SMEM, SMEM, VMEM, VMEM, VMEM] + [ANY] * 4,
        out_specs=(VMEM,) * 4,
        scratch_shapes=[
            low(D, 3 * D),
            low(D, D),
            low(D, FF),
            low(FF, D),
            low(tok, D),
            low(D, tok),
            low(2 * tok, 2 * D),
            low(D, 2 * tok),
            low(HEADS, tok, 2 * tok),
            low(tok, D),
            low(tok, D),
            low(tok, D),
            low(tok, D),
            low(2 * tok, HALF),
            low(2 * tok, HALF),
            low(2 * tok, HALF),
            low(2 * tok, HALF),
            low(2 * tok, FF),
            low(2 * tok, FF),
            low(D, 2 * tok),
            low(3 * D, 2 * tok),
            low(2, HEADS // 2, 5 * LANES, tok),
            low(tok, D),
            low(D, tok),
            wide(tok, FF),
            wide(tok, D),
            wide(tok, D),
            wide(tok, LANES),
            wide(tok, D),
            wide(tok, D),
            wide(8, 16, LANES),
            wide(8, 16, LANES),
            wide(8, 16, LANES),
            wide(3, 4, 16, LANES),
            wide(3, 16, LANES),
            low(3, 2, 2, 2, 2, *side),
            low(3, 2, 2, 2, *side),
            low(3, 2, 2, *side),
            low(3, 2, *side),
            low(3, *side),
            pltpu.SemaphoreType.DMA((4,)),
            pltpu.SemaphoreType.DMA((12,)),
            pltpu.SemaphoreType.DMA((12,)),
            pltpu.SemaphoreType.DMA((len(CHUNKS) + 1, 6)),
            pltpu.SemaphoreType.DMA((len(CHUNKS) + 1, 6)),
        ],
        compiler_params=pltpu.CompilerParams(
            vmem_limit_bytes=63 * MIB, collective_id=0, has_side_effects=True
        ),
        name="layer",
    )(row_class, lengths, tokens, cotangent, vectors[None, :], qkv_w, out_w, up_w, down_w)


GRAM_AXES = ("far", "near", "x")
GRAM_GROUPS = (
    (1, "xnf"),
    (2, "xnf"),
    (2, "xnf"),
    (3, "xnf"),
    (3, "nxf"),
    (3, "fxn"),
    (3, "nxf"),
    (2, "xnf"),
    (1, "xnf"),
    (1, "xnf"),
)
GRAM_PLAN = (
    6, 0, 9, 2, 5, 4, 7, 3, 0, 9, 6, 8, 2, 0, 9, 1, 0, 7, 9, 8, 2, 6,
    0, 5, 4, 3, 1, 8, 2, 7, 0, 6, 9, 5, 4, 8, 0, 2, 7, 1, 8, 9, 6, 3,
    5, 4, 7, 1, 8, 6, 2, 9, 3, 5, 8, 1, 4, 7, 2, 3, 5, 1, 4, 6, 7, 3,
    1, 5, 3, 4,
)


def muon_kernel(
    sums,
    qkv_hbm,
    out_hbm,
    up_hbm,
    down_hbm,
    factors,
    own_sum,
    qkv_old,
    out_old,
    old,
    moment,
    out,
    part,
    came_one,
    came_two,
    came_three,
    high,
    low,
    load_sem,
    send_sem,
    recv_sem,
    share_send,
    share_recv,
    *ortho,
):
    z, x, y, core = position()
    here = {"far": z // 2, "near": z % 2, "x": x}
    others = {
        "far": device(flip_z(z, 2), x, y, core),
        "near": device(flip_z(z, 1), x, y, core),
        "x": device(z, 1 - x, y, core),
    }
    beyond = device(z, x, 1 - y, core)
    partner = device(z, x, y, 1 - core)
    own = 2 * y + core
    all_here = greet(list(others.values()) + [beyond, partner])

    def load_two(source, target, matrix):
        loads = [
            pltpu.make_async_copy(source, target, load_sem.at[0]),
            pltpu.make_async_copy(sums.at[matrix], own_sum, load_sem.at[1]),
        ]
        for load in loads:
            load.start()
        for load in loads:
            load.wait()

    def from_turned(source, target, skip):
        load_two(source, target, 2)
        rows = target.shape[0]
        moment[...] = jnp.zeros_like(moment)
        for half in range(2):
            cols = slice(half * HALF, (half + 1) * HALF)
            start = half * UNIT + skip
            value = own_sum[start : start + rows, :].astype(f32)
            moment[cols, skip : skip + rows] = (muon_keep * target[:, cols] + value).T

    @pl.when(own == 0)
    def _():
        from_turned(qkv_hbm, qkv_old, 0)

    @pl.when(own == 1)
    def _():
        from_turned(out_hbm, out_old, qkv_old.shape[0])

    @pl.when(own == 2)
    def _():
        load_two(up_hbm, old, 1)
        moment[...] = muon_keep * old[...] + own_sum[...].astype(f32)

    @pl.when(own == 3)
    def _():
        load_two(down_hbm, old, 0)
        moment[...] = muon_keep * old[...] + own_sum[...].astype(f32)

    all_here()
    blocks = sub_blocks(moment.shape[0])
    starts = [sum(count for count, _ in GRAM_GROUPS[:group]) for group in range(len(GRAM_GROUPS))]
    high[...] = moment[...].astype(bf16)
    low[...] = (moment[...] - high[...].astype(f32)).astype(bf16)
    started = []

    def product(index):
        i, j = blocks[index]
        left, right = pl.ds(i * SUB, SUB), pl.ds(j * SUB, SUB)
        total = dot(high[left, :], high[right, :], 1, 1)
        total = total + dot(high[left, :], low[right, :], 1, 1)
        total = total + dot(low[left, :], high[right, :], 1, 1)
        rows = SUB // 8
        for owner in range(8):
            cell = (owner // 4, owner // 2 % 2, owner % 2)
            part[cell + (index,)] = total[
                owner * rows : (owner + 1) * rows
            ]

    def send(source, target, group, slot, axis):
        copy = pltpu.make_async_remote_copy(
            src_ref=source,
            dst_ref=target,
            send_sem=send_sem.at[group, slot],
            recv_sem=recv_sem.at[group, slot],
            device_id=others[axis],
            device_id_type=MESH,
        )
        copy.start()
        started.append(copy)
        return copy

    def cells(fixed, flipped=None):
        return tuple(
            1 - here[name] if name == flipped else here[name] if name in fixed else slice(None)
            for name in GRAM_AXES
        )

    class Walk:
        def __init__(self, group):
            count, order = GRAM_GROUPS[group]
            self.group, self.stage = group, 0
            self.order = [GRAM_AXES["fnx".index(letter)] for letter in order]
            self.mine = (pl.ds(starts[group], count),)
            self.came = [
                ref.at[(slice(None),) * (2 - stage) + self.mine]
                for stage, ref in enumerate((came_one, came_two, came_three))
            ]

        def advance(self):
            stage, order = self.stage, self.order
            mine = self.mine
            if stage:
                self.copy.wait_recv()
            if 1 <= stage <= 3:
                kept = cells(order[:stage]) + mine
                total = part[kept] + self.came[stage - 1][...]
                if stage == 3:
                    out[kept] = total
                else:
                    part[kept] = total
            if stage < 3:
                source = part.at[cells(order[:stage], order[stage]) + mine]
                self.copy = send(source, self.came[stage], self.group, stage, order[stage])
            elif stage < 6:
                block = out.at[cells(order[: 6 - stage]) + mine]
                self.copy = send(block, block, self.group, stage, order[5 - stage])
            self.stage += 1

    walks = [Walk(group) for group in range(len(GRAM_GROUPS))]
    for group in GRAM_PLAN:
        if walks[group].stage == 0:
            for index in range(starts[group], starts[group] + GRAM_GROUPS[group][0]):
                product(index)
        walks[group].advance()

    e = ortho[0]
    for index, (i, j) in enumerate(blocks):
        value = out[:, :, :, index].reshape(SUB, SUB)
        e[i * SUB : (i + 1) * SUB, j * SUB : (j + 1) * SUB] = value
        if i != j:
            e[j * SUB : (j + 1) * SUB, i * SUB : (i + 1) * SUB] = value.T

    across, beside = [], []

    def share(slot, rows, kind, other):
        block = factors.at[slot, rows]
        index = rows.start // TILE
        copy = pltpu.make_async_remote_copy(
            src_ref=block,
            dst_ref=block,
            send_sem=share_send.at[index, kind],
            recv_sem=share_recv.at[index, kind],
            device_id=other,
            device_id_type=MESH,
        )
        copy.start()
        started.append(copy)
        return copy

    def emit(rows, value):
        factors[own, rows, :] = value
        across.append((rows, share(own, rows, 0, beyond)))
        beside.append(share(own, rows, 1, partner))

    newton_schulz(e, moment, *ortho, emit)
    for rows, copy in across:
        copy.wait_recv()
        beside.append(share(2 * (1 - y) + core, rows, 2, partner))
    for copy in beside:
        copy.wait_recv()
    for copy in started:
        copy.wait_send()


def muon_factors(sums, *olds):
    size, cols = olds[2].shape
    count = len(sub_blocks(size))
    groups = len(GRAM_GROUPS)
    rows = (SUB // 8, SUB)

    def wide(*dims):
        return pltpu.VMEM(dims, f32)

    return pl.pallas_call(
        muon_kernel,
        out_shape=jax.ShapeDtypeStruct((4, size, cols), bf16),
        in_specs=[ANY] * 5,
        out_specs=VMEM,
        scratch_shapes=[
            pltpu.VMEM((size, cols), bf16),
            wide(*olds[0].shape),
            wide(*olds[1].shape),
            wide(size, cols),
            wide(size, cols),
            wide(2, 2, 2, count, *rows),
            wide(2, 2, 2, count, *rows),
            wide(2, 2, count, *rows),
            wide(2, count, *rows),
            wide(count, *rows),
            pltpu.VMEM((size, cols), bf16),
            pltpu.VMEM((size, cols), bf16),
            pltpu.SemaphoreType.DMA((2,)),
            pltpu.SemaphoreType.DMA((groups, 6)),
            pltpu.SemaphoreType.DMA((groups, 6)),
            pltpu.SemaphoreType.DMA((size // TILE, 3)),
            pltpu.SemaphoreType.DMA((size // TILE, 3)),
        ]
        + ortho_scratch(size, cols),
        compiler_params=pltpu.CompilerParams(
            vmem_limit_bytes=58 * MIB, collective_id=1, has_side_effects=True
        ),
        name="muon_factors",
    )(sums, *olds)


def window(start, width, total):
    size = -(-(width + 96) // LANES) * LANES
    first = jnp.minimum(start // LANES * LANES, total - size)
    return pl.ds(pl.multiple_of(first, LANES), size), start - first


def finish_kernel(
    factors_hbm,
    sums_hbm,
    qkv_hbm,
    out_hbm,
    up_hbm,
    down_hbm,
    qkv_old_hbm,
    out_old_hbm,
    up_old_hbm,
    down_old_hbm,
    mixed_hbm,
    grad_hbm,
    mixed_out,
    grad_out,
    qkv_moment_out,
    out_moment_out,
    up_moment_out,
    down_moment_out,
    qkv_out,
    out_out,
    up_out,
    down_out,
    factors,
    sums,
    qkv_w,
    out_w,
    up_w,
    down_w,
    qkv_moment,
    out_moment,
    up_moment,
    down_moment,
    qkv_new,
    out_new,
    up_new,
    down_new,
    turned,
    load_sem,
    store_sem,
):
    shrink = 1.0 - muon_rate * muon_decay
    dp_id = lax.axis_index("dp")
    qkv_cols, out_cols = qkv_new.shape[0], out_new.shape[0]
    qkv_lanes, qkv_skip = window(dp_id * qkv_cols, qkv_cols, 3 * D)
    out_lanes, out_skip = window(dp_id * out_cols, out_cols, D)
    block = pl.ds(pl.multiple_of(dp_id * UNIT, UNIT), UNIT)
    pairs = {
        "sums": (sums_hbm, sums),
        "up_moment": (up_old_hbm, up_moment),
        "down_moment": (down_old_hbm, down_moment),
        "factors": (factors_hbm, factors),
        "up": (up_hbm.at[:, block], up_w),
        "down": (down_hbm.at[block], down_w),
        "qkv_moment": (qkv_old_hbm, qkv_moment),
        "out_moment": (out_old_hbm, out_moment),
        "qkv": (qkv_hbm.at[:, qkv_lanes], qkv_w),
        "out": (out_hbm.at[:, out_lanes], out_w),
    }
    loads = {
        name: pltpu.make_async_copy(source, target, load_sem.at[index])
        for index, (name, (source, target)) in enumerate(pairs.items())
    }
    for load in loads.values():
        load.start()
    stores = []

    def store(source, target):
        stores.append(pltpu.make_async_copy(source, target, store_sem.at[len(stores)]))
        stores[-1].start()

    store(mixed_hbm, mixed_out)
    store(grad_hbm, grad_out)

    def step(index, rate):
        return muon_rate * rate * factors[index].astype(f32)

    loads["sums"].wait()
    for index, name, target, out in (
        (1, "up_moment", up_moment, up_moment_out),
        (0, "down_moment", down_moment, down_moment_out),
    ):
        loads[name].wait()
        target[...] = muon_keep * target[...] + sums[index].astype(f32)
        store(target, out)
    loads["qkv_moment"].wait()
    loads["out_moment"].wait()
    for half in range(2):
        cols = slice(half * HALF, (half + 1) * HALF)
        value = sums[2, cols].astype(f32)
        qkv_moment[:, cols] = muon_keep * qkv_moment[:, cols] + value[:qkv_cols]
        out_moment[:, cols] = muon_keep * out_moment[:, cols] + value[qkv_cols:]
    store(qkv_moment, qkv_moment_out)
    store(out_moment, out_moment_out)
    loads["factors"].wait()
    loads["up"].wait()
    up_new[...] = up_w[...].astype(f32) * shrink - step(2, math.sqrt(max(1.0, FF / D)))
    store(up_new, up_out)
    loads["down"].wait()
    down_new[...] = down_w[...].astype(f32) * shrink - step(3, 1.0).T
    store(down_new, down_out)
    loads["qkv"].wait()
    turned[...] = qkv_w[...].astype(f32).T
    rows = pl.ds(pl.multiple_of(qkv_skip, 32), qkv_cols)
    qkv_new[...] = turned[rows, :] * shrink - step(0, math.sqrt(3.0)).T[:qkv_cols]
    store(qkv_new, qkv_out)
    loads["out"].wait()
    turned[: out_w.shape[1], :] = out_w[...].astype(f32).T
    rows = pl.ds(pl.multiple_of(out_skip, 32), out_cols)
    out_new[...] = turned[rows, :] * shrink - step(1, 1.0).T[qkv_cols:]
    store(out_new, out_out)
    for copy in stores:
        copy.wait()


def finish(factors, sums, weights, olds, mixed, input_grad):
    shapes = [old.shape for old in olds]
    news = shapes[:3] + [shapes[3][::-1]]

    def wide(shape):
        return pltpu.VMEM(shape, f32)

    return pl.pallas_call(
        finish_kernel,
        out_shape=tuple(
            jax.ShapeDtypeStruct(shape, f32)
            for shape in [mixed.shape, input_grad.shape] + shapes + news
        ),
        in_specs=[ANY] * 12,
        out_specs=(ANY,) * 10,
        scratch_shapes=[
            pltpu.VMEM(factors.shape, bf16),
            pltpu.VMEM(sums.shape, bf16),
            pltpu.VMEM((D, 384), bf16),
            pltpu.VMEM((D, 256), bf16),
            pltpu.VMEM((D, UNIT), bf16),
            pltpu.VMEM((UNIT, D), bf16),
        ]
        + [wide(shape) for shape in shapes + news]
        + [
            wide((384, D)),
            pltpu.SemaphoreType.DMA((10,)),
            pltpu.SemaphoreType.DMA((10,)),
        ],
        compiler_params=pltpu.CompilerParams(vmem_limit_bytes=48 * MIB),
        name="finish",
    )(factors, sums, *weights, *olds, mixed, input_grad)


def swap(value, axis, bit):
    size = lax.axis_size(axis)
    return lax.ppermute(value, axis, [(i, i ^ bit) for i in range(size)])


def scatter_head(value, bit, position):
    half = value.shape[1] // 2
    mine = lax.dynamic_slice_in_dim(value, position * half, half, 1)
    other = lax.dynamic_slice_in_dim(value, (1 - position) * half, half, 1)
    return (mine.astype(f32) + swap(other, "head", bit).astype(f32)).astype(bf16)


def scatter_dp_pair(value, position):
    paired = value.reshape((value.shape[0] // 2, 2) + value.shape[1:])
    mine = lax.dynamic_index_in_dim(paired, position, 1, False)
    other = lax.dynamic_index_in_dim(paired, 1 - position, 1, False)
    return (mine.astype(f32) + swap(other, "dp", 1).astype(f32)).astype(bf16)


def scatter_dp_rest(value, place):
    ranks = value.shape[0]
    total = lax.dynamic_index_in_dim(value, place, 0, False).astype(f32)
    for step in range(1, ranks):
        sent = lax.dynamic_index_in_dim(value, place ^ step, 0, False)
        total = total + swap(sent, "dp", 2 * step).astype(f32)
    return total


def local(
    tokens,
    cotangent,
    qkv_weight,
    out_weight,
    up_weight,
    down_weight,
    vectors,
    qkv_moment,
    out_moment,
    up_moment,
    down_moment,
    adam_first,
    adam_second,
    bucket_class,
    row_lengths,
):
    n_dp = lax.axis_size("dp")
    n_head = lax.axis_size("head")
    dp_id = lax.axis_index("dp")
    head_id = lax.axis_index("head")
    core, side = head_id % 2, head_id // 2
    tok, width = tokens.shape
    hidden = up_weight.shape[1]
    half = width // 2
    qkv_cols, out_cols = qkv_moment.shape[1], out_moment.shape[1]
    shrink = 1.0 - muon_rate * muon_decay

    def weight_block(weight, cols, dim):
        return lax.dynamic_slice_in_dim(weight, dp_id * cols, cols, dim)

    block = head_id.astype(jnp.int32)[None]
    vec_len = vectors.shape[0] // n_dp
    if (n_dp, n_head, tok) == (8, 4, 256):
        mixed, input_grad, sums, vec = layer(
            bucket_class,
            row_lengths,
            tokens,
            cotangent,
            vectors,
            qkv_weight,
            out_weight,
            up_weight,
            down_weight,
        )
        grad_vec = vec[:VEC_BLOCK].reshape(vec_len)
        sums = sums.reshape(3, width, -1)
        olds = [qkv_moment.T, out_moment.T, up_moment, down_moment]
        mixed, input_grad, *results = finish(
            muon_factors(sums, *olds),
            sums,
            [qkv_weight, out_weight, up_weight, down_weight],
            olds,
            mixed,
            input_grad,
        )
        moments, new_weights = results[:4], results[4:]
        moments = [moments[0].T, moments[1].T, *moments[2:]]
        new_weights = [new_weights[0].T, new_weights[1].T, *new_weights[2:]]
    else:
        pieces = split_vectors(vectors, width, hidden)
        bias_query, bias_value, bias_out, gain_one, shift_one = pieces[:5]
        bias_up, bias_down, gain_two, shift_two = pieces[5:]
        bias_qkv = jnp.concatenate([bias_query, jnp.zeros_like(bias_query), bias_value])

        def column_half(value, which):
            return lax.dynamic_slice_in_dim(value, which * half, half, 1)

        qkv = (dot(tokens, qkv_weight, 1, 0) + bias_qkv).astype(bf16)
        other = swap(qkv[:, width:], "head", 1)
        attended = attend(block, bucket_class, row_lengths, qkv, other)
        attn_val = dot(attended, out_weight, 1, 0) + bias_out
        resid_one = tokens.astype(f32) + attn_val
        centre = resid_one - jnp.mean(resid_one, axis=-1, keepdims=True)
        rstd_one = lax.rsqrt(jnp.mean(centre * centre, axis=-1, keepdims=True) + norm_eps)
        zhat_one = centre * rstd_one
        normed_one = zhat_one * gain_one + shift_one
        normed_low = normed_one.astype(bf16)
        up_val = dot(normed_low, up_weight, 1, 0) + bias_up
        phi_cum = 0.5 * (1.0 + lax.erf(up_val * (0.5**0.5)))
        active_low = (up_val * phi_cum).astype(bf16)
        slope = phi_cum + up_val * jnp.exp(-0.5 * up_val * up_val) * (1.0 / math.sqrt(2.0 * math.pi))
        down_val = dot(active_low, down_weight, 1, 0) + bias_down
        resid_two = normed_one + down_val
        centre = resid_two - jnp.mean(resid_two, axis=-1, keepdims=True)
        rstd_two = lax.rsqrt(jnp.mean(centre * centre, axis=-1, keepdims=True) + norm_eps)
        zhat_two = centre * rstd_two
        mixed = zhat_two * gain_two + shift_two

        def norm_back(grad, gain, zhat, rstd):
            inner = grad * gain
            mean = jnp.mean(inner, axis=-1, keepdims=True)
            slant = jnp.mean(inner * zhat, axis=-1, keepdims=True)
            return (inner - mean - zhat * slant) * rstd, jnp.sum(grad * zhat, axis=0), jnp.sum(grad, axis=0)

        grad_two, grad_gain_two, grad_shift_two = norm_back(
            cotangent.astype(f32), gain_two, zhat_two, rstd_two
        )
        grad_down_low = grad_two.astype(bf16)
        grad_bias_down = jnp.sum(grad_down_low, axis=0, dtype=f32)

        x_id, z_id = dp_id % 2, dp_id // 2

        grad_up_low = (dot(grad_down_low, down_weight, 1, 1) * slope).astype(bf16)
        grad_bias_up = jnp.sum(grad_up_low, axis=0, dtype=f32)
        grad_normed = grad_two + dot(grad_up_low, up_weight, 1, 1)
        grad_one, grad_gain_one, grad_shift_one = norm_back(grad_normed, gain_one, zhat_one, rstd_one)
        grad_attn_low = grad_one.astype(bf16)
        grad_bias_out = jnp.sum(grad_attn_low, axis=0, dtype=f32)
        grad_heads = dot(grad_attn_low, out_weight, 1, 1).astype(bf16)
        grad_query, own, sent = attend_back(block, bucket_class, row_lengths, qkv, other, grad_heads)
        grad_kv = (own + swap(sent, "head", 1).astype(f32)).astype(bf16)
        grad_qkv = jnp.concatenate([grad_query, grad_kv], axis=1)
        grad_bias_qkv = jnp.sum(grad_qkv, axis=0, dtype=f32)
        input_grad = grad_one + dot(grad_qkv, qkv_weight, 1, 1)
        grad_vector = jnp.concatenate(
            [
                grad_bias_qkv[:width],
                grad_bias_qkv[2 * width :],
                grad_bias_out,
                grad_gain_one,
                grad_shift_one,
                grad_bias_up,
                grad_bias_down,
                grad_gain_two,
                grad_shift_two,
            ]
        )
        grad_vector = grad_vector + swap(grad_vector, "head", 1)
        wides = [active_low, grad_up_low, grad_attn_low, grad_qkv]
        narrows = [grad_down_low, normed_low, attended, tokens]

        def both_halves(value):
            return jnp.concatenate(
                [column_half(value, core), swap(column_half(value, 1 - core), "head", 1)], axis=0
            )

        def weight_grad(wide, narrow):
            wide = jnp.concatenate([wide, swap(wide, "head", 1)], axis=0)
            value = dot(wide, both_halves(narrow), 0, 0).astype(bf16)
            return value.reshape(n_dp, value.shape[0] // n_dp, half)

        def reduce_y_first(value):
            return scatter_dp_rest(scatter_dp_pair(scatter_head(value, 2, side), x_id), z_id)

        def reduce_x_first(value):
            return scatter_dp_rest(scatter_head(scatter_dp_pair(value, x_id), 2, side), z_id)

        def spread(value):
            value = value.astype(bf16)
            came = swap(value, "head", 2)
            value = jnp.concatenate(
                [jnp.where(side == 0, value, came), jnp.where(side == 0, came, value)], axis=0
            )
            came = swap(value, "head", 1)
            return jnp.concatenate(
                [jnp.where(core == 0, value, came), jnp.where(core == 0, came, value)], axis=1
            ).astype(f32)

        down_part, up_part, out_part, qkv_part = [
            weight_grad(wide, narrow) for wide, narrow in zip(wides, narrows)
        ]
        vec_rows = 16
        vec_part = grad_vector.reshape(n_dp, vec_len)
        vec_part = jnp.pad(vec_part, ((0, 0), (0, vec_rows * width - vec_len)))
        vec_part = vec_part.reshape(n_dp, vec_rows, width)
        vec_part = lax.dynamic_slice_in_dim(vec_part, core * half, half, 2).astype(bf16)
        down_new = spread(reduce_x_first(down_part))
        up_new = spread(reduce_y_first(up_part))
        tail_new = spread(
            reduce_y_first(jnp.concatenate([qkv_part, out_part, vec_part], axis=1))
        )
        grads = [
            tail_new[:qkv_cols].T,
            tail_new[qkv_cols : qkv_cols + out_cols].T,
            up_new.T,
            down_new.T,
        ]
        grad_vec = tail_new[qkv_cols + out_cols :].reshape(-1)[:vec_len]
        moments = [
            muon_keep * old + grad
            for old, grad in zip([qkv_moment, out_moment, up_moment, down_moment], grads)
        ]
        most = max(m.shape[1] for m in moments)
        padded = [jnp.pad(m, ((0, 0), (0, most - m.shape[1]))) for m in moments]
        chosen = padded[-1]
        for index in range(len(padded) - 2, -1, -1):
            chosen = jnp.where(head_id == index, padded[index], chosen)
        gram_mat = lax.dot_general(
            chosen, chosen, (((1,), (1,)), ((), ())), precision=lax.Precision.HIGH
        )
        own_factor = orthogonalize(lax.psum(gram_mat, "dp"), chosen)
        across = swap(own_factor, "head", 2)
        low_pair = jnp.where(side == 0, own_factor, across)
        high_pair = jnp.where(side == 0, across, own_factor)
        near_low = swap(low_pair, "head", 1)
        near_high = swap(high_pair, "head", 1)
        factors = [
            jnp.where(core == 0, low_pair, near_low),
            jnp.where(core == 0, near_low, low_pair),
            jnp.where(core == 0, high_pair, near_high),
            jnp.where(core == 0, near_high, high_pair),
        ]
        factors = [o[:, : m.shape[1]].astype(f32) for o, m in zip(factors, moments)]
        factors[3] = factors[3].T
        old_weights = [
            weight_block(qkv_weight, qkv_cols, 1),
            weight_block(out_weight, out_cols, 1),
            weight_block(up_weight, up_moment.shape[1], 1),
            weight_block(down_weight, down_moment.shape[1], 0),
        ]

        rates = (math.sqrt(3.0), 1.0, math.sqrt(max(1.0, hidden / width)), 1.0)
        new_weights = [
            old.astype(f32) * shrink - muon_rate * rate * factor
            for old, rate, factor in zip(old_weights, rates, factors)
        ]

    vec_old = lax.dynamic_slice_in_dim(vectors, dp_id * vec_len, vec_len, 0)
    vec_first = beta_first * adam_first + (1.0 - beta_first) * grad_vec
    vec_second = beta_second * adam_second + (1.0 - beta_second) * grad_vec * grad_vec
    first_hat = vec_first / (1.0 - beta_first**STEP)
    second_hat = vec_second / (1.0 - beta_second**STEP)
    vec_new = vec_old - adam_rate * first_hat / (jnp.sqrt(second_hat) + adam_eps)
    return (mixed, input_grad, *moments, *new_weights, vec_first, vec_second, vec_new)


def solution(mesh):
    tokens_spec = P(("dp", "head"), None)
    block_spec = P(None, "dp")
    return jax.shard_map(
        local,
        mesh=mesh,
        in_specs=(
            tokens_spec,
            tokens_spec,
            P(),
            P(),
            P(),
            P(),
            P(),
            block_spec,
            block_spec,
            block_spec,
            block_spec,
            P("dp"),
            P("dp"),
            P("dp"),
            P("dp", None),
        ),
        out_specs=(
            tokens_spec,
            tokens_spec,
            block_spec,
            block_spec,
            block_spec,
            block_spec,
            block_spec,
            block_spec,
            block_spec,
            P("dp", None),
            P("dp"),
            P("dp"),
            P("dp"),
        ),
        check_vma=False,
    )
```

```python
import functools
import itertools
import math

import jax
import jax.numpy as jnp
from jax import lax
from jax.experimental import pallas as pl
from jax.experimental.pallas import tpu as pltpu
from jax.sharding import PartitionSpec as P

D = 768
HEADS = 12
HEAD_DIM = 64
FF = 3072
BASE_LEN = 128
NS_STEPS = 5
STEP = 5
MAX_LEN = 512

f32 = jnp.float32
bf16 = jnp.bfloat16

norm_eps = 1e-12
masked_score = -1000000000.0
quintic_a = 3.4445
quintic_b = -4.775
quintic_c = 2.0315
muon_rate = 1.0
muon_decay = 0.01
muon_keep = 0.5
adam_rate = 0.2
beta_first = 0.9
beta_second = 0.999
adam_eps = 1e-08
MIB = 1024 * 1024


def dot(left, right, left_dim, right_dim):
    return lax.dot_general(
        left, right, (((left_dim,), (right_dim,)), ((), ())), preferred_element_type=f32
    )


def split_vectors(vectors, width, hidden):
    lengths_list = [width] * 5 + [hidden] + [width] * 3
    pieces = []
    offset = 0
    for length in lengths_list:
        pieces.append(vectors[offset : offset + length])
        offset = offset + length
    return pieces


def allowed_mask(class_ref, length_ref, block, tok):
    shift = class_ref[0] + int(math.log2(BASE_LEN))
    query_place = block * tok + lax.broadcasted_iota(jnp.int32, (tok, 1), 0)
    lane = lax.broadcasted_iota(jnp.int32, (1, 2 * tok), 1)
    own = lane < tok
    key_place = jnp.where(own, block * tok + lane, (block ^ 1) * tok + lane - tok)
    key_row = lax.shift_right_logical(key_place, jnp.broadcast_to(shift, key_place.shape))
    offset = key_place - lax.shift_left(key_row, jnp.broadcast_to(shift, key_place.shape))
    row_len = jnp.zeros_like(key_row)
    for slot in range(length_ref.shape[1]):
        row_len = jnp.where(key_row == slot, length_ref[0, slot], row_len)
    key_row = jnp.where(offset < row_len, key_row, -1)
    query_row = lax.shift_right_logical(query_place, jnp.broadcast_to(shift, query_place.shape))
    return query_row == key_row


def half_masks():
    lane = lax.broadcasted_iota(jnp.int32, (1, 2 * HEAD_DIM), 1)
    first = (lane < HEAD_DIM).astype(f32)
    return (first.astype(bf16), (1.0 - first).astype(bf16)), lane < HEAD_DIM


def head_prob(query, keys, allowed):
    score = jnp.where(allowed, dot(query, keys, 1, 1) * HEAD_DIM ** (-0.5), masked_score)
    exponent = jnp.exp(score - jnp.max(score, axis=-1, keepdims=True))
    return exponent / jnp.sum(exponent, axis=-1, keepdims=True)


def attend_kernel(block_ref, class_ref, length_ref, qkv_ref, other_ref, out_ref):
    tok = qkv_ref.shape[0]
    allowed = allowed_mask(class_ref, length_ref, block_ref[0], tok)
    masks, first = half_masks()
    for pair in range(HEADS // 2):
        cols = pl.ds(pair * 2 * HEAD_DIM, 2 * HEAD_DIM)
        kcols = pl.ds(D + pair * 2 * HEAD_DIM, 2 * HEAD_DIM)
        vcols = pl.ds(2 * D + pair * 2 * HEAD_DIM, 2 * HEAD_DIM)
        query = qkv_ref[:, cols]
        keys = jnp.concatenate([qkv_ref[:, kcols], other_ref[:, cols]], axis=0)
        values = jnp.concatenate([qkv_ref[:, vcols], other_ref[:, kcols]], axis=0)
        outs = []
        for mask in masks:
            prob = head_prob(query * mask, keys, allowed)
            outs.append(dot(prob.astype(bf16), values, 1, 0))
        out_ref[:, cols] = jnp.where(first, outs[0], outs[1]).astype(bf16)


def attend_back_kernel(
    block_ref, class_ref, length_ref, qkv_ref, other_ref, grad_ref, dq_ref, own_ref, send_ref
):
    tok = qkv_ref.shape[0]
    allowed = allowed_mask(class_ref, length_ref, block_ref[0], tok)
    masks, first = half_masks()
    scale = HEAD_DIM ** (-0.5)
    for pair in range(HEADS // 2):
        cols = pl.ds(pair * 2 * HEAD_DIM, 2 * HEAD_DIM)
        kcols = pl.ds(D + pair * 2 * HEAD_DIM, 2 * HEAD_DIM)
        vcols = pl.ds(2 * D + pair * 2 * HEAD_DIM, 2 * HEAD_DIM)
        query = qkv_ref[:, cols]
        keys = jnp.concatenate([qkv_ref[:, kcols], other_ref[:, cols]], axis=0)
        values = jnp.concatenate([qkv_ref[:, vcols], other_ref[:, kcols]], axis=0)
        grad = grad_ref[:, cols]
        dqs, dk, dv = [], None, None
        for mask in masks:
            head_query = query * mask
            head_grad = grad * mask
            prob = head_prob(head_query, keys, allowed)
            part_v = dot(prob.astype(bf16), head_grad, 0, 0)
            dprob = dot(head_grad, values, 1, 1)
            dscore = prob * (dprob - jnp.sum(prob * dprob, axis=-1, keepdims=True))
            dscore = dscore.astype(bf16)
            dqs.append(dot(dscore, keys, 1, 0))
            part_k = dot(dscore, head_query, 0, 0)
            dk = part_k if dk is None else dk + part_k
            dv = part_v if dv is None else dv + part_v
        dk = dk * scale
        dq_ref[:, cols] = (jnp.where(first, dqs[0], dqs[1]) * scale).astype(bf16)
        own_ref[:, cols] = dk[:tok]
        own_ref[:, kcols] = dv[:tok]
        send_ref[:, cols] = dk[tok:].astype(bf16)
        send_ref[:, kcols] = dv[tok:].astype(bf16)


SMEM = pl.BlockSpec(memory_space=pltpu.SMEM)
VMEM = pl.BlockSpec(memory_space=pltpu.VMEM)
ANY = pl.BlockSpec(memory_space=pl.ANY)


def attend(block, row_class, lengths, qkv, other):
    tok = qkv.shape[0]
    return pl.pallas_call(
        attend_kernel,
        out_shape=jax.ShapeDtypeStruct((tok, D), bf16),
        in_specs=[SMEM, SMEM, SMEM, VMEM, VMEM],
        out_specs=VMEM,
        compiler_params=pltpu.CompilerParams(vmem_limit_bytes=32 * MIB),
        name="attend",
    )(block, row_class, lengths, qkv, other)


def attend_back(block, row_class, lengths, qkv, other, grad):
    tok = qkv.shape[0]
    return pl.pallas_call(
        attend_back_kernel,
        out_shape=(
            jax.ShapeDtypeStruct((tok, D), bf16),
            jax.ShapeDtypeStruct((tok, 2 * D), f32),
            jax.ShapeDtypeStruct((tok, 2 * D), bf16),
        ),
        in_specs=[SMEM, SMEM, SMEM, VMEM, VMEM, VMEM],
        out_specs=(VMEM, VMEM, VMEM),
        compiler_params=pltpu.CompilerParams(vmem_limit_bytes=32 * MIB),
        name="attend_back",
    )(block, row_class, lengths, qkv, other, grad)


CENTRES = (0.0, 0.0, 0.0, 0.8, 0.8)
TILE = 256
SUB = 128


def sub_blocks(size):
    count = size // SUB
    return [(i, j) for i in range(count) for j in range(i, count)]


def newton_schulz(gram, moment, e, f, g, eb, fb, gb, yy, y, emit):
    size = e.shape[0]
    tiles = [slice(i * TILE, (i + 1) * TILE) for i in range(size // TILE)]

    def unit(rows):
        row_id = rows.start + lax.broadcasted_iota(jnp.int32, (TILE, size), 0)
        col_id = lax.broadcasted_iota(jnp.int32, (TILE, size), 1)
        return (row_id == col_id).astype(f32)

    diagonal = jnp.zeros((TILE, size), f32)
    for rows in tiles:
        diagonal = diagonal + gram[rows, :] * unit(rows)
    trace = jnp.sum(jnp.sum(diagonal, axis=0, keepdims=True), axis=1, keepdims=True)
    factor = 1.0 / (jnp.sqrt(trace) + 1e-07)
    square_factor = factor * factor
    for rows in tiles:
        value = gram[rows, :] * square_factor
        e[rows, :] = value
        eb[rows, :] = value.astype(bf16)
        value = moment[rows, :] * factor
        y[rows, :] = value
        yy[0, rows, :] = value.astype(bf16)

    def one_step(centre, after, now, then, last=False):
        keep = quintic_a + quintic_b * centre + quintic_c * centre * centre
        linear = quintic_b + 2.0 * quintic_c * centre
        for rows in tiles:
            value = linear * e[rows, :] + quintic_c * dot(eb[rows, :], eb[...], 1, 0)
            fb[rows, :] = value.astype(bf16)
            if centre:
                f[rows, :] = value
        for rows in tiles:
            value = keep * y[rows, :] + dot(fb[rows, :], now[...], 1, 0)
            if last:
                emit(rows, value.astype(bf16))
            else:
                y[rows, :] = value
                then[rows, :] = value.astype(bf16)
        if last:
            return
        for rows in tiles:
            value = keep * e[rows, :] + dot(eb[rows, :], fb[...], 1, 0)
            if centre:
                value = value + centre * f[rows, :]
            g[rows, :] = value
            gb[rows, :] = value.astype(bf16)
        for rows in tiles:
            value = keep * g[rows, :] + dot(gb[rows, :], fb[...], 1, 0)
            if centre:
                value = value + (centre * keep) * f[rows, :]
            shift = centre * keep * keep - after
            if not isinstance(shift, float) or shift:
                value = value + shift * unit(rows)
            e[rows, :] = value
            eb[rows, :] = value.astype(bf16)

    plain = sum(centre == 0.0 for centre in CENTRES)

    def plain_step(step, carry):
        after = jnp.where(step == plain - 1, CENTRES[plain], 0.0)
        one_step(0.0, after, yy.at[step % 2], yy.at[(step + 1) % 2])
        return carry

    lax.fori_loop(0, plain, plain_step, 0)
    for step in range(plain, NS_STEPS):
        last = step + 1 == NS_STEPS
        after = 0.0 if last else CENTRES[step + 1]
        one_step(CENTRES[step], after, yy.at[step % 2], yy.at[(step + 1) % 2], last)


def ortho_kernel(gram, moment, out, *scratch):
    def emit(rows, value):
        out[rows, :] = value

    newton_schulz(gram, moment, *scratch, emit)


def ortho_scratch(size, cols):
    square, square_low = pltpu.VMEM((size, size), f32), pltpu.VMEM((size, size), bf16)
    wide_low = pltpu.VMEM((2, size, cols), bf16)
    return [square] * 3 + [square_low] * 3 + [wide_low, pltpu.VMEM((size, cols), f32)]


def orthogonalize(gram_mat, moment):
    size, cols = moment.shape
    return pl.pallas_call(
        ortho_kernel,
        out_shape=jax.ShapeDtypeStruct((size, cols), bf16),
        in_specs=[VMEM, VMEM],
        out_specs=VMEM,
        scratch_shapes=ortho_scratch(size, cols),
        compiler_params=pltpu.CompilerParams(vmem_limit_bytes=48 * MIB),
        name="ortho",
    )(gram_mat, moment)


MESH = pl.DeviceIdType.MESH
PIECE = 48
SIDE = 192
UNIT = 2 * SIDE
HALF = D // 2
LANES = 128
VEC_BLOCK = 9
ROWS = 16
CHUNKS = (
    (0, 0, 64, "nfyx"),
    (0, 64, 64, "xynf"),
    (0, 128, 64, "yxnf"),
    (1, 0, 64, "ynxf"),
    (1, 64, 64, "nxyf"),
    (1, 128, 64, "xynf"),
    (2, 0, 48, "xynf"),
    (2, 48, 48, "nxyf"),
    (2, 96, 48, "yxnf"),
    (2, 144, 32, "xynf"),
    (2, 176, 16, "xfyn"),
)
CHUNK_PLAN = (
    (0, 1, 2),
    (),
    (),
    (),
    (),
    (3, 5, 4),
    (0, 1, 2),
    (),
    (),
    (),
    (0, 1, 2, 4, 5, 3),
    (),
    (),
    (0, 7, 8, 10, 9, 6),
    (
        1, 4, 2, 5, 0, 1, 10, 4, 0, 2, 0, 1, 9, 1, 3, 2, 5, 10, 4, 8, 2, 6,
        10, 5, 9, 3, 4, 10, 7, 4, 8, 10, 5, 9, 3, 10, 5, 6, 9, 8, 7, 3, 9, 6,
        3, 9, 8, 7, 8, 6, 8, 7, 6, 7, 6, 7,
    ),
)
BIAS_QUERY, BIAS_VALUE, BIAS_OUT, GAIN_ONE, SHIFT_ONE, BIAS_UP = (i * D for i in range(6))
BIAS_DOWN, GAIN_TWO, SHIFT_TWO = (BIAS_UP + FF + i * D for i in range(3))


def position():
    dp_id, head_id = lax.axis_index("dp"), lax.axis_index("head")
    z, x = dp_id // 2, dp_id % 2
    y, core = head_id // 2, head_id % 2
    return z, x, y, core


def device(z, x, y, core):
    return (2 * z + x, 2 * y + core)


def flip_z(z, step):
    high, low = z // 2, z % 2
    high = 1 - high if step // 2 else high
    low = 1 - low if step % 2 else low
    return 2 * high + low


def greet(others):
    barrier = pltpu.get_barrier_semaphore()
    for other in others:
        pl.semaphore_signal(barrier, inc=1, device_id=other, device_id_type=MESH)
    return lambda: pl.semaphore_wait(barrier, len(others))


def by_rows(count, body, init=None, together=4):
    def step(index, carry):
        for part in range(together):
            start = (index * together + part) * ROWS
            carry = body(pl.ds(pl.multiple_of(start, ROWS), ROWS), carry)
        return carry

    return lax.fori_loop(0, count // (ROWS * together), step, init)


def row_mean(value):
    return jnp.sum(value, axis=-1, keepdims=True) * (1.0 / D)


def fold(value):
    return jnp.sum(value.reshape(value.shape[0] // 8, 8, value.shape[1]), axis=0)


def column_sum(value):
    return jnp.sum(value, axis=0, keepdims=True)


def normal_parts(value):
    size = jnp.abs(value)
    decay = jnp.exp(-0.5 * value * value)
    below = 1.0 + (0.3275911 * 0.5**0.5) * size
    t = pl.reciprocal(below, approx=True)
    t = t * (2.0 - below * t)
    series = t * (1.061405429 * 0.5)
    for term in (-1.453152027, 1.421413741, -0.284496736, 0.254829592):
        series = (series + term * 0.5) * t
    tail = series * decay
    return jnp.where(value < 0.0, tail, 1.0 - tail), decay * (1.0 / math.sqrt(2.0 * math.pi))


def transposed(value):
    side = 2 * LANES
    row_id = lax.broadcasted_iota(jnp.int32, (side, side), 0)
    unit = (row_id == lax.broadcasted_iota(jnp.int32, (side, side), 1)).astype(f32).astype(bf16)
    blocks = []
    for start in range(0, value.shape[1], side):
        block = value[:, start : start + side]
        size = block.shape[1]
        blocks.append(dot(unit[:size, :size], block, 1, 1).astype(bf16))
    return jnp.concatenate(blocks, axis=0)


def layer_kernel(
    row_class,
    lengths,
    tokens,
    cotangent,
    vectors,
    qkv_hbm,
    out_hbm,
    up_hbm,
    down_hbm,
    mixed_hbm,
    grad_hbm,
    sums_hbm,
    vec_sum,
    mixed,
    input_grad,
    sums,
    qkv_w,
    out_w,
    up_w,
    down_w,
    query,
    query_turned,
    keys_values,
    keys_turned,
    prob,
    attended,
    normed_low,
    grad_down,
    grad_attn,
    narrow_tokens,
    narrow_attended,
    narrow_normed,
    narrow_grad,
    active,
    grad_up,
    attn_turned,
    qkv_turned,
    exchanged,
    grad_heads,
    heads_turned,
    slope,
    normed_one,
    zhat_one,
    rstd_one,
    grad_two,
    work,
    vec,
    vec_core,
    vec_y,
    vec_x,
    vec_z,
    part,
    came_one,
    came_two,
    came_three,
    came_four,
    load_sem,
    store_sem,
    pair_send,
    pair_recv,
    send_sem,
    recv_sem,
):
    grad_one = normed_one
    z, x, y, core = position()
    tok = tokens.shape[0]
    thirds = [slice(index * D, (index + 1) * D) for index in range(3)]
    loads = {
        name: pltpu.make_async_copy(source, target, load_sem.at[index])
        for index, (name, source, target) in enumerate(
            (
                ("key", qkv_hbm.at[:, thirds[1]], qkv_w.at[:, thirds[1]]),
                ("value", qkv_hbm.at[:, thirds[2]], qkv_w.at[:, thirds[2]]),
                ("query", qkv_hbm.at[:, thirds[0]], qkv_w.at[:, thirds[0]]),
                ("out", out_hbm, out_w),
                ("up", up_hbm, up_w),
                ("down", down_hbm, down_w),
            )
        )
    }
    for name in ("key", "value", "query"):
        loads[name].start()
    stores = []

    def store(source, target):
        stores.append(pltpu.make_async_copy(source, target, store_sem.at[len(stores)]))
        stores[-1].start()

    beyond = device(z, x, 1 - y, core)
    beside = device(z, 1 - x, y, core)
    partner = device(z, x, y, 1 - core)
    along = [device(flip_z(z, step), x, y, core) for step in (1, 2, 3)]
    all_here = greet([beyond, beside, partner] + along)
    started = []

    def remote(source, target, send_at, recv_at, other):
        copy = pltpu.make_async_remote_copy(
            src_ref=source,
            dst_ref=target,
            send_sem=send_at,
            recv_sem=recv_at,
            device_id=other,
            device_id_type=MESH,
        )
        copy.start()
        started.append(copy)
        return copy

    pair_count = []

    def to_partner(source, target):
        slot = len(pair_count)
        pair_count.append(slot)
        return remote(source, target, pair_send.at[slot], pair_recv.at[slot], partner)

    own_half = pl.ds(pl.multiple_of(core * HALF, HALF), HALF)
    other_half = pl.ds(pl.multiple_of((1 - core) * HALF, HALF), HALF)

    def span(start, length=D):
        return vectors[0:1, start : start + length]

    def put_vec(start, value):
        for index in range(value.shape[1] // LANES):
            block, row = divmod(start // LANES + index, VEC_BLOCK)
            vec[block, row : row + 1, :] = value[:, index * LANES : (index + 1) * LANES]

    vec[...] = jnp.zeros_like(vec)

    own_rows = pl.ds(0, tok)
    far_rows = pl.ds(tok, tok)
    own_lanes, far_lanes = own_rows, far_rows

    def share_half(value, narrow):
        narrow[own_rows, :] = value[:, own_half]
        return to_partner(value.at[:, other_half], narrow.at[far_rows])

    kv_came = []
    for name, index, start in (("key", 1, None), ("value", 2, BIAS_VALUE)):
        loads[name].wait()
        value = dot(tokens[...], qkv_w[:, thirds[index]], 1, 0)
        if start is not None:
            value = value + span(start)
        cols = slice((index - 1) * D, index * D)
        keys_values[own_rows, cols] = value.astype(bf16)
        if index == 1:
            all_here()
            for name in ("out", "up", "down"):
                loads[name].start()
        kv_came.append(
            to_partner(keys_values.at[own_rows, cols], keys_values.at[far_rows, cols])
        )
    loads["query"].wait()
    value = dot(tokens[...], qkv_w[:, thirds[0]], 1, 0) + span(BIAS_QUERY)
    query[...] = value.astype(bf16)
    query_turned[...] = transposed(query[...])
    allowed = allowed_mask(row_class, lengths, 2 * y + core, tok)
    masks, first = half_masks()
    tokens_came = share_half(tokens, narrow_tokens)
    for copy in kv_came:
        copy.wait_recv()

    scale = HEAD_DIM ** (-0.5)

    def lanes_at(start):
        return pl.ds(pl.multiple_of(start, LANES), LANES)

    def attend_pair(pair, carry):
        cols = lanes_at(pair * LANES)
        keys = keys_values[:, cols]
        values = keys_values[:, lanes_at(D + pair * LANES)]
        outs = []
        for side, mask in enumerate(masks):
            score = dot(query[:, cols] * (mask * scale), keys, 1, 1)
            score = jnp.where(allowed, score, masked_score)
            exponent = jnp.exp(score - jnp.max(score, axis=-1, keepdims=True))
            chance = exponent * (1.0 / jnp.sum(exponent, axis=-1, keepdims=True))
            chance = chance.astype(bf16)
            prob[2 * pair + side] = chance
            outs.append(dot(chance, values, 1, 0))
        attended[:, cols] = jnp.where(first, outs[0], outs[1]).astype(bf16)
        return carry

    lax.fori_loop(0, HEADS // 2, attend_pair, 0)
    attended_came = share_half(attended, narrow_attended)

    loads["out"].wait()
    work[...] = dot(attended[...], out_w[...], 1, 0)

    def norm_one(rows, carry):
        value = tokens[rows, :].astype(f32) + (work[rows, :] + span(BIAS_OUT))
        centre = value - row_mean(value)
        rstd = lax.rsqrt(row_mean(centre * centre) + norm_eps)
        zhat = centre * rstd
        normed = zhat * span(GAIN_ONE) + span(SHIFT_ONE)
        zhat_one[rows, :] = zhat
        rstd_one[rows, :] = jnp.broadcast_to(rstd, (ROWS, LANES))
        normed_one[rows, :] = normed
        normed_low[rows, :] = normed.astype(bf16)
        return carry

    by_rows(tok, norm_one)
    normed_came = share_half(normed_low, narrow_normed)

    loads["up"].wait()
    for tile in range(FF // D):
        cols = slice(tile * D, (tile + 1) * D)
        work[...] = dot(normed_low[...], up_w[:, cols], 1, 0)

        def gelu(rows, carry):
            value = work[rows, :] + span(BIAS_UP + cols.start)
            chance, density = normal_parts(value)
            active[rows, cols] = (value * chance).astype(bf16)
            slope[rows, cols] = chance + value * density
            return carry

        by_rows(tok, gelu)
    active_came = to_partner(active.at[own_rows], active.at[far_rows])
    loads["down"].wait()
    work[...] = dot(active[own_rows, :], down_w[...], 1, 0)

    def norm_two(rows, carry):
        value = normed_one[rows, :] + (work[rows, :] + span(BIAS_DOWN))
        centre = value - row_mean(value)
        rstd = lax.rsqrt(row_mean(centre * centre) + norm_eps)
        zhat = centre * rstd
        mixed[rows, :] = zhat * span(GAIN_TWO) + span(SHIFT_TWO)
        grad = cotangent[rows, :].astype(f32)
        inner = grad * span(GAIN_TWO)
        grad_in = (inner - row_mean(inner) - zhat * row_mean(inner * zhat)) * rstd
        grad_two[rows, :] = grad_in
        low = grad_in.astype(bf16)
        grad_down[rows, :] = low
        gain, shift, bias = carry
        return gain + fold(grad * zhat), shift + fold(grad), bias + fold(low.astype(f32))

    zero = jnp.zeros((8, D), f32)
    gain, shift, bias = by_rows(tok, norm_two, (zero, zero, zero))
    store(mixed, mixed_hbm)
    put_vec(GAIN_TWO, column_sum(gain))
    put_vec(SHIFT_TWO, column_sum(shift))
    put_vec(BIAS_DOWN, column_sum(bias))
    grad_down_came = share_half(grad_down, narrow_grad)
    keys_turned[...] = transposed(keys_values[:, :D])

    here = {"f": z // 2, "n": z % 2, "x": x, "y": y}
    across = {"f": along[1], "n": along[0], "x": beside, "y": beyond}

    class Chain:
        def __init__(self, index):
            matrix, start, rows, order = CHUNKS[index]
            self.index, self.order, self.stage = index, order, 0
            self.rows = pl.ds(start, rows)
            self.own = part.at[matrix]
            self.came = [ref.at[matrix] for ref in (came_one, came_two, came_three, came_four)]
            self.final = sums.at[matrix]

        def cells(self, free, flipped=None):
            return tuple(
                slice(None) if name in free else 1 - here[name] if name == flipped else here[name]
                for name in "fnxy"
            ) + (self.rows,)

        def send(self, source, target, other):
            sems = (send_sem.at[self.index, self.stage], recv_sem.at[self.index, self.stage])
            self.copy = remote(source, target, *sems, other)

        def advance(self):
            stage, order = self.stage, self.order
            if stage:
                self.copy.wait_recv()
            if 1 <= stage <= 4:
                free = order[stage:]
                for choice in itertools.product((0, 1), repeat=len(free)):
                    taken = dict(zip(sorted(free, key="fnxy".index), choice))
                    at = tuple(taken.get(name, here[name]) for name in "fnxy") + (self.rows,)
                    value = self.own[at] + self.came[stage - 1][choice + (self.rows,)]
                    if stage == 4:
                        self.final[core, y, self.rows] = value
                    else:
                        self.own[at] = value
            if stage < 4:
                name = order[stage]
                source = self.own.at[self.cells(order[stage + 1 :], name)]
                target = self.came[stage].at[(slice(None),) * (3 - stage) + (self.rows,)]
                self.send(source, target, across[name])
            elif stage == 4:
                block = self.final.at[core, y, self.rows]
                self.send(block, block, beyond)
            elif stage == 5:
                block = self.final.at[core, :, self.rows]
                self.send(block, block, partner)
            self.stage += 1

    chains = [Chain(index) for index in range(len(CHUNKS))]
    plan = iter(CHUNK_PLAN)

    def pump():
        for index in next(plan):
            chains[index].advance()

    def feed_forward(matrix, narrow, wide):
        left = transposed(narrow[...])

        def block(index, carry):
            cols = pl.ds(pl.multiple_of(index * UNIT, UNIT), UNIT)
            value = dot(left, wide[:, cols], 1, 0).astype(bf16)
            for side in range(2):
                part[matrix, index // 4, index // 2 % 2, index % 2, side] = value[
                    side * SIDE : (side + 1) * SIDE
                ]
            return carry

        lax.fori_loop(0, 8, block, 0)

    def projections(matrix, turned, narrow, width, offset, between=None):
        for tile in range(turned.shape[0] // UNIT):
            if between and tile % 2 == 0:
                between()
            value = dot(turned[tile * UNIT : (tile + 1) * UNIT, :], narrow[...], 1, 0).astype(bf16)
            for start in range(0, UNIT, PIECE):
                block, row = divmod(tile * UNIT + start, width)
                side, row = divmod(offset + row, SIDE)
                cell = (matrix, block // 4, block // 2 % 2, block % 2, side)
                part[cell + (pl.ds(row, PIECE),)] = value[start : start + PIECE]

    grad_down_came.wait_recv()
    active_came.wait_recv()
    feed_forward(0, narrow_grad, active)

    for tile in range(FF // D):
        pump()
        cols = slice(tile * D, (tile + 1) * D)
        work[...] = dot(grad_down[...], down_w[cols, :], 1, 1)

        def gelu_back(rows, carry):
            low = (work[rows, :] * slope[rows, cols]).astype(bf16)
            grad_up[rows, cols] = low
            return carry + fold(low.astype(f32))

        put_vec(BIAS_UP + cols.start, column_sum(by_rows(tok, gelu_back, zero)))
    grad_up_came = to_partner(grad_up.at[own_rows], grad_up.at[far_rows])
    pump()
    normed_came.wait_recv()
    grad_up_came.wait_recv()
    feed_forward(1, narrow_normed, grad_up)
    pump()

    work[...] = dot(grad_up[own_rows, :], up_w[...], 1, 1)

    def norm_one_back(rows, carry):
        grad = grad_two[rows, :] + work[rows, :]
        zhat = zhat_one[rows, :]
        inner = grad * span(GAIN_ONE)
        grad_in = inner - row_mean(inner) - zhat * row_mean(inner * zhat)
        grad_in = grad_in * rstd_one[rows, 0:1]
        grad_one[rows, :] = grad_in
        low = grad_in.astype(bf16)
        grad_attn[rows, :] = low
        gain, shift, bias = carry
        return gain + fold(grad * zhat), shift + fold(grad), bias + fold(low.astype(f32))

    gain, shift, bias = by_rows(tok, norm_one_back, (zero, zero, zero))
    put_vec(GAIN_ONE, column_sum(gain))
    put_vec(SHIFT_ONE, column_sum(shift))
    put_vec(BIAS_OUT, column_sum(bias))
    grad_heads[...] = dot(grad_attn[...], out_w[...], 1, 1).astype(bf16)
    heads_turned[...] = dot(out_w[...], grad_attn[...], 1, 1).astype(bf16)

    half_lanes = LANES // 2

    def attend_pair_back(pair, carry):
        cols = lanes_at(pair * LANES)
        values = keys_values[:, lanes_at(D + pair * LANES)]
        for side, mask in enumerate(masks):
            start = pl.multiple_of(pair * LANES + side * half_lanes, half_lanes)
            rows = pl.ds(start, half_lanes)
            low_chance = prob[2 * pair + side]
            chance = low_chance.astype(f32)
            grad_chance = dot(grad_heads[:, cols] * mask, values, 1, 1)
            mean = jnp.sum(chance * grad_chance, axis=-1, keepdims=True)
            grad_score = (chance * (grad_chance - mean)).astype(bf16)
            values_grad = dot(heads_turned[rows, :], low_chance, 1, 0).astype(bf16)
            keys_grad = (dot(query_turned[rows, :], grad_score, 1, 0) * scale).astype(bf16)
            query_grad = (dot(keys_turned[rows, :], grad_score, 1, 1) * scale).astype(bf16)
            blocks = (
                query_grad,
                keys_grad[:, :tok],
                values_grad[:, :tok],
                keys_grad[:, tok:],
                values_grad[:, tok:],
            )
            for index, value in enumerate(blocks):
                start = index * LANES + side * half_lanes
                exchanged[0, pair, start : start + half_lanes, :] = value
        return carry

    half_came = []
    for half in range(2):
        pump()
        pairs = pl.ds(half * HEADS // 4, HEADS // 4)
        lax.fori_loop(half * HEADS // 4, (half + 1) * HEADS // 4, attend_pair_back, 0)
        half_came.append(to_partner(exchanged.at[0, pairs], exchanged.at[1, pairs]))
    pump()
    attn_turned[:, own_lanes] = transposed(grad_attn[...])
    grad_attn_came = to_partner(attn_turned.at[:, own_lanes], attn_turned.at[:, far_lanes])

    for pair in range(HEADS // 2):
        if pair % (HEADS // 4) == 0:
            half_came[pair // (HEADS // 4)].wait_recv()
        for who, lanes in enumerate((own_lanes, far_lanes)):
            start = pair * LANES
            mine, theirs = exchanged.at[who, pair], exchanged.at[1 - who, pair]
            qkv_turned[start : start + LANES, lanes] = mine[:LANES]
            for index in (1, 2):
                rows = slice(index * LANES, (index + 1) * LANES)
                sent = slice((index + 2) * LANES, (index + 3) * LANES)
                value = mine[rows].astype(f32) + theirs[sent].astype(f32)
                start = index * D + pair * LANES
                qkv_turned[start : start + LANES, lanes] = value.astype(bf16)
    pump()
    tokens_came.wait_recv()
    projections(2, qkv_turned, narrow_tokens, 3 * D // 8, 0, pump)
    attended_came.wait_recv()
    grad_attn_came.wait_recv()
    projections(2, attn_turned, narrow_attended, D // 8, 3 * D // 8)
    pump()

    ones = jnp.ones((8, tok), bf16)
    for start, rows in ((BIAS_QUERY, slice(0, D)), (BIAS_VALUE, slice(2 * D, 3 * D))):
        put_vec(start, dot(ones, qkv_turned[rows, own_lanes], 1, 1)[0:1])
    vec_came = to_partner(vec, vec_core)
    value = dot(qkv_w[...], qkv_turned[:, own_lanes], 1, 0)
    input_grad[...] = grad_one[...] + value.T
    store(input_grad, grad_hbm)

    vec_slots = [(send_sem.at[len(CHUNKS), i], recv_sem.at[len(CHUNKS), i]) for i in range(5)]

    def vec_steps():
        vec_came.wait_recv()
        vec_core[...] = vec[...] + vec_core[...]
        copy = remote(vec_core, vec_y, *vec_slots[0], beyond)
        yield
        copy.wait_recv()
        for i in range(4):
            vec_x[0, i] = vec_core[2 * i + x] + vec_y[2 * i + x]
            vec_x[1, i] = vec_core[2 * i + 1 - x] + vec_y[2 * i + 1 - x]
        copy = remote(vec_x.at[1], vec_x.at[2], *vec_slots[1], beside)
        yield
        copy.wait_recv()
        vec_x[0] = vec_x[0] + vec_x[2]
        copies = [
            remote(
                vec_x.at[0, flip_z(z, step)],
                vec_z.at[step - 1],
                *vec_slots[1 + step],
                along[step - 1],
            )
            for step in (1, 2, 3)
        ]
        yield
        total = vec_x[0, z]
        for step, copy in enumerate(copies):
            copy.wait_recv()
            total = total + vec_z[step]
        vec_sum[...] = total
        yield

    steps = vec_steps()
    left = [sum(chunk[0] == matrix for chunk in CHUNKS) for matrix in range(3)]
    for turn, index in enumerate(next(plan)):
        chains[index].advance()
        matrix = CHUNKS[index][0]
        left[matrix] -= chains[index].stage == 7
        if not left[matrix]:
            store(sums.at[matrix], sums_hbm.at[matrix])
            left[matrix] = -1
        if turn % 10 == 9 and turn < 40:
            next(steps)
    for copy in stores:
        copy.wait()
    for copy in started:
        copy.wait_send()


def layer(row_class, lengths, tokens, cotangent, vectors, qkv_w, out_w, up_w, down_w):
    tok = tokens.shape[0]
    side = (SIDE, UNIT)

    def low(*dims):
        return pltpu.VMEM(dims, bf16)

    def wide(*dims):
        return pltpu.VMEM(dims, f32)

    return pl.pallas_call(
        layer_kernel,
        out_shape=(
            jax.ShapeDtypeStruct((tok, D), f32),
            jax.ShapeDtypeStruct((tok, D), f32),
            jax.ShapeDtypeStruct((3, 2, 2) + side, bf16),
            jax.ShapeDtypeStruct((16, LANES), f32),
        ),
        in_specs=[SMEM, SMEM, VMEM, VMEM, VMEM] + [ANY] * 4,
        out_specs=(ANY, ANY, ANY, VMEM),
        scratch_shapes=[
            wide(tok, D),
            wide(tok, D),
            low(3, 2, 2, *side),
            low(D, 3 * D),
            low(D, D),
            low(D, FF),
            low(FF, D),
            low(tok, D),
            low(D, tok),
            low(2 * tok, 2 * D),
            low(D, 2 * tok),
            low(HEADS, tok, 2 * tok),
            low(tok, D),
            low(tok, D),
            low(tok, D),
            low(tok, D),
            low(2 * tok, HALF),
            low(2 * tok, HALF),
            low(2 * tok, HALF),
            low(2 * tok, HALF),
            low(2 * tok, FF),
            low(2 * tok, FF),
            low(D, 2 * tok),
            low(3 * D, 2 * tok),
            low(2, HEADS // 2, 5 * LANES, tok),
            low(tok, D),
            low(D, tok),
            wide(tok, FF),
            wide(tok, D),
            wide(tok, D),
            wide(tok, LANES),
            wide(tok, D),
            wide(tok, D),
            wide(8, 16, LANES),
            wide(8, 16, LANES),
            wide(8, 16, LANES),
            wide(3, 4, 16, LANES),
            wide(3, 16, LANES),
            low(3, 2, 2, 2, 2, *side),
            low(3, 2, 2, 2, *side),
            low(3, 2, 2, *side),
            low(3, 2, *side),
            low(3, *side),
            pltpu.SemaphoreType.DMA((6,)),
            pltpu.SemaphoreType.DMA((5,)),
            pltpu.SemaphoreType.DMA((12,)),
            pltpu.SemaphoreType.DMA((12,)),
            pltpu.SemaphoreType.DMA((len(CHUNKS) + 1, 6)),
            pltpu.SemaphoreType.DMA((len(CHUNKS) + 1, 6)),
        ],
        compiler_params=pltpu.CompilerParams(
            vmem_limit_bytes=63 * MIB, collective_id=0, has_side_effects=True
        ),
        name="layer",
    )(row_class, lengths, tokens, cotangent, vectors[None, :], qkv_w, out_w, up_w, down_w)


GRAM_AXES = ("far", "near", "x")
GRAM_GROUPS = (
    (1, "xnf"),
    (2, "xnf"),
    (2, "xnf"),
    (3, "xnf"),
    (3, "nxf"),
    (3, "fxn"),
    (3, "nxf"),
    (2, "xnf"),
    (1, "xnf"),
    (1, "xnf"),
)
GRAM_PLAN = (
    6, 0, 9, 2, 5, 4, 7, 3, 0, 9, 6, 8, 2, 0, 9, 1, 0, 7, 9, 8, 2, 6,
    0, 5, 4, 3, 1, 8, 2, 7, 0, 6, 9, 5, 4, 8, 0, 2, 7, 1, 8, 9, 6, 3,
    5, 4, 7, 1, 8, 6, 2, 9, 3, 5, 8, 1, 4, 7, 2, 3, 5, 1, 4, 6, 7, 3,
    1, 5, 3, 4,
)


def muon_kernel(
    sums,
    qkv_hbm,
    out_hbm,
    up_hbm,
    down_hbm,
    factors,
    own_sum,
    qkv_old,
    out_old,
    old,
    moment,
    out,
    part,
    came_one,
    came_two,
    came_three,
    high,
    low,
    load_sem,
    send_sem,
    recv_sem,
    share_send,
    share_recv,
    *ortho,
):
    z, x, y, core = position()
    here = {"far": z // 2, "near": z % 2, "x": x}
    others = {
        "far": device(flip_z(z, 2), x, y, core),
        "near": device(flip_z(z, 1), x, y, core),
        "x": device(z, 1 - x, y, core),
    }
    beyond = device(z, x, 1 - y, core)
    partner = device(z, x, y, 1 - core)
    own = 2 * y + core
    all_here = greet(list(others.values()) + [beyond, partner])

    def load_two(source, target, matrix):
        loads = [
            pltpu.make_async_copy(source, target, load_sem.at[0]),
            pltpu.make_async_copy(sums.at[matrix], own_sum, load_sem.at[1]),
        ]
        for load in loads:
            load.start()
        for load in loads:
            load.wait()

    def from_turned(source, target, skip):
        load_two(source, target, 2)
        rows = target.shape[0]
        moment[...] = jnp.zeros_like(moment)
        for half in range(2):
            cols = slice(half * HALF, (half + 1) * HALF)
            start = half * UNIT + skip
            value = own_sum[start : start + rows, :].astype(f32)
            moment[cols, skip : skip + rows] = (muon_keep * target[:, cols] + value).T

    @pl.when(own == 0)
    def _():
        from_turned(qkv_hbm, qkv_old, 0)

    @pl.when(own == 1)
    def _():
        from_turned(out_hbm, out_old, qkv_old.shape[0])

    @pl.when(own == 2)
    def _():
        load_two(up_hbm, old, 1)
        moment[...] = muon_keep * old[...] + own_sum[...].astype(f32)

    @pl.when(own == 3)
    def _():
        load_two(down_hbm, old, 0)
        moment[...] = muon_keep * old[...] + own_sum[...].astype(f32)

    all_here()
    blocks = sub_blocks(moment.shape[0])
    starts = [sum(count for count, _ in GRAM_GROUPS[:group]) for group in range(len(GRAM_GROUPS))]
    high[...] = moment[...].astype(bf16)
    low[...] = (moment[...] - high[...].astype(f32)).astype(bf16)
    started = []

    def product(index):
        i, j = blocks[index]
        left, right = pl.ds(i * SUB, SUB), pl.ds(j * SUB, SUB)
        total = dot(high[left, :], high[right, :], 1, 1)
        total = total + dot(high[left, :], low[right, :], 1, 1)
        total = total + dot(low[left, :], high[right, :], 1, 1)
        rows = SUB // 8
        for owner in range(8):
            cell = (owner // 4, owner // 2 % 2, owner % 2)
            part[cell + (index,)] = total[
                owner * rows : (owner + 1) * rows
            ]

    def send(source, target, group, slot, axis):
        copy = pltpu.make_async_remote_copy(
            src_ref=source,
            dst_ref=target,
            send_sem=send_sem.at[group, slot],
            recv_sem=recv_sem.at[group, slot],
            device_id=others[axis],
            device_id_type=MESH,
        )
        copy.start()
        started.append(copy)
        return copy

    def cells(fixed, flipped=None):
        return tuple(
            1 - here[name] if name == flipped else here[name] if name in fixed else slice(None)
            for name in GRAM_AXES
        )

    class Walk:
        def __init__(self, group):
            count, order = GRAM_GROUPS[group]
            self.group, self.stage = group, 0
            self.order = [GRAM_AXES["fnx".index(letter)] for letter in order]
            self.mine = (pl.ds(starts[group], count),)
            self.came = [
                ref.at[(slice(None),) * (2 - stage) + self.mine]
                for stage, ref in enumerate((came_one, came_two, came_three))
            ]

        def advance(self):
            stage, order = self.stage, self.order
            mine = self.mine
            if stage:
                self.copy.wait_recv()
            if 1 <= stage <= 3:
                kept = cells(order[:stage]) + mine
                total = part[kept] + self.came[stage - 1][...]
                if stage == 3:
                    out[kept] = total
                else:
                    part[kept] = total
            if stage < 3:
                source = part.at[cells(order[:stage], order[stage]) + mine]
                self.copy = send(source, self.came[stage], self.group, stage, order[stage])
            elif stage < 6:
                block = out.at[cells(order[: 6 - stage]) + mine]
                self.copy = send(block, block, self.group, stage, order[5 - stage])
            self.stage += 1

    walks = [Walk(group) for group in range(len(GRAM_GROUPS))]
    for group in GRAM_PLAN:
        if walks[group].stage == 0:
            for index in range(starts[group], starts[group] + GRAM_GROUPS[group][0]):
                product(index)
        walks[group].advance()

    e = ortho[0]
    for index, (i, j) in enumerate(blocks):
        value = out[:, :, :, index].reshape(SUB, SUB)
        e[i * SUB : (i + 1) * SUB, j * SUB : (j + 1) * SUB] = value
        if i != j:
            e[j * SUB : (j + 1) * SUB, i * SUB : (i + 1) * SUB] = value.T

    across, beside = [], []

    def share(slot, rows, kind, other):
        block = factors.at[slot, rows]
        index = rows.start // TILE
        copy = pltpu.make_async_remote_copy(
            src_ref=block,
            dst_ref=block,
            send_sem=share_send.at[index, kind],
            recv_sem=share_recv.at[index, kind],
            device_id=other,
            device_id_type=MESH,
        )
        copy.start()
        started.append(copy)
        return copy

    def emit(rows, value):
        factors[own, rows, :] = value
        across.append((rows, share(own, rows, 0, beyond)))
        beside.append(share(own, rows, 1, partner))

    newton_schulz(e, moment, *ortho, emit)
    for rows, copy in across:
        copy.wait_recv()
        beside.append(share(2 * (1 - y) + core, rows, 2, partner))
    for copy in beside:
        copy.wait_recv()
    for copy in started:
        copy.wait_send()


def muon_factors(sums, *olds):
    size, cols = olds[2].shape
    count = len(sub_blocks(size))
    groups = len(GRAM_GROUPS)
    rows = (SUB // 8, SUB)

    def wide(*dims):
        return pltpu.VMEM(dims, f32)

    return pl.pallas_call(
        muon_kernel,
        out_shape=jax.ShapeDtypeStruct((4, size, cols), bf16),
        in_specs=[ANY] * 5,
        out_specs=VMEM,
        scratch_shapes=[
            pltpu.VMEM((size, cols), bf16),
            wide(*olds[0].shape),
            wide(*olds[1].shape),
            wide(size, cols),
            wide(size, cols),
            wide(2, 2, 2, count, *rows),
            wide(2, 2, 2, count, *rows),
            wide(2, 2, count, *rows),
            wide(2, count, *rows),
            wide(count, *rows),
            pltpu.VMEM((size, cols), bf16),
            pltpu.VMEM((size, cols), bf16),
            pltpu.SemaphoreType.DMA((2,)),
            pltpu.SemaphoreType.DMA((groups, 6)),
            pltpu.SemaphoreType.DMA((groups, 6)),
            pltpu.SemaphoreType.DMA((size // TILE, 3)),
            pltpu.SemaphoreType.DMA((size // TILE, 3)),
        ]
        + ortho_scratch(size, cols),
        compiler_params=pltpu.CompilerParams(
            vmem_limit_bytes=58 * MIB, collective_id=1, has_side_effects=True
        ),
        name="muon_factors",
    )(sums, *olds)


def window(start, width, total):
    size = -(-(width + 96) // LANES) * LANES
    first = jnp.minimum(start // LANES * LANES, total - size)
    return pl.ds(pl.multiple_of(first, LANES), size), start - first


def finish_kernel(
    factors_hbm,
    sums_hbm,
    qkv_hbm,
    out_hbm,
    up_hbm,
    down_hbm,
    qkv_old_hbm,
    out_old_hbm,
    up_old_hbm,
    down_old_hbm,
    mixed_hbm,
    grad_hbm,
    mixed_out,
    grad_out,
    qkv_moment_out,
    out_moment_out,
    up_moment_out,
    down_moment_out,
    qkv_out,
    out_out,
    up_out,
    down_out,
    factors,
    sums,
    qkv_w,
    out_w,
    up_w,
    down_w,
    qkv_moment,
    out_moment,
    up_moment,
    down_moment,
    qkv_new,
    out_new,
    up_new,
    down_new,
    turned,
    load_sem,
    store_sem,
):
    shrink = 1.0 - muon_rate * muon_decay
    dp_id = lax.axis_index("dp")
    qkv_cols, out_cols = qkv_new.shape[0], out_new.shape[0]
    qkv_lanes, qkv_skip = window(dp_id * qkv_cols, qkv_cols, 3 * D)
    out_lanes, out_skip = window(dp_id * out_cols, out_cols, D)
    block = pl.ds(pl.multiple_of(dp_id * UNIT, UNIT), UNIT)
    pairs = {
        "sums": (sums_hbm, sums),
        "up_moment": (up_old_hbm, up_moment),
        "down_moment": (down_old_hbm, down_moment),
        "factors": (factors_hbm, factors),
        "up": (up_hbm.at[:, block], up_w),
        "down": (down_hbm.at[block], down_w),
        "qkv_moment": (qkv_old_hbm, qkv_moment),
        "out_moment": (out_old_hbm, out_moment),
        "qkv": (qkv_hbm.at[:, qkv_lanes], qkv_w),
        "out": (out_hbm.at[:, out_lanes], out_w),
    }
    loads = {
        name: pltpu.make_async_copy(source, target, load_sem.at[index])
        for index, (name, (source, target)) in enumerate(pairs.items())
    }
    for load in loads.values():
        load.start()
    stores = []

    def store(source, target):
        stores.append(pltpu.make_async_copy(source, target, store_sem.at[len(stores)]))
        stores[-1].start()

    store(mixed_hbm, mixed_out)
    store(grad_hbm, grad_out)

    def step(index, rate, turned=False):
        value = factors[index]
        value = transposed(value) if turned else value
        return muon_rate * rate * value.astype(f32)

    loads["sums"].wait()
    for index, name, target, out in (
        (1, "up_moment", up_moment, up_moment_out),
        (0, "down_moment", down_moment, down_moment_out),
    ):
        loads[name].wait()
        target[...] = muon_keep * target[...] + sums[index].astype(f32)
        store(target, out)
    loads["qkv_moment"].wait()
    loads["out_moment"].wait()
    for half in range(2):
        cols = slice(half * HALF, (half + 1) * HALF)
        value = sums[2, cols].astype(f32)
        qkv_moment[:, cols] = muon_keep * qkv_moment[:, cols] + value[:qkv_cols]
        out_moment[:, cols] = muon_keep * out_moment[:, cols] + value[qkv_cols:]
    store(qkv_moment, qkv_moment_out)
    store(out_moment, out_moment_out)
    loads["factors"].wait()
    loads["up"].wait()
    up_new[...] = up_w[...].astype(f32) * shrink - step(2, math.sqrt(max(1.0, FF / D)))
    store(up_new, up_out)
    loads["down"].wait()
    down_new[...] = down_w[...].astype(f32) * shrink - step(3, 1.0, True)
    store(down_new, down_out)
    loads["qkv"].wait()
    turned[...] = transposed(qkv_w[...]).astype(f32)
    rows = pl.ds(pl.multiple_of(qkv_skip, 32), qkv_cols)
    qkv_new[...] = turned[rows, :] * shrink - step(0, math.sqrt(3.0), True)[:qkv_cols]
    store(qkv_new, qkv_out)
    loads["out"].wait()
    turned[: out_w.shape[1], :] = transposed(out_w[...]).astype(f32)
    rows = pl.ds(pl.multiple_of(out_skip, 32), out_cols)
    out_new[...] = turned[rows, :] * shrink - step(1, 1.0, True)[qkv_cols:]
    store(out_new, out_out)
    for copy in stores:
        copy.wait()


def finish(factors, sums, weights, olds, mixed, input_grad):
    shapes = [old.shape for old in olds]
    news = shapes[:3] + [shapes[3][::-1]]

    def wide(shape):
        return pltpu.VMEM(shape, f32)

    return pl.pallas_call(
        finish_kernel,
        out_shape=tuple(
            jax.ShapeDtypeStruct(shape, f32)
            for shape in [mixed.shape, input_grad.shape] + shapes + news
        ),
        in_specs=[ANY] * 12,
        out_specs=(ANY,) * 10,
        scratch_shapes=[
            pltpu.VMEM(factors.shape, bf16),
            pltpu.VMEM(sums.shape, bf16),
            pltpu.VMEM((D, 384), bf16),
            pltpu.VMEM((D, 256), bf16),
            pltpu.VMEM((D, UNIT), bf16),
            pltpu.VMEM((UNIT, D), bf16),
        ]
        + [wide(shape) for shape in shapes + news]
        + [
            wide((384, D)),
            pltpu.SemaphoreType.DMA((10,)),
            pltpu.SemaphoreType.DMA((10,)),
        ],
        compiler_params=pltpu.CompilerParams(vmem_limit_bytes=48 * MIB),
        name="finish",
    )(factors, sums, *weights, *olds, mixed, input_grad)


def swap(value, axis, bit):
    size = lax.axis_size(axis)
    return lax.ppermute(value, axis, [(i, i ^ bit) for i in range(size)])


def scatter_head(value, bit, position):
    half = value.shape[1] // 2
    mine = lax.dynamic_slice_in_dim(value, position * half, half, 1)
    other = lax.dynamic_slice_in_dim(value, (1 - position) * half, half, 1)
    return (mine.astype(f32) + swap(other, "head", bit).astype(f32)).astype(bf16)


def scatter_dp_pair(value, position):
    paired = value.reshape((value.shape[0] // 2, 2) + value.shape[1:])
    mine = lax.dynamic_index_in_dim(paired, position, 1, False)
    other = lax.dynamic_index_in_dim(paired, 1 - position, 1, False)
    return (mine.astype(f32) + swap(other, "dp", 1).astype(f32)).astype(bf16)


def scatter_dp_rest(value, place):
    ranks = value.shape[0]
    total = lax.dynamic_index_in_dim(value, place, 0, False).astype(f32)
    for step in range(1, ranks):
        sent = lax.dynamic_index_in_dim(value, place ^ step, 0, False)
        total = total + swap(sent, "dp", 2 * step).astype(f32)
    return total


def local(
    tokens,
    cotangent,
    qkv_weight,
    out_weight,
    up_weight,
    down_weight,
    vectors,
    qkv_moment,
    out_moment,
    up_moment,
    down_moment,
    adam_first,
    adam_second,
    bucket_class,
    row_lengths,
):
    n_dp = lax.axis_size("dp")
    n_head = lax.axis_size("head")
    dp_id = lax.axis_index("dp")
    head_id = lax.axis_index("head")
    core, side = head_id % 2, head_id // 2
    tok, width = tokens.shape
    hidden = up_weight.shape[1]
    half = width // 2
    qkv_cols, out_cols = qkv_moment.shape[1], out_moment.shape[1]
    shrink = 1.0 - muon_rate * muon_decay

    def weight_block(weight, cols, dim):
        return lax.dynamic_slice_in_dim(weight, dp_id * cols, cols, dim)

    block = head_id.astype(jnp.int32)[None]
    vec_len = vectors.shape[0] // n_dp
    if (n_dp, n_head, tok) == (8, 4, 256):
        mixed, input_grad, sums, vec = layer(
            bucket_class,
            row_lengths,
            tokens,
            cotangent,
            vectors,
            qkv_weight,
            out_weight,
            up_weight,
            down_weight,
        )
        grad_vec = vec[:VEC_BLOCK].reshape(vec_len)
        sums = sums.reshape(3, width, -1)
        olds = [qkv_moment.T, out_moment.T, up_moment, down_moment]
        mixed, input_grad, *results = finish(
            muon_factors(sums, *olds),
            sums,
            [qkv_weight, out_weight, up_weight, down_weight],
            olds,
            mixed,
            input_grad,
        )
        moments, new_weights = results[:4], results[4:]
        moments = [moments[0].T, moments[1].T, *moments[2:]]
        new_weights = [new_weights[0].T, new_weights[1].T, *new_weights[2:]]
    else:
        pieces = split_vectors(vectors, width, hidden)
        bias_query, bias_value, bias_out, gain_one, shift_one = pieces[:5]
        bias_up, bias_down, gain_two, shift_two = pieces[5:]
        bias_qkv = jnp.concatenate([bias_query, jnp.zeros_like(bias_query), bias_value])

        def column_half(value, which):
            return lax.dynamic_slice_in_dim(value, which * half, half, 1)

        qkv = (dot(tokens, qkv_weight, 1, 0) + bias_qkv).astype(bf16)
        other = swap(qkv[:, width:], "head", 1)
        attended = attend(block, bucket_class, row_lengths, qkv, other)
        attn_val = dot(attended, out_weight, 1, 0) + bias_out
        resid_one = tokens.astype(f32) + attn_val
        centre = resid_one - jnp.mean(resid_one, axis=-1, keepdims=True)
        rstd_one = lax.rsqrt(jnp.mean(centre * centre, axis=-1, keepdims=True) + norm_eps)
        zhat_one = centre * rstd_one
        normed_one = zhat_one * gain_one + shift_one
        normed_low = normed_one.astype(bf16)
        up_val = dot(normed_low, up_weight, 1, 0) + bias_up
        phi_cum = 0.5 * (1.0 + lax.erf(up_val * (0.5**0.5)))
        active_low = (up_val * phi_cum).astype(bf16)
        slope = phi_cum + up_val * jnp.exp(-0.5 * up_val * up_val) * (1.0 / math.sqrt(2.0 * math.pi))
        down_val = dot(active_low, down_weight, 1, 0) + bias_down
        resid_two = normed_one + down_val
        centre = resid_two - jnp.mean(resid_two, axis=-1, keepdims=True)
        rstd_two = lax.rsqrt(jnp.mean(centre * centre, axis=-1, keepdims=True) + norm_eps)
        zhat_two = centre * rstd_two
        mixed = zhat_two * gain_two + shift_two

        def norm_back(grad, gain, zhat, rstd):
            inner = grad * gain
            mean = jnp.mean(inner, axis=-1, keepdims=True)
            slant = jnp.mean(inner * zhat, axis=-1, keepdims=True)
            return (inner - mean - zhat * slant) * rstd, jnp.sum(grad * zhat, axis=0), jnp.sum(grad, axis=0)

        grad_two, grad_gain_two, grad_shift_two = norm_back(
            cotangent.astype(f32), gain_two, zhat_two, rstd_two
        )
        grad_down_low = grad_two.astype(bf16)
        grad_bias_down = jnp.sum(grad_down_low, axis=0, dtype=f32)

        x_id, z_id = dp_id % 2, dp_id // 2

        grad_up_low = (dot(grad_down_low, down_weight, 1, 1) * slope).astype(bf16)
        grad_bias_up = jnp.sum(grad_up_low, axis=0, dtype=f32)
        grad_normed = grad_two + dot(grad_up_low, up_weight, 1, 1)
        grad_one, grad_gain_one, grad_shift_one = norm_back(grad_normed, gain_one, zhat_one, rstd_one)
        grad_attn_low = grad_one.astype(bf16)
        grad_bias_out = jnp.sum(grad_attn_low, axis=0, dtype=f32)
        grad_heads = dot(grad_attn_low, out_weight, 1, 1).astype(bf16)
        grad_query, own, sent = attend_back(block, bucket_class, row_lengths, qkv, other, grad_heads)
        grad_kv = (own + swap(sent, "head", 1).astype(f32)).astype(bf16)
        grad_qkv = jnp.concatenate([grad_query, grad_kv], axis=1)
        grad_bias_qkv = jnp.sum(grad_qkv, axis=0, dtype=f32)
        input_grad = grad_one + dot(grad_qkv, qkv_weight, 1, 1)
        grad_vector = jnp.concatenate(
            [
                grad_bias_qkv[:width],
                grad_bias_qkv[2 * width :],
                grad_bias_out,
                grad_gain_one,
                grad_shift_one,
                grad_bias_up,
                grad_bias_down,
                grad_gain_two,
                grad_shift_two,
            ]
        )
        grad_vector = grad_vector + swap(grad_vector, "head", 1)
        wides = [active_low, grad_up_low, grad_attn_low, grad_qkv]
        narrows = [grad_down_low, normed_low, attended, tokens]

        def both_halves(value):
            return jnp.concatenate(
                [column_half(value, core), swap(column_half(value, 1 - core), "head", 1)], axis=0
            )

        def weight_grad(wide, narrow):
            wide = jnp.concatenate([wide, swap(wide, "head", 1)], axis=0)
            value = dot(wide, both_halves(narrow), 0, 0).astype(bf16)
            return value.reshape(n_dp, value.shape[0] // n_dp, half)

        def reduce_y_first(value):
            return scatter_dp_rest(scatter_dp_pair(scatter_head(value, 2, side), x_id), z_id)

        def reduce_x_first(value):
            return scatter_dp_rest(scatter_head(scatter_dp_pair(value, x_id), 2, side), z_id)

        def spread(value):
            value = value.astype(bf16)
            came = swap(value, "head", 2)
            value = jnp.concatenate(
                [jnp.where(side == 0, value, came), jnp.where(side == 0, came, value)], axis=0
            )
            came = swap(value, "head", 1)
            return jnp.concatenate(
                [jnp.where(core == 0, value, came), jnp.where(core == 0, came, value)], axis=1
            ).astype(f32)

        down_part, up_part, out_part, qkv_part = [
            weight_grad(wide, narrow) for wide, narrow in zip(wides, narrows)
        ]
        vec_rows = 16
        vec_part = grad_vector.reshape(n_dp, vec_len)
        vec_part = jnp.pad(vec_part, ((0, 0), (0, vec_rows * width - vec_len)))
        vec_part = vec_part.reshape(n_dp, vec_rows, width)
        vec_part = lax.dynamic_slice_in_dim(vec_part, core * half, half, 2).astype(bf16)
        down_new = spread(reduce_x_first(down_part))
        up_new = spread(reduce_y_first(up_part))
        tail_new = spread(
            reduce_y_first(jnp.concatenate([qkv_part, out_part, vec_part], axis=1))
        )
        grads = [
            tail_new[:qkv_cols].T,
            tail_new[qkv_cols : qkv_cols + out_cols].T,
            up_new.T,
            down_new.T,
        ]
        grad_vec = tail_new[qkv_cols + out_cols :].reshape(-1)[:vec_len]
        moments = [
            muon_keep * old + grad
            for old, grad in zip([qkv_moment, out_moment, up_moment, down_moment], grads)
        ]
        most = max(m.shape[1] for m in moments)
        padded = [jnp.pad(m, ((0, 0), (0, most - m.shape[1]))) for m in moments]
        chosen = padded[-1]
        for index in range(len(padded) - 2, -1, -1):
            chosen = jnp.where(head_id == index, padded[index], chosen)
        gram_mat = lax.dot_general(
            chosen, chosen, (((1,), (1,)), ((), ())), precision=lax.Precision.HIGH
        )
        own_factor = orthogonalize(lax.psum(gram_mat, "dp"), chosen)
        across = swap(own_factor, "head", 2)
        low_pair = jnp.where(side == 0, own_factor, across)
        high_pair = jnp.where(side == 0, across, own_factor)
        near_low = swap(low_pair, "head", 1)
        near_high = swap(high_pair, "head", 1)
        factors = [
            jnp.where(core == 0, low_pair, near_low),
            jnp.where(core == 0, near_low, low_pair),
            jnp.where(core == 0, high_pair, near_high),
            jnp.where(core == 0, near_high, high_pair),
        ]
        factors = [o[:, : m.shape[1]].astype(f32) for o, m in zip(factors, moments)]
        factors[3] = factors[3].T
        old_weights = [
            weight_block(qkv_weight, qkv_cols, 1),
            weight_block(out_weight, out_cols, 1),
            weight_block(up_weight, up_moment.shape[1], 1),
            weight_block(down_weight, down_moment.shape[1], 0),
        ]

        rates = (math.sqrt(3.0), 1.0, math.sqrt(max(1.0, hidden / width)), 1.0)
        new_weights = [
            old.astype(f32) * shrink - muon_rate * rate * factor
            for old, rate, factor in zip(old_weights, rates, factors)
        ]

    vec_old = lax.dynamic_slice_in_dim(vectors, dp_id * vec_len, vec_len, 0)
    vec_first = beta_first * adam_first + (1.0 - beta_first) * grad_vec
    vec_second = beta_second * adam_second + (1.0 - beta_second) * grad_vec * grad_vec
    first_hat = vec_first / (1.0 - beta_first**STEP)
    second_hat = vec_second / (1.0 - beta_second**STEP)
    vec_new = vec_old - adam_rate * first_hat / (jnp.sqrt(second_hat) + adam_eps)
    return (mixed, input_grad, *moments, *new_weights, vec_first, vec_second, vec_new)


def solution(mesh):
    tokens_spec = P(("dp", "head"), None)
    block_spec = P(None, "dp")
    return jax.shard_map(
        local,
        mesh=mesh,
        in_specs=(
            tokens_spec,
            tokens_spec,
            P(),
            P(),
            P(),
            P(),
            P(),
            block_spec,
            block_spec,
            block_spec,
            block_spec,
            P("dp"),
            P("dp"),
            P("dp"),
            P("dp", None),
        ),
        out_specs=(
            tokens_spec,
            tokens_spec,
            block_spec,
            block_spec,
            block_spec,
            block_spec,
            block_spec,
            block_spec,
            block_spec,
            P("dp", None),
            P("dp"),
            P("dp"),
            P("dp"),
        ),
        check_vma=False,
    )
```

```python
import functools
import itertools
import math

import jax
import jax.numpy as jnp
from jax import lax
from jax.experimental import pallas as pl
from jax.experimental.pallas import tpu as pltpu
from jax.sharding import PartitionSpec as P

D = 768
HEADS = 12
HEAD_DIM = 64
FF = 3072
BASE_LEN = 128
NS_STEPS = 5
STEP = 5
MAX_LEN = 512

f32 = jnp.float32
bf16 = jnp.bfloat16

norm_eps = 1e-12
masked_score = -1000000000.0
quintic_a = 3.4445
quintic_b = -4.775
quintic_c = 2.0315
muon_rate = 1.0
muon_decay = 0.01
muon_keep = 0.5
adam_rate = 0.2
beta_first = 0.9
beta_second = 0.999
adam_eps = 1e-08
MIB = 1024 * 1024


def dot(left, right, left_dim, right_dim):
    return lax.dot_general(
        left, right, (((left_dim,), (right_dim,)), ((), ())), preferred_element_type=f32
    )


def split_vectors(vectors, width, hidden):
    lengths_list = [width] * 5 + [hidden] + [width] * 3
    pieces = []
    offset = 0
    for length in lengths_list:
        pieces.append(vectors[offset : offset + length])
        offset = offset + length
    return pieces


def allowed_mask(class_ref, length_ref, block, tok):
    shift = class_ref[0] + int(math.log2(BASE_LEN))
    query_place = block * tok + lax.broadcasted_iota(jnp.int32, (tok, 1), 0)
    lane = lax.broadcasted_iota(jnp.int32, (1, 2 * tok), 1)
    own = lane < tok
    key_place = jnp.where(own, block * tok + lane, (block ^ 1) * tok + lane - tok)
    key_row = lax.shift_right_logical(key_place, jnp.broadcast_to(shift, key_place.shape))
    offset = key_place - lax.shift_left(key_row, jnp.broadcast_to(shift, key_place.shape))
    row_len = jnp.zeros_like(key_row)
    for slot in range(length_ref.shape[1]):
        row_len = jnp.where(key_row == slot, length_ref[0, slot], row_len)
    key_row = jnp.where(offset < row_len, key_row, -1)
    query_row = lax.shift_right_logical(query_place, jnp.broadcast_to(shift, query_place.shape))
    return query_row == key_row


def half_masks():
    lane = lax.broadcasted_iota(jnp.int32, (1, 2 * HEAD_DIM), 1)
    first = (lane < HEAD_DIM).astype(f32)
    return (first.astype(bf16), (1.0 - first).astype(bf16)), lane < HEAD_DIM


def head_prob(query, keys, allowed):
    score = jnp.where(allowed, dot(query, keys, 1, 1) * HEAD_DIM ** (-0.5), masked_score)
    exponent = jnp.exp(score - jnp.max(score, axis=-1, keepdims=True))
    return exponent / jnp.sum(exponent, axis=-1, keepdims=True)


def attend_kernel(block_ref, class_ref, length_ref, qkv_ref, other_ref, out_ref):
    tok = qkv_ref.shape[0]
    allowed = allowed_mask(class_ref, length_ref, block_ref[0], tok)
    masks, first = half_masks()
    for pair in range(HEADS // 2):
        cols = pl.ds(pair * 2 * HEAD_DIM, 2 * HEAD_DIM)
        kcols = pl.ds(D + pair * 2 * HEAD_DIM, 2 * HEAD_DIM)
        vcols = pl.ds(2 * D + pair * 2 * HEAD_DIM, 2 * HEAD_DIM)
        query = qkv_ref[:, cols]
        keys = jnp.concatenate([qkv_ref[:, kcols], other_ref[:, cols]], axis=0)
        values = jnp.concatenate([qkv_ref[:, vcols], other_ref[:, kcols]], axis=0)
        outs = []
        for mask in masks:
            prob = head_prob(query * mask, keys, allowed)
            outs.append(dot(prob.astype(bf16), values, 1, 0))
        out_ref[:, cols] = jnp.where(first, outs[0], outs[1]).astype(bf16)


def attend_back_kernel(
    block_ref, class_ref, length_ref, qkv_ref, other_ref, grad_ref, dq_ref, own_ref, send_ref
):
    tok = qkv_ref.shape[0]
    allowed = allowed_mask(class_ref, length_ref, block_ref[0], tok)
    masks, first = half_masks()
    scale = HEAD_DIM ** (-0.5)
    for pair in range(HEADS // 2):
        cols = pl.ds(pair * 2 * HEAD_DIM, 2 * HEAD_DIM)
        kcols = pl.ds(D + pair * 2 * HEAD_DIM, 2 * HEAD_DIM)
        vcols = pl.ds(2 * D + pair * 2 * HEAD_DIM, 2 * HEAD_DIM)
        query = qkv_ref[:, cols]
        keys = jnp.concatenate([qkv_ref[:, kcols], other_ref[:, cols]], axis=0)
        values = jnp.concatenate([qkv_ref[:, vcols], other_ref[:, kcols]], axis=0)
        grad = grad_ref[:, cols]
        dqs, dk, dv = [], None, None
        for mask in masks:
            head_query = query * mask
            head_grad = grad * mask
            prob = head_prob(head_query, keys, allowed)
            part_v = dot(prob.astype(bf16), head_grad, 0, 0)
            dprob = dot(head_grad, values, 1, 1)
            dscore = prob * (dprob - jnp.sum(prob * dprob, axis=-1, keepdims=True))
            dscore = dscore.astype(bf16)
            dqs.append(dot(dscore, keys, 1, 0))
            part_k = dot(dscore, head_query, 0, 0)
            dk = part_k if dk is None else dk + part_k
            dv = part_v if dv is None else dv + part_v
        dk = dk * scale
        dq_ref[:, cols] = (jnp.where(first, dqs[0], dqs[1]) * scale).astype(bf16)
        own_ref[:, cols] = dk[:tok]
        own_ref[:, kcols] = dv[:tok]
        send_ref[:, cols] = dk[tok:].astype(bf16)
        send_ref[:, kcols] = dv[tok:].astype(bf16)


SMEM = pl.BlockSpec(memory_space=pltpu.SMEM)
VMEM = pl.BlockSpec(memory_space=pltpu.VMEM)
ANY = pl.BlockSpec(memory_space=pl.ANY)


def attend(block, row_class, lengths, qkv, other):
    tok = qkv.shape[0]
    return pl.pallas_call(
        attend_kernel,
        out_shape=jax.ShapeDtypeStruct((tok, D), bf16),
        in_specs=[SMEM, SMEM, SMEM, VMEM, VMEM],
        out_specs=VMEM,
        compiler_params=pltpu.CompilerParams(vmem_limit_bytes=32 * MIB),
        name="attend",
    )(block, row_class, lengths, qkv, other)


def attend_back(block, row_class, lengths, qkv, other, grad):
    tok = qkv.shape[0]
    return pl.pallas_call(
        attend_back_kernel,
        out_shape=(
            jax.ShapeDtypeStruct((tok, D), bf16),
            jax.ShapeDtypeStruct((tok, 2 * D), f32),
            jax.ShapeDtypeStruct((tok, 2 * D), bf16),
        ),
        in_specs=[SMEM, SMEM, SMEM, VMEM, VMEM, VMEM],
        out_specs=(VMEM, VMEM, VMEM),
        compiler_params=pltpu.CompilerParams(vmem_limit_bytes=32 * MIB),
        name="attend_back",
    )(block, row_class, lengths, qkv, other, grad)


CENTRES = (0.0, 0.0, 0.0, 0.8, 0.8)
TILE = 256
SUB = 128


def sub_blocks(size):
    count = size // SUB
    return [(i, j) for i in range(count) for j in range(i, count)]


def newton_schulz(gram, moment, e, f, g, eb, fb, gb, yy, y, emit):
    size = e.shape[0]
    tiles = [slice(i * TILE, (i + 1) * TILE) for i in range(size // TILE)]

    def unit(rows):
        row_id = rows.start + lax.broadcasted_iota(jnp.int32, (TILE, size), 0)
        col_id = lax.broadcasted_iota(jnp.int32, (TILE, size), 1)
        return (row_id == col_id).astype(f32)

    diagonal = jnp.zeros((TILE, size), f32)
    for rows in tiles:
        diagonal = diagonal + gram[rows, :] * unit(rows)
    trace = jnp.sum(jnp.sum(diagonal, axis=0, keepdims=True), axis=1, keepdims=True)
    factor = 1.0 / (jnp.sqrt(trace) + 1e-07)
    square_factor = factor * factor
    for rows in tiles:
        value = gram[rows, :] * square_factor
        e[rows, :] = value
        eb[rows, :] = value.astype(bf16)
        value = moment[rows, :] * factor
        y[rows, :] = value
        yy[0, rows, :] = value.astype(bf16)

    def one_step(centre, after, now, then, last=False):
        keep = quintic_a + quintic_b * centre + quintic_c * centre * centre
        linear = quintic_b + 2.0 * quintic_c * centre
        for rows in tiles:
            value = linear * e[rows, :] + quintic_c * dot(eb[rows, :], eb[...], 1, 0)
            fb[rows, :] = value.astype(bf16)
            if centre:
                f[rows, :] = value
        for rows in tiles:
            value = keep * y[rows, :] + dot(fb[rows, :], now[...], 1, 0)
            if last:
                emit(rows, value.astype(bf16))
            else:
                y[rows, :] = value
                then[rows, :] = value.astype(bf16)
        if last:
            return
        for rows in tiles:
            value = keep * e[rows, :] + dot(eb[rows, :], fb[...], 1, 0)
            if centre:
                value = value + centre * f[rows, :]
            g[rows, :] = value
            gb[rows, :] = value.astype(bf16)
        for rows in tiles:
            value = keep * g[rows, :] + dot(gb[rows, :], fb[...], 1, 0)
            if centre:
                value = value + (centre * keep) * f[rows, :]
            shift = centre * keep * keep - after
            if not isinstance(shift, float) or shift:
                value = value + shift * unit(rows)
            e[rows, :] = value
            eb[rows, :] = value.astype(bf16)

    plain = sum(centre == 0.0 for centre in CENTRES)

    def plain_step(step, carry):
        after = jnp.where(step == plain - 1, CENTRES[plain], 0.0)
        one_step(0.0, after, yy.at[step % 2], yy.at[(step + 1) % 2])
        return carry

    lax.fori_loop(0, plain, plain_step, 0)
    for step in range(plain, NS_STEPS):
        last = step + 1 == NS_STEPS
        after = 0.0 if last else CENTRES[step + 1]
        one_step(CENTRES[step], after, yy.at[step % 2], yy.at[(step + 1) % 2], last)


def ortho_kernel(gram, moment, out, *scratch):
    def emit(rows, value):
        out[rows, :] = value

    newton_schulz(gram, moment, *scratch, emit)


def ortho_scratch(size, cols):
    square, square_low = pltpu.VMEM((size, size), f32), pltpu.VMEM((size, size), bf16)
    wide_low = pltpu.VMEM((2, size, cols), bf16)
    return [square] * 3 + [square_low] * 3 + [wide_low, pltpu.VMEM((size, cols), f32)]


def orthogonalize(gram_mat, moment):
    size, cols = moment.shape
    return pl.pallas_call(
        ortho_kernel,
        out_shape=jax.ShapeDtypeStruct((size, cols), bf16),
        in_specs=[VMEM, VMEM],
        out_specs=VMEM,
        scratch_shapes=ortho_scratch(size, cols),
        compiler_params=pltpu.CompilerParams(vmem_limit_bytes=48 * MIB),
        name="ortho",
    )(gram_mat, moment)


MESH = pl.DeviceIdType.MESH
PIECE = 48
SIDE = 192
UNIT = 2 * SIDE
HALF = D // 2
LANES = 128
VEC_BLOCK = 9
ROWS = 16
CHUNKS = (
    (0, 0, 64, "nfyx"),
    (0, 64, 64, "xynf"),
    (0, 128, 64, "yxnf"),
    (1, 0, 64, "ynxf"),
    (1, 64, 64, "nxyf"),
    (1, 128, 64, "xynf"),
    (2, 0, 48, "xynf"),
    (2, 48, 48, "nxyf"),
    (2, 96, 48, "yxnf"),
    (2, 144, 32, "xynf"),
    (2, 176, 16, "xfyn"),
)
CHUNK_PLAN = (
    (0, 1, 2),
    (),
    (),
    (),
    (),
    (3, 5, 4),
    (0, 1, 2),
    (),
    (),
    (),
    (0, 1, 2, 4, 5, 3),
    (),
    (),
    (0, 7, 8, 10, 9, 6),
    (
        1, 4, 2, 5, 0, 1, 10, 4, 0, 2, 0, 1, 9, 1, 3, 2, 5, 10, 4, 8, 2, 6,
        10, 5, 9, 3, 4, 10, 7, 4, 8, 10, 5, 9, 3, 10, 5, 6, 9, 8, 7, 3, 9, 6,
        3, 9, 8, 7, 8, 6, 8, 7, 6, 7, 6, 7,
    ),
)
BIAS_QUERY, BIAS_VALUE, BIAS_OUT, GAIN_ONE, SHIFT_ONE, BIAS_UP = (i * D for i in range(6))
BIAS_DOWN, GAIN_TWO, SHIFT_TWO = (BIAS_UP + FF + i * D for i in range(3))


def position():
    dp_id, head_id = lax.axis_index("dp"), lax.axis_index("head")
    z, x = dp_id // 2, dp_id % 2
    y, core = head_id // 2, head_id % 2
    return z, x, y, core


def device(z, x, y, core):
    return (2 * z + x, 2 * y + core)


def flip_z(z, step):
    high, low = z // 2, z % 2
    high = 1 - high if step // 2 else high
    low = 1 - low if step % 2 else low
    return 2 * high + low


def greet(others):
    barrier = pltpu.get_barrier_semaphore()
    for other in others:
        pl.semaphore_signal(barrier, inc=1, device_id=other, device_id_type=MESH)
    return lambda: pl.semaphore_wait(barrier, len(others))


def by_rows(count, body, init=None, together=4):
    def step(index, carry):
        for part in range(together):
            start = (index * together + part) * ROWS
            carry = body(pl.ds(pl.multiple_of(start, ROWS), ROWS), carry)
        return carry

    return lax.fori_loop(0, count // (ROWS * together), step, init)


def row_mean(value):
    return jnp.sum(value, axis=-1, keepdims=True) * (1.0 / D)


def fold(value):
    return jnp.sum(value.reshape(value.shape[0] // 8, 8, value.shape[1]), axis=0)


def column_sum(value):
    return jnp.sum(value, axis=0, keepdims=True)


def normal_parts(value):
    size = jnp.abs(value)
    decay = jnp.exp(-0.5 * value * value)
    below = 1.0 + (0.3275911 * 0.5**0.5) * size
    t = pl.reciprocal(below, approx=True)
    t = t * (2.0 - below * t)
    series = t * (1.061405429 * 0.5)
    for term in (-1.453152027, 1.421413741, -0.284496736, 0.254829592):
        series = (series + term * 0.5) * t
    tail = series * decay
    return jnp.where(value < 0.0, tail, 1.0 - tail), decay * (1.0 / math.sqrt(2.0 * math.pi))


def transposed(value):
    side = 2 * LANES
    row_id = lax.broadcasted_iota(jnp.int32, (side, side), 0)
    unit = (row_id == lax.broadcasted_iota(jnp.int32, (side, side), 1)).astype(f32).astype(bf16)
    blocks = []
    for start in range(0, value.shape[1], side):
        block = value[:, start : start + side]
        size = block.shape[1]
        blocks.append(dot(unit[:size, :size], block, 1, 1).astype(bf16))
    return jnp.concatenate(blocks, axis=0)


def layer_kernel(
    row_class,
    lengths,
    tokens,
    cotangent,
    vectors,
    qkv_hbm,
    out_hbm,
    up_hbm,
    down_hbm,
    mixed_hbm,
    grad_hbm,
    sums_hbm,
    vec_sum,
    mixed,
    input_grad,
    sums,
    qkv_w,
    out_w,
    up_w,
    down_w,
    query,
    query_turned,
    keys_values,
    keys_turned,
    prob,
    attended,
    normed_low,
    grad_down,
    grad_attn,
    narrow_tokens,
    narrow_attended,
    narrow_normed,
    narrow_grad,
    active,
    grad_up,
    attn_turned,
    qkv_turned,
    exchanged,
    grad_heads,
    heads_turned,
    slope,
    normed_one,
    zhat_one,
    rstd_one,
    grad_two,
    work,
    vec,
    vec_core,
    vec_y,
    vec_x,
    vec_z,
    part,
    came_one,
    came_two,
    came_three,
    came_four,
    load_sem,
    store_sem,
    pair_send,
    pair_recv,
    send_sem,
    recv_sem,
):
    grad_one = normed_one
    z, x, y, core = position()
    tok = tokens.shape[0]
    thirds = [slice(index * D, (index + 1) * D) for index in range(3)]
    loads = {
        name: pltpu.make_async_copy(source, target, load_sem.at[index])
        for index, (name, source, target) in enumerate(
            (
                ("key", qkv_hbm.at[:, thirds[1]], qkv_w.at[:, thirds[1]]),
                ("value", qkv_hbm.at[:, thirds[2]], qkv_w.at[:, thirds[2]]),
                ("query", qkv_hbm.at[:, thirds[0]], qkv_w.at[:, thirds[0]]),
                ("out", out_hbm, out_w),
                ("up", up_hbm, up_w),
                ("down", down_hbm, down_w),
            )
        )
    }
    for name in ("key", "value", "query"):
        loads[name].start()
    stores = []

    def store(source, target):
        stores.append(pltpu.make_async_copy(source, target, store_sem.at[len(stores)]))
        stores[-1].start()

    beyond = device(z, x, 1 - y, core)
    beside = device(z, 1 - x, y, core)
    partner = device(z, x, y, 1 - core)
    along = [device(flip_z(z, step), x, y, core) for step in (1, 2, 3)]
    all_here = greet([beyond, beside, partner] + along)
    started = []

    def remote(source, target, send_at, recv_at, other):
        copy = pltpu.make_async_remote_copy(
            src_ref=source,
            dst_ref=target,
            send_sem=send_at,
            recv_sem=recv_at,
            device_id=other,
            device_id_type=MESH,
        )
        copy.start()
        started.append(copy)
        return copy

    pair_count = []

    def to_partner(source, target):
        slot = len(pair_count)
        pair_count.append(slot)
        return remote(source, target, pair_send.at[slot], pair_recv.at[slot], partner)

    own_half = pl.ds(pl.multiple_of(core * HALF, HALF), HALF)
    other_half = pl.ds(pl.multiple_of((1 - core) * HALF, HALF), HALF)

    def span(start, length=D):
        return vectors[0:1, start : start + length]

    def put_vec(start, value):
        for index in range(value.shape[1] // LANES):
            block, row = divmod(start // LANES + index, VEC_BLOCK)
            vec[block, row : row + 1, :] = value[:, index * LANES : (index + 1) * LANES]

    vec[...] = jnp.zeros_like(vec)

    own_rows = pl.ds(0, tok)
    far_rows = pl.ds(tok, tok)
    own_lanes, far_lanes = own_rows, far_rows

    def share_half(value, narrow):
        narrow[own_rows, :] = value[:, own_half]
        return to_partner(value.at[:, other_half], narrow.at[far_rows])

    kv_came = []
    for name, index, start in (("key", 1, None), ("value", 2, BIAS_VALUE)):
        loads[name].wait()
        value = dot(tokens[...], qkv_w[:, thirds[index]], 1, 0)
        if start is not None:
            value = value + span(start)
        cols = slice((index - 1) * D, index * D)
        keys_values[own_rows, cols] = value.astype(bf16)
        if index == 1:
            all_here()
            for name in ("out", "up", "down"):
                loads[name].start()
        kv_came.append(
            to_partner(keys_values.at[own_rows, cols], keys_values.at[far_rows, cols])
        )
    loads["query"].wait()
    value = dot(tokens[...], qkv_w[:, thirds[0]], 1, 0) + span(BIAS_QUERY)
    query[...] = value.astype(bf16)
    query_turned[...] = transposed(query[...])
    allowed = allowed_mask(row_class, lengths, 2 * y + core, tok)
    masks, first = half_masks()
    tokens_came = share_half(tokens, narrow_tokens)
    for copy in kv_came:
        copy.wait_recv()

    scale = HEAD_DIM ** (-0.5)

    def lanes_at(start):
        return pl.ds(pl.multiple_of(start, LANES), LANES)

    def attend_pair(pair, carry):
        cols = lanes_at(pair * LANES)
        keys = keys_values[:, cols]
        values = keys_values[:, lanes_at(D + pair * LANES)]
        outs = []
        for side, mask in enumerate(masks):
            score = dot(query[:, cols] * (mask * scale), keys, 1, 1)
            score = jnp.where(allowed, score, masked_score)
            exponent = jnp.exp(score - jnp.max(score, axis=-1, keepdims=True))
            chance = exponent * (1.0 / jnp.sum(exponent, axis=-1, keepdims=True))
            chance = chance.astype(bf16)
            prob[2 * pair + side] = chance
            outs.append(dot(chance, values, 1, 0))
        attended[:, cols] = jnp.where(first, outs[0], outs[1]).astype(bf16)
        return carry

    lax.fori_loop(0, HEADS // 2, attend_pair, 0)
    attended_came = share_half(attended, narrow_attended)

    loads["out"].wait()
    work[...] = dot(attended[...], out_w[...], 1, 0)

    def norm_one(rows, carry):
        value = tokens[rows, :].astype(f32) + (work[rows, :] + span(BIAS_OUT))
        centre = value - row_mean(value)
        rstd = lax.rsqrt(row_mean(centre * centre) + norm_eps)
        zhat = centre * rstd
        normed = zhat * span(GAIN_ONE) + span(SHIFT_ONE)
        zhat_one[rows, :] = zhat
        rstd_one[rows, :] = jnp.broadcast_to(rstd, (ROWS, LANES))
        normed_one[rows, :] = normed
        normed_low[rows, :] = normed.astype(bf16)
        return carry

    by_rows(tok, norm_one)
    normed_came = share_half(normed_low, narrow_normed)

    loads["up"].wait()
    for tile in range(FF // D):
        cols = slice(tile * D, (tile + 1) * D)
        work[...] = dot(normed_low[...], up_w[:, cols], 1, 0)

        def gelu(rows, carry):
            value = work[rows, :] + span(BIAS_UP + cols.start)
            chance, density = normal_parts(value)
            active[rows, cols] = (value * chance).astype(bf16)
            slope[rows, cols] = chance + value * density
            return carry

        by_rows(tok, gelu)
    active_came = to_partner(active.at[own_rows], active.at[far_rows])
    loads["down"].wait()
    work[...] = dot(active[own_rows, :], down_w[...], 1, 0)

    def norm_two(rows, carry):
        value = normed_one[rows, :] + (work[rows, :] + span(BIAS_DOWN))
        centre = value - row_mean(value)
        rstd = lax.rsqrt(row_mean(centre * centre) + norm_eps)
        zhat = centre * rstd
        mixed[rows, :] = zhat * span(GAIN_TWO) + span(SHIFT_TWO)
        grad = cotangent[rows, :].astype(f32)
        inner = grad * span(GAIN_TWO)
        grad_in = (inner - row_mean(inner) - zhat * row_mean(inner * zhat)) * rstd
        grad_two[rows, :] = grad_in
        low = grad_in.astype(bf16)
        grad_down[rows, :] = low
        gain, shift, bias = carry
        return gain + fold(grad * zhat), shift + fold(grad), bias + fold(low.astype(f32))

    zero = jnp.zeros((8, D), f32)
    gain, shift, bias = by_rows(tok, norm_two, (zero, zero, zero))
    store(mixed, mixed_hbm)
    put_vec(GAIN_TWO, column_sum(gain))
    put_vec(SHIFT_TWO, column_sum(shift))
    put_vec(BIAS_DOWN, column_sum(bias))
    grad_down_came = share_half(grad_down, narrow_grad)
    keys_turned[...] = transposed(keys_values[:, :D])

    here = {"f": z // 2, "n": z % 2, "x": x, "y": y}
    across = {"f": along[1], "n": along[0], "x": beside, "y": beyond}

    class Chain:
        def __init__(self, index):
            matrix, start, rows, order = CHUNKS[index]
            self.index, self.order, self.stage = index, order, 0
            self.rows = pl.ds(start, rows)
            self.own = part.at[matrix]
            self.came = [ref.at[matrix] for ref in (came_one, came_two, came_three, came_four)]
            self.final = sums.at[matrix]

        def cells(self, free, flipped=None):
            return tuple(
                slice(None) if name in free else 1 - here[name] if name == flipped else here[name]
                for name in "fnxy"
            ) + (self.rows,)

        def send(self, source, target, other):
            sems = (send_sem.at[self.index, self.stage], recv_sem.at[self.index, self.stage])
            self.copy = remote(source, target, *sems, other)

        def advance(self):
            stage, order = self.stage, self.order
            if stage:
                self.copy.wait_recv()
            if 1 <= stage <= 4:
                free = order[stage:]
                for choice in itertools.product((0, 1), repeat=len(free)):
                    taken = dict(zip(sorted(free, key="fnxy".index), choice))
                    at = tuple(taken.get(name, here[name]) for name in "fnxy") + (self.rows,)
                    value = self.own[at] + self.came[stage - 1][choice + (self.rows,)]
                    if stage == 4:
                        self.final[core, y, self.rows] = value
                    else:
                        self.own[at] = value
            if stage < 4:
                name = order[stage]
                source = self.own.at[self.cells(order[stage + 1 :], name)]
                target = self.came[stage].at[(slice(None),) * (3 - stage) + (self.rows,)]
                self.send(source, target, across[name])
            elif stage == 4:
                block = self.final.at[core, y, self.rows]
                self.send(block, block, beyond)
            elif stage == 5:
                block = self.final.at[core, :, self.rows]
                self.send(block, block, partner)
            self.stage += 1

    chains = [Chain(index) for index in range(len(CHUNKS))]
    plan = iter(CHUNK_PLAN)

    def pump():
        for index in next(plan):
            chains[index].advance()

    def feed_forward(matrix, narrow, wide):
        left = transposed(narrow[...])

        def block(index, carry):
            cols = pl.ds(pl.multiple_of(index * UNIT, UNIT), UNIT)
            value = dot(left, wide[:, cols], 1, 0).astype(bf16)
            for side in range(2):
                part[matrix, index // 4, index // 2 % 2, index % 2, side] = value[
                    side * SIDE : (side + 1) * SIDE
                ]
            return carry

        lax.fori_loop(0, 8, block, 0)

    def projections(matrix, turned, narrow, width, offset, between=None):
        for tile in range(turned.shape[0] // UNIT):
            if between and tile % 2 == 0:
                between()
            value = dot(turned[tile * UNIT : (tile + 1) * UNIT, :], narrow[...], 1, 0).astype(bf16)
            for start in range(0, UNIT, PIECE):
                block, row = divmod(tile * UNIT + start, width)
                side, row = divmod(offset + row, SIDE)
                cell = (matrix, block // 4, block // 2 % 2, block % 2, side)
                part[cell + (pl.ds(row, PIECE),)] = value[start : start + PIECE]

    grad_down_came.wait_recv()
    active_came.wait_recv()
    feed_forward(0, narrow_grad, active)

    for tile in range(FF // D):
        pump()
        cols = slice(tile * D, (tile + 1) * D)
        work[...] = dot(grad_down[...], down_w[cols, :], 1, 1)

        def gelu_back(rows, carry):
            low = (work[rows, :] * slope[rows, cols]).astype(bf16)
            grad_up[rows, cols] = low
            return carry + fold(low.astype(f32))

        put_vec(BIAS_UP + cols.start, column_sum(by_rows(tok, gelu_back, zero)))
    grad_up_came = to_partner(grad_up.at[own_rows], grad_up.at[far_rows])
    pump()
    normed_came.wait_recv()
    grad_up_came.wait_recv()
    feed_forward(1, narrow_normed, grad_up)
    pump()

    work[...] = dot(grad_up[own_rows, :], up_w[...], 1, 1)

    def norm_one_back(rows, carry):
        grad = grad_two[rows, :] + work[rows, :]
        zhat = zhat_one[rows, :]
        inner = grad * span(GAIN_ONE)
        grad_in = inner - row_mean(inner) - zhat * row_mean(inner * zhat)
        grad_in = grad_in * rstd_one[rows, 0:1]
        grad_one[rows, :] = grad_in
        low = grad_in.astype(bf16)
        grad_attn[rows, :] = low
        gain, shift, bias = carry
        return gain + fold(grad * zhat), shift + fold(grad), bias + fold(low.astype(f32))

    gain, shift, bias = by_rows(tok, norm_one_back, (zero, zero, zero))
    put_vec(GAIN_ONE, column_sum(gain))
    put_vec(SHIFT_ONE, column_sum(shift))
    put_vec(BIAS_OUT, column_sum(bias))
    grad_heads[...] = dot(grad_attn[...], out_w[...], 1, 1).astype(bf16)
    heads_turned[...] = dot(out_w[...], grad_attn[...], 1, 1).astype(bf16)

    half_lanes = LANES // 2

    def attend_pair_back(pair, carry):
        cols = lanes_at(pair * LANES)
        values = keys_values[:, lanes_at(D + pair * LANES)]
        for side, mask in enumerate(masks):
            start = pl.multiple_of(pair * LANES + side * half_lanes, half_lanes)
            rows = pl.ds(start, half_lanes)
            low_chance = prob[2 * pair + side]
            chance = low_chance.astype(f32)
            grad_chance = dot(grad_heads[:, cols] * mask, values, 1, 1)
            mean = jnp.sum(chance * grad_chance, axis=-1, keepdims=True)
            grad_score = (chance * (grad_chance - mean)).astype(bf16)
            values_grad = dot(heads_turned[rows, :], low_chance, 1, 0).astype(bf16)
            keys_grad = (dot(query_turned[rows, :], grad_score, 1, 0) * scale).astype(bf16)
            query_grad = (dot(keys_turned[rows, :], grad_score, 1, 1) * scale).astype(bf16)
            blocks = (
                query_grad,
                keys_grad[:, :tok],
                values_grad[:, :tok],
                keys_grad[:, tok:],
                values_grad[:, tok:],
            )
            for index, value in enumerate(blocks):
                start = index * LANES + side * half_lanes
                exchanged[0, pair, start : start + half_lanes, :] = value
        return carry

    half_came = []
    for half in range(2):
        pump()
        pairs = pl.ds(half * HEADS // 4, HEADS // 4)
        lax.fori_loop(half * HEADS // 4, (half + 1) * HEADS // 4, attend_pair_back, 0)
        half_came.append(to_partner(exchanged.at[0, pairs], exchanged.at[1, pairs]))
    pump()
    attn_turned[:, own_lanes] = transposed(grad_attn[...])
    grad_attn_came = to_partner(attn_turned.at[:, own_lanes], attn_turned.at[:, far_lanes])

    for pair in range(HEADS // 2):
        if pair % (HEADS // 4) == 0:
            half_came[pair // (HEADS // 4)].wait_recv()
        for who, lanes in enumerate((own_lanes, far_lanes)):
            start = pair * LANES
            mine, theirs = exchanged.at[who, pair], exchanged.at[1 - who, pair]
            qkv_turned[start : start + LANES, lanes] = mine[:LANES]
            for index in (1, 2):
                rows = slice(index * LANES, (index + 1) * LANES)
                sent = slice((index + 2) * LANES, (index + 3) * LANES)
                value = mine[rows].astype(f32) + theirs[sent].astype(f32)
                start = index * D + pair * LANES
                qkv_turned[start : start + LANES, lanes] = value.astype(bf16)
    pump()
    tokens_came.wait_recv()
    projections(2, qkv_turned, narrow_tokens, 3 * D // 8, 0, pump)
    attended_came.wait_recv()
    grad_attn_came.wait_recv()
    projections(2, attn_turned, narrow_attended, D // 8, 3 * D // 8)
    pump()

    ones = jnp.ones((8, tok), bf16)
    for start, rows in ((BIAS_QUERY, slice(0, D)), (BIAS_VALUE, slice(2 * D, 3 * D))):
        put_vec(start, dot(ones, qkv_turned[rows, own_lanes], 1, 1)[0:1])
    vec_came = to_partner(vec, vec_core)
    value = dot(qkv_w[...], qkv_turned[:, own_lanes], 1, 0)
    input_grad[...] = grad_one[...] + value.T
    store(input_grad, grad_hbm)

    vec_slots = [(send_sem.at[len(CHUNKS), i], recv_sem.at[len(CHUNKS), i]) for i in range(5)]

    def vec_steps():
        vec_came.wait_recv()
        vec_core[...] = vec[...] + vec_core[...]
        copy = remote(vec_core, vec_y, *vec_slots[0], beyond)
        yield
        copy.wait_recv()
        for i in range(4):
            vec_x[0, i] = vec_core[2 * i + x] + vec_y[2 * i + x]
            vec_x[1, i] = vec_core[2 * i + 1 - x] + vec_y[2 * i + 1 - x]
        copy = remote(vec_x.at[1], vec_x.at[2], *vec_slots[1], beside)
        yield
        copy.wait_recv()
        vec_x[0] = vec_x[0] + vec_x[2]
        copies = [
            remote(
                vec_x.at[0, flip_z(z, step)],
                vec_z.at[step - 1],
                *vec_slots[1 + step],
                along[step - 1],
            )
            for step in (1, 2, 3)
        ]
        yield
        total = vec_x[0, z]
        for step, copy in enumerate(copies):
            copy.wait_recv()
            total = total + vec_z[step]
        vec_sum[...] = total
        yield

    steps = vec_steps()
    left = [sum(chunk[0] == matrix for chunk in CHUNKS) for matrix in range(3)]
    for turn, index in enumerate(next(plan)):
        chains[index].advance()
        matrix = CHUNKS[index][0]
        left[matrix] -= chains[index].stage == 7
        if not left[matrix]:
            store(sums.at[matrix], sums_hbm.at[matrix])
            left[matrix] = -1
        if turn % 10 == 9 and turn < 40:
            next(steps)
    for copy in stores:
        copy.wait()
    for copy in started:
        copy.wait_send()


def layer(row_class, lengths, tokens, cotangent, vectors, qkv_w, out_w, up_w, down_w):
    tok = tokens.shape[0]
    side = (SIDE, UNIT)

    def low(*dims):
        return pltpu.VMEM(dims, bf16)

    def wide(*dims):
        return pltpu.VMEM(dims, f32)

    return pl.pallas_call(
        layer_kernel,
        out_shape=(
            jax.ShapeDtypeStruct((tok, D), f32),
            jax.ShapeDtypeStruct((tok, D), f32),
            jax.ShapeDtypeStruct((3, 2, 2) + side, bf16),
            jax.ShapeDtypeStruct((16, LANES), f32),
        ),
        in_specs=[SMEM, SMEM, VMEM, VMEM, VMEM] + [ANY] * 4,
        out_specs=(ANY, ANY, ANY, VMEM),
        scratch_shapes=[
            wide(tok, D),
            wide(tok, D),
            low(3, 2, 2, *side),
            low(D, 3 * D),
            low(D, D),
            low(D, FF),
            low(FF, D),
            low(tok, D),
            low(D, tok),
            low(2 * tok, 2 * D),
            low(D, 2 * tok),
            low(HEADS, tok, 2 * tok),
            low(tok, D),
            low(tok, D),
            low(tok, D),
            low(tok, D),
            low(2 * tok, HALF),
            low(2 * tok, HALF),
            low(2 * tok, HALF),
            low(2 * tok, HALF),
            low(2 * tok, FF),
            low(2 * tok, FF),
            low(D, 2 * tok),
            low(3 * D, 2 * tok),
            low(2, HEADS // 2, 5 * LANES, tok),
            low(tok, D),
            low(D, tok),
            wide(tok, FF),
            wide(tok, D),
            wide(tok, D),
            wide(tok, LANES),
            wide(tok, D),
            wide(tok, D),
            wide(8, 16, LANES),
            wide(8, 16, LANES),
            wide(8, 16, LANES),
            wide(3, 4, 16, LANES),
            wide(3, 16, LANES),
            low(3, 2, 2, 2, 2, *side),
            low(3, 2, 2, 2, *side),
            low(3, 2, 2, *side),
            low(3, 2, *side),
            low(3, *side),
            pltpu.SemaphoreType.DMA((6,)),
            pltpu.SemaphoreType.DMA((5,)),
            pltpu.SemaphoreType.DMA((12,)),
            pltpu.SemaphoreType.DMA((12,)),
            pltpu.SemaphoreType.DMA((len(CHUNKS) + 1, 6)),
            pltpu.SemaphoreType.DMA((len(CHUNKS) + 1, 6)),
        ],
        compiler_params=pltpu.CompilerParams(
            vmem_limit_bytes=63 * MIB, collective_id=0, has_side_effects=True
        ),
        name="layer",
    )(row_class, lengths, tokens, cotangent, vectors[None, :], qkv_w, out_w, up_w, down_w)


GRAM_AXES = ("far", "near", "x")
GRAM_GROUPS = (
    (1, "xnf"),
    (2, "xnf"),
    (2, "xnf"),
    (3, "xnf"),
    (3, "nxf"),
    (3, "fxn"),
    (3, "nxf"),
    (2, "xnf"),
    (1, "xnf"),
    (1, "xnf"),
)
GRAM_PLAN = (
    6, 0, 9, 2, 5, 4, 7, 3, 0, 9, 6, 8, 2, 0, 9, 1, 0, 7, 9, 8, 2, 6,
    0, 5, 4, 3, 1, 8, 2, 7, 0, 6, 9, 5, 4, 8, 0, 2, 7, 1, 8, 9, 6, 3,
    5, 4, 7, 1, 8, 6, 2, 9, 3, 5, 8, 1, 4, 7, 2, 3, 5, 1, 4, 6, 7, 3,
    1, 5, 3, 4,
)


def muon_kernel(
    sums,
    qkv_hbm,
    out_hbm,
    up_hbm,
    down_hbm,
    factors_hbm,
    factors,
    own_sum,
    qkv_old,
    out_old,
    old,
    moment,
    out,
    part,
    came_one,
    came_two,
    came_three,
    high,
    low,
    load_sem,
    send_sem,
    recv_sem,
    share_send,
    share_recv,
    *ortho,
):
    z, x, y, core = position()
    here = {"far": z // 2, "near": z % 2, "x": x}
    others = {
        "far": device(flip_z(z, 2), x, y, core),
        "near": device(flip_z(z, 1), x, y, core),
        "x": device(z, 1 - x, y, core),
    }
    beyond = device(z, x, 1 - y, core)
    partner = device(z, x, y, 1 - core)
    own = 2 * y + core
    all_here = greet(list(others.values()) + [beyond, partner])

    def load_two(source, target, matrix):
        loads = [
            pltpu.make_async_copy(source, target, load_sem.at[0]),
            pltpu.make_async_copy(sums.at[matrix], own_sum, load_sem.at[1]),
        ]
        for load in loads:
            load.start()
        for load in loads:
            load.wait()

    def from_turned(source, target, skip):
        load_two(source, target, 2)
        rows = target.shape[0]
        moment[...] = jnp.zeros_like(moment)
        for half in range(2):
            cols = slice(half * HALF, (half + 1) * HALF)
            start = half * UNIT + skip
            value = own_sum[start : start + rows, :].astype(f32)
            moment[cols, skip : skip + rows] = (muon_keep * target[:, cols] + value).T

    @pl.when(own == 0)
    def _():
        from_turned(qkv_hbm, qkv_old, 0)

    @pl.when(own == 1)
    def _():
        from_turned(out_hbm, out_old, qkv_old.shape[0])

    @pl.when(own == 2)
    def _():
        load_two(up_hbm, old, 1)
        moment[...] = muon_keep * old[...] + own_sum[...].astype(f32)

    @pl.when(own == 3)
    def _():
        load_two(down_hbm, old, 0)
        moment[...] = muon_keep * old[...] + own_sum[...].astype(f32)

    all_here()
    blocks = sub_blocks(moment.shape[0])
    starts = [sum(count for count, _ in GRAM_GROUPS[:group]) for group in range(len(GRAM_GROUPS))]
    high[...] = moment[...].astype(bf16)
    low[...] = (moment[...] - high[...].astype(f32)).astype(bf16)
    started = []

    def products(first, count):
        i, j = blocks[first]
        count = min(count, sum(row == i for row, _ in blocks[first:]))
        left, right = pl.ds(i * SUB, SUB), pl.ds(j * SUB, count * SUB)
        total = dot(high[left, :], high[right, :], 1, 1)
        total = total + dot(high[left, :], low[right, :], 1, 1)
        total = total + dot(low[left, :], high[right, :], 1, 1)
        rows = SUB // 8
        for index in range(count):
            for owner in range(8):
                cell = (owner // 4, owner // 2 % 2, owner % 2, first + index)
                part[cell] = total[
                    owner * rows : (owner + 1) * rows, index * SUB : (index + 1) * SUB
                ]
        return count

    def send(source, target, group, slot, axis):
        copy = pltpu.make_async_remote_copy(
            src_ref=source,
            dst_ref=target,
            send_sem=send_sem.at[group, slot],
            recv_sem=recv_sem.at[group, slot],
            device_id=others[axis],
            device_id_type=MESH,
        )
        copy.start()
        started.append(copy)
        return copy

    def cells(fixed, flipped=None):
        return tuple(
            1 - here[name] if name == flipped else here[name] if name in fixed else slice(None)
            for name in GRAM_AXES
        )

    class Walk:
        def __init__(self, group):
            count, order = GRAM_GROUPS[group]
            self.group, self.stage = group, 0
            self.order = [GRAM_AXES["fnx".index(letter)] for letter in order]
            self.mine = (pl.ds(starts[group], count),)
            self.came = [
                ref.at[(slice(None),) * (2 - stage) + self.mine]
                for stage, ref in enumerate((came_one, came_two, came_three))
            ]

        def advance(self):
            stage, order = self.stage, self.order
            mine = self.mine
            if stage:
                self.copy.wait_recv()
            if 1 <= stage <= 3:
                kept = cells(order[:stage]) + mine
                total = part[kept] + self.came[stage - 1][...]
                if stage == 3:
                    out[kept] = total
                else:
                    part[kept] = total
            if stage < 3:
                source = part.at[cells(order[:stage], order[stage]) + mine]
                self.copy = send(source, self.came[stage], self.group, stage, order[stage])
            elif stage < 6:
                block = out.at[cells(order[: 6 - stage]) + mine]
                self.copy = send(block, block, self.group, stage, order[5 - stage])
            self.stage += 1

    walks = [Walk(group) for group in range(len(GRAM_GROUPS))]
    for group in GRAM_PLAN:
        if walks[group].stage == 0:
            first, end = starts[group], starts[group] + GRAM_GROUPS[group][0]
            while first < end:
                first += products(first, end - first)
        walks[group].advance()

    e = ortho[0]
    for index, (i, j) in enumerate(blocks):
        value = out[:, :, :, index].reshape(SUB, SUB)
        e[i * SUB : (i + 1) * SUB, j * SUB : (j + 1) * SUB] = value
        if i != j:
            e[j * SUB : (j + 1) * SUB, i * SUB : (i + 1) * SUB] = value.T

    across, beside = [], []

    def share(slot, rows, kind, other):
        block = factors.at[slot, rows]
        index = rows.start // TILE
        copy = pltpu.make_async_remote_copy(
            src_ref=block,
            dst_ref=block,
            send_sem=share_send.at[index, kind],
            recv_sem=share_recv.at[index, kind],
            device_id=other,
            device_id_type=MESH,
        )
        copy.start()
        started.append(copy)
        return copy

    def emit(rows, value):
        factors[own, rows, :] = value
        across.append((rows, share(own, rows, 0, beyond)))
        beside.append(share(own, rows, 1, partner))

    newton_schulz(e, moment, *ortho, emit)
    far = 2 * (1 - y) + core
    stores = []

    def store(slot):
        copy = pltpu.make_async_copy(
            factors.at[slot], factors_hbm.at[slot], load_sem.at[2 + len(stores)]
        )
        copy.start()
        stores.append(copy)

    store(own)
    for copy in beside:
        copy.wait_recv()
    store(2 * y + 1 - core)
    passed = []
    for rows, copy in across:
        copy.wait_recv()
        passed.append(share(far, rows, 2, partner))
    store(far)
    for copy in passed:
        copy.wait_recv()
    store(2 * (1 - y) + 1 - core)
    for copy in stores:
        copy.wait()
    for copy in started:
        copy.wait_send()


def muon_factors(sums, *olds):
    size, cols = olds[2].shape
    count = len(sub_blocks(size))
    groups = len(GRAM_GROUPS)
    rows = (SUB // 8, SUB)

    def wide(*dims):
        return pltpu.VMEM(dims, f32)

    return pl.pallas_call(
        muon_kernel,
        out_shape=jax.ShapeDtypeStruct((4, size, cols), bf16),
        in_specs=[ANY] * 5,
        out_specs=ANY,
        scratch_shapes=[
            pltpu.VMEM((4, size, cols), bf16),
            pltpu.VMEM((size, cols), bf16),
            wide(*olds[0].shape),
            wide(*olds[1].shape),
            wide(size, cols),
            wide(size, cols),
            wide(2, 2, 2, count, *rows),
            wide(2, 2, 2, count, *rows),
            wide(2, 2, count, *rows),
            wide(2, count, *rows),
            wide(count, *rows),
            pltpu.VMEM((size, cols), bf16),
            pltpu.VMEM((size, cols), bf16),
            pltpu.SemaphoreType.DMA((6,)),
            pltpu.SemaphoreType.DMA((groups, 6)),
            pltpu.SemaphoreType.DMA((groups, 6)),
            pltpu.SemaphoreType.DMA((size // TILE, 3)),
            pltpu.SemaphoreType.DMA((size // TILE, 3)),
        ]
        + ortho_scratch(size, cols),
        compiler_params=pltpu.CompilerParams(
            vmem_limit_bytes=58 * MIB, collective_id=1, has_side_effects=True
        ),
        name="muon_factors",
    )(sums, *olds)


def window(start, width, total):
    size = -(-(width + 96) // LANES) * LANES
    first = jnp.minimum(start // LANES * LANES, total - size)
    return pl.ds(pl.multiple_of(first, LANES), size), start - first


def finish_kernel(
    factors_hbm,
    sums_hbm,
    qkv_hbm,
    out_hbm,
    up_hbm,
    down_hbm,
    qkv_old_hbm,
    out_old_hbm,
    up_old_hbm,
    down_old_hbm,
    mixed_hbm,
    grad_hbm,
    vec_grad,
    vectors,
    first_old,
    second_old,
    mixed_out,
    grad_out,
    qkv_moment_out,
    out_moment_out,
    up_moment_out,
    down_moment_out,
    qkv_out,
    out_out,
    up_out,
    down_out,
    first_new,
    second_new,
    vec_new,
    factors,
    sums,
    qkv_w,
    out_w,
    up_w,
    down_w,
    qkv_moment,
    out_moment,
    up_moment,
    down_moment,
    qkv_new,
    out_new,
    up_new,
    down_new,
    turned,
    load_sem,
    store_sem,
):
    shrink = 1.0 - muon_rate * muon_decay
    dp_id = lax.axis_index("dp")
    qkv_cols, out_cols = qkv_new.shape[0], out_new.shape[0]
    qkv_lanes, qkv_skip = window(dp_id * qkv_cols, qkv_cols, 3 * D)
    out_lanes, out_skip = window(dp_id * out_cols, out_cols, D)
    block = pl.ds(pl.multiple_of(dp_id * UNIT, UNIT), UNIT)
    pairs = {
        "sums": (sums_hbm, sums),
        "up_moment": (up_old_hbm, up_moment),
        "down_moment": (down_old_hbm, down_moment),
        "factors": (factors_hbm, factors),
        "up": (up_hbm.at[:, block], up_w),
        "down": (down_hbm.at[block], down_w),
        "qkv_moment": (qkv_old_hbm, qkv_moment),
        "out_moment": (out_old_hbm, out_moment),
        "qkv": (qkv_hbm.at[:, qkv_lanes], qkv_w),
        "out": (out_hbm.at[:, out_lanes], out_w),
    }
    loads = {
        name: pltpu.make_async_copy(source, target, load_sem.at[index])
        for index, (name, (source, target)) in enumerate(pairs.items())
    }
    for load in loads.values():
        load.start()
    stores = []

    def store(source, target):
        stores.append(pltpu.make_async_copy(source, target, store_sem.at[len(stores)]))
        stores[-1].start()

    store(mixed_hbm, mixed_out)
    store(grad_hbm, grad_out)

    grad = vec_grad[:VEC_BLOCK]
    first = beta_first * first_old[...] + (1.0 - beta_first) * grad
    second = beta_second * second_old[...] + (1.0 - beta_second) * grad * grad
    first_new[...] = first
    second_new[...] = second
    first = first / (1.0 - beta_first**STEP)
    second = second / (1.0 - beta_second**STEP)
    own = jnp.zeros_like(grad)
    for index in range(8):
        rows = vectors[index * VEC_BLOCK : (index + 1) * VEC_BLOCK]
        own = jnp.where(dp_id == index, rows, own)
    vec_new[...] = own - adam_rate * first / (jnp.sqrt(second) + adam_eps)

    def step(index, rate, turned=False):
        value = factors[index]
        value = transposed(value) if turned else value
        return muon_rate * rate * value.astype(f32)

    loads["sums"].wait()
    for index, name, target, out in (
        (1, "up_moment", up_moment, up_moment_out),
        (0, "down_moment", down_moment, down_moment_out),
    ):
        loads[name].wait()
        target[...] = muon_keep * target[...] + sums[index].astype(f32)
        store(target, out)
    loads["qkv_moment"].wait()
    loads["out_moment"].wait()
    for half in range(2):
        cols = slice(half * HALF, (half + 1) * HALF)
        value = sums[2, cols].astype(f32)
        qkv_moment[:, cols] = muon_keep * qkv_moment[:, cols] + value[:qkv_cols]
        out_moment[:, cols] = muon_keep * out_moment[:, cols] + value[qkv_cols:]
    store(qkv_moment, qkv_moment_out)
    store(out_moment, out_moment_out)
    loads["factors"].wait()
    loads["up"].wait()
    up_new[...] = up_w[...].astype(f32) * shrink - step(2, math.sqrt(max(1.0, FF / D)))
    store(up_new, up_out)
    loads["down"].wait()
    down_new[...] = down_w[...].astype(f32) * shrink - step(3, 1.0, True)
    store(down_new, down_out)
    loads["qkv"].wait()
    turned[...] = transposed(qkv_w[...]).astype(f32)
    rows = pl.ds(pl.multiple_of(qkv_skip, 32), qkv_cols)
    qkv_new[...] = turned[rows, :] * shrink - step(0, math.sqrt(3.0), True)[:qkv_cols]
    store(qkv_new, qkv_out)
    loads["out"].wait()
    turned[: out_w.shape[1], :] = transposed(out_w[...]).astype(f32)
    rows = pl.ds(pl.multiple_of(out_skip, 32), out_cols)
    out_new[...] = turned[rows, :] * shrink - step(1, 1.0, True)[qkv_cols:]
    store(out_new, out_out)
    for copy in stores:
        copy.wait()


def finish(factors, sums, weights, olds, mixed, input_grad, vec, vectors, adam):
    shapes = [old.shape for old in olds]
    news = shapes[:3] + [shapes[3][::-1]]

    def wide(shape):
        return pltpu.VMEM(shape, f32)

    return pl.pallas_call(
        finish_kernel,
        out_shape=tuple(
            jax.ShapeDtypeStruct(shape, f32)
            for shape in [mixed.shape, input_grad.shape] + shapes + news + [(VEC_BLOCK, LANES)] * 3
        ),
        in_specs=[ANY] * 12 + [VMEM] * 4,
        out_specs=(ANY,) * 10 + (VMEM,) * 3,
        scratch_shapes=[
            pltpu.VMEM(factors.shape, bf16),
            pltpu.VMEM(sums.shape, bf16),
            pltpu.VMEM((D, 384), bf16),
            pltpu.VMEM((D, 256), bf16),
            pltpu.VMEM((D, UNIT), bf16),
            pltpu.VMEM((UNIT, D), bf16),
        ]
        + [wide(shape) for shape in shapes + news]
        + [
            wide((384, D)),
            pltpu.SemaphoreType.DMA((10,)),
            pltpu.SemaphoreType.DMA((10,)),
        ],
        compiler_params=pltpu.CompilerParams(vmem_limit_bytes=48 * MIB),
        name="finish",
    )(factors, sums, *weights, *olds, mixed, input_grad, vec, vectors, *adam)


def swap(value, axis, bit):
    size = lax.axis_size(axis)
    return lax.ppermute(value, axis, [(i, i ^ bit) for i in range(size)])


def scatter_head(value, bit, position):
    half = value.shape[1] // 2
    mine = lax.dynamic_slice_in_dim(value, position * half, half, 1)
    other = lax.dynamic_slice_in_dim(value, (1 - position) * half, half, 1)
    return (mine.astype(f32) + swap(other, "head", bit).astype(f32)).astype(bf16)


def scatter_dp_pair(value, position):
    paired = value.reshape((value.shape[0] // 2, 2) + value.shape[1:])
    mine = lax.dynamic_index_in_dim(paired, position, 1, False)
    other = lax.dynamic_index_in_dim(paired, 1 - position, 1, False)
    return (mine.astype(f32) + swap(other, "dp", 1).astype(f32)).astype(bf16)


def scatter_dp_rest(value, place):
    ranks = value.shape[0]
    total = lax.dynamic_index_in_dim(value, place, 0, False).astype(f32)
    for step in range(1, ranks):
        sent = lax.dynamic_index_in_dim(value, place ^ step, 0, False)
        total = total + swap(sent, "dp", 2 * step).astype(f32)
    return total


def local(
    tokens,
    cotangent,
    qkv_weight,
    out_weight,
    up_weight,
    down_weight,
    vectors,
    qkv_moment,
    out_moment,
    up_moment,
    down_moment,
    adam_first,
    adam_second,
    bucket_class,
    row_lengths,
):
    n_dp = lax.axis_size("dp")
    n_head = lax.axis_size("head")
    dp_id = lax.axis_index("dp")
    head_id = lax.axis_index("head")
    core, side = head_id % 2, head_id // 2
    tok, width = tokens.shape
    hidden = up_weight.shape[1]
    half = width // 2
    qkv_cols, out_cols = qkv_moment.shape[1], out_moment.shape[1]
    shrink = 1.0 - muon_rate * muon_decay

    def weight_block(weight, cols, dim):
        return lax.dynamic_slice_in_dim(weight, dp_id * cols, cols, dim)

    block = head_id.astype(jnp.int32)[None]
    vec_len = vectors.shape[0] // n_dp
    if (n_dp, n_head, tok) == (8, 4, 256):
        mixed, input_grad, sums, vec = layer(
            bucket_class,
            row_lengths,
            tokens,
            cotangent,
            vectors,
            qkv_weight,
            out_weight,
            up_weight,
            down_weight,
        )
        sums = sums.reshape(3, width, -1)
        olds = [qkv_moment.T, out_moment.T, up_moment, down_moment]
        mixed, input_grad, *results = finish(
            muon_factors(sums, *olds),
            sums,
            [qkv_weight, out_weight, up_weight, down_weight],
            olds,
            mixed,
            input_grad,
            vec,
            vectors.reshape(-1, LANES),
            [adam_first.reshape(-1, LANES), adam_second.reshape(-1, LANES)],
        )
        moments, new_weights = results[:4], results[4:8]
        vec_first, vec_second, vec_new = (value.reshape(vec_len) for value in results[8:])
        moments = [moments[0].T, moments[1].T, *moments[2:]]
        new_weights = [new_weights[0].T, new_weights[1].T, *new_weights[2:]]
    else:
        pieces = split_vectors(vectors, width, hidden)
        bias_query, bias_value, bias_out, gain_one, shift_one = pieces[:5]
        bias_up, bias_down, gain_two, shift_two = pieces[5:]
        bias_qkv = jnp.concatenate([bias_query, jnp.zeros_like(bias_query), bias_value])

        def column_half(value, which):
            return lax.dynamic_slice_in_dim(value, which * half, half, 1)

        qkv = (dot(tokens, qkv_weight, 1, 0) + bias_qkv).astype(bf16)
        other = swap(qkv[:, width:], "head", 1)
        attended = attend(block, bucket_class, row_lengths, qkv, other)
        attn_val = dot(attended, out_weight, 1, 0) + bias_out
        resid_one = tokens.astype(f32) + attn_val
        centre = resid_one - jnp.mean(resid_one, axis=-1, keepdims=True)
        rstd_one = lax.rsqrt(jnp.mean(centre * centre, axis=-1, keepdims=True) + norm_eps)
        zhat_one = centre * rstd_one
        normed_one = zhat_one * gain_one + shift_one
        normed_low = normed_one.astype(bf16)
        up_val = dot(normed_low, up_weight, 1, 0) + bias_up
        phi_cum = 0.5 * (1.0 + lax.erf(up_val * (0.5**0.5)))
        active_low = (up_val * phi_cum).astype(bf16)
        slope = phi_cum + up_val * jnp.exp(-0.5 * up_val * up_val) * (1.0 / math.sqrt(2.0 * math.pi))
        down_val = dot(active_low, down_weight, 1, 0) + bias_down
        resid_two = normed_one + down_val
        centre = resid_two - jnp.mean(resid_two, axis=-1, keepdims=True)
        rstd_two = lax.rsqrt(jnp.mean(centre * centre, axis=-1, keepdims=True) + norm_eps)
        zhat_two = centre * rstd_two
        mixed = zhat_two * gain_two + shift_two

        def norm_back(grad, gain, zhat, rstd):
            inner = grad * gain
            mean = jnp.mean(inner, axis=-1, keepdims=True)
            slant = jnp.mean(inner * zhat, axis=-1, keepdims=True)
            return (inner - mean - zhat * slant) * rstd, jnp.sum(grad * zhat, axis=0), jnp.sum(grad, axis=0)

        grad_two, grad_gain_two, grad_shift_two = norm_back(
            cotangent.astype(f32), gain_two, zhat_two, rstd_two
        )
        grad_down_low = grad_two.astype(bf16)
        grad_bias_down = jnp.sum(grad_down_low, axis=0, dtype=f32)

        x_id, z_id = dp_id % 2, dp_id // 2

        grad_up_low = (dot(grad_down_low, down_weight, 1, 1) * slope).astype(bf16)
        grad_bias_up = jnp.sum(grad_up_low, axis=0, dtype=f32)
        grad_normed = grad_two + dot(grad_up_low, up_weight, 1, 1)
        grad_one, grad_gain_one, grad_shift_one = norm_back(grad_normed, gain_one, zhat_one, rstd_one)
        grad_attn_low = grad_one.astype(bf16)
        grad_bias_out = jnp.sum(grad_attn_low, axis=0, dtype=f32)
        grad_heads = dot(grad_attn_low, out_weight, 1, 1).astype(bf16)
        grad_query, own, sent = attend_back(block, bucket_class, row_lengths, qkv, other, grad_heads)
        grad_kv = (own + swap(sent, "head", 1).astype(f32)).astype(bf16)
        grad_qkv = jnp.concatenate([grad_query, grad_kv], axis=1)
        grad_bias_qkv = jnp.sum(grad_qkv, axis=0, dtype=f32)
        input_grad = grad_one + dot(grad_qkv, qkv_weight, 1, 1)
        grad_vector = jnp.concatenate(
            [
                grad_bias_qkv[:width],
                grad_bias_qkv[2 * width :],
                grad_bias_out,
                grad_gain_one,
                grad_shift_one,
                grad_bias_up,
                grad_bias_down,
                grad_gain_two,
                grad_shift_two,
            ]
        )
        grad_vector = grad_vector + swap(grad_vector, "head", 1)
        wides = [active_low, grad_up_low, grad_attn_low, grad_qkv]
        narrows = [grad_down_low, normed_low, attended, tokens]

        def both_halves(value):
            return jnp.concatenate(
                [column_half(value, core), swap(column_half(value, 1 - core), "head", 1)], axis=0
            )

        def weight_grad(wide, narrow):
            wide = jnp.concatenate([wide, swap(wide, "head", 1)], axis=0)
            value = dot(wide, both_halves(narrow), 0, 0).astype(bf16)
            return value.reshape(n_dp, value.shape[0] // n_dp, half)

        def reduce_y_first(value):
            return scatter_dp_rest(scatter_dp_pair(scatter_head(value, 2, side), x_id), z_id)

        def reduce_x_first(value):
            return scatter_dp_rest(scatter_head(scatter_dp_pair(value, x_id), 2, side), z_id)

        def spread(value):
            value = value.astype(bf16)
            came = swap(value, "head", 2)
            value = jnp.concatenate(
                [jnp.where(side == 0, value, came), jnp.where(side == 0, came, value)], axis=0
            )
            came = swap(value, "head", 1)
            return jnp.concatenate(
                [jnp.where(core == 0, value, came), jnp.where(core == 0, came, value)], axis=1
            ).astype(f32)

        down_part, up_part, out_part, qkv_part = [
            weight_grad(wide, narrow) for wide, narrow in zip(wides, narrows)
        ]
        vec_rows = 16
        vec_part = grad_vector.reshape(n_dp, vec_len)
        vec_part = jnp.pad(vec_part, ((0, 0), (0, vec_rows * width - vec_len)))
        vec_part = vec_part.reshape(n_dp, vec_rows, width)
        vec_part = lax.dynamic_slice_in_dim(vec_part, core * half, half, 2).astype(bf16)
        down_new = spread(reduce_x_first(down_part))
        up_new = spread(reduce_y_first(up_part))
        tail_new = spread(
            reduce_y_first(jnp.concatenate([qkv_part, out_part, vec_part], axis=1))
        )
        grads = [
            tail_new[:qkv_cols].T,
            tail_new[qkv_cols : qkv_cols + out_cols].T,
            up_new.T,
            down_new.T,
        ]
        grad_vec = tail_new[qkv_cols + out_cols :].reshape(-1)[:vec_len]
        moments = [
            muon_keep * old + grad
            for old, grad in zip([qkv_moment, out_moment, up_moment, down_moment], grads)
        ]
        most = max(m.shape[1] for m in moments)
        padded = [jnp.pad(m, ((0, 0), (0, most - m.shape[1]))) for m in moments]
        chosen = padded[-1]
        for index in range(len(padded) - 2, -1, -1):
            chosen = jnp.where(head_id == index, padded[index], chosen)
        gram_mat = lax.dot_general(
            chosen, chosen, (((1,), (1,)), ((), ())), precision=lax.Precision.HIGH
        )
        own_factor = orthogonalize(lax.psum(gram_mat, "dp"), chosen)
        across = swap(own_factor, "head", 2)
        low_pair = jnp.where(side == 0, own_factor, across)
        high_pair = jnp.where(side == 0, across, own_factor)
        near_low = swap(low_pair, "head", 1)
        near_high = swap(high_pair, "head", 1)
        factors = [
            jnp.where(core == 0, low_pair, near_low),
            jnp.where(core == 0, near_low, low_pair),
            jnp.where(core == 0, high_pair, near_high),
            jnp.where(core == 0, near_high, high_pair),
        ]
        factors = [o[:, : m.shape[1]].astype(f32) for o, m in zip(factors, moments)]
        factors[3] = factors[3].T
        old_weights = [
            weight_block(qkv_weight, qkv_cols, 1),
            weight_block(out_weight, out_cols, 1),
            weight_block(up_weight, up_moment.shape[1], 1),
            weight_block(down_weight, down_moment.shape[1], 0),
        ]

        rates = (math.sqrt(3.0), 1.0, math.sqrt(max(1.0, hidden / width)), 1.0)
        new_weights = [
            old.astype(f32) * shrink - muon_rate * rate * factor
            for old, rate, factor in zip(old_weights, rates, factors)
        ]

        vec_old = lax.dynamic_slice_in_dim(vectors, dp_id * vec_len, vec_len, 0)
        vec_first = beta_first * adam_first + (1.0 - beta_first) * grad_vec
        vec_second = beta_second * adam_second + (1.0 - beta_second) * grad_vec * grad_vec
        first_hat = vec_first / (1.0 - beta_first**STEP)
        second_hat = vec_second / (1.0 - beta_second**STEP)
        vec_new = vec_old - adam_rate * first_hat / (jnp.sqrt(second_hat) + adam_eps)
    return (mixed, input_grad, *moments, *new_weights, vec_first, vec_second, vec_new)


def solution(mesh):
    tokens_spec = P(("dp", "head"), None)
    block_spec = P(None, "dp")
    return jax.shard_map(
        local,
        mesh=mesh,
        in_specs=(
            tokens_spec,
            tokens_spec,
            P(),
            P(),
            P(),
            P(),
            P(),
            block_spec,
            block_spec,
            block_spec,
            block_spec,
            P("dp"),
            P("dp"),
            P("dp"),
            P("dp", None),
        ),
        out_specs=(
            tokens_spec,
            tokens_spec,
            block_spec,
            block_spec,
            block_spec,
            block_spec,
            block_spec,
            block_spec,
            block_spec,
            P("dp", None),
            P("dp"),
            P("dp"),
            P("dp"),
        ),
        check_vma=False,
    )
```

```python
import functools
import itertools
import math

import jax
import jax.numpy as jnp
from jax import lax
from jax.experimental import pallas as pl
from jax.experimental.pallas import tpu as pltpu
from jax.sharding import PartitionSpec as P

D = 768
HEADS = 12
HEAD_DIM = 64
FF = 3072
BASE_LEN = 128
NS_STEPS = 5
STEP = 5
MAX_LEN = 512

f32 = jnp.float32
bf16 = jnp.bfloat16

norm_eps = 1e-12
masked_score = -1000000000.0
quintic_a = 3.4445
quintic_b = -4.775
quintic_c = 2.0315
muon_rate = 1.0
muon_decay = 0.01
muon_keep = 0.5
adam_rate = 0.2
beta_first = 0.9
beta_second = 0.999
adam_eps = 1e-08
MIB = 1024 * 1024


def dot(left, right, left_dim, right_dim):
    return lax.dot_general(
        left, right, (((left_dim,), (right_dim,)), ((), ())), preferred_element_type=f32
    )


def split_vectors(vectors, width, hidden):
    lengths_list = [width] * 5 + [hidden] + [width] * 3
    pieces = []
    offset = 0
    for length in lengths_list:
        pieces.append(vectors[offset : offset + length])
        offset = offset + length
    return pieces


def allowed_mask(class_ref, length_ref, block, tok):
    shift = class_ref[0] + int(math.log2(BASE_LEN))
    query_place = block * tok + lax.broadcasted_iota(jnp.int32, (tok, 1), 0)
    lane = lax.broadcasted_iota(jnp.int32, (1, 2 * tok), 1)
    own = lane < tok
    key_place = jnp.where(own, block * tok + lane, (block ^ 1) * tok + lane - tok)
    key_row = lax.shift_right_logical(key_place, jnp.broadcast_to(shift, key_place.shape))
    offset = key_place - lax.shift_left(key_row, jnp.broadcast_to(shift, key_place.shape))
    row_len = jnp.zeros_like(key_row)
    for slot in range(length_ref.shape[1]):
        row_len = jnp.where(key_row == slot, length_ref[0, slot], row_len)
    key_row = jnp.where(offset < row_len, key_row, -1)
    query_row = lax.shift_right_logical(query_place, jnp.broadcast_to(shift, query_place.shape))
    return query_row == key_row


def half_masks():
    lane = lax.broadcasted_iota(jnp.int32, (1, 2 * HEAD_DIM), 1)
    first = (lane < HEAD_DIM).astype(f32)
    return (first.astype(bf16), (1.0 - first).astype(bf16)), lane < HEAD_DIM


def head_prob(query, keys, allowed):
    score = jnp.where(allowed, dot(query, keys, 1, 1) * HEAD_DIM ** (-0.5), masked_score)
    exponent = jnp.exp(score - jnp.max(score, axis=-1, keepdims=True))
    return exponent / jnp.sum(exponent, axis=-1, keepdims=True)


def attend_kernel(block_ref, class_ref, length_ref, qkv_ref, other_ref, out_ref):
    tok = qkv_ref.shape[0]
    allowed = allowed_mask(class_ref, length_ref, block_ref[0], tok)
    masks, first = half_masks()
    for pair in range(HEADS // 2):
        cols = pl.ds(pair * 2 * HEAD_DIM, 2 * HEAD_DIM)
        kcols = pl.ds(D + pair * 2 * HEAD_DIM, 2 * HEAD_DIM)
        vcols = pl.ds(2 * D + pair * 2 * HEAD_DIM, 2 * HEAD_DIM)
        query = qkv_ref[:, cols]
        keys = jnp.concatenate([qkv_ref[:, kcols], other_ref[:, cols]], axis=0)
        values = jnp.concatenate([qkv_ref[:, vcols], other_ref[:, kcols]], axis=0)
        outs = []
        for mask in masks:
            prob = head_prob(query * mask, keys, allowed)
            outs.append(dot(prob.astype(bf16), values, 1, 0))
        out_ref[:, cols] = jnp.where(first, outs[0], outs[1]).astype(bf16)


def attend_back_kernel(
    block_ref, class_ref, length_ref, qkv_ref, other_ref, grad_ref, dq_ref, own_ref, send_ref
):
    tok = qkv_ref.shape[0]
    allowed = allowed_mask(class_ref, length_ref, block_ref[0], tok)
    masks, first = half_masks()
    scale = HEAD_DIM ** (-0.5)
    for pair in range(HEADS // 2):
        cols = pl.ds(pair * 2 * HEAD_DIM, 2 * HEAD_DIM)
        kcols = pl.ds(D + pair * 2 * HEAD_DIM, 2 * HEAD_DIM)
        vcols = pl.ds(2 * D + pair * 2 * HEAD_DIM, 2 * HEAD_DIM)
        query = qkv_ref[:, cols]
        keys = jnp.concatenate([qkv_ref[:, kcols], other_ref[:, cols]], axis=0)
        values = jnp.concatenate([qkv_ref[:, vcols], other_ref[:, kcols]], axis=0)
        grad = grad_ref[:, cols]
        dqs, dk, dv = [], None, None
        for mask in masks:
            head_query = query * mask
            head_grad = grad * mask
            prob = head_prob(head_query, keys, allowed)
            part_v = dot(prob.astype(bf16), head_grad, 0, 0)
            dprob = dot(head_grad, values, 1, 1)
            dscore = prob * (dprob - jnp.sum(prob * dprob, axis=-1, keepdims=True))
            dscore = dscore.astype(bf16)
            dqs.append(dot(dscore, keys, 1, 0))
            part_k = dot(dscore, head_query, 0, 0)
            dk = part_k if dk is None else dk + part_k
            dv = part_v if dv is None else dv + part_v
        dk = dk * scale
        dq_ref[:, cols] = (jnp.where(first, dqs[0], dqs[1]) * scale).astype(bf16)
        own_ref[:, cols] = dk[:tok]
        own_ref[:, kcols] = dv[:tok]
        send_ref[:, cols] = dk[tok:].astype(bf16)
        send_ref[:, kcols] = dv[tok:].astype(bf16)


SMEM = pl.BlockSpec(memory_space=pltpu.SMEM)
VMEM = pl.BlockSpec(memory_space=pltpu.VMEM)
ANY = pl.BlockSpec(memory_space=pl.ANY)


def attend(block, row_class, lengths, qkv, other):
    tok = qkv.shape[0]
    return pl.pallas_call(
        attend_kernel,
        out_shape=jax.ShapeDtypeStruct((tok, D), bf16),
        in_specs=[SMEM, SMEM, SMEM, VMEM, VMEM],
        out_specs=VMEM,
        compiler_params=pltpu.CompilerParams(vmem_limit_bytes=32 * MIB),
        name="attend",
    )(block, row_class, lengths, qkv, other)


def attend_back(block, row_class, lengths, qkv, other, grad):
    tok = qkv.shape[0]
    return pl.pallas_call(
        attend_back_kernel,
        out_shape=(
            jax.ShapeDtypeStruct((tok, D), bf16),
            jax.ShapeDtypeStruct((tok, 2 * D), f32),
            jax.ShapeDtypeStruct((tok, 2 * D), bf16),
        ),
        in_specs=[SMEM, SMEM, SMEM, VMEM, VMEM, VMEM],
        out_specs=(VMEM, VMEM, VMEM),
        compiler_params=pltpu.CompilerParams(vmem_limit_bytes=32 * MIB),
        name="attend_back",
    )(block, row_class, lengths, qkv, other, grad)


CENTRES = (0.0, 0.0, 0.0, 0.8, 0.8)
TILE = 256
SUB = 128


def sub_blocks(size):
    count = size // SUB
    return [(i, j) for i in range(count) for j in range(i, count)]


def newton_schulz(gram, moment, e, f, g, eb, fb, gb, yy, y, emit):
    size = e.shape[0]
    tiles = [slice(i * TILE, (i + 1) * TILE) for i in range(size // TILE)]

    def unit(rows):
        row_id = rows.start + lax.broadcasted_iota(jnp.int32, (TILE, size), 0)
        col_id = lax.broadcasted_iota(jnp.int32, (TILE, size), 1)
        return (row_id == col_id).astype(f32)

    diagonal = jnp.zeros((TILE, size), f32)
    for rows in tiles:
        diagonal = diagonal + gram[rows, :] * unit(rows)
    trace = jnp.sum(jnp.sum(diagonal, axis=0, keepdims=True), axis=1, keepdims=True)
    factor = 1.0 / (jnp.sqrt(trace) + 1e-07)
    square_factor = factor * factor
    for rows in tiles:
        value = gram[rows, :] * square_factor
        e[rows, :] = value
        eb[rows, :] = value.astype(bf16)
        value = moment[rows, :] * factor
        y[rows, :] = value
        yy[0, rows, :] = value.astype(bf16)

    def one_step(centre, after, now, then, last=False):
        keep = quintic_a + quintic_b * centre + quintic_c * centre * centre
        linear = quintic_b + 2.0 * quintic_c * centre
        for rows in tiles:
            value = linear * e[rows, :] + quintic_c * dot(eb[rows, :], eb[...], 1, 0)
            fb[rows, :] = value.astype(bf16)
            if centre:
                f[rows, :] = value
        for rows in tiles:
            value = keep * y[rows, :] + dot(fb[rows, :], now[...], 1, 0)
            if last:
                emit(rows, value.astype(bf16))
            else:
                y[rows, :] = value
                then[rows, :] = value.astype(bf16)
        if last:
            return
        for rows in tiles:
            value = keep * e[rows, :] + dot(eb[rows, :], fb[...], 1, 0)
            if centre:
                value = value + centre * f[rows, :]
            g[rows, :] = value
            gb[rows, :] = value.astype(bf16)
        for rows in tiles:
            value = keep * g[rows, :] + dot(gb[rows, :], fb[...], 1, 0)
            if centre:
                value = value + (centre * keep) * f[rows, :]
            shift = centre * keep * keep - after
            if not isinstance(shift, float) or shift:
                value = value + shift * unit(rows)
            e[rows, :] = value
            eb[rows, :] = value.astype(bf16)

    plain = sum(centre == 0.0 for centre in CENTRES)

    def plain_step(step, carry):
        after = jnp.where(step == plain - 1, CENTRES[plain], 0.0)
        one_step(0.0, after, yy.at[step % 2], yy.at[(step + 1) % 2])
        return carry

    lax.fori_loop(0, plain, plain_step, 0)
    for step in range(plain, NS_STEPS):
        last = step + 1 == NS_STEPS
        after = 0.0 if last else CENTRES[step + 1]
        one_step(CENTRES[step], after, yy.at[step % 2], yy.at[(step + 1) % 2], last)


def ortho_kernel(gram, moment, out, *scratch):
    def emit(rows, value):
        out[rows, :] = value

    newton_schulz(gram, moment, *scratch, emit)


def ortho_scratch(size, cols):
    square, square_low = pltpu.VMEM((size, size), f32), pltpu.VMEM((size, size), bf16)
    wide_low = pltpu.VMEM((2, size, cols), bf16)
    return [square] * 3 + [square_low] * 3 + [wide_low, pltpu.VMEM((size, cols), f32)]


def orthogonalize(gram_mat, moment):
    size, cols = moment.shape
    return pl.pallas_call(
        ortho_kernel,
        out_shape=jax.ShapeDtypeStruct((size, cols), bf16),
        in_specs=[VMEM, VMEM],
        out_specs=VMEM,
        scratch_shapes=ortho_scratch(size, cols),
        compiler_params=pltpu.CompilerParams(vmem_limit_bytes=48 * MIB),
        name="ortho",
    )(gram_mat, moment)


MESH = pl.DeviceIdType.MESH
PIECE = 48
SIDE = 192
UNIT = 2 * SIDE
HALF = D // 2
LANES = 128
VEC_BLOCK = 9
ROWS = 16
CHUNKS = (
    (0, 0, 64, "nfyx"),
    (0, 64, 64, "xynf"),
    (0, 128, 64, "yxnf"),
    (1, 0, 64, "ynxf"),
    (1, 64, 64, "nxyf"),
    (1, 128, 64, "xynf"),
    (2, 0, 48, "xynf"),
    (2, 48, 48, "nxyf"),
    (2, 96, 48, "yxnf"),
    (2, 144, 32, "xynf"),
    (2, 176, 16, "xfyn"),
)
CHUNK_PLAN = (
    (0, 1, 2),
    (),
    (),
    (),
    (),
    (3, 5, 4),
    (0, 1, 2),
    (),
    (),
    (),
    (0, 1, 2, 4, 5, 3),
    (),
    (),
    (0, 7, 8, 10, 9, 6),
    (
        1, 4, 2, 5, 0, 1, 10, 4, 0, 2, 0, 1, 9, 1, 3, 2, 5, 10, 4, 8, 2, 6,
        10, 5, 9, 3, 4, 10, 7, 4, 8, 10, 5, 9, 3, 10, 5, 6, 9, 8, 7, 3, 9, 6,
        3, 9, 8, 7, 8, 6, 8, 7, 6, 7, 6, 7,
    ),
)
BIAS_QUERY, BIAS_VALUE, BIAS_OUT, GAIN_ONE, SHIFT_ONE, BIAS_UP = (i * D for i in range(6))
BIAS_DOWN, GAIN_TWO, SHIFT_TWO = (BIAS_UP + FF + i * D for i in range(3))


def position():
    dp_id, head_id = lax.axis_index("dp"), lax.axis_index("head")
    z, x = dp_id // 2, dp_id % 2
    y, core = head_id // 2, head_id % 2
    return z, x, y, core


def device(z, x, y, core):
    return (2 * z + x, 2 * y + core)


def flip_z(z, step):
    high, low = z // 2, z % 2
    high = 1 - high if step // 2 else high
    low = 1 - low if step % 2 else low
    return 2 * high + low


def greet(others):
    barrier = pltpu.get_barrier_semaphore()
    for other in others:
        pl.semaphore_signal(barrier, inc=1, device_id=other, device_id_type=MESH)
    return lambda: pl.semaphore_wait(barrier, len(others))


def by_rows(count, body, init=None, together=4):
    def step(index, carry):
        for part in range(together):
            start = (index * together + part) * ROWS
            carry = body(pl.ds(pl.multiple_of(start, ROWS), ROWS), carry)
        return carry

    return lax.fori_loop(0, count // (ROWS * together), step, init)


def row_mean(value):
    return jnp.sum(value, axis=-1, keepdims=True) * (1.0 / D)


def fold(value):
    return jnp.sum(value.reshape(value.shape[0] // 8, 8, value.shape[1]), axis=0)


def column_sum(value):
    return jnp.sum(value, axis=0, keepdims=True)


def transposed(value):
    side = 2 * LANES
    row_id = lax.broadcasted_iota(jnp.int32, (side, side), 0)
    unit = (row_id == lax.broadcasted_iota(jnp.int32, (side, side), 1)).astype(f32).astype(bf16)
    blocks = []
    for start in range(0, value.shape[1], side):
        block = value[:, start : start + side]
        size = block.shape[1]
        blocks.append(dot(unit[:size, :size], block, 1, 1).astype(bf16))
    return jnp.concatenate(blocks, axis=0)


def layer_kernel(
    row_class,
    lengths,
    tokens,
    cotangent,
    vectors,
    qkv_hbm,
    out_hbm,
    up_hbm,
    down_hbm,
    mixed_hbm,
    grad_hbm,
    sums_hbm,
    vec_sum,
    mixed,
    input_grad,
    sums,
    qkv_w,
    out_w,
    up_w,
    down_w,
    query,
    query_turned,
    keys_values,
    keys_turned,
    prob,
    attended,
    normed_low,
    grad_down,
    grad_attn,
    narrow_tokens,
    narrow_attended,
    narrow_normed,
    narrow_grad,
    active,
    grad_up,
    attn_turned,
    qkv_turned,
    exchanged,
    grad_heads,
    heads_turned,
    slope,
    normed_one,
    zhat_one,
    rstd_one,
    grad_two,
    work,
    vec,
    vec_core,
    vec_y,
    vec_x,
    vec_z,
    part,
    came_one,
    came_two,
    came_three,
    came_four,
    load_sem,
    store_sem,
    pair_send,
    pair_recv,
    send_sem,
    recv_sem,
):
    grad_one = normed_one
    z, x, y, core = position()
    tok = tokens.shape[0]
    thirds = [slice(index * D, (index + 1) * D) for index in range(3)]
    loads = {
        name: pltpu.make_async_copy(source, target, load_sem.at[index])
        for index, (name, source, target) in enumerate(
            (
                ("key", qkv_hbm.at[:, thirds[1]], qkv_w.at[:, thirds[1]]),
                ("value", qkv_hbm.at[:, thirds[2]], qkv_w.at[:, thirds[2]]),
                ("query", qkv_hbm.at[:, thirds[0]], qkv_w.at[:, thirds[0]]),
                ("out", out_hbm, out_w),
                ("up", up_hbm, up_w),
                ("down", down_hbm, down_w),
            )
        )
    }
    for name in ("key", "value", "query"):
        loads[name].start()
    stores = []

    def store(source, target):
        stores.append(pltpu.make_async_copy(source, target, store_sem.at[len(stores)]))
        stores[-1].start()

    beyond = device(z, x, 1 - y, core)
    beside = device(z, 1 - x, y, core)
    partner = device(z, x, y, 1 - core)
    along = [device(flip_z(z, step), x, y, core) for step in (1, 2, 3)]
    all_here = greet([beyond, beside, partner] + along)
    started = []

    def remote(source, target, send_at, recv_at, other):
        copy = pltpu.make_async_remote_copy(
            src_ref=source,
            dst_ref=target,
            send_sem=send_at,
            recv_sem=recv_at,
            device_id=other,
            device_id_type=MESH,
        )
        copy.start()
        started.append(copy)
        return copy

    pair_count = []

    def to_partner(source, target):
        slot = len(pair_count)
        pair_count.append(slot)
        return remote(source, target, pair_send.at[slot], pair_recv.at[slot], partner)

    own_half = pl.ds(pl.multiple_of(core * HALF, HALF), HALF)
    other_half = pl.ds(pl.multiple_of((1 - core) * HALF, HALF), HALF)

    def span(start, length=D):
        return vectors[0:1, start : start + length]

    def put_vec(start, value):
        for index in range(value.shape[1] // LANES):
            block, row = divmod(start // LANES + index, VEC_BLOCK)
            vec[block, row : row + 1, :] = value[:, index * LANES : (index + 1) * LANES]

    vec[...] = jnp.zeros_like(vec)

    own_rows = pl.ds(0, tok)
    far_rows = pl.ds(tok, tok)
    own_lanes, far_lanes = own_rows, far_rows

    def share_half(value, narrow):
        narrow[own_rows, :] = value[:, own_half]
        return to_partner(value.at[:, other_half], narrow.at[far_rows])

    kv_came = []
    for name, index, start in (("key", 1, None), ("value", 2, BIAS_VALUE)):
        loads[name].wait()
        value = dot(tokens[...], qkv_w[:, thirds[index]], 1, 0)
        if start is not None:
            value = value + span(start)
        cols = slice((index - 1) * D, index * D)
        keys_values[own_rows, cols] = value.astype(bf16)
        if index == 1:
            all_here()
            for name in ("out", "up", "down"):
                loads[name].start()
        kv_came.append(
            to_partner(keys_values.at[own_rows, cols], keys_values.at[far_rows, cols])
        )
    loads["query"].wait()
    value = dot(tokens[...], qkv_w[:, thirds[0]], 1, 0) + span(BIAS_QUERY)
    query[...] = value.astype(bf16)
    query_turned[...] = transposed(query[...])
    allowed = allowed_mask(row_class, lengths, 2 * y + core, tok)
    masks, first = half_masks()
    tokens_came = share_half(tokens, narrow_tokens)
    for copy in kv_came:
        copy.wait_recv()

    scale = HEAD_DIM ** (-0.5)

    def lanes_at(start):
        return pl.ds(pl.multiple_of(start, LANES), LANES)

    def attend_pair(pair, carry):
        cols = lanes_at(pair * LANES)
        keys = keys_values[:, cols]
        values = keys_values[:, lanes_at(D + pair * LANES)]
        outs = []
        for side, mask in enumerate(masks):
            score = dot(query[:, cols] * (mask * scale), keys, 1, 1)
            score = jnp.where(allowed, score, masked_score)
            exponent = jnp.exp(score - jnp.max(score, axis=-1, keepdims=True))
            chance = exponent * (1.0 / jnp.sum(exponent, axis=-1, keepdims=True))
            chance = chance.astype(bf16)
            prob[2 * pair + side] = chance
            outs.append(dot(chance, values, 1, 0))
        attended[:, cols] = jnp.where(first, outs[0], outs[1]).astype(bf16)
        return carry

    lax.fori_loop(0, HEADS // 2, attend_pair, 0)
    attended_came = share_half(attended, narrow_attended)

    loads["out"].wait()
    work[...] = dot(attended[...], out_w[...], 1, 0)

    def norm_one(rows, carry):
        value = tokens[rows, :].astype(f32) + (work[rows, :] + span(BIAS_OUT))
        centre = value - row_mean(value)
        rstd = lax.rsqrt(row_mean(centre * centre) + norm_eps)
        zhat = centre * rstd
        normed = zhat * span(GAIN_ONE) + span(SHIFT_ONE)
        zhat_one[rows, :] = zhat
        rstd_one[rows, :] = jnp.broadcast_to(rstd, (ROWS, LANES))
        normed_one[rows, :] = normed
        normed_low[rows, :] = normed.astype(bf16)
        return carry

    by_rows(tok, norm_one)
    normed_came = share_half(normed_low, narrow_normed)

    loads["up"].wait()
    for tile in range(FF // D):
        cols = slice(tile * D, (tile + 1) * D)
        work[...] = dot(normed_low[...], up_w[:, cols], 1, 0)

        def gelu(rows, carry):
            value = work[rows, :] + span(BIAS_UP + cols.start)
            chance = 0.5 * (1.0 + lax.erf(value * (0.5**0.5)))
            density = jnp.exp(-0.5 * value * value) * (1.0 / math.sqrt(2.0 * math.pi))
            active[rows, cols] = (value * chance).astype(bf16)
            slope[rows, cols] = chance + value * density
            return carry

        by_rows(tok, gelu)
    active_came = to_partner(active.at[own_rows], active.at[far_rows])
    loads["down"].wait()
    work[...] = dot(active[own_rows, :], down_w[...], 1, 0)

    def norm_two(rows, carry):
        value = normed_one[rows, :] + (work[rows, :] + span(BIAS_DOWN))
        centre = value - row_mean(value)
        rstd = lax.rsqrt(row_mean(centre * centre) + norm_eps)
        zhat = centre * rstd
        mixed[rows, :] = zhat * span(GAIN_TWO) + span(SHIFT_TWO)
        grad = cotangent[rows, :].astype(f32)
        inner = grad * span(GAIN_TWO)
        grad_in = (inner - row_mean(inner) - zhat * row_mean(inner * zhat)) * rstd
        grad_two[rows, :] = grad_in
        low = grad_in.astype(bf16)
        grad_down[rows, :] = low
        gain, shift, bias = carry
        return gain + fold(grad * zhat), shift + fold(grad), bias + fold(low.astype(f32))

    zero = jnp.zeros((8, D), f32)
    gain, shift, bias = by_rows(tok, norm_two, (zero, zero, zero))
    store(mixed, mixed_hbm)
    put_vec(GAIN_TWO, column_sum(gain))
    put_vec(SHIFT_TWO, column_sum(shift))
    put_vec(BIAS_DOWN, column_sum(bias))
    grad_down_came = share_half(grad_down, narrow_grad)
    keys_turned[...] = transposed(keys_values[:, :D])

    here = {"f": z // 2, "n": z % 2, "x": x, "y": y}
    across = {"f": along[1], "n": along[0], "x": beside, "y": beyond}

    class Chain:
        def __init__(self, index):
            matrix, start, rows, order = CHUNKS[index]
            self.index, self.order, self.stage = index, order, 0
            self.rows = pl.ds(start, rows)
            self.own = part.at[matrix]
            self.came = [ref.at[matrix] for ref in (came_one, came_two, came_three, came_four)]
            self.final = sums.at[matrix]

        def cells(self, free, flipped=None):
            return tuple(
                slice(None) if name in free else 1 - here[name] if name == flipped else here[name]
                for name in "fnxy"
            ) + (self.rows,)

        def send(self, source, target, other):
            sems = (send_sem.at[self.index, self.stage], recv_sem.at[self.index, self.stage])
            self.copy = remote(source, target, *sems, other)

        def advance(self):
            stage, order = self.stage, self.order
            if stage:
                self.copy.wait_recv()
            if 1 <= stage <= 4:
                free = order[stage:]
                for choice in itertools.product((0, 1), repeat=len(free)):
                    taken = dict(zip(sorted(free, key="fnxy".index), choice))
                    at = tuple(taken.get(name, here[name]) for name in "fnxy") + (self.rows,)
                    value = self.own[at] + self.came[stage - 1][choice + (self.rows,)]
                    if stage == 4:
                        self.final[core, y, self.rows] = value
                    else:
                        self.own[at] = value
            if stage < 4:
                name = order[stage]
                source = self.own.at[self.cells(order[stage + 1 :], name)]
                target = self.came[stage].at[(slice(None),) * (3 - stage) + (self.rows,)]
                self.send(source, target, across[name])
            elif stage == 4:
                block = self.final.at[core, y, self.rows]
                self.send(block, block, beyond)
            elif stage == 5:
                block = self.final.at[core, :, self.rows]
                self.send(block, block, partner)
            self.stage += 1

    chains = [Chain(index) for index in range(len(CHUNKS))]
    plan = iter(CHUNK_PLAN)

    def pump():
        for index in next(plan):
            chains[index].advance()

    def feed_forward(matrix, narrow, wide):
        left = transposed(narrow[...])

        def block(index, carry):
            cols = pl.ds(pl.multiple_of(index * UNIT, UNIT), UNIT)
            value = dot(left, wide[:, cols], 1, 0).astype(bf16)
            for side in range(2):
                part[matrix, index // 4, index // 2 % 2, index % 2, side] = value[
                    side * SIDE : (side + 1) * SIDE
                ]
            return carry

        lax.fori_loop(0, 8, block, 0)

    def projections(matrix, turned, narrow, width, offset, between=None):
        for tile in range(turned.shape[0] // UNIT):
            if between and tile % 2 == 0:
                between()
            value = dot(turned[tile * UNIT : (tile + 1) * UNIT, :], narrow[...], 1, 0).astype(bf16)
            for start in range(0, UNIT, PIECE):
                block, row = divmod(tile * UNIT + start, width)
                side, row = divmod(offset + row, SIDE)
                cell = (matrix, block // 4, block // 2 % 2, block % 2, side)
                part[cell + (pl.ds(row, PIECE),)] = value[start : start + PIECE]

    grad_down_came.wait_recv()
    active_came.wait_recv()
    feed_forward(0, narrow_grad, active)

    for tile in range(FF // D):
        pump()
        cols = slice(tile * D, (tile + 1) * D)
        work[...] = dot(grad_down[...], down_w[cols, :], 1, 1)

        def gelu_back(rows, carry):
            low = (work[rows, :] * slope[rows, cols]).astype(bf16)
            grad_up[rows, cols] = low
            return carry + fold(low.astype(f32))

        put_vec(BIAS_UP + cols.start, column_sum(by_rows(tok, gelu_back, zero)))
    grad_up_came = to_partner(grad_up.at[own_rows], grad_up.at[far_rows])
    pump()
    normed_came.wait_recv()
    grad_up_came.wait_recv()
    feed_forward(1, narrow_normed, grad_up)
    pump()

    work[...] = dot(grad_up[own_rows, :], up_w[...], 1, 1)

    def norm_one_back(rows, carry):
        grad = grad_two[rows, :] + work[rows, :]
        zhat = zhat_one[rows, :]
        inner = grad * span(GAIN_ONE)
        grad_in = inner - row_mean(inner) - zhat * row_mean(inner * zhat)
        grad_in = grad_in * rstd_one[rows, 0:1]
        grad_one[rows, :] = grad_in
        low = grad_in.astype(bf16)
        grad_attn[rows, :] = low
        gain, shift, bias = carry
        return gain + fold(grad * zhat), shift + fold(grad), bias + fold(low.astype(f32))

    gain, shift, bias = by_rows(tok, norm_one_back, (zero, zero, zero))
    put_vec(GAIN_ONE, column_sum(gain))
    put_vec(SHIFT_ONE, column_sum(shift))
    put_vec(BIAS_OUT, column_sum(bias))
    grad_heads[...] = dot(grad_attn[...], out_w[...], 1, 1).astype(bf16)
    heads_turned[...] = dot(out_w[...], grad_attn[...], 1, 1).astype(bf16)

    half_lanes = LANES // 2

    def attend_pair_back(pair, carry):
        cols = lanes_at(pair * LANES)
        values = keys_values[:, lanes_at(D + pair * LANES)]
        for side, mask in enumerate(masks):
            start = pl.multiple_of(pair * LANES + side * half_lanes, half_lanes)
            rows = pl.ds(start, half_lanes)
            low_chance = prob[2 * pair + side]
            chance = low_chance.astype(f32)
            grad_chance = dot(grad_heads[:, cols] * mask, values, 1, 1)
            mean = jnp.sum(chance * grad_chance, axis=-1, keepdims=True)
            grad_score = (chance * (grad_chance - mean)).astype(bf16)
            values_grad = dot(heads_turned[rows, :], low_chance, 1, 0).astype(bf16)
            keys_grad = (dot(query_turned[rows, :], grad_score, 1, 0) * scale).astype(bf16)
            query_grad = (dot(keys_turned[rows, :], grad_score, 1, 1) * scale).astype(bf16)
            blocks = (
                query_grad,
                keys_grad[:, :tok],
                values_grad[:, :tok],
                keys_grad[:, tok:],
                values_grad[:, tok:],
            )
            for index, value in enumerate(blocks):
                start = index * LANES + side * half_lanes
                exchanged[0, pair, start : start + half_lanes, :] = value
        return carry

    half_came = []
    for half in range(2):
        pump()
        pairs = pl.ds(half * HEADS // 4, HEADS // 4)
        lax.fori_loop(half * HEADS // 4, (half + 1) * HEADS // 4, attend_pair_back, 0)
        half_came.append(to_partner(exchanged.at[0, pairs], exchanged.at[1, pairs]))
    pump()
    attn_turned[:, own_lanes] = transposed(grad_attn[...])
    grad_attn_came = to_partner(attn_turned.at[:, own_lanes], attn_turned.at[:, far_lanes])

    for pair in range(HEADS // 2):
        if pair % (HEADS // 4) == 0:
            half_came[pair // (HEADS // 4)].wait_recv()
        for who, lanes in enumerate((own_lanes, far_lanes)):
            start = pair * LANES
            mine, theirs = exchanged.at[who, pair], exchanged.at[1 - who, pair]
            qkv_turned[start : start + LANES, lanes] = mine[:LANES]
            for index in (1, 2):
                rows = slice(index * LANES, (index + 1) * LANES)
                sent = slice((index + 2) * LANES, (index + 3) * LANES)
                value = mine[rows].astype(f32) + theirs[sent].astype(f32)
                start = index * D + pair * LANES
                qkv_turned[start : start + LANES, lanes] = value.astype(bf16)
    pump()
    tokens_came.wait_recv()
    projections(2, qkv_turned, narrow_tokens, 3 * D // 8, 0, pump)
    attended_came.wait_recv()
    grad_attn_came.wait_recv()
    projections(2, attn_turned, narrow_attended, D // 8, 3 * D // 8)
    pump()

    ones = jnp.ones((8, tok), bf16)
    for start, rows in ((BIAS_QUERY, slice(0, D)), (BIAS_VALUE, slice(2 * D, 3 * D))):
        put_vec(start, dot(ones, qkv_turned[rows, own_lanes], 1, 1)[0:1])
    vec_came = to_partner(vec, vec_core)
    value = dot(qkv_w[...], qkv_turned[:, own_lanes], 1, 0)
    input_grad[...] = grad_one[...] + value.T
    store(input_grad, grad_hbm)

    vec_slots = [(send_sem.at[len(CHUNKS), i], recv_sem.at[len(CHUNKS), i]) for i in range(5)]

    def vec_steps():
        vec_came.wait_recv()
        vec_core[...] = vec[...] + vec_core[...]
        copy = remote(vec_core, vec_y, *vec_slots[0], beyond)
        yield
        copy.wait_recv()
        for i in range(4):
            vec_x[0, i] = vec_core[2 * i + x] + vec_y[2 * i + x]
            vec_x[1, i] = vec_core[2 * i + 1 - x] + vec_y[2 * i + 1 - x]
        copy = remote(vec_x.at[1], vec_x.at[2], *vec_slots[1], beside)
        yield
        copy.wait_recv()
        vec_x[0] = vec_x[0] + vec_x[2]
        copies = [
            remote(
                vec_x.at[0, flip_z(z, step)],
                vec_z.at[step - 1],
                *vec_slots[1 + step],
                along[step - 1],
            )
            for step in (1, 2, 3)
        ]
        yield
        total = vec_x[0, z]
        for step, copy in enumerate(copies):
            copy.wait_recv()
            total = total + vec_z[step]
        vec_sum[...] = total
        yield

    steps = vec_steps()
    left = [sum(chunk[0] == matrix for chunk in CHUNKS) for matrix in range(3)]
    for turn, index in enumerate(next(plan)):
        chains[index].advance()
        matrix = CHUNKS[index][0]
        left[matrix] -= chains[index].stage == 7
        if not left[matrix]:
            store(sums.at[matrix], sums_hbm.at[matrix])
            left[matrix] = -1
        if turn % 10 == 9 and turn < 40:
            next(steps)
    for copy in stores:
        copy.wait()
    for copy in started:
        copy.wait_send()


def layer(row_class, lengths, tokens, cotangent, vectors, qkv_w, out_w, up_w, down_w):
    tok = tokens.shape[0]
    side = (SIDE, UNIT)

    def low(*dims):
        return pltpu.VMEM(dims, bf16)

    def wide(*dims):
        return pltpu.VMEM(dims, f32)

    return pl.pallas_call(
        layer_kernel,
        out_shape=(
            jax.ShapeDtypeStruct((tok, D), f32),
            jax.ShapeDtypeStruct((tok, D), f32),
            jax.ShapeDtypeStruct((3, 2, 2) + side, bf16),
            jax.ShapeDtypeStruct((16, LANES), f32),
        ),
        in_specs=[SMEM, SMEM, VMEM, VMEM, VMEM] + [ANY] * 4,
        out_specs=(ANY, ANY, ANY, VMEM),
        scratch_shapes=[
            wide(tok, D),
            wide(tok, D),
            low(3, 2, 2, *side),
            low(D, 3 * D),
            low(D, D),
            low(D, FF),
            low(FF, D),
            low(tok, D),
            low(D, tok),
            low(2 * tok, 2 * D),
            low(D, 2 * tok),
            low(HEADS, tok, 2 * tok),
            low(tok, D),
            low(tok, D),
            low(tok, D),
            low(tok, D),
            low(2 * tok, HALF),
            low(2 * tok, HALF),
            low(2 * tok, HALF),
            low(2 * tok, HALF),
            low(2 * tok, FF),
            low(2 * tok, FF),
            low(D, 2 * tok),
            low(3 * D, 2 * tok),
            low(2, HEADS // 2, 5 * LANES, tok),
            low(tok, D),
            low(D, tok),
            wide(tok, FF),
            wide(tok, D),
            wide(tok, D),
            wide(tok, LANES),
            wide(tok, D),
            wide(tok, D),
            wide(8, 16, LANES),
            wide(8, 16, LANES),
            wide(8, 16, LANES),
            wide(3, 4, 16, LANES),
            wide(3, 16, LANES),
            low(3, 2, 2, 2, 2, *side),
            low(3, 2, 2, 2, *side),
            low(3, 2, 2, *side),
            low(3, 2, *side),
            low(3, *side),
            pltpu.SemaphoreType.DMA((6,)),
            pltpu.SemaphoreType.DMA((5,)),
            pltpu.SemaphoreType.DMA((12,)),
            pltpu.SemaphoreType.DMA((12,)),
            pltpu.SemaphoreType.DMA((len(CHUNKS) + 1, 6)),
            pltpu.SemaphoreType.DMA((len(CHUNKS) + 1, 6)),
        ],
        compiler_params=pltpu.CompilerParams(
            vmem_limit_bytes=63 * MIB, collective_id=0, has_side_effects=True
        ),
        name="layer",
    )(row_class, lengths, tokens, cotangent, vectors[None, :], qkv_w, out_w, up_w, down_w)


GRAM_AXES = ("far", "near", "x")
GRAM_GROUPS = (
    (1, "xnf"),
    (2, "xnf"),
    (2, "xnf"),
    (3, "xnf"),
    (3, "nxf"),
    (3, "fxn"),
    (3, "nxf"),
    (2, "xnf"),
    (1, "xnf"),
    (1, "xnf"),
)
GRAM_PLAN = (
    6, 0, 9, 2, 5, 4, 7, 3, 0, 9, 6, 8, 2, 0, 9, 1, 0, 7, 9, 8, 2, 6,
    0, 5, 4, 3, 1, 8, 2, 7, 0, 6, 9, 5, 4, 8, 0, 2, 7, 1, 8, 9, 6, 3,
    5, 4, 7, 1, 8, 6, 2, 9, 3, 5, 8, 1, 4, 7, 2, 3, 5, 1, 4, 6, 7, 3,
    1, 5, 3, 4,
)


def muon_kernel(
    sums,
    qkv_hbm,
    out_hbm,
    up_hbm,
    down_hbm,
    factors_hbm,
    factors,
    own_sum,
    qkv_old,
    out_old,
    old,
    moment,
    out,
    part,
    came_one,
    came_two,
    came_three,
    high,
    low,
    load_sem,
    send_sem,
    recv_sem,
    share_send,
    share_recv,
    *ortho,
):
    z, x, y, core = position()
    here = {"far": z // 2, "near": z % 2, "x": x}
    others = {
        "far": device(flip_z(z, 2), x, y, core),
        "near": device(flip_z(z, 1), x, y, core),
        "x": device(z, 1 - x, y, core),
    }
    beyond = device(z, x, 1 - y, core)
    partner = device(z, x, y, 1 - core)
    own = 2 * y + core
    all_here = greet(list(others.values()) + [beyond, partner])

    def load_two(source, target, matrix):
        loads = [
            pltpu.make_async_copy(source, target, load_sem.at[0]),
            pltpu.make_async_copy(sums.at[matrix], own_sum, load_sem.at[1]),
        ]
        for load in loads:
            load.start()
        for load in loads:
            load.wait()

    def from_turned(source, target, skip):
        load_two(source, target, 2)
        rows = target.shape[0]
        moment[...] = jnp.zeros_like(moment)
        for half in range(2):
            cols = slice(half * HALF, (half + 1) * HALF)
            start = half * UNIT + skip
            value = own_sum[start : start + rows, :].astype(f32)
            moment[cols, skip : skip + rows] = (muon_keep * target[:, cols] + value).T

    @pl.when(own == 0)
    def _():
        from_turned(qkv_hbm, qkv_old, 0)

    @pl.when(own == 1)
    def _():
        from_turned(out_hbm, out_old, qkv_old.shape[0])

    @pl.when(own == 2)
    def _():
        load_two(up_hbm, old, 1)
        moment[...] = muon_keep * old[...] + own_sum[...].astype(f32)

    @pl.when(own == 3)
    def _():
        load_two(down_hbm, old, 0)
        moment[...] = muon_keep * old[...] + own_sum[...].astype(f32)

    all_here()
    blocks = sub_blocks(moment.shape[0])
    starts = [sum(count for count, _ in GRAM_GROUPS[:group]) for group in range(len(GRAM_GROUPS))]
    high[...] = moment[...].astype(bf16)
    low[...] = (moment[...] - high[...].astype(f32)).astype(bf16)
    started = []

    def products(first, count):
        i, j = blocks[first]
        count = min(count, sum(row == i for row, _ in blocks[first:]))
        left, right = pl.ds(i * SUB, SUB), pl.ds(j * SUB, count * SUB)
        total = dot(high[left, :], high[right, :], 1, 1)
        total = total + dot(high[left, :], low[right, :], 1, 1)
        total = total + dot(low[left, :], high[right, :], 1, 1)
        rows = SUB // 8
        for index in range(count):
            for owner in range(8):
                cell = (owner // 4, owner // 2 % 2, owner % 2, first + index)
                part[cell] = total[
                    owner * rows : (owner + 1) * rows, index * SUB : (index + 1) * SUB
                ]
        return count

    def send(source, target, group, slot, axis):
        copy = pltpu.make_async_remote_copy(
            src_ref=source,
            dst_ref=target,
            send_sem=send_sem.at[group, slot],
            recv_sem=recv_sem.at[group, slot],
            device_id=others[axis],
            device_id_type=MESH,
        )
        copy.start()
        started.append(copy)
        return copy

    def cells(fixed, flipped=None):
        return tuple(
            1 - here[name] if name == flipped else here[name] if name in fixed else slice(None)
            for name in GRAM_AXES
        )

    class Walk:
        def __init__(self, group):
            count, order = GRAM_GROUPS[group]
            self.group, self.stage = group, 0
            self.order = [GRAM_AXES["fnx".index(letter)] for letter in order]
            self.mine = (pl.ds(starts[group], count),)
            self.came = [
                ref.at[(slice(None),) * (2 - stage) + self.mine]
                for stage, ref in enumerate((came_one, came_two, came_three))
            ]

        def advance(self):
            stage, order = self.stage, self.order
            mine = self.mine
            if stage:
                self.copy.wait_recv()
            if 1 <= stage <= 3:
                kept = cells(order[:stage]) + mine
                total = part[kept] + self.came[stage - 1][...]
                if stage == 3:
                    out[kept] = total
                else:
                    part[kept] = total
            if stage < 3:
                source = part.at[cells(order[:stage], order[stage]) + mine]
                self.copy = send(source, self.came[stage], self.group, stage, order[stage])
            elif stage < 6:
                block = out.at[cells(order[: 6 - stage]) + mine]
                self.copy = send(block, block, self.group, stage, order[5 - stage])
            self.stage += 1

    walks = [Walk(group) for group in range(len(GRAM_GROUPS))]
    for group in GRAM_PLAN:
        if walks[group].stage == 0:
            first, end = starts[group], starts[group] + GRAM_GROUPS[group][0]
            while first < end:
                first += products(first, end - first)
        walks[group].advance()

    e = ortho[0]
    for index, (i, j) in enumerate(blocks):
        value = out[:, :, :, index].reshape(SUB, SUB)
        e[i * SUB : (i + 1) * SUB, j * SUB : (j + 1) * SUB] = value
        if i != j:
            e[j * SUB : (j + 1) * SUB, i * SUB : (i + 1) * SUB] = value.T

    across, beside = [], []

    def share(slot, rows, kind, other):
        block = factors.at[slot, rows]
        index = rows.start // TILE
        copy = pltpu.make_async_remote_copy(
            src_ref=block,
            dst_ref=block,
            send_sem=share_send.at[index, kind],
            recv_sem=share_recv.at[index, kind],
            device_id=other,
            device_id_type=MESH,
        )
        copy.start()
        started.append(copy)
        return copy

    def emit(rows, value):
        factors[own, rows, :] = value
        across.append((rows, share(own, rows, 0, beyond)))
        beside.append(share(own, rows, 1, partner))

    newton_schulz(e, moment, *ortho, emit)
    far = 2 * (1 - y) + core
    stores = []

    def store(slot):
        copy = pltpu.make_async_copy(
            factors.at[slot], factors_hbm.at[slot], load_sem.at[2 + len(stores)]
        )
        copy.start()
        stores.append(copy)

    store(own)
    for copy in beside:
        copy.wait_recv()
    store(2 * y + 1 - core)
    passed = []
    for rows, copy in across:
        copy.wait_recv()
        passed.append(share(far, rows, 2, partner))
    store(far)
    for copy in passed:
        copy.wait_recv()
    store(2 * (1 - y) + 1 - core)
    for copy in stores:
        copy.wait()
    for copy in started:
        copy.wait_send()


def muon_factors(sums, *olds):
    size, cols = olds[2].shape
    count = len(sub_blocks(size))
    groups = len(GRAM_GROUPS)
    rows = (SUB // 8, SUB)

    def wide(*dims):
        return pltpu.VMEM(dims, f32)

    return pl.pallas_call(
        muon_kernel,
        out_shape=jax.ShapeDtypeStruct((4, size, cols), bf16),
        in_specs=[ANY] * 5,
        out_specs=ANY,
        scratch_shapes=[
            pltpu.VMEM((4, size, cols), bf16),
            pltpu.VMEM((size, cols), bf16),
            wide(*olds[0].shape),
            wide(*olds[1].shape),
            wide(size, cols),
            wide(size, cols),
            wide(2, 2, 2, count, *rows),
            wide(2, 2, 2, count, *rows),
            wide(2, 2, count, *rows),
            wide(2, count, *rows),
            wide(count, *rows),
            pltpu.VMEM((size, cols), bf16),
            pltpu.VMEM((size, cols), bf16),
            pltpu.SemaphoreType.DMA((6,)),
            pltpu.SemaphoreType.DMA((groups, 6)),
            pltpu.SemaphoreType.DMA((groups, 6)),
            pltpu.SemaphoreType.DMA((size // TILE, 3)),
            pltpu.SemaphoreType.DMA((size // TILE, 3)),
        ]
        + ortho_scratch(size, cols),
        compiler_params=pltpu.CompilerParams(
            vmem_limit_bytes=58 * MIB, collective_id=1, has_side_effects=True
        ),
        name="muon_factors",
    )(sums, *olds)


def window(start, width, total):
    size = -(-(width + 96) // LANES) * LANES
    first = jnp.minimum(start // LANES * LANES, total - size)
    return pl.ds(pl.multiple_of(first, LANES), size), start - first


def finish_kernel(
    factors_hbm,
    sums_hbm,
    qkv_hbm,
    out_hbm,
    up_hbm,
    down_hbm,
    qkv_old_hbm,
    out_old_hbm,
    up_old_hbm,
    down_old_hbm,
    mixed_hbm,
    grad_hbm,
    vec_grad,
    vectors,
    first_old,
    second_old,
    mixed_out,
    grad_out,
    qkv_moment_out,
    out_moment_out,
    up_moment_out,
    down_moment_out,
    qkv_out,
    out_out,
    up_out,
    down_out,
    first_new,
    second_new,
    vec_new,
    factors,
    sums,
    qkv_w,
    out_w,
    up_w,
    down_w,
    qkv_moment,
    out_moment,
    up_moment,
    down_moment,
    qkv_new,
    out_new,
    up_new,
    down_new,
    turned,
    load_sem,
    store_sem,
):
    shrink = 1.0 - muon_rate * muon_decay
    dp_id = lax.axis_index("dp")
    qkv_cols, out_cols = qkv_new.shape[0], out_new.shape[0]
    qkv_lanes, qkv_skip = window(dp_id * qkv_cols, qkv_cols, 3 * D)
    out_lanes, out_skip = window(dp_id * out_cols, out_cols, D)
    block = pl.ds(pl.multiple_of(dp_id * UNIT, UNIT), UNIT)
    pairs = {
        "sums": (sums_hbm, sums),
        "up_moment": (up_old_hbm, up_moment),
        "down_moment": (down_old_hbm, down_moment),
        "factors": (factors_hbm, factors),
        "up": (up_hbm.at[:, block], up_w),
        "down": (down_hbm.at[block], down_w),
        "qkv_moment": (qkv_old_hbm, qkv_moment),
        "out_moment": (out_old_hbm, out_moment),
        "qkv": (qkv_hbm.at[:, qkv_lanes], qkv_w),
        "out": (out_hbm.at[:, out_lanes], out_w),
    }
    loads = {
        name: pltpu.make_async_copy(source, target, load_sem.at[index])
        for index, (name, (source, target)) in enumerate(pairs.items())
    }
    for load in loads.values():
        load.start()
    stores = []

    def store(source, target):
        stores.append(pltpu.make_async_copy(source, target, store_sem.at[len(stores)]))
        stores[-1].start()

    store(mixed_hbm, mixed_out)
    store(grad_hbm, grad_out)

    grad = vec_grad[:VEC_BLOCK]
    first = beta_first * first_old[...] + (1.0 - beta_first) * grad
    second = beta_second * second_old[...] + (1.0 - beta_second) * grad * grad
    first_new[...] = first
    second_new[...] = second
    first = first / (1.0 - beta_first**STEP)
    second = second / (1.0 - beta_second**STEP)
    own = jnp.zeros_like(grad)
    for index in range(8):
        rows = vectors[index * VEC_BLOCK : (index + 1) * VEC_BLOCK]
        own = jnp.where(dp_id == index, rows, own)
    vec_new[...] = own - adam_rate * first / (jnp.sqrt(second) + adam_eps)

    def step(index, rate, turned=False):
        value = factors[index]
        value = transposed(value) if turned else value
        return muon_rate * rate * value.astype(f32)

    loads["sums"].wait()
    for index, name, target, out in (
        (1, "up_moment", up_moment, up_moment_out),
        (0, "down_moment", down_moment, down_moment_out),
    ):
        loads[name].wait()
        target[...] = muon_keep * target[...] + sums[index].astype(f32)
        store(target, out)
    loads["qkv_moment"].wait()
    loads["out_moment"].wait()
    for half in range(2):
        cols = slice(half * HALF, (half + 1) * HALF)
        value = sums[2, cols].astype(f32)
        qkv_moment[:, cols] = muon_keep * qkv_moment[:, cols] + value[:qkv_cols]
        out_moment[:, cols] = muon_keep * out_moment[:, cols] + value[qkv_cols:]
    store(qkv_moment, qkv_moment_out)
    store(out_moment, out_moment_out)
    loads["factors"].wait()
    loads["up"].wait()
    up_new[...] = up_w[...].astype(f32) * shrink - step(2, math.sqrt(max(1.0, FF / D)))
    store(up_new, up_out)
    loads["down"].wait()
    down_new[...] = down_w[...].astype(f32) * shrink - step(3, 1.0, True)
    store(down_new, down_out)
    loads["qkv"].wait()
    turned[...] = transposed(qkv_w[...]).astype(f32)
    rows = pl.ds(pl.multiple_of(qkv_skip, 32), qkv_cols)
    qkv_new[...] = turned[rows, :] * shrink - step(0, math.sqrt(3.0), True)[:qkv_cols]
    store(qkv_new, qkv_out)
    loads["out"].wait()
    turned[: out_w.shape[1], :] = transposed(out_w[...]).astype(f32)
    rows = pl.ds(pl.multiple_of(out_skip, 32), out_cols)
    out_new[...] = turned[rows, :] * shrink - step(1, 1.0, True)[qkv_cols:]
    store(out_new, out_out)
    for copy in stores:
        copy.wait()


def finish(factors, sums, weights, olds, mixed, input_grad, vec, vectors, adam):
    shapes = [old.shape for old in olds]
    news = shapes[:3] + [shapes[3][::-1]]

    def wide(shape):
        return pltpu.VMEM(shape, f32)

    return pl.pallas_call(
        finish_kernel,
        out_shape=tuple(
            jax.ShapeDtypeStruct(shape, f32)
            for shape in [mixed.shape, input_grad.shape] + shapes + news + [(VEC_BLOCK, LANES)] * 3
        ),
        in_specs=[ANY] * 12 + [VMEM] * 4,
        out_specs=(ANY,) * 10 + (VMEM,) * 3,
        scratch_shapes=[
            pltpu.VMEM(factors.shape, bf16),
            pltpu.VMEM(sums.shape, bf16),
            pltpu.VMEM((D, 384), bf16),
            pltpu.VMEM((D, 256), bf16),
            pltpu.VMEM((D, UNIT), bf16),
            pltpu.VMEM((UNIT, D), bf16),
        ]
        + [wide(shape) for shape in shapes + news]
        + [
            wide((384, D)),
            pltpu.SemaphoreType.DMA((10,)),
            pltpu.SemaphoreType.DMA((10,)),
        ],
        compiler_params=pltpu.CompilerParams(vmem_limit_bytes=48 * MIB),
        name="finish",
    )(factors, sums, *weights, *olds, mixed, input_grad, vec, vectors, *adam)


def swap(value, axis, bit):
    size = lax.axis_size(axis)
    return lax.ppermute(value, axis, [(i, i ^ bit) for i in range(size)])


def scatter_head(value, bit, position):
    half = value.shape[1] // 2
    mine = lax.dynamic_slice_in_dim(value, position * half, half, 1)
    other = lax.dynamic_slice_in_dim(value, (1 - position) * half, half, 1)
    return (mine.astype(f32) + swap(other, "head", bit).astype(f32)).astype(bf16)


def scatter_dp_pair(value, position):
    paired = value.reshape((value.shape[0] // 2, 2) + value.shape[1:])
    mine = lax.dynamic_index_in_dim(paired, position, 1, False)
    other = lax.dynamic_index_in_dim(paired, 1 - position, 1, False)
    return (mine.astype(f32) + swap(other, "dp", 1).astype(f32)).astype(bf16)


def scatter_dp_rest(value, place):
    ranks = value.shape[0]
    total = lax.dynamic_index_in_dim(value, place, 0, False).astype(f32)
    for step in range(1, ranks):
        sent = lax.dynamic_index_in_dim(value, place ^ step, 0, False)
        total = total + swap(sent, "dp", 2 * step).astype(f32)
    return total


def local(
    tokens,
    cotangent,
    qkv_weight,
    out_weight,
    up_weight,
    down_weight,
    vectors,
    qkv_moment,
    out_moment,
    up_moment,
    down_moment,
    adam_first,
    adam_second,
    bucket_class,
    row_lengths,
):
    n_dp = lax.axis_size("dp")
    n_head = lax.axis_size("head")
    dp_id = lax.axis_index("dp")
    head_id = lax.axis_index("head")
    core, side = head_id % 2, head_id // 2
    tok, width = tokens.shape
    hidden = up_weight.shape[1]
    half = width // 2
    qkv_cols, out_cols = qkv_moment.shape[1], out_moment.shape[1]
    shrink = 1.0 - muon_rate * muon_decay

    def weight_block(weight, cols, dim):
        return lax.dynamic_slice_in_dim(weight, dp_id * cols, cols, dim)

    block = head_id.astype(jnp.int32)[None]
    vec_len = vectors.shape[0] // n_dp
    if (n_dp, n_head, tok) == (8, 4, 256):
        mixed, input_grad, sums, vec = layer(
            bucket_class,
            row_lengths,
            tokens,
            cotangent,
            vectors,
            qkv_weight,
            out_weight,
            up_weight,
            down_weight,
        )
        sums = sums.reshape(3, width, -1)
        olds = [qkv_moment.T, out_moment.T, up_moment, down_moment]
        mixed, input_grad, *results = finish(
            muon_factors(sums, *olds),
            sums,
            [qkv_weight, out_weight, up_weight, down_weight],
            olds,
            mixed,
            input_grad,
            vec,
            vectors.reshape(-1, LANES),
            [adam_first.reshape(-1, LANES), adam_second.reshape(-1, LANES)],
        )
        moments, new_weights = results[:4], results[4:8]
        vec_first, vec_second, vec_new = (value.reshape(vec_len) for value in results[8:])
        moments = [moments[0].T, moments[1].T, *moments[2:]]
        new_weights = [new_weights[0].T, new_weights[1].T, *new_weights[2:]]
    else:
        pieces = split_vectors(vectors, width, hidden)
        bias_query, bias_value, bias_out, gain_one, shift_one = pieces[:5]
        bias_up, bias_down, gain_two, shift_two = pieces[5:]
        bias_qkv = jnp.concatenate([bias_query, jnp.zeros_like(bias_query), bias_value])

        def column_half(value, which):
            return lax.dynamic_slice_in_dim(value, which * half, half, 1)

        qkv = (dot(tokens, qkv_weight, 1, 0) + bias_qkv).astype(bf16)
        other = swap(qkv[:, width:], "head", 1)
        attended = attend(block, bucket_class, row_lengths, qkv, other)
        attn_val = dot(attended, out_weight, 1, 0) + bias_out
        resid_one = tokens.astype(f32) + attn_val
        centre = resid_one - jnp.mean(resid_one, axis=-1, keepdims=True)
        rstd_one = lax.rsqrt(jnp.mean(centre * centre, axis=-1, keepdims=True) + norm_eps)
        zhat_one = centre * rstd_one
        normed_one = zhat_one * gain_one + shift_one
        normed_low = normed_one.astype(bf16)
        up_val = dot(normed_low, up_weight, 1, 0) + bias_up
        phi_cum = 0.5 * (1.0 + lax.erf(up_val * (0.5**0.5)))
        active_low = (up_val * phi_cum).astype(bf16)
        slope = phi_cum + up_val * jnp.exp(-0.5 * up_val * up_val) * (1.0 / math.sqrt(2.0 * math.pi))
        down_val = dot(active_low, down_weight, 1, 0) + bias_down
        resid_two = normed_one + down_val
        centre = resid_two - jnp.mean(resid_two, axis=-1, keepdims=True)
        rstd_two = lax.rsqrt(jnp.mean(centre * centre, axis=-1, keepdims=True) + norm_eps)
        zhat_two = centre * rstd_two
        mixed = zhat_two * gain_two + shift_two

        def norm_back(grad, gain, zhat, rstd):
            inner = grad * gain
            mean = jnp.mean(inner, axis=-1, keepdims=True)
            slant = jnp.mean(inner * zhat, axis=-1, keepdims=True)
            return (inner - mean - zhat * slant) * rstd, jnp.sum(grad * zhat, axis=0), jnp.sum(grad, axis=0)

        grad_two, grad_gain_two, grad_shift_two = norm_back(
            cotangent.astype(f32), gain_two, zhat_two, rstd_two
        )
        grad_down_low = grad_two.astype(bf16)
        grad_bias_down = jnp.sum(grad_down_low, axis=0, dtype=f32)

        x_id, z_id = dp_id % 2, dp_id // 2

        grad_up_low = (dot(grad_down_low, down_weight, 1, 1) * slope).astype(bf16)
        grad_bias_up = jnp.sum(grad_up_low, axis=0, dtype=f32)
        grad_normed = grad_two + dot(grad_up_low, up_weight, 1, 1)
        grad_one, grad_gain_one, grad_shift_one = norm_back(grad_normed, gain_one, zhat_one, rstd_one)
        grad_attn_low = grad_one.astype(bf16)
        grad_bias_out = jnp.sum(grad_attn_low, axis=0, dtype=f32)
        grad_heads = dot(grad_attn_low, out_weight, 1, 1).astype(bf16)
        grad_query, own, sent = attend_back(block, bucket_class, row_lengths, qkv, other, grad_heads)
        grad_kv = (own + swap(sent, "head", 1).astype(f32)).astype(bf16)
        grad_qkv = jnp.concatenate([grad_query, grad_kv], axis=1)
        grad_bias_qkv = jnp.sum(grad_qkv, axis=0, dtype=f32)
        input_grad = grad_one + dot(grad_qkv, qkv_weight, 1, 1)
        grad_vector = jnp.concatenate(
            [
                grad_bias_qkv[:width],
                grad_bias_qkv[2 * width :],
                grad_bias_out,
                grad_gain_one,
                grad_shift_one,
                grad_bias_up,
                grad_bias_down,
                grad_gain_two,
                grad_shift_two,
            ]
        )
        grad_vector = grad_vector + swap(grad_vector, "head", 1)
        wides = [active_low, grad_up_low, grad_attn_low, grad_qkv]
        narrows = [grad_down_low, normed_low, attended, tokens]

        def both_halves(value):
            return jnp.concatenate(
                [column_half(value, core), swap(column_half(value, 1 - core), "head", 1)], axis=0
            )

        def weight_grad(wide, narrow):
            wide = jnp.concatenate([wide, swap(wide, "head", 1)], axis=0)
            value = dot(wide, both_halves(narrow), 0, 0).astype(bf16)
            return value.reshape(n_dp, value.shape[0] // n_dp, half)

        def reduce_y_first(value):
            return scatter_dp_rest(scatter_dp_pair(scatter_head(value, 2, side), x_id), z_id)

        def reduce_x_first(value):
            return scatter_dp_rest(scatter_head(scatter_dp_pair(value, x_id), 2, side), z_id)

        def spread(value):
            value = value.astype(bf16)
            came = swap(value, "head", 2)
            value = jnp.concatenate(
                [jnp.where(side == 0, value, came), jnp.where(side == 0, came, value)], axis=0
            )
            came = swap(value, "head", 1)
            return jnp.concatenate(
                [jnp.where(core == 0, value, came), jnp.where(core == 0, came, value)], axis=1
            ).astype(f32)

        down_part, up_part, out_part, qkv_part = [
            weight_grad(wide, narrow) for wide, narrow in zip(wides, narrows)
        ]
        vec_rows = 16
        vec_part = grad_vector.reshape(n_dp, vec_len)
        vec_part = jnp.pad(vec_part, ((0, 0), (0, vec_rows * width - vec_len)))
        vec_part = vec_part.reshape(n_dp, vec_rows, width)
        vec_part = lax.dynamic_slice_in_dim(vec_part, core * half, half, 2).astype(bf16)
        down_new = spread(reduce_x_first(down_part))
        up_new = spread(reduce_y_first(up_part))
        tail_new = spread(
            reduce_y_first(jnp.concatenate([qkv_part, out_part, vec_part], axis=1))
        )
        grads = [
            tail_new[:qkv_cols].T,
            tail_new[qkv_cols : qkv_cols + out_cols].T,
            up_new.T,
            down_new.T,
        ]
        grad_vec = tail_new[qkv_cols + out_cols :].reshape(-1)[:vec_len]
        moments = [
            muon_keep * old + grad
            for old, grad in zip([qkv_moment, out_moment, up_moment, down_moment], grads)
        ]
        most = max(m.shape[1] for m in moments)
        padded = [jnp.pad(m, ((0, 0), (0, most - m.shape[1]))) for m in moments]
        chosen = padded[-1]
        for index in range(len(padded) - 2, -1, -1):
            chosen = jnp.where(head_id == index, padded[index], chosen)
        gram_mat = lax.dot_general(
            chosen, chosen, (((1,), (1,)), ((), ())), precision=lax.Precision.HIGH
        )
        own_factor = orthogonalize(lax.psum(gram_mat, "dp"), chosen)
        across = swap(own_factor, "head", 2)
        low_pair = jnp.where(side == 0, own_factor, across)
        high_pair = jnp.where(side == 0, across, own_factor)
        near_low = swap(low_pair, "head", 1)
        near_high = swap(high_pair, "head", 1)
        factors = [
            jnp.where(core == 0, low_pair, near_low),
            jnp.where(core == 0, near_low, low_pair),
            jnp.where(core == 0, high_pair, near_high),
            jnp.where(core == 0, near_high, high_pair),
        ]
        factors = [o[:, : m.shape[1]].astype(f32) for o, m in zip(factors, moments)]
        factors[3] = factors[3].T
        old_weights = [
            weight_block(qkv_weight, qkv_cols, 1),
            weight_block(out_weight, out_cols, 1),
            weight_block(up_weight, up_moment.shape[1], 1),
            weight_block(down_weight, down_moment.shape[1], 0),
        ]

        rates = (math.sqrt(3.0), 1.0, math.sqrt(max(1.0, hidden / width)), 1.0)
        new_weights = [
            old.astype(f32) * shrink - muon_rate * rate * factor
            for old, rate, factor in zip(old_weights, rates, factors)
        ]

        vec_old = lax.dynamic_slice_in_dim(vectors, dp_id * vec_len, vec_len, 0)
        vec_first = beta_first * adam_first + (1.0 - beta_first) * grad_vec
        vec_second = beta_second * adam_second + (1.0 - beta_second) * grad_vec * grad_vec
        first_hat = vec_first / (1.0 - beta_first**STEP)
        second_hat = vec_second / (1.0 - beta_second**STEP)
        vec_new = vec_old - adam_rate * first_hat / (jnp.sqrt(second_hat) + adam_eps)
    return (mixed, input_grad, *moments, *new_weights, vec_first, vec_second, vec_new)


def solution(mesh):
    tokens_spec = P(("dp", "head"), None)
    block_spec = P(None, "dp")
    return jax.shard_map(
        local,
        mesh=mesh,
        in_specs=(
            tokens_spec,
            tokens_spec,
            P(),
            P(),
            P(),
            P(),
            P(),
            block_spec,
            block_spec,
            block_spec,
            block_spec,
            P("dp"),
            P("dp"),
            P("dp"),
            P("dp", None),
        ),
        out_specs=(
            tokens_spec,
            tokens_spec,
            block_spec,
            block_spec,
            block_spec,
            block_spec,
            block_spec,
            block_spec,
            block_spec,
            P("dp", None),
            P("dp"),
            P("dp"),
            P("dp"),
        ),
        check_vma=False,
    )
```

```python
import functools
import itertools
import math

import jax
import jax.numpy as jnp
from jax import lax
from jax.experimental import pallas as pl
from jax.experimental.pallas import tpu as pltpu
from jax.sharding import PartitionSpec as P

D = 768
HEADS = 12
HEAD_DIM = 64
FF = 3072
BASE_LEN = 128
NS_STEPS = 5
STEP = 5
MAX_LEN = 512

f32 = jnp.float32
bf16 = jnp.bfloat16

norm_eps = 1e-12
masked_score = -1000000000.0
quintic_a = 3.4445
quintic_b = -4.775
quintic_c = 2.0315
muon_rate = 1.0
muon_decay = 0.01
muon_keep = 0.5
adam_rate = 0.2
beta_first = 0.9
beta_second = 0.999
adam_eps = 1e-08
MIB = 1024 * 1024


def dot(left, right, left_dim, right_dim):
    return lax.dot_general(
        left, right, (((left_dim,), (right_dim,)), ((), ())), preferred_element_type=f32
    )


def split_vectors(vectors, width, hidden):
    lengths_list = [width] * 5 + [hidden] + [width] * 3
    pieces = []
    offset = 0
    for length in lengths_list:
        pieces.append(vectors[offset : offset + length])
        offset = offset + length
    return pieces


def allowed_mask(class_ref, length_ref, block, tok):
    shift = class_ref[0] + int(math.log2(BASE_LEN))
    query_place = block * tok + lax.broadcasted_iota(jnp.int32, (tok, 1), 0)
    lane = lax.broadcasted_iota(jnp.int32, (1, 2 * tok), 1)
    own = lane < tok
    key_place = jnp.where(own, block * tok + lane, (block ^ 1) * tok + lane - tok)
    key_row = lax.shift_right_logical(key_place, jnp.broadcast_to(shift, key_place.shape))
    offset = key_place - lax.shift_left(key_row, jnp.broadcast_to(shift, key_place.shape))
    row_len = jnp.zeros_like(key_row)
    for slot in range(length_ref.shape[1]):
        row_len = jnp.where(key_row == slot, length_ref[0, slot], row_len)
    key_row = jnp.where(offset < row_len, key_row, -1)
    query_row = lax.shift_right_logical(query_place, jnp.broadcast_to(shift, query_place.shape))
    return query_row == key_row


def half_masks():
    lane = lax.broadcasted_iota(jnp.int32, (1, 2 * HEAD_DIM), 1)
    first = (lane < HEAD_DIM).astype(f32)
    return (first.astype(bf16), (1.0 - first).astype(bf16)), lane < HEAD_DIM


def head_prob(query, keys, allowed):
    score = jnp.where(allowed, dot(query, keys, 1, 1) * HEAD_DIM ** (-0.5), masked_score)
    exponent = jnp.exp(score - jnp.max(score, axis=-1, keepdims=True))
    return exponent / jnp.sum(exponent, axis=-1, keepdims=True)


def attend_kernel(block_ref, class_ref, length_ref, qkv_ref, other_ref, out_ref):
    tok = qkv_ref.shape[0]
    allowed = allowed_mask(class_ref, length_ref, block_ref[0], tok)
    masks, first = half_masks()
    for pair in range(HEADS // 2):
        cols = pl.ds(pair * 2 * HEAD_DIM, 2 * HEAD_DIM)
        kcols = pl.ds(D + pair * 2 * HEAD_DIM, 2 * HEAD_DIM)
        vcols = pl.ds(2 * D + pair * 2 * HEAD_DIM, 2 * HEAD_DIM)
        query = qkv_ref[:, cols]
        keys = jnp.concatenate([qkv_ref[:, kcols], other_ref[:, cols]], axis=0)
        values = jnp.concatenate([qkv_ref[:, vcols], other_ref[:, kcols]], axis=0)
        outs = []
        for mask in masks:
            prob = head_prob(query * mask, keys, allowed)
            outs.append(dot(prob.astype(bf16), values, 1, 0))
        out_ref[:, cols] = jnp.where(first, outs[0], outs[1]).astype(bf16)


def attend_back_kernel(
    block_ref, class_ref, length_ref, qkv_ref, other_ref, grad_ref, dq_ref, own_ref, send_ref
):
    tok = qkv_ref.shape[0]
    allowed = allowed_mask(class_ref, length_ref, block_ref[0], tok)
    masks, first = half_masks()
    scale = HEAD_DIM ** (-0.5)
    for pair in range(HEADS // 2):
        cols = pl.ds(pair * 2 * HEAD_DIM, 2 * HEAD_DIM)
        kcols = pl.ds(D + pair * 2 * HEAD_DIM, 2 * HEAD_DIM)
        vcols = pl.ds(2 * D + pair * 2 * HEAD_DIM, 2 * HEAD_DIM)
        query = qkv_ref[:, cols]
        keys = jnp.concatenate([qkv_ref[:, kcols], other_ref[:, cols]], axis=0)
        values = jnp.concatenate([qkv_ref[:, vcols], other_ref[:, kcols]], axis=0)
        grad = grad_ref[:, cols]
        dqs, dk, dv = [], None, None
        for mask in masks:
            head_query = query * mask
            head_grad = grad * mask
            prob = head_prob(head_query, keys, allowed)
            part_v = dot(prob.astype(bf16), head_grad, 0, 0)
            dprob = dot(head_grad, values, 1, 1)
            dscore = prob * (dprob - jnp.sum(prob * dprob, axis=-1, keepdims=True))
            dscore = dscore.astype(bf16)
            dqs.append(dot(dscore, keys, 1, 0))
            part_k = dot(dscore, head_query, 0, 0)
            dk = part_k if dk is None else dk + part_k
            dv = part_v if dv is None else dv + part_v
        dk = dk * scale
        dq_ref[:, cols] = (jnp.where(first, dqs[0], dqs[1]) * scale).astype(bf16)
        own_ref[:, cols] = dk[:tok]
        own_ref[:, kcols] = dv[:tok]
        send_ref[:, cols] = dk[tok:].astype(bf16)
        send_ref[:, kcols] = dv[tok:].astype(bf16)


SMEM = pl.BlockSpec(memory_space=pltpu.SMEM)
VMEM = pl.BlockSpec(memory_space=pltpu.VMEM)
ANY = pl.BlockSpec(memory_space=pl.ANY)


def attend(block, row_class, lengths, qkv, other):
    tok = qkv.shape[0]
    return pl.pallas_call(
        attend_kernel,
        out_shape=jax.ShapeDtypeStruct((tok, D), bf16),
        in_specs=[SMEM, SMEM, SMEM, VMEM, VMEM],
        out_specs=VMEM,
        compiler_params=pltpu.CompilerParams(vmem_limit_bytes=32 * MIB),
        name="attend",
    )(block, row_class, lengths, qkv, other)


def attend_back(block, row_class, lengths, qkv, other, grad):
    tok = qkv.shape[0]
    return pl.pallas_call(
        attend_back_kernel,
        out_shape=(
            jax.ShapeDtypeStruct((tok, D), bf16),
            jax.ShapeDtypeStruct((tok, 2 * D), f32),
            jax.ShapeDtypeStruct((tok, 2 * D), bf16),
        ),
        in_specs=[SMEM, SMEM, SMEM, VMEM, VMEM, VMEM],
        out_specs=(VMEM, VMEM, VMEM),
        compiler_params=pltpu.CompilerParams(vmem_limit_bytes=32 * MIB),
        name="attend_back",
    )(block, row_class, lengths, qkv, other, grad)


CENTRES = (0.0, 0.0, 0.0, 0.8, 0.8)
TILE = 384
SUB = 128


def sub_blocks(size):
    count = size // SUB
    return [(i, j) for i in range(count) for j in range(i, count)]


def newton_schulz(gram, moment, e, f, g, eb, fb, gb, yy, y, emit):
    size = e.shape[0]
    tiles = [slice(i * TILE, (i + 1) * TILE) for i in range(size // TILE)]

    def unit(rows):
        row_id = rows.start + lax.broadcasted_iota(jnp.int32, (TILE, size), 0)
        col_id = lax.broadcasted_iota(jnp.int32, (TILE, size), 1)
        return (row_id == col_id).astype(f32)

    diagonal = jnp.zeros((TILE, size), f32)
    for rows in tiles:
        diagonal = diagonal + gram[rows, :] * unit(rows)
    trace = jnp.sum(jnp.sum(diagonal, axis=0, keepdims=True), axis=1, keepdims=True)
    factor = 1.0 / (jnp.sqrt(trace) + 1e-07)
    square_factor = factor * factor
    for rows in tiles:
        value = gram[rows, :] * square_factor
        e[rows, :] = value
        eb[rows, :] = value.astype(bf16)
        value = moment[rows, :] * factor
        y[rows, :] = value
        yy[0, rows, :] = value.astype(bf16)

    def one_step(centre, after, now, then, last=False):
        keep = quintic_a + quintic_b * centre + quintic_c * centre * centre
        linear = quintic_b + 2.0 * quintic_c * centre
        for rows in tiles:
            value = linear * e[rows, :] + quintic_c * dot(eb[rows, :], eb[...], 1, 0)
            fb[rows, :] = value.astype(bf16)
            if centre:
                f[rows, :] = value
        for rows in tiles:
            value = keep * y[rows, :] + dot(fb[rows, :], now[...], 1, 0)
            if last:
                emit(rows, value.astype(bf16))
            else:
                y[rows, :] = value
                then[rows, :] = value.astype(bf16)
        if last:
            return
        for rows in tiles:
            value = keep * e[rows, :] + dot(eb[rows, :], fb[...], 1, 0)
            if centre:
                value = value + centre * f[rows, :]
            g[rows, :] = value
            gb[rows, :] = value.astype(bf16)
        for rows in tiles:
            value = keep * g[rows, :] + dot(gb[rows, :], fb[...], 1, 0)
            if centre:
                value = value + (centre * keep) * f[rows, :]
            shift = centre * keep * keep - after
            if not isinstance(shift, float) or shift:
                value = value + shift * unit(rows)
            e[rows, :] = value
            eb[rows, :] = value.astype(bf16)

    plain = sum(centre == 0.0 for centre in CENTRES)

    def plain_step(step, carry):
        after = jnp.where(step == plain - 1, CENTRES[plain], 0.0)
        one_step(0.0, after, yy.at[step % 2], yy.at[(step + 1) % 2])
        return carry

    lax.fori_loop(0, plain, plain_step, 0)
    for step in range(plain, NS_STEPS):
        last = step + 1 == NS_STEPS
        after = 0.0 if last else CENTRES[step + 1]
        one_step(CENTRES[step], after, yy.at[step % 2], yy.at[(step + 1) % 2], last)


def ortho_kernel(gram, moment, out, *scratch):
    def emit(rows, value):
        out[rows, :] = value

    newton_schulz(gram, moment, *scratch, emit)


def ortho_scratch(size, cols):
    square, square_low = pltpu.VMEM((size, size), f32), pltpu.VMEM((size, size), bf16)
    wide_low = pltpu.VMEM((2, size, cols), bf16)
    return [square] * 3 + [square_low] * 3 + [wide_low, pltpu.VMEM((size, cols), f32)]


def orthogonalize(gram_mat, moment):
    size, cols = moment.shape
    return pl.pallas_call(
        ortho_kernel,
        out_shape=jax.ShapeDtypeStruct((size, cols), bf16),
        in_specs=[VMEM, VMEM],
        out_specs=VMEM,
        scratch_shapes=ortho_scratch(size, cols),
        compiler_params=pltpu.CompilerParams(vmem_limit_bytes=48 * MIB),
        name="ortho",
    )(gram_mat, moment)


MESH = pl.DeviceIdType.MESH
PIECE = 48
SIDE = 192
UNIT = 2 * SIDE
HALF = D // 2
LANES = 128
VEC_BLOCK = 9
ROWS = 16
CHUNKS = (
    (0, 0, 64, "nfyx"),
    (0, 64, 64, "xynf"),
    (0, 128, 64, "yxnf"),
    (1, 0, 64, "ynxf"),
    (1, 64, 64, "nxyf"),
    (1, 128, 64, "xynf"),
    (2, 0, 48, "xynf"),
    (2, 48, 48, "nxyf"),
    (2, 96, 48, "yxnf"),
    (2, 144, 32, "xynf"),
    (2, 176, 16, "xfyn"),
)
CHUNK_PLAN = (
    (0, 1, 2),
    (),
    (),
    (),
    (),
    (3, 5, 4),
    (0, 1, 2),
    (),
    (),
    (),
    (0, 1, 2, 4, 5, 3),
    (),
    (),
    (0, 7, 8, 10, 9, 6),
    (
        1, 4, 2, 5, 0, 1, 10, 4, 0, 2, 0, 1, 9, 1, 3, 2, 5, 10, 4, 8, 2, 6,
        10, 5, 9, 3, 4, 10, 7, 4, 8, 10, 5, 9, 3, 10, 5, 6, 9, 8, 7, 3, 9, 6,
        3, 9, 8, 7, 8, 6, 8, 7, 6, 7, 6, 7,
    ),
)
BIAS_QUERY, BIAS_VALUE, BIAS_OUT, GAIN_ONE, SHIFT_ONE, BIAS_UP = (i * D for i in range(6))
BIAS_DOWN, GAIN_TWO, SHIFT_TWO = (BIAS_UP + FF + i * D for i in range(3))


def position():
    dp_id, head_id = lax.axis_index("dp"), lax.axis_index("head")
    z, x = dp_id // 2, dp_id % 2
    y, core = head_id // 2, head_id % 2
    return z, x, y, core


def device(z, x, y, core):
    return (2 * z + x, 2 * y + core)


def flip_z(z, step):
    high, low = z // 2, z % 2
    high = 1 - high if step // 2 else high
    low = 1 - low if step % 2 else low
    return 2 * high + low


def greet(others):
    barrier = pltpu.get_barrier_semaphore()
    for other in others:
        pl.semaphore_signal(barrier, inc=1, device_id=other, device_id_type=MESH)
    return lambda: pl.semaphore_wait(barrier, len(others))


def by_rows(count, body, init=None, together=4):
    def step(index, carry):
        for part in range(together):
            start = (index * together + part) * ROWS
            carry = body(pl.ds(pl.multiple_of(start, ROWS), ROWS), carry)
        return carry

    return lax.fori_loop(0, count // (ROWS * together), step, init)


def row_mean(value):
    return jnp.sum(value, axis=-1, keepdims=True) * (1.0 / D)


def fold(value):
    return jnp.sum(value.reshape(value.shape[0] // 8, 8, value.shape[1]), axis=0)


def column_sum(value):
    return jnp.sum(value, axis=0, keepdims=True)


def transposed(value):
    side = 2 * LANES
    row_id = lax.broadcasted_iota(jnp.int32, (side, side), 0)
    unit = (row_id == lax.broadcasted_iota(jnp.int32, (side, side), 1)).astype(f32).astype(bf16)
    blocks = []
    for start in range(0, value.shape[1], side):
        block = value[:, start : start + side]
        size = block.shape[1]
        blocks.append(dot(unit[:size, :size], block, 1, 1).astype(bf16))
    return jnp.concatenate(blocks, axis=0)


def layer_kernel(
    row_class,
    lengths,
    tokens,
    cotangent,
    vectors,
    qkv_hbm,
    out_hbm,
    up_hbm,
    down_hbm,
    mixed_hbm,
    grad_hbm,
    sums_hbm,
    vec_sum,
    mixed,
    input_grad,
    sums,
    qkv_w,
    out_w,
    up_w,
    down_w,
    query,
    query_turned,
    keys_values,
    keys_turned,
    prob,
    attended,
    normed_low,
    grad_down,
    grad_attn,
    narrow_tokens,
    narrow_attended,
    narrow_normed,
    narrow_grad,
    active,
    grad_up,
    attn_turned,
    qkv_turned,
    exchanged,
    grad_heads,
    heads_turned,
    slope,
    normed_one,
    zhat_one,
    rstd_one,
    grad_two,
    work,
    vec,
    vec_core,
    vec_y,
    vec_x,
    vec_z,
    part,
    came_one,
    came_two,
    came_three,
    came_four,
    load_sem,
    store_sem,
    pair_send,
    pair_recv,
    send_sem,
    recv_sem,
):
    grad_one = normed_one
    z, x, y, core = position()
    tok = tokens.shape[0]
    thirds = [slice(index * D, (index + 1) * D) for index in range(3)]
    loads = {
        name: pltpu.make_async_copy(source, target, load_sem.at[index])
        for index, (name, source, target) in enumerate(
            (
                ("key", qkv_hbm.at[:, thirds[1]], qkv_w.at[:, thirds[1]]),
                ("value", qkv_hbm.at[:, thirds[2]], qkv_w.at[:, thirds[2]]),
                ("query", qkv_hbm.at[:, thirds[0]], qkv_w.at[:, thirds[0]]),
                ("out", out_hbm, out_w),
                ("up", up_hbm, up_w),
                ("down", down_hbm, down_w),
            )
        )
    }
    for name in ("key", "value", "query"):
        loads[name].start()
    stores = []

    def store(source, target):
        stores.append(pltpu.make_async_copy(source, target, store_sem.at[len(stores)]))
        stores[-1].start()

    beyond = device(z, x, 1 - y, core)
    beside = device(z, 1 - x, y, core)
    partner = device(z, x, y, 1 - core)
    along = [device(flip_z(z, step), x, y, core) for step in (1, 2, 3)]
    all_here = greet([beyond, beside, partner] + along)
    started = []

    def remote(source, target, send_at, recv_at, other):
        copy = pltpu.make_async_remote_copy(
            src_ref=source,
            dst_ref=target,
            send_sem=send_at,
            recv_sem=recv_at,
            device_id=other,
            device_id_type=MESH,
        )
        copy.start()
        started.append(copy)
        return copy

    pair_count = []

    def to_partner(source, target):
        slot = len(pair_count)
        pair_count.append(slot)
        return remote(source, target, pair_send.at[slot], pair_recv.at[slot], partner)

    own_half = pl.ds(pl.multiple_of(core * HALF, HALF), HALF)
    other_half = pl.ds(pl.multiple_of((1 - core) * HALF, HALF), HALF)

    def span(start, length=D):
        return vectors[0:1, start : start + length]

    def put_vec(start, value):
        for index in range(value.shape[1] // LANES):
            block, row = divmod(start // LANES + index, VEC_BLOCK)
            vec[block, row : row + 1, :] = value[:, index * LANES : (index + 1) * LANES]

    vec[...] = jnp.zeros_like(vec)

    own_rows = pl.ds(0, tok)
    far_rows = pl.ds(tok, tok)
    own_lanes, far_lanes = own_rows, far_rows

    def share_half(value, narrow):
        narrow[own_rows, :] = value[:, own_half]
        return to_partner(value.at[:, other_half], narrow.at[far_rows])

    kv_came = []
    for name, index, start in (("key", 1, None), ("value", 2, BIAS_VALUE)):
        loads[name].wait()
        value = dot(tokens[...], qkv_w[:, thirds[index]], 1, 0)
        if start is not None:
            value = value + span(start)
        cols = slice((index - 1) * D, index * D)
        keys_values[own_rows, cols] = value.astype(bf16)
        if index == 1:
            all_here()
            for name in ("out", "up", "down"):
                loads[name].start()
        kv_came.append(
            to_partner(keys_values.at[own_rows, cols], keys_values.at[far_rows, cols])
        )
    loads["query"].wait()
    value = dot(tokens[...], qkv_w[:, thirds[0]], 1, 0) + span(BIAS_QUERY)
    query[...] = value.astype(bf16)
    query_turned[...] = transposed(query[...])
    allowed = allowed_mask(row_class, lengths, 2 * y + core, tok)
    penalty = jnp.where(allowed, 0.0, masked_score)
    masks, first = half_masks()
    tokens_came = share_half(tokens, narrow_tokens)
    for copy in kv_came:
        copy.wait_recv()

    scale = HEAD_DIM ** (-0.5)

    def lanes_at(start):
        return pl.ds(pl.multiple_of(start, LANES), LANES)

    def attend_pair(pair, carry):
        cols = lanes_at(pair * LANES)
        keys = keys_values[:, cols]
        values = keys_values[:, lanes_at(D + pair * LANES)]
        outs = []
        for side, mask in enumerate(masks):
            score = dot(query[:, cols] * (mask * scale), keys, 1, 1) + penalty
            exponent = jnp.exp(score - jnp.max(score, axis=-1, keepdims=True))
            chance = exponent * (1.0 / jnp.sum(exponent, axis=-1, keepdims=True))
            chance = chance.astype(bf16)
            prob[2 * pair + side] = chance
            outs.append(dot(chance, values, 1, 0))
        attended[:, cols] = jnp.where(first, outs[0], outs[1]).astype(bf16)
        return carry

    lax.fori_loop(0, HEADS // 2, attend_pair, 0)
    attended_came = share_half(attended, narrow_attended)

    loads["out"].wait()
    work[...] = dot(attended[...], out_w[...], 1, 0)

    def norm_one(rows, carry):
        value = tokens[rows, :].astype(f32) + (work[rows, :] + span(BIAS_OUT))
        centre = value - row_mean(value)
        rstd = lax.rsqrt(row_mean(centre * centre) + norm_eps)
        zhat = centre * rstd
        normed = zhat * span(GAIN_ONE) + span(SHIFT_ONE)
        zhat_one[rows, :] = zhat
        rstd_one[rows, :] = jnp.broadcast_to(rstd, (ROWS, LANES))
        normed_one[rows, :] = normed
        normed_low[rows, :] = normed.astype(bf16)
        return carry

    by_rows(tok, norm_one)
    normed_came = share_half(normed_low, narrow_normed)

    loads["up"].wait()
    for tile in range(FF // D):
        cols = slice(tile * D, (tile + 1) * D)
        work[...] = dot(normed_low[...], up_w[:, cols], 1, 0)

        def gelu(rows, carry):
            value = work[rows, :] + span(BIAS_UP + cols.start)
            chance = 0.5 * (1.0 + lax.erf(value * (0.5**0.5)))
            density = jnp.exp(-0.5 * value * value) * (1.0 / math.sqrt(2.0 * math.pi))
            active[rows, cols] = (value * chance).astype(bf16)
            slope[rows, cols] = chance + value * density
            return carry

        by_rows(tok, gelu)
    active_came = to_partner(active.at[own_rows], active.at[far_rows])
    loads["down"].wait()
    work[...] = dot(active[own_rows, :], down_w[...], 1, 0)

    def norm_two(rows, carry):
        value = normed_one[rows, :] + (work[rows, :] + span(BIAS_DOWN))
        centre = value - row_mean(value)
        rstd = lax.rsqrt(row_mean(centre * centre) + norm_eps)
        zhat = centre * rstd
        mixed[rows, :] = zhat * span(GAIN_TWO) + span(SHIFT_TWO)
        grad = cotangent[rows, :].astype(f32)
        inner = grad * span(GAIN_TWO)
        grad_in = (inner - row_mean(inner) - zhat * row_mean(inner * zhat)) * rstd
        grad_two[rows, :] = grad_in
        low = grad_in.astype(bf16)
        grad_down[rows, :] = low
        gain, shift, bias = carry
        return gain + fold(grad * zhat), shift + fold(grad), bias + fold(low.astype(f32))

    zero = jnp.zeros((8, D), f32)
    gain, shift, bias = by_rows(tok, norm_two, (zero, zero, zero))
    store(mixed, mixed_hbm)
    put_vec(GAIN_TWO, column_sum(gain))
    put_vec(SHIFT_TWO, column_sum(shift))
    put_vec(BIAS_DOWN, column_sum(bias))
    grad_down_came = share_half(grad_down, narrow_grad)
    keys_turned[...] = transposed(keys_values[:, :D])

    here = {"f": z // 2, "n": z % 2, "x": x, "y": y}
    across = {"f": along[1], "n": along[0], "x": beside, "y": beyond}

    class Chain:
        def __init__(self, index):
            matrix, start, rows, order = CHUNKS[index]
            self.index, self.order, self.stage = index, order, 0
            self.rows = pl.ds(start, rows)
            self.own = part.at[matrix]
            self.came = [ref.at[matrix] for ref in (came_one, came_two, came_three, came_four)]
            self.final = sums.at[matrix]

        def cells(self, free, flipped=None):
            return tuple(
                slice(None) if name in free else 1 - here[name] if name == flipped else here[name]
                for name in "fnxy"
            ) + (self.rows,)

        def send(self, source, target, other):
            sems = (send_sem.at[self.index, self.stage], recv_sem.at[self.index, self.stage])
            self.copy = remote(source, target, *sems, other)

        def advance(self):
            stage, order = self.stage, self.order
            if stage:
                self.copy.wait_recv()
            if 1 <= stage <= 4:
                free = order[stage:]
                for choice in itertools.product((0, 1), repeat=len(free)):
                    taken = dict(zip(sorted(free, key="fnxy".index), choice))
                    at = tuple(taken.get(name, here[name]) for name in "fnxy") + (self.rows,)
                    value = self.own[at] + self.came[stage - 1][choice + (self.rows,)]
                    if stage == 4:
                        self.final[core, y, self.rows] = value
                    else:
                        self.own[at] = value
            if stage < 4:
                name = order[stage]
                source = self.own.at[self.cells(order[stage + 1 :], name)]
                target = self.came[stage].at[(slice(None),) * (3 - stage) + (self.rows,)]
                self.send(source, target, across[name])
            elif stage == 4:
                block = self.final.at[core, y, self.rows]
                self.send(block, block, beyond)
            elif stage == 5:
                block = self.final.at[core, :, self.rows]
                self.send(block, block, partner)
            self.stage += 1

    chains = [Chain(index) for index in range(len(CHUNKS))]
    plan = iter(CHUNK_PLAN)

    def pump():
        for index in next(plan):
            chains[index].advance()

    def feed_forward(matrix, narrow, wide):
        left = transposed(narrow[...])

        def block(index, carry):
            cols = pl.ds(pl.multiple_of(index * UNIT, UNIT), UNIT)
            value = dot(left, wide[:, cols], 1, 0).astype(bf16)
            for side in range(2):
                part[matrix, index // 4, index // 2 % 2, index % 2, side] = value[
                    side * SIDE : (side + 1) * SIDE
                ]
            return carry

        lax.fori_loop(0, 8, block, 0)

    def projections(matrix, turned, narrow, width, offset, between=None):
        for tile in range(turned.shape[0] // UNIT):
            if between and tile % 2 == 0:
                between()
            value = dot(turned[tile * UNIT : (tile + 1) * UNIT, :], narrow[...], 1, 0).astype(bf16)
            for start in range(0, UNIT, PIECE):
                block, row = divmod(tile * UNIT + start, width)
                side, row = divmod(offset + row, SIDE)
                cell = (matrix, block // 4, block // 2 % 2, block % 2, side)
                part[cell + (pl.ds(row, PIECE),)] = value[start : start + PIECE]

    grad_down_came.wait_recv()
    active_came.wait_recv()
    feed_forward(0, narrow_grad, active)

    for tile in range(FF // D):
        pump()
        cols = slice(tile * D, (tile + 1) * D)
        work[...] = dot(grad_down[...], down_w[cols, :], 1, 1)

        def gelu_back(rows, carry):
            low = (work[rows, :] * slope[rows, cols]).astype(bf16)
            grad_up[rows, cols] = low
            return carry + fold(low.astype(f32))

        put_vec(BIAS_UP + cols.start, column_sum(by_rows(tok, gelu_back, zero)))
    grad_up_came = to_partner(grad_up.at[own_rows], grad_up.at[far_rows])
    pump()
    normed_came.wait_recv()
    grad_up_came.wait_recv()
    feed_forward(1, narrow_normed, grad_up)
    pump()

    work[...] = dot(grad_up[own_rows, :], up_w[...], 1, 1)

    def norm_one_back(rows, carry):
        grad = grad_two[rows, :] + work[rows, :]
        zhat = zhat_one[rows, :]
        inner = grad * span(GAIN_ONE)
        grad_in = inner - row_mean(inner) - zhat * row_mean(inner * zhat)
        grad_in = grad_in * rstd_one[rows, 0:1]
        grad_one[rows, :] = grad_in
        low = grad_in.astype(bf16)
        grad_attn[rows, :] = low
        gain, shift, bias = carry
        return gain + fold(grad * zhat), shift + fold(grad), bias + fold(low.astype(f32))

    gain, shift, bias = by_rows(tok, norm_one_back, (zero, zero, zero))
    put_vec(GAIN_ONE, column_sum(gain))
    put_vec(SHIFT_ONE, column_sum(shift))
    put_vec(BIAS_OUT, column_sum(bias))
    grad_heads[...] = dot(grad_attn[...], out_w[...], 1, 1).astype(bf16)
    heads_turned[...] = dot(out_w[...], grad_attn[...], 1, 1).astype(bf16)

    half_lanes = LANES // 2

    def attend_pair_back(pair, carry):
        cols = lanes_at(pair * LANES)
        values = keys_values[:, lanes_at(D + pair * LANES)]
        for side, mask in enumerate(masks):
            start = pl.multiple_of(pair * LANES + side * half_lanes, half_lanes)
            rows = pl.ds(start, half_lanes)
            low_chance = prob[2 * pair + side]
            chance = low_chance.astype(f32)
            grad_chance = dot(grad_heads[:, cols] * mask, values, 1, 1)
            mean = jnp.sum(chance * grad_chance, axis=-1, keepdims=True)
            grad_score = (chance * (grad_chance - mean)).astype(bf16)
            values_grad = dot(heads_turned[rows, :], low_chance, 1, 0).astype(bf16)
            keys_grad = (dot(query_turned[rows, :], grad_score, 1, 0) * scale).astype(bf16)
            query_grad = (dot(keys_turned[rows, :], grad_score, 1, 1) * scale).astype(bf16)
            blocks = (
                query_grad,
                keys_grad[:, :tok],
                values_grad[:, :tok],
                keys_grad[:, tok:],
                values_grad[:, tok:],
            )
            for index, value in enumerate(blocks):
                start = index * LANES + side * half_lanes
                exchanged[0, pair, start : start + half_lanes, :] = value
        return carry

    half_came = []
    for half in range(2):
        pump()
        pairs = pl.ds(half * HEADS // 4, HEADS // 4)
        lax.fori_loop(half * HEADS // 4, (half + 1) * HEADS // 4, attend_pair_back, 0)
        half_came.append(to_partner(exchanged.at[0, pairs], exchanged.at[1, pairs]))
    pump()
    attn_turned[:, own_lanes] = transposed(grad_attn[...])
    grad_attn_came = to_partner(attn_turned.at[:, own_lanes], attn_turned.at[:, far_lanes])

    for pair in range(HEADS // 2):
        if pair % (HEADS // 4) == 0:
            half_came[pair // (HEADS // 4)].wait_recv()
        for who, lanes in enumerate((own_lanes, far_lanes)):
            start = pair * LANES
            mine, theirs = exchanged.at[who, pair], exchanged.at[1 - who, pair]
            qkv_turned[start : start + LANES, lanes] = mine[:LANES]
            for index in (1, 2):
                rows = slice(index * LANES, (index + 1) * LANES)
                sent = slice((index + 2) * LANES, (index + 3) * LANES)
                value = mine[rows].astype(f32) + theirs[sent].astype(f32)
                start = index * D + pair * LANES
                qkv_turned[start : start + LANES, lanes] = value.astype(bf16)
    pump()
    tokens_came.wait_recv()
    projections(2, qkv_turned, narrow_tokens, 3 * D // 8, 0, pump)
    attended_came.wait_recv()
    grad_attn_came.wait_recv()
    projections(2, attn_turned, narrow_attended, D // 8, 3 * D // 8)
    pump()

    ones = jnp.ones((8, tok), bf16)
    for start, rows in ((BIAS_QUERY, slice(0, D)), (BIAS_VALUE, slice(2 * D, 3 * D))):
        put_vec(start, dot(ones, qkv_turned[rows, own_lanes], 1, 1)[0:1])
    vec_came = to_partner(vec, vec_core)
    value = dot(qkv_w[...], qkv_turned[:, own_lanes], 1, 0)
    input_grad[...] = grad_one[...] + value.T
    store(input_grad, grad_hbm)

    vec_slots = [(send_sem.at[len(CHUNKS), i], recv_sem.at[len(CHUNKS), i]) for i in range(5)]

    def vec_steps():
        vec_came.wait_recv()
        vec_core[...] = vec[...] + vec_core[...]
        copy = remote(vec_core, vec_y, *vec_slots[0], beyond)
        yield
        copy.wait_recv()
        for i in range(4):
            vec_x[0, i] = vec_core[2 * i + x] + vec_y[2 * i + x]
            vec_x[1, i] = vec_core[2 * i + 1 - x] + vec_y[2 * i + 1 - x]
        copy = remote(vec_x.at[1], vec_x.at[2], *vec_slots[1], beside)
        yield
        copy.wait_recv()
        vec_x[0] = vec_x[0] + vec_x[2]
        copies = [
            remote(
                vec_x.at[0, flip_z(z, step)],
                vec_z.at[step - 1],
                *vec_slots[1 + step],
                along[step - 1],
            )
            for step in (1, 2, 3)
        ]
        yield
        total = vec_x[0, z]
        for step, copy in enumerate(copies):
            copy.wait_recv()
            total = total + vec_z[step]
        vec_sum[...] = total
        yield

    steps = vec_steps()
    left = [sum(chunk[0] == matrix for chunk in CHUNKS) for matrix in range(3)]
    for turn, index in enumerate(next(plan)):
        chains[index].advance()
        matrix = CHUNKS[index][0]
        left[matrix] -= chains[index].stage == 7
        if not left[matrix]:
            store(sums.at[matrix], sums_hbm.at[matrix])
            left[matrix] = -1
        if turn % 10 == 9 and turn < 40:
            next(steps)
    for copy in stores:
        copy.wait()
    for copy in started:
        copy.wait_send()


def layer(row_class, lengths, tokens, cotangent, vectors, qkv_w, out_w, up_w, down_w):
    tok = tokens.shape[0]
    side = (SIDE, UNIT)

    def low(*dims):
        return pltpu.VMEM(dims, bf16)

    def wide(*dims):
        return pltpu.VMEM(dims, f32)

    return pl.pallas_call(
        layer_kernel,
        out_shape=(
            jax.ShapeDtypeStruct((tok, D), f32),
            jax.ShapeDtypeStruct((tok, D), f32),
            jax.ShapeDtypeStruct((3, 2, 2) + side, bf16),
            jax.ShapeDtypeStruct((16, LANES), f32),
        ),
        in_specs=[SMEM, SMEM, VMEM, VMEM, VMEM] + [ANY] * 4,
        out_specs=(ANY, ANY, ANY, VMEM),
        scratch_shapes=[
            wide(tok, D),
            wide(tok, D),
            low(3, 2, 2, *side),
            low(D, 3 * D),
            low(D, D),
            low(D, FF),
            low(FF, D),
            low(tok, D),
            low(D, tok),
            low(2 * tok, 2 * D),
            low(D, 2 * tok),
            low(HEADS, tok, 2 * tok),
            low(tok, D),
            low(tok, D),
            low(tok, D),
            low(tok, D),
            low(2 * tok, HALF),
            low(2 * tok, HALF),
            low(2 * tok, HALF),
            low(2 * tok, HALF),
            low(2 * tok, FF),
            low(2 * tok, FF),
            low(D, 2 * tok),
            low(3 * D, 2 * tok),
            low(2, HEADS // 2, 5 * LANES, tok),
            low(tok, D),
            low(D, tok),
            wide(tok, FF),
            wide(tok, D),
            wide(tok, D),
            wide(tok, LANES),
            wide(tok, D),
            wide(tok, D),
            wide(8, 16, LANES),
            wide(8, 16, LANES),
            wide(8, 16, LANES),
            wide(3, 4, 16, LANES),
            wide(3, 16, LANES),
            low(3, 2, 2, 2, 2, *side),
            low(3, 2, 2, 2, *side),
            low(3, 2, 2, *side),
            low(3, 2, *side),
            low(3, *side),
            pltpu.SemaphoreType.DMA((6,)),
            pltpu.SemaphoreType.DMA((5,)),
            pltpu.SemaphoreType.DMA((12,)),
            pltpu.SemaphoreType.DMA((12,)),
            pltpu.SemaphoreType.DMA((len(CHUNKS) + 1, 6)),
            pltpu.SemaphoreType.DMA((len(CHUNKS) + 1, 6)),
        ],
        compiler_params=pltpu.CompilerParams(
            vmem_limit_bytes=63 * MIB, collective_id=0, has_side_effects=True
        ),
        name="layer",
    )(row_class, lengths, tokens, cotangent, vectors[None, :], qkv_w, out_w, up_w, down_w)


GRAM_AXES = ("far", "near", "x")
GRAM_GROUPS = (
    (1, "xnf"),
    (2, "xnf"),
    (2, "xnf"),
    (3, "xnf"),
    (3, "nxf"),
    (3, "fxn"),
    (3, "nxf"),
    (2, "xnf"),
    (1, "xnf"),
    (1, "xnf"),
)
GRAM_PLAN = (
    6, 0, 9, 2, 5, 4, 7, 3, 0, 9, 6, 8, 2, 0, 9, 1, 0, 7, 9, 8, 2, 6,
    0, 5, 4, 3, 1, 8, 2, 7, 0, 6, 9, 5, 4, 8, 0, 2, 7, 1, 8, 9, 6, 3,
    5, 4, 7, 1, 8, 6, 2, 9, 3, 5, 8, 1, 4, 7, 2, 3, 5, 1, 4, 6, 7, 3,
    1, 5, 3, 4,
)


def muon_kernel(
    sums,
    qkv_hbm,
    out_hbm,
    up_hbm,
    down_hbm,
    factors_hbm,
    factors,
    own_sum,
    qkv_old,
    out_old,
    old,
    moment,
    out,
    part,
    came_one,
    came_two,
    came_three,
    high,
    low,
    load_sem,
    send_sem,
    recv_sem,
    share_send,
    share_recv,
    *ortho,
):
    z, x, y, core = position()
    here = {"far": z // 2, "near": z % 2, "x": x}
    others = {
        "far": device(flip_z(z, 2), x, y, core),
        "near": device(flip_z(z, 1), x, y, core),
        "x": device(z, 1 - x, y, core),
    }
    beyond = device(z, x, 1 - y, core)
    partner = device(z, x, y, 1 - core)
    own = 2 * y + core
    all_here = greet(list(others.values()) + [beyond, partner])

    def load_two(source, target, matrix):
        loads = [
            pltpu.make_async_copy(source, target, load_sem.at[0]),
            pltpu.make_async_copy(sums.at[matrix], own_sum, load_sem.at[1]),
        ]
        for load in loads:
            load.start()
        for load in loads:
            load.wait()

    def from_turned(source, target, skip):
        load_two(source, target, 2)
        rows = target.shape[0]
        moment[...] = jnp.zeros_like(moment)
        for half in range(2):
            cols = slice(half * HALF, (half + 1) * HALF)
            start = half * UNIT + skip
            value = own_sum[start : start + rows, :].astype(f32)
            moment[cols, skip : skip + rows] = (muon_keep * target[:, cols] + value).T

    @pl.when(own == 0)
    def _():
        from_turned(qkv_hbm, qkv_old, 0)

    @pl.when(own == 1)
    def _():
        from_turned(out_hbm, out_old, qkv_old.shape[0])

    @pl.when(own == 2)
    def _():
        load_two(up_hbm, old, 1)
        moment[...] = muon_keep * old[...] + own_sum[...].astype(f32)

    @pl.when(own == 3)
    def _():
        load_two(down_hbm, old, 0)
        moment[...] = muon_keep * old[...] + own_sum[...].astype(f32)

    all_here()
    blocks = sub_blocks(moment.shape[0])
    starts = [sum(count for count, _ in GRAM_GROUPS[:group]) for group in range(len(GRAM_GROUPS))]
    high[...] = moment[...].astype(bf16)
    low[...] = (moment[...] - high[...].astype(f32)).astype(bf16)
    started = []

    def products(first, count):
        i, j = blocks[first]
        count = min(count, sum(row == i for row, _ in blocks[first:]))
        left, right = pl.ds(i * SUB, SUB), pl.ds(j * SUB, count * SUB)
        total = dot(high[left, :], high[right, :], 1, 1)
        total = total + dot(high[left, :], low[right, :], 1, 1)
        total = total + dot(low[left, :], high[right, :], 1, 1)
        rows = SUB // 8
        for index in range(count):
            for owner in range(8):
                cell = (owner // 4, owner // 2 % 2, owner % 2, first + index)
                part[cell] = total[
                    owner * rows : (owner + 1) * rows, index * SUB : (index + 1) * SUB
                ]
        return count

    def send(source, target, group, slot, axis):
        copy = pltpu.make_async_remote_copy(
            src_ref=source,
            dst_ref=target,
            send_sem=send_sem.at[group, slot],
            recv_sem=recv_sem.at[group, slot],
            device_id=others[axis],
            device_id_type=MESH,
        )
        copy.start()
        started.append(copy)
        return copy

    def cells(fixed, flipped=None):
        return tuple(
            1 - here[name] if name == flipped else here[name] if name in fixed else slice(None)
            for name in GRAM_AXES
        )

    class Walk:
        def __init__(self, group):
            count, order = GRAM_GROUPS[group]
            self.group, self.stage = group, 0
            self.order = [GRAM_AXES["fnx".index(letter)] for letter in order]
            self.mine = (pl.ds(starts[group], count),)
            self.came = [
                ref.at[(slice(None),) * (2 - stage) + self.mine]
                for stage, ref in enumerate((came_one, came_two, came_three))
            ]

        def advance(self):
            stage, order = self.stage, self.order
            mine = self.mine
            if stage:
                self.copy.wait_recv()
            if 1 <= stage <= 3:
                kept = cells(order[:stage]) + mine
                total = part[kept] + self.came[stage - 1][...]
                if stage == 3:
                    out[kept] = total
                else:
                    part[kept] = total
            if stage < 3:
                source = part.at[cells(order[:stage], order[stage]) + mine]
                self.copy = send(source, self.came[stage], self.group, stage, order[stage])
            elif stage < 6:
                block = out.at[cells(order[: 6 - stage]) + mine]
                self.copy = send(block, block, self.group, stage, order[5 - stage])
            self.stage += 1

    walks = [Walk(group) for group in range(len(GRAM_GROUPS))]
    for group in GRAM_PLAN:
        if walks[group].stage == 0:
            first, end = starts[group], starts[group] + GRAM_GROUPS[group][0]
            while first < end:
                first += products(first, end - first)
        walks[group].advance()

    e = ortho[0]
    for index, (i, j) in enumerate(blocks):
        value = out[:, :, :, index].reshape(SUB, SUB)
        e[i * SUB : (i + 1) * SUB, j * SUB : (j + 1) * SUB] = value
        if i != j:
            e[j * SUB : (j + 1) * SUB, i * SUB : (i + 1) * SUB] = value.T

    across, beside = [], []

    def share(slot, rows, kind, other):
        block = factors.at[slot, rows]
        index = rows.start // TILE
        copy = pltpu.make_async_remote_copy(
            src_ref=block,
            dst_ref=block,
            send_sem=share_send.at[index, kind],
            recv_sem=share_recv.at[index, kind],
            device_id=other,
            device_id_type=MESH,
        )
        copy.start()
        started.append(copy)
        return copy

    def emit(rows, value):
        factors[own, rows, :] = value
        across.append((rows, share(own, rows, 0, beyond)))
        beside.append(share(own, rows, 1, partner))

    newton_schulz(e, moment, *ortho, emit)
    far = 2 * (1 - y) + core
    stores = []

    def store(slot):
        copy = pltpu.make_async_copy(
            factors.at[slot], factors_hbm.at[slot], load_sem.at[2 + len(stores)]
        )
        copy.start()
        stores.append(copy)

    store(own)
    for copy in beside:
        copy.wait_recv()
    store(2 * y + 1 - core)
    passed = []
    for rows, copy in across:
        copy.wait_recv()
        passed.append(share(far, rows, 2, partner))
    store(far)
    for copy in passed:
        copy.wait_recv()
    store(2 * (1 - y) + 1 - core)
    for copy in stores:
        copy.wait()
    for copy in started:
        copy.wait_send()


def muon_factors(sums, *olds):
    size, cols = olds[2].shape
    count = len(sub_blocks(size))
    groups = len(GRAM_GROUPS)
    rows = (SUB // 8, SUB)

    def wide(*dims):
        return pltpu.VMEM(dims, f32)

    return pl.pallas_call(
        muon_kernel,
        out_shape=jax.ShapeDtypeStruct((4, size, cols), bf16),
        in_specs=[ANY] * 5,
        out_specs=ANY,
        scratch_shapes=[
            pltpu.VMEM((4, size, cols), bf16),
            pltpu.VMEM((size, cols), bf16),
            wide(*olds[0].shape),
            wide(*olds[1].shape),
            wide(size, cols),
            wide(size, cols),
            wide(2, 2, 2, count, *rows),
            wide(2, 2, 2, count, *rows),
            wide(2, 2, count, *rows),
            wide(2, count, *rows),
            wide(count, *rows),
            pltpu.VMEM((size, cols), bf16),
            pltpu.VMEM((size, cols), bf16),
            pltpu.SemaphoreType.DMA((6,)),
            pltpu.SemaphoreType.DMA((groups, 6)),
            pltpu.SemaphoreType.DMA((groups, 6)),
            pltpu.SemaphoreType.DMA((size // TILE, 3)),
            pltpu.SemaphoreType.DMA((size // TILE, 3)),
        ]
        + ortho_scratch(size, cols),
        compiler_params=pltpu.CompilerParams(
            vmem_limit_bytes=58 * MIB, collective_id=1, has_side_effects=True
        ),
        name="muon_factors",
    )(sums, *olds)


def window(start, width, total):
    size = -(-(width + 96) // LANES) * LANES
    first = jnp.minimum(start // LANES * LANES, total - size)
    return pl.ds(pl.multiple_of(first, LANES), size), start - first


def finish_kernel(
    factors_hbm,
    sums_hbm,
    qkv_hbm,
    out_hbm,
    up_hbm,
    down_hbm,
    qkv_old_hbm,
    out_old_hbm,
    up_old_hbm,
    down_old_hbm,
    mixed_hbm,
    grad_hbm,
    vec_grad,
    vectors,
    first_old,
    second_old,
    mixed_out,
    grad_out,
    qkv_moment_out,
    out_moment_out,
    up_moment_out,
    down_moment_out,
    qkv_out,
    out_out,
    up_out,
    down_out,
    first_new,
    second_new,
    vec_new,
    factors,
    sums,
    qkv_w,
    out_w,
    up_w,
    down_w,
    qkv_moment,
    out_moment,
    up_moment,
    down_moment,
    qkv_new,
    out_new,
    up_new,
    down_new,
    turned,
    load_sem,
    store_sem,
):
    shrink = 1.0 - muon_rate * muon_decay
    dp_id = lax.axis_index("dp")
    qkv_cols, out_cols = qkv_new.shape[0], out_new.shape[0]
    qkv_lanes, qkv_skip = window(dp_id * qkv_cols, qkv_cols, 3 * D)
    out_lanes, out_skip = window(dp_id * out_cols, out_cols, D)
    block = pl.ds(pl.multiple_of(dp_id * UNIT, UNIT), UNIT)
    pairs = {
        "sums": (sums_hbm, sums),
        "up_moment": (up_old_hbm, up_moment),
        "down_moment": (down_old_hbm, down_moment),
        "factors": (factors_hbm, factors),
        "up": (up_hbm.at[:, block], up_w),
        "down": (down_hbm.at[block], down_w),
        "qkv_moment": (qkv_old_hbm, qkv_moment),
        "out_moment": (out_old_hbm, out_moment),
        "qkv": (qkv_hbm.at[:, qkv_lanes], qkv_w),
        "out": (out_hbm.at[:, out_lanes], out_w),
    }
    loads = {
        name: pltpu.make_async_copy(source, target, load_sem.at[index])
        for index, (name, (source, target)) in enumerate(pairs.items())
    }
    for load in loads.values():
        load.start()
    stores = []

    def store(source, target):
        stores.append(pltpu.make_async_copy(source, target, store_sem.at[len(stores)]))
        stores[-1].start()

    store(mixed_hbm, mixed_out)
    store(grad_hbm, grad_out)

    grad = vec_grad[:VEC_BLOCK]
    first = beta_first * first_old[...] + (1.0 - beta_first) * grad
    second = beta_second * second_old[...] + (1.0 - beta_second) * grad * grad
    first_new[...] = first
    second_new[...] = second
    first = first / (1.0 - beta_first**STEP)
    second = second / (1.0 - beta_second**STEP)
    own = jnp.zeros_like(grad)
    for index in range(8):
        rows = vectors[index * VEC_BLOCK : (index + 1) * VEC_BLOCK]
        own = jnp.where(dp_id == index, rows, own)
    vec_new[...] = own - adam_rate * first / (jnp.sqrt(second) + adam_eps)

    def step(index, rate, turned=False):
        value = factors[index]
        value = transposed(value) if turned else value
        return muon_rate * rate * value.astype(f32)

    loads["sums"].wait()
    for index, name, target, out in (
        (1, "up_moment", up_moment, up_moment_out),
        (0, "down_moment", down_moment, down_moment_out),
    ):
        loads[name].wait()
        target[...] = muon_keep * target[...] + sums[index].astype(f32)
        store(target, out)
    loads["qkv_moment"].wait()
    loads["out_moment"].wait()
    for half in range(2):
        cols = slice(half * HALF, (half + 1) * HALF)
        value = sums[2, cols].astype(f32)
        qkv_moment[:, cols] = muon_keep * qkv_moment[:, cols] + value[:qkv_cols]
        out_moment[:, cols] = muon_keep * out_moment[:, cols] + value[qkv_cols:]
    store(qkv_moment, qkv_moment_out)
    store(out_moment, out_moment_out)
    loads["factors"].wait()
    loads["up"].wait()
    up_new[...] = up_w[...].astype(f32) * shrink - step(2, math.sqrt(max(1.0, FF / D)))
    store(up_new, up_out)
    loads["down"].wait()
    down_new[...] = down_w[...].astype(f32) * shrink - step(3, 1.0, True)
    store(down_new, down_out)
    loads["qkv"].wait()
    turned[...] = transposed(qkv_w[...]).astype(f32)
    rows = pl.ds(pl.multiple_of(qkv_skip, 32), qkv_cols)
    qkv_new[...] = turned[rows, :] * shrink - step(0, math.sqrt(3.0), True)[:qkv_cols]
    store(qkv_new, qkv_out)
    loads["out"].wait()
    turned[: out_w.shape[1], :] = transposed(out_w[...]).astype(f32)
    rows = pl.ds(pl.multiple_of(out_skip, 32), out_cols)
    out_new[...] = turned[rows, :] * shrink - step(1, 1.0, True)[qkv_cols:]
    store(out_new, out_out)
    for copy in stores:
        copy.wait()


def finish(factors, sums, weights, olds, mixed, input_grad, vec, vectors, adam):
    shapes = [old.shape for old in olds]
    news = shapes[:3] + [shapes[3][::-1]]

    def wide(shape):
        return pltpu.VMEM(shape, f32)

    return pl.pallas_call(
        finish_kernel,
        out_shape=tuple(
            jax.ShapeDtypeStruct(shape, f32)
            for shape in [mixed.shape, input_grad.shape] + shapes + news + [(VEC_BLOCK, LANES)] * 3
        ),
        in_specs=[ANY] * 12 + [VMEM] * 4,
        out_specs=(ANY,) * 10 + (VMEM,) * 3,
        scratch_shapes=[
            pltpu.VMEM(factors.shape, bf16),
            pltpu.VMEM(sums.shape, bf16),
            pltpu.VMEM((D, 384), bf16),
            pltpu.VMEM((D, 256), bf16),
            pltpu.VMEM((D, UNIT), bf16),
            pltpu.VMEM((UNIT, D), bf16),
        ]
        + [wide(shape) for shape in shapes + news]
        + [
            wide((384, D)),
            pltpu.SemaphoreType.DMA((10,)),
            pltpu.SemaphoreType.DMA((10,)),
        ],
        compiler_params=pltpu.CompilerParams(vmem_limit_bytes=48 * MIB),
        name="finish",
    )(factors, sums, *weights, *olds, mixed, input_grad, vec, vectors, *adam)


def swap(value, axis, bit):
    size = lax.axis_size(axis)
    return lax.ppermute(value, axis, [(i, i ^ bit) for i in range(size)])


def scatter_head(value, bit, position):
    half = value.shape[1] // 2
    mine = lax.dynamic_slice_in_dim(value, position * half, half, 1)
    other = lax.dynamic_slice_in_dim(value, (1 - position) * half, half, 1)
    return (mine.astype(f32) + swap(other, "head", bit).astype(f32)).astype(bf16)


def scatter_dp_pair(value, position):
    paired = value.reshape((value.shape[0] // 2, 2) + value.shape[1:])
    mine = lax.dynamic_index_in_dim(paired, position, 1, False)
    other = lax.dynamic_index_in_dim(paired, 1 - position, 1, False)
    return (mine.astype(f32) + swap(other, "dp", 1).astype(f32)).astype(bf16)


def scatter_dp_rest(value, place):
    ranks = value.shape[0]
    total = lax.dynamic_index_in_dim(value, place, 0, False).astype(f32)
    for step in range(1, ranks):
        sent = lax.dynamic_index_in_dim(value, place ^ step, 0, False)
        total = total + swap(sent, "dp", 2 * step).astype(f32)
    return total


def local(
    tokens,
    cotangent,
    qkv_weight,
    out_weight,
    up_weight,
    down_weight,
    vectors,
    qkv_moment,
    out_moment,
    up_moment,
    down_moment,
    adam_first,
    adam_second,
    bucket_class,
    row_lengths,
):
    n_dp = lax.axis_size("dp")
    n_head = lax.axis_size("head")
    dp_id = lax.axis_index("dp")
    head_id = lax.axis_index("head")
    core, side = head_id % 2, head_id // 2
    tok, width = tokens.shape
    hidden = up_weight.shape[1]
    half = width // 2
    qkv_cols, out_cols = qkv_moment.shape[1], out_moment.shape[1]
    shrink = 1.0 - muon_rate * muon_decay

    def weight_block(weight, cols, dim):
        return lax.dynamic_slice_in_dim(weight, dp_id * cols, cols, dim)

    block = head_id.astype(jnp.int32)[None]
    vec_len = vectors.shape[0] // n_dp
    if (n_dp, n_head, tok) == (8, 4, 256):
        mixed, input_grad, sums, vec = layer(
            bucket_class,
            row_lengths,
            tokens,
            cotangent,
            vectors,
            qkv_weight,
            out_weight,
            up_weight,
            down_weight,
        )
        sums = sums.reshape(3, width, -1)
        olds = [qkv_moment.T, out_moment.T, up_moment, down_moment]
        mixed, input_grad, *results = finish(
            muon_factors(sums, *olds),
            sums,
            [qkv_weight, out_weight, up_weight, down_weight],
            olds,
            mixed,
            input_grad,
            vec,
            vectors.reshape(-1, LANES),
            [adam_first.reshape(-1, LANES), adam_second.reshape(-1, LANES)],
        )
        moments, new_weights = results[:4], results[4:8]
        vec_first, vec_second, vec_new = (value.reshape(vec_len) for value in results[8:])
        moments = [moments[0].T, moments[1].T, *moments[2:]]
        new_weights = [new_weights[0].T, new_weights[1].T, *new_weights[2:]]
    else:
        pieces = split_vectors(vectors, width, hidden)
        bias_query, bias_value, bias_out, gain_one, shift_one = pieces[:5]
        bias_up, bias_down, gain_two, shift_two = pieces[5:]
        bias_qkv = jnp.concatenate([bias_query, jnp.zeros_like(bias_query), bias_value])

        def column_half(value, which):
            return lax.dynamic_slice_in_dim(value, which * half, half, 1)

        qkv = (dot(tokens, qkv_weight, 1, 0) + bias_qkv).astype(bf16)
        other = swap(qkv[:, width:], "head", 1)
        attended = attend(block, bucket_class, row_lengths, qkv, other)
        attn_val = dot(attended, out_weight, 1, 0) + bias_out
        resid_one = tokens.astype(f32) + attn_val
        centre = resid_one - jnp.mean(resid_one, axis=-1, keepdims=True)
        rstd_one = lax.rsqrt(jnp.mean(centre * centre, axis=-1, keepdims=True) + norm_eps)
        zhat_one = centre * rstd_one
        normed_one = zhat_one * gain_one + shift_one
        normed_low = normed_one.astype(bf16)
        up_val = dot(normed_low, up_weight, 1, 0) + bias_up
        phi_cum = 0.5 * (1.0 + lax.erf(up_val * (0.5**0.5)))
        active_low = (up_val * phi_cum).astype(bf16)
        slope = phi_cum + up_val * jnp.exp(-0.5 * up_val * up_val) * (1.0 / math.sqrt(2.0 * math.pi))
        down_val = dot(active_low, down_weight, 1, 0) + bias_down
        resid_two = normed_one + down_val
        centre = resid_two - jnp.mean(resid_two, axis=-1, keepdims=True)
        rstd_two = lax.rsqrt(jnp.mean(centre * centre, axis=-1, keepdims=True) + norm_eps)
        zhat_two = centre * rstd_two
        mixed = zhat_two * gain_two + shift_two

        def norm_back(grad, gain, zhat, rstd):
            inner = grad * gain
            mean = jnp.mean(inner, axis=-1, keepdims=True)
            slant = jnp.mean(inner * zhat, axis=-1, keepdims=True)
            return (inner - mean - zhat * slant) * rstd, jnp.sum(grad * zhat, axis=0), jnp.sum(grad, axis=0)

        grad_two, grad_gain_two, grad_shift_two = norm_back(
            cotangent.astype(f32), gain_two, zhat_two, rstd_two
        )
        grad_down_low = grad_two.astype(bf16)
        grad_bias_down = jnp.sum(grad_down_low, axis=0, dtype=f32)

        x_id, z_id = dp_id % 2, dp_id // 2

        grad_up_low = (dot(grad_down_low, down_weight, 1, 1) * slope).astype(bf16)
        grad_bias_up = jnp.sum(grad_up_low, axis=0, dtype=f32)
        grad_normed = grad_two + dot(grad_up_low, up_weight, 1, 1)
        grad_one, grad_gain_one, grad_shift_one = norm_back(grad_normed, gain_one, zhat_one, rstd_one)
        grad_attn_low = grad_one.astype(bf16)
        grad_bias_out = jnp.sum(grad_attn_low, axis=0, dtype=f32)
        grad_heads = dot(grad_attn_low, out_weight, 1, 1).astype(bf16)
        grad_query, own, sent = attend_back(block, bucket_class, row_lengths, qkv, other, grad_heads)
        grad_kv = (own + swap(sent, "head", 1).astype(f32)).astype(bf16)
        grad_qkv = jnp.concatenate([grad_query, grad_kv], axis=1)
        grad_bias_qkv = jnp.sum(grad_qkv, axis=0, dtype=f32)
        input_grad = grad_one + dot(grad_qkv, qkv_weight, 1, 1)
        grad_vector = jnp.concatenate(
            [
                grad_bias_qkv[:width],
                grad_bias_qkv[2 * width :],
                grad_bias_out,
                grad_gain_one,
                grad_shift_one,
                grad_bias_up,
                grad_bias_down,
                grad_gain_two,
                grad_shift_two,
            ]
        )
        grad_vector = grad_vector + swap(grad_vector, "head", 1)
        wides = [active_low, grad_up_low, grad_attn_low, grad_qkv]
        narrows = [grad_down_low, normed_low, attended, tokens]

        def both_halves(value):
            return jnp.concatenate(
                [column_half(value, core), swap(column_half(value, 1 - core), "head", 1)], axis=0
            )

        def weight_grad(wide, narrow):
            wide = jnp.concatenate([wide, swap(wide, "head", 1)], axis=0)
            value = dot(wide, both_halves(narrow), 0, 0).astype(bf16)
            return value.reshape(n_dp, value.shape[0] // n_dp, half)

        def reduce_y_first(value):
            return scatter_dp_rest(scatter_dp_pair(scatter_head(value, 2, side), x_id), z_id)

        def reduce_x_first(value):
            return scatter_dp_rest(scatter_head(scatter_dp_pair(value, x_id), 2, side), z_id)

        def spread(value):
            value = value.astype(bf16)
            came = swap(value, "head", 2)
            value = jnp.concatenate(
                [jnp.where(side == 0, value, came), jnp.where(side == 0, came, value)], axis=0
            )
            came = swap(value, "head", 1)
            return jnp.concatenate(
                [jnp.where(core == 0, value, came), jnp.where(core == 0, came, value)], axis=1
            ).astype(f32)

        down_part, up_part, out_part, qkv_part = [
            weight_grad(wide, narrow) for wide, narrow in zip(wides, narrows)
        ]
        vec_rows = 16
        vec_part = grad_vector.reshape(n_dp, vec_len)
        vec_part = jnp.pad(vec_part, ((0, 0), (0, vec_rows * width - vec_len)))
        vec_part = vec_part.reshape(n_dp, vec_rows, width)
        vec_part = lax.dynamic_slice_in_dim(vec_part, core * half, half, 2).astype(bf16)
        down_new = spread(reduce_x_first(down_part))
        up_new = spread(reduce_y_first(up_part))
        tail_new = spread(
            reduce_y_first(jnp.concatenate([qkv_part, out_part, vec_part], axis=1))
        )
        grads = [
            tail_new[:qkv_cols].T,
            tail_new[qkv_cols : qkv_cols + out_cols].T,
            up_new.T,
            down_new.T,
        ]
        grad_vec = tail_new[qkv_cols + out_cols :].reshape(-1)[:vec_len]
        moments = [
            muon_keep * old + grad
            for old, grad in zip([qkv_moment, out_moment, up_moment, down_moment], grads)
        ]
        most = max(m.shape[1] for m in moments)
        padded = [jnp.pad(m, ((0, 0), (0, most - m.shape[1]))) for m in moments]
        chosen = padded[-1]
        for index in range(len(padded) - 2, -1, -1):
            chosen = jnp.where(head_id == index, padded[index], chosen)
        gram_mat = lax.dot_general(
            chosen, chosen, (((1,), (1,)), ((), ())), precision=lax.Precision.HIGH
        )
        own_factor = orthogonalize(lax.psum(gram_mat, "dp"), chosen)
        across = swap(own_factor, "head", 2)
        low_pair = jnp.where(side == 0, own_factor, across)
        high_pair = jnp.where(side == 0, across, own_factor)
        near_low = swap(low_pair, "head", 1)
        near_high = swap(high_pair, "head", 1)
        factors = [
            jnp.where(core == 0, low_pair, near_low),
            jnp.where(core == 0, near_low, low_pair),
            jnp.where(core == 0, high_pair, near_high),
            jnp.where(core == 0, near_high, high_pair),
        ]
        factors = [o[:, : m.shape[1]].astype(f32) for o, m in zip(factors, moments)]
        factors[3] = factors[3].T
        old_weights = [
            weight_block(qkv_weight, qkv_cols, 1),
            weight_block(out_weight, out_cols, 1),
            weight_block(up_weight, up_moment.shape[1], 1),
            weight_block(down_weight, down_moment.shape[1], 0),
        ]

        rates = (math.sqrt(3.0), 1.0, math.sqrt(max(1.0, hidden / width)), 1.0)
        new_weights = [
            old.astype(f32) * shrink - muon_rate * rate * factor
            for old, rate, factor in zip(old_weights, rates, factors)
        ]

        vec_old = lax.dynamic_slice_in_dim(vectors, dp_id * vec_len, vec_len, 0)
        vec_first = beta_first * adam_first + (1.0 - beta_first) * grad_vec
        vec_second = beta_second * adam_second + (1.0 - beta_second) * grad_vec * grad_vec
        first_hat = vec_first / (1.0 - beta_first**STEP)
        second_hat = vec_second / (1.0 - beta_second**STEP)
        vec_new = vec_old - adam_rate * first_hat / (jnp.sqrt(second_hat) + adam_eps)
    return (mixed, input_grad, *moments, *new_weights, vec_first, vec_second, vec_new)


def solution(mesh):
    tokens_spec = P(("dp", "head"), None)
    block_spec = P(None, "dp")
    return jax.shard_map(
        local,
        mesh=mesh,
        in_specs=(
            tokens_spec,
            tokens_spec,
            P(),
            P(),
            P(),
            P(),
            P(),
            block_spec,
            block_spec,
            block_spec,
            block_spec,
            P("dp"),
            P("dp"),
            P("dp"),
            P("dp", None),
        ),
        out_specs=(
            tokens_spec,
            tokens_spec,
            block_spec,
            block_spec,
            block_spec,
            block_spec,
            block_spec,
            block_spec,
            block_spec,
            P("dp", None),
            P("dp"),
            P("dp"),
            P("dp"),
        ),
        check_vma=False,
    )
```
